32 devices in a mesh: seq: 8 (over y, x, core), fsdp: 4 (over z).
Axes of the slice: x: 2, y: 2, z: 4, core: 2. Of those that a mesh axis runs over, the one named last changes fastest.
Arguments:
- block_input: bfloat16 [4, 1536, 2560], P('fsdp', 'seq'), may hold values from -6 to 6
- cotangent: bfloat16 [4, 1536, 2560], P('fsdp', 'seq'), may hold values from -6 to 6
- mixer_gain: bfloat16 [2560], P(('seq', 'fsdp')), may hold values from 0.099609375 to 1.8984375
- branch_proj: bfloat16 [2560, 2560], P(('seq', 'fsdp')), may hold values from -0.125 to 0.125
- gelu_proj: bfloat16 [2560, 2560], P(('seq', 'fsdp')), may hold values from -0.125 to 0.125
- conv_taps: bfloat16 [4, 2560], P(None, ('seq', 'fsdp')), may hold values from -3 to 3
- conv_bias: bfloat16 [2560], P(('seq', 'fsdp')), may hold values from -3 to 3
- rate_blocks: bfloat16 [2560, 256], P(('seq', 'fsdp')), may hold values from -0.375 to 0.375
- input_blocks: bfloat16 [2560, 256], P(('seq', 'fsdp')), may hold values from -0.375 to 0.375
- rate_bias: bfloat16 [2560], P(('seq', 'fsdp')), may hold values from -4 to 4
- input_bias: bfloat16 [2560], P(('seq', 'fsdp')), may hold values from -4 to 4
- decay_param: bfloat16 [2560], P(('seq', 'fsdp')), may hold values from 3 to 16
- out_proj: bfloat16 [2560, 2560], P(('seq', 'fsdp')), may hold values from -0.3125 to 0.3125
- mlp_gain: bfloat16 [2560], P(('seq', 'fsdp')), may hold values from 0.099609375 to 1.8984375
- gate_proj: bfloat16 [2560, 7680], P(('seq', 'fsdp')), may hold values from -0.125 to 0.125
- up_proj: bfloat16 [2560, 7680], P(('seq', 'fsdp')), may hold values from -0.125 to 0.125
- down_proj: bfloat16 [2560, 7680], P(('seq', 'fsdp')), may hold values from -0.0625 to 0.0625
Outputs:
- block_output: bfloat16 [4, 1536, 2560], P('fsdp', 'seq')
- input_grad: bfloat16 [4, 1536, 2560], P('fsdp', 'seq')
- dmixer_gain: float32 [2560], P(('seq', 'fsdp'))
- dbranch_proj: float32 [2560, 2560], P(('seq', 'fsdp'))
- dgelu_proj: float32 [2560, 2560], P(('seq', 'fsdp'))
- dconv_taps: float32 [4, 2560], P(None, ('seq', 'fsdp'))
- dconv_bias: float32 [2560], P(('seq', 'fsdp'))
- drate_blocks: float32 [2560, 256], P(('seq', 'fsdp'))
- dinput_blocks: float32 [2560, 256], P(('seq', 'fsdp'))
- drate_bias: float32 [2560], P(('seq', 'fsdp'))
- dinput_bias: float32 [2560], P(('seq', 'fsdp'))
- ddecay_param: float32 [2560], P(('seq', 'fsdp'))
- dout_proj: float32 [2560, 2560], P(('seq', 'fsdp'))
- dmlp_gain: float32 [2560], P(('seq', 'fsdp'))
- dgate_proj: float32 [2560, 7680], P(('seq', 'fsdp'))
- dup_proj: float32 [2560, 7680], P(('seq', 'fsdp'))
- ddown_proj: float32 [2560, 7680], P(('seq', 'fsdp'))
The draws below stay inside these ranges and needn't reach their ends.
All inputs are finite; a program needn't handle non-finite values.
Results may differ from the reference program's by a relative error of at most 0.012.
Values may be sent and summed in bfloat16 or wider, within the bound.
A program may use at most 832 MiB of HBM per device.

```python
import jax
import jax.numpy as jnp
from jax import lax

D = 2560
LRU = 2560
HEADS = 10
BW = 256
FF = 7680
CONV = 4
SEQS = 4
LENGTH = 1536


def draw_decay_param(key, part):
    key = jax.random.fold_in(key, 11)
    pick_key, slow_key, fast_key = jax.random.split(key, 3)
    portion = 0.5
    slow_pick = jax.random.uniform(pick_key, (LRU,)) < portion
    floor_log = jnp.log(0.05 / LENGTH)
    middle_log = jnp.log(0.5 / LENGTH)
    top_log = jnp.log(0.03)
    slow_log = jax.random.uniform(slow_key, (LRU,), minval=floor_log, maxval=middle_log)
    fast_log = jax.random.uniform(fast_key, (LRU,), minval=middle_log, maxval=top_log)
    per_step = jnp.exp(jnp.where(slow_pick, slow_log, fast_log))
    return (-jnp.log(jnp.expm1(per_step))).astype(jnp.bfloat16)


def strengthened(values, rng, source, target, shards_of, factor):
    owner, partner = [(jnp.arange(values.shape[position]) // (values.shape[position] // shards_of)).reshape([-1 if axis == position else 1 for axis in range(values.ndim)]) for position in (source, target)]
    chosen = jax.random.permutation(rng, shards_of)[partner]
    strong = (owner == chosen) | (owner == (partner + shards_of // 2) % shards_of)
    return jnp.where(strong, factor * values, values)


def shard_levels(rng, shape, pieces, low, top_value):
    gain = 1.0
    for position, parts in pieces:
        steps = jax.random.uniform(jax.random.fold_in(jax.random.fold_in(rng, 6), position), (parts,), jnp.float32, low / len(pieces), top_value / len(pieces))
        gain = gain * jnp.repeat(jnp.exp(steps), shape[position] // parts).reshape((-1,) + (1,) * (len(shape) - 1 - position))
    return gain


def gaussian(own_key, shape, scale, bound, shards=(), kind=jnp.bfloat16):
    level = shard_levels(own_key, shape, shards, -0.22, 0.18) if shards else 1.0
    array = jax.random.normal(own_key, shape, jnp.float32) * scale * level
    return jnp.minimum(jnp.maximum(array, -bound), bound).astype(kind)


def bell_draw_with(rng, shape, spread, most, cuts, heavy, held_as=jnp.bfloat16):
    array = spread * jax.random.normal(rng, shape, jnp.float32)
    if cuts:
        array = array * shard_levels(rng, shape, cuts, -0.22, 0.18)
    return jnp.clip(strengthened(array, jax.random.fold_in(rng, 3), *heavy), -most, most).astype(held_as)


def setup_inputs(seed: int = 0) -> dict:
    splits = jax.random.split(jax.random.key(seed), 18)
    block_input = gaussian(splits[0], (SEQS, LENGTH, D), 1.0, 6.0, ((0, 4), (1, 8)))
    cotangent = bell_draw_with(splits[1], (SEQS, LENGTH, D), 1.0, 6.0, ((0, 4), (1, 8)), (1, 2, 8, 2.0))
    mixer_gain = jnp.clip(1.0 + 0.18 * jax.random.normal(splits[2], (D,), jnp.float32), 0.099609375, 1.8984375).astype(jnp.bfloat16)
    branch_proj = gaussian(splits[3], (D, LRU), D ** -0.5, 0.125, ((0, 32),))
    gelu_proj = gaussian(splits[4], (D, LRU), D ** -0.5, 0.125, ((0, 32),))
    conv_taps = gaussian(splits[5], (CONV, LRU), CONV ** -0.5, 3.0, ((1, 32),))
    conv_bias = gaussian(splits[6], (LRU,), 0.5, 3.0, ((0, 32),))
    rate_blocks = gaussian(splits[7], (LRU, BW), BW ** -0.5, 0.375, ((0, 32),))
    input_blocks = gaussian(splits[8], (LRU, BW), BW ** -0.5, 0.375, ((0, 32),))
    rate_bias = gaussian(splits[9], (LRU,), 1.0, 4.0, ((0, 32),))
    input_bias = gaussian(splits[10], (LRU,), 1.0, 4.0, ((0, 32),))
    decay_param = draw_decay_param(jax.random.fold_in(splits[17], 71), 0)
    out_proj = gaussian(splits[12], (D, LRU), (LRU // 8) ** -0.5, 0.3125, ((0, 32),))
    mlp_gain = jnp.clip(1.0 + 0.18 * jax.random.normal(splits[13], (D,), jnp.float32), 0.099609375, 1.8984375).astype(jnp.bfloat16)
    gate_proj = gaussian(splits[14], (D, FF), D ** -0.5, 0.125, ((0, 32),))
    up_proj = gaussian(splits[15], (D, FF), D ** -0.5, 0.125, ((0, 32),))
    down_proj = gaussian(splits[16], (D, FF), FF ** -0.5, 0.0625, ((0, 32),))
    return {"block_input": block_input, "cotangent": cotangent, "mixer_gain": mixer_gain, "branch_proj": branch_proj, "gelu_proj": gelu_proj, "conv_taps": conv_taps, "conv_bias": conv_bias, "rate_blocks": rate_blocks, "input_blocks": input_blocks, "rate_bias": rate_bias, "input_bias": input_bias, "decay_param": decay_param, "out_proj": out_proj, "mlp_gain": mlp_gain, "gate_proj": gate_proj, "up_proj": up_proj, "down_proj": down_proj}


@jax.custom_vjp
def low(v):
    return lax.optimization_barrier(v.astype(jnp.bfloat16)).astype(jnp.float32)

@jax.custom_vjp
def low_back(v):
    return v

def low_keep(v):
    return (low(v), None)

def low_pass(kept, grad):
    return (grad,)

def back_keep(v):
    return (v, None)

def back_low(kept, grad):
    return (low(grad),)
low.defvjp(low_keep, low_pass)
low_back.defvjp(back_keep, back_low)
epsilon = 1e-06

def product(left, right):
    return jnp.dot(left, right, precision=lax.Precision.HIGHEST, preferred_element_type=jnp.float32)

def norm_rows(values, scales):
    return values * lax.rsqrt(lax.optimization_barrier(jnp.mean(values * values, axis=-1, keepdims=True)) + epsilon) * scales

def combine_pairs(earlier, later):
    return (earlier[0] * later[0], later[1] + later[0] * earlier[1])

def block_product(values, blocks):
    grouped = values.reshape(values.shape[0], HEADS, BW)
    result = jnp.einsum('thi,hij->thj', grouped, blocks.reshape(HEADS, BW, BW), precision=lax.Precision.HIGHEST)
    return result.reshape(values.shape[0], LRU)

def layer(tokens, mixer_gain, branch_proj, gelu_proj, conv_taps, conv_bias, rate_blocks, input_blocks, rate_bias, input_bias, decay_param, out_proj, mlp_gain, gate_proj, up_proj, down_proj):
    normed = low(norm_rows(tokens, mixer_gain))
    gelu_out = jax.nn.gelu(low_back(product(normed, gelu_proj)), approximate=True)
    branch = low_back(low(product(normed, branch_proj)))
    conv_sum = conv_bias + conv_taps[0] * branch
    for offset in range(1, CONV):
        shifted = jnp.concatenate([jnp.zeros((offset, LRU), jnp.float32), branch[:LENGTH - offset]], axis=0)
        conv_sum = conv_sum + conv_taps[offset] * shifted
    conv_low = low(conv_sum)
    rate_pre = low_back(block_product(conv_low, rate_blocks) + rate_bias)
    input_pre = low_back(block_product(conv_low, input_blocks) + input_bias)
    decay_log = -8.0 * jax.nn.sigmoid(rate_pre) * jax.nn.softplus(-decay_param)
    driven = jnp.sqrt(-jnp.expm1(2.0 * decay_log)) * jax.nn.sigmoid(input_pre) * conv_low
    states = lax.associative_scan(combine_pairs, (jnp.exp(decay_log), driven), axis=0)[1]
    mixed = low(states * gelu_out)
    middle = tokens + low_back(product(mixed, out_proj.T))
    normed_two = low(norm_rows(middle, mlp_gain))
    gate = low_back(product(normed_two, gate_proj))
    up_val = low_back(product(normed_two, up_proj))
    hidden = low(jax.nn.gelu(gate, approximate=True) * up_val)
    return middle + product(hidden, down_proj.T)

def reference(block_input, cotangent, mixer_gain, branch_proj, gelu_proj, conv_taps, conv_bias, rate_blocks, input_blocks, rate_bias, input_bias, decay_param, out_proj, mlp_gain, gate_proj, up_proj, down_proj):
    weights = tuple((member.astype(jnp.float32) for member in (mixer_gain, branch_proj, gelu_proj, conv_taps, conv_bias, rate_blocks, input_blocks, rate_bias, input_bias, decay_param, out_proj, mlp_gain, gate_proj, up_proj, down_proj)))

    def one_sequence(running, seq_pair):
        tokens, grads_in = seq_pair
        output, pullback = jax.vjp(layer, tokens.astype(jnp.float32), *weights)
        grads = pullback(grads_in.astype(jnp.float32))
        running = tuple((before + added for before, added in zip(running, grads[1:])))
        return (running, (output.astype(jnp.bfloat16), grads[0].astype(jnp.bfloat16)))
    start_totals = tuple((jnp.zeros(member.shape, jnp.float32) for member in weights))
    totals, (outputs, input_grads) = lax.scan(one_sequence, start_totals, (block_input, cotangent))
    return (outputs, input_grads, totals[0], totals[1], totals[2], totals[3], totals[4], totals[5], totals[6], totals[7], totals[8], totals[9], totals[10], totals[11], totals[12], totals[13], totals[14])
```

```python
import functools

import jax
import jax.numpy as jnp
from jax import lax
from jax.experimental import pallas as pl
from jax.experimental.pallas import tpu as pltpu
from jax.sharding import PartitionSpec as P

epsilon = 1e-06
f32 = jnp.float32
bf16 = jnp.bfloat16
both = ("seq", "fsdp")
TAP, CONV_BIAS, RATE_BIAS, INPUT_BIAS, SOFT, SOFT_SLOPE = 0, 4, 5, 6, 7, 8
GELU_C = 0.7978845608028654
GELU_A = 0.044715


def from_behind(shard, axis, by):
    devices = lax.axis_size(axis)
    pairs = [(i, i + by) for i in range(devices) if 0 <= i + by < devices]
    return lax.ppermute(shard, axis, pairs)


def prefix(part, axis, reverse):
    count = lax.axis_size(axis)
    place = lax.axis_index(axis)
    gathered = lax.all_gather(jnp.stack(part), axis)
    state = jnp.zeros_like(part[1])
    for hop in range(count):
        source = count - 1 - hop if reverse else hop
        ahead = source > place if reverse else source < place
        state = jnp.where(ahead, gathered[source, 1] + gathered[source, 0] * state, state)
    return state


def norm_rows(values, scales):
    return values * lax.rsqrt(jnp.mean(values * values, axis=-1, keepdims=True) + epsilon) * scales


def gelu_parts(x):
    inner = jnp.tanh(GELU_C * (x + GELU_A * x * x * x))
    return 0.5 * x * (1.0 + inner), 0.5 * (1.0 + inner) + 0.5 * x * (1.0 - inner * inner) * (
        GELU_C * (1.0 + 3.0 * GELU_A * x * x)
    )


def mm(left, right, dims):
    return lax.dot_general(left, right, (dims, ((), ())), preferred_element_type=f32)


def sigmoid(x):
    return 1.0 / (1.0 + jnp.exp(-x))


def scan_rows(decay, value, reverse):
    rows = decay.shape[0]
    place = lax.broadcasted_iota(jnp.int32, decay.shape, 0)
    step = 1
    while step < rows:
        shift = rows - step if reverse else step
        inside = place < rows - step if reverse else place >= step
        before_value = jnp.where(inside, pltpu.roll(value, shift, 0), 0.0)
        before_decay = jnp.where(inside, pltpu.roll(decay, shift, 0), 1.0)
        value = value + decay * before_value
        decay = decay * before_decay
        step *= 2
    return decay, value


def gates(rate_pre, input_pre, soft):
    rate = sigmoid(rate_pre)
    log_decay = -8.0 * rate * soft
    decay = jnp.exp(log_decay)
    square = decay * decay
    root = jnp.sqrt(-jnp.tanh(log_decay) * (1.0 + square))
    return rate, decay, square, root, sigmoid(input_pre)


def mixer_forward(branch, prior, small, rate_w, input_w, conv, rate_pre, input_pre, cum, local, ext):
    rows = branch.shape[0]
    ext[0:8, :] = prior[...]
    ext[8:, :] = branch[...].astype(f32)
    total = small[CONV_BIAS : CONV_BIAS + 1, :] + small[TAP : TAP + 1, :] * ext[8:, :]
    for offset in range(1, 4):
        total = total + small[TAP + offset : TAP + offset + 1, :] * ext[pl.ds(8 - offset, rows), :]
    low = total.astype(bf16)
    conv[...] = low
    rate = mm(low, rate_w[...], ((1,), (0,))) + small[RATE_BIAS : RATE_BIAS + 1, :]
    inp = mm(low, input_w[...], ((1,), (0,))) + small[INPUT_BIAS : INPUT_BIAS + 1, :]
    rate_pre[...] = rate
    input_pre[...] = inp
    _, decay, _, root, opened = gates(rate, inp, small[SOFT : SOFT + 1, :])
    product, states = scan_rows(decay, root * opened * low.astype(f32), False)
    cum[...] = product
    local[...] = states


def mixer_backward_scan(grad_mixed, gelu_pre, rate_pre, cum, local, carried, small, grad_pre, rev_cum, rev_grad, pair, ext):
    rows = grad_mixed.shape[0]
    states = local[...] + cum[...] * carried[0:1, :]
    value, slope = gelu_parts(gelu_pre[...])
    grad = grad_mixed[...]
    grad_pre[...] = (grad * states * slope).astype(bf16)
    decay = jnp.exp(-8.0 * sigmoid(rate_pre[...]) * small[SOFT : SOFT + 1, :])
    ext[0:rows, :] = decay
    ext[rows:, :] = jnp.ones((8, decay.shape[1]), f32)
    product, back = scan_rows(ext[pl.ds(1, rows), :], grad * value, True)
    rev_cum[...] = product
    rev_grad[...] = back
    pair[...] = jnp.broadcast_to(decay[0:1, :] * back[0:1, :], pair.shape)


def mixer_backward(
    rev_cum, rev_grad, incoming, cum, local, carried, rate_pre, input_pre, conv, branch, prior, small, rate_w, input_w,
    own, head, rate_w_grad, input_w_grad, sums, ext, gext,
):
    rows = rev_cum.shape[0]
    soft = small[SOFT : SOFT + 1, :]
    grad_states = rev_grad[...] + rev_cum[...] * incoming[0:1, :]
    rate, decay, square, root, opened = gates(rate_pre[...], input_pre[...], soft)
    ext[0:8, :] = jnp.broadcast_to(carried[0:1, :], (8, carried.shape[1]))
    ext[8:, :] = local[...] + cum[...] * carried[0:1, :]
    before = ext[pl.ds(7, rows), :]
    low = conv[...]
    conv_in = low.astype(f32)
    grad_log = grad_states * decay * before - grad_states * opened * conv_in * square / root
    driven = grad_states * root
    grad_input = (driven * conv_in * opened * (1.0 - opened)).astype(bf16)
    by_rate = grad_log * (-8.0 * rate)
    grad_rate = (by_rate * soft * (1.0 - rate)).astype(bf16)
    sums[6:7, :] = jnp.sum(by_rate, axis=0, keepdims=True) * small[SOFT_SLOPE : SOFT_SLOPE + 1, :]
    sums[4:5, :] = jnp.sum(grad_rate.astype(f32), axis=0, keepdims=True)
    sums[5:6, :] = jnp.sum(grad_input.astype(f32), axis=0, keepdims=True)
    rate_w_grad[...] = mm(low, grad_rate, ((0,), (0,))).astype(rate_w_grad.dtype)
    input_w_grad[...] = mm(low, grad_input, ((0,), (0,))).astype(input_w_grad.dtype)
    grad_conv = (
        driven * opened
        + mm(grad_rate, rate_w[...], ((1,), (1,)))
        + mm(grad_input, input_w[...], ((1,), (1,)))
    )
    sums[7:8, :] = jnp.sum(grad_conv, axis=0, keepdims=True)
    ext[0:8, :] = prior[...]
    ext[8:, :] = branch[...].astype(f32)
    gext[0:8, :] = jnp.zeros((8, grad_conv.shape[1]), f32)
    gext[8 : 8 + rows, :] = grad_conv
    gext[8 + rows :, :] = jnp.zeros((8, grad_conv.shape[1]), f32)
    back = jnp.zeros_like(grad_conv)
    front = jnp.zeros((8, grad_conv.shape[1]), f32)
    for offset in range(4):
        tap = small[TAP + offset : TAP + offset + 1, :]
        sums[offset : offset + 1, :] = jnp.sum(
            grad_conv * ext[pl.ds(8 - offset, rows), :], axis=0, keepdims=True
        )
        back = back + tap * gext[pl.ds(8 + offset, rows), :]
        front = front + tap * gext[pl.ds(offset, 8), :]
    own[...] = back
    head[...] = front


def call_heads(kernel, width, heads, ins, outs, scratch, name):
    def spec(rows_cols):
        rows, by_row = rows_cols
        if by_row:
            return pl.BlockSpec((rows, width), lambda h: (h, 0))
        return pl.BlockSpec((rows, width), lambda h: (0, h))

    in_specs = [spec((width, True)) if rowwise else spec((a.shape[0], False)) for a, rowwise in ins]
    out_specs = [spec((width, True)) if rowwise else spec((rows, False)) for rows, _, rowwise in outs]
    out_shape = [
        jax.ShapeDtypeStruct((heads * width, width) if rowwise else (rows, heads * width), kind)
        for rows, kind, rowwise in outs
    ]
    return pl.pallas_call(
        kernel,
        grid=(heads,),
        in_specs=in_specs,
        out_specs=out_specs,
        out_shape=out_shape,
        scratch_shapes=[pltpu.VMEM((rows, width), f32) for rows in scratch],
        compiler_params=pltpu.CompilerParams(vmem_limit_bytes=40 * 1024 * 1024),
        name=name,
    )(*[a for a, _ in ins])


def on_device(
    block_input,
    cotangent,
    mixer_gain,
    branch_proj,
    gelu_proj,
    conv_taps,
    conv_bias,
    rate_blocks,
    input_blocks,
    rate_bias,
    input_bias,
    decay_param,
    out_proj,
    mlp_gain,
    gate_proj,
    up_proj,
    down_proj,
):
    groups = lax.axis_size("fsdp")
    part_rows, lru = branch_proj.shape
    width = rate_blocks.shape[1]
    heads = lru // width
    margin = conv_taps.shape[0] - 1
    tokens = block_input[0].astype(f32)
    tok_count, model = tokens.shape
    ff = gate_proj.shape[1]
    ff_part = ff // groups
    grad_out = cotangent[0]

    smalls = jnp.stack(
        [conv_taps[k] for k in range(margin + 1)]
        + [conv_bias, rate_bias, input_bias, decay_param, mixer_gain, mlp_gain],
        axis=1,
    )
    small_count = smalls.shape[1]
    smalls = jnp.pad(smalls, ((0, 0), (0, 128 - small_count)))
    first = lax.all_gather(
        jnp.concatenate([smalls, rate_blocks, input_blocks], axis=1), both, axis=0, tiled=True
    )
    wide = lax.all_gather(jnp.concatenate([branch_proj, gelu_proj], axis=1), both, axis=0, tiled=True)
    proj_out = lax.all_gather(out_proj, both, axis=0, tiled=True)

    def to_columns(weight):
        return jnp.transpose(weight.reshape(part_rows, groups, ff_part), (1, 0, 2))

    mlp_own = jnp.stack([to_columns(w) for w in (gate_proj, up_proj, down_proj)], axis=2)
    mlp_mine = lax.all_to_all(mlp_own, "fsdp", 0, 0, tiled=True)
    mlp_mine = mlp_mine.reshape(groups * part_rows, 3 * ff_part)
    mlp_w = lax.all_gather(mlp_mine, "seq", axis=0, tiled=True)
    grad_out_all = lax.all_gather(grad_out, "fsdp", axis=0, tiled=True)

    table = first[:, :small_count].astype(f32).T
    blocks_rate = first[:, 128 : 128 + width]
    blocks_input = first[:, 128 + width :]
    param_decay = table[margin + 4]
    gain_one = table[margin + 5]
    gain_two = table[margin + 6]
    small = jnp.concatenate(
        [
            table[: margin + 4],
            jax.nn.softplus(-param_decay)[None],
            -jax.nn.sigmoid(-param_decay)[None],
            jnp.zeros((16 - margin - 6, lru), f32),
        ],
        axis=0,
    )

    normed = norm_rows(tokens, gain_one).astype(bf16)
    both_pre = mm(normed, wide, ((1,), (0,)))
    branch = both_pre[:, :lru].astype(bf16)
    gelu_pre = both_pre[:, lru:]
    prior = from_behind(branch[tok_count - margin :], "seq", 1).astype(f32)
    prior = jnp.concatenate([jnp.zeros((8 - margin, lru), f32), prior], axis=0)
    conv, rate_pre, input_pre, cum, local = call_heads(
        mixer_forward,
        width,
        heads,
        [(branch, False), (prior, False), (small, False), (blocks_rate, True), (blocks_input, True)],
        [(tok_count, bf16, False)] + [(tok_count, f32, False)] * 4,
        [tok_count + 8],
        "mixer_forward",
    )
    carried = prefix((cum[-1], local[-1]), "seq", False)
    states = local + cum * carried[None]
    mixed = (states * jax.nn.gelu(gelu_pre, approximate=True)).astype(bf16)
    middle = tokens + mm(mixed, proj_out, ((1,), (1,)))
    normed_two = norm_rows(middle, gain_two).astype(bf16)

    normed_all = lax.all_gather(normed_two, "fsdp", axis=0, tiled=True)
    w_pair = mlp_w[:, : 2 * ff_part]
    w_down = mlp_w[:, 2 * ff_part :]
    pair = mm(normed_all, w_pair, ((1,), (0,)))
    gate = pair[:, :ff_part]
    up_val = pair[:, ff_part:]
    gelu_gate, gelu_slope = gelu_parts(gate)
    hidden = (gelu_gate * up_val).astype(bf16)
    grad_hidden = mm(grad_out_all, w_down, ((1,), (0,)))
    grad_gate = (grad_hidden * up_val * gelu_slope).astype(bf16)
    grad_up = (grad_hidden * gelu_gate).astype(bf16)
    grad_pair = jnp.concatenate([grad_gate, grad_up], axis=1)
    grad_normed_two = lax.psum_scatter(
        mm(grad_pair, w_pair, ((1,), (1,))).astype(bf16), "fsdp", scatter_dimension=0, tiled=True
    ).astype(f32)
    out_part = lax.psum_scatter(
        mm(hidden, w_down, ((1,), (1,))).astype(bf16), "fsdp", scatter_dimension=0, tiled=True
    )
    block_output = (middle + out_part.astype(f32)).astype(bf16)[None]
    term_pair = mm(normed_all, grad_pair, ((0,), (0,))).astype(bf16)
    term_down = mm(grad_out_all, hidden, ((0,), (0,))).astype(bf16)
    mlp_sum = lax.psum_scatter(
        jnp.concatenate([term_pair, term_down], axis=1), "seq", scatter_dimension=0, tiled=True
    )
    mlp_back = lax.all_to_all(
        mlp_sum.reshape(groups, part_rows, 3, ff_part), "fsdp", 0, 0, tiled=True
    )
    mlp_grads = [
        jnp.transpose(mlp_back[:, :, i], (1, 0, 2)).reshape(part_rows, ff).astype(f32) for i in range(3)
    ]

    second_pull = jax.vjp(norm_rows, middle, gain_two)[1]
    grad_mid_part, grad_gain_two = second_pull(grad_normed_two)
    grad_middle = grad_out.astype(f32) + grad_mid_part
    grad_mix = grad_middle.astype(bf16)
    grad_mixed = mm(grad_mix, proj_out, ((1,), (0,)))
    carried_rows = jnp.broadcast_to(carried[None], (8, lru))
    grad_gelu_pre, rev_cum, rev_grad, pair_grad = call_heads(
        mixer_backward_scan,
        width,
        heads,
        [(a, False) for a in (grad_mixed, gelu_pre, rate_pre, cum, local, carried_rows, small)],
        [(tok_count, bf16, False), (tok_count, f32, False), (tok_count, f32, False), (8, f32, False)],
        [tok_count + 8],
        "mixer_backward_scan",
    )
    incoming = prefix((cum[-1], pair_grad[0]), "seq", True)
    incoming_rows = jnp.broadcast_to(incoming[None], (8, lru))
    own, head, rate_w_grad, input_w_grad, sums = call_heads(
        mixer_backward,
        width,
        heads,
        [
            (a, False)
            for a in (rev_cum, rev_grad, incoming_rows, cum, local, carried_rows, rate_pre, input_pre, conv, branch, prior, small)
        ]
        + [(blocks_rate, True), (blocks_input, True)],
        [(tok_count, f32, False), (8, f32, False), (0, bf16, True), (0, bf16, True), (8, f32, False)],
        [tok_count + 8, tok_count + 16],
        "mixer_backward",
    )
    received = from_behind(head[8 - margin :], "seq", -1)
    grad_branch = jnp.concatenate(
        [own[: tok_count - margin], own[tok_count - margin :] + received], axis=0
    ).astype(bf16)
    grad_both = jnp.concatenate([grad_branch, grad_gelu_pre], axis=1)
    grad_normed = mm(grad_both, wide, ((1,), (1,)))
    first_pull = jax.vjp(norm_rows, tokens, gain_one)[1]
    grad_tok_part, grad_gain_one = first_pull(grad_normed)
    input_grad = (grad_middle + grad_tok_part).astype(bf16)[None]
    term_wide = mm(normed, grad_both, ((0,), (0,))).astype(bf16)
    term_out = mm(grad_mix, mixed, ((0,), (0,))).astype(bf16)
    vectors = jnp.concatenate([sums, grad_gain_one[None], grad_gain_two[None]], axis=0).T
    vectors = jnp.pad(vectors, ((0, 0), (0, 128 - vectors.shape[1]))).astype(bf16)
    mixer_sum = lax.psum_scatter(
        jnp.concatenate([term_wide, term_out, rate_w_grad, input_w_grad, vectors], axis=1),
        "seq",
        scatter_dimension=0,
        tiled=True,
    )
    mixer_sum = lax.psum_scatter(mixer_sum, "fsdp", scatter_dimension=0, tiled=True).astype(f32)
    edges = [lru, 2 * lru, 3 * lru, 3 * lru + width, 3 * lru + 2 * width]
    dbranch, dgelu, dout, drate, dinput, vec = jnp.split(mixer_sum, edges, axis=1)
    vec = vec.T
    return (
        block_output,
        input_grad,
        vec[8],
        dbranch,
        dgelu,
        vec[: margin + 1],
        vec[7],
        drate,
        dinput,
        vec[4],
        vec[5],
        vec[6],
        dout,
        vec[9],
        mlp_grads[0],
        mlp_grads[1],
        mlp_grads[2],
    )


def solution(mesh):
    tokens = P("fsdp", "seq", None)
    vector = P(both)
    matrix = P(both, None)
    taps = P(None, both)
    return jax.shard_map(
        on_device,
        mesh=mesh,
        in_specs=(
            tokens, tokens, vector, matrix, matrix, taps, vector, matrix, matrix,
            vector, vector, vector, matrix, vector, matrix, matrix, matrix,
        ),
        out_specs=(
            tokens, tokens, vector, matrix, matrix, taps, vector, matrix, matrix,
            vector, vector, vector, matrix, vector, matrix, matrix, matrix,
        ),
        check_vma=False,
    )
```

```python
import functools

import jax
import jax.numpy as jnp
from jax import lax
from jax.experimental import pallas as pl
from jax.experimental.pallas import tpu as pltpu
from jax.sharding import PartitionSpec as P

epsilon = 1e-06
f32 = jnp.float32
bf16 = jnp.bfloat16
both = ("seq", "fsdp")
MESH = pl.DeviceIdType.MESH
TAP, CONV_BIAS, RATE_BIAS, INPUT_BIAS, SOFT, SOFT_SLOPE = 0, 4, 5, 6, 7, 8
GELU_C = 0.7978845608028654
GELU_A = 0.044715


def from_behind(shard, axis, by):
    devices = lax.axis_size(axis)
    pairs = [(i, i + by) for i in range(devices) if 0 <= i + by < devices]
    return lax.ppermute(shard, axis, pairs)


def prefix(part, axis, reverse):
    count = lax.axis_size(axis)
    place = lax.axis_index(axis)
    gathered = lax.all_gather(jnp.stack(part), axis)
    state = jnp.zeros_like(part[1])
    for hop in range(count):
        source = count - 1 - hop if reverse else hop
        ahead = source > place if reverse else source < place
        state = jnp.where(ahead, gathered[source, 1] + gathered[source, 0] * state, state)
    return state


def norm_rows(values, scales):
    return values * lax.rsqrt(jnp.mean(values * values, axis=-1, keepdims=True) + epsilon) * scales


def gelu_parts(x):
    inner = jnp.tanh(GELU_C * (x + GELU_A * x * x * x))
    return 0.5 * x * (1.0 + inner), 0.5 * (1.0 + inner) + 0.5 * x * (1.0 - inner * inner) * (
        GELU_C * (1.0 + 3.0 * GELU_A * x * x)
    )


def mm(left, right, dims):
    return lax.dot_general(left, right, (dims, ((), ())), preferred_element_type=f32)


def sigmoid(x):
    return 1.0 / (1.0 + jnp.exp(-x))


def scan_rows(decay, value, reverse):
    rows = decay.shape[0]
    place = lax.broadcasted_iota(jnp.int32, decay.shape, 0)
    step = 1
    while step < rows:
        shift = rows - step if reverse else step
        inside = place < rows - step if reverse else place >= step
        before_value = jnp.where(inside, pltpu.roll(value, shift, 0), 0.0)
        before_decay = jnp.where(inside, pltpu.roll(decay, shift, 0), 1.0)
        value = value + decay * before_value
        decay = decay * before_decay
        step *= 2
    return decay, value


def gates(rate_pre, input_pre, soft):
    rate = sigmoid(rate_pre)
    log_decay = -8.0 * rate * soft
    decay = jnp.exp(log_decay)
    square = decay * decay
    root = jnp.sqrt(-jnp.tanh(log_decay) * (1.0 + square))
    return rate, decay, square, root, sigmoid(input_pre)


def mixer_forward(branch, prior, small, rate_w, input_w, conv, rate_pre, input_pre, cum, local, ext):
    rows = branch.shape[0]
    ext[0:8, :] = prior[...]
    ext[8:, :] = branch[...].astype(f32)
    total = small[CONV_BIAS : CONV_BIAS + 1, :] + small[TAP : TAP + 1, :] * ext[8:, :]
    for offset in range(1, 4):
        total = total + small[TAP + offset : TAP + offset + 1, :] * ext[pl.ds(8 - offset, rows), :]
    low = total.astype(bf16)
    conv[...] = low
    rate = mm(low, rate_w[...], ((1,), (0,))) + small[RATE_BIAS : RATE_BIAS + 1, :]
    inp = mm(low, input_w[...], ((1,), (0,))) + small[INPUT_BIAS : INPUT_BIAS + 1, :]
    rate_pre[...] = rate
    input_pre[...] = inp
    _, decay, _, root, opened = gates(rate, inp, small[SOFT : SOFT + 1, :])
    product, states = scan_rows(decay, root * opened * low.astype(f32), False)
    cum[...] = product
    local[...] = states


def mixer_backward_scan(grad_mixed, gelu_pre, rate_pre, cum, local, carried, small, grad_pre, rev_cum, rev_grad, pair, ext):
    rows = grad_mixed.shape[0]
    states = local[...] + cum[...] * carried[0:1, :]
    value, slope = gelu_parts(gelu_pre[...])
    grad = grad_mixed[...]
    grad_pre[...] = (grad * states * slope).astype(bf16)
    decay = jnp.exp(-8.0 * sigmoid(rate_pre[...]) * small[SOFT : SOFT + 1, :])
    ext[0:rows, :] = decay
    ext[rows:, :] = jnp.ones((8, decay.shape[1]), f32)
    product, back = scan_rows(ext[pl.ds(1, rows), :], grad * value, True)
    rev_cum[...] = product
    rev_grad[...] = back
    pair[...] = jnp.broadcast_to(decay[0:1, :] * back[0:1, :], pair.shape)


def mixer_backward(
    rev_cum, rev_grad, incoming, cum, local, carried, rate_pre, input_pre, conv, branch, prior, small, rate_w, input_w,
    own, head, rate_w_grad, input_w_grad, sums, ext, gext,
):
    rows = rev_cum.shape[0]
    soft = small[SOFT : SOFT + 1, :]
    grad_states = rev_grad[...] + rev_cum[...] * incoming[0:1, :]
    rate, decay, square, root, opened = gates(rate_pre[...], input_pre[...], soft)
    ext[0:8, :] = jnp.broadcast_to(carried[0:1, :], (8, carried.shape[1]))
    ext[8:, :] = local[...] + cum[...] * carried[0:1, :]
    before = ext[pl.ds(7, rows), :]
    low = conv[...]
    conv_in = low.astype(f32)
    grad_log = grad_states * decay * before - grad_states * opened * conv_in * square / root
    driven = grad_states * root
    grad_input = (driven * conv_in * opened * (1.0 - opened)).astype(bf16)
    by_rate = grad_log * (-8.0 * rate)
    grad_rate = (by_rate * soft * (1.0 - rate)).astype(bf16)
    sums[6:7, :] = jnp.sum(by_rate, axis=0, keepdims=True) * small[SOFT_SLOPE : SOFT_SLOPE + 1, :]
    sums[4:5, :] = jnp.sum(grad_rate.astype(f32), axis=0, keepdims=True)
    sums[5:6, :] = jnp.sum(grad_input.astype(f32), axis=0, keepdims=True)
    rate_w_grad[...] = mm(low, grad_rate, ((0,), (0,))).astype(rate_w_grad.dtype)
    input_w_grad[...] = mm(low, grad_input, ((0,), (0,))).astype(input_w_grad.dtype)
    grad_conv = (
        driven * opened
        + mm(grad_rate, rate_w[...], ((1,), (1,)))
        + mm(grad_input, input_w[...], ((1,), (1,)))
    )
    sums[7:8, :] = jnp.sum(grad_conv, axis=0, keepdims=True)
    ext[0:8, :] = prior[...]
    ext[8:, :] = branch[...].astype(f32)
    gext[0:8, :] = jnp.zeros((8, grad_conv.shape[1]), f32)
    gext[8 : 8 + rows, :] = grad_conv
    gext[8 + rows :, :] = jnp.zeros((8, grad_conv.shape[1]), f32)
    back = jnp.zeros_like(grad_conv)
    front = jnp.zeros((8, grad_conv.shape[1]), f32)
    for offset in range(4):
        tap = small[TAP + offset : TAP + offset + 1, :]
        sums[offset : offset + 1, :] = jnp.sum(
            grad_conv * ext[pl.ds(8 - offset, rows), :], axis=0, keepdims=True
        )
        back = back + tap * gext[pl.ds(8 + offset, rows), :]
        front = front + tap * gext[pl.ds(offset, 8), :]
    own[...] = back
    head[...] = front


def places():
    s = lax.axis_index("seq")
    z = lax.axis_index("fsdp")
    core = s + 1 - 2 * (s % 2)
    beside = s + 2 - 4 * ((s // 2) % 2)
    across = s + 4 - 8 * (s // 4)
    return s, z, core, beside, across


def greet(peers):
    barrier = pltpu.get_barrier_semaphore()
    for peer in peers:
        pl.semaphore_signal(barrier, inc=1, device_id=peer, device_id_type=MESH)
    pl.semaphore_wait(barrier, len(peers))


def gather_kernel(
    mixer, gate, up, down, grad, mixer_all, mlp_all, grad_all,
    flow_send, flow_recv, line_send, line_recv, swap_send, swap_recv, own_sem,
):
    s, z, core, beside, across = places()
    rows = mixer.shape[0]
    mixer_cols = mixer.shape[1]
    ff_part = mlp_all.shape[2]
    tok = grad.shape[0]
    mixer_cut = mixer_cols // 256 * 128
    mlp_cut = ff_part // 256 * 128
    diag = beside + across - s
    greet([(core, z), (beside, z), (across, z)] + [(s, (z + k) % 4) for k in range(1, 4)])

    def remote(src, dst, send, recv, target):
        return pltpu.make_async_remote_copy(
            src_ref=src, dst_ref=dst, send_sem=send, recv_sem=recv, device_id=target, device_id_type=MESH
        )

    def span(seq, zz):
        return pl.ds(pl.multiple_of((seq * 4 + zz) * rows, 16), rows)

    def piece(kind, seq, zz, half=None):
        if kind == 0:
            if half is None:
                return mixer_all.at[span(seq, zz), :]
            cols = pl.ds(0, mixer_cut) if half == 0 else pl.ds(mixer_cut, mixer_cols - mixer_cut)
            return mixer_all.at[span(seq, zz), cols]
        if half is None:
            return mlp_all.at[:, span(seq, zz), :]
        cols = pl.ds(0, mlp_cut) if half == 0 else pl.ds(mlp_cut, ff_part - mlp_cut)
        return mlp_all.at[:, span(seq, zz), cols]

    def flow(kind, zz, index, seq, half, target, src=None):
        ref = piece(kind, seq, zz, half)
        return remote(
            ref if src is None else src, ref, flow_send.at[kind, zz, index], flow_recv.at[kind, zz, index], (target, z)
        )

    def sends(kind, zz, src=None):
        return [
            flow(kind, zz, 0, s, None, beside, src),
            flow(kind, zz, 1, s, None, across, src),
            flow(kind, zz, 4, s, None, core, src),
        ]

    def spread(kind, zz, src=None):
        for copy in sends(kind, zz, src):
            copy.start()

    def relay(kind, zz):
        flow(kind, zz, 0, beside, None, beside).wait_recv()
        flow(kind, zz, 3, beside, 0, across).start()
        flow(kind, zz, 5, beside, None, core).start()
        flow(kind, zz, 1, across, None, across).wait_recv()
        flow(kind, zz, 2, across, 1, beside).start()
        flow(kind, zz, 6, across, None, core).start()

    def finish(kind, zz):
        flow(kind, zz, 3, diag, 0, across).wait_recv()
        flow(kind, zz, 7, diag, 0, core).start()
        flow(kind, zz, 2, diag, 1, beside).wait_recv()
        flow(kind, zz, 8, diag, 1, core).start()

    def drain(kind, zz, src=None):
        other = core
        for copy in sends(kind, zz, src):
            copy.wait_send()
        flow(kind, zz, 3, beside, 0, across).wait_send()
        flow(kind, zz, 5, beside, None, core).wait_send()
        flow(kind, zz, 2, across, 1, beside).wait_send()
        flow(kind, zz, 6, across, None, core).wait_send()
        flow(kind, zz, 7, diag, 0, core).wait_send()
        flow(kind, zz, 8, diag, 1, core).wait_send()
        flip = core - s
        flow(kind, zz, 4, other, None, core).wait_recv()
        flow(kind, zz, 5, beside + flip, None, core).wait_recv()
        flow(kind, zz, 6, across + flip, None, core).wait_recv()
        flow(kind, zz, 7, diag + flip, 0, core).wait_recv()
        flow(kind, zz, 8, diag + flip, 1, core).wait_recv()

    def line(kind, zz, up_way, hop, src=None):
        if kind == 0:
            ref = mixer_all.at[span(s, zz), :]
        else:
            ref = grad_all.at[pl.ds(pl.multiple_of(zz * tok, 16), tok), :]
        way = 0 if up_way else 1
        target = z + 1 if up_way else z - 1
        return remote(
            ref if src is None else src, ref, line_send.at[kind, way, hop], line_recv.at[kind, way, hop], (s, target)
        )

    def line_start(kind, src):
        pl.when(z < 3)(lambda: line(kind, z, True, 0, src).start())
        pl.when(z > 0)(lambda: line(kind, z, False, 0, src).start())

    def line_hop(kind, hop):
        def below():
            line(kind, z - hop, True, hop - 1).wait_recv()

            @pl.when(z < 3)
            def _():
                line(kind, z - hop, True, hop).start()

        def above():
            line(kind, z + hop, False, hop - 1).wait_recv()

            @pl.when(z > 0)
            def _():
                line(kind, z + hop, False, hop).start()

        pl.when(z >= hop)(below)
        pl.when(z + hop <= 3)(above)

    def line_drain(kind, src):
        pl.when(z < 3)(lambda: line(kind, z, True, 0, src).wait_send())
        pl.when(z > 0)(lambda: line(kind, z, False, 0, src).wait_send())
        for hop in range(1, 3):
            pl.when((z >= hop) & (z < 3))(lambda: line(kind, z - hop, True, hop).wait_send())
            pl.when((z + hop <= 3) & (z > 0))(lambda: line(kind, z + hop, False, hop).wait_send())

    def at_hop(hop, act):
        pl.when(z >= hop)(lambda: act(z - hop))
        pl.when(z + hop <= 3)(lambda: act(z + hop))

    def swap(k, m, arriving=False):
        weight = (gate, up, down)[m]
        to = (z + k) % 4
        came = (z + 4 - k) % 4
        cols = pl.ds(pl.multiple_of(to * ff_part, 128), ff_part)
        dst = mlp_all.at[m, span(s, came if arriving else z), :]
        return remote(weight.at[:, cols], dst, swap_send.at[k - 1, m], swap_recv.at[k - 1, m], (s, to))

    own_cols = pl.ds(pl.multiple_of(z * ff_part, 128), ff_part)
    local = [
        pltpu.make_async_copy(weight.at[:, own_cols], mlp_all.at[m, span(s, z), :], own_sem.at[m])
        for m, weight in enumerate((gate, up, down))
    ]
    local.append(pltpu.make_async_copy(mixer, mixer_all.at[span(s, z), :], own_sem.at[3]))
    local.append(
        pltpu.make_async_copy(grad, grad_all.at[pl.ds(pl.multiple_of(z * tok, 16), tok), :], own_sem.at[4])
    )

    line_start(0, mixer)
    spread(0, z, mixer)
    for copy in local:
        copy.start()
    line_hop(0, 1)
    at_hop(1, lambda zz: spread(0, zz))
    relay(0, z)
    line_hop(0, 2)
    at_hop(2, lambda zz: spread(0, zz))
    finish(0, z)
    at_hop(1, lambda zz: relay(0, zz))
    line_hop(0, 3)
    at_hop(3, lambda zz: spread(0, zz))
    for k in (1, 3, 2):
        for m in range(3):
            swap(k, m).start()
    for copy in local:
        copy.wait()
    spread(1, z)
    at_hop(1, lambda zz: finish(0, zz))
    at_hop(2, lambda zz: relay(0, zz))
    at_hop(3, lambda zz: relay(0, zz))
    relay(1, z)
    at_hop(2, lambda zz: finish(0, zz))
    at_hop(3, lambda zz: finish(0, zz))
    for k in (1, 3, 2):
        for m in range(3):
            swap(k, m, True).wait_recv()
        spread(1, (z + 4 - k) % 4)
    line_start(1, grad)
    finish(1, z)
    line_hop(1, 1)
    relay(1, (z + 3) % 4)
    line_hop(1, 2)
    relay(1, (z + 1) % 4)
    finish(1, (z + 3) % 4)
    line_hop(1, 3)
    relay(1, (z + 2) % 4)
    finish(1, (z + 1) % 4)
    finish(1, (z + 2) % 4)
    drain(0, z, mixer)
    for hop in range(1, 4):
        at_hop(hop, lambda zz: drain(0, zz))
    drain(1, z)
    for k in (1, 3, 2):
        drain(1, (z + 4 - k) % 4)
        for m in range(3):
            swap(k, m).wait_send()
    line_drain(0, mixer)
    line_drain(1, grad)


def gather(mixer, gate, up, down, grad):
    rows, cols = mixer.shape
    tok, model = grad.shape
    ff_part = gate.shape[1] // 4
    anyspec = pl.BlockSpec(memory_space=pl.ANY)
    dma = pltpu.SemaphoreType.DMA
    return pl.pallas_call(
        gather_kernel,
        in_specs=[anyspec] * 5,
        out_specs=[anyspec] * 3,
        out_shape=[
            jax.ShapeDtypeStruct((32 * rows, cols), bf16),
            jax.ShapeDtypeStruct((3, 32 * rows, ff_part), bf16),
            jax.ShapeDtypeStruct((4 * tok, model), bf16),
        ],
        scratch_shapes=[
            dma((2, 4, 9)), dma((2, 4, 9)), dma((2, 2, 3)), dma((2, 2, 3)), dma((3, 3)), dma((3, 3)), dma((5,)),
        ],
        compiler_params=pltpu.CompilerParams(collective_id=1, has_side_effects=True),
        name="gather_weights",
    )(mixer, gate, up, down, grad)


def gather_plain(mixer, gate, up, down, grad):
    groups = lax.axis_size("fsdp")
    part_rows, ff = gate.shape

    def columns(weight):
        return jnp.transpose(weight.reshape(part_rows, groups, ff // groups), (1, 0, 2))

    own = jnp.stack([columns(w) for w in (gate, up, down)], axis=1)
    mine = lax.all_to_all(own, "fsdp", 0, 0, tiled=True)
    mine = jnp.transpose(mine, (1, 0, 2, 3)).reshape(3, groups * part_rows, ff // groups)
    return (
        lax.all_gather(mixer, both, axis=0, tiled=True),
        lax.all_gather(mine, "seq", axis=1, tiled=True),
        lax.all_gather(grad, "fsdp", axis=0, tiled=True),
    )


def call_heads(kernel, width, heads, ins, outs, scratch, name):
    def spec(rows_cols):
        rows, by_row = rows_cols
        if by_row:
            return pl.BlockSpec((rows, width), lambda h: (h, 0))
        return pl.BlockSpec((rows, width), lambda h: (0, h))

    in_specs = [spec((width, True)) if rowwise else spec((a.shape[0], False)) for a, rowwise in ins]
    out_specs = [spec((width, True)) if rowwise else spec((rows, False)) for rows, _, rowwise in outs]
    out_shape = [
        jax.ShapeDtypeStruct((heads * width, width) if rowwise else (rows, heads * width), kind)
        for rows, kind, rowwise in outs
    ]
    return pl.pallas_call(
        kernel,
        grid=(heads,),
        in_specs=in_specs,
        out_specs=out_specs,
        out_shape=out_shape,
        scratch_shapes=[pltpu.VMEM((rows, width), f32) for rows in scratch],
        compiler_params=pltpu.CompilerParams(vmem_limit_bytes=40 * 1024 * 1024),
        name=name,
    )(*[a for a, _ in ins])


def on_device(
    block_input,
    cotangent,
    mixer_gain,
    branch_proj,
    gelu_proj,
    conv_taps,
    conv_bias,
    rate_blocks,
    input_blocks,
    rate_bias,
    input_bias,
    decay_param,
    out_proj,
    mlp_gain,
    gate_proj,
    up_proj,
    down_proj,
):
    groups = lax.axis_size("fsdp")
    part_rows, lru = branch_proj.shape
    width = rate_blocks.shape[1]
    heads = lru // width
    margin = conv_taps.shape[0] - 1
    tokens = block_input[0].astype(f32)
    tok_count, model = tokens.shape
    ff = gate_proj.shape[1]
    ff_part = ff // groups
    grad_out = cotangent[0]

    smalls = jnp.stack(
        [conv_taps[k] for k in range(margin + 1)]
        + [conv_bias, rate_bias, input_bias, decay_param, mixer_gain, mlp_gain],
        axis=1,
    )
    small_count = smalls.shape[1]
    smalls = jnp.pad(smalls, ((0, 0), (0, 128 - small_count)))
    mixer_own = jnp.concatenate(
        [smalls, rate_blocks, input_blocks, branch_proj, gelu_proj, out_proj], axis=1
    )
    if lax.axis_size("seq") == 8 and groups == 4:
        mixer_w, mlp_w, grad_out_all = gather(mixer_own, gate_proj, up_proj, down_proj, grad_out)
    else:
        mixer_w, mlp_w, grad_out_all = gather_plain(mixer_own, gate_proj, up_proj, down_proj, grad_out)
    first = mixer_w[:, : 128 + 2 * width]
    wide = mixer_w[:, 128 + 2 * width : 128 + 2 * width + 2 * lru]
    proj_out = mixer_w[:, 128 + 2 * width + 2 * lru :]

    table = first[:, :small_count].astype(f32).T
    blocks_rate = first[:, 128 : 128 + width]
    blocks_input = first[:, 128 + width :]
    param_decay = table[margin + 4]
    gain_one = table[margin + 5]
    gain_two = table[margin + 6]
    small = jnp.concatenate(
        [
            table[: margin + 4],
            jax.nn.softplus(-param_decay)[None],
            -jax.nn.sigmoid(-param_decay)[None],
            jnp.zeros((16 - margin - 6, lru), f32),
        ],
        axis=0,
    )

    normed = norm_rows(tokens, gain_one).astype(bf16)
    both_pre = mm(normed, wide, ((1,), (0,)))
    branch = both_pre[:, :lru].astype(bf16)
    gelu_pre = both_pre[:, lru:]
    prior = from_behind(branch[tok_count - margin :], "seq", 1).astype(f32)
    prior = jnp.concatenate([jnp.zeros((8 - margin, lru), f32), prior], axis=0)
    conv, rate_pre, input_pre, cum, local = call_heads(
        mixer_forward,
        width,
        heads,
        [(branch, False), (prior, False), (small, False), (blocks_rate, True), (blocks_input, True)],
        [(tok_count, bf16, False)] + [(tok_count, f32, False)] * 4,
        [tok_count + 8],
        "mixer_forward",
    )
    carried = prefix((cum[-1], local[-1]), "seq", False)
    states = local + cum * carried[None]
    mixed = (states * jax.nn.gelu(gelu_pre, approximate=True)).astype(bf16)
    middle = tokens + mm(mixed, proj_out, ((1,), (1,)))
    normed_two = norm_rows(middle, gain_two).astype(bf16)

    normed_all = lax.all_gather(normed_two, "fsdp", axis=0, tiled=True)
    w_gate, w_up, w_down = mlp_w[0], mlp_w[1], mlp_w[2]
    gate = mm(normed_all, w_gate, ((1,), (0,)))
    up_val = mm(normed_all, w_up, ((1,), (0,)))
    gelu_gate, gelu_slope = gelu_parts(gate)
    hidden = (gelu_gate * up_val).astype(bf16)
    grad_hidden = mm(grad_out_all, w_down, ((1,), (0,)))
    grad_gate = (grad_hidden * up_val * gelu_slope).astype(bf16)
    grad_up = (grad_hidden * gelu_gate).astype(bf16)
    grad_pair = jnp.concatenate([grad_gate, grad_up], axis=1)
    grad_normed_part = mm(grad_gate, w_gate, ((1,), (1,))) + mm(grad_up, w_up, ((1,), (1,)))
    grad_normed_two = lax.psum_scatter(
        grad_normed_part.astype(bf16), "fsdp", scatter_dimension=0, tiled=True
    ).astype(f32)
    out_part = lax.psum_scatter(
        mm(hidden, w_down, ((1,), (1,))).astype(bf16), "fsdp", scatter_dimension=0, tiled=True
    )
    block_output = (middle + out_part.astype(f32)).astype(bf16)[None]
    term_pair = mm(normed_all, grad_pair, ((0,), (0,))).astype(bf16)
    term_down = mm(grad_out_all, hidden, ((0,), (0,))).astype(bf16)
    mlp_sum = lax.psum_scatter(
        jnp.concatenate([term_pair, term_down], axis=1), "seq", scatter_dimension=0, tiled=True
    )
    mlp_back = lax.all_to_all(
        mlp_sum.reshape(groups, part_rows, 3, ff_part), "fsdp", 0, 0, tiled=True
    )
    mlp_grads = [
        jnp.transpose(mlp_back[:, :, i], (1, 0, 2)).reshape(part_rows, ff).astype(f32) for i in range(3)
    ]

    second_pull = jax.vjp(norm_rows, middle, gain_two)[1]
    grad_mid_part, grad_gain_two = second_pull(grad_normed_two)
    grad_middle = grad_out.astype(f32) + grad_mid_part
    grad_mix = grad_middle.astype(bf16)
    grad_mixed = mm(grad_mix, proj_out, ((1,), (0,)))
    carried_rows = jnp.broadcast_to(carried[None], (8, lru))
    grad_gelu_pre, rev_cum, rev_grad, pair_grad = call_heads(
        mixer_backward_scan,
        width,
        heads,
        [(a, False) for a in (grad_mixed, gelu_pre, rate_pre, cum, local, carried_rows, small)],
        [(tok_count, bf16, False), (tok_count, f32, False), (tok_count, f32, False), (8, f32, False)],
        [tok_count + 8],
        "mixer_backward_scan",
    )
    incoming = prefix((cum[-1], pair_grad[0]), "seq", True)
    incoming_rows = jnp.broadcast_to(incoming[None], (8, lru))
    own, head, rate_w_grad, input_w_grad, sums = call_heads(
        mixer_backward,
        width,
        heads,
        [
            (a, False)
            for a in (rev_cum, rev_grad, incoming_rows, cum, local, carried_rows, rate_pre, input_pre, conv, branch, prior, small)
        ]
        + [(blocks_rate, True), (blocks_input, True)],
        [(tok_count, f32, False), (8, f32, False), (0, bf16, True), (0, bf16, True), (8, f32, False)],
        [tok_count + 8, tok_count + 16],
        "mixer_backward",
    )
    received = from_behind(head[8 - margin :], "seq", -1)
    grad_branch = jnp.concatenate(
        [own[: tok_count - margin], own[tok_count - margin :] + received], axis=0
    ).astype(bf16)
    grad_both = jnp.concatenate([grad_branch, grad_gelu_pre], axis=1)
    grad_normed = mm(grad_both, wide, ((1,), (1,)))
    first_pull = jax.vjp(norm_rows, tokens, gain_one)[1]
    grad_tok_part, grad_gain_one = first_pull(grad_normed)
    input_grad = (grad_middle + grad_tok_part).astype(bf16)[None]
    term_wide = mm(normed, grad_both, ((0,), (0,))).astype(bf16)
    term_out = mm(grad_mix, mixed, ((0,), (0,))).astype(bf16)
    vectors = jnp.concatenate([sums, grad_gain_one[None], grad_gain_two[None]], axis=0).T
    vectors = jnp.pad(vectors, ((0, 0), (0, 128 - vectors.shape[1]))).astype(bf16)
    mixer_sum = lax.psum_scatter(
        jnp.concatenate([term_wide, term_out, rate_w_grad, input_w_grad, vectors], axis=1),
        "seq",
        scatter_dimension=0,
        tiled=True,
    )
    mixer_sum = lax.psum_scatter(mixer_sum, "fsdp", scatter_dimension=0, tiled=True).astype(f32)
    edges = [lru, 2 * lru, 3 * lru, 3 * lru + width, 3 * lru + 2 * width]
    dbranch, dgelu, dout, drate, dinput, vec = jnp.split(mixer_sum, edges, axis=1)
    vec = vec.T
    return (
        block_output,
        input_grad,
        vec[8],
        dbranch,
        dgelu,
        vec[: margin + 1],
        vec[7],
        drate,
        dinput,
        vec[4],
        vec[5],
        vec[6],
        dout,
        vec[9],
        mlp_grads[0],
        mlp_grads[1],
        mlp_grads[2],
    )


def solution(mesh):
    tokens = P("fsdp", "seq", None)
    vector = P(both)
    matrix = P(both, None)
    taps = P(None, both)
    return jax.shard_map(
        on_device,
        mesh=mesh,
        in_specs=(
            tokens, tokens, vector, matrix, matrix, taps, vector, matrix, matrix,
            vector, vector, vector, matrix, vector, matrix, matrix, matrix,
        ),
        out_specs=(
            tokens, tokens, vector, matrix, matrix, taps, vector, matrix, matrix,
            vector, vector, vector, matrix, vector, matrix, matrix, matrix,
        ),
        check_vma=False,
    )
```

```python
import functools

import jax
import jax.numpy as jnp
from jax import lax
from jax.experimental import pallas as pl
from jax.experimental.pallas import tpu as pltpu
from jax.sharding import PartitionSpec as P

epsilon = 1e-06
f32 = jnp.float32
bf16 = jnp.bfloat16
both = ("seq", "fsdp")
MESH = pl.DeviceIdType.MESH
TAP, CONV_BIAS, RATE_BIAS, INPUT_BIAS, SOFT, SOFT_SLOPE = 0, 4, 5, 6, 7, 8
GELU_C = 0.7978845608028654
GELU_A = 0.044715


def from_behind(shard, axis, by):
    devices = lax.axis_size(axis)
    pairs = [(i, i + by) for i in range(devices) if 0 <= i + by < devices]
    return lax.ppermute(shard, axis, pairs)


def prefix(part, axis, reverse):
    count = lax.axis_size(axis)
    place = lax.axis_index(axis)
    gathered = lax.all_gather(jnp.stack(part), axis)
    state = jnp.zeros_like(part[1])
    for hop in range(count):
        source = count - 1 - hop if reverse else hop
        ahead = source > place if reverse else source < place
        state = jnp.where(ahead, gathered[source, 1] + gathered[source, 0] * state, state)
    return state


def norm_rows(values, scales):
    return values * lax.rsqrt(jnp.mean(values * values, axis=-1, keepdims=True) + epsilon) * scales


def gelu_parts(x):
    inner = jnp.tanh(GELU_C * (x + GELU_A * x * x * x))
    return 0.5 * x * (1.0 + inner), 0.5 * (1.0 + inner) + 0.5 * x * (1.0 - inner * inner) * (
        GELU_C * (1.0 + 3.0 * GELU_A * x * x)
    )


def mm(left, right, dims):
    return lax.dot_general(left, right, (dims, ((), ())), preferred_element_type=f32)


def sigmoid(x):
    return 1.0 / (1.0 + jnp.exp(-x))


def scan_rows(decay, value, reverse):
    rows = decay.shape[0]
    place = lax.broadcasted_iota(jnp.int32, decay.shape, 0)
    step = 1
    while step < rows:
        shift = rows - step if reverse else step
        inside = place < rows - step if reverse else place >= step
        before_value = jnp.where(inside, pltpu.roll(value, shift, 0), 0.0)
        before_decay = jnp.where(inside, pltpu.roll(decay, shift, 0), 1.0)
        value = value + decay * before_value
        decay = decay * before_decay
        step *= 2
    return decay, value


def gates(rate_pre, input_pre, soft):
    rate = sigmoid(rate_pre)
    log_decay = -8.0 * rate * soft
    decay = jnp.exp(log_decay)
    square = decay * decay
    root = jnp.sqrt(-jnp.tanh(log_decay) * (1.0 + square))
    return rate, decay, square, root, sigmoid(input_pre)


def mixer_forward(branch, prior, small, rate_w, input_w, conv, rate_pre, input_pre, cum, local, ext):
    rows = branch.shape[0]
    ext[0:8, :] = prior[...]
    ext[8:, :] = branch[...].astype(f32)
    total = small[CONV_BIAS : CONV_BIAS + 1, :] + small[TAP : TAP + 1, :] * ext[8:, :]
    for offset in range(1, 4):
        total = total + small[TAP + offset : TAP + offset + 1, :] * ext[pl.ds(8 - offset, rows), :]
    low = total.astype(bf16)
    conv[...] = low
    rate = mm(low, rate_w[...], ((1,), (0,))) + small[RATE_BIAS : RATE_BIAS + 1, :]
    inp = mm(low, input_w[...], ((1,), (0,))) + small[INPUT_BIAS : INPUT_BIAS + 1, :]
    rate_pre[...] = rate
    input_pre[...] = inp
    _, decay, _, root, opened = gates(rate, inp, small[SOFT : SOFT + 1, :])
    product, states = scan_rows(decay, root * opened * low.astype(f32), False)
    cum[...] = product
    local[...] = states


def mixer_backward_scan(grad_mixed, gelu_pre, rate_pre, cum, local, carried, small, grad_pre, rev_cum, rev_grad, pair, ext):
    rows = grad_mixed.shape[0]
    states = local[...] + cum[...] * carried[0:1, :]
    value, slope = gelu_parts(gelu_pre[...])
    grad = grad_mixed[...]
    grad_pre[...] = (grad * states * slope).astype(bf16)
    decay = jnp.exp(-8.0 * sigmoid(rate_pre[...]) * small[SOFT : SOFT + 1, :])
    ext[0:rows, :] = decay
    ext[rows:, :] = jnp.ones((8, decay.shape[1]), f32)
    product, back = scan_rows(ext[pl.ds(1, rows), :], grad * value, True)
    rev_cum[...] = product
    rev_grad[...] = back
    pair[...] = jnp.broadcast_to(decay[0:1, :] * back[0:1, :], pair.shape)


def mixer_backward(
    rev_cum, rev_grad, incoming, cum, local, carried, rate_pre, input_pre, conv, branch, prior, small, rate_w, input_w,
    own, head, rate_w_grad, input_w_grad, sums, ext, gext,
):
    rows = rev_cum.shape[0]
    soft = small[SOFT : SOFT + 1, :]
    grad_states = rev_grad[...] + rev_cum[...] * incoming[0:1, :]
    rate, decay, square, root, opened = gates(rate_pre[...], input_pre[...], soft)
    ext[0:8, :] = jnp.broadcast_to(carried[0:1, :], (8, carried.shape[1]))
    ext[8:, :] = local[...] + cum[...] * carried[0:1, :]
    before = ext[pl.ds(7, rows), :]
    low = conv[...]
    conv_in = low.astype(f32)
    grad_log = grad_states * decay * before - grad_states * opened * conv_in * square / root
    driven = grad_states * root
    grad_input = (driven * conv_in * opened * (1.0 - opened)).astype(bf16)
    by_rate = grad_log * (-8.0 * rate)
    grad_rate = (by_rate * soft * (1.0 - rate)).astype(bf16)
    sums[6:7, :] = jnp.sum(by_rate, axis=0, keepdims=True) * small[SOFT_SLOPE : SOFT_SLOPE + 1, :]
    sums[4:5, :] = jnp.sum(grad_rate.astype(f32), axis=0, keepdims=True)
    sums[5:6, :] = jnp.sum(grad_input.astype(f32), axis=0, keepdims=True)
    rate_w_grad[...] = mm(low, grad_rate, ((0,), (0,))).astype(rate_w_grad.dtype)
    input_w_grad[...] = mm(low, grad_input, ((0,), (0,))).astype(input_w_grad.dtype)
    grad_conv = (
        driven * opened
        + mm(grad_rate, rate_w[...], ((1,), (1,)))
        + mm(grad_input, input_w[...], ((1,), (1,)))
    )
    sums[7:8, :] = jnp.sum(grad_conv, axis=0, keepdims=True)
    ext[0:8, :] = prior[...]
    ext[8:, :] = branch[...].astype(f32)
    gext[0:8, :] = jnp.zeros((8, grad_conv.shape[1]), f32)
    gext[8 : 8 + rows, :] = grad_conv
    gext[8 + rows :, :] = jnp.zeros((8, grad_conv.shape[1]), f32)
    back = jnp.zeros_like(grad_conv)
    front = jnp.zeros((8, grad_conv.shape[1]), f32)
    for offset in range(4):
        tap = small[TAP + offset : TAP + offset + 1, :]
        sums[offset : offset + 1, :] = jnp.sum(
            grad_conv * ext[pl.ds(8 - offset, rows), :], axis=0, keepdims=True
        )
        back = back + tap * gext[pl.ds(8 + offset, rows), :]
        front = front + tap * gext[pl.ds(offset, 8), :]
    own[...] = back
    head[...] = front


def places():
    s = lax.axis_index("seq")
    z = lax.axis_index("fsdp")
    core = s + 1 - 2 * (s % 2)
    beside = s + 2 - 4 * ((s // 2) % 2)
    across = s + 4 - 8 * (s // 4)
    return s, z, core, beside, across


def greet(peers):
    barrier = pltpu.get_barrier_semaphore()
    for peer in peers:
        pl.semaphore_signal(barrier, inc=1, device_id=peer, device_id_type=MESH)
    pl.semaphore_wait(barrier, len(peers))


def gather_kernel(
    mixer, gate, up, down, grad, mixer_all, mlp_all, grad_all,
    flow_send, flow_recv, line_send, line_recv, swap_send, swap_recv, own_sem,
):
    s, z, core, beside, across = places()
    rows = mixer.shape[0]
    mixer_cols = mixer.shape[1]
    ff_part = mlp_all.shape[2]
    tok = grad.shape[0]
    mixer_cut = mixer_cols // 256 * 128
    mlp_cut = ff_part // 256 * 128
    diag = beside + across - s
    greet([(core, z), (beside, z), (across, z)] + [(s, (z + k) % 4) for k in range(1, 4)])

    def remote(src, dst, send, recv, target):
        return pltpu.make_async_remote_copy(
            src_ref=src, dst_ref=dst, send_sem=send, recv_sem=recv, device_id=target, device_id_type=MESH
        )

    def span(seq, zz):
        return pl.ds(pl.multiple_of((seq * 4 + zz) * rows, 16), rows)

    def piece(kind, seq, zz, half=None):
        if kind == 0:
            if half is None:
                return mixer_all.at[span(seq, zz), :]
            cols = pl.ds(0, mixer_cut) if half == 0 else pl.ds(mixer_cut, mixer_cols - mixer_cut)
            return mixer_all.at[span(seq, zz), cols]
        if half is None:
            return mlp_all.at[:, span(seq, zz), :]
        cols = pl.ds(0, mlp_cut) if half == 0 else pl.ds(mlp_cut, ff_part - mlp_cut)
        return mlp_all.at[:, span(seq, zz), cols]

    def flow(kind, zz, index, seq, half, target, src=None):
        ref = piece(kind, seq, zz, half)
        return remote(
            ref if src is None else src, ref, flow_send.at[kind, zz, index], flow_recv.at[kind, zz, index], (target, z)
        )

    def sends(kind, zz, src=None):
        return [
            flow(kind, zz, 0, s, None, beside, src),
            flow(kind, zz, 1, s, None, across, src),
            flow(kind, zz, 4, s, None, core, src),
        ]

    def spread(kind, zz, src=None):
        for copy in sends(kind, zz, src):
            copy.start()

    def relay(kind, zz):
        flow(kind, zz, 0, beside, None, beside).wait_recv()
        flow(kind, zz, 3, beside, 0, across).start()
        flow(kind, zz, 5, beside, None, core).start()
        flow(kind, zz, 1, across, None, across).wait_recv()
        flow(kind, zz, 2, across, 1, beside).start()
        flow(kind, zz, 6, across, None, core).start()

    def finish(kind, zz):
        flow(kind, zz, 3, diag, 0, across).wait_recv()
        flow(kind, zz, 7, diag, 0, core).start()
        flow(kind, zz, 2, diag, 1, beside).wait_recv()
        flow(kind, zz, 8, diag, 1, core).start()

    def drain(kind, zz, src=None):
        other = core
        for copy in sends(kind, zz, src):
            copy.wait_send()
        flow(kind, zz, 3, beside, 0, across).wait_send()
        flow(kind, zz, 5, beside, None, core).wait_send()
        flow(kind, zz, 2, across, 1, beside).wait_send()
        flow(kind, zz, 6, across, None, core).wait_send()
        flow(kind, zz, 7, diag, 0, core).wait_send()
        flow(kind, zz, 8, diag, 1, core).wait_send()
        flip = core - s
        flow(kind, zz, 4, other, None, core).wait_recv()
        flow(kind, zz, 5, beside + flip, None, core).wait_recv()
        flow(kind, zz, 6, across + flip, None, core).wait_recv()
        flow(kind, zz, 7, diag + flip, 0, core).wait_recv()
        flow(kind, zz, 8, diag + flip, 1, core).wait_recv()

    def line(kind, zz, up_way, hop, src=None):
        if kind == 0:
            ref = mixer_all.at[span(s, zz), :]
        else:
            ref = grad_all.at[pl.ds(pl.multiple_of(zz * tok, 16), tok), :]
        way = 0 if up_way else 1
        target = z + 1 if up_way else z - 1
        return remote(
            ref if src is None else src, ref, line_send.at[kind, way, hop], line_recv.at[kind, way, hop], (s, target)
        )

    def line_start(kind, src):
        pl.when(z < 3)(lambda: line(kind, z, True, 0, src).start())
        pl.when(z > 0)(lambda: line(kind, z, False, 0, src).start())

    def line_hop(kind, hop):
        def below():
            line(kind, z - hop, True, hop - 1).wait_recv()

            @pl.when(z < 3)
            def _():
                line(kind, z - hop, True, hop).start()

        def above():
            line(kind, z + hop, False, hop - 1).wait_recv()

            @pl.when(z > 0)
            def _():
                line(kind, z + hop, False, hop).start()

        pl.when(z >= hop)(below)
        pl.when(z + hop <= 3)(above)

    def line_drain(kind, src):
        pl.when(z < 3)(lambda: line(kind, z, True, 0, src).wait_send())
        pl.when(z > 0)(lambda: line(kind, z, False, 0, src).wait_send())
        for hop in range(1, 3):
            pl.when((z >= hop) & (z < 3))(lambda: line(kind, z - hop, True, hop).wait_send())
            pl.when((z + hop <= 3) & (z > 0))(lambda: line(kind, z + hop, False, hop).wait_send())

    def at_hop(hop, act):
        pl.when(z >= hop)(lambda: act(z - hop))
        pl.when(z + hop <= 3)(lambda: act(z + hop))

    def swap(k, m, arriving=False):
        weight = (gate, up, down)[m]
        to = (z + k) % 4
        came = (z + 4 - k) % 4
        cols = pl.ds(pl.multiple_of(to * ff_part, 128), ff_part)
        dst = mlp_all.at[m, span(s, came if arriving else z), :]
        return remote(weight.at[:, cols], dst, swap_send.at[k - 1, m], swap_recv.at[k - 1, m], (s, to))

    own_cols = pl.ds(pl.multiple_of(z * ff_part, 128), ff_part)
    local = [
        pltpu.make_async_copy(weight.at[:, own_cols], mlp_all.at[m, span(s, z), :], own_sem.at[m])
        for m, weight in enumerate((gate, up, down))
    ]
    local.append(pltpu.make_async_copy(mixer, mixer_all.at[span(s, z), :], own_sem.at[3]))
    local.append(
        pltpu.make_async_copy(grad, grad_all.at[pl.ds(pl.multiple_of(z * tok, 16), tok), :], own_sem.at[4])
    )

    line_start(0, mixer)
    spread(0, z, mixer)
    for copy in local:
        copy.start()
    line_hop(0, 1)
    at_hop(1, lambda zz: spread(0, zz))
    relay(0, z)
    line_hop(0, 2)
    at_hop(2, lambda zz: spread(0, zz))
    finish(0, z)
    at_hop(1, lambda zz: relay(0, zz))
    line_hop(0, 3)
    at_hop(3, lambda zz: spread(0, zz))
    for k in (1, 3, 2):
        for m in range(3):
            swap(k, m).start()
    for copy in local:
        copy.wait()
    spread(1, z)
    at_hop(1, lambda zz: finish(0, zz))
    at_hop(2, lambda zz: relay(0, zz))
    at_hop(3, lambda zz: relay(0, zz))
    relay(1, z)
    at_hop(2, lambda zz: finish(0, zz))
    at_hop(3, lambda zz: finish(0, zz))
    for k in (1, 3, 2):
        for m in range(3):
            swap(k, m, True).wait_recv()
        spread(1, (z + 4 - k) % 4)
    line_start(1, grad)
    finish(1, z)
    line_hop(1, 1)
    relay(1, (z + 3) % 4)
    line_hop(1, 2)
    relay(1, (z + 1) % 4)
    finish(1, (z + 3) % 4)
    line_hop(1, 3)
    relay(1, (z + 2) % 4)
    finish(1, (z + 1) % 4)
    finish(1, (z + 2) % 4)
    drain(0, z, mixer)
    for hop in range(1, 4):
        at_hop(hop, lambda zz: drain(0, zz))
    drain(1, z)
    for k in (1, 3, 2):
        drain(1, (z + 4 - k) % 4)
        for m in range(3):
            swap(k, m).wait_send()
    line_drain(0, mixer)
    line_drain(1, grad)


def gather(mixer, gate, up, down, grad):
    rows, cols = mixer.shape
    tok, model = grad.shape
    ff_part = gate.shape[1] // 4
    anyspec = pl.BlockSpec(memory_space=pl.ANY)
    dma = pltpu.SemaphoreType.DMA
    return pl.pallas_call(
        gather_kernel,
        in_specs=[anyspec] * 5,
        out_specs=[anyspec] * 3,
        out_shape=[
            jax.ShapeDtypeStruct((32 * rows, cols), bf16),
            jax.ShapeDtypeStruct((3, 32 * rows, ff_part), bf16),
            jax.ShapeDtypeStruct((4 * tok, model), bf16),
        ],
        scratch_shapes=[
            dma((2, 4, 9)), dma((2, 4, 9)), dma((2, 2, 3)), dma((2, 2, 3)), dma((3, 3)), dma((3, 3)), dma((5,)),
        ],
        compiler_params=pltpu.CompilerParams(collective_id=1, has_side_effects=True),
        name="gather_weights",
    )(mixer, gate, up, down, grad)


def add_columns(target, sources, start, size, step):
    def one(turn, carry):
        cols = pl.ds(pl.multiple_of(start + turn * step, 128), step)
        total = target[:, cols].astype(f32)
        for source in sources:
            total = total + source[:, cols].astype(f32)
        target[:, cols] = total.astype(target.dtype)
        return carry

    lax.fori_loop(0, size // step, one, 0)


def scatter_kernel(
    wide, outer, rest, mlp_pair, mlp_down, out, mixer_sum, mlp_back, out_sum,
    held, cross, near, lined, held_out, lined_out,
    load_sem, flow_send, flow_recv, line_send, line_recv, swap_send, swap_recv, own_sem,
):
    s, z, _, beside, across = places()
    chip, chip_beside, chip_across = s // 2, beside // 2, across // 2
    chip_diag = chip_beside + chip_across - chip
    rows = held.shape[1] // 4
    cols = held.shape[2]
    cut = cols // 256 * 128
    tok = held_out.shape[1]
    ff_part = mlp_down.shape[1]
    parts = (wide, outer, rest)
    order = (3 * (1 - z // 2), (2 + 3 * z) % 5, 1 + z % 2, z)

    def remote(src, dst, send, recv, target):
        return pltpu.make_async_remote_copy(
            src_ref=src, dst_ref=dst, send_sem=send, recv_sem=recv, device_id=target, device_id_type=MESH
        )

    def span(k):
        return pl.ds(pl.multiple_of(k * rows, 16), rows)

    def loads(i):
        copies, start = [], 0
        for n, part in enumerate(parts):
            size = part.shape[2]
            copies.append(
                pltpu.make_async_copy(
                    part.at[:, span(order[i]), :], held.at[:, span(order[i]), pl.ds(start, size)], load_sem.at[i, n]
                )
            )
            start += size
        return copies

    left, right = pl.ds(0, cut), pl.ds(cut, cols - cut)

    def block(q, i, side):
        return held.at[q, span(order[i]), side]

    def flow(i, index):
        send, recv = flow_send.at[i, index], flow_recv.at[i, index]
        to_beside, to_across = (beside, z), (across, z)
        if index == 0:
            return remote(block(chip_diag, i, left), cross.at[i, :, left], send, recv, to_across)
        if index == 1:
            return remote(block(chip_diag, i, right), cross.at[i, :, right], send, recv, to_beside)
        if index == 2:
            return remote(block(chip_beside, i, right), near.at[0, i, :, right], send, recv, to_beside)
        if index == 3:
            return remote(block(chip_beside, i, left), near.at[0, i, :, left], send, recv, to_beside)
        if index == 4:
            return remote(block(chip_across, i, left), near.at[1, i, :, left], send, recv, to_across)
        return remote(block(chip_across, i, right), near.at[1, i, :, right], send, recv, to_across)

    def cross_step(i):
        flow(i, 0).wait_recv()
        add_columns(held.at[chip_beside, span(order[i]), :], [cross.at[i]], 0, cut, 512)
        flow(i, 3).start()
        flow(i, 1).wait_recv()
        add_columns(held.at[chip_across, span(order[i]), :], [cross.at[i]], cut, cols - cut, 384)
        flow(i, 5).start()

    def near_step(i):
        for index in (2, 4, 3, 5):
            flow(i, index).wait_recv()
        add_columns(held.at[chip, span(order[i]), :], [near.at[0, i], near.at[1, i]], 0, cols, 640)

    def mine(kind, k):
        return held.at[chip, span(k), :] if kind == 0 else held_out.at[k]

    def landing(kind, slot):
        return lined.at[slot] if kind == 0 else lined_out.at[slot]

    def line(kind, k, slot, target):
        return remote(
            mine(kind, k), landing(kind, slot), line_send.at[kind, k], line_recv.at[kind, slot], (s, target)
        )

    def absorb(kind, k, slot, source):
        line(kind, k, slot, source).wait_recv()
        if kind == 0:
            add_columns(mine(kind, k), [landing(kind, slot)], 0, cols, 640)
        else:
            add_columns(mine(kind, k), [landing(kind, slot)], 0, held_out.shape[2], 512)

    def chain(kind, i):
        k = order[i]
        if i == 3:
            pl.when(z > 0)(lambda: absorb(kind, k, k, z - 1))
            pl.when(z < 3)(lambda: absorb(kind, k, 4, z + 1))
            return

        @pl.when(k > z)
        def _():
            pl.when(z > 0)(lambda: absorb(kind, k, k, z - 1))
            line(kind, k, k, z + 1).start()

        @pl.when(k < z)
        def _():
            pl.when(z < 3)(lambda: absorb(kind, k, k, z + 1))
            pl.when(k == z - 1)(lambda: line(kind, k, 4, z - 1).start())
            pl.when(k < z - 1)(lambda: line(kind, k, k, z - 1).start())

    def chain_drain(kind):
        for i in range(3):
            k = order[i]
            line(kind, k, k, (z + 1) % 4).wait_send()

    def pieces():
        for m in range(3):
            source = mlp_down if m == 2 else mlp_pair
            yield m, source, pl.ds(0 if m == 2 else m * ff_part, ff_part)

    def swap(k):
        to = (z + k) % 4
        here = pl.ds(pl.multiple_of(z * ff_part, 128), ff_part)
        return [
            remote(
                source.at[span(to), at], mlp_back.at[m, :, here], swap_send.at[k - 1, m], swap_recv.at[k - 1, m], (s, to)
            )
            for m, source, at in pieces()
        ]

    own = [
        pltpu.make_async_copy(
            source.at[span(z), at], mlp_back.at[m, :, pl.ds(pl.multiple_of(z * ff_part, 128), ff_part)], own_sem.at[m]
        )
        for m, source, at in pieces()
    ]
    out_load = pltpu.make_async_copy(out, held_out, own_sem.at[3])
    out_load.start()
    for i in range(4):
        for copy in loads(i):
            copy.start()
    greet([(beside, z), (across, z)] + [(s, (z + k) % 4) for k in range(1, 4)])
    out_load.wait()
    chain(1, 0)
    for k in (1, 3, 2):
        for copy in swap(k):
            copy.start()
    for copy in own:
        copy.start()
    for i in range(2):
        for copy in loads(i):
            copy.wait()
        flow(i, 0).start()
        flow(i, 1).start()
        if i == 0:
            flow(i, 2).start()
            flow(i, 4).start()
    for i in range(4):
        cross_step(i)
        if i + 1 < 4:
            flow(i + 1, 2).start()
            flow(i + 1, 4).start()
        if i + 2 < 4:
            for copy in loads(i + 2):
                copy.wait()
            flow(i + 2, 0).start()
            flow(i + 2, 1).start()
        if i + 1 < 4:
            chain(1, i + 1)
        if i > 0:
            near_step(i - 1)
            chain(0, i - 1)
    out_done = pltpu.make_async_copy(held_out.at[z], out_sum, own_sem.at[4])
    out_done.start()
    near_step(3)
    chain(0, 3)
    done = pltpu.make_async_copy(held.at[chip, span(z), :], mixer_sum, own_sem.at[5])
    done.start()
    for i in range(4):
        for index in range(6):
            flow(i, index).wait_send()
    chain_drain(0)
    chain_drain(1)
    for k in range(1, 4):
        for copy in swap(k):
            copy.wait()
    for copy in own:
        copy.wait()
    out_done.wait()
    done.wait()


def scatter(wide, outer, rest, mlp_pair, mlp_down, out):
    rows = wide.shape[1] // 4
    cols = wide.shape[2] + outer.shape[2] + rest.shape[2]
    _, tok, model = out.shape
    ff_part = mlp_down.shape[1]
    anyspec = pl.BlockSpec(memory_space=pl.ANY)
    dma = pltpu.SemaphoreType.DMA
    return pl.pallas_call(
        scatter_kernel,
        in_specs=[anyspec] * 6,
        out_specs=[anyspec] * 3,
        out_shape=[
            jax.ShapeDtypeStruct((rows, cols), bf16),
            jax.ShapeDtypeStruct((3, rows, 4 * ff_part), bf16),
            jax.ShapeDtypeStruct((tok, model), bf16),
        ],
        scratch_shapes=[
            pltpu.VMEM((4, 4 * rows, cols), bf16),
            pltpu.VMEM((4, rows, cols), bf16),
            pltpu.VMEM((2, 4, rows, cols), bf16),
            pltpu.VMEM((5, rows, cols), bf16),
            pltpu.VMEM((4, tok, model), bf16),
            pltpu.VMEM((5, tok, model), bf16),
            dma((4, 3)), dma((4, 6)), dma((4, 6)), dma((2, 4)), dma((2, 5)), dma((3, 3)), dma((3, 3)), dma((6,)),
        ],
        compiler_params=pltpu.CompilerParams(
            collective_id=2, has_side_effects=True, vmem_limit_bytes=60 * 1024 * 1024
        ),
        name="scatter_gradients",
    )(wide, outer, rest, mlp_pair, mlp_down, out)


def gather_plain(mixer, gate, up, down, grad):
    groups = lax.axis_size("fsdp")
    part_rows, ff = gate.shape

    def columns(weight):
        return jnp.transpose(weight.reshape(part_rows, groups, ff // groups), (1, 0, 2))

    own = jnp.stack([columns(w) for w in (gate, up, down)], axis=1)
    mine = lax.all_to_all(own, "fsdp", 0, 0, tiled=True)
    mine = jnp.transpose(mine, (1, 0, 2, 3)).reshape(3, groups * part_rows, ff // groups)
    return (
        lax.all_gather(mixer, both, axis=0, tiled=True),
        lax.all_gather(mine, "seq", axis=1, tiled=True),
        lax.all_gather(grad, "fsdp", axis=0, tiled=True),
    )


def swap_cores(shard):
    count = lax.axis_size("seq")
    return lax.ppermute(shard, "seq", [(i, i + 1 - 2 * (i % 2)) for i in range(count)])


def scatter_paired(normed, grad_both, grad_mix, mixed, rest, pair_sum, down_sum, out_part):
    core = lax.axis_index("seq") % 2
    chips = lax.axis_size("seq") // 2

    def pairs(shard):
        return jnp.concatenate([shard, swap_cores(shard)], axis=0)

    def halves(values, which):
        grouped = values.reshape(values.shape[0], chips, 2, values.shape[1] // (2 * chips))
        return lax.dynamic_index_in_dim(grouped, which, 2, False).reshape(values.shape[0], -1)

    def product(left, right):
        result = mm(halves(left, core), right, ((0,), (0,))).astype(bf16)
        return result.reshape(chips, -1, right.shape[1])

    wide = product(pairs(normed), pairs(grad_both))
    outer = product(pairs(grad_mix), pairs(mixed))
    grouped = rest.reshape(chips, 2, -1, rest.shape[1])
    own = lax.dynamic_index_in_dim(grouped, core, 1, False)
    other = swap_cores(lax.dynamic_index_in_dim(grouped, 1 - core, 1, False))
    rest = (own.astype(f32) + other.astype(f32)).astype(bf16)
    groups = lax.axis_size("fsdp")
    return scatter(wide, outer, rest, pair_sum, down_sum, out_part.reshape(groups, -1, out_part.shape[1]))


def scatter_plain(normed, grad_both, grad_mix, mixed, rest, pair_sum, down_sum, out_part):
    groups = lax.axis_size("fsdp")
    term_wide = mm(normed, grad_both, ((0,), (0,))).astype(bf16)
    term_out = mm(grad_mix, mixed, ((0,), (0,))).astype(bf16)
    mixer_sum = lax.psum_scatter(
        jnp.concatenate([term_wide, term_out, rest], axis=1), "seq", scatter_dimension=0, tiled=True
    )
    mixer_sum = lax.psum_scatter(mixer_sum, "fsdp", scatter_dimension=0, tiled=True)
    ff_part = down_sum.shape[1]
    part_rows = down_sum.shape[0] // groups
    mlp_sum = jnp.concatenate([pair_sum, down_sum], axis=1).reshape(groups, part_rows, 3, ff_part)
    mlp_back = lax.all_to_all(mlp_sum, "fsdp", 0, 0, tiled=True)
    mlp_back = jnp.transpose(mlp_back, (2, 1, 0, 3)).reshape(3, part_rows, groups * ff_part)
    return mixer_sum, mlp_back, lax.psum_scatter(out_part, "fsdp", scatter_dimension=0, tiled=True)


def call_heads(kernel, width, heads, ins, outs, scratch, name):
    def spec(rows_cols):
        rows, by_row = rows_cols
        if by_row:
            return pl.BlockSpec((rows, width), lambda h: (h, 0))
        return pl.BlockSpec((rows, width), lambda h: (0, h))

    in_specs = [spec((width, True)) if rowwise else spec((a.shape[0], False)) for a, rowwise in ins]
    out_specs = [spec((width, True)) if rowwise else spec((rows, False)) for rows, _, rowwise in outs]
    out_shape = [
        jax.ShapeDtypeStruct((heads * width, width) if rowwise else (rows, heads * width), kind)
        for rows, kind, rowwise in outs
    ]
    return pl.pallas_call(
        kernel,
        grid=(heads,),
        in_specs=in_specs,
        out_specs=out_specs,
        out_shape=out_shape,
        scratch_shapes=[pltpu.VMEM((rows, width), f32) for rows in scratch],
        compiler_params=pltpu.CompilerParams(vmem_limit_bytes=40 * 1024 * 1024),
        name=name,
    )(*[a for a, _ in ins])


def on_device(
    block_input,
    cotangent,
    mixer_gain,
    branch_proj,
    gelu_proj,
    conv_taps,
    conv_bias,
    rate_blocks,
    input_blocks,
    rate_bias,
    input_bias,
    decay_param,
    out_proj,
    mlp_gain,
    gate_proj,
    up_proj,
    down_proj,
):
    groups = lax.axis_size("fsdp")
    part_rows, lru = branch_proj.shape
    width = rate_blocks.shape[1]
    heads = lru // width
    margin = conv_taps.shape[0] - 1
    tokens = block_input[0].astype(f32)
    tok_count, model = tokens.shape
    ff = gate_proj.shape[1]
    ff_part = ff // groups
    grad_out = cotangent[0]

    smalls = jnp.stack(
        [conv_taps[k] for k in range(margin + 1)]
        + [conv_bias, rate_bias, input_bias, decay_param, mixer_gain, mlp_gain],
        axis=1,
    )
    small_count = smalls.shape[1]
    smalls = jnp.pad(smalls, ((0, 0), (0, 128 - small_count)))
    mixer_own = jnp.concatenate(
        [smalls, rate_blocks, input_blocks, branch_proj, gelu_proj, out_proj], axis=1
    )
    custom = lax.axis_size("seq") == 8 and groups == 4
    if custom:
        mixer_w, mlp_w, grad_out_all = gather(mixer_own, gate_proj, up_proj, down_proj, grad_out)
    else:
        mixer_w, mlp_w, grad_out_all = gather_plain(mixer_own, gate_proj, up_proj, down_proj, grad_out)
    first = lax.optimization_barrier(mixer_w[:, : 128 + 2 * width])
    wide = mixer_w[:, 128 + 2 * width : 128 + 2 * width + 2 * lru]
    proj_out = mixer_w[:, 128 + 2 * width + 2 * lru :]

    table = first[:, :small_count].astype(f32).T
    blocks_rate = first[:, 128 : 128 + width]
    blocks_input = first[:, 128 + width :]
    param_decay = table[margin + 4]
    gain_one = table[margin + 5]
    gain_two = table[margin + 6]
    small = jnp.concatenate(
        [
            table[: margin + 4],
            jax.nn.softplus(-param_decay)[None],
            -jax.nn.sigmoid(-param_decay)[None],
            jnp.zeros((16 - margin - 6, lru), f32),
        ],
        axis=0,
    )

    normed = norm_rows(tokens, gain_one).astype(bf16)
    both_pre = mm(normed, wide, ((1,), (0,)))
    branch = both_pre[:, :lru].astype(bf16)
    gelu_pre = both_pre[:, lru:]
    prior = from_behind(branch[tok_count - margin :], "seq", 1).astype(f32)
    prior = jnp.concatenate([jnp.zeros((8 - margin, lru), f32), prior], axis=0)
    conv, rate_pre, input_pre, cum, local = call_heads(
        mixer_forward,
        width,
        heads,
        [(branch, False), (prior, False), (small, False), (blocks_rate, True), (blocks_input, True)],
        [(tok_count, bf16, False)] + [(tok_count, f32, False)] * 4,
        [tok_count + 8],
        "mixer_forward",
    )
    carried = prefix((cum[-1], local[-1]), "seq", False)
    states = local + cum * carried[None]
    mixed = (states * jax.nn.gelu(gelu_pre, approximate=True)).astype(bf16)
    middle = tokens + mm(mixed, proj_out, ((1,), (1,)))
    normed_two = norm_rows(middle, gain_two).astype(bf16)

    normed_all = lax.all_gather(normed_two, "fsdp", axis=0, tiled=True)
    w_gate, w_up, w_down = mlp_w[0], mlp_w[1], mlp_w[2]
    gate = mm(normed_all, w_gate, ((1,), (0,)))
    up_val = mm(normed_all, w_up, ((1,), (0,)))
    gelu_gate, gelu_slope = gelu_parts(gate)
    hidden = (gelu_gate * up_val).astype(bf16)
    grad_hidden = mm(grad_out_all, w_down, ((1,), (0,)))
    grad_gate = (grad_hidden * up_val * gelu_slope).astype(bf16)
    grad_up = (grad_hidden * gelu_gate).astype(bf16)
    grad_pair = jnp.concatenate([grad_gate, grad_up], axis=1)
    grad_normed_part = mm(grad_gate, w_gate, ((1,), (1,))) + mm(grad_up, w_up, ((1,), (1,)))
    grad_normed_two = lax.psum_scatter(
        grad_normed_part.astype(bf16), "fsdp", scatter_dimension=0, tiled=True
    )
    out_part = mm(hidden, w_down, ((1,), (1,))).astype(bf16)
    term_pair = mm(normed_all, grad_pair, ((0,), (0,))).astype(bf16)
    term_down = mm(grad_out_all, hidden, ((0,), (0,))).astype(bf16)
    term_pair, term_down, grad_normed_two = lax.optimization_barrier(
        (term_pair, term_down, grad_normed_two)
    )
    grad_normed_two = grad_normed_two.astype(f32)
    pair_sum = lax.psum_scatter(term_pair, "seq", scatter_dimension=0, tiled=True)
    down_sum = lax.psum_scatter(term_down, "seq", scatter_dimension=0, tiled=True)

    second_pull = jax.vjp(norm_rows, middle, gain_two)[1]
    grad_mid_part, grad_gain_two = second_pull(grad_normed_two)
    grad_middle = grad_out.astype(f32) + grad_mid_part
    grad_mix = grad_middle.astype(bf16)
    grad_mixed = mm(grad_mix, proj_out, ((1,), (0,)))
    carried_rows = jnp.broadcast_to(carried[None], (8, lru))
    grad_gelu_pre, rev_cum, rev_grad, pair_grad = call_heads(
        mixer_backward_scan,
        width,
        heads,
        [(a, False) for a in (grad_mixed, gelu_pre, rate_pre, cum, local, carried_rows, small)],
        [(tok_count, bf16, False), (tok_count, f32, False), (tok_count, f32, False), (8, f32, False)],
        [tok_count + 8],
        "mixer_backward_scan",
    )
    incoming = prefix((cum[-1], pair_grad[0]), "seq", True)
    incoming_rows = jnp.broadcast_to(incoming[None], (8, lru))
    own, head, rate_w_grad, input_w_grad, sums = call_heads(
        mixer_backward,
        width,
        heads,
        [
            (a, False)
            for a in (rev_cum, rev_grad, incoming_rows, cum, local, carried_rows, rate_pre, input_pre, conv, branch, prior, small)
        ]
        + [(blocks_rate, True), (blocks_input, True)],
        [(tok_count, f32, False), (8, f32, False), (0, bf16, True), (0, bf16, True), (8, f32, False)],
        [tok_count + 8, tok_count + 16],
        "mixer_backward",
    )
    received = from_behind(head[8 - margin :], "seq", -1)
    grad_branch = jnp.concatenate(
        [own[: tok_count - margin], own[tok_count - margin :] + received], axis=0
    ).astype(bf16)
    grad_both = jnp.concatenate([grad_branch, grad_gelu_pre], axis=1)
    grad_normed = mm(grad_both, wide, ((1,), (1,)))
    first_pull = jax.vjp(norm_rows, tokens, gain_one)[1]
    grad_tok_part, grad_gain_one = first_pull(grad_normed)
    input_grad = (grad_middle + grad_tok_part).astype(bf16)[None]
    vectors = jnp.concatenate([sums, grad_gain_one[None], grad_gain_two[None]], axis=0).T
    vectors = jnp.pad(vectors, ((0, 0), (0, 128 - vectors.shape[1]))).astype(bf16)
    rest = jnp.concatenate([rate_w_grad, input_w_grad, vectors], axis=1)
    if custom:
        scattered = scatter_paired(normed, grad_both, grad_mix, mixed, rest, pair_sum, down_sum, out_part)
    else:
        scattered = scatter_plain(normed, grad_both, grad_mix, mixed, rest, pair_sum, down_sum, out_part)
    mixer_sum, mlp_back, out_sum = scattered
    block_output = (middle + out_sum.astype(f32)).astype(bf16)[None]
    mlp_grads = [mlp_back[m].astype(f32) for m in range(3)]
    mixer_sum = mixer_sum.astype(f32)
    edges = [lru, 2 * lru, 3 * lru, 3 * lru + width, 3 * lru + 2 * width]
    dbranch, dgelu, dout, drate, dinput, vec = jnp.split(mixer_sum, edges, axis=1)
    vec = vec.T
    return (
        block_output,
        input_grad,
        vec[8],
        dbranch,
        dgelu,
        vec[: margin + 1],
        vec[7],
        drate,
        dinput,
        vec[4],
        vec[5],
        vec[6],
        dout,
        vec[9],
        mlp_grads[0],
        mlp_grads[1],
        mlp_grads[2],
    )


def solution(mesh):
    tokens = P("fsdp", "seq", None)
    vector = P(both)
    matrix = P(both, None)
    taps = P(None, both)
    return jax.shard_map(
        on_device,
        mesh=mesh,
        in_specs=(
            tokens, tokens, vector, matrix, matrix, taps, vector, matrix, matrix,
            vector, vector, vector, matrix, vector, matrix, matrix, matrix,
        ),
        out_specs=(
            tokens, tokens, vector, matrix, matrix, taps, vector, matrix, matrix,
            vector, vector, vector, matrix, vector, matrix, matrix, matrix,
        ),
        check_vma=False,
    )
```

```python
import functools

import jax
import jax.numpy as jnp
from jax import lax
from jax.experimental import pallas as pl
from jax.experimental.pallas import tpu as pltpu
from jax.sharding import PartitionSpec as P

epsilon = 1e-06
f32 = jnp.float32
bf16 = jnp.bfloat16
both = ("seq", "fsdp")
MESH = pl.DeviceIdType.MESH
TAP, CONV_BIAS, RATE_BIAS, INPUT_BIAS, SOFT, SOFT_SLOPE = 0, 4, 5, 6, 7, 8
GELU_C = 0.7978845608028654
GELU_A = 0.044715


def from_behind(shard, axis, by):
    devices = lax.axis_size(axis)
    pairs = [(i, i + by) for i in range(devices) if 0 <= i + by < devices]
    return lax.ppermute(shard, axis, pairs)


def prefix(part, axis, reverse):
    count = lax.axis_size(axis)
    place = lax.axis_index(axis)
    gathered = lax.all_gather(jnp.stack(part), axis)
    state = jnp.zeros_like(part[1])
    for hop in range(count):
        source = count - 1 - hop if reverse else hop
        ahead = source > place if reverse else source < place
        state = jnp.where(ahead, gathered[source, 1] + gathered[source, 0] * state, state)
    return state


def norm_rows(values, scales):
    return values * lax.rsqrt(jnp.mean(values * values, axis=-1, keepdims=True) + epsilon) * scales


def gelu_parts(x):
    inner = jnp.tanh(GELU_C * (x + GELU_A * x * x * x))
    return 0.5 * x * (1.0 + inner), 0.5 * (1.0 + inner) + 0.5 * x * (1.0 - inner * inner) * (
        GELU_C * (1.0 + 3.0 * GELU_A * x * x)
    )


def mm(left, right, dims):
    return lax.dot_general(left, right, (dims, ((), ())), preferred_element_type=f32)


def sigmoid(x):
    return 1.0 / (1.0 + jnp.exp(-x))


def scan_rows(decay, value, reverse):
    rows = decay.shape[0]
    place = lax.broadcasted_iota(jnp.int32, decay.shape, 0)
    step = 1
    while step < rows:
        shift = rows - step if reverse else step
        inside = place < rows - step if reverse else place >= step
        before_value = jnp.where(inside, pltpu.roll(value, shift, 0), 0.0)
        before_decay = jnp.where(inside, pltpu.roll(decay, shift, 0), 1.0)
        value = value + decay * before_value
        decay = decay * before_decay
        step *= 2
    return decay, value


def gates(rate_pre, input_pre, soft):
    rate = sigmoid(rate_pre)
    log_decay = -8.0 * rate * soft
    decay = jnp.exp(log_decay)
    square = decay * decay
    root = jnp.sqrt(-jnp.tanh(log_decay) * (1.0 + square))
    return rate, decay, square, root, sigmoid(input_pre)


def mixer_forward(branch, prior, small, rate_w, input_w, conv, rate_pre, input_pre, cum, local, ext):
    rows = branch.shape[0]
    ext[0:8, :] = prior[...]
    ext[8:, :] = branch[...].astype(f32)
    total = small[CONV_BIAS : CONV_BIAS + 1, :] + small[TAP : TAP + 1, :] * ext[8:, :]
    for offset in range(1, 4):
        total = total + small[TAP + offset : TAP + offset + 1, :] * ext[pl.ds(8 - offset, rows), :]
    low = total.astype(bf16)
    conv[...] = low
    rate = mm(low, rate_w[...], ((1,), (0,))) + small[RATE_BIAS : RATE_BIAS + 1, :]
    inp = mm(low, input_w[...], ((1,), (0,))) + small[INPUT_BIAS : INPUT_BIAS + 1, :]
    rate_pre[...] = rate
    input_pre[...] = inp
    _, decay, _, root, opened = gates(rate, inp, small[SOFT : SOFT + 1, :])
    product, states = scan_rows(decay, root * opened * low.astype(f32), False)
    cum[...] = product
    local[...] = states


def mixer_backward_scan(grad_mixed, gelu_pre, rate_pre, cum, local, carried, small, grad_pre, rev_cum, rev_grad, pair, ext):
    rows = grad_mixed.shape[0]
    states = local[...] + cum[...] * carried[0:1, :]
    value, slope = gelu_parts(gelu_pre[...])
    grad = grad_mixed[...]
    grad_pre[...] = (grad * states * slope).astype(bf16)
    decay = jnp.exp(-8.0 * sigmoid(rate_pre[...]) * small[SOFT : SOFT + 1, :])
    ext[0:rows, :] = decay
    ext[rows:, :] = jnp.ones((8, decay.shape[1]), f32)
    product, back = scan_rows(ext[pl.ds(1, rows), :], grad * value, True)
    rev_cum[...] = product
    rev_grad[...] = back
    pair[...] = jnp.broadcast_to(decay[0:1, :] * back[0:1, :], pair.shape)


def mixer_backward(
    rev_cum, rev_grad, incoming, cum, local, carried, rate_pre, input_pre, conv, branch, prior, small, rate_w, input_w,
    own, head, rate_w_grad, input_w_grad, sums, ext, gext,
):
    rows = rev_cum.shape[0]
    soft = small[SOFT : SOFT + 1, :]
    grad_states = rev_grad[...] + rev_cum[...] * incoming[0:1, :]
    rate, decay, square, root, opened = gates(rate_pre[...], input_pre[...], soft)
    ext[0:8, :] = jnp.broadcast_to(carried[0:1, :], (8, carried.shape[1]))
    ext[8:, :] = local[...] + cum[...] * carried[0:1, :]
    before = ext[pl.ds(7, rows), :]
    low = conv[...]
    conv_in = low.astype(f32)
    grad_log = grad_states * decay * before - grad_states * opened * conv_in * square / root
    driven = grad_states * root
    grad_input = (driven * conv_in * opened * (1.0 - opened)).astype(bf16)
    by_rate = grad_log * (-8.0 * rate)
    grad_rate = (by_rate * soft * (1.0 - rate)).astype(bf16)
    sums[6:7, :] = jnp.sum(by_rate, axis=0, keepdims=True) * small[SOFT_SLOPE : SOFT_SLOPE + 1, :]
    sums[4:5, :] = jnp.sum(grad_rate.astype(f32), axis=0, keepdims=True)
    sums[5:6, :] = jnp.sum(grad_input.astype(f32), axis=0, keepdims=True)
    rate_w_grad[...] = mm(low, grad_rate, ((0,), (0,))).astype(rate_w_grad.dtype)
    input_w_grad[...] = mm(low, grad_input, ((0,), (0,))).astype(input_w_grad.dtype)
    grad_conv = (
        driven * opened
        + mm(grad_rate, rate_w[...], ((1,), (1,)))
        + mm(grad_input, input_w[...], ((1,), (1,)))
    )
    sums[7:8, :] = jnp.sum(grad_conv, axis=0, keepdims=True)
    ext[0:8, :] = prior[...]
    ext[8:, :] = branch[...].astype(f32)
    gext[0:8, :] = jnp.zeros((8, grad_conv.shape[1]), f32)
    gext[8 : 8 + rows, :] = grad_conv
    gext[8 + rows :, :] = jnp.zeros((8, grad_conv.shape[1]), f32)
    back = jnp.zeros_like(grad_conv)
    front = jnp.zeros((8, grad_conv.shape[1]), f32)
    for offset in range(4):
        tap = small[TAP + offset : TAP + offset + 1, :]
        sums[offset : offset + 1, :] = jnp.sum(
            grad_conv * ext[pl.ds(8 - offset, rows), :], axis=0, keepdims=True
        )
        back = back + tap * gext[pl.ds(8 + offset, rows), :]
        front = front + tap * gext[pl.ds(offset, 8), :]
    own[...] = back
    head[...] = front


def places():
    s = lax.axis_index("seq")
    z = lax.axis_index("fsdp")
    core = s + 1 - 2 * (s % 2)
    beside = s + 2 - 4 * ((s // 2) % 2)
    across = s + 4 - 8 * (s // 4)
    return s, z, core, beside, across


def greet(peers):
    barrier = pltpu.get_barrier_semaphore()
    for peer in peers:
        pl.semaphore_signal(barrier, inc=1, device_id=peer, device_id_type=MESH)
    pl.semaphore_wait(barrier, len(peers))


def gather_kernel(
    mixer, gate, up, down, mixer_all, mlp_mine,
    flow_send, flow_recv, line_send, line_recv, swap_send, swap_recv, own_sem,
):
    s, z, core, beside, across = places()
    rows, cols = mixer.shape
    ff_part = mlp_mine.shape[1] // 3
    cut = cols // 256 * 128
    diag = beside + across - s
    greet([(core, z), (beside, z), (across, z)] + [(s, (z + k) % 4) for k in range(1, 4)])

    def remote(src, dst, send, recv, target):
        return pltpu.make_async_remote_copy(
            src_ref=src, dst_ref=dst, send_sem=send, recv_sem=recv, device_id=target, device_id_type=MESH
        )

    def piece(seq, zz, half=None):
        span = pl.ds(pl.multiple_of((seq * 4 + zz) * rows, 16), rows)
        if half is None:
            return mixer_all.at[span, :]
        return mixer_all.at[span, pl.ds(0, cut) if half == 0 else pl.ds(cut, cols - cut)]

    def flow(zz, index, seq, half, target, src=None):
        ref = piece(seq, zz, half)
        return remote(
            ref if src is None else src, ref, flow_send.at[zz, index], flow_recv.at[zz, index], (target, z)
        )

    def sends(zz, src=None):
        return [
            flow(zz, 0, s, None, beside, src),
            flow(zz, 1, s, None, across, src),
            flow(zz, 4, s, None, core, src),
        ]

    def spread(zz, src=None):
        for copy in sends(zz, src):
            copy.start()

    def relay(zz):
        flow(zz, 0, beside, None, beside).wait_recv()
        flow(zz, 3, beside, 0, across).start()
        flow(zz, 5, beside, None, core).start()
        flow(zz, 1, across, None, across).wait_recv()
        flow(zz, 2, across, 1, beside).start()
        flow(zz, 6, across, None, core).start()

    def finish(zz):
        flow(zz, 3, diag, 0, across).wait_recv()
        flow(zz, 7, diag, 0, core).start()
        flow(zz, 2, diag, 1, beside).wait_recv()
        flow(zz, 8, diag, 1, core).start()

    def drain(zz, src=None):
        for copy in sends(zz, src):
            copy.wait_send()
        flow(zz, 3, beside, 0, across).wait_send()
        flow(zz, 5, beside, None, core).wait_send()
        flow(zz, 2, across, 1, beside).wait_send()
        flow(zz, 6, across, None, core).wait_send()
        flow(zz, 7, diag, 0, core).wait_send()
        flow(zz, 8, diag, 1, core).wait_send()
        flip = core - s
        flow(zz, 4, core, None, core).wait_recv()
        flow(zz, 5, beside + flip, None, core).wait_recv()
        flow(zz, 6, across + flip, None, core).wait_recv()
        flow(zz, 7, diag + flip, 0, core).wait_recv()
        flow(zz, 8, diag + flip, 1, core).wait_recv()

    def line(zz, up_way, hop, src=None):
        ref = piece(s, zz)
        way = 0 if up_way else 1
        target = z + 1 if up_way else z - 1
        return remote(
            ref if src is None else src, ref, line_send.at[way, hop], line_recv.at[way, hop], (s, target)
        )

    def line_hop(hop):
        def below():
            line(z - hop, True, hop - 1).wait_recv()
            pl.when(z < 3)(lambda: line(z - hop, True, hop).start())

        def above():
            line(z + hop, False, hop - 1).wait_recv()
            pl.when(z > 0)(lambda: line(z + hop, False, hop).start())

        pl.when(z >= hop)(below)
        pl.when(z + hop <= 3)(above)

    def at_hop(hop, act):
        pl.when(z >= hop)(lambda: act(z - hop))
        pl.when(z + hop <= 3)(lambda: act(z + hop))

    def landing(m, zz):
        return mlp_mine.at[pl.ds(pl.multiple_of(zz * rows, 16), rows), pl.ds(m * ff_part, ff_part)]

    def columns(m, zz):
        return (gate, up, down)[m].at[:, pl.ds(pl.multiple_of(zz * ff_part, 128), ff_part)]

    def swap(k, m, arriving=False):
        to = (z + k) % 4
        came = (z + 4 - k) % 4
        return remote(
            columns(m, to), landing(m, came if arriving else z), swap_send.at[k - 1, m], swap_recv.at[k - 1, m], (s, to)
        )

    local = [pltpu.make_async_copy(columns(m, z), landing(m, z), own_sem.at[m]) for m in range(3)]
    local.append(pltpu.make_async_copy(mixer, piece(s, z), own_sem.at[3]))

    pl.when(z < 3)(lambda: line(z, True, 0, mixer).start())
    pl.when(z > 0)(lambda: line(z, False, 0, mixer).start())
    spread(z, mixer)
    for copy in local:
        copy.start()
    line_hop(1)
    at_hop(1, spread)
    relay(z)
    line_hop(2)
    at_hop(2, spread)
    finish(z)
    at_hop(1, relay)
    line_hop(3)
    at_hop(3, spread)
    for k in (1, 3, 2):
        for m in range(3):
            swap(k, m).start()
    at_hop(1, finish)
    at_hop(2, relay)
    at_hop(3, relay)
    at_hop(2, finish)
    at_hop(3, finish)
    drain(z, mixer)
    for hop in range(1, 4):
        at_hop(hop, drain)
    for copy in local:
        copy.wait()
    for k in (1, 3, 2):
        for m in range(3):
            swap(k, m).wait_send()
            swap(k, m, True).wait_recv()
    pl.when(z < 3)(lambda: line(z, True, 0, mixer).wait_send())
    pl.when(z > 0)(lambda: line(z, False, 0, mixer).wait_send())
    for hop in range(1, 3):
        pl.when((z >= hop) & (z < 3))(lambda: line(z - hop, True, hop).wait_send())
        pl.when((z + hop <= 3) & (z > 0))(lambda: line(z + hop, False, hop).wait_send())


def gather(mixer, gate, up, down):
    rows, cols = mixer.shape
    ff_part = gate.shape[1] // 4
    anyspec = pl.BlockSpec(memory_space=pl.ANY)
    dma = pltpu.SemaphoreType.DMA
    return pl.pallas_call(
        gather_kernel,
        in_specs=[anyspec] * 4,
        out_specs=[anyspec] * 2,
        out_shape=[
            jax.ShapeDtypeStruct((32 * rows, cols), bf16),
            jax.ShapeDtypeStruct((4 * rows, 3 * ff_part), bf16),
        ],
        scratch_shapes=[
            dma((4, 9)), dma((4, 9)), dma((2, 3)), dma((2, 3)), dma((3, 3)), dma((3, 3)), dma((4,)),
        ],
        compiler_params=pltpu.CompilerParams(collective_id=1, has_side_effects=True),
        name="gather_weights",
    )(mixer, gate, up, down)


def add_columns(target, sources, start, size, step):
    def one(turn, carry):
        cols = pl.ds(pl.multiple_of(start + turn * step, 128), step)
        total = target[:, cols].astype(f32)
        for source in sources:
            total = total + source[:, cols].astype(f32)
        target[:, cols] = total.astype(target.dtype)
        return carry

    lax.fori_loop(0, size // step, one, 0)


def scatter_kernel(
    wide, outer, rest, mlp_pair, mlp_down, mixer_sum, mlp_back,
    held, cross, near, lined,
    load_sem, flow_send, flow_recv, line_send, line_recv, swap_send, swap_recv, own_sem,
):
    s, z, _, beside, across = places()
    chip, chip_beside, chip_across = s // 2, beside // 2, across // 2
    chip_diag = chip_beside + chip_across - chip
    rows = held.shape[1] // 4
    cols = held.shape[2]
    cut = cols // 256 * 128
    ff_part = mlp_down.shape[1]
    parts = (wide, outer, rest)
    order = (3 * (1 - z // 2), (2 + 3 * z) % 5, 1 + z % 2, z)

    def remote(src, dst, send, recv, target):
        return pltpu.make_async_remote_copy(
            src_ref=src, dst_ref=dst, send_sem=send, recv_sem=recv, device_id=target, device_id_type=MESH
        )

    def span(k):
        return pl.ds(pl.multiple_of(k * rows, 16), rows)

    def loads(i):
        copies, start = [], 0
        for n, part in enumerate(parts):
            size = part.shape[2]
            copies.append(
                pltpu.make_async_copy(
                    part.at[:, span(order[i]), :], held.at[:, span(order[i]), pl.ds(start, size)], load_sem.at[i, n]
                )
            )
            start += size
        return copies

    left, right = pl.ds(0, cut), pl.ds(cut, cols - cut)

    def block(q, i, side):
        return held.at[q, span(order[i]), side]

    def flow(i, index):
        send, recv = flow_send.at[i, index], flow_recv.at[i, index]
        to_beside, to_across = (beside, z), (across, z)
        if index == 0:
            return remote(block(chip_diag, i, left), cross.at[i, :, left], send, recv, to_across)
        if index == 1:
            return remote(block(chip_diag, i, right), cross.at[i, :, right], send, recv, to_beside)
        if index == 2:
            return remote(block(chip_beside, i, right), near.at[0, i, :, right], send, recv, to_beside)
        if index == 3:
            return remote(block(chip_beside, i, left), near.at[0, i, :, left], send, recv, to_beside)
        if index == 4:
            return remote(block(chip_across, i, left), near.at[1, i, :, left], send, recv, to_across)
        return remote(block(chip_across, i, right), near.at[1, i, :, right], send, recv, to_across)

    def cross_step(i):
        flow(i, 0).wait_recv()
        add_columns(held.at[chip_beside, span(order[i]), :], [cross.at[i]], 0, cut, 512)
        flow(i, 3).start()
        flow(i, 1).wait_recv()
        add_columns(held.at[chip_across, span(order[i]), :], [cross.at[i]], cut, cols - cut, 384)
        flow(i, 5).start()

    def near_step(i):
        for index in (2, 4, 3, 5):
            flow(i, index).wait_recv()
        add_columns(held.at[chip, span(order[i]), :], [near.at[0, i], near.at[1, i]], 0, cols, 640)

    def line(k, slot, target):
        return remote(
            held.at[chip, span(k), :], lined.at[slot], line_send.at[k], line_recv.at[slot], (s, target)
        )

    def absorb(k, slot, source):
        line(k, slot, source).wait_recv()
        add_columns(held.at[chip, span(k), :], [lined.at[slot]], 0, cols, 640)

    def chain(i):
        k = order[i]
        if i == 3:
            pl.when(z > 0)(lambda: absorb(k, k, z - 1))
            pl.when(z < 3)(lambda: absorb(k, 4, z + 1))
            return

        @pl.when(k > z)
        def _():
            pl.when(z > 0)(lambda: absorb(k, k, z - 1))
            line(k, k, z + 1).start()

        @pl.when(k < z)
        def _():
            pl.when(z < 3)(lambda: absorb(k, k, z + 1))
            pl.when(k == z - 1)(lambda: line(k, 4, z - 1).start())
            pl.when(k < z - 1)(lambda: line(k, k, z - 1).start())

    def chain_drain():
        for i in range(3):
            k = order[i]
            line(k, k, (z + 1) % 4).wait_send()

    def pieces():
        for m in range(3):
            source = mlp_down if m == 2 else mlp_pair
            yield m, source, pl.ds(0 if m == 2 else m * ff_part, ff_part)

    def swap(k):
        to = (z + k) % 4
        here = pl.ds(pl.multiple_of(z * ff_part, 128), ff_part)
        return [
            remote(
                source.at[span(to), at], mlp_back.at[m, :, here], swap_send.at[k - 1, m], swap_recv.at[k - 1, m], (s, to)
            )
            for m, source, at in pieces()
        ]

    own = [
        pltpu.make_async_copy(
            source.at[span(z), at], mlp_back.at[m, :, pl.ds(pl.multiple_of(z * ff_part, 128), ff_part)], own_sem.at[m]
        )
        for m, source, at in pieces()
    ]
    for i in range(4):
        for copy in loads(i):
            copy.start()
    greet([(beside, z), (across, z)] + [(s, (z + k) % 4) for k in range(1, 4)])
    for k in (1, 3, 2):
        for copy in swap(k):
            copy.start()
    for copy in own:
        copy.start()
    for i in range(2):
        for copy in loads(i):
            copy.wait()
        flow(i, 0).start()
        flow(i, 1).start()
        if i == 0:
            flow(i, 2).start()
            flow(i, 4).start()
    for i in range(4):
        cross_step(i)
        if i + 1 < 4:
            flow(i + 1, 2).start()
            flow(i + 1, 4).start()
        if i + 2 < 4:
            for copy in loads(i + 2):
                copy.wait()
            flow(i + 2, 0).start()
            flow(i + 2, 1).start()
        if i > 0:
            near_step(i - 1)
            chain(i - 1)
    near_step(3)
    chain(3)
    done = pltpu.make_async_copy(held.at[chip, span(z), :], mixer_sum, own_sem.at[3])
    done.start()
    for i in range(4):
        for index in range(6):
            flow(i, index).wait_send()
    chain_drain()
    for k in range(1, 4):
        for copy in swap(k):
            copy.wait()
    for copy in own:
        copy.wait()
    done.wait()


def scatter(wide, outer, rest, mlp_pair, mlp_down):
    rows = wide.shape[1] // 4
    cols = wide.shape[2] + outer.shape[2] + rest.shape[2]
    ff_part = mlp_down.shape[1]
    anyspec = pl.BlockSpec(memory_space=pl.ANY)
    dma = pltpu.SemaphoreType.DMA
    return pl.pallas_call(
        scatter_kernel,
        in_specs=[anyspec] * 5,
        out_specs=[anyspec] * 2,
        out_shape=[
            jax.ShapeDtypeStruct((rows, cols), bf16),
            jax.ShapeDtypeStruct((3, rows, 4 * ff_part), bf16),
        ],
        scratch_shapes=[
            pltpu.VMEM((4, 4 * rows, cols), bf16),
            pltpu.VMEM((4, rows, cols), bf16),
            pltpu.VMEM((2, 4, rows, cols), bf16),
            pltpu.VMEM((5, rows, cols), bf16),
            dma((4, 3)), dma((4, 6)), dma((4, 6)), dma((4,)), dma((5,)), dma((3, 3)), dma((3, 3)), dma((4,)),
        ],
        compiler_params=pltpu.CompilerParams(
            collective_id=2, has_side_effects=True, vmem_limit_bytes=52 * 1024 * 1024
        ),
        name="scatter_gradients",
    )(wide, outer, rest, mlp_pair, mlp_down)


def gather_plain(mixer, gate, up, down):
    groups = lax.axis_size("fsdp")
    part_rows, ff = gate.shape
    own = jnp.stack([w.reshape(part_rows, groups, ff // groups) for w in (gate, up, down)], axis=2)
    mine = lax.all_to_all(jnp.transpose(own, (1, 0, 2, 3)), "fsdp", 0, 0, tiled=True)
    return lax.all_gather(mixer, both, axis=0, tiled=True), mine.reshape(groups * part_rows, -1)


def along_line(shard):
    count = lax.axis_size("fsdp")
    rows = shard.shape[0]
    below, above = [shard], [shard]
    for _ in range(count - 1):
        below.append(from_behind(below[-1], "fsdp", 1))
        above.append(from_behind(above[-1], "fsdp", -1))
    pieces = jnp.concatenate(below[:0:-1] + above, axis=0)
    start = (count - 1 - lax.axis_index("fsdp")) * rows
    return lax.dynamic_slice_in_dim(pieces, start, count * rows, 0)


def swap_cores(shard):
    count = lax.axis_size("seq")
    return lax.ppermute(shard, "seq", [(i, i + 1 - 2 * (i % 2)) for i in range(count)])


def swap_beside(shard):
    return lax.ppermute(shard, "seq", [(i, i ^ 2) for i in range(8)])


def swap_across(shard):
    return lax.ppermute(shard, "seq", [(i, i ^ 4) for i in range(8)])


def pairs(shard):
    return jnp.concatenate([shard, swap_cores(shard)], axis=0)


def partial_blocks(left, right):
    place = lax.axis_index("seq")
    blocks = jnp.transpose(left).reshape(lax.axis_size("seq"), -1, left.shape[0])
    rows = blocks.shape[1]
    half = rows // 2
    core, beside, across = place % 2, (place // 2) % 2, place // 4

    def block(flip_beside, flip_across, start, size):
        x = 1 - beside if flip_beside else beside
        y = 1 - across if flip_across else across
        chosen = lax.dynamic_slice(
            blocks, (y * 4 + x * 2 + core, start, 0), (1, size, blocks.shape[2])
        )[0]
        return mm(chosen, right, ((1,), (0,))).astype(bf16)

    return (
        block(True, True, 0, half),
        block(True, True, half, half),
        block(True, False, half, half),
        block(False, True, 0, half),
        block(True, False, 0, half),
        block(False, True, half, half),
        block(False, False, 0, rows),
    )


def sum_blocks(blocks):
    diag_low, diag_high, beside_high, across_low, beside_low, across_high, mine = blocks
    by_across = swap_across(diag_low)
    by_beside = swap_beside(diag_high)
    from_beside_high = swap_beside(beside_high)
    from_across_low = swap_across(across_low)
    from_beside_low = swap_beside((beside_low.astype(f32) + by_across.astype(f32)).astype(bf16))
    from_across_high = swap_across((across_high.astype(f32) + by_beside.astype(f32)).astype(bf16))
    half = diag_low.shape[0]
    low = mine[:half].astype(f32) + from_across_low.astype(f32) + from_beside_low.astype(f32)
    high = mine[half:].astype(f32) + from_across_high.astype(f32) + from_beside_high.astype(f32)
    return jnp.concatenate([low.astype(bf16), high.astype(bf16)], axis=0)


def scatter_paired(normed, grad_both, grad_mix, mixed, rest, pair_sum, down_sum):
    core = lax.axis_index("seq") % 2
    chips = lax.axis_size("seq") // 2

    def halves(values, which):
        grouped = values.reshape(values.shape[0], chips, 2, values.shape[1] // (2 * chips))
        return lax.dynamic_index_in_dim(grouped, which, 2, False).reshape(values.shape[0], -1)

    def product(left, right):
        result = mm(halves(left, core), right, ((0,), (0,))).astype(bf16)
        return result.reshape(chips, -1, right.shape[1])

    wide = product(pairs(normed), pairs(grad_both))
    outer = product(pairs(grad_mix), pairs(mixed))
    grouped = rest.reshape(chips, 2, -1, rest.shape[1])
    own = lax.dynamic_index_in_dim(grouped, core, 1, False)
    other = swap_cores(lax.dynamic_index_in_dim(grouped, 1 - core, 1, False))
    rest = (own.astype(f32) + other.astype(f32)).astype(bf16)
    return scatter(wide, outer, rest, pair_sum, down_sum)


def scatter_plain(normed, grad_both, grad_mix, mixed, rest, pair_sum, down_sum):
    groups = lax.axis_size("fsdp")
    term_wide = mm(normed, grad_both, ((0,), (0,))).astype(bf16)
    term_out = mm(grad_mix, mixed, ((0,), (0,))).astype(bf16)
    mixer_sum = lax.psum_scatter(
        jnp.concatenate([term_wide, term_out, rest], axis=1), "seq", scatter_dimension=0, tiled=True
    )
    mixer_sum = lax.psum_scatter(mixer_sum, "fsdp", scatter_dimension=0, tiled=True)
    ff_part = down_sum.shape[1]
    part_rows = down_sum.shape[0] // groups
    mlp_sum = jnp.concatenate([pair_sum, down_sum], axis=1).reshape(groups, part_rows, 3, ff_part)
    mlp_back = lax.all_to_all(mlp_sum, "fsdp", 0, 0, tiled=True)
    mlp_back = jnp.transpose(mlp_back, (2, 1, 0, 3)).reshape(3, part_rows, groups * ff_part)
    return mixer_sum, mlp_back


def call_heads(kernel, width, heads, ins, outs, scratch, name):
    def spec(rows_cols):
        rows, by_row = rows_cols
        if by_row:
            return pl.BlockSpec((rows, width), lambda h: (h, 0))
        return pl.BlockSpec((rows, width), lambda h: (0, h))

    in_specs = [spec((width, True)) if rowwise else spec((a.shape[0], False)) for a, rowwise in ins]
    out_specs = [spec((width, True)) if rowwise else spec((rows, False)) for rows, _, rowwise in outs]
    out_shape = [
        jax.ShapeDtypeStruct((heads * width, width) if rowwise else (rows, heads * width), kind)
        for rows, kind, rowwise in outs
    ]
    return pl.pallas_call(
        kernel,
        grid=(heads,),
        in_specs=in_specs,
        out_specs=out_specs,
        out_shape=out_shape,
        scratch_shapes=[pltpu.VMEM((rows, width), f32) for rows in scratch],
        compiler_params=pltpu.CompilerParams(vmem_limit_bytes=40 * 1024 * 1024),
        name=name,
    )(*[a for a, _ in ins])


def on_device(
    block_input,
    cotangent,
    mixer_gain,
    branch_proj,
    gelu_proj,
    conv_taps,
    conv_bias,
    rate_blocks,
    input_blocks,
    rate_bias,
    input_bias,
    decay_param,
    out_proj,
    mlp_gain,
    gate_proj,
    up_proj,
    down_proj,
):
    groups = lax.axis_size("fsdp")
    part_rows, lru = branch_proj.shape
    width = rate_blocks.shape[1]
    heads = lru // width
    margin = conv_taps.shape[0] - 1
    tokens = block_input[0].astype(f32)
    tok_count, model = tokens.shape
    ff = gate_proj.shape[1]
    ff_part = ff // groups
    grad_out = cotangent[0]

    smalls = jnp.stack(
        [conv_taps[k] for k in range(margin + 1)]
        + [conv_bias, rate_bias, input_bias, decay_param, mixer_gain, mlp_gain],
        axis=1,
    )
    small_count = smalls.shape[1]
    smalls = jnp.pad(smalls, ((0, 0), (0, 128 - small_count)))
    mixer_own = jnp.concatenate(
        [smalls, rate_blocks, input_blocks, branch_proj, gelu_proj, out_proj], axis=1
    )
    custom = lax.axis_size("seq") == 8 and groups == 4
    if custom:
        mixer_w, mlp_mine = gather(mixer_own, gate_proj, up_proj, down_proj)
    else:
        mixer_w, mlp_mine = gather_plain(mixer_own, gate_proj, up_proj, down_proj)
    mlp_w = lax.all_gather(mlp_mine, "seq", axis=0, tiled=True)
    grad_out_late = lax.optimization_barrier((grad_out, mlp_mine))[0]
    grad_out_all = along_line(grad_out_late)
    first = lax.optimization_barrier(mixer_w[:, : 128 + 2 * width])
    wide = mixer_w[:, 128 + 2 * width : 128 + 2 * width + 2 * lru]
    proj_out = mixer_w[:, 128 + 2 * width + 2 * lru :]

    table = first[:, :small_count].astype(f32).T
    blocks_rate = first[:, 128 : 128 + width]
    blocks_input = first[:, 128 + width :]
    param_decay = table[margin + 4]
    gain_one = table[margin + 5]
    gain_two = table[margin + 6]
    small = jnp.concatenate(
        [
            table[: margin + 4],
            jax.nn.softplus(-param_decay)[None],
            -jax.nn.sigmoid(-param_decay)[None],
            jnp.zeros((16 - margin - 6, lru), f32),
        ],
        axis=0,
    )

    normed = norm_rows(tokens, gain_one).astype(bf16)
    both_pre = mm(normed, wide, ((1,), (0,)))
    branch = both_pre[:, :lru].astype(bf16)
    gelu_pre = both_pre[:, lru:]
    prior = from_behind(branch[tok_count - margin :], "seq", 1).astype(f32)
    prior = jnp.concatenate([jnp.zeros((8 - margin, lru), f32), prior], axis=0)
    conv, rate_pre, input_pre, cum, local = call_heads(
        mixer_forward,
        width,
        heads,
        [(branch, False), (prior, False), (small, False), (blocks_rate, True), (blocks_input, True)],
        [(tok_count, bf16, False)] + [(tok_count, f32, False)] * 4,
        [tok_count + 8],
        "mixer_forward",
    )
    carried = prefix((cum[-1], local[-1]), "seq", False)
    states = local + cum * carried[None]
    mixed = (states * jax.nn.gelu(gelu_pre, approximate=True)).astype(bf16)
    middle = tokens + mm(mixed, proj_out, ((1,), (1,)))
    normed_two = norm_rows(middle, gain_two).astype(bf16)

    normed_all = along_line(normed_two)
    w_gate, w_up, w_down = mlp_w[:, :ff_part], mlp_w[:, ff_part : 2 * ff_part], mlp_w[:, 2 * ff_part :]
    gate = mm(normed_all, w_gate, ((1,), (0,)))
    up_val = mm(normed_all, w_up, ((1,), (0,)))
    gelu_gate, gelu_slope = gelu_parts(gate)
    hidden = (gelu_gate * up_val).astype(bf16)
    grad_hidden = mm(grad_out_all, w_down, ((1,), (0,)))
    grad_gate = (grad_hidden * up_val * gelu_slope).astype(bf16)
    grad_up = (grad_hidden * gelu_gate).astype(bf16)
    grad_pair = jnp.concatenate([grad_gate, grad_up], axis=1)
    grad_normed_part = mm(grad_gate, w_gate, ((1,), (1,))) + mm(grad_up, w_up, ((1,), (1,)))
    grad_normed_two = lax.psum_scatter(
        grad_normed_part.astype(bf16), "fsdp", scatter_dimension=0, tiled=True
    )
    out_part = mm(hidden, w_down, ((1,), (1,))).astype(bf16)
    if custom:
        pair_blocks = partial_blocks(pairs(normed_all), pairs(grad_pair))
        down_blocks = partial_blocks(pairs(grad_out_all), pairs(hidden))
        pair_blocks, down_blocks, grad_normed_two = lax.optimization_barrier(
            (pair_blocks, down_blocks, grad_normed_two)
        )
        pair_sum, down_sum = sum_blocks(pair_blocks), sum_blocks(down_blocks)
    else:
        term_pair = mm(normed_all, grad_pair, ((0,), (0,))).astype(bf16)
        term_down = mm(grad_out_all, hidden, ((0,), (0,))).astype(bf16)
        pair_sum = lax.psum_scatter(term_pair, "seq", scatter_dimension=0, tiled=True)
        down_sum = lax.psum_scatter(term_down, "seq", scatter_dimension=0, tiled=True)
    out_sum = lax.psum_scatter(out_part, "fsdp", scatter_dimension=0, tiled=True)
    block_output = (middle + out_sum.astype(f32)).astype(bf16)[None]
    grad_normed_two = grad_normed_two.astype(f32)

    second_pull = jax.vjp(norm_rows, middle, gain_two)[1]
    grad_mid_part, grad_gain_two = second_pull(grad_normed_two)
    grad_middle = grad_out.astype(f32) + grad_mid_part
    grad_mix = grad_middle.astype(bf16)
    grad_mixed = mm(grad_mix, proj_out, ((1,), (0,)))
    carried_rows = jnp.broadcast_to(carried[None], (8, lru))
    grad_gelu_pre, rev_cum, rev_grad, pair_grad = call_heads(
        mixer_backward_scan,
        width,
        heads,
        [(a, False) for a in (grad_mixed, gelu_pre, rate_pre, cum, local, carried_rows, small)],
        [(tok_count, bf16, False), (tok_count, f32, False), (tok_count, f32, False), (8, f32, False)],
        [tok_count + 8],
        "mixer_backward_scan",
    )
    incoming = prefix((cum[-1], pair_grad[0]), "seq", True)
    incoming_rows = jnp.broadcast_to(incoming[None], (8, lru))
    own, head, rate_w_grad, input_w_grad, sums = call_heads(
        mixer_backward,
        width,
        heads,
        [
            (a, False)
            for a in (rev_cum, rev_grad, incoming_rows, cum, local, carried_rows, rate_pre, input_pre, conv, branch, prior, small)
        ]
        + [(blocks_rate, True), (blocks_input, True)],
        [(tok_count, f32, False), (8, f32, False), (0, bf16, True), (0, bf16, True), (8, f32, False)],
        [tok_count + 8, tok_count + 16],
        "mixer_backward",
    )
    received = from_behind(head[8 - margin :], "seq", -1)
    grad_branch = jnp.concatenate(
        [own[: tok_count - margin], own[tok_count - margin :] + received], axis=0
    ).astype(bf16)
    grad_both = jnp.concatenate([grad_branch, grad_gelu_pre], axis=1)
    grad_normed = mm(grad_both, wide, ((1,), (1,)))
    first_pull = jax.vjp(norm_rows, tokens, gain_one)[1]
    grad_tok_part, grad_gain_one = first_pull(grad_normed)
    input_grad = (grad_middle + grad_tok_part).astype(bf16)[None]
    vectors = jnp.concatenate([sums, grad_gain_one[None], grad_gain_two[None]], axis=0).T
    vectors = jnp.pad(vectors, ((0, 0), (0, 128 - vectors.shape[1]))).astype(bf16)
    rest = jnp.concatenate([rate_w_grad, input_w_grad, vectors], axis=1)
    scatter_all = scatter_paired if custom else scatter_plain
    mixer_sum, mlp_back = scatter_all(normed, grad_both, grad_mix, mixed, rest, pair_sum, down_sum)
    mlp_grads = [mlp_back[m].astype(f32) for m in range(3)]
    mixer_sum = mixer_sum.astype(f32)
    edges = [lru, 2 * lru, 3 * lru, 3 * lru + width, 3 * lru + 2 * width]
    dbranch, dgelu, dout, drate, dinput, vec = jnp.split(mixer_sum, edges, axis=1)
    vec = vec.T
    return (
        block_output,
        input_grad,
        vec[8],
        dbranch,
        dgelu,
        vec[: margin + 1],
        vec[7],
        drate,
        dinput,
        vec[4],
        vec[5],
        vec[6],
        dout,
        vec[9],
        mlp_grads[0],
        mlp_grads[1],
        mlp_grads[2],
    )


def solution(mesh):
    tokens = P("fsdp", "seq", None)
    vector = P(both)
    matrix = P(both, None)
    taps = P(None, both)
    return jax.shard_map(
        on_device,
        mesh=mesh,
        in_specs=(
            tokens, tokens, vector, matrix, matrix, taps, vector, matrix, matrix,
            vector, vector, vector, matrix, vector, matrix, matrix, matrix,
        ),
        out_specs=(
            tokens, tokens, vector, matrix, matrix, taps, vector, matrix, matrix,
            vector, vector, vector, matrix, vector, matrix, matrix, matrix,
        ),
        check_vma=False,
    )
```

```python
import functools

import jax
import jax.numpy as jnp
from jax import lax
from jax.experimental import pallas as pl
from jax.experimental.pallas import tpu as pltpu
from jax.sharding import PartitionSpec as P

epsilon = 1e-06
f32 = jnp.float32
bf16 = jnp.bfloat16
both = ("seq", "fsdp")
MESH = pl.DeviceIdType.MESH
TAP, CONV_BIAS, RATE_BIAS, INPUT_BIAS, SOFT, SOFT_SLOPE = 0, 4, 5, 6, 7, 8
GELU_C = 0.7978845608028654
GELU_A = 0.044715


def from_behind(shard, axis, by):
    devices = lax.axis_size(axis)
    pairs = [(i, i + by) for i in range(devices) if 0 <= i + by < devices]
    return lax.ppermute(shard, axis, pairs)


def prefix(part, axis, reverse):
    count = lax.axis_size(axis)
    place = lax.axis_index(axis)
    gathered = lax.all_gather(jnp.stack(part), axis)
    state = jnp.zeros_like(part[1])
    for hop in range(count):
        source = count - 1 - hop if reverse else hop
        ahead = source > place if reverse else source < place
        state = jnp.where(ahead, gathered[source, 1] + gathered[source, 0] * state, state)
    return state


def norm_rows(values, scales):
    return values * lax.rsqrt(jnp.mean(values * values, axis=-1, keepdims=True) + epsilon) * scales


def gelu_parts(x):
    inner = jnp.tanh(GELU_C * (x + GELU_A * x * x * x))
    return 0.5 * x * (1.0 + inner), 0.5 * (1.0 + inner) + 0.5 * x * (1.0 - inner * inner) * (
        GELU_C * (1.0 + 3.0 * GELU_A * x * x)
    )


def mm(left, right, dims):
    return lax.dot_general(left, right, (dims, ((), ())), preferred_element_type=f32)


def sigmoid(x):
    return 1.0 / (1.0 + jnp.exp(-x))


def scan_rows(decay, value, reverse):
    rows = decay.shape[0]
    place = lax.broadcasted_iota(jnp.int32, decay.shape, 0)
    step = 1
    while step < rows:
        shift = rows - step if reverse else step
        inside = place < rows - step if reverse else place >= step
        before_value = jnp.where(inside, pltpu.roll(value, shift, 0), 0.0)
        before_decay = jnp.where(inside, pltpu.roll(decay, shift, 0), 1.0)
        value = value + decay * before_value
        decay = decay * before_decay
        step *= 2
    return decay, value


def gates(rate_pre, input_pre, soft):
    rate = sigmoid(rate_pre)
    log_decay = -8.0 * rate * soft
    decay = jnp.exp(log_decay)
    square = decay * decay
    root = jnp.sqrt(-jnp.tanh(log_decay) * (1.0 + square))
    return rate, decay, square, root, sigmoid(input_pre)


def mixer_forward(branch, prior, small, rate_w, input_w, conv, rate_pre, input_pre, cum, local, ext):
    rows = branch.shape[0]
    ext[0:8, :] = prior[...]
    ext[8:, :] = branch[...].astype(f32)
    total = small[CONV_BIAS : CONV_BIAS + 1, :] + small[TAP : TAP + 1, :] * ext[8:, :]
    for offset in range(1, 4):
        total = total + small[TAP + offset : TAP + offset + 1, :] * ext[pl.ds(8 - offset, rows), :]
    low = total.astype(bf16)
    conv[...] = low
    rate = mm(low, rate_w[...], ((1,), (0,))) + small[RATE_BIAS : RATE_BIAS + 1, :]
    inp = mm(low, input_w[...], ((1,), (0,))) + small[INPUT_BIAS : INPUT_BIAS + 1, :]
    rate_pre[...] = rate
    input_pre[...] = inp
    _, decay, _, root, opened = gates(rate, inp, small[SOFT : SOFT + 1, :])
    product, states = scan_rows(decay, root * opened * low.astype(f32), False)
    cum[...] = product
    local[...] = states


def mixer_backward_scan(grad_mixed, gelu_pre, rate_pre, cum, local, carried, small, grad_pre, rev_cum, rev_grad, pair, ext):
    rows = grad_mixed.shape[0]
    states = local[...] + cum[...] * carried[0:1, :]
    value, slope = gelu_parts(gelu_pre[...])
    grad = grad_mixed[...]
    grad_pre[...] = (grad * states * slope).astype(bf16)
    decay = jnp.exp(-8.0 * sigmoid(rate_pre[...]) * small[SOFT : SOFT + 1, :])
    ext[0:rows, :] = decay
    ext[rows:, :] = jnp.ones((8, decay.shape[1]), f32)
    product, back = scan_rows(ext[pl.ds(1, rows), :], grad * value, True)
    rev_cum[...] = product
    rev_grad[...] = back
    pair[...] = jnp.broadcast_to(decay[0:1, :] * back[0:1, :], pair.shape)


def mixer_backward(
    rev_cum, rev_grad, incoming, cum, local, carried, rate_pre, input_pre, conv, branch, prior, small, rate_w, input_w,
    own, head, rate_w_grad, input_w_grad, sums, ext, gext,
):
    rows = rev_cum.shape[0]
    soft = small[SOFT : SOFT + 1, :]
    grad_states = rev_grad[...] + rev_cum[...] * incoming[0:1, :]
    rate, decay, square, root, opened = gates(rate_pre[...], input_pre[...], soft)
    ext[0:8, :] = jnp.broadcast_to(carried[0:1, :], (8, carried.shape[1]))
    ext[8:, :] = local[...] + cum[...] * carried[0:1, :]
    before = ext[pl.ds(7, rows), :]
    low = conv[...]
    conv_in = low.astype(f32)
    grad_log = grad_states * decay * before - grad_states * opened * conv_in * square / root
    driven = grad_states * root
    grad_input = (driven * conv_in * opened * (1.0 - opened)).astype(bf16)
    by_rate = grad_log * (-8.0 * rate)
    grad_rate = (by_rate * soft * (1.0 - rate)).astype(bf16)
    sums[6:7, :] = jnp.sum(by_rate, axis=0, keepdims=True) * small[SOFT_SLOPE : SOFT_SLOPE + 1, :]
    sums[4:5, :] = jnp.sum(grad_rate.astype(f32), axis=0, keepdims=True)
    sums[5:6, :] = jnp.sum(grad_input.astype(f32), axis=0, keepdims=True)
    rate_w_grad[...] = mm(low, grad_rate, ((0,), (0,))).astype(rate_w_grad.dtype)
    input_w_grad[...] = mm(low, grad_input, ((0,), (0,))).astype(input_w_grad.dtype)
    grad_conv = (
        driven * opened
        + mm(grad_rate, rate_w[...], ((1,), (1,)))
        + mm(grad_input, input_w[...], ((1,), (1,)))
    )
    sums[7:8, :] = jnp.sum(grad_conv, axis=0, keepdims=True)
    ext[0:8, :] = prior[...]
    ext[8:, :] = branch[...].astype(f32)
    gext[0:8, :] = jnp.zeros((8, grad_conv.shape[1]), f32)
    gext[8 : 8 + rows, :] = grad_conv
    gext[8 + rows :, :] = jnp.zeros((8, grad_conv.shape[1]), f32)
    back = jnp.zeros_like(grad_conv)
    front = jnp.zeros((8, grad_conv.shape[1]), f32)
    for offset in range(4):
        tap = small[TAP + offset : TAP + offset + 1, :]
        sums[offset : offset + 1, :] = jnp.sum(
            grad_conv * ext[pl.ds(8 - offset, rows), :], axis=0, keepdims=True
        )
        back = back + tap * gext[pl.ds(8 + offset, rows), :]
        front = front + tap * gext[pl.ds(offset, 8), :]
    own[...] = back
    head[...] = front


def places():
    s = lax.axis_index("seq")
    z = lax.axis_index("fsdp")
    core = s + 1 - 2 * (s % 2)
    beside = s + 2 - 4 * ((s // 2) % 2)
    across = s + 4 - 8 * (s // 4)
    return s, z, core, beside, across


def greet(peers):
    barrier = pltpu.get_barrier_semaphore()
    for peer in peers:
        pl.semaphore_signal(barrier, inc=1, device_id=peer, device_id_type=MESH)
    pl.semaphore_wait(barrier, len(peers))


def gather_kernel(
    mixer, gate, up, down, mixer_all, mlp_mine,
    flow_send, flow_recv, line_send, line_recv, swap_send, swap_recv, own_sem,
):
    s, z, core, beside, across = places()
    rows, cols = mixer.shape
    ff_part = mlp_mine.shape[1] // 3
    cut = cols // 256 * 128
    diag = beside + across - s
    greet([(core, z), (beside, z), (across, z)] + [(s, (z + k) % 4) for k in range(1, 4)])

    def remote(src, dst, send, recv, target):
        return pltpu.make_async_remote_copy(
            src_ref=src, dst_ref=dst, send_sem=send, recv_sem=recv, device_id=target, device_id_type=MESH
        )

    def piece(seq, zz, half=None):
        span = pl.ds(pl.multiple_of((seq * 4 + zz) * rows, 16), rows)
        if half is None:
            return mixer_all.at[span, :]
        return mixer_all.at[span, pl.ds(0, cut) if half == 0 else pl.ds(cut, cols - cut)]

    def flow(zz, index, seq, half, target, src=None):
        ref = piece(seq, zz, half)
        return remote(
            ref if src is None else src, ref, flow_send.at[zz, index], flow_recv.at[zz, index], (target, z)
        )

    def sends(zz, src=None):
        return [
            flow(zz, 0, s, None, beside, src),
            flow(zz, 1, s, None, across, src),
            flow(zz, 4, s, None, core, src),
        ]

    def spread(zz, src=None):
        for copy in sends(zz, src):
            copy.start()

    def relay(zz):
        flow(zz, 0, beside, None, beside).wait_recv()
        flow(zz, 3, beside, 0, across).start()
        flow(zz, 5, beside, None, core).start()
        flow(zz, 1, across, None, across).wait_recv()
        flow(zz, 2, across, 1, beside).start()
        flow(zz, 6, across, None, core).start()

    def finish(zz):
        flow(zz, 3, diag, 0, across).wait_recv()
        flow(zz, 7, diag, 0, core).start()
        flow(zz, 2, diag, 1, beside).wait_recv()
        flow(zz, 8, diag, 1, core).start()

    def drain(zz, src=None):
        for copy in sends(zz, src):
            copy.wait_send()
        flow(zz, 3, beside, 0, across).wait_send()
        flow(zz, 5, beside, None, core).wait_send()
        flow(zz, 2, across, 1, beside).wait_send()
        flow(zz, 6, across, None, core).wait_send()
        flow(zz, 7, diag, 0, core).wait_send()
        flow(zz, 8, diag, 1, core).wait_send()
        flip = core - s
        flow(zz, 4, core, None, core).wait_recv()
        flow(zz, 5, beside + flip, None, core).wait_recv()
        flow(zz, 6, across + flip, None, core).wait_recv()
        flow(zz, 7, diag + flip, 0, core).wait_recv()
        flow(zz, 8, diag + flip, 1, core).wait_recv()

    def line(zz, up_way, hop, src=None):
        ref = piece(s, zz)
        way = 0 if up_way else 1
        target = z + 1 if up_way else z - 1
        return remote(
            ref if src is None else src, ref, line_send.at[way, hop], line_recv.at[way, hop], (s, target)
        )

    def line_hop(hop):
        def below():
            line(z - hop, True, hop - 1).wait_recv()
            pl.when(z < 3)(lambda: line(z - hop, True, hop).start())

        def above():
            line(z + hop, False, hop - 1).wait_recv()
            pl.when(z > 0)(lambda: line(z + hop, False, hop).start())

        pl.when(z >= hop)(below)
        pl.when(z + hop <= 3)(above)

    def at_hop(hop, act):
        pl.when(z >= hop)(lambda: act(z - hop))
        pl.when(z + hop <= 3)(lambda: act(z + hop))

    def landing(m, zz):
        return mlp_mine.at[pl.ds(pl.multiple_of(zz * rows, 16), rows), pl.ds(m * ff_part, ff_part)]

    def columns(m, zz):
        return (gate, up, down)[m].at[:, pl.ds(pl.multiple_of(zz * ff_part, 128), ff_part)]

    def swap(k, m, arriving=False):
        to = (z + k) % 4
        came = (z + 4 - k) % 4
        return remote(
            columns(m, to), landing(m, came if arriving else z), swap_send.at[k - 1, m], swap_recv.at[k - 1, m], (s, to)
        )

    local = [pltpu.make_async_copy(columns(m, z), landing(m, z), own_sem.at[m]) for m in range(3)]
    local.append(pltpu.make_async_copy(mixer, piece(s, z), own_sem.at[3]))

    pl.when(z < 3)(lambda: line(z, True, 0, mixer).start())
    pl.when(z > 0)(lambda: line(z, False, 0, mixer).start())
    spread(z, mixer)
    for copy in local:
        copy.start()
    line_hop(1)
    at_hop(1, spread)
    relay(z)
    line_hop(2)
    at_hop(2, spread)
    finish(z)
    at_hop(1, relay)
    line_hop(3)
    at_hop(3, spread)
    for k in (1, 3, 2):
        for m in range(3):
            swap(k, m).start()
    at_hop(1, finish)
    at_hop(2, relay)
    at_hop(3, relay)
    at_hop(2, finish)
    at_hop(3, finish)
    drain(z, mixer)
    for hop in range(1, 4):
        at_hop(hop, drain)
    for copy in local:
        copy.wait()
    for k in (1, 3, 2):
        for m in range(3):
            swap(k, m).wait_send()
            swap(k, m, True).wait_recv()
    pl.when(z < 3)(lambda: line(z, True, 0, mixer).wait_send())
    pl.when(z > 0)(lambda: line(z, False, 0, mixer).wait_send())
    for hop in range(1, 3):
        pl.when((z >= hop) & (z < 3))(lambda: line(z - hop, True, hop).wait_send())
        pl.when((z + hop <= 3) & (z > 0))(lambda: line(z + hop, False, hop).wait_send())


def gather(mixer, gate, up, down):
    rows, cols = mixer.shape
    ff_part = gate.shape[1] // 4
    anyspec = pl.BlockSpec(memory_space=pl.ANY)
    dma = pltpu.SemaphoreType.DMA
    return pl.pallas_call(
        gather_kernel,
        in_specs=[anyspec] * 4,
        out_specs=[anyspec] * 2,
        out_shape=[
            jax.ShapeDtypeStruct((32 * rows, cols), bf16),
            jax.ShapeDtypeStruct((4 * rows, 3 * ff_part), bf16),
        ],
        scratch_shapes=[
            dma((4, 9)), dma((4, 9)), dma((2, 3)), dma((2, 3)), dma((3, 3)), dma((3, 3)), dma((4,)),
        ],
        compiler_params=pltpu.CompilerParams(collective_id=1, has_side_effects=True),
        name="gather_weights",
    )(mixer, gate, up, down)


def rows_kernel(
    normed, grad0, grad1, grad2, grad3, normed_all, normed_other, grad_all, grad_other,
    line_send, line_recv, core_send, core_recv, own_sem,
):
    s, z, core, _, _ = places()
    tok = normed.shape[0]
    grads = (grad0, grad1, grad2, grad3)
    greet([(core, z)] + [(s, (z + k) % 4) for k in range(1, 4)])

    def rows(ref, zz):
        return ref.at[pl.ds(pl.multiple_of(zz * tok, 16), tok), :]

    def remote(src, dst, send, recv, target):
        return pltpu.make_async_remote_copy(
            src_ref=src, dst_ref=dst, send_sem=send, recv_sem=recv, device_id=target, device_id_type=MESH
        )

    def line(zz, up_way, hop):
        way = 0 if up_way else 1
        target = z + 1 if up_way else z - 1
        src = normed if hop == 0 else rows(normed_all, zz)
        return remote(src, rows(normed_all, zz), line_send.at[way, hop], line_recv.at[way, hop], (s, target))

    def over(zz, own=False):
        src = normed if own else rows(normed_all, zz)
        return remote(src, rows(normed_other, zz), core_send.at[0, zz], core_recv.at[0, zz], (core, z))

    def grad_over(k):
        zz = (z + 4 - k) % 4
        return remote(grads[k], rows(grad_other, zz), core_send.at[1, zz], core_recv.at[1, zz], (core, z))

    def hop_step(hop):
        def below():
            line(z - hop, True, hop - 1).wait_recv()
            pl.when(z < 3)(lambda: line(z - hop, True, hop).start())
            over(z - hop).start()

        def above():
            line(z + hop, False, hop - 1).wait_recv()
            pl.when(z > 0)(lambda: line(z + hop, False, hop).start())
            over(z + hop).start()

        pl.when(z >= hop)(below)
        pl.when(z + hop <= 3)(above)

    local = [
        pltpu.make_async_copy(grads[k], rows(grad_all, (z + 4 - k) % 4), own_sem.at[k]) for k in range(4)
    ]
    local.append(pltpu.make_async_copy(normed, rows(normed_all, z), own_sem.at[4]))
    pl.when(z < 3)(lambda: line(z, True, 0).start())
    pl.when(z > 0)(lambda: line(z, False, 0).start())
    over(z, True).start()
    for copy in local:
        copy.start()
    for k in range(4):
        grad_over(k).start()
    for hop in range(1, 4):
        hop_step(hop)
    for copy in local:
        copy.wait()
    for k in range(4):
        grad_over(k).wait()
    over(z, True).wait()
    for k in range(1, 4):
        over((z + k) % 4).wait()
    pl.when(z < 3)(lambda: line(z, True, 0).wait_send())
    pl.when(z > 0)(lambda: line(z, False, 0).wait_send())
    for hop in range(1, 3):
        pl.when((z >= hop) & (z < 3))(lambda: line(z - hop, True, hop).wait_send())
        pl.when((z + hop <= 3) & (z > 0))(lambda: line(z + hop, False, hop).wait_send())


def gather_rows(normed, grads):
    tok, model = normed.shape
    anyspec = pl.BlockSpec(memory_space=pl.ANY)
    dma = pltpu.SemaphoreType.DMA
    return pl.pallas_call(
        rows_kernel,
        in_specs=[anyspec] * 5,
        out_specs=[anyspec] * 4,
        out_shape=[jax.ShapeDtypeStruct((4 * tok, model), bf16)] * 4,
        scratch_shapes=[dma((2, 3)), dma((2, 3)), dma((2, 4)), dma((2, 4)), dma((5,))],
        compiler_params=pltpu.CompilerParams(collective_id=3, has_side_effects=True),
        name="gather_rows",
    )(normed, *grads)


def products_kernel(sides, tile, cuts, place, *refs):
    lefts = 1 + max(side for side, _ in sides)
    left_refs = refs[: 2 * lefts]
    right_refs = refs[2 * lefts : 2 * lefts + 2 * len(sides)]
    outs = refs[2 * lefts + 2 * len(sides) : -3]
    turned, stage, right = refs[-3:]
    tok = left_refs[0].shape[0]
    chip_cols = left_refs[0].shape[1] // 4
    half = chip_cols // 2
    step = pl.program_id(0)

    @pl.when(step == 0)
    def _():
        for side in range(lefts):
            for q in range(4):
                cols = pl.ds(pl.multiple_of(place[q] * chip_cols, 128), chip_cols)
                stage[:, :] = jnp.concatenate(
                    [left_refs[2 * side][:, cols], left_refs[2 * side + 1][:, cols]], axis=0
                ).T
                turned[side, q] = stage[pl.ds(pl.multiple_of(place[4] * half, 16), half), :]

    first = 0
    side_now = 0
    for n, (side, tiles) in enumerate(sides):

        @pl.when((step >= first) & (step < first + tiles))
        def _(n=n):
            right[0:tok, :] = right_refs[2 * n][...]
            right[tok:, :] = right_refs[2 * n + 1][...]

        side_now = jnp.where(step >= first, side, side_now)
        first += tiles

    start, index, inside = 0, 0, 0
    for q in range(4):
        block = mm(turned[side_now, q], right[...], ((1,), (0,))).astype(bf16)
        taken = 0
        while taken < half:
            size = min(cuts[index] - inside, half - taken)
            outs[index][inside : inside + size, :] = block[taken : taken + size]
            taken += size
            inside += size
            if inside == cuts[index]:
                index, inside = index + 1, 0


def products(lefts, rights, cuts, name):
    seq = lax.axis_index("seq")
    core, x, y = seq % 2, (seq // 2) % 2, seq // 4
    place = jnp.stack([(1 - y) * 2 + 1 - x, y * 2 + 1 - x, (1 - y) * 2 + x, y * 2 + x, core]).astype(jnp.int32)
    tile = 640
    tok, model = lefts[0][0].shape
    sides = tuple((side, own.shape[1] // tile) for side, own, _ in rights)
    total = sum(tiles for _, tiles in sides)
    in_specs = [
        pl.BlockSpec((tok, model), lambda j, place: (0, 0), pipeline_mode=pl.Buffered(1))
    ] * (2 * len(lefts))
    first = 0
    for _, tiles in sides:

        def index(j, place, first=first, tiles=tiles):
            return (0, jnp.clip(j - first, 0, tiles - 1))

        in_specs += [pl.BlockSpec((tok, tile), index)] * 2
        first += tiles
    half = model // 8
    return pl.pallas_call(
        functools.partial(products_kernel, sides, tile, cuts),
        grid_spec=pltpu.PrefetchScalarGridSpec(
            num_scalar_prefetch=1,
            grid=(total,),
            in_specs=in_specs,
            out_specs=[pl.BlockSpec((rows, tile), lambda j, place: (0, j)) for rows in cuts],
            scratch_shapes=[
                pltpu.VMEM((len(lefts), 4, half, 2 * tok), bf16),
                pltpu.VMEM((2 * half, 2 * tok), bf16),
                pltpu.VMEM((2 * tok, tile), bf16),
            ],
        ),
        out_shape=[jax.ShapeDtypeStruct((rows, total * tile), bf16) for rows in cuts],
        compiler_params=pltpu.CompilerParams(vmem_limit_bytes=56 * 1024 * 1024),
        cost_estimate=pl.CostEstimate(
            flops=2 * 4 * half * 2 * tok * total * tile, bytes_accessed=4 * half * total * tile * 2, transcendentals=0
        ),
        name=name,
    )(place, *[a for pair in lefts for a in pair], *[a for _, own, other in rights for a in (own, other)])


def add_columns(target, sources, start, size, step):
    def one(turn, carry):
        cols = pl.ds(pl.multiple_of(start + turn * step, 128), step)
        total = target[:, cols].astype(f32)
        for source in sources:
            total = total + source[:, cols].astype(f32)
        target[:, cols] = total.astype(target.dtype)
        return carry

    lax.fori_loop(0, size // step, one, 0)


def scatter_kernel(
    main, rest, mlp, mixer_sum, mlp_back,
    held, cross, near, lined,
    load_sem, flow_send, flow_recv, line_send, line_recv, swap_send, swap_recv, own_sem,
):
    s, z, _, beside, across = places()
    chip_diag, chip_beside, chip_across, chip = 0, 1, 2, 3
    rows = held.shape[1] // 4
    cols = held.shape[2]
    cut = cols // 256 * 128
    ff_part = mlp.shape[1] // 3
    parts = (main, rest)
    order = (3 * (1 - z // 2), (2 + 3 * z) % 5, 1 + z % 2, z)

    def remote(src, dst, send, recv, target):
        return pltpu.make_async_remote_copy(
            src_ref=src, dst_ref=dst, send_sem=send, recv_sem=recv, device_id=target, device_id_type=MESH
        )

    def span(k):
        return pl.ds(pl.multiple_of(k * rows, 16), rows)

    def loads(i):
        copies, start = [], 0
        for n, part in enumerate(parts):
            size = part.shape[2]
            copies.append(
                pltpu.make_async_copy(
                    part.at[:, span(order[i]), :], held.at[:, span(order[i]), pl.ds(start, size)], load_sem.at[i, n]
                )
            )
            start += size
        return copies

    left, right = pl.ds(0, cut), pl.ds(cut, cols - cut)

    def block(q, i, side):
        return held.at[q, span(order[i]), side]

    def flow(i, index):
        send, recv = flow_send.at[i, index], flow_recv.at[i, index]
        to_beside, to_across = (beside, z), (across, z)
        if index == 0:
            return remote(block(chip_diag, i, left), cross.at[i, :, left], send, recv, to_across)
        if index == 1:
            return remote(block(chip_diag, i, right), cross.at[i, :, right], send, recv, to_beside)
        if index == 2:
            return remote(block(chip_beside, i, right), near.at[0, i, :, right], send, recv, to_beside)
        if index == 3:
            return remote(block(chip_beside, i, left), near.at[0, i, :, left], send, recv, to_beside)
        if index == 4:
            return remote(block(chip_across, i, left), near.at[1, i, :, left], send, recv, to_across)
        return remote(block(chip_across, i, right), near.at[1, i, :, right], send, recv, to_across)

    def cross_step(i):
        flow(i, 0).wait_recv()
        add_columns(held.at[chip_beside, span(order[i]), :], [cross.at[i]], 0, cut, 512)
        flow(i, 3).start()
        flow(i, 1).wait_recv()
        add_columns(held.at[chip_across, span(order[i]), :], [cross.at[i]], cut, cols - cut, 384)
        flow(i, 5).start()

    def near_step(i):
        for index in (2, 4, 3, 5):
            flow(i, index).wait_recv()
        add_columns(held.at[chip, span(order[i]), :], [near.at[0, i], near.at[1, i]], 0, cols, 640)

    def line(k, slot, target):
        return remote(
            held.at[chip, span(k), :], lined.at[slot], line_send.at[k], line_recv.at[slot], (s, target)
        )

    def absorb(k, slot, source):
        line(k, slot, source).wait_recv()
        add_columns(held.at[chip, span(k), :], [lined.at[slot]], 0, cols, 640)

    def chain(i):
        k = order[i]
        if i == 3:
            pl.when(z > 0)(lambda: absorb(k, k, z - 1))
            pl.when(z < 3)(lambda: absorb(k, 4, z + 1))
            return

        @pl.when(k > z)
        def _():
            pl.when(z > 0)(lambda: absorb(k, k, z - 1))
            line(k, k, z + 1).start()

        @pl.when(k < z)
        def _():
            pl.when(z < 3)(lambda: absorb(k, k, z + 1))
            pl.when(k == z - 1)(lambda: line(k, 4, z - 1).start())
            pl.when(k < z - 1)(lambda: line(k, k, z - 1).start())

    def chain_drain():
        for i in range(3):
            k = order[i]
            line(k, k, (z + 1) % 4).wait_send()

    def pieces():
        for m in range(3):
            yield m, mlp, pl.ds(m * ff_part, ff_part)

    def swap(k):
        to = (z + k) % 4
        here = pl.ds(pl.multiple_of(z * ff_part, 128), ff_part)
        return [
            remote(
                source.at[span(to), at], mlp_back.at[m, :, here], swap_send.at[k - 1, m], swap_recv.at[k - 1, m], (s, to)
            )
            for m, source, at in pieces()
        ]

    own = [
        pltpu.make_async_copy(
            source.at[span(z), at], mlp_back.at[m, :, pl.ds(pl.multiple_of(z * ff_part, 128), ff_part)], own_sem.at[m]
        )
        for m, source, at in pieces()
    ]
    for i in range(4):
        for copy in loads(i):
            copy.start()
    greet([(beside, z), (across, z)] + [(s, (z + k) % 4) for k in range(1, 4)])
    for k in (1, 3, 2):
        for copy in swap(k):
            copy.start()
    for copy in own:
        copy.start()
    for i in range(2):
        for copy in loads(i):
            copy.wait()
        flow(i, 0).start()
        flow(i, 1).start()
        if i == 0:
            flow(i, 2).start()
            flow(i, 4).start()
    for i in range(4):
        cross_step(i)
        if i + 1 < 4:
            flow(i + 1, 2).start()
            flow(i + 1, 4).start()
        if i + 2 < 4:
            for copy in loads(i + 2):
                copy.wait()
            flow(i + 2, 0).start()
            flow(i + 2, 1).start()
        if i > 0:
            near_step(i - 1)
            chain(i - 1)
    near_step(3)
    chain(3)
    done = pltpu.make_async_copy(held.at[chip, span(z), :], mixer_sum, own_sem.at[3])
    done.start()
    for i in range(4):
        for index in range(6):
            flow(i, index).wait_send()
    chain_drain()
    for k in range(1, 4):
        for copy in swap(k):
            copy.wait()
    for copy in own:
        copy.wait()
    done.wait()


def scatter(main, rest, mlp):
    rows = main.shape[1] // 4
    cols = main.shape[2] + rest.shape[2]
    ff_part = mlp.shape[1] // 3
    anyspec = pl.BlockSpec(memory_space=pl.ANY)
    dma = pltpu.SemaphoreType.DMA
    return pl.pallas_call(
        scatter_kernel,
        in_specs=[anyspec] * 3,
        out_specs=[anyspec] * 2,
        out_shape=[
            jax.ShapeDtypeStruct((rows, cols), bf16),
            jax.ShapeDtypeStruct((3, rows, 4 * ff_part), bf16),
        ],
        scratch_shapes=[
            pltpu.VMEM((4, 4 * rows, cols), bf16),
            pltpu.VMEM((4, rows, cols), bf16),
            pltpu.VMEM((2, 4, rows, cols), bf16),
            pltpu.VMEM((5, rows, cols), bf16),
            dma((4, 2)), dma((4, 6)), dma((4, 6)), dma((4,)), dma((5,)), dma((3, 3)), dma((3, 3)), dma((4,)),
        ],
        compiler_params=pltpu.CompilerParams(
            collective_id=2, has_side_effects=True, vmem_limit_bytes=52 * 1024 * 1024
        ),
        name="scatter_gradients",
    )(main, rest, mlp)


def gather_plain(mixer, gate, up, down):
    groups = lax.axis_size("fsdp")
    part_rows, ff = gate.shape
    own = jnp.stack([w.reshape(part_rows, groups, ff // groups) for w in (gate, up, down)], axis=2)
    mine = lax.all_to_all(jnp.transpose(own, (1, 0, 2, 3)), "fsdp", 0, 0, tiled=True)
    return lax.all_gather(mixer, both, axis=0, tiled=True), mine.reshape(groups * part_rows, -1)


def from_line(shard):
    count = lax.axis_size("fsdp")
    return [shard] + [
        lax.ppermute(shard, "fsdp", [(i, (i + k) % count) for i in range(count)]) for k in range(1, count)
    ]


def swap_cores(shard):
    count = lax.axis_size("seq")
    return lax.ppermute(shard, "seq", [(i, i + 1 - 2 * (i % 2)) for i in range(count)])


def swap_beside(shard):
    return lax.ppermute(shard, "seq", [(i, i ^ 2) for i in range(8)])


def swap_across(shard):
    return lax.ppermute(shard, "seq", [(i, i ^ 4) for i in range(8)])


def sum_blocks(blocks):
    diag_low, diag_high, beside_low, beside_high, across_low, across_high, mine = blocks
    by_across = swap_across(diag_low)
    by_beside = swap_beside(diag_high)
    from_beside_high = swap_beside(beside_high)
    from_across_low = swap_across(across_low)
    from_beside_low = swap_beside((beside_low.astype(f32) + by_across.astype(f32)).astype(bf16))
    from_across_high = swap_across((across_high.astype(f32) + by_beside.astype(f32)).astype(bf16))
    half = diag_low.shape[0]
    low = mine[:half].astype(f32) + from_across_low.astype(f32) + from_beside_low.astype(f32)
    high = mine[half:].astype(f32) + from_across_high.astype(f32) + from_beside_high.astype(f32)
    return jnp.concatenate([low.astype(bf16), high.astype(bf16)], axis=0)


def scatter_paired(normed, grad_both, grad_mix, mixed, rest, mlp_sum):
    seq = lax.axis_index("seq")
    core, x, y = seq % 2, (seq // 2) % 2, seq // 4
    main = products(
        [(normed, swap_cores(normed)), (grad_mix, swap_cores(grad_mix))],
        [(0, grad_both, swap_cores(grad_both)), (1, mixed, swap_cores(mixed))],
        (lru_rows(normed),),
        "mixer_products",
    )[0]
    grouped = rest.reshape(4, 2, -1, rest.shape[1])
    own = lax.dynamic_index_in_dim(grouped, core, 1, False)
    other = swap_cores(lax.dynamic_index_in_dim(grouped, 1 - core, 1, False))
    rest = (own.astype(f32) + other.astype(f32)).astype(bf16)
    rest = jnp.concatenate(
        [
            lax.dynamic_slice_in_dim(rest, q, 1, 0)
            for q in ((1 - y) * 2 + 1 - x, y * 2 + 1 - x, (1 - y) * 2 + x, y * 2 + x)
        ],
        axis=0,
    )
    return scatter(main.reshape(4, -1, main.shape[1]), rest, mlp_sum)


def lru_rows(values):
    return values.shape[1] // 2


def scatter_plain(normed, grad_both, grad_mix, mixed, rest, mlp_sum):
    groups = lax.axis_size("fsdp")
    term_wide = mm(normed, grad_both, ((0,), (0,))).astype(bf16)
    term_out = mm(grad_mix, mixed, ((0,), (0,))).astype(bf16)
    mixer_sum = lax.psum_scatter(
        jnp.concatenate([term_wide, term_out, rest], axis=1), "seq", scatter_dimension=0, tiled=True
    )
    mixer_sum = lax.psum_scatter(mixer_sum, "fsdp", scatter_dimension=0, tiled=True)
    ff_part = mlp_sum.shape[1] // 3
    part_rows = mlp_sum.shape[0] // groups
    mlp_sum = mlp_sum.reshape(groups, part_rows, 3, ff_part)
    mlp_back = lax.all_to_all(mlp_sum, "fsdp", 0, 0, tiled=True)
    mlp_back = jnp.transpose(mlp_back, (2, 1, 0, 3)).reshape(3, part_rows, groups * ff_part)
    return mixer_sum, mlp_back


def call_heads(kernel, width, heads, ins, outs, scratch, name):
    def spec(rows_cols):
        rows, by_row = rows_cols
        if by_row:
            return pl.BlockSpec((rows, width), lambda h: (h, 0))
        return pl.BlockSpec((rows, width), lambda h: (0, h))

    in_specs = [spec((width, True)) if rowwise else spec((a.shape[0], False)) for a, rowwise in ins]
    out_specs = [spec((width, True)) if rowwise else spec((rows, False)) for rows, _, rowwise in outs]
    out_shape = [
        jax.ShapeDtypeStruct((heads * width, width) if rowwise else (rows, heads * width), kind)
        for rows, kind, rowwise in outs
    ]
    return pl.pallas_call(
        kernel,
        grid=(heads,),
        in_specs=in_specs,
        out_specs=out_specs,
        out_shape=out_shape,
        scratch_shapes=[pltpu.VMEM((rows, width), f32) for rows in scratch],
        compiler_params=pltpu.CompilerParams(vmem_limit_bytes=40 * 1024 * 1024),
        name=name,
    )(*[a for a, _ in ins])


def on_device(
    block_input,
    cotangent,
    mixer_gain,
    branch_proj,
    gelu_proj,
    conv_taps,
    conv_bias,
    rate_blocks,
    input_blocks,
    rate_bias,
    input_bias,
    decay_param,
    out_proj,
    mlp_gain,
    gate_proj,
    up_proj,
    down_proj,
):
    groups = lax.axis_size("fsdp")
    part_rows, lru = branch_proj.shape
    width = rate_blocks.shape[1]
    heads = lru // width
    margin = conv_taps.shape[0] - 1
    tokens = block_input[0].astype(f32)
    tok_count, model = tokens.shape
    ff = gate_proj.shape[1]
    ff_part = ff // groups
    grad_out = cotangent[0]

    smalls = jnp.stack(
        [conv_taps[k] for k in range(margin + 1)]
        + [conv_bias, rate_bias, input_bias, decay_param, mixer_gain, mlp_gain],
        axis=1,
    )
    small_count = smalls.shape[1]
    smalls = jnp.pad(smalls, ((0, 0), (0, 128 - small_count)))
    mixer_own = jnp.concatenate(
        [smalls, rate_blocks, input_blocks, branch_proj, gelu_proj, out_proj], axis=1
    )
    custom = lax.axis_size("seq") == 8 and groups == 4
    if custom:
        mixer_w, mlp_mine = gather(mixer_own, gate_proj, up_proj, down_proj)
    else:
        mixer_w, mlp_mine = gather_plain(mixer_own, gate_proj, up_proj, down_proj)
    mlp_w = lax.all_gather(mlp_mine, "seq", axis=0, tiled=True)
    grad_out_late = lax.optimization_barrier((grad_out, mlp_mine))[0]
    if custom:
        grad_pieces = from_line(grad_out_late)
    first = lax.optimization_barrier(mixer_w[:, : 128 + 2 * width])
    wide = mixer_w[:, 128 + 2 * width : 128 + 2 * width + 2 * lru]
    proj_out = mixer_w[:, 128 + 2 * width + 2 * lru :]

    table = first[:, :small_count].astype(f32).T
    blocks_rate = first[:, 128 : 128 + width]
    blocks_input = first[:, 128 + width :]
    param_decay = table[margin + 4]
    gain_one = table[margin + 5]
    gain_two = table[margin + 6]
    small = jnp.concatenate(
        [
            table[: margin + 4],
            jax.nn.softplus(-param_decay)[None],
            -jax.nn.sigmoid(-param_decay)[None],
            jnp.zeros((16 - margin - 6, lru), f32),
        ],
        axis=0,
    )

    normed = norm_rows(tokens, gain_one).astype(bf16)
    both_pre = mm(normed, wide, ((1,), (0,)))
    branch = both_pre[:, :lru].astype(bf16)
    gelu_pre = both_pre[:, lru:]
    prior = from_behind(branch[tok_count - margin :], "seq", 1).astype(f32)
    prior = jnp.concatenate([jnp.zeros((8 - margin, lru), f32), prior], axis=0)
    conv, rate_pre, input_pre, cum, local = call_heads(
        mixer_forward,
        width,
        heads,
        [(branch, False), (prior, False), (small, False), (blocks_rate, True), (blocks_input, True)],
        [(tok_count, bf16, False)] + [(tok_count, f32, False)] * 4,
        [tok_count + 8],
        "mixer_forward",
    )
    carried = prefix((cum[-1], local[-1]), "seq", False)
    states = local + cum * carried[None]
    mixed = (states * jax.nn.gelu(gelu_pre, approximate=True)).astype(bf16)
    middle = tokens + mm(mixed, proj_out, ((1,), (1,)))
    normed_two = norm_rows(middle, gain_two).astype(bf16)

    if custom:
        normed_all, normed_other, grad_out_all, grad_out_other = gather_rows(normed_two, grad_pieces)
    else:
        normed_all = lax.all_gather(normed_two, "fsdp", axis=0, tiled=True)
        grad_out_all = lax.all_gather(grad_out_late, "fsdp", axis=0, tiled=True)
    w_gate, w_up, w_down = mlp_w[:, :ff_part], mlp_w[:, ff_part : 2 * ff_part], mlp_w[:, 2 * ff_part :]
    gate = mm(normed_all, w_gate, ((1,), (0,)))
    up_val = mm(normed_all, w_up, ((1,), (0,)))
    gelu_gate, gelu_slope = gelu_parts(gate)
    hidden = (gelu_gate * up_val).astype(bf16)
    grad_hidden = mm(grad_out_all, w_down, ((1,), (0,)))
    grad_gate = (grad_hidden * up_val * gelu_slope).astype(bf16)
    grad_up = (grad_hidden * gelu_gate).astype(bf16)
    grad_normed_part = mm(grad_gate, w_gate, ((1,), (1,))) + mm(grad_up, w_up, ((1,), (1,)))
    grad_normed_two = lax.psum_scatter(
        grad_normed_part.astype(bf16), "fsdp", scatter_dimension=0, tiled=True
    )
    out_part = mm(hidden, w_down, ((1,), (1,))).astype(bf16)
    if custom:
        half = model // 16
        blocks = products(
            [(normed_all, normed_other), (grad_out_all, grad_out_other)],
            [
                (0, grad_gate, swap_cores(grad_gate)),
                (0, grad_up, swap_cores(grad_up)),
                (1, hidden, swap_cores(hidden)),
            ],
            (half,) * 6 + (2 * half,),
            "feed_forward_products",
        )
        blocks, grad_normed_two = lax.optimization_barrier((blocks, grad_normed_two))
        mlp_sum = sum_blocks(blocks)
    else:
        grad_pair = jnp.concatenate([grad_gate, grad_up], axis=1)
        term_pair = mm(normed_all, grad_pair, ((0,), (0,))).astype(bf16)
        term_down = mm(grad_out_all, hidden, ((0,), (0,))).astype(bf16)
        pair_sum = lax.psum_scatter(term_pair, "seq", scatter_dimension=0, tiled=True)
        down_sum = lax.psum_scatter(term_down, "seq", scatter_dimension=0, tiled=True)
        mlp_sum = jnp.concatenate([pair_sum, down_sum], axis=1)
    out_sum = lax.psum_scatter(out_part, "fsdp", scatter_dimension=0, tiled=True)
    block_output = (middle + out_sum.astype(f32)).astype(bf16)[None]
    grad_normed_two = grad_normed_two.astype(f32)

    second_pull = jax.vjp(norm_rows, middle, gain_two)[1]
    grad_mid_part, grad_gain_two = second_pull(grad_normed_two)
    grad_middle = grad_out.astype(f32) + grad_mid_part
    grad_mix = grad_middle.astype(bf16)
    grad_mixed = mm(grad_mix, proj_out, ((1,), (0,)))
    carried_rows = jnp.broadcast_to(carried[None], (8, lru))
    grad_gelu_pre, rev_cum, rev_grad, pair_grad = call_heads(
        mixer_backward_scan,
        width,
        heads,
        [(a, False) for a in (grad_mixed, gelu_pre, rate_pre, cum, local, carried_rows, small)],
        [(tok_count, bf16, False), (tok_count, f32, False), (tok_count, f32, False), (8, f32, False)],
        [tok_count + 8],
        "mixer_backward_scan",
    )
    incoming = prefix((cum[-1], pair_grad[0]), "seq", True)
    incoming_rows = jnp.broadcast_to(incoming[None], (8, lru))
    own, head, rate_w_grad, input_w_grad, sums = call_heads(
        mixer_backward,
        width,
        heads,
        [
            (a, False)
            for a in (rev_cum, rev_grad, incoming_rows, cum, local, carried_rows, rate_pre, input_pre, conv, branch, prior, small)
        ]
        + [(blocks_rate, True), (blocks_input, True)],
        [(tok_count, f32, False), (8, f32, False), (0, bf16, True), (0, bf16, True), (8, f32, False)],
        [tok_count + 8, tok_count + 16],
        "mixer_backward",
    )
    received = from_behind(head[8 - margin :], "seq", -1)
    grad_branch = jnp.concatenate(
        [own[: tok_count - margin], own[tok_count - margin :] + received], axis=0
    ).astype(bf16)
    grad_both = jnp.concatenate([grad_branch, grad_gelu_pre], axis=1)
    grad_normed = mm(grad_both, wide, ((1,), (1,)))
    first_pull = jax.vjp(norm_rows, tokens, gain_one)[1]
    grad_tok_part, grad_gain_one = first_pull(grad_normed)
    input_grad = (grad_middle + grad_tok_part).astype(bf16)[None]
    vectors = jnp.concatenate([sums, grad_gain_one[None], grad_gain_two[None]], axis=0).T
    vectors = jnp.pad(vectors, ((0, 0), (0, 128 - vectors.shape[1]))).astype(bf16)
    rest = jnp.concatenate([rate_w_grad, input_w_grad, vectors], axis=1)
    scatter_all = scatter_paired if custom else scatter_plain
    mixer_sum, mlp_back = scatter_all(normed, grad_both, grad_mix, mixed, rest, mlp_sum)
    mlp_grads = [mlp_back[m].astype(f32) for m in range(3)]
    mixer_sum = mixer_sum.astype(f32)
    edges = [lru, 2 * lru, 3 * lru, 3 * lru + width, 3 * lru + 2 * width]
    dbranch, dgelu, dout, drate, dinput, vec = jnp.split(mixer_sum, edges, axis=1)
    vec = vec.T
    return (
        block_output,
        input_grad,
        vec[8],
        dbranch,
        dgelu,
        vec[: margin + 1],
        vec[7],
        drate,
        dinput,
        vec[4],
        vec[5],
        vec[6],
        dout,
        vec[9],
        mlp_grads[0],
        mlp_grads[1],
        mlp_grads[2],
    )


def solution(mesh):
    tokens = P("fsdp", "seq", None)
    vector = P(both)
    matrix = P(both, None)
    taps = P(None, both)
    return jax.shard_map(
        on_device,
        mesh=mesh,
        in_specs=(
            tokens, tokens, vector, matrix, matrix, taps, vector, matrix, matrix,
            vector, vector, vector, matrix, vector, matrix, matrix, matrix,
        ),
        out_specs=(
            tokens, tokens, vector, matrix, matrix, taps, vector, matrix, matrix,
            vector, vector, vector, matrix, vector, matrix, matrix, matrix,
        ),
        check_vma=False,
    )
```

```python
import functools

import jax
import jax.numpy as jnp
from jax import lax
from jax.experimental import pallas as pl
from jax.experimental.pallas import tpu as pltpu
from jax.sharding import PartitionSpec as P

epsilon = 1e-06
f32 = jnp.float32
bf16 = jnp.bfloat16
both = ("seq", "fsdp")
MESH = pl.DeviceIdType.MESH
TAP, CONV_BIAS, RATE_BIAS, INPUT_BIAS, SOFT, SOFT_SLOPE = 0, 4, 5, 6, 7, 8
GELU_C = 0.7978845608028654
GELU_A = 0.044715


def from_behind(shard, axis, by):
    devices = lax.axis_size(axis)
    pairs = [(i, i + by) for i in range(devices) if 0 <= i + by < devices]
    return lax.ppermute(shard, axis, pairs)


def prefix(part, axis, reverse):
    count = lax.axis_size(axis)
    place = lax.axis_index(axis)
    gathered = lax.all_gather(jnp.stack(part), axis)
    state = jnp.zeros_like(part[1])
    for hop in range(count):
        source = count - 1 - hop if reverse else hop
        ahead = source > place if reverse else source < place
        state = jnp.where(ahead, gathered[source, 1] + gathered[source, 0] * state, state)
    return state


def norm_rows(values, scales):
    return values * lax.rsqrt(jnp.mean(values * values, axis=-1, keepdims=True) + epsilon) * scales


def gelu_parts(x):
    inner = jnp.tanh(GELU_C * (x + GELU_A * x * x * x))
    return 0.5 * x * (1.0 + inner), 0.5 * (1.0 + inner) + 0.5 * x * (1.0 - inner * inner) * (
        GELU_C * (1.0 + 3.0 * GELU_A * x * x)
    )


def mm(left, right, dims):
    return lax.dot_general(left, right, (dims, ((), ())), preferred_element_type=f32)


def sigmoid(x):
    return 1.0 / (1.0 + jnp.exp(-x))


def scan_rows(decay, value, reverse):
    rows = decay.shape[0]
    place = lax.broadcasted_iota(jnp.int32, decay.shape, 0)
    step = 1
    while step < rows:
        shift = rows - step if reverse else step
        inside = place < rows - step if reverse else place >= step
        before_value = jnp.where(inside, pltpu.roll(value, shift, 0), 0.0)
        before_decay = jnp.where(inside, pltpu.roll(decay, shift, 0), 1.0)
        value = value + decay * before_value
        decay = decay * before_decay
        step *= 2
    return decay, value


def gates(rate_pre, input_pre, soft):
    rate = sigmoid(rate_pre)
    log_decay = -8.0 * rate * soft
    decay = jnp.exp(log_decay)
    square = decay * decay
    root = jnp.sqrt(-jnp.tanh(log_decay) * (1.0 + square))
    return rate, decay, square, root, sigmoid(input_pre)


def mixer_forward(branch, prior, small, rate_w, input_w, conv, rate_pre, input_pre, cum, local, ext):
    rows = branch.shape[0]
    ext[0:8, :] = prior[...]
    ext[8:, :] = branch[...].astype(f32)
    total = small[CONV_BIAS : CONV_BIAS + 1, :] + small[TAP : TAP + 1, :] * ext[8:, :]
    for offset in range(1, 4):
        total = total + small[TAP + offset : TAP + offset + 1, :] * ext[pl.ds(8 - offset, rows), :]
    low = total.astype(bf16)
    conv[...] = low
    rate = mm(low, rate_w[...], ((1,), (0,))) + small[RATE_BIAS : RATE_BIAS + 1, :]
    inp = mm(low, input_w[...], ((1,), (0,))) + small[INPUT_BIAS : INPUT_BIAS + 1, :]
    rate_pre[...] = rate
    input_pre[...] = inp
    _, decay, _, root, opened = gates(rate, inp, small[SOFT : SOFT + 1, :])
    product, states = scan_rows(decay, root * opened * low.astype(f32), False)
    cum[...] = product
    local[...] = states


def mixer_backward_scan(grad_mixed, gelu_pre, rate_pre, cum, local, carried, small, grad_pre, rev_cum, rev_grad, pair, ext):
    rows = grad_mixed.shape[0]
    states = local[...] + cum[...] * carried[0:1, :]
    value, slope = gelu_parts(gelu_pre[...])
    grad = grad_mixed[...]
    grad_pre[...] = (grad * states * slope).astype(bf16)
    decay = jnp.exp(-8.0 * sigmoid(rate_pre[...]) * small[SOFT : SOFT + 1, :])
    ext[0:rows, :] = decay
    ext[rows:, :] = jnp.ones((8, decay.shape[1]), f32)
    product, back = scan_rows(ext[pl.ds(1, rows), :], grad * value, True)
    rev_cum[...] = product
    rev_grad[...] = back
    pair[...] = jnp.broadcast_to(decay[0:1, :] * back[0:1, :], pair.shape)


def mixer_backward(
    rev_cum, rev_grad, incoming, cum, local, carried, rate_pre, input_pre, conv, branch, prior, small, rate_w, input_w,
    own, head, rate_w_grad, input_w_grad, sums, ext, gext,
):
    rows = rev_cum.shape[0]
    soft = small[SOFT : SOFT + 1, :]
    grad_states = rev_grad[...] + rev_cum[...] * incoming[0:1, :]
    rate, decay, square, root, opened = gates(rate_pre[...], input_pre[...], soft)
    ext[0:8, :] = jnp.broadcast_to(carried[0:1, :], (8, carried.shape[1]))
    ext[8:, :] = local[...] + cum[...] * carried[0:1, :]
    before = ext[pl.ds(7, rows), :]
    low = conv[...]
    conv_in = low.astype(f32)
    grad_log = grad_states * decay * before - grad_states * opened * conv_in * square / root
    driven = grad_states * root
    grad_input = (driven * conv_in * opened * (1.0 - opened)).astype(bf16)
    by_rate = grad_log * (-8.0 * rate)
    grad_rate = (by_rate * soft * (1.0 - rate)).astype(bf16)
    sums[6:7, :] = jnp.sum(by_rate, axis=0, keepdims=True) * small[SOFT_SLOPE : SOFT_SLOPE + 1, :]
    sums[4:5, :] = jnp.sum(grad_rate.astype(f32), axis=0, keepdims=True)
    sums[5:6, :] = jnp.sum(grad_input.astype(f32), axis=0, keepdims=True)
    rate_w_grad[...] = mm(low, grad_rate, ((0,), (0,))).astype(rate_w_grad.dtype)
    input_w_grad[...] = mm(low, grad_input, ((0,), (0,))).astype(input_w_grad.dtype)
    grad_conv = (
        driven * opened
        + mm(grad_rate, rate_w[...], ((1,), (1,)))
        + mm(grad_input, input_w[...], ((1,), (1,)))
    )
    sums[7:8, :] = jnp.sum(grad_conv, axis=0, keepdims=True)
    ext[0:8, :] = prior[...]
    ext[8:, :] = branch[...].astype(f32)
    gext[0:8, :] = jnp.zeros((8, grad_conv.shape[1]), f32)
    gext[8 : 8 + rows, :] = grad_conv
    gext[8 + rows :, :] = jnp.zeros((8, grad_conv.shape[1]), f32)
    back = jnp.zeros_like(grad_conv)
    front = jnp.zeros((8, grad_conv.shape[1]), f32)
    for offset in range(4):
        tap = small[TAP + offset : TAP + offset + 1, :]
        sums[offset : offset + 1, :] = jnp.sum(
            grad_conv * ext[pl.ds(8 - offset, rows), :], axis=0, keepdims=True
        )
        back = back + tap * gext[pl.ds(8 + offset, rows), :]
        front = front + tap * gext[pl.ds(offset, 8), :]
    own[...] = back
    head[...] = front


def places():
    s = lax.axis_index("seq")
    z = lax.axis_index("fsdp")
    core = s + 1 - 2 * (s % 2)
    beside = s + 2 - 4 * ((s // 2) % 2)
    across = s + 4 - 8 * (s // 4)
    return s, z, core, beside, across


def greet(peers):
    barrier = pltpu.get_barrier_semaphore()
    for peer in peers:
        pl.semaphore_signal(barrier, inc=1, device_id=peer, device_id_type=MESH)
    pl.semaphore_wait(barrier, len(peers))


def gather_kernel(
    mixer, gate, up, down, mixer_all, mlp_mine,
    flow_send, flow_recv, line_send, line_recv, swap_send, swap_recv, own_sem,
):
    s, z, core, beside, across = places()
    rows, cols = mixer.shape
    ff_part = mlp_mine.shape[1] // 3
    cut = cols // 256 * 128
    diag = beside + across - s
    greet([(core, z), (beside, z), (across, z)] + [(s, (z + k) % 4) for k in range(1, 4)])

    def remote(src, dst, send, recv, target):
        return pltpu.make_async_remote_copy(
            src_ref=src, dst_ref=dst, send_sem=send, recv_sem=recv, device_id=target, device_id_type=MESH
        )

    def piece(seq, zz, half=None):
        span = pl.ds(pl.multiple_of((seq * 4 + zz) * rows, 16), rows)
        if half is None:
            return mixer_all.at[span, :]
        return mixer_all.at[span, pl.ds(0, cut) if half == 0 else pl.ds(cut, cols - cut)]

    def flow(zz, index, seq, half, target, src=None):
        ref = piece(seq, zz, half)
        return remote(
            ref if src is None else src, ref, flow_send.at[zz, index], flow_recv.at[zz, index], (target, z)
        )

    def sends(zz, src=None):
        return [
            flow(zz, 0, s, None, beside, src),
            flow(zz, 1, s, None, across, src),
            flow(zz, 4, s, None, core, src),
        ]

    def spread(zz, src=None):
        for copy in sends(zz, src):
            copy.start()

    def relay(zz):
        flow(zz, 0, beside, None, beside).wait_recv()
        flow(zz, 3, beside, 0, across).start()
        flow(zz, 5, beside, None, core).start()
        flow(zz, 1, across, None, across).wait_recv()
        flow(zz, 2, across, 1, beside).start()
        flow(zz, 6, across, None, core).start()

    def finish(zz):
        flow(zz, 3, diag, 0, across).wait_recv()
        flow(zz, 7, diag, 0, core).start()
        flow(zz, 2, diag, 1, beside).wait_recv()
        flow(zz, 8, diag, 1, core).start()

    def drain(zz, src=None):
        for copy in sends(zz, src):
            copy.wait_send()
        flow(zz, 3, beside, 0, across).wait_send()
        flow(zz, 5, beside, None, core).wait_send()
        flow(zz, 2, across, 1, beside).wait_send()
        flow(zz, 6, across, None, core).wait_send()
        flow(zz, 7, diag, 0, core).wait_send()
        flow(zz, 8, diag, 1, core).wait_send()
        flip = core - s
        flow(zz, 4, core, None, core).wait_recv()
        flow(zz, 5, beside + flip, None, core).wait_recv()
        flow(zz, 6, across + flip, None, core).wait_recv()
        flow(zz, 7, diag + flip, 0, core).wait_recv()
        flow(zz, 8, diag + flip, 1, core).wait_recv()

    def line(zz, up_way, hop, src=None):
        ref = piece(s, zz)
        way = 0 if up_way else 1
        target = z + 1 if up_way else z - 1
        return remote(
            ref if src is None else src, ref, line_send.at[way, hop], line_recv.at[way, hop], (s, target)
        )

    def line_hop(hop):
        def below():
            line(z - hop, True, hop - 1).wait_recv()
            pl.when(z < 3)(lambda: line(z - hop, True, hop).start())

        def above():
            line(z + hop, False, hop - 1).wait_recv()
            pl.when(z > 0)(lambda: line(z + hop, False, hop).start())

        pl.when(z >= hop)(below)
        pl.when(z + hop <= 3)(above)

    def at_hop(hop, act):
        pl.when(z >= hop)(lambda: act(z - hop))
        pl.when(z + hop <= 3)(lambda: act(z + hop))

    def landing(m, zz):
        return mlp_mine.at[pl.ds(pl.multiple_of(zz * rows, 16), rows), pl.ds(m * ff_part, ff_part)]

    def columns(m, zz):
        return (gate, up, down)[m].at[:, pl.ds(pl.multiple_of(zz * ff_part, 128), ff_part)]

    def swap(k, m, arriving=False):
        to = (z + k) % 4
        came = (z + 4 - k) % 4
        return remote(
            columns(m, to), landing(m, came if arriving else z), swap_send.at[k - 1, m], swap_recv.at[k - 1, m], (s, to)
        )

    local = [pltpu.make_async_copy(columns(m, z), landing(m, z), own_sem.at[m]) for m in range(3)]
    local.append(pltpu.make_async_copy(mixer, piece(s, z), own_sem.at[3]))

    pl.when(z < 3)(lambda: line(z, True, 0, mixer).start())
    pl.when(z > 0)(lambda: line(z, False, 0, mixer).start())
    spread(z, mixer)
    for copy in local:
        copy.start()
    line_hop(1)
    at_hop(1, spread)
    relay(z)
    line_hop(2)
    at_hop(2, spread)
    finish(z)
    at_hop(1, relay)
    line_hop(3)
    at_hop(3, spread)
    for k in (1, 3, 2):
        for m in range(3):
            swap(k, m).start()
    at_hop(1, finish)
    at_hop(2, relay)
    at_hop(3, relay)
    at_hop(2, finish)
    at_hop(3, finish)
    drain(z, mixer)
    for hop in range(1, 4):
        at_hop(hop, drain)
    for copy in local:
        copy.wait()
    for k in (1, 3, 2):
        for m in range(3):
            swap(k, m).wait_send()
            swap(k, m, True).wait_recv()
    pl.when(z < 3)(lambda: line(z, True, 0, mixer).wait_send())
    pl.when(z > 0)(lambda: line(z, False, 0, mixer).wait_send())
    for hop in range(1, 3):
        pl.when((z >= hop) & (z < 3))(lambda: line(z - hop, True, hop).wait_send())
        pl.when((z + hop <= 3) & (z > 0))(lambda: line(z + hop, False, hop).wait_send())


def gather(mixer, gate, up, down):
    rows, cols = mixer.shape
    ff_part = gate.shape[1] // 4
    anyspec = pl.BlockSpec(memory_space=pl.ANY)
    dma = pltpu.SemaphoreType.DMA
    return pl.pallas_call(
        gather_kernel,
        in_specs=[anyspec] * 4,
        out_specs=[anyspec] * 2,
        out_shape=[
            jax.ShapeDtypeStruct((32 * rows, cols), bf16),
            jax.ShapeDtypeStruct((4 * rows, 3 * ff_part), bf16),
        ],
        scratch_shapes=[
            dma((4, 9)), dma((4, 9)), dma((2, 3)), dma((2, 3)), dma((3, 3)), dma((3, 3)), dma((4,)),
        ],
        compiler_params=pltpu.CompilerParams(collective_id=1, has_side_effects=True),
        name="gather_weights",
    )(mixer, gate, up, down)


def rows_kernel(
    normed, grad0, grad1, grad2, grad3, normed_all, normed_other, grad_all, grad_other,
    line_send, line_recv, core_send, core_recv, own_sem, held,
):
    s, z, core, _, _ = places()
    tok = normed.shape[0]
    cuts = 4
    grads = (grad0, grad1, grad2, grad3)
    greet([(core, z)] + [(s, (z + k) % 4) for k in range(1, 4)])

    def rows(ref, zz):
        return ref.at[pl.ds(pl.multiple_of(zz * tok, 16), tok), :]

    def remote(src, dst, send, recv, target):
        return pltpu.make_async_remote_copy(
            src_ref=src, dst_ref=dst, send_sem=send, recv_sem=recv, device_id=target, device_id_type=MESH
        )

    def parts(ref):
        size = tok // cuts
        return [ref.at[pl.ds(n * size, size), :] for n in range(cuts)]

    def line(zz, up_way, hop):
        way = 0 if up_way else 1
        target = z + 1 if up_way else z - 1
        src = normed if hop == 0 else rows(normed_all, zz)
        dst = rows(normed_all, zz)
        return [
            remote(a, b, line_send.at[way, hop, n], line_recv.at[way, hop, n], (s, target))
            for n, (a, b) in enumerate(zip(parts(src), parts(dst)))
        ]

    def over(zz, own=False):
        src = normed if own else rows(normed_all, zz)
        return remote(src, rows(normed_other, zz), core_send.at[0, zz], core_recv.at[0, zz], (core, z))

    def grad_over(k):
        zz = (z + 4 - k) % 4
        return remote(grads[k], rows(grad_other, zz), core_send.at[1, zz], core_recv.at[1, zz], (core, z))

    def line_start(zz, up_way, hop):
        for copy in line(zz, up_way, hop):
            copy.start()

    def line_drain(zz, up_way, hop):
        for copy in line(zz, up_way, hop):
            copy.wait_send()

    def hop_step(hop):
        def below():
            for came, on in zip(line(z - hop, True, hop - 1), line(z - hop, True, hop) if hop < 3 else [None] * cuts):
                came.wait_recv()
                if on is not None:
                    pl.when(z < 3)(on.start)
            over(z - hop).start()

        def above():
            for came, on in zip(line(z + hop, False, hop - 1), line(z + hop, False, hop) if hop < 3 else [None] * cuts):
                came.wait_recv()
                if on is not None:
                    pl.when(z > 0)(on.start)
            over(z + hop).start()

        pl.when(z >= hop)(below)
        pl.when(z + hop <= 3)(above)

    local = [pltpu.make_async_copy(grads[k], held.at[k], own_sem.at[k]) for k in range(4)]
    local.append(pltpu.make_async_copy(normed, held.at[4], own_sem.at[4]))
    stored = [
        pltpu.make_async_copy(held.at[k], rows(grad_all, (z + 4 - k) % 4), own_sem.at[k]) for k in range(4)
    ]
    stored.append(pltpu.make_async_copy(held.at[4], rows(normed_all, z), own_sem.at[4]))
    pl.when(z < 3)(lambda: line_start(z, True, 0))
    pl.when(z > 0)(lambda: line_start(z, False, 0))
    over(z, True).start()
    for copy in local:
        copy.start()
    for k in range(4):
        grad_over(k).start()
    for copy, store in zip(local, stored):
        copy.wait()
        store.start()
    for hop in range(1, 4):
        hop_step(hop)
    for copy in stored:
        copy.wait()
    for k in range(4):
        grad_over(k).wait()
    over(z, True).wait()
    for k in range(1, 4):
        over((z + k) % 4).wait()
    pl.when(z < 3)(lambda: line_drain(z, True, 0))
    pl.when(z > 0)(lambda: line_drain(z, False, 0))
    for hop in range(1, 3):
        pl.when((z >= hop) & (z < 3))(lambda: line_drain(z - hop, True, hop))
        pl.when((z + hop <= 3) & (z > 0))(lambda: line_drain(z + hop, False, hop))


def gather_rows(normed, grads):
    tok, model = normed.shape
    anyspec = pl.BlockSpec(memory_space=pl.ANY)
    dma = pltpu.SemaphoreType.DMA
    return pl.pallas_call(
        rows_kernel,
        in_specs=[anyspec] * 5,
        out_specs=[anyspec] * 4,
        out_shape=[jax.ShapeDtypeStruct((4 * tok, model), bf16)] * 4,
        scratch_shapes=[dma((2, 3, 4)), dma((2, 3, 4)), dma((2, 4)), dma((2, 4)), dma((5,)), pltpu.VMEM((5, tok, model), bf16)],
        compiler_params=pltpu.CompilerParams(collective_id=3, has_side_effects=True),
        name="gather_rows",
    )(normed, *grads)


def products_kernel(sides, tile, cuts, place, *refs):
    lefts = 1 + max(side for side, _ in sides)
    left_refs = refs[: 2 * lefts]
    right_refs = refs[2 * lefts : 2 * lefts + 2 * len(sides)]
    outs = refs[2 * lefts + 2 * len(sides) : -3]
    turned, stage, right = refs[-3:]
    tok = left_refs[0].shape[0]
    chip_cols = left_refs[0].shape[1] // 4
    half = chip_cols // 2
    step = pl.program_id(0)

    @pl.when(step == 0)
    def _():
        for side in range(lefts):
            for q in range(4):
                cols = pl.ds(pl.multiple_of(place[q] * chip_cols, 128), chip_cols)
                stage[:, :] = jnp.concatenate(
                    [left_refs[2 * side][:, cols], left_refs[2 * side + 1][:, cols]], axis=0
                ).T
                turned[side, q] = stage[pl.ds(pl.multiple_of(place[4] * half, 16), half), :]

    first = 0
    side_now = 0
    for n, (side, tiles) in enumerate(sides):

        @pl.when((step >= first) & (step < first + tiles))
        def _(n=n):
            right[0:tok, :] = right_refs[2 * n][...]
            right[tok:, :] = right_refs[2 * n + 1][...]

        side_now = jnp.where(step >= first, side, side_now)
        first += tiles

    start, index, inside = 0, 0, 0
    for q in range(4):
        block = mm(turned[side_now, q], right[...], ((1,), (0,))).astype(bf16)
        taken = 0
        while taken < half:
            size = min(cuts[index] - inside, half - taken)
            outs[index][inside : inside + size, :] = block[taken : taken + size]
            taken += size
            inside += size
            if inside == cuts[index]:
                index, inside = index + 1, 0


def products(lefts, rights, cuts, name):
    seq = lax.axis_index("seq")
    core, x, y = seq % 2, (seq // 2) % 2, seq // 4
    place = jnp.stack([(1 - y) * 2 + 1 - x, y * 2 + 1 - x, (1 - y) * 2 + x, y * 2 + x, core]).astype(jnp.int32)
    tile = 640
    tok, model = lefts[0][0].shape
    sides = tuple((side, own.shape[1] // tile) for side, own, _ in rights)
    total = sum(tiles for _, tiles in sides)
    in_specs = [
        pl.BlockSpec((tok, model), lambda j, place: (0, 0), pipeline_mode=pl.Buffered(1))
    ] * (2 * len(lefts))
    first = 0
    for _, tiles in sides:

        def index(j, place, first=first, tiles=tiles):
            return (0, jnp.clip(j - first, 0, tiles - 1))

        in_specs += [pl.BlockSpec((tok, tile), index)] * 2
        first += tiles
    half = model // 8
    return pl.pallas_call(
        functools.partial(products_kernel, sides, tile, cuts),
        grid_spec=pltpu.PrefetchScalarGridSpec(
            num_scalar_prefetch=1,
            grid=(total,),
            in_specs=in_specs,
            out_specs=[pl.BlockSpec((rows, tile), lambda j, place: (0, j)) for rows in cuts],
            scratch_shapes=[
                pltpu.VMEM((len(lefts), 4, half, 2 * tok), bf16),
                pltpu.VMEM((2 * half, 2 * tok), bf16),
                pltpu.VMEM((2 * tok, tile), bf16),
            ],
        ),
        out_shape=[jax.ShapeDtypeStruct((rows, total * tile), bf16) for rows in cuts],
        compiler_params=pltpu.CompilerParams(vmem_limit_bytes=56 * 1024 * 1024),
        cost_estimate=pl.CostEstimate(
            flops=2 * 4 * half * 2 * tok * total * tile, bytes_accessed=4 * half * total * tile * 2, transcendentals=0
        ),
        name=name,
    )(place, *[a for pair in lefts for a in pair], *[a for _, own, other in rights for a in (own, other)])


def add_columns(target, sources, start, size, step):
    def one(turn, carry):
        cols = pl.ds(pl.multiple_of(start + turn * step, 128), step)
        total = target[:, cols].astype(f32)
        for source in sources:
            total = total + source[:, cols].astype(f32)
        target[:, cols] = total.astype(target.dtype)
        return carry

    lax.fori_loop(0, size // step, one, 0)


def scatter_kernel(
    main, rest, mlp, mixer_sum, mlp_back,
    held, cross, near, lined,
    load_sem, flow_send, flow_recv, line_send, line_recv, swap_send, swap_recv, own_sem,
):
    s, z, _, beside, across = places()
    chip_diag, chip_beside, chip_across, chip = 0, 1, 2, 3
    rows = held.shape[1] // 4
    cols = held.shape[2]
    cut = cols // 256 * 128
    ff_part = mlp.shape[1] // 3
    parts = (main, rest)
    order = (3 * (1 - z // 2), (2 + 3 * z) % 5, 1 + z % 2, z)

    def remote(src, dst, send, recv, target):
        return pltpu.make_async_remote_copy(
            src_ref=src, dst_ref=dst, send_sem=send, recv_sem=recv, device_id=target, device_id_type=MESH
        )

    def span(k):
        return pl.ds(pl.multiple_of(k * rows, 16), rows)

    def loads(i):
        copies, start = [], 0
        for n, part in enumerate(parts):
            size = part.shape[2]
            copies.append(
                pltpu.make_async_copy(
                    part.at[:, span(order[i]), :], held.at[:, span(order[i]), pl.ds(start, size)], load_sem.at[i, n]
                )
            )
            start += size
        return copies

    left, right = pl.ds(0, cut), pl.ds(cut, cols - cut)

    def block(q, i, side):
        return held.at[q, span(order[i]), side]

    def flow(i, index):
        send, recv = flow_send.at[i, index], flow_recv.at[i, index]
        to_beside, to_across = (beside, z), (across, z)
        if index == 0:
            return remote(block(chip_diag, i, left), cross.at[i, :, left], send, recv, to_across)
        if index == 1:
            return remote(block(chip_diag, i, right), cross.at[i, :, right], send, recv, to_beside)
        if index == 2:
            return remote(block(chip_beside, i, right), near.at[0, i, :, right], send, recv, to_beside)
        if index == 3:
            return remote(block(chip_beside, i, left), near.at[0, i, :, left], send, recv, to_beside)
        if index == 4:
            return remote(block(chip_across, i, left), near.at[1, i, :, left], send, recv, to_across)
        return remote(block(chip_across, i, right), near.at[1, i, :, right], send, recv, to_across)

    def cross_step(i):
        flow(i, 0).wait_recv()
        add_columns(held.at[chip_beside, span(order[i]), :], [cross.at[i]], 0, cut, 512)
        flow(i, 3).start()
        flow(i, 1).wait_recv()
        add_columns(held.at[chip_across, span(order[i]), :], [cross.at[i]], cut, cols - cut, 384)
        flow(i, 5).start()

    def near_step(i):
        for index in (2, 4, 3, 5):
            flow(i, index).wait_recv()
        add_columns(held.at[chip, span(order[i]), :], [near.at[0, i], near.at[1, i]], 0, cols, 640)

    def line(k, slot, target):
        return remote(
            held.at[chip, span(k), :], lined.at[slot], line_send.at[k], line_recv.at[slot], (s, target)
        )

    def absorb(k, slot, source):
        line(k, slot, source).wait_recv()
        add_columns(held.at[chip, span(k), :], [lined.at[slot]], 0, cols, 640)

    def chain(i):
        k = order[i]
        if i == 3:
            pl.when(z > 0)(lambda: absorb(k, k, z - 1))
            pl.when(z < 3)(lambda: absorb(k, 4, z + 1))
            return

        @pl.when(k > z)
        def _():
            pl.when(z > 0)(lambda: absorb(k, k, z - 1))
            line(k, k, z + 1).start()

        @pl.when(k < z)
        def _():
            pl.when(z < 3)(lambda: absorb(k, k, z + 1))
            pl.when(k == z - 1)(lambda: line(k, 4, z - 1).start())
            pl.when(k < z - 1)(lambda: line(k, k, z - 1).start())

    def chain_drain():
        for i in range(3):
            k = order[i]
            line(k, k, (z + 1) % 4).wait_send()

    def pieces():
        for m in range(3):
            yield m, mlp, pl.ds(m * ff_part, ff_part)

    def swap(k):
        to = (z + k) % 4
        here = pl.ds(pl.multiple_of(z * ff_part, 128), ff_part)
        return [
            remote(
                source.at[span(to), at], mlp_back.at[m, :, here], swap_send.at[k - 1, m], swap_recv.at[k - 1, m], (s, to)
            )
            for m, source, at in pieces()
        ]

    own = [
        pltpu.make_async_copy(
            source.at[span(z), at], mlp_back.at[m, :, pl.ds(pl.multiple_of(z * ff_part, 128), ff_part)], own_sem.at[m]
        )
        for m, source, at in pieces()
    ]
    for i in range(4):
        for copy in loads(i):
            copy.start()
    greet([(beside, z), (across, z)] + [(s, (z + k) % 4) for k in range(1, 4)])
    for k in (1, 3, 2):
        for copy in swap(k):
            copy.start()
    for copy in own:
        copy.start()
    for i in range(2):
        for copy in loads(i):
            copy.wait()
        flow(i, 0).start()
        flow(i, 1).start()
        if i == 0:
            flow(i, 2).start()
            flow(i, 4).start()
    for i in range(4):
        cross_step(i)
        if i + 1 < 4:
            flow(i + 1, 2).start()
            flow(i + 1, 4).start()
        if i + 2 < 4:
            for copy in loads(i + 2):
                copy.wait()
            flow(i + 2, 0).start()
            flow(i + 2, 1).start()
        if i > 0:
            near_step(i - 1)
            chain(i - 1)
    near_step(3)
    chain(3)
    done = pltpu.make_async_copy(held.at[chip, span(z), :], mixer_sum, own_sem.at[3])
    done.start()
    for i in range(4):
        for index in range(6):
            flow(i, index).wait_send()
    chain_drain()
    for k in range(1, 4):
        for copy in swap(k):
            copy.wait()
    for copy in own:
        copy.wait()
    done.wait()


def scatter(main, rest, mlp):
    rows = main.shape[1] // 4
    cols = main.shape[2] + rest.shape[2]
    ff_part = mlp.shape[1] // 3
    anyspec = pl.BlockSpec(memory_space=pl.ANY)
    dma = pltpu.SemaphoreType.DMA
    return pl.pallas_call(
        scatter_kernel,
        in_specs=[anyspec] * 3,
        out_specs=[anyspec] * 2,
        out_shape=[
            jax.ShapeDtypeStruct((rows, cols), bf16),
            jax.ShapeDtypeStruct((3, rows, 4 * ff_part), bf16),
        ],
        scratch_shapes=[
            pltpu.VMEM((4, 4 * rows, cols), bf16),
            pltpu.VMEM((4, rows, cols), bf16),
            pltpu.VMEM((2, 4, rows, cols), bf16),
            pltpu.VMEM((5, rows, cols), bf16),
            dma((4, 2)), dma((4, 6)), dma((4, 6)), dma((4,)), dma((5,)), dma((3, 3)), dma((3, 3)), dma((4,)),
        ],
        compiler_params=pltpu.CompilerParams(
            collective_id=2, has_side_effects=True, vmem_limit_bytes=52 * 1024 * 1024
        ),
        name="scatter_gradients",
    )(main, rest, mlp)


def gather_plain(mixer, gate, up, down):
    groups = lax.axis_size("fsdp")
    part_rows, ff = gate.shape
    own = jnp.stack([w.reshape(part_rows, groups, ff // groups) for w in (gate, up, down)], axis=2)
    mine = lax.all_to_all(jnp.transpose(own, (1, 0, 2, 3)), "fsdp", 0, 0, tiled=True)
    return lax.all_gather(mixer, both, axis=0, tiled=True), mine.reshape(groups * part_rows, -1)


def from_line(shard):
    count = lax.axis_size("fsdp")
    return [shard] + [
        lax.ppermute(shard, "fsdp", [(i, (i + k) % count) for i in range(count)]) for k in range(1, count)
    ]


def swap_cores(shard):
    count = lax.axis_size("seq")
    return lax.ppermute(shard, "seq", [(i, i + 1 - 2 * (i % 2)) for i in range(count)])


def swap_beside(shard):
    return lax.ppermute(shard, "seq", [(i, i ^ 2) for i in range(8)])


def swap_across(shard):
    return lax.ppermute(shard, "seq", [(i, i ^ 4) for i in range(8)])


def add_low(left, right):
    return (left.astype(f32) + right.astype(f32)).astype(bf16)


def scatter_paired(normed, grad_both, grad_mix, mixed, rest, mlp_sum):
    seq = lax.axis_index("seq")
    core, x, y = seq % 2, (seq // 2) % 2, seq // 4
    main = products(
        [(normed, swap_cores(normed)), (grad_mix, swap_cores(grad_mix))],
        [(0, grad_both, swap_cores(grad_both)), (1, mixed, swap_cores(mixed))],
        (lru_rows(normed),),
        "mixer_products",
    )[0]
    grouped = rest.reshape(4, 2, -1, rest.shape[1])
    own = lax.dynamic_index_in_dim(grouped, core, 1, False)
    other = swap_cores(lax.dynamic_index_in_dim(grouped, 1 - core, 1, False))
    rest = (own.astype(f32) + other.astype(f32)).astype(bf16)
    rest = jnp.concatenate(
        [
            lax.dynamic_slice_in_dim(rest, q, 1, 0)
            for q in ((1 - y) * 2 + 1 - x, y * 2 + 1 - x, (1 - y) * 2 + x, y * 2 + x)
        ],
        axis=0,
    )
    return scatter(main.reshape(4, -1, main.shape[1]), rest, mlp_sum)


def lru_rows(values):
    return values.shape[1] // 2


def scatter_plain(normed, grad_both, grad_mix, mixed, rest, mlp_sum):
    groups = lax.axis_size("fsdp")
    term_wide = mm(normed, grad_both, ((0,), (0,))).astype(bf16)
    term_out = mm(grad_mix, mixed, ((0,), (0,))).astype(bf16)
    mixer_sum = lax.psum_scatter(
        jnp.concatenate([term_wide, term_out, rest], axis=1), "seq", scatter_dimension=0, tiled=True
    )
    mixer_sum = lax.psum_scatter(mixer_sum, "fsdp", scatter_dimension=0, tiled=True)
    ff_part = mlp_sum.shape[1] // 3
    part_rows = mlp_sum.shape[0] // groups
    mlp_sum = mlp_sum.reshape(groups, part_rows, 3, ff_part)
    mlp_back = lax.all_to_all(mlp_sum, "fsdp", 0, 0, tiled=True)
    mlp_back = jnp.transpose(mlp_back, (2, 1, 0, 3)).reshape(3, part_rows, groups * ff_part)
    return mixer_sum, mlp_back


def call_heads(kernel, width, heads, ins, outs, scratch, name):
    def spec(rows_cols):
        rows, by_row = rows_cols
        if by_row:
            return pl.BlockSpec((rows, width), lambda h: (h, 0))
        return pl.BlockSpec((rows, width), lambda h: (0, h))

    in_specs = [spec((width, True)) if rowwise else spec((a.shape[0], False)) for a, rowwise in ins]
    out_specs = [spec((width, True)) if rowwise else spec((rows, False)) for rows, _, rowwise in outs]
    out_shape = [
        jax.ShapeDtypeStruct((heads * width, width) if rowwise else (rows, heads * width), kind)
        for rows, kind, rowwise in outs
    ]
    return pl.pallas_call(
        kernel,
        grid=(heads,),
        in_specs=in_specs,
        out_specs=out_specs,
        out_shape=out_shape,
        scratch_shapes=[pltpu.VMEM((rows, width), f32) for rows in scratch],
        compiler_params=pltpu.CompilerParams(vmem_limit_bytes=40 * 1024 * 1024),
        name=name,
    )(*[a for a, _ in ins])


def on_device(
    block_input,
    cotangent,
    mixer_gain,
    branch_proj,
    gelu_proj,
    conv_taps,
    conv_bias,
    rate_blocks,
    input_blocks,
    rate_bias,
    input_bias,
    decay_param,
    out_proj,
    mlp_gain,
    gate_proj,
    up_proj,
    down_proj,
):
    groups = lax.axis_size("fsdp")
    part_rows, lru = branch_proj.shape
    width = rate_blocks.shape[1]
    heads = lru // width
    margin = conv_taps.shape[0] - 1
    tokens = block_input[0].astype(f32)
    tok_count, model = tokens.shape
    ff = gate_proj.shape[1]
    ff_part = ff // groups
    grad_out = cotangent[0]

    smalls = jnp.stack(
        [conv_taps[k] for k in range(margin + 1)]
        + [conv_bias, rate_bias, input_bias, decay_param, mixer_gain, mlp_gain],
        axis=1,
    )
    small_count = smalls.shape[1]
    smalls = jnp.pad(smalls, ((0, 0), (0, 128 - small_count)))
    mixer_own = jnp.concatenate(
        [smalls, rate_blocks, input_blocks, branch_proj, gelu_proj, out_proj], axis=1
    )
    custom = lax.axis_size("seq") == 8 and groups == 4
    if custom:
        mixer_w, mlp_mine = gather(mixer_own, gate_proj, up_proj, down_proj)
    else:
        mixer_w, mlp_mine = gather_plain(mixer_own, gate_proj, up_proj, down_proj)
    mlp_w = lax.all_gather(mlp_mine, "seq", axis=0, tiled=True)
    grad_out_late = lax.optimization_barrier((grad_out, mlp_mine))[0]
    if custom:
        grad_pieces = from_line(grad_out_late)
    first = lax.optimization_barrier(mixer_w[:, : 128 + 2 * width])
    wide = mixer_w[:, 128 + 2 * width : 128 + 2 * width + 2 * lru]
    proj_out = mixer_w[:, 128 + 2 * width + 2 * lru :]

    table = first[:, :small_count].astype(f32).T
    blocks_rate = first[:, 128 : 128 + width]
    blocks_input = first[:, 128 + width :]
    param_decay = table[margin + 4]
    gain_one = table[margin + 5]
    gain_two = table[margin + 6]
    small = jnp.concatenate(
        [
            table[: margin + 4],
            jax.nn.softplus(-param_decay)[None],
            -jax.nn.sigmoid(-param_decay)[None],
            jnp.zeros((16 - margin - 6, lru), f32),
        ],
        axis=0,
    )

    normed = norm_rows(tokens, gain_one).astype(bf16)
    both_pre = mm(normed, wide, ((1,), (0,)))
    branch = both_pre[:, :lru].astype(bf16)
    gelu_pre = both_pre[:, lru:]
    prior = from_behind(branch[tok_count - margin :], "seq", 1).astype(f32)
    prior = jnp.concatenate([jnp.zeros((8 - margin, lru), f32), prior], axis=0)
    conv, rate_pre, input_pre, cum, local = call_heads(
        mixer_forward,
        width,
        heads,
        [(branch, False), (prior, False), (small, False), (blocks_rate, True), (blocks_input, True)],
        [(tok_count, bf16, False)] + [(tok_count, f32, False)] * 4,
        [tok_count + 8],
        "mixer_forward",
    )
    carried = prefix((cum[-1], local[-1]), "seq", False)
    states = local + cum * carried[None]
    mixed = (states * jax.nn.gelu(gelu_pre, approximate=True)).astype(bf16)
    middle = tokens + mm(mixed, proj_out, ((1,), (1,)))
    normed_two = norm_rows(middle, gain_two).astype(bf16)

    if custom:
        normed_all, normed_other, grad_out_all, grad_out_other = gather_rows(normed_two, grad_pieces)
    else:
        normed_all = lax.all_gather(normed_two, "fsdp", axis=0, tiled=True)
        grad_out_all = lax.all_gather(grad_out_late, "fsdp", axis=0, tiled=True)
    w_gate, w_up, w_down = mlp_w[:, :ff_part], mlp_w[:, ff_part : 2 * ff_part], mlp_w[:, 2 * ff_part :]
    gate = mm(normed_all, w_gate, ((1,), (0,)))
    up_val = mm(normed_all, w_up, ((1,), (0,)))
    gelu_gate, gelu_slope = gelu_parts(gate)
    hidden = (gelu_gate * up_val).astype(bf16)
    grad_hidden = mm(grad_out_all, w_down, ((1,), (0,)))
    grad_gate = (grad_hidden * up_val * gelu_slope).astype(bf16)
    grad_up = (grad_hidden * gelu_gate).astype(bf16)
    grad_normed_part = mm(grad_gate, w_gate, ((1,), (1,))) + mm(grad_up, w_up, ((1,), (1,)))
    grad_normed_two = lax.psum_scatter(
        grad_normed_part.astype(bf16), "fsdp", scatter_dimension=0, tiled=True
    )
    out_part = mm(hidden, w_down, ((1,), (1,))).astype(bf16)
    if custom:
        half = model // 16
        blocks = products(
            [(normed_all, normed_other), (grad_out_all, grad_out_other)],
            [
                (0, grad_gate, swap_cores(grad_gate)),
                (0, grad_up, swap_cores(grad_up)),
                (1, hidden, swap_cores(hidden)),
            ],
            (half,) * 6 + (2 * half,),
            "feed_forward_products",
        )
        blocks, grad_normed_two = lax.optimization_barrier((blocks, grad_normed_two))
        diag_low, diag_high, beside_low, beside_high, across_low, across_high, mine = blocks
        by_across = swap_across(diag_low)
        by_beside = swap_beside(diag_high)
    else:
        grad_pair = jnp.concatenate([grad_gate, grad_up], axis=1)
        term_pair = mm(normed_all, grad_pair, ((0,), (0,))).astype(bf16)
        term_down = mm(grad_out_all, hidden, ((0,), (0,))).astype(bf16)
        pair_sum = lax.psum_scatter(term_pair, "seq", scatter_dimension=0, tiled=True)
        down_sum = lax.psum_scatter(term_down, "seq", scatter_dimension=0, tiled=True)
        mlp_sum = jnp.concatenate([pair_sum, down_sum], axis=1)
    out_sum = lax.psum_scatter(out_part, "fsdp", scatter_dimension=0, tiled=True)
    block_output = (middle + out_sum.astype(f32)).astype(bf16)[None]
    grad_normed_two = grad_normed_two.astype(f32)

    second_pull = jax.vjp(norm_rows, middle, gain_two)[1]
    grad_mid_part, grad_gain_two = second_pull(grad_normed_two)
    grad_middle = grad_out.astype(f32) + grad_mid_part
    grad_mix = grad_middle.astype(bf16)
    grad_mixed = mm(grad_mix, proj_out, ((1,), (0,)))
    if custom:
        beside_high, across_low, grad_mixed = lax.optimization_barrier((beside_high, across_low, grad_mixed))
        from_beside_high = swap_beside(beside_high)
        from_across_low = swap_across(across_low)
    carried_rows = jnp.broadcast_to(carried[None], (8, lru))
    grad_gelu_pre, rev_cum, rev_grad, pair_grad = call_heads(
        mixer_backward_scan,
        width,
        heads,
        [(a, False) for a in (grad_mixed, gelu_pre, rate_pre, cum, local, carried_rows, small)],
        [(tok_count, bf16, False), (tok_count, f32, False), (tok_count, f32, False), (8, f32, False)],
        [tok_count + 8],
        "mixer_backward_scan",
    )
    incoming = prefix((cum[-1], pair_grad[0]), "seq", True)
    incoming_rows = jnp.broadcast_to(incoming[None], (8, lru))
    own, head, rate_w_grad, input_w_grad, sums = call_heads(
        mixer_backward,
        width,
        heads,
        [
            (a, False)
            for a in (rev_cum, rev_grad, incoming_rows, cum, local, carried_rows, rate_pre, input_pre, conv, branch, prior, small)
        ]
        + [(blocks_rate, True), (blocks_input, True)],
        [(tok_count, f32, False), (8, f32, False), (0, bf16, True), (0, bf16, True), (8, f32, False)],
        [tok_count + 8, tok_count + 16],
        "mixer_backward",
    )
    if custom:
        by_across, by_beside, own = lax.optimization_barrier((by_across, by_beside, own))
        beside_low, across_high = add_low(beside_low, by_across), add_low(across_high, by_beside)
        beside_low, across_high, own = lax.optimization_barrier((beside_low, across_high, own))
        from_beside_low = swap_beside(beside_low)
        from_across_high = swap_across(across_high)
        mlp_sum = mine.astype(f32) + jnp.concatenate(
            [
                from_across_low.astype(f32) + from_beside_low.astype(f32),
                from_across_high.astype(f32) + from_beside_high.astype(f32),
            ],
            axis=0,
        )
        mlp_sum = mlp_sum.astype(bf16)
    received = from_behind(head[8 - margin :], "seq", -1)
    grad_branch = jnp.concatenate(
        [own[: tok_count - margin], own[tok_count - margin :] + received], axis=0
    ).astype(bf16)
    grad_both = jnp.concatenate([grad_branch, grad_gelu_pre], axis=1)
    grad_normed = mm(grad_both, wide, ((1,), (1,)))
    first_pull = jax.vjp(norm_rows, tokens, gain_one)[1]
    grad_tok_part, grad_gain_one = first_pull(grad_normed)
    input_grad = (grad_middle + grad_tok_part).astype(bf16)[None]
    vectors = jnp.concatenate([sums, grad_gain_one[None], grad_gain_two[None]], axis=0).T
    vectors = jnp.pad(vectors, ((0, 0), (0, 128 - vectors.shape[1]))).astype(bf16)
    rest = jnp.concatenate([rate_w_grad, input_w_grad, vectors], axis=1)
    scatter_all = scatter_paired if custom else scatter_plain
    mixer_sum, mlp_back = scatter_all(normed, grad_both, grad_mix, mixed, rest, mlp_sum)
    mlp_grads = [mlp_back[m].astype(f32) for m in range(3)]
    mixer_sum = mixer_sum.astype(f32)
    edges = [lru, 2 * lru, 3 * lru, 3 * lru + width, 3 * lru + 2 * width]
    dbranch, dgelu, dout, drate, dinput, vec = jnp.split(mixer_sum, edges, axis=1)
    vec = vec.T
    return (
        block_output,
        input_grad,
        vec[8],
        dbranch,
        dgelu,
        vec[: margin + 1],
        vec[7],
        drate,
        dinput,
        vec[4],
        vec[5],
        vec[6],
        dout,
        vec[9],
        mlp_grads[0],
        mlp_grads[1],
        mlp_grads[2],
    )


def solution(mesh):
    tokens = P("fsdp", "seq", None)
    vector = P(both)
    matrix = P(both, None)
    taps = P(None, both)
    return jax.shard_map(
        on_device,
        mesh=mesh,
        in_specs=(
            tokens, tokens, vector, matrix, matrix, taps, vector, matrix, matrix,
            vector, vector, vector, matrix, vector, matrix, matrix, matrix,
        ),
        out_specs=(
            tokens, tokens, vector, matrix, matrix, taps, vector, matrix, matrix,
            vector, vector, vector, matrix, vector, matrix, matrix, matrix,
        ),
        check_vma=False,
    )
```

```python
import functools

import jax
import jax.numpy as jnp
from jax import lax
from jax.experimental import pallas as pl
from jax.experimental.pallas import tpu as pltpu
from jax.sharding import PartitionSpec as P

epsilon = 1e-06
f32 = jnp.float32
bf16 = jnp.bfloat16
both = ("seq", "fsdp")
MESH = pl.DeviceIdType.MESH
TAP, CONV_BIAS, RATE_BIAS, INPUT_BIAS, SOFT, SOFT_SLOPE = 0, 4, 5, 6, 7, 8
GELU_C = 0.7978845608028654
GELU_A = 0.044715


def from_behind(shard, axis, by):
    devices = lax.axis_size(axis)
    pairs = [(i, i + by) for i in range(devices) if 0 <= i + by < devices]
    return lax.ppermute(shard, axis, pairs)


def prefix(part, axis, reverse):
    count = lax.axis_size(axis)
    place = lax.axis_index(axis)
    gathered = lax.all_gather(jnp.stack(part), axis)
    state = jnp.zeros_like(part[1])
    for hop in range(count):
        source = count - 1 - hop if reverse else hop
        ahead = source > place if reverse else source < place
        state = jnp.where(ahead, gathered[source, 1] + gathered[source, 0] * state, state)
    return state


def norm_rows(values, scales):
    return values * lax.rsqrt(jnp.mean(values * values, axis=-1, keepdims=True) + epsilon) * scales


def gelu_parts(x):
    inner = jnp.tanh(GELU_C * (x + GELU_A * x * x * x))
    return 0.5 * x * (1.0 + inner), 0.5 * (1.0 + inner) + 0.5 * x * (1.0 - inner * inner) * (
        GELU_C * (1.0 + 3.0 * GELU_A * x * x)
    )


def mm(left, right, dims):
    return lax.dot_general(left, right, (dims, ((), ())), preferred_element_type=f32)


def sigmoid(x):
    return 1.0 / (1.0 + jnp.exp(-x))


def scan_rows(decay, value, reverse):
    rows = decay.shape[0]
    place = lax.broadcasted_iota(jnp.int32, decay.shape, 0)
    step = 1
    while step < rows:
        shift = rows - step if reverse else step
        inside = place < rows - step if reverse else place >= step
        before_value = jnp.where(inside, pltpu.roll(value, shift, 0), 0.0)
        before_decay = jnp.where(inside, pltpu.roll(decay, shift, 0), 1.0)
        value = value + decay * before_value
        decay = decay * before_decay
        step *= 2
    return decay, value


def gates(rate_pre, input_pre, soft):
    rate = sigmoid(rate_pre)
    log_decay = -8.0 * rate * soft
    decay = jnp.exp(log_decay)
    square = decay * decay
    root = jnp.sqrt(-jnp.tanh(log_decay) * (1.0 + square))
    return rate, decay, square, root, sigmoid(input_pre)


def mixer_forward(branch, prior, small, rate_w, input_w, conv, rate_pre, input_pre, cum, local, ext):
    rows = branch.shape[0]
    ext[0:8, :] = prior[...]
    ext[8:, :] = branch[...].astype(f32)
    total = small[CONV_BIAS : CONV_BIAS + 1, :] + small[TAP : TAP + 1, :] * ext[8:, :]
    for offset in range(1, 4):
        total = total + small[TAP + offset : TAP + offset + 1, :] * ext[pl.ds(8 - offset, rows), :]
    low = total.astype(bf16)
    conv[...] = low
    rate = mm(low, rate_w[...], ((1,), (0,))) + small[RATE_BIAS : RATE_BIAS + 1, :]
    inp = mm(low, input_w[...], ((1,), (0,))) + small[INPUT_BIAS : INPUT_BIAS + 1, :]
    rate_pre[...] = rate
    input_pre[...] = inp
    _, decay, _, root, opened = gates(rate, inp, small[SOFT : SOFT + 1, :])
    product, states = scan_rows(decay, root * opened * low.astype(f32), False)
    cum[...] = product
    local[...] = states


def mixer_backward_scan(grad_mixed, gelu_pre, rate_pre, cum, local, carried, small, grad_pre, rev_cum, rev_grad, pair, ext):
    rows = grad_mixed.shape[0]
    states = local[...] + cum[...] * carried[0:1, :]
    value, slope = gelu_parts(gelu_pre[...])
    grad = grad_mixed[...]
    grad_pre[...] = (grad * states * slope).astype(bf16)
    decay = jnp.exp(-8.0 * sigmoid(rate_pre[...]) * small[SOFT : SOFT + 1, :])
    ext[0:rows, :] = decay
    ext[rows:, :] = jnp.ones((8, decay.shape[1]), f32)
    product, back = scan_rows(ext[pl.ds(1, rows), :], grad * value, True)
    rev_cum[...] = product
    rev_grad[...] = back
    pair[...] = jnp.broadcast_to(decay[0:1, :] * back[0:1, :], pair.shape)


def mixer_backward(
    rev_cum, rev_grad, incoming, cum, local, carried, rate_pre, input_pre, conv, branch, prior, small, rate_w, input_w,
    own, head, rate_w_grad, input_w_grad, sums, ext, gext,
):
    rows = rev_cum.shape[0]
    soft = small[SOFT : SOFT + 1, :]
    grad_states = rev_grad[...] + rev_cum[...] * incoming[0:1, :]
    rate, decay, square, root, opened = gates(rate_pre[...], input_pre[...], soft)
    ext[0:8, :] = jnp.broadcast_to(carried[0:1, :], (8, carried.shape[1]))
    ext[8:, :] = local[...] + cum[...] * carried[0:1, :]
    before = ext[pl.ds(7, rows), :]
    low = conv[...]
    conv_in = low.astype(f32)
    grad_log = grad_states * decay * before - grad_states * opened * conv_in * square / root
    driven = grad_states * root
    grad_input = (driven * conv_in * opened * (1.0 - opened)).astype(bf16)
    by_rate = grad_log * (-8.0 * rate)
    grad_rate = (by_rate * soft * (1.0 - rate)).astype(bf16)
    sums[6:7, :] = jnp.sum(by_rate, axis=0, keepdims=True) * small[SOFT_SLOPE : SOFT_SLOPE + 1, :]
    sums[4:5, :] = jnp.sum(grad_rate.astype(f32), axis=0, keepdims=True)
    sums[5:6, :] = jnp.sum(grad_input.astype(f32), axis=0, keepdims=True)
    rate_w_grad[...] = mm(low, grad_rate, ((0,), (0,))).astype(rate_w_grad.dtype)
    input_w_grad[...] = mm(low, grad_input, ((0,), (0,))).astype(input_w_grad.dtype)
    grad_conv = (
        driven * opened
        + mm(grad_rate, rate_w[...], ((1,), (1,)))
        + mm(grad_input, input_w[...], ((1,), (1,)))
    )
    sums[7:8, :] = jnp.sum(grad_conv, axis=0, keepdims=True)
    ext[0:8, :] = prior[...]
    ext[8:, :] = branch[...].astype(f32)
    gext[0:8, :] = jnp.zeros((8, grad_conv.shape[1]), f32)
    gext[8 : 8 + rows, :] = grad_conv
    gext[8 + rows :, :] = jnp.zeros((8, grad_conv.shape[1]), f32)
    back = jnp.zeros_like(grad_conv)
    front = jnp.zeros((8, grad_conv.shape[1]), f32)
    for offset in range(4):
        tap = small[TAP + offset : TAP + offset + 1, :]
        sums[offset : offset + 1, :] = jnp.sum(
            grad_conv * ext[pl.ds(8 - offset, rows), :], axis=0, keepdims=True
        )
        back = back + tap * gext[pl.ds(8 + offset, rows), :]
        front = front + tap * gext[pl.ds(offset, 8), :]
    own[...] = back
    head[...] = front


def places():
    s = lax.axis_index("seq")
    z = lax.axis_index("fsdp")
    core = s + 1 - 2 * (s % 2)
    beside = s + 2 - 4 * ((s // 2) % 2)
    across = s + 4 - 8 * (s // 4)
    return s, z, core, beside, across


def greet(peers):
    barrier = pltpu.get_barrier_semaphore()
    for peer in peers:
        pl.semaphore_signal(barrier, inc=1, device_id=peer, device_id_type=MESH)
    pl.semaphore_wait(barrier, len(peers))


def gather_kernel(
    mixer, gate, up, down, mixer_all, mlp_mine,
    flow_send, flow_recv, line_send, line_recv, swap_send, swap_recv, own_sem,
):
    s, z, core, beside, across = places()
    rows, cols = mixer.shape
    ff_part = mlp_mine.shape[1] // 3
    cut = cols // 256 * 128
    diag = beside + across - s
    greet([(core, z), (beside, z), (across, z)] + [(s, (z + k) % 4) for k in range(1, 4)])

    def remote(src, dst, send, recv, target):
        return pltpu.make_async_remote_copy(
            src_ref=src, dst_ref=dst, send_sem=send, recv_sem=recv, device_id=target, device_id_type=MESH
        )

    def piece(seq, zz, half=None):
        span = pl.ds(pl.multiple_of((seq * 4 + zz) * rows, 16), rows)
        if half is None:
            return mixer_all.at[span, :]
        return mixer_all.at[span, pl.ds(0, cut) if half == 0 else pl.ds(cut, cols - cut)]

    def flow(zz, index, seq, half, target, src=None):
        ref = piece(seq, zz, half)
        return remote(
            ref if src is None else src, ref, flow_send.at[zz, index], flow_recv.at[zz, index], (target, z)
        )

    def sends(zz, src=None):
        return [
            flow(zz, 0, s, None, beside, src),
            flow(zz, 1, s, None, across, src),
            flow(zz, 4, s, None, core, src),
        ]

    def spread(zz, src=None):
        for copy in sends(zz, src):
            copy.start()

    def relay(zz):
        flow(zz, 0, beside, None, beside).wait_recv()
        flow(zz, 3, beside, 0, across).start()
        flow(zz, 5, beside, None, core).start()
        flow(zz, 1, across, None, across).wait_recv()
        flow(zz, 2, across, 1, beside).start()
        flow(zz, 6, across, None, core).start()

    def finish(zz):
        flow(zz, 3, diag, 0, across).wait_recv()
        flow(zz, 7, diag, 0, core).start()
        flow(zz, 2, diag, 1, beside).wait_recv()
        flow(zz, 8, diag, 1, core).start()

    def drain(zz, src=None):
        for copy in sends(zz, src):
            copy.wait_send()
        flow(zz, 3, beside, 0, across).wait_send()
        flow(zz, 5, beside, None, core).wait_send()
        flow(zz, 2, across, 1, beside).wait_send()
        flow(zz, 6, across, None, core).wait_send()
        flow(zz, 7, diag, 0, core).wait_send()
        flow(zz, 8, diag, 1, core).wait_send()
        flip = core - s
        flow(zz, 4, core, None, core).wait_recv()
        flow(zz, 5, beside + flip, None, core).wait_recv()
        flow(zz, 6, across + flip, None, core).wait_recv()
        flow(zz, 7, diag + flip, 0, core).wait_recv()
        flow(zz, 8, diag + flip, 1, core).wait_recv()

    def line(zz, up_way, hop, src=None):
        ref = piece(s, zz)
        way = 0 if up_way else 1
        target = z + 1 if up_way else z - 1
        return remote(
            ref if src is None else src, ref, line_send.at[way, hop], line_recv.at[way, hop], (s, target)
        )

    def line_hop(hop):
        def below():
            line(z - hop, True, hop - 1).wait_recv()
            pl.when(z < 3)(lambda: line(z - hop, True, hop).start())

        def above():
            line(z + hop, False, hop - 1).wait_recv()
            pl.when(z > 0)(lambda: line(z + hop, False, hop).start())

        pl.when(z >= hop)(below)
        pl.when(z + hop <= 3)(above)

    def at_hop(hop, act):
        pl.when(z >= hop)(lambda: act(z - hop))
        pl.when(z + hop <= 3)(lambda: act(z + hop))

    def landing(m, zz):
        return mlp_mine.at[pl.ds(pl.multiple_of(zz * rows, 16), rows), pl.ds(m * ff_part, ff_part)]

    def columns(m, zz):
        return (gate, up, down)[m].at[:, pl.ds(pl.multiple_of(zz * ff_part, 128), ff_part)]

    def swap(k, m, arriving=False):
        to = (z + k) % 4
        came = (z + 4 - k) % 4
        return remote(
            columns(m, to), landing(m, came if arriving else z), swap_send.at[k - 1, m], swap_recv.at[k - 1, m], (s, to)
        )

    local = [pltpu.make_async_copy(columns(m, z), landing(m, z), own_sem.at[m]) for m in range(3)]
    local.append(pltpu.make_async_copy(mixer, piece(s, z), own_sem.at[3]))

    pl.when(z < 3)(lambda: line(z, True, 0, mixer).start())
    pl.when(z > 0)(lambda: line(z, False, 0, mixer).start())
    spread(z, mixer)
    for copy in local:
        copy.start()
    line_hop(1)
    at_hop(1, spread)
    relay(z)
    line_hop(2)
    at_hop(2, spread)
    finish(z)
    at_hop(1, relay)
    line_hop(3)
    at_hop(3, spread)
    for k in (1, 3, 2):
        for m in range(3):
            swap(k, m).start()
    at_hop(1, finish)
    at_hop(2, relay)
    at_hop(3, relay)
    at_hop(2, finish)
    at_hop(3, finish)
    drain(z, mixer)
    for hop in range(1, 4):
        at_hop(hop, drain)
    for copy in local:
        copy.wait()
    for k in (1, 3, 2):
        for m in range(3):
            swap(k, m).wait_send()
            swap(k, m, True).wait_recv()
    pl.when(z < 3)(lambda: line(z, True, 0, mixer).wait_send())
    pl.when(z > 0)(lambda: line(z, False, 0, mixer).wait_send())
    for hop in range(1, 3):
        pl.when((z >= hop) & (z < 3))(lambda: line(z - hop, True, hop).wait_send())
        pl.when((z + hop <= 3) & (z > 0))(lambda: line(z + hop, False, hop).wait_send())


def gather(mixer, gate, up, down):
    rows, cols = mixer.shape
    ff_part = gate.shape[1] // 4
    anyspec = pl.BlockSpec(memory_space=pl.ANY)
    dma = pltpu.SemaphoreType.DMA
    return pl.pallas_call(
        gather_kernel,
        in_specs=[anyspec] * 4,
        out_specs=[anyspec] * 2,
        out_shape=[
            jax.ShapeDtypeStruct((32 * rows, cols), bf16),
            jax.ShapeDtypeStruct((4 * rows, 3 * ff_part), bf16),
        ],
        scratch_shapes=[
            dma((4, 9)), dma((4, 9)), dma((2, 3)), dma((2, 3)), dma((3, 3)), dma((3, 3)), dma((4,)),
        ],
        compiler_params=pltpu.CompilerParams(collective_id=1, has_side_effects=True),
        name="gather_weights",
    )(mixer, gate, up, down)


def rows_kernel(
    normed, grad0, grad1, grad2, grad3, normed_all, normed_other, grad_all, grad_other,
    line_send, line_recv, core_send, core_recv, own_sem, held,
):
    s, z, core, _, _ = places()
    tok = normed.shape[0]
    cuts = 4
    grads = (grad0, grad1, grad2, grad3)
    greet([(core, z)] + [(s, (z + k) % 4) for k in range(1, 4)])

    def rows(ref, zz):
        return ref.at[pl.ds(pl.multiple_of(zz * tok, 16), tok), :]

    def remote(src, dst, send, recv, target):
        return pltpu.make_async_remote_copy(
            src_ref=src, dst_ref=dst, send_sem=send, recv_sem=recv, device_id=target, device_id_type=MESH
        )

    def parts(ref):
        size = tok // cuts
        return [ref.at[pl.ds(n * size, size), :] for n in range(cuts)]

    def line(zz, up_way, hop):
        way = 0 if up_way else 1
        target = z + 1 if up_way else z - 1
        src = normed if hop == 0 else rows(normed_all, zz)
        dst = rows(normed_all, zz)
        return [
            remote(a, b, line_send.at[way, hop, n], line_recv.at[way, hop, n], (s, target))
            for n, (a, b) in enumerate(zip(parts(src), parts(dst)))
        ]

    def over(zz, own=False):
        src = normed if own else rows(normed_all, zz)
        return remote(src, rows(normed_other, zz), core_send.at[0, zz], core_recv.at[0, zz], (core, z))

    def grad_over(k):
        zz = (z + 4 - k) % 4
        return remote(grads[k], rows(grad_other, zz), core_send.at[1, zz], core_recv.at[1, zz], (core, z))

    def line_start(zz, up_way, hop):
        for copy in line(zz, up_way, hop):
            copy.start()

    def line_drain(zz, up_way, hop):
        for copy in line(zz, up_way, hop):
            copy.wait_send()

    def hop_step(hop):
        def below():
            for came, on in zip(line(z - hop, True, hop - 1), line(z - hop, True, hop) if hop < 3 else [None] * cuts):
                came.wait_recv()
                if on is not None:
                    pl.when(z < 3)(on.start)
            over(z - hop).start()

        def above():
            for came, on in zip(line(z + hop, False, hop - 1), line(z + hop, False, hop) if hop < 3 else [None] * cuts):
                came.wait_recv()
                if on is not None:
                    pl.when(z > 0)(on.start)
            over(z + hop).start()

        pl.when(z >= hop)(below)
        pl.when(z + hop <= 3)(above)

    local = [pltpu.make_async_copy(grads[k], held.at[k], own_sem.at[k]) for k in range(4)]
    local.append(pltpu.make_async_copy(normed, held.at[4], own_sem.at[4]))
    stored = [
        pltpu.make_async_copy(held.at[k], rows(grad_all, (z + 4 - k) % 4), own_sem.at[k]) for k in range(4)
    ]
    stored.append(pltpu.make_async_copy(held.at[4], rows(normed_all, z), own_sem.at[4]))
    pl.when(z < 3)(lambda: line_start(z, True, 0))
    pl.when(z > 0)(lambda: line_start(z, False, 0))
    over(z, True).start()
    for copy in local:
        copy.start()
    for k in range(4):
        grad_over(k).start()
    for copy, store in zip(local, stored):
        copy.wait()
        store.start()
    for hop in range(1, 4):
        hop_step(hop)
    for copy in stored:
        copy.wait()
    for k in range(4):
        grad_over(k).wait()
    over(z, True).wait()
    for k in range(1, 4):
        over((z + k) % 4).wait()
    pl.when(z < 3)(lambda: line_drain(z, True, 0))
    pl.when(z > 0)(lambda: line_drain(z, False, 0))
    for hop in range(1, 3):
        pl.when((z >= hop) & (z < 3))(lambda: line_drain(z - hop, True, hop))
        pl.when((z + hop <= 3) & (z > 0))(lambda: line_drain(z + hop, False, hop))


def gather_rows(normed, grads):
    tok, model = normed.shape
    anyspec = pl.BlockSpec(memory_space=pl.ANY)
    dma = pltpu.SemaphoreType.DMA
    return pl.pallas_call(
        rows_kernel,
        in_specs=[anyspec] * 5,
        out_specs=[anyspec] * 4,
        out_shape=[jax.ShapeDtypeStruct((4 * tok, model), bf16)] * 4,
        scratch_shapes=[dma((2, 3, 4)), dma((2, 3, 4)), dma((2, 4)), dma((2, 4)), dma((5,)), pltpu.VMEM((5, tok, model), bf16)],
        compiler_params=pltpu.CompilerParams(collective_id=3, has_side_effects=True),
        name="gather_rows",
    )(normed, *grads)


def products_kernel(sides, tile, cuts, place, *refs):
    lefts = 1 + max(side for side, _ in sides)
    left_refs = refs[: 2 * lefts]
    right_refs = refs[2 * lefts : 2 * lefts + 2 * len(sides)]
    outs = refs[2 * lefts + 2 * len(sides) : -3]
    turned, stage, right = refs[-3:]
    tok = left_refs[0].shape[0]
    chip_cols = left_refs[0].shape[1] // 4
    half = chip_cols // 2
    step = pl.program_id(0)

    @pl.when(step == 0)
    def _():
        for side in range(lefts):
            for q in range(4):
                cols = pl.ds(pl.multiple_of(place[q] * chip_cols, 128), chip_cols)
                stage[:, :] = jnp.concatenate(
                    [left_refs[2 * side][:, cols], left_refs[2 * side + 1][:, cols]], axis=0
                ).T
                turned[side, q] = stage[pl.ds(pl.multiple_of(place[4] * half, 16), half), :]

    first = 0
    side_now = 0
    for n, (side, tiles) in enumerate(sides):

        @pl.when((step >= first) & (step < first + tiles))
        def _(n=n):
            right[0:tok, :] = right_refs[2 * n][...]
            right[tok:, :] = right_refs[2 * n + 1][...]

        side_now = jnp.where(step >= first, side, side_now)
        first += tiles

    start, index, inside = 0, 0, 0
    for q in range(4):
        block = mm(turned[side_now, q], right[...], ((1,), (0,))).astype(bf16)
        taken = 0
        while taken < half:
            size = min(cuts[index] - inside, half - taken)
            outs[index][inside : inside + size, :] = block[taken : taken + size]
            taken += size
            inside += size
            if inside == cuts[index]:
                index, inside = index + 1, 0


def products(lefts, rights, cuts, name):
    seq = lax.axis_index("seq")
    core, x, y = seq % 2, (seq // 2) % 2, seq // 4
    place = jnp.stack([(1 - y) * 2 + 1 - x, y * 2 + 1 - x, (1 - y) * 2 + x, y * 2 + x, core]).astype(jnp.int32)
    tile = 640
    tok, model = lefts[0][0].shape
    sides = tuple((side, own.shape[1] // tile) for side, own, _ in rights)
    total = sum(tiles for _, tiles in sides)
    in_specs = [
        pl.BlockSpec((tok, model), lambda j, place: (0, 0), pipeline_mode=pl.Buffered(1))
    ] * (2 * len(lefts))
    first = 0
    for _, tiles in sides:

        def index(j, place, first=first, tiles=tiles):
            return (0, jnp.clip(j - first, 0, tiles - 1))

        in_specs += [pl.BlockSpec((tok, tile), index)] * 2
        first += tiles
    half = model // 8
    return pl.pallas_call(
        functools.partial(products_kernel, sides, tile, cuts),
        grid_spec=pltpu.PrefetchScalarGridSpec(
            num_scalar_prefetch=1,
            grid=(total,),
            in_specs=in_specs,
            out_specs=[pl.BlockSpec((rows, tile), lambda j, place: (0, j)) for rows in cuts],
            scratch_shapes=[
                pltpu.VMEM((len(lefts), 4, half, 2 * tok), bf16),
                pltpu.VMEM((2 * half, 2 * tok), bf16),
                pltpu.VMEM((2 * tok, tile), bf16),
            ],
        ),
        out_shape=[jax.ShapeDtypeStruct((rows, total * tile), bf16) for rows in cuts],
        compiler_params=pltpu.CompilerParams(vmem_limit_bytes=56 * 1024 * 1024),
        cost_estimate=pl.CostEstimate(
            flops=2 * 4 * half * 2 * tok * total * tile, bytes_accessed=4 * half * total * tile * 2, transcendentals=0
        ),
        name=name,
    )(place, *[a for pair in lefts for a in pair], *[a for _, own, other in rights for a in (own, other)])


def add_columns(target, sources, start, size, step):
    def one(turn, carry):
        cols = pl.ds(pl.multiple_of(start + turn * step, 128), step)
        total = target[:, cols].astype(f32)
        for source in sources:
            total = total + source[:, cols].astype(f32)
        target[:, cols] = total.astype(target.dtype)
        return carry

    lax.fori_loop(0, size // step, one, 0)


def scatter_kernel(
    main, rest, mlp, mixer_sum, mlp_back,
    held, cross, near, lined,
    load_sem, flow_send, flow_recv, line_send, line_recv, swap_send, swap_recv, own_sem,
):
    s, z, _, beside, across = places()
    chip_diag, chip_beside, chip_across, chip = 0, 1, 2, 3
    rows = held.shape[1] // 4
    cols = held.shape[2]
    cut = cols // 256 * 128
    ff_part = mlp.shape[1] // 3
    parts = (main, rest)
    order = (3 * (1 - z // 2), (2 + 3 * z) % 5, 1 + z % 2, z)

    def remote(src, dst, send, recv, target):
        return pltpu.make_async_remote_copy(
            src_ref=src, dst_ref=dst, send_sem=send, recv_sem=recv, device_id=target, device_id_type=MESH
        )

    def span(k):
        return pl.ds(pl.multiple_of(k * rows, 16), rows)

    def loads(i):
        copies, start = [], 0
        for n, part in enumerate(parts):
            size = part.shape[2]
            copies.append(
                pltpu.make_async_copy(
                    part.at[:, span(order[i]), :], held.at[:, span(order[i]), pl.ds(start, size)], load_sem.at[i, n]
                )
            )
            start += size
        return copies

    left, right = pl.ds(0, cut), pl.ds(cut, cols - cut)

    def block(q, i, side):
        return held.at[q, span(order[i]), side]

    def flow(i, index):
        send, recv = flow_send.at[i, index], flow_recv.at[i, index]
        to_beside, to_across = (beside, z), (across, z)
        if index == 0:
            return remote(block(chip_diag, i, left), cross.at[i, :, left], send, recv, to_across)
        if index == 1:
            return remote(block(chip_diag, i, right), cross.at[i, :, right], send, recv, to_beside)
        if index == 2:
            return remote(block(chip_beside, i, right), near.at[0, i, :, right], send, recv, to_beside)
        if index == 3:
            return remote(block(chip_beside, i, left), near.at[0, i, :, left], send, recv, to_beside)
        if index == 4:
            return remote(block(chip_across, i, left), near.at[1, i, :, left], send, recv, to_across)
        return remote(block(chip_across, i, right), near.at[1, i, :, right], send, recv, to_across)

    def cross_step(i):
        flow(i, 0).wait_recv()
        add_columns(held.at[chip_beside, span(order[i]), :], [cross.at[i]], 0, cut, 512)
        flow(i, 3).start()
        flow(i, 1).wait_recv()
        add_columns(held.at[chip_across, span(order[i]), :], [cross.at[i]], cut, cols - cut, 384)
        flow(i, 5).start()

    def near_step(i):
        for index in (2, 4, 3, 5):
            flow(i, index).wait_recv()
        add_columns(held.at[chip, span(order[i]), :], [near.at[0, i], near.at[1, i]], 0, cols, 640)

    def line(k, slot, target):
        return remote(
            held.at[chip, span(k), :], lined.at[slot], line_send.at[k], line_recv.at[slot], (s, target)
        )

    def absorb(k, slot, source):
        line(k, slot, source).wait_recv()
        add_columns(held.at[chip, span(k), :], [lined.at[slot]], 0, cols, 640)

    def chain(i):
        k = order[i]
        if i == 3:
            pl.when(z > 0)(lambda: absorb(k, k, z - 1))
            pl.when(z < 3)(lambda: absorb(k, 4, z + 1))
            return

        @pl.when(k > z)
        def _():
            pl.when(z > 0)(lambda: absorb(k, k, z - 1))
            line(k, k, z + 1).start()

        @pl.when(k < z)
        def _():
            pl.when(z < 3)(lambda: absorb(k, k, z + 1))
            pl.when(k == z - 1)(lambda: line(k, 4, z - 1).start())
            pl.when(k < z - 1)(lambda: line(k, k, z - 1).start())

    def chain_drain():
        for i in range(3):
            k = order[i]
            line(k, k, (z + 1) % 4).wait_send()

    def pieces():
        for m in range(3):
            yield m, mlp, pl.ds(m * ff_part, ff_part)

    def swap(k):
        to = (z + k) % 4
        here = pl.ds(pl.multiple_of(z * ff_part, 128), ff_part)
        return [
            remote(
                source.at[span(to), at], mlp_back.at[m, :, here], swap_send.at[k - 1, m], swap_recv.at[k - 1, m], (s, to)
            )
            for m, source, at in pieces()
        ]

    own = [
        pltpu.make_async_copy(
            source.at[span(z), at], mlp_back.at[m, :, pl.ds(pl.multiple_of(z * ff_part, 128), ff_part)], own_sem.at[m]
        )
        for m, source, at in pieces()
    ]
    for i in range(4):
        for copy in loads(i):
            copy.start()
    greet([(beside, z), (across, z)] + [(s, (z + k) % 4) for k in range(1, 4)])
    for k in (1, 3, 2):
        for copy in swap(k):
            copy.start()
    for copy in own:
        copy.start()
    for i in range(2):
        for copy in loads(i):
            copy.wait()
        flow(i, 0).start()
        flow(i, 1).start()
        if i == 0:
            flow(i, 2).start()
            flow(i, 4).start()
    for i in range(4):
        cross_step(i)
        if i + 1 < 4:
            flow(i + 1, 2).start()
            flow(i + 1, 4).start()
        if i + 2 < 4:
            for copy in loads(i + 2):
                copy.wait()
            flow(i + 2, 0).start()
            flow(i + 2, 1).start()
        if i > 0:
            near_step(i - 1)
            chain(i - 1)
    near_step(3)
    chain(3)
    done = pltpu.make_async_copy(held.at[chip, span(z), :], mixer_sum, own_sem.at[3])
    done.start()
    for i in range(4):
        for index in range(6):
            flow(i, index).wait_send()
    chain_drain()
    for k in range(1, 4):
        for copy in swap(k):
            copy.wait()
    for copy in own:
        copy.wait()
    done.wait()


def scatter(main, rest, mlp):
    rows = main.shape[1] // 4
    cols = main.shape[2] + rest.shape[2]
    ff_part = mlp.shape[1] // 3
    anyspec = pl.BlockSpec(memory_space=pl.ANY)
    dma = pltpu.SemaphoreType.DMA
    return pl.pallas_call(
        scatter_kernel,
        in_specs=[anyspec] * 3,
        out_specs=[anyspec] * 2,
        out_shape=[
            jax.ShapeDtypeStruct((rows, cols), bf16),
            jax.ShapeDtypeStruct((3, rows, 4 * ff_part), bf16),
        ],
        scratch_shapes=[
            pltpu.VMEM((4, 4 * rows, cols), bf16),
            pltpu.VMEM((4, rows, cols), bf16),
            pltpu.VMEM((2, 4, rows, cols), bf16),
            pltpu.VMEM((5, rows, cols), bf16),
            dma((4, 2)), dma((4, 6)), dma((4, 6)), dma((4,)), dma((5,)), dma((3, 3)), dma((3, 3)), dma((4,)),
        ],
        compiler_params=pltpu.CompilerParams(
            collective_id=2, has_side_effects=True, vmem_limit_bytes=52 * 1024 * 1024
        ),
        name="scatter_gradients",
    )(main, rest, mlp)


def gather_plain(mixer, gate, up, down):
    groups = lax.axis_size("fsdp")
    part_rows, ff = gate.shape
    own = jnp.stack([w.reshape(part_rows, groups, ff // groups) for w in (gate, up, down)], axis=2)
    mine = lax.all_to_all(jnp.transpose(own, (1, 0, 2, 3)), "fsdp", 0, 0, tiled=True)
    return lax.all_gather(mixer, both, axis=0, tiled=True), mine.reshape(groups * part_rows, -1)


def from_line(shard):
    count = lax.axis_size("fsdp")
    return [shard] + [
        lax.ppermute(shard, "fsdp", [(i, (i + k) % count) for i in range(count)]) for k in range(1, count)
    ]


def swap_cores(shard):
    count = lax.axis_size("seq")
    return lax.ppermute(shard, "seq", [(i, i + 1 - 2 * (i % 2)) for i in range(count)])


def swap_beside(shard):
    return lax.ppermute(shard, "seq", [(i, i ^ 2) for i in range(8)])


def swap_across(shard):
    return lax.ppermute(shard, "seq", [(i, i ^ 4) for i in range(8)])


def add_low(left, right):
    return (left.astype(f32) + right.astype(f32)).astype(bf16)


def scatter_paired(normed, grad_both, grad_mix, mixed, rest, mlp_parts):
    seq = lax.axis_index("seq")
    core, x, y = seq % 2, (seq // 2) % 2, seq // 4
    main = products(
        [(normed, swap_cores(normed)), (grad_mix, swap_cores(grad_mix))],
        [(0, grad_both, swap_cores(grad_both)), (1, mixed, swap_cores(mixed))],
        (lru_rows(normed),),
        "mixer_products",
    )[0]
    grouped = rest.reshape(4, 2, -1, rest.shape[1])
    own = lax.dynamic_index_in_dim(grouped, core, 1, False)
    other = swap_cores(lax.dynamic_index_in_dim(grouped, 1 - core, 1, False))
    rest = (own.astype(f32) + other.astype(f32)).astype(bf16)
    rest = jnp.concatenate(
        [
            lax.dynamic_slice_in_dim(rest, q, 1, 0)
            for q in ((1 - y) * 2 + 1 - x, y * 2 + 1 - x, (1 - y) * 2 + x, y * 2 + x)
        ],
        axis=0,
    )
    main, rest, mlp_parts = lax.optimization_barrier((main, rest, mlp_parts))
    mine, *sent = [part.astype(f32) for part in mlp_parts]
    mlp_sum = mine + jnp.concatenate([sent[0] + sent[2], sent[1] + sent[3]], axis=0)
    return scatter(main.reshape(4, -1, main.shape[1]), rest, mlp_sum.astype(bf16))


def lru_rows(values):
    return values.shape[1] // 2


def scatter_plain(normed, grad_both, grad_mix, mixed, rest, mlp_sum):
    groups = lax.axis_size("fsdp")
    term_wide = mm(normed, grad_both, ((0,), (0,))).astype(bf16)
    term_out = mm(grad_mix, mixed, ((0,), (0,))).astype(bf16)
    mixer_sum = lax.psum_scatter(
        jnp.concatenate([term_wide, term_out, rest], axis=1), "seq", scatter_dimension=0, tiled=True
    )
    mixer_sum = lax.psum_scatter(mixer_sum, "fsdp", scatter_dimension=0, tiled=True)
    ff_part = mlp_sum.shape[1] // 3
    part_rows = mlp_sum.shape[0] // groups
    mlp_sum = mlp_sum.reshape(groups, part_rows, 3, ff_part)
    mlp_back = lax.all_to_all(mlp_sum, "fsdp", 0, 0, tiled=True)
    mlp_back = jnp.transpose(mlp_back, (2, 1, 0, 3)).reshape(3, part_rows, groups * ff_part)
    return mixer_sum, mlp_back


def call_heads(kernel, width, heads, ins, outs, scratch, name):
    def spec(rows_cols):
        rows, by_row = rows_cols
        if by_row:
            return pl.BlockSpec((rows, width), lambda h: (h, 0))
        return pl.BlockSpec((rows, width), lambda h: (0, h))

    in_specs = [spec((width, True)) if rowwise else spec((a.shape[0], False)) for a, rowwise in ins]
    out_specs = [spec((width, True)) if rowwise else spec((rows, False)) for rows, _, rowwise in outs]
    out_shape = [
        jax.ShapeDtypeStruct((heads * width, width) if rowwise else (rows, heads * width), kind)
        for rows, kind, rowwise in outs
    ]
    return pl.pallas_call(
        kernel,
        grid=(heads,),
        in_specs=in_specs,
        out_specs=out_specs,
        out_shape=out_shape,
        scratch_shapes=[pltpu.VMEM((rows, width), f32) for rows in scratch],
        compiler_params=pltpu.CompilerParams(vmem_limit_bytes=40 * 1024 * 1024),
        name=name,
    )(*[a for a, _ in ins])


def on_device(
    block_input,
    cotangent,
    mixer_gain,
    branch_proj,
    gelu_proj,
    conv_taps,
    conv_bias,
    rate_blocks,
    input_blocks,
    rate_bias,
    input_bias,
    decay_param,
    out_proj,
    mlp_gain,
    gate_proj,
    up_proj,
    down_proj,
):
    groups = lax.axis_size("fsdp")
    part_rows, lru = branch_proj.shape
    width = rate_blocks.shape[1]
    heads = lru // width
    margin = conv_taps.shape[0] - 1
    tokens = block_input[0].astype(f32)
    tok_count, model = tokens.shape
    ff = gate_proj.shape[1]
    ff_part = ff // groups
    grad_out = cotangent[0]

    smalls = jnp.stack(
        [conv_taps[k] for k in range(margin + 1)]
        + [conv_bias, rate_bias, input_bias, decay_param, mixer_gain, mlp_gain],
        axis=1,
    )
    small_count = smalls.shape[1]
    smalls = jnp.pad(smalls, ((0, 0), (0, 128 - small_count)))
    mixer_own = jnp.concatenate(
        [smalls, rate_blocks, input_blocks, branch_proj, gelu_proj, out_proj], axis=1
    )
    custom = lax.axis_size("seq") == 8 and groups == 4
    if custom:
        mixer_w, mlp_mine = gather(mixer_own, gate_proj, up_proj, down_proj)
    else:
        mixer_w, mlp_mine = gather_plain(mixer_own, gate_proj, up_proj, down_proj)
    mlp_w = lax.all_gather(mlp_mine, "seq", axis=0, tiled=True)
    grad_out_late = lax.optimization_barrier((grad_out, mlp_mine))[0]
    if custom:
        grad_pieces = from_line(grad_out_late)
    first = lax.optimization_barrier(mixer_w[:, : 128 + 2 * width])
    wide = mixer_w[:, 128 + 2 * width : 128 + 2 * width + 2 * lru]
    proj_out = mixer_w[:, 128 + 2 * width + 2 * lru :]

    table = first[:, :small_count].astype(f32).T
    blocks_rate = first[:, 128 : 128 + width]
    blocks_input = first[:, 128 + width :]
    param_decay = table[margin + 4]
    gain_one = table[margin + 5]
    gain_two = table[margin + 6]
    small = jnp.concatenate(
        [
            table[: margin + 4],
            jax.nn.softplus(-param_decay)[None],
            -jax.nn.sigmoid(-param_decay)[None],
            jnp.zeros((16 - margin - 6, lru), f32),
        ],
        axis=0,
    )

    normed = norm_rows(tokens, gain_one).astype(bf16)
    both_pre = mm(normed, wide, ((1,), (0,)))
    branch = both_pre[:, :lru].astype(bf16)
    gelu_pre = both_pre[:, lru:]
    prior = from_behind(branch[tok_count - margin :], "seq", 1).astype(f32)
    prior = jnp.concatenate([jnp.zeros((8 - margin, lru), f32), prior], axis=0)
    conv, rate_pre, input_pre, cum, local = call_heads(
        mixer_forward,
        width,
        heads,
        [(branch, False), (prior, False), (small, False), (blocks_rate, True), (blocks_input, True)],
        [(tok_count, bf16, False)] + [(tok_count, f32, False)] * 4,
        [tok_count + 8],
        "mixer_forward",
    )
    carried = prefix((cum[-1], local[-1]), "seq", False)
    states = local + cum * carried[None]
    mixed = (states * jax.nn.gelu(gelu_pre, approximate=True)).astype(bf16)
    middle = tokens + mm(mixed, proj_out, ((1,), (1,)))
    normed_two = norm_rows(middle, gain_two).astype(bf16)

    if custom:
        normed_all, normed_other, grad_out_all, grad_out_other = gather_rows(normed_two, grad_pieces)
    else:
        normed_all = lax.all_gather(normed_two, "fsdp", axis=0, tiled=True)
        grad_out_all = lax.all_gather(grad_out_late, "fsdp", axis=0, tiled=True)
    w_gate, w_up, w_down = mlp_w[:, :ff_part], mlp_w[:, ff_part : 2 * ff_part], mlp_w[:, 2 * ff_part :]
    gate = mm(normed_all, w_gate, ((1,), (0,)))
    up_val = mm(normed_all, w_up, ((1,), (0,)))
    gelu_gate, gelu_slope = gelu_parts(gate)
    hidden = (gelu_gate * up_val).astype(bf16)
    grad_hidden = mm(grad_out_all, w_down, ((1,), (0,)))
    grad_gate = (grad_hidden * up_val * gelu_slope).astype(bf16)
    grad_up = (grad_hidden * gelu_gate).astype(bf16)
    grad_normed_part = mm(grad_gate, w_gate, ((1,), (1,))) + mm(grad_up, w_up, ((1,), (1,)))
    grad_normed_two = lax.psum_scatter(
        grad_normed_part.astype(bf16), "fsdp", scatter_dimension=0, tiled=True
    )
    out_part = mm(hidden, w_down, ((1,), (1,))).astype(bf16)
    if custom:
        half = model // 16
        blocks = products(
            [(normed_all, normed_other), (grad_out_all, grad_out_other)],
            [
                (0, grad_gate, swap_cores(grad_gate)),
                (0, grad_up, swap_cores(grad_up)),
                (1, hidden, swap_cores(hidden)),
            ],
            (half,) * 6 + (2 * half,),
            "feed_forward_products",
        )
        mine, grad_normed_two = lax.optimization_barrier((blocks[6], grad_normed_two))
        diag_low, diag_high, beside_low, beside_high, across_low, across_high = blocks[:6]
        by_across = swap_across(diag_low)
        by_beside = swap_beside(diag_high)
    else:
        grad_pair = jnp.concatenate([grad_gate, grad_up], axis=1)
        term_pair = mm(normed_all, grad_pair, ((0,), (0,))).astype(bf16)
        term_down = mm(grad_out_all, hidden, ((0,), (0,))).astype(bf16)
        pair_sum = lax.psum_scatter(term_pair, "seq", scatter_dimension=0, tiled=True)
        down_sum = lax.psum_scatter(term_down, "seq", scatter_dimension=0, tiled=True)
        mlp_sum = jnp.concatenate([pair_sum, down_sum], axis=1)
    out_sum = lax.psum_scatter(out_part, "fsdp", scatter_dimension=0, tiled=True)
    block_output = (middle + out_sum.astype(f32)).astype(bf16)[None]
    grad_normed_two = grad_normed_two.astype(f32)

    second_pull = jax.vjp(norm_rows, middle, gain_two)[1]
    grad_mid_part, grad_gain_two = second_pull(grad_normed_two)
    grad_middle = grad_out.astype(f32) + grad_mid_part
    grad_mix = grad_middle.astype(bf16)
    grad_mixed = mm(grad_mix, proj_out, ((1,), (0,)))
    if custom:
        beside_high, across_low, grad_mixed = lax.optimization_barrier((beside_high, across_low, grad_mixed))
        from_beside_high = swap_beside(beside_high)
        from_across_low = swap_across(across_low)
    carried_rows = jnp.broadcast_to(carried[None], (8, lru))
    grad_gelu_pre, rev_cum, rev_grad, pair_grad = call_heads(
        mixer_backward_scan,
        width,
        heads,
        [(a, False) for a in (grad_mixed, gelu_pre, rate_pre, cum, local, carried_rows, small)],
        [(tok_count, bf16, False), (tok_count, f32, False), (tok_count, f32, False), (8, f32, False)],
        [tok_count + 8],
        "mixer_backward_scan",
    )
    incoming = prefix((cum[-1], pair_grad[0]), "seq", True)
    incoming_rows = jnp.broadcast_to(incoming[None], (8, lru))
    own, head, rate_w_grad, input_w_grad, sums = call_heads(
        mixer_backward,
        width,
        heads,
        [
            (a, False)
            for a in (rev_cum, rev_grad, incoming_rows, cum, local, carried_rows, rate_pre, input_pre, conv, branch, prior, small)
        ]
        + [(blocks_rate, True), (blocks_input, True)],
        [(tok_count, f32, False), (8, f32, False), (0, bf16, True), (0, bf16, True), (8, f32, False)],
        [tok_count + 8, tok_count + 16],
        "mixer_backward",
    )
    if custom:
        by_across, by_beside, own = lax.optimization_barrier((by_across, by_beside, own))
        beside_low, across_high = add_low(beside_low, by_across), add_low(across_high, by_beside)
        beside_low, across_high, own = lax.optimization_barrier((beside_low, across_high, own))
        from_beside_low = swap_beside(beside_low)
        from_across_high = swap_across(across_high)
        mlp_parts = (mine, from_across_low, from_across_high, from_beside_low, from_beside_high)
    received = from_behind(head[8 - margin :], "seq", -1)
    grad_branch = jnp.concatenate(
        [own[: tok_count - margin], own[tok_count - margin :] + received], axis=0
    ).astype(bf16)
    grad_both = jnp.concatenate([grad_branch, grad_gelu_pre], axis=1)
    grad_normed = mm(grad_both, wide, ((1,), (1,)))
    first_pull = jax.vjp(norm_rows, tokens, gain_one)[1]
    grad_tok_part, grad_gain_one = first_pull(grad_normed)
    input_grad = (grad_middle + grad_tok_part).astype(bf16)[None]
    vectors = jnp.concatenate([sums, grad_gain_one[None], grad_gain_two[None]], axis=0).T
    vectors = jnp.pad(vectors, ((0, 0), (0, 128 - vectors.shape[1]))).astype(bf16)
    rest = jnp.concatenate([rate_w_grad, input_w_grad, vectors], axis=1)
    if custom:
        mixer_sum, mlp_back = scatter_paired(normed, grad_both, grad_mix, mixed, rest, mlp_parts)
    else:
        mixer_sum, mlp_back = scatter_plain(normed, grad_both, grad_mix, mixed, rest, mlp_sum)
    mlp_grads = [mlp_back[m].astype(f32) for m in range(3)]
    mixer_sum = mixer_sum.astype(f32)
    edges = [lru, 2 * lru, 3 * lru, 3 * lru + width, 3 * lru + 2 * width]
    dbranch, dgelu, dout, drate, dinput, vec = jnp.split(mixer_sum, edges, axis=1)
    vec = vec.T
    return (
        block_output,
        input_grad,
        vec[8],
        dbranch,
        dgelu,
        vec[: margin + 1],
        vec[7],
        drate,
        dinput,
        vec[4],
        vec[5],
        vec[6],
        dout,
        vec[9],
        mlp_grads[0],
        mlp_grads[1],
        mlp_grads[2],
    )


def solution(mesh):
    tokens = P("fsdp", "seq", None)
    vector = P(both)
    matrix = P(both, None)
    taps = P(None, both)
    return jax.shard_map(
        on_device,
        mesh=mesh,
        in_specs=(
            tokens, tokens, vector, matrix, matrix, taps, vector, matrix, matrix,
            vector, vector, vector, matrix, vector, matrix, matrix, matrix,
        ),
        out_specs=(
            tokens, tokens, vector, matrix, matrix, taps, vector, matrix, matrix,
            vector, vector, vector, matrix, vector, matrix, matrix, matrix,
        ),
        check_vma=False,
    )
```

```python
import functools

import jax
import jax.numpy as jnp
from jax import lax
from jax.experimental import pallas as pl
from jax.experimental.pallas import tpu as pltpu
from jax.sharding import PartitionSpec as P

epsilon = 1e-06
f32 = jnp.float32
bf16 = jnp.bfloat16
both = ("seq", "fsdp")
MESH = pl.DeviceIdType.MESH
TAP, CONV_BIAS, RATE_BIAS, INPUT_BIAS, SOFT, SOFT_SLOPE = 0, 4, 5, 6, 7, 8
GELU_C = 0.7978845608028654
GELU_A = 0.044715


def from_behind(shard, axis, by):
    devices = lax.axis_size(axis)
    pairs = [(i, i + by) for i in range(devices) if 0 <= i + by < devices]
    return lax.ppermute(shard, axis, pairs)


def prefix(part, axis, reverse):
    count = lax.axis_size(axis)
    place = lax.axis_index(axis)
    gathered = lax.all_gather(jnp.stack(part), axis)
    state = jnp.zeros_like(part[1])
    for hop in range(count):
        source = count - 1 - hop if reverse else hop
        ahead = source > place if reverse else source < place
        state = jnp.where(ahead, gathered[source, 1] + gathered[source, 0] * state, state)
    return state


def norm_rows(values, scales):
    return values * lax.rsqrt(jnp.mean(values * values, axis=-1, keepdims=True) + epsilon) * scales


def gelu_parts(x):
    inner = jnp.tanh(GELU_C * (x + GELU_A * x * x * x))
    return 0.5 * x * (1.0 + inner), 0.5 * (1.0 + inner) + 0.5 * x * (1.0 - inner * inner) * (
        GELU_C * (1.0 + 3.0 * GELU_A * x * x)
    )


def mm(left, right, dims):
    return lax.dot_general(left, right, (dims, ((), ())), preferred_element_type=f32)


def sigmoid(x):
    return 1.0 / (1.0 + jnp.exp(-x))


def scan_rows(decay, value, reverse):
    rows = decay.shape[0]
    place = lax.broadcasted_iota(jnp.int32, decay.shape, 0)
    step = 1
    while step < rows:
        shift = rows - step if reverse else step
        inside = place < rows - step if reverse else place >= step
        before_value = jnp.where(inside, pltpu.roll(value, shift, 0), 0.0)
        before_decay = jnp.where(inside, pltpu.roll(decay, shift, 0), 1.0)
        value = value + decay * before_value
        decay = decay * before_decay
        step *= 2
    return decay, value


def gates(rate_pre, input_pre, soft):
    rate = sigmoid(rate_pre)
    log_decay = -8.0 * rate * soft
    decay = jnp.exp(log_decay)
    square = decay * decay
    root = jnp.sqrt(-jnp.tanh(log_decay) * (1.0 + square))
    return rate, decay, square, root, sigmoid(input_pre)


def mixer_forward(branch, prior, small, rate_w, input_w, conv, rate_pre, input_pre, cum, local, ext):
    rows = branch.shape[0]
    ext[0:8, :] = prior[...]
    ext[8:, :] = branch[...].astype(f32)
    total = small[CONV_BIAS : CONV_BIAS + 1, :] + small[TAP : TAP + 1, :] * ext[8:, :]
    for offset in range(1, 4):
        total = total + small[TAP + offset : TAP + offset + 1, :] * ext[pl.ds(8 - offset, rows), :]
    low = total.astype(bf16)
    conv[...] = low
    rate = mm(low, rate_w[...], ((1,), (0,))) + small[RATE_BIAS : RATE_BIAS + 1, :]
    inp = mm(low, input_w[...], ((1,), (0,))) + small[INPUT_BIAS : INPUT_BIAS + 1, :]
    rate_pre[...] = rate
    input_pre[...] = inp
    _, decay, _, root, opened = gates(rate, inp, small[SOFT : SOFT + 1, :])
    product, states = scan_rows(decay, root * opened * low.astype(f32), False)
    cum[...] = product
    local[...] = states


def mixer_backward_scan(grad_mixed, gelu_pre, rate_pre, cum, local, carried, small, grad_pre, rev_cum, rev_grad, pair, ext):
    rows = grad_mixed.shape[0]
    states = local[...] + cum[...] * carried[0:1, :]
    value, slope = gelu_parts(gelu_pre[...])
    grad = grad_mixed[...]
    grad_pre[...] = (grad * states * slope).astype(bf16)
    decay = jnp.exp(-8.0 * sigmoid(rate_pre[...]) * small[SOFT : SOFT + 1, :])
    ext[0:rows, :] = decay
    ext[rows:, :] = jnp.ones((8, decay.shape[1]), f32)
    product, back = scan_rows(ext[pl.ds(1, rows), :], grad * value, True)
    rev_cum[...] = product
    rev_grad[...] = back
    pair[...] = jnp.broadcast_to(decay[0:1, :] * back[0:1, :], pair.shape)


def mixer_backward(
    rev_cum, rev_grad, incoming, cum, local, carried, rate_pre, input_pre, conv, branch, prior, small, rate_w, input_w,
    own, head, rate_w_grad, input_w_grad, sums, ext, gext,
):
    rows = rev_cum.shape[0]
    soft = small[SOFT : SOFT + 1, :]
    grad_states = rev_grad[...] + rev_cum[...] * incoming[0:1, :]
    rate, decay, square, root, opened = gates(rate_pre[...], input_pre[...], soft)
    ext[0:8, :] = jnp.broadcast_to(carried[0:1, :], (8, carried.shape[1]))
    ext[8:, :] = local[...] + cum[...] * carried[0:1, :]
    before = ext[pl.ds(7, rows), :]
    low = conv[...]
    conv_in = low.astype(f32)
    grad_log = grad_states * decay * before - grad_states * opened * conv_in * square / root
    driven = grad_states * root
    grad_input = (driven * conv_in * opened * (1.0 - opened)).astype(bf16)
    by_rate = grad_log * (-8.0 * rate)
    grad_rate = (by_rate * soft * (1.0 - rate)).astype(bf16)
    sums[6:7, :] = jnp.sum(by_rate, axis=0, keepdims=True) * small[SOFT_SLOPE : SOFT_SLOPE + 1, :]
    sums[4:5, :] = jnp.sum(grad_rate.astype(f32), axis=0, keepdims=True)
    sums[5:6, :] = jnp.sum(grad_input.astype(f32), axis=0, keepdims=True)
    rate_w_grad[...] = mm(low, grad_rate, ((0,), (0,))).astype(rate_w_grad.dtype)
    input_w_grad[...] = mm(low, grad_input, ((0,), (0,))).astype(input_w_grad.dtype)
    grad_conv = (
        driven * opened
        + mm(grad_rate, rate_w[...], ((1,), (1,)))
        + mm(grad_input, input_w[...], ((1,), (1,)))
    )
    sums[7:8, :] = jnp.sum(grad_conv, axis=0, keepdims=True)
    ext[0:8, :] = prior[...]
    ext[8:, :] = branch[...].astype(f32)
    gext[0:8, :] = jnp.zeros((8, grad_conv.shape[1]), f32)
    gext[8 : 8 + rows, :] = grad_conv
    gext[8 + rows :, :] = jnp.zeros((8, grad_conv.shape[1]), f32)
    back = jnp.zeros_like(grad_conv)
    front = jnp.zeros((8, grad_conv.shape[1]), f32)
    for offset in range(4):
        tap = small[TAP + offset : TAP + offset + 1, :]
        sums[offset : offset + 1, :] = jnp.sum(
            grad_conv * ext[pl.ds(8 - offset, rows), :], axis=0, keepdims=True
        )
        back = back + tap * gext[pl.ds(8 + offset, rows), :]
        front = front + tap * gext[pl.ds(offset, 8), :]
    own[...] = back
    head[...] = front


def places():
    s = lax.axis_index("seq")
    z = lax.axis_index("fsdp")
    core = s + 1 - 2 * (s % 2)
    beside = s + 2 - 4 * ((s // 2) % 2)
    across = s + 4 - 8 * (s // 4)
    return s, z, core, beside, across


def greet(peers):
    barrier = pltpu.get_barrier_semaphore()
    for peer in peers:
        pl.semaphore_signal(barrier, inc=1, device_id=peer, device_id_type=MESH)
    pl.semaphore_wait(barrier, len(peers))


def gather_kernel(
    mixer, gate, up, down, mixer_all, mlp_mine,
    flow_send, flow_recv, line_send, line_recv, swap_send, swap_recv, own_sem,
):
    s, z, core, beside, across = places()
    rows, cols = mixer.shape
    ff_part = mlp_mine.shape[1] // 3
    cut = cols // 256 * 128
    diag = beside + across - s
    greet([(core, z), (beside, z), (across, z)] + [(s, (z + k) % 4) for k in range(1, 4)])

    def remote(src, dst, send, recv, target):
        return pltpu.make_async_remote_copy(
            src_ref=src, dst_ref=dst, send_sem=send, recv_sem=recv, device_id=target, device_id_type=MESH
        )

    def piece(seq, zz, half=None):
        span = pl.ds(pl.multiple_of((seq * 4 + zz) * rows, 16), rows)
        if half is None:
            return mixer_all.at[span, :]
        return mixer_all.at[span, pl.ds(0, cut) if half == 0 else pl.ds(cut, cols - cut)]

    def flow(zz, index, seq, half, target, src=None):
        ref = piece(seq, zz, half)
        return remote(
            ref if src is None else src, ref, flow_send.at[zz, index], flow_recv.at[zz, index], (target, z)
        )

    def sends(zz, src=None):
        return [
            flow(zz, 0, s, None, beside, src),
            flow(zz, 1, s, None, across, src),
            flow(zz, 4, s, None, core, src),
        ]

    def spread(zz, src=None):
        for copy in sends(zz, src):
            copy.start()

    def relay(zz):
        flow(zz, 0, beside, None, beside).wait_recv()
        flow(zz, 3, beside, 0, across).start()
        flow(zz, 5, beside, None, core).start()
        flow(zz, 1, across, None, across).wait_recv()
        flow(zz, 2, across, 1, beside).start()
        flow(zz, 6, across, None, core).start()

    def finish(zz):
        flow(zz, 3, diag, 0, across).wait_recv()
        flow(zz, 7, diag, 0, core).start()
        flow(zz, 2, diag, 1, beside).wait_recv()
        flow(zz, 8, diag, 1, core).start()

    def drain(zz, src=None):
        for copy in sends(zz, src):
            copy.wait_send()
        flow(zz, 3, beside, 0, across).wait_send()
        flow(zz, 5, beside, None, core).wait_send()
        flow(zz, 2, across, 1, beside).wait_send()
        flow(zz, 6, across, None, core).wait_send()
        flow(zz, 7, diag, 0, core).wait_send()
        flow(zz, 8, diag, 1, core).wait_send()
        flip = core - s
        flow(zz, 4, core, None, core).wait_recv()
        flow(zz, 5, beside + flip, None, core).wait_recv()
        flow(zz, 6, across + flip, None, core).wait_recv()
        flow(zz, 7, diag + flip, 0, core).wait_recv()
        flow(zz, 8, diag + flip, 1, core).wait_recv()

    def line(zz, up_way, hop, src=None):
        ref = piece(s, zz)
        way = 0 if up_way else 1
        target = z + 1 if up_way else z - 1
        return remote(
            ref if src is None else src, ref, line_send.at[way, hop], line_recv.at[way, hop], (s, target)
        )

    def line_hop(hop):
        def below():
            line(z - hop, True, hop - 1).wait_recv()
            pl.when(z < 3)(lambda: line(z - hop, True, hop).start())

        def above():
            line(z + hop, False, hop - 1).wait_recv()
            pl.when(z > 0)(lambda: line(z + hop, False, hop).start())

        pl.when(z >= hop)(below)
        pl.when(z + hop <= 3)(above)

    def at_hop(hop, act):
        pl.when(z >= hop)(lambda: act(z - hop))
        pl.when(z + hop <= 3)(lambda: act(z + hop))

    def landing(m, zz):
        return mlp_mine.at[pl.ds(pl.multiple_of(zz * rows, 16), rows), pl.ds(m * ff_part, ff_part)]

    def columns(m, zz):
        return (gate, up, down)[m].at[:, pl.ds(pl.multiple_of(zz * ff_part, 128), ff_part)]

    def swap(k, m, arriving=False):
        to = (z + k) % 4
        came = (z + 4 - k) % 4
        return remote(
            columns(m, to), landing(m, came if arriving else z), swap_send.at[k - 1, m], swap_recv.at[k - 1, m], (s, to)
        )

    local = [pltpu.make_async_copy(columns(m, z), landing(m, z), own_sem.at[m]) for m in range(3)]
    local.append(pltpu.make_async_copy(mixer, piece(s, z), own_sem.at[3]))

    pl.when(z < 3)(lambda: line(z, True, 0, mixer).start())
    pl.when(z > 0)(lambda: line(z, False, 0, mixer).start())
    spread(z, mixer)
    for copy in local:
        copy.start()
    line_hop(1)
    at_hop(1, spread)
    relay(z)
    line_hop(2)
    at_hop(2, spread)
    finish(z)
    at_hop(1, relay)
    line_hop(3)
    at_hop(3, spread)
    for k in (1, 3, 2):
        for m in range(3):
            swap(k, m).start()
    at_hop(1, finish)
    at_hop(2, relay)
    at_hop(3, relay)
    at_hop(2, finish)
    at_hop(3, finish)
    drain(z, mixer)
    for hop in range(1, 4):
        at_hop(hop, drain)
    for copy in local:
        copy.wait()
    for k in (1, 3, 2):
        for m in range(3):
            swap(k, m).wait_send()
            swap(k, m, True).wait_recv()
    pl.when(z < 3)(lambda: line(z, True, 0, mixer).wait_send())
    pl.when(z > 0)(lambda: line(z, False, 0, mixer).wait_send())
    for hop in range(1, 3):
        pl.when((z >= hop) & (z < 3))(lambda: line(z - hop, True, hop).wait_send())
        pl.when((z + hop <= 3) & (z > 0))(lambda: line(z + hop, False, hop).wait_send())


def gather(mixer, gate, up, down):
    rows, cols = mixer.shape
    ff_part = gate.shape[1] // 4
    anyspec = pl.BlockSpec(memory_space=pl.ANY)
    dma = pltpu.SemaphoreType.DMA
    return pl.pallas_call(
        gather_kernel,
        in_specs=[anyspec] * 4,
        out_specs=[anyspec] * 2,
        out_shape=[
            jax.ShapeDtypeStruct((32 * rows, cols), bf16),
            jax.ShapeDtypeStruct((4 * rows, 3 * ff_part), bf16),
        ],
        scratch_shapes=[
            dma((4, 9)), dma((4, 9)), dma((2, 3)), dma((2, 3)), dma((3, 3)), dma((3, 3)), dma((4,)),
        ],
        compiler_params=pltpu.CompilerParams(collective_id=1, has_side_effects=True),
        name="gather_weights",
    )(mixer, gate, up, down)


def rows_kernel(
    normed, grad0, grad1, grad2, grad3, normed_all, normed_other, grad_all, grad_other,
    line_send, line_recv, core_send, core_recv, own_sem, held,
):
    s, z, core, _, _ = places()
    tok = normed.shape[0]
    cuts = 4
    grads = (grad0, grad1, grad2, grad3)
    greet([(core, z)] + [(s, (z + k) % 4) for k in range(1, 4)])

    def rows(ref, zz):
        return ref.at[pl.ds(pl.multiple_of(zz * tok, 16), tok), :]

    def remote(src, dst, send, recv, target):
        return pltpu.make_async_remote_copy(
            src_ref=src, dst_ref=dst, send_sem=send, recv_sem=recv, device_id=target, device_id_type=MESH
        )

    def parts(ref):
        size = tok // cuts
        return [ref.at[pl.ds(n * size, size), :] for n in range(cuts)]

    def line(zz, up_way, hop):
        way = 0 if up_way else 1
        target = z + 1 if up_way else z - 1
        src = normed if hop == 0 else rows(normed_all, zz)
        dst = rows(normed_all, zz)
        return [
            remote(a, b, line_send.at[way, hop, n], line_recv.at[way, hop, n], (s, target))
            for n, (a, b) in enumerate(zip(parts(src), parts(dst)))
        ]

    def over(zz, own=False):
        src = normed if own else rows(normed_all, zz)
        return remote(src, rows(normed_other, zz), core_send.at[0, zz], core_recv.at[0, zz], (core, z))

    def grad_over(k):
        zz = (z + 4 - k) % 4
        return remote(grads[k], rows(grad_other, zz), core_send.at[1, zz], core_recv.at[1, zz], (core, z))

    def line_start(zz, up_way, hop):
        for copy in line(zz, up_way, hop):
            copy.start()

    def line_drain(zz, up_way, hop):
        for copy in line(zz, up_way, hop):
            copy.wait_send()

    def hop_step(hop):
        def below():
            for came, on in zip(line(z - hop, True, hop - 1), line(z - hop, True, hop) if hop < 3 else [None] * cuts):
                came.wait_recv()
                if on is not None:
                    pl.when(z < 3)(on.start)
            over(z - hop).start()

        def above():
            for came, on in zip(line(z + hop, False, hop - 1), line(z + hop, False, hop) if hop < 3 else [None] * cuts):
                came.wait_recv()
                if on is not None:
                    pl.when(z > 0)(on.start)
            over(z + hop).start()

        pl.when(z >= hop)(below)
        pl.when(z + hop <= 3)(above)

    local = [pltpu.make_async_copy(grads[k], held.at[k], own_sem.at[k]) for k in range(4)]
    local.append(pltpu.make_async_copy(normed, held.at[4], own_sem.at[4]))
    stored = [
        pltpu.make_async_copy(held.at[k], rows(grad_all, (z + 4 - k) % 4), own_sem.at[k]) for k in range(4)
    ]
    stored.append(pltpu.make_async_copy(held.at[4], rows(normed_all, z), own_sem.at[4]))
    pl.when(z < 3)(lambda: line_start(z, True, 0))
    pl.when(z > 0)(lambda: line_start(z, False, 0))
    over(z, True).start()
    for copy in local:
        copy.start()
    for k in range(4):
        grad_over(k).start()
    for copy, store in zip(local, stored):
        copy.wait()
        store.start()
    for hop in range(1, 4):
        hop_step(hop)
    for copy in stored:
        copy.wait()
    for k in range(4):
        grad_over(k).wait()
    over(z, True).wait()
    for k in range(1, 4):
        over((z + k) % 4).wait()
    pl.when(z < 3)(lambda: line_drain(z, True, 0))
    pl.when(z > 0)(lambda: line_drain(z, False, 0))
    for hop in range(1, 3):
        pl.when((z >= hop) & (z < 3))(lambda: line_drain(z - hop, True, hop))
        pl.when((z + hop <= 3) & (z > 0))(lambda: line_drain(z + hop, False, hop))


def gather_rows(normed, grads):
    tok, model = normed.shape
    anyspec = pl.BlockSpec(memory_space=pl.ANY)
    dma = pltpu.SemaphoreType.DMA
    return pl.pallas_call(
        rows_kernel,
        in_specs=[anyspec] * 5,
        out_specs=[anyspec] * 4,
        out_shape=[jax.ShapeDtypeStruct((4 * tok, model), bf16)] * 4,
        scratch_shapes=[dma((2, 3, 4)), dma((2, 3, 4)), dma((2, 4)), dma((2, 4)), dma((5,)), pltpu.VMEM((5, tok, model), bf16)],
        compiler_params=pltpu.CompilerParams(collective_id=3, has_side_effects=True),
        name="gather_rows",
    )(normed, *grads)


def column_tiles(cols, size=512):
    return [(start, min(size, cols - start)) for start in range(0, cols, size)]


def feed_forward_kernel(
    normed, grad_out, weights, hidden, hidden_other, pair, pair_other, back,
    held, hidden_now, pair_now, sems, store_sem, core_send, core_recv,
):
    s, z, core, _, _ = places()
    step = pl.program_id(0)
    ff_part = held.shape[2]
    model = held.shape[1]
    rows = normed.shape[0]
    tiles = column_tiles(ff_part)
    made = ((hidden_now, hidden, hidden_other), (pair_now, pair, pair_other))

    def load(n, m):
        start, size = tiles[n]
        return pltpu.make_async_copy(
            weights.at[:, pl.ds(m * ff_part + start, size)], held.at[m, :, pl.ds(start, size)], sems.at[n, m]
        )

    def kept(n, turn):
        now, mine, _ = made[n]
        return pltpu.make_async_copy(now.at[turn], mine.at[pl.ds(turn * rows, rows), :], store_sem.at[turn, n])

    def handed(n, turn):
        now, _, other = made[n]
        return pltpu.make_async_remote_copy(
            src_ref=now.at[turn],
            dst_ref=other.at[pl.ds(turn * rows, rows), :],
            send_sem=core_send.at[turn, n],
            recv_sem=core_recv.at[turn, n],
            device_id=(core, z),
            device_id_type=MESH,
        )

    @pl.when(step == 0)
    def _():
        for n in range(len(tiles)):
            for m in range(3):
                load(n, m).start()
        greet([(core, z)])

    for n, (start, size) in enumerate(tiles):
        cols = slice(start, start + size)

        @pl.when(step == 0)
        def _(n=n):
            for m in range(3):
                load(n, m).wait()

        gate = mm(normed[...], held[0, :, cols], ((1,), (0,)))
        value, slope = gelu_parts(gate)
        up = mm(normed[...], held[1, :, cols], ((1,), (0,)))
        hidden_now[step, :, cols] = (value * up).astype(bf16)
        grad_hidden = mm(grad_out[...], held[2, :, cols], ((1,), (0,)))
        pair_now[step, :, cols] = (grad_hidden * up * slope).astype(bf16)
        pair_now[step, :, slice(ff_part + start, ff_part + start + size)] = (grad_hidden * value).astype(bf16)

    for turn in range(2):

        @pl.when(step == turn)
        def _(turn=turn):
            for n in range(2):
                handed(n, turn).start()
                kept(n, turn).start()

    def back_tile(turn, carry):
        cols = pl.ds(pl.multiple_of(turn * 512, 512), 512)
        total = mm(pair_now[step, :, :ff_part], held[0, cols, :], ((1,), (1,)))
        total = total + mm(pair_now[step, :, ff_part:], held[1, cols, :], ((1,), (1,)))
        back[:, cols] = total.astype(bf16)
        return carry

    lax.fori_loop(0, model // 512, back_tile, 0)

    @pl.when(step == 1)
    def _():
        for turn in range(2):
            for n in range(2):
                kept(n, turn).wait()
                handed(n, turn).wait()


def feed_forward(normed, grad_out, weights):
    tok, model = normed.shape
    ff_part = weights.shape[1] // 3
    rows = tok // 2
    anyspec = pl.BlockSpec(memory_space=pl.ANY)
    dma = pltpu.SemaphoreType.DMA
    block = pl.BlockSpec((rows, model), lambda i: (i, 0))
    return pl.pallas_call(
        feed_forward_kernel,
        grid=(2,),
        in_specs=[block, block, anyspec],
        out_specs=[anyspec] * 4 + [block],
        out_shape=[
            jax.ShapeDtypeStruct((tok, cols), bf16)
            for cols in (ff_part, ff_part, 2 * ff_part, 2 * ff_part, model)
        ],
        scratch_shapes=[
            pltpu.VMEM((3, model, ff_part), bf16),
            pltpu.VMEM((2, rows, ff_part), bf16),
            pltpu.VMEM((2, rows, 2 * ff_part), bf16),
            dma((len(column_tiles(ff_part)), 3)), dma((2, 2)), dma((2, 2)), dma((2, 2)),
        ],
        compiler_params=pltpu.CompilerParams(
            collective_id=4, has_side_effects=True, vmem_limit_bytes=60 * 1024 * 1024
        ),
        name="feed_forward",
    )(normed, grad_out, weights)


def products_kernel(sides, cuts, spots, place, *refs):
    lefts = 1 + max(side for side, _ in sides)
    left_refs = refs[: 2 * lefts]
    right_refs = refs[2 * lefts : 2 * lefts + 2 * len(sides)]
    outs = refs[2 * lefts + 2 * len(sides) : -4]
    turned, slots, stage, sems = refs[-4:]
    tok = left_refs[0].shape[0]
    chip_cols = left_refs[0].shape[1] // 4
    half = chip_cols // 2
    step = pl.program_id(0)

    def load(side, q, who):
        cols = pl.ds(pl.multiple_of(place[q] * chip_cols, 128), chip_cols)
        return pltpu.make_async_copy(
            left_refs[2 * side + who].at[:, cols], slots.at[q % 2, who], sems.at[q % 2, who]
        )

    def fetch(side):
        for q in range(2):
            for who in range(2):
                load(side, q, who).start()

    def turn(side):
        piece = half // 2
        for q in range(4):
            for who in range(2):
                load(side, q, who).wait()
                stage[...] = slots[q % 2, who].T
                for part in range(2):
                    spot = spots[2 * q + part] * piece
                    turned[who, spot : spot + piece, :] = stage[
                        pl.ds(pl.multiple_of(place[4] * half + part * piece, 16), piece), :
                    ]
                if q < 2:
                    load(side, q + 2, who).start()

    def multiply(own, other):
        def tile(cols):
            block = mm(turned[0], own[:, cols], ((1,), (0,)))
            block = (block + mm(turned[1], other[:, cols], ((1,), (0,)))).astype(bf16)
            start = 0
            for out, size in zip(outs, cuts):
                out[:, cols] = block[start : start + size]
                start += size

        width = own.shape[1]

        def one(turn, carry):
            tile(pl.ds(pl.multiple_of(turn * 512, 512), 512))
            return carry

        lax.fori_loop(0, width // 512, one, 0)
        if width % 512:
            tile(slice(width // 512 * 512, width))

    first = 0
    before = None
    for n, (side, blocks) in enumerate(sides):
        if side != before:
            if first == 0:
                pl.when(step == 0)(functools.partial(fetch, side))
            pl.when(step == first)(functools.partial(turn, side))
        before = side
        inside = (step >= first) & (step < first + blocks)
        pl.when(inside)(functools.partial(multiply, right_refs[2 * n], right_refs[2 * n + 1]))
        first += blocks
        if n + 1 < len(sides) and sides[n + 1][0] != side:
            pl.when(step == first - 1)(functools.partial(fetch, sides[n + 1][0]))


def products(lefts, rights, cuts, spots, width, name):
    seq = lax.axis_index("seq")
    core, x, y = seq % 2, (seq // 2) % 2, seq // 4
    place = jnp.stack([(1 - y) * 2 + 1 - x, y * 2 + 1 - x, (1 - y) * 2 + x, y * 2 + x, core]).astype(jnp.int32)
    tok, model = lefts[0][0].shape
    sides = tuple((side, own.shape[1] // width) for side, own, _ in rights)
    total = sum(blocks for _, blocks in sides)
    in_specs = [pl.BlockSpec(memory_space=pl.ANY)] * (2 * len(lefts))
    first = 0
    for _, blocks in sides:

        def index(j, place, first=first, blocks=blocks):
            return (0, jnp.clip(j - first, 0, blocks - 1))

        in_specs += [pl.BlockSpec((tok, width), index)] * 2
        first += blocks
    half = model // 8
    return pl.pallas_call(
        functools.partial(products_kernel, sides, cuts, spots),
        grid_spec=pltpu.PrefetchScalarGridSpec(
            num_scalar_prefetch=1,
            grid=(total,),
            in_specs=in_specs,
            out_specs=[pl.BlockSpec((rows, width), lambda j, place: (0, j)) for rows in cuts],
            scratch_shapes=[
                pltpu.VMEM((2, 4 * half, tok), bf16),
                pltpu.VMEM((2, 2, tok, 2 * half), bf16),
                pltpu.VMEM((2 * half, tok), bf16),
                pltpu.SemaphoreType.DMA((2, 2)),
            ],
        ),
        out_shape=[jax.ShapeDtypeStruct((rows, total * width), bf16) for rows in cuts],
        compiler_params=pltpu.CompilerParams(vmem_limit_bytes=58 * 1024 * 1024),
        name=name,
    )(place, *[a for pair in lefts for a in pair], *[a for _, own, other in rights for a in (own, other)])


def add_columns(target, sources, start, size, step):
    def one(turn, carry):
        cols = pl.ds(pl.multiple_of(start + turn * step, 128), step)
        total = target[:, cols].astype(f32)
        for source in sources:
            total = total + source[:, cols].astype(f32)
        target[:, cols] = total.astype(target.dtype)
        return carry

    lax.fori_loop(0, size // step, one, 0)


def scatter_kernel(
    main, rest, mlp, mixer_sum, mlp_back,
    held, cross, near, lined,
    load_sem, flow_send, flow_recv, line_send, line_recv, swap_send, swap_recv, own_sem,
):
    s, z, _, beside, across = places()
    chip_diag, chip_beside, chip_across, chip = 0, 1, 2, 3
    rows = held.shape[1] // 4
    cols = held.shape[2]
    cut = cols // 256 * 128
    ff_part = mlp.shape[1] // 3
    parts = (main, rest)
    order = (3 * (1 - z // 2), (2 + 3 * z) % 5, 1 + z % 2, z)

    def remote(src, dst, send, recv, target):
        return pltpu.make_async_remote_copy(
            src_ref=src, dst_ref=dst, send_sem=send, recv_sem=recv, device_id=target, device_id_type=MESH
        )

    def span(k):
        return pl.ds(pl.multiple_of(k * rows, 16), rows)

    def loads(i):
        copies, start = [], 0
        for n, part in enumerate(parts):
            size = part.shape[2]
            copies.append(
                pltpu.make_async_copy(
                    part.at[:, span(order[i]), :], held.at[:, span(order[i]), pl.ds(start, size)], load_sem.at[i, n]
                )
            )
            start += size
        return copies

    left, right = pl.ds(0, cut), pl.ds(cut, cols - cut)

    def block(q, i, side):
        return held.at[q, span(order[i]), side]

    def flow(i, index):
        send, recv = flow_send.at[i, index], flow_recv.at[i, index]
        to_beside, to_across = (beside, z), (across, z)
        if index == 0:
            return remote(block(chip_diag, i, left), cross.at[i, :, left], send, recv, to_across)
        if index == 1:
            return remote(block(chip_diag, i, right), cross.at[i, :, right], send, recv, to_beside)
        if index == 2:
            return remote(block(chip_beside, i, right), near.at[0, i, :, right], send, recv, to_beside)
        if index == 3:
            return remote(block(chip_beside, i, left), near.at[0, i, :, left], send, recv, to_beside)
        if index == 4:
            return remote(block(chip_across, i, left), near.at[1, i, :, left], send, recv, to_across)
        return remote(block(chip_across, i, right), near.at[1, i, :, right], send, recv, to_across)

    def cross_step(i):
        flow(i, 0).wait_recv()
        add_columns(held.at[chip_beside, span(order[i]), :], [cross.at[i]], 0, cut, 512)
        flow(i, 3).start()
        flow(i, 1).wait_recv()
        add_columns(held.at[chip_across, span(order[i]), :], [cross.at[i]], cut, cols - cut, 384)
        flow(i, 5).start()

    def near_step(i):
        for index in (2, 4, 3, 5):
            flow(i, index).wait_recv()
        add_columns(held.at[chip, span(order[i]), :], [near.at[0, i], near.at[1, i]], 0, cols, 640)

    def line(k, slot, target):
        return remote(
            held.at[chip, span(k), :], lined.at[slot], line_send.at[k], line_recv.at[slot], (s, target)
        )

    def absorb(k, slot, source):
        line(k, slot, source).wait_recv()
        add_columns(held.at[chip, span(k), :], [lined.at[slot]], 0, cols, 640)

    def chain(i):
        k = order[i]
        if i == 3:
            pl.when(z > 0)(lambda: absorb(k, k, z - 1))
            pl.when(z < 3)(lambda: absorb(k, 4, z + 1))
            return

        @pl.when(k > z)
        def _():
            pl.when(z > 0)(lambda: absorb(k, k, z - 1))
            line(k, k, z + 1).start()

        @pl.when(k < z)
        def _():
            pl.when(z < 3)(lambda: absorb(k, k, z + 1))
            pl.when(k == z - 1)(lambda: line(k, 4, z - 1).start())
            pl.when(k < z - 1)(lambda: line(k, k, z - 1).start())

    def chain_drain():
        for i in range(3):
            k = order[i]
            line(k, k, (z + 1) % 4).wait_send()

    def pieces():
        for m in range(3):
            yield m, mlp, pl.ds(m * ff_part, ff_part)

    def swap(k):
        to = (z + k) % 4
        here = pl.ds(pl.multiple_of(z * ff_part, 128), ff_part)
        return [
            remote(
                source.at[span(to), at], mlp_back.at[m, :, here], swap_send.at[k - 1, m], swap_recv.at[k - 1, m], (s, to)
            )
            for m, source, at in pieces()
        ]

    own = [
        pltpu.make_async_copy(
            source.at[span(z), at], mlp_back.at[m, :, pl.ds(pl.multiple_of(z * ff_part, 128), ff_part)], own_sem.at[m]
        )
        for m, source, at in pieces()
    ]
    for i in range(4):
        for copy in loads(i):
            copy.start()
    greet([(beside, z), (across, z)] + [(s, (z + k) % 4) for k in range(1, 4)])
    for k in (1, 3, 2):
        for copy in swap(k):
            copy.start()
    for copy in own:
        copy.start()
    for i in range(2):
        for copy in loads(i):
            copy.wait()
        flow(i, 0).start()
        flow(i, 1).start()
        if i == 0:
            flow(i, 2).start()
            flow(i, 4).start()
    for i in range(4):
        cross_step(i)
        if i + 1 < 4:
            flow(i + 1, 2).start()
            flow(i + 1, 4).start()
        if i + 2 < 4:
            for copy in loads(i + 2):
                copy.wait()
            flow(i + 2, 0).start()
            flow(i + 2, 1).start()
        if i > 0:
            near_step(i - 1)
            chain(i - 1)
    near_step(3)
    chain(3)
    done = pltpu.make_async_copy(held.at[chip, span(z), :], mixer_sum, own_sem.at[3])
    done.start()
    for i in range(4):
        for index in range(6):
            flow(i, index).wait_send()
    chain_drain()
    for k in range(1, 4):
        for copy in swap(k):
            copy.wait()
    for copy in own:
        copy.wait()
    done.wait()


def scatter(main, rest, mlp):
    rows = main.shape[1] // 4
    cols = main.shape[2] + rest.shape[2]
    ff_part = mlp.shape[1] // 3
    anyspec = pl.BlockSpec(memory_space=pl.ANY)
    dma = pltpu.SemaphoreType.DMA
    return pl.pallas_call(
        scatter_kernel,
        in_specs=[anyspec] * 3,
        out_specs=[anyspec] * 2,
        out_shape=[
            jax.ShapeDtypeStruct((rows, cols), bf16),
            jax.ShapeDtypeStruct((3, rows, 4 * ff_part), bf16),
        ],
        scratch_shapes=[
            pltpu.VMEM((4, 4 * rows, cols), bf16),
            pltpu.VMEM((4, rows, cols), bf16),
            pltpu.VMEM((2, 4, rows, cols), bf16),
            pltpu.VMEM((5, rows, cols), bf16),
            dma((4, 2)), dma((4, 6)), dma((4, 6)), dma((4,)), dma((5,)), dma((3, 3)), dma((3, 3)), dma((4,)),
        ],
        compiler_params=pltpu.CompilerParams(
            collective_id=2, has_side_effects=True, vmem_limit_bytes=52 * 1024 * 1024
        ),
        name="scatter_gradients",
    )(main, rest, mlp)


def gather_plain(mixer, gate, up, down):
    groups = lax.axis_size("fsdp")
    part_rows, ff = gate.shape
    own = jnp.stack([w.reshape(part_rows, groups, ff // groups) for w in (gate, up, down)], axis=2)
    mine = lax.all_to_all(jnp.transpose(own, (1, 0, 2, 3)), "fsdp", 0, 0, tiled=True)
    return lax.all_gather(mixer, both, axis=0, tiled=True), mine.reshape(groups * part_rows, -1)


def from_line(shard):
    count = lax.axis_size("fsdp")
    return [shard] + [
        lax.ppermute(shard, "fsdp", [(i, (i + k) % count) for i in range(count)]) for k in range(1, count)
    ]


def swap_cores(shard):
    count = lax.axis_size("seq")
    return lax.ppermute(shard, "seq", [(i, i + 1 - 2 * (i % 2)) for i in range(count)])


def swap_beside(shard):
    return lax.ppermute(shard, "seq", [(i, i ^ 2) for i in range(8)])


def swap_across(shard):
    return lax.ppermute(shard, "seq", [(i, i ^ 4) for i in range(8)])


def add_low(left, right):
    return (left.astype(f32) + right.astype(f32)).astype(bf16)


def scatter_paired(normed, grad_both, grad_mix, mixed, rest, mlp_parts):
    seq = lax.axis_index("seq")
    core, x, y = seq % 2, (seq // 2) % 2, seq // 4
    main = products(
        [(normed, swap_cores(normed)), (grad_mix, swap_cores(grad_mix))],
        [(0, grad_both, swap_cores(grad_both)), (1, mixed, swap_cores(mixed))],
        (normed.shape[1] // 2,),
        tuple(range(8)),
        normed.shape[1],
        "mixer_products",
    )[0]
    grouped = rest.reshape(4, 2, -1, rest.shape[1])
    own = lax.dynamic_index_in_dim(grouped, core, 1, False)
    other = swap_cores(lax.dynamic_index_in_dim(grouped, 1 - core, 1, False))
    rest = (own.astype(f32) + other.astype(f32)).astype(bf16)
    rest = jnp.concatenate(
        [
            lax.dynamic_slice_in_dim(rest, q, 1, 0)
            for q in ((1 - y) * 2 + 1 - x, y * 2 + 1 - x, (1 - y) * 2 + x, y * 2 + x)
        ],
        axis=0,
    )
    main, rest, mlp_parts = lax.optimization_barrier((main, rest, mlp_parts))
    mine, *sent = [part.astype(f32) for part in mlp_parts]
    mlp_sum = mine + jnp.concatenate([sent[0] + sent[2], sent[1] + sent[3]], axis=0)
    return scatter(main.reshape(4, -1, main.shape[1]), rest, mlp_sum.astype(bf16))


def scatter_plain(normed, grad_both, grad_mix, mixed, rest, mlp_sum):
    groups = lax.axis_size("fsdp")
    term_wide = mm(normed, grad_both, ((0,), (0,))).astype(bf16)
    term_out = mm(grad_mix, mixed, ((0,), (0,))).astype(bf16)
    mixer_sum = lax.psum_scatter(
        jnp.concatenate([term_wide, term_out, rest], axis=1), "seq", scatter_dimension=0, tiled=True
    )
    mixer_sum = lax.psum_scatter(mixer_sum, "fsdp", scatter_dimension=0, tiled=True)
    ff_part = mlp_sum.shape[1] // 3
    part_rows = mlp_sum.shape[0] // groups
    mlp_sum = mlp_sum.reshape(groups, part_rows, 3, ff_part)
    mlp_back = lax.all_to_all(mlp_sum, "fsdp", 0, 0, tiled=True)
    mlp_back = jnp.transpose(mlp_back, (2, 1, 0, 3)).reshape(3, part_rows, groups * ff_part)
    return mixer_sum, mlp_back


def call_heads(kernel, width, heads, ins, outs, scratch, name):
    def spec(rows_cols):
        rows, by_row = rows_cols
        if by_row:
            return pl.BlockSpec((rows, width), lambda h: (h, 0))
        return pl.BlockSpec((rows, width), lambda h: (0, h))

    in_specs = [spec((width, True)) if rowwise else spec((a.shape[0], False)) for a, rowwise in ins]
    out_specs = [spec((width, True)) if rowwise else spec((rows, False)) for rows, _, rowwise in outs]
    out_shape = [
        jax.ShapeDtypeStruct((heads * width, width) if rowwise else (rows, heads * width), kind)
        for rows, kind, rowwise in outs
    ]
    return pl.pallas_call(
        kernel,
        grid=(heads,),
        in_specs=in_specs,
        out_specs=out_specs,
        out_shape=out_shape,
        scratch_shapes=[pltpu.VMEM((rows, width), f32) for rows in scratch],
        compiler_params=pltpu.CompilerParams(vmem_limit_bytes=40 * 1024 * 1024),
        name=name,
    )(*[a for a, _ in ins])


def on_device(
    block_input,
    cotangent,
    mixer_gain,
    branch_proj,
    gelu_proj,
    conv_taps,
    conv_bias,
    rate_blocks,
    input_blocks,
    rate_bias,
    input_bias,
    decay_param,
    out_proj,
    mlp_gain,
    gate_proj,
    up_proj,
    down_proj,
):
    groups = lax.axis_size("fsdp")
    part_rows, lru = branch_proj.shape
    width = rate_blocks.shape[1]
    heads = lru // width
    margin = conv_taps.shape[0] - 1
    tokens = block_input[0].astype(f32)
    tok_count, model = tokens.shape
    ff = gate_proj.shape[1]
    ff_part = ff // groups
    grad_out = cotangent[0]

    smalls = jnp.stack(
        [conv_taps[k] for k in range(margin + 1)]
        + [conv_bias, rate_bias, input_bias, decay_param, mixer_gain, mlp_gain],
        axis=1,
    )
    small_count = smalls.shape[1]
    smalls = jnp.pad(smalls, ((0, 0), (0, 128 - small_count)))
    mixer_own = jnp.concatenate(
        [smalls, rate_blocks, input_blocks, branch_proj, gelu_proj, out_proj], axis=1
    )
    custom = lax.axis_size("seq") == 8 and groups == 4
    if custom:
        mixer_w, mlp_mine = gather(mixer_own, gate_proj, up_proj, down_proj)
    else:
        mixer_w, mlp_mine = gather_plain(mixer_own, gate_proj, up_proj, down_proj)
    mlp_w = lax.all_gather(mlp_mine, "seq", axis=0, tiled=True)
    grad_out_late = lax.optimization_barrier((grad_out, mlp_mine))[0]
    if custom:
        grad_pieces = from_line(grad_out_late)
    first = lax.optimization_barrier(mixer_w[:, : 128 + 2 * width])
    wide = mixer_w[:, 128 + 2 * width : 128 + 2 * width + 2 * lru]
    proj_out = mixer_w[:, 128 + 2 * width + 2 * lru :]

    table = first[:, :small_count].astype(f32).T
    blocks_rate = first[:, 128 : 128 + width]
    blocks_input = first[:, 128 + width :]
    param_decay = table[margin + 4]
    gain_one = table[margin + 5]
    gain_two = table[margin + 6]
    small = jnp.concatenate(
        [
            table[: margin + 4],
            jax.nn.softplus(-param_decay)[None],
            -jax.nn.sigmoid(-param_decay)[None],
            jnp.zeros((16 - margin - 6, lru), f32),
        ],
        axis=0,
    )

    normed = norm_rows(tokens, gain_one).astype(bf16)
    both_pre = mm(normed, wide, ((1,), (0,)))
    branch = both_pre[:, :lru].astype(bf16)
    gelu_pre = both_pre[:, lru:]
    prior = from_behind(branch[tok_count - margin :], "seq", 1).astype(f32)
    prior = jnp.concatenate([jnp.zeros((8 - margin, lru), f32), prior], axis=0)
    conv, rate_pre, input_pre, cum, local = call_heads(
        mixer_forward,
        width,
        heads,
        [(branch, False), (prior, False), (small, False), (blocks_rate, True), (blocks_input, True)],
        [(tok_count, bf16, False)] + [(tok_count, f32, False)] * 4,
        [tok_count + 8],
        "mixer_forward",
    )
    carried = prefix((cum[-1], local[-1]), "seq", False)
    states = local + cum * carried[None]
    mixed = (states * jax.nn.gelu(gelu_pre, approximate=True)).astype(bf16)
    middle = tokens + mm(mixed, proj_out, ((1,), (1,)))
    normed_two = norm_rows(middle, gain_two).astype(bf16)

    if custom:
        normed_all, normed_other, grad_out_all, grad_out_other = gather_rows(normed_two, grad_pieces)
    else:
        normed_all = lax.all_gather(normed_two, "fsdp", axis=0, tiled=True)
        grad_out_all = lax.all_gather(grad_out_late, "fsdp", axis=0, tiled=True)
    w_gate, w_up, w_down = mlp_w[:, :ff_part], mlp_w[:, ff_part : 2 * ff_part], mlp_w[:, 2 * ff_part :]
    if custom:
        hidden, hidden_other, grad_pair, pair_other, grad_normed_part = feed_forward(
            normed_all, grad_out_all, mlp_w
        )
    else:
        gate = mm(normed_all, w_gate, ((1,), (0,)))
        up_val = mm(normed_all, w_up, ((1,), (0,)))
        gelu_gate, gelu_slope = gelu_parts(gate)
        hidden = (gelu_gate * up_val).astype(bf16)
        grad_hidden = mm(grad_out_all, w_down, ((1,), (0,)))
        grad_gate = (grad_hidden * up_val * gelu_slope).astype(bf16)
        grad_up = (grad_hidden * gelu_gate).astype(bf16)
        grad_normed_part = (
            mm(grad_gate, w_gate, ((1,), (1,))) + mm(grad_up, w_up, ((1,), (1,)))
        ).astype(bf16)
    grad_normed_two = lax.psum_scatter(grad_normed_part, "fsdp", scatter_dimension=0, tiled=True)
    if custom:
        half = model // 16
        early_across, early_beside, beside_low, across_high, mine = products(
            [(normed_all, normed_other), (grad_out_all, grad_out_other)],
            [(0, grad_pair, pair_other), (1, hidden, hidden_other)],
            (2 * half, 2 * half, half, half, 2 * half),
            (0, 2, 4, 3, 1, 5, 6, 7),
            ff_part,
            "feed_forward_products",
        )
        hidden = lax.optimization_barrier((hidden, mine))[0]
        out_part = mm(hidden, w_down, ((1,), (1,))).astype(bf16)
        out_part, grad_normed_two = lax.optimization_barrier((out_part, grad_normed_two))
        from_across = swap_across(early_across)
        from_beside = swap_beside(early_beside)
    else:
        grad_pair = jnp.concatenate([grad_gate, grad_up], axis=1)
        term_pair = mm(normed_all, grad_pair, ((0,), (0,))).astype(bf16)
        term_down = mm(grad_out_all, hidden, ((0,), (0,))).astype(bf16)
        pair_sum = lax.psum_scatter(term_pair, "seq", scatter_dimension=0, tiled=True)
        down_sum = lax.psum_scatter(term_down, "seq", scatter_dimension=0, tiled=True)
        mlp_sum = jnp.concatenate([pair_sum, down_sum], axis=1)
        out_part = mm(hidden, w_down, ((1,), (1,))).astype(bf16)
    out_sum = lax.psum_scatter(out_part, "fsdp", scatter_dimension=0, tiled=True)
    block_output = (middle + out_sum.astype(f32)).astype(bf16)[None]
    grad_normed_two = grad_normed_two.astype(f32)

    second_pull = jax.vjp(norm_rows, middle, gain_two)[1]
    grad_mid_part, grad_gain_two = second_pull(grad_normed_two)
    grad_middle = grad_out.astype(f32) + grad_mid_part
    grad_mix = grad_middle.astype(bf16)
    grad_mixed = mm(grad_mix, proj_out, ((1,), (0,)))
    carried_rows = jnp.broadcast_to(carried[None], (8, lru))
    grad_gelu_pre, rev_cum, rev_grad, pair_grad = call_heads(
        mixer_backward_scan,
        width,
        heads,
        [(a, False) for a in (grad_mixed, gelu_pre, rate_pre, cum, local, carried_rows, small)],
        [(tok_count, bf16, False), (tok_count, f32, False), (tok_count, f32, False), (8, f32, False)],
        [tok_count + 8],
        "mixer_backward_scan",
    )
    incoming = prefix((cum[-1], pair_grad[0]), "seq", True)
    incoming_rows = jnp.broadcast_to(incoming[None], (8, lru))
    own, head, rate_w_grad, input_w_grad, sums = call_heads(
        mixer_backward,
        width,
        heads,
        [
            (a, False)
            for a in (rev_cum, rev_grad, incoming_rows, cum, local, carried_rows, rate_pre, input_pre, conv, branch, prior, small)
        ]
        + [(blocks_rate, True), (blocks_input, True)],
        [(tok_count, f32, False), (8, f32, False), (0, bf16, True), (0, bf16, True), (8, f32, False)],
        [tok_count + 8, tok_count + 16],
        "mixer_backward",
    )
    received = from_behind(head[8 - margin :], "seq", -1)
    grad_branch = jnp.concatenate(
        [own[: tok_count - margin], own[tok_count - margin :] + received], axis=0
    ).astype(bf16)
    grad_both = jnp.concatenate([grad_branch, grad_gelu_pre], axis=1)
    grad_normed = mm(grad_both, wide, ((1,), (1,)))
    if custom:
        from_across, from_beside, grad_normed = lax.optimization_barrier((from_across, from_beside, grad_normed))
        beside_low = add_low(beside_low, from_across[:half])
        across_high = add_low(across_high, from_beside[:half])
        beside_low, across_high, grad_normed = lax.optimization_barrier((beside_low, across_high, grad_normed))
        mlp_parts = (
            mine, from_across[half:], swap_across(across_high), swap_beside(beside_low), from_beside[half:]
        )
    first_pull = jax.vjp(norm_rows, tokens, gain_one)[1]
    grad_tok_part, grad_gain_one = first_pull(grad_normed)
    input_grad = (grad_middle + grad_tok_part).astype(bf16)[None]
    vectors = jnp.concatenate([sums, grad_gain_one[None], grad_gain_two[None]], axis=0).T
    vectors = jnp.pad(vectors, ((0, 0), (0, 128 - vectors.shape[1]))).astype(bf16)
    rest = jnp.concatenate([rate_w_grad, input_w_grad, vectors], axis=1)
    if custom:
        mixer_sum, mlp_back = scatter_paired(normed, grad_both, grad_mix, mixed, rest, mlp_parts)
    else:
        mixer_sum, mlp_back = scatter_plain(normed, grad_both, grad_mix, mixed, rest, mlp_sum)
    mlp_grads = [mlp_back[m].astype(f32) for m in range(3)]
    mixer_sum = mixer_sum.astype(f32)
    edges = [lru, 2 * lru, 3 * lru, 3 * lru + width, 3 * lru + 2 * width]
    dbranch, dgelu, dout, drate, dinput, vec = jnp.split(mixer_sum, edges, axis=1)
    vec = vec.T
    return (
        block_output,
        input_grad,
        vec[8],
        dbranch,
        dgelu,
        vec[: margin + 1],
        vec[7],
        drate,
        dinput,
        vec[4],
        vec[5],
        vec[6],
        dout,
        vec[9],
        mlp_grads[0],
        mlp_grads[1],
        mlp_grads[2],
    )


def solution(mesh):
    tokens = P("fsdp", "seq", None)
    vector = P(both)
    matrix = P(both, None)
    taps = P(None, both)
    return jax.shard_map(
        on_device,
        mesh=mesh,
        in_specs=(
            tokens, tokens, vector, matrix, matrix, taps, vector, matrix, matrix,
            vector, vector, vector, matrix, vector, matrix, matrix, matrix,
        ),
        out_specs=(
            tokens, tokens, vector, matrix, matrix, taps, vector, matrix, matrix,
            vector, vector, vector, matrix, vector, matrix, matrix, matrix,
        ),
        check_vma=False,
    )
```

```python
import functools

import jax
import jax.numpy as jnp
from jax import lax
from jax.experimental import pallas as pl
from jax.experimental.pallas import tpu as pltpu
from jax.sharding import PartitionSpec as P

epsilon = 1e-06
f32 = jnp.float32
bf16 = jnp.bfloat16
both = ("seq", "fsdp")
MESH = pl.DeviceIdType.MESH
TAP, CONV_BIAS, RATE_BIAS, INPUT_BIAS, SOFT, SOFT_SLOPE = 0, 4, 5, 6, 7, 8
GELU_C = 0.7978845608028654
GELU_A = 0.044715


def from_behind(shard, axis, by):
    devices = lax.axis_size(axis)
    pairs = [(i, i + by) for i in range(devices) if 0 <= i + by < devices]
    return lax.ppermute(shard, axis, pairs)


def prefix(part, axis, reverse):
    count = lax.axis_size(axis)
    place = lax.axis_index(axis)
    gathered = lax.all_gather(jnp.stack(part), axis)
    state = jnp.zeros_like(part[1])
    for hop in range(count):
        source = count - 1 - hop if reverse else hop
        ahead = source > place if reverse else source < place
        state = jnp.where(ahead, gathered[source, 1] + gathered[source, 0] * state, state)
    return state


def norm_rows(values, scales):
    return values * lax.rsqrt(jnp.mean(values * values, axis=-1, keepdims=True) + epsilon) * scales


def norm_back(values, scales, grads):
    inverse = lax.rsqrt(jnp.mean(values * values, axis=-1, keepdims=True) + epsilon)
    scaled = grads * scales
    shared = jnp.mean(values * scaled, axis=-1, keepdims=True)
    return inverse * scaled - values * (inverse * inverse * inverse * shared)


def gain_back(gain, *pairs):
    total = sum(jnp.sum(weight.astype(f32) * grad, axis=1) for weight, grad in pairs)
    return total / gain.astype(f32)


def gelu_parts(x):
    inner = jnp.tanh(GELU_C * (x + GELU_A * x * x * x))
    return 0.5 * x * (1.0 + inner), 0.5 * (1.0 + inner) + 0.5 * x * (1.0 - inner * inner) * (
        GELU_C * (1.0 + 3.0 * GELU_A * x * x)
    )


def mm(left, right, dims):
    return lax.dot_general(left, right, (dims, ((), ())), preferred_element_type=f32)


def sigmoid(x):
    return 1.0 / (1.0 + jnp.exp(-x))


def scan_rows(decay, value, reverse):
    rows = decay.shape[0]
    place = lax.broadcasted_iota(jnp.int32, decay.shape, 0)
    step = 1
    while step < rows:
        shift = rows - step if reverse else step
        inside = place < rows - step if reverse else place >= step
        before_value = jnp.where(inside, pltpu.roll(value, shift, 0), 0.0)
        before_decay = jnp.where(inside, pltpu.roll(decay, shift, 0), 1.0)
        value = value + decay * before_value
        decay = decay * before_decay
        step *= 2
    return decay, value


def gates(rate_pre, input_pre, soft):
    rate = sigmoid(rate_pre)
    log_decay = -8.0 * rate * soft
    decay = jnp.exp(log_decay)
    square = decay * decay
    root = jnp.sqrt(-jnp.tanh(log_decay) * (1.0 + square))
    return rate, decay, square, root, sigmoid(input_pre)


def mixer_forward(branch, prior, small, rate_w, input_w, conv, rate_pre, input_pre, cum, local, ext):
    rows = branch.shape[0]
    ext[0:8, :] = prior[...]
    ext[8:, :] = branch[...].astype(f32)
    total = small[CONV_BIAS : CONV_BIAS + 1, :] + small[TAP : TAP + 1, :] * ext[8:, :]
    for offset in range(1, 4):
        total = total + small[TAP + offset : TAP + offset + 1, :] * ext[pl.ds(8 - offset, rows), :]
    low = total.astype(bf16)
    conv[...] = low
    rate = mm(low, rate_w[...], ((1,), (0,))) + small[RATE_BIAS : RATE_BIAS + 1, :]
    inp = mm(low, input_w[...], ((1,), (0,))) + small[INPUT_BIAS : INPUT_BIAS + 1, :]
    rate_pre[...] = rate
    input_pre[...] = inp
    _, decay, _, root, opened = gates(rate, inp, small[SOFT : SOFT + 1, :])
    product, states = scan_rows(decay, root * opened * low.astype(f32), False)
    cum[...] = product
    local[...] = states


def mixer_backward_scan(grad_mixed, gelu_pre, rate_pre, cum, local, carried, small, grad_pre, rev_cum, rev_grad, pair, ext):
    rows = grad_mixed.shape[0]
    states = local[...] + cum[...] * carried[0:1, :]
    value, slope = gelu_parts(gelu_pre[...])
    grad = grad_mixed[...]
    grad_pre[...] = (grad * states * slope).astype(bf16)
    decay = jnp.exp(-8.0 * sigmoid(rate_pre[...]) * small[SOFT : SOFT + 1, :])
    ext[0:rows, :] = decay
    ext[rows:, :] = jnp.ones((8, decay.shape[1]), f32)
    product, back = scan_rows(ext[pl.ds(1, rows), :], grad * value, True)
    rev_cum[...] = product
    rev_grad[...] = back
    pair[...] = jnp.broadcast_to(decay[0:1, :] * back[0:1, :], pair.shape)


def mixer_backward(
    rev_cum, rev_grad, incoming, cum, local, carried, rate_pre, input_pre, conv, branch, prior, small, rate_w, input_w,
    own, head, rate_w_grad, input_w_grad, sums, ext, gext,
):
    rows = rev_cum.shape[0]
    soft = small[SOFT : SOFT + 1, :]
    grad_states = rev_grad[...] + rev_cum[...] * incoming[0:1, :]
    rate, decay, square, root, opened = gates(rate_pre[...], input_pre[...], soft)
    ext[0:8, :] = jnp.broadcast_to(carried[0:1, :], (8, carried.shape[1]))
    ext[8:, :] = local[...] + cum[...] * carried[0:1, :]
    before = ext[pl.ds(7, rows), :]
    low = conv[...]
    conv_in = low.astype(f32)
    grad_log = grad_states * decay * before - grad_states * opened * conv_in * square / root
    driven = grad_states * root
    grad_input = (driven * conv_in * opened * (1.0 - opened)).astype(bf16)
    by_rate = grad_log * (-8.0 * rate)
    grad_rate = (by_rate * soft * (1.0 - rate)).astype(bf16)
    sums[6:7, :] = jnp.sum(by_rate, axis=0, keepdims=True) * small[SOFT_SLOPE : SOFT_SLOPE + 1, :]
    sums[4:5, :] = jnp.sum(grad_rate.astype(f32), axis=0, keepdims=True)
    sums[5:6, :] = jnp.sum(grad_input.astype(f32), axis=0, keepdims=True)
    rate_w_grad[...] = mm(low, grad_rate, ((0,), (0,))).astype(rate_w_grad.dtype)
    input_w_grad[...] = mm(low, grad_input, ((0,), (0,))).astype(input_w_grad.dtype)
    grad_conv = (
        driven * opened
        + mm(grad_rate, rate_w[...], ((1,), (1,)))
        + mm(grad_input, input_w[...], ((1,), (1,)))
    )
    sums[7:8, :] = jnp.sum(grad_conv, axis=0, keepdims=True)
    ext[0:8, :] = prior[...]
    ext[8:, :] = branch[...].astype(f32)
    gext[0:8, :] = jnp.zeros((8, grad_conv.shape[1]), f32)
    gext[8 : 8 + rows, :] = grad_conv
    gext[8 + rows :, :] = jnp.zeros((8, grad_conv.shape[1]), f32)
    back = jnp.zeros_like(grad_conv)
    front = jnp.zeros((8, grad_conv.shape[1]), f32)
    for offset in range(4):
        tap = small[TAP + offset : TAP + offset + 1, :]
        sums[offset : offset + 1, :] = jnp.sum(
            grad_conv * ext[pl.ds(8 - offset, rows), :], axis=0, keepdims=True
        )
        back = back + tap * gext[pl.ds(8 + offset, rows), :]
        front = front + tap * gext[pl.ds(offset, 8), :]
    own[...] = back
    head[...] = front


def places():
    s = lax.axis_index("seq")
    z = lax.axis_index("fsdp")
    core = s + 1 - 2 * (s % 2)
    beside = s + 2 - 4 * ((s // 2) % 2)
    across = s + 4 - 8 * (s // 4)
    return s, z, core, beside, across


def greet(peers):
    barrier = pltpu.get_barrier_semaphore()
    for peer in peers:
        pl.semaphore_signal(barrier, inc=1, device_id=peer, device_id_type=MESH)
    pl.semaphore_wait(barrier, len(peers))


def gather_kernel(
    first, branch, gelu, outer, gate, up, down, mixer_all, mlp_mine,
    mixer, load_sem, flow_send, flow_recv, line_send, line_recv, swap_send, swap_recv, own_sem,
):
    s, z, core, beside, across = places()
    rows, cols = mixer.shape
    ff_part = mlp_mine.shape[1] // 3
    cut = cols // 256 * 128
    diag = beside + across - s
    loads, start = [], 0
    for n, part in enumerate((first, branch, gelu, outer)):
        size = part.shape[1]
        loads.append(pltpu.make_async_copy(part, mixer.at[:, pl.ds(start, size)], load_sem.at[n]))
        loads[-1].start()
        start += size
    greet([(core, z), (beside, z), (across, z)] + [(s, (z + k) % 4) for k in range(1, 4)])

    def remote(src, dst, send, recv, target):
        return pltpu.make_async_remote_copy(
            src_ref=src, dst_ref=dst, send_sem=send, recv_sem=recv, device_id=target, device_id_type=MESH
        )

    def piece(seq, zz, half=None):
        span = pl.ds(pl.multiple_of((seq * 4 + zz) * rows, 16), rows)
        if half is None:
            return mixer_all.at[span, :]
        return mixer_all.at[span, pl.ds(0, cut) if half == 0 else pl.ds(cut, cols - cut)]

    def flow(zz, index, seq, half, target, src=None):
        ref = piece(seq, zz, half)
        return remote(
            ref if src is None else src, ref, flow_send.at[zz, index], flow_recv.at[zz, index], (target, z)
        )

    def sends(zz, src=None):
        return [
            flow(zz, 0, s, None, beside, src),
            flow(zz, 1, s, None, across, src),
            flow(zz, 4, s, None, core, src),
        ]

    def spread(zz, src=None):
        for copy in sends(zz, src):
            copy.start()

    def relay(zz):
        flow(zz, 0, beside, None, beside).wait_recv()
        flow(zz, 3, beside, 0, across).start()
        flow(zz, 5, beside, None, core).start()
        flow(zz, 1, across, None, across).wait_recv()
        flow(zz, 2, across, 1, beside).start()
        flow(zz, 6, across, None, core).start()

    def finish(zz):
        flow(zz, 3, diag, 0, across).wait_recv()
        flow(zz, 7, diag, 0, core).start()
        flow(zz, 2, diag, 1, beside).wait_recv()
        flow(zz, 8, diag, 1, core).start()

    def drain(zz, src=None):
        for copy in sends(zz, src):
            copy.wait_send()
        flow(zz, 3, beside, 0, across).wait_send()
        flow(zz, 5, beside, None, core).wait_send()
        flow(zz, 2, across, 1, beside).wait_send()
        flow(zz, 6, across, None, core).wait_send()
        flow(zz, 7, diag, 0, core).wait_send()
        flow(zz, 8, diag, 1, core).wait_send()
        flip = core - s
        flow(zz, 4, core, None, core).wait_recv()
        flow(zz, 5, beside + flip, None, core).wait_recv()
        flow(zz, 6, across + flip, None, core).wait_recv()
        flow(zz, 7, diag + flip, 0, core).wait_recv()
        flow(zz, 8, diag + flip, 1, core).wait_recv()

    def line(zz, up_way, hop, src=None):
        ref = piece(s, zz)
        way = 0 if up_way else 1
        target = z + 1 if up_way else z - 1
        return remote(
            ref if src is None else src, ref, line_send.at[way, hop], line_recv.at[way, hop], (s, target)
        )

    def line_hop(hop):
        def below():
            line(z - hop, True, hop - 1).wait_recv()
            pl.when(z < 3)(lambda: line(z - hop, True, hop).start())

        def above():
            line(z + hop, False, hop - 1).wait_recv()
            pl.when(z > 0)(lambda: line(z + hop, False, hop).start())

        pl.when(z >= hop)(below)
        pl.when(z + hop <= 3)(above)

    def at_hop(hop, act):
        pl.when(z >= hop)(lambda: act(z - hop))
        pl.when(z + hop <= 3)(lambda: act(z + hop))

    def landing(m, zz):
        return mlp_mine.at[pl.ds(pl.multiple_of(zz * rows, 16), rows), pl.ds(m * ff_part, ff_part)]

    def columns(m, zz):
        return (gate, up, down)[m].at[:, pl.ds(pl.multiple_of(zz * ff_part, 128), ff_part)]

    def swap(k, m, arriving=False):
        to = (z + k) % 4
        came = (z + 4 - k) % 4
        return remote(
            columns(m, to), landing(m, came if arriving else z), swap_send.at[k - 1, m], swap_recv.at[k - 1, m], (s, to)
        )

    local = [pltpu.make_async_copy(columns(m, z), landing(m, z), own_sem.at[m]) for m in range(3)]
    local.append(pltpu.make_async_copy(mixer, piece(s, z), own_sem.at[3]))
    for copy in loads:
        copy.wait()

    pl.when(z < 3)(lambda: line(z, True, 0, mixer).start())
    pl.when(z > 0)(lambda: line(z, False, 0, mixer).start())
    spread(z, mixer)
    for copy in local:
        copy.start()
    line_hop(1)
    at_hop(1, spread)
    relay(z)
    line_hop(2)
    at_hop(2, spread)
    finish(z)
    at_hop(1, relay)
    line_hop(3)
    at_hop(3, spread)
    for k in (1, 3, 2):
        for m in range(3):
            swap(k, m).start()
    at_hop(1, finish)
    at_hop(2, relay)
    at_hop(3, relay)
    at_hop(2, finish)
    at_hop(3, finish)
    drain(z, mixer)
    for hop in range(1, 4):
        at_hop(hop, drain)
    for copy in local:
        copy.wait()
    for k in (1, 3, 2):
        for m in range(3):
            swap(k, m).wait_send()
            swap(k, m, True).wait_recv()
    pl.when(z < 3)(lambda: line(z, True, 0, mixer).wait_send())
    pl.when(z > 0)(lambda: line(z, False, 0, mixer).wait_send())
    for hop in range(1, 3):
        pl.when((z >= hop) & (z < 3))(lambda: line(z - hop, True, hop).wait_send())
        pl.when((z + hop <= 3) & (z > 0))(lambda: line(z + hop, False, hop).wait_send())


def gather(first, branch, gelu, outer, gate, up, down):
    rows = first.shape[0]
    cols = first.shape[1] + branch.shape[1] + gelu.shape[1] + outer.shape[1]
    ff_part = gate.shape[1] // 4
    anyspec = pl.BlockSpec(memory_space=pl.ANY)
    dma = pltpu.SemaphoreType.DMA
    return pl.pallas_call(
        gather_kernel,
        in_specs=[anyspec] * 7,
        out_specs=[anyspec] * 2,
        out_shape=[
            jax.ShapeDtypeStruct((32 * rows, cols), bf16),
            jax.ShapeDtypeStruct((4 * rows, 3 * ff_part), bf16),
        ],
        scratch_shapes=[
            pltpu.VMEM((rows, cols), bf16), dma((4,)),
            dma((4, 9)), dma((4, 9)), dma((2, 3)), dma((2, 3)), dma((3, 3)), dma((3, 3)), dma((4,)),
        ],
        compiler_params=pltpu.CompilerParams(collective_id=1, has_side_effects=True),
        name="gather_weights",
    )(first, branch, gelu, outer, gate, up, down)


def rows_kernel(
    normed, grad0, grad1, grad2, grad3, normed_all, normed_other, grad_all, grad_other,
    line_send, line_recv, core_send, core_recv, own_sem, held,
):
    s, z, core, _, _ = places()
    tok = normed.shape[0]
    cuts = 4
    grads = (grad0, grad1, grad2, grad3)
    greet([(core, z)] + [(s, (z + k) % 4) for k in range(1, 4)])

    def rows(ref, zz):
        return ref.at[pl.ds(pl.multiple_of(zz * tok, 16), tok), :]

    def remote(src, dst, send, recv, target):
        return pltpu.make_async_remote_copy(
            src_ref=src, dst_ref=dst, send_sem=send, recv_sem=recv, device_id=target, device_id_type=MESH
        )

    def parts(ref):
        size = tok // cuts
        return [ref.at[pl.ds(n * size, size), :] for n in range(cuts)]

    def line(zz, up_way, hop):
        way = 0 if up_way else 1
        target = z + 1 if up_way else z - 1
        src = normed if hop == 0 else rows(normed_all, zz)
        dst = rows(normed_all, zz)
        return [
            remote(a, b, line_send.at[way, hop, n], line_recv.at[way, hop, n], (s, target))
            for n, (a, b) in enumerate(zip(parts(src), parts(dst)))
        ]

    def over(zz, own=False):
        src = normed if own else rows(normed_all, zz)
        return remote(src, rows(normed_other, zz), core_send.at[0, zz], core_recv.at[0, zz], (core, z))

    def grad_over(k):
        zz = (z + 4 - k) % 4
        return remote(grads[k], rows(grad_other, zz), core_send.at[1, zz], core_recv.at[1, zz], (core, z))

    def line_start(zz, up_way, hop):
        for copy in line(zz, up_way, hop):
            copy.start()

    def line_drain(zz, up_way, hop):
        for copy in line(zz, up_way, hop):
            copy.wait_send()

    def hop_step(hop):
        def below():
            for came, on in zip(line(z - hop, True, hop - 1), line(z - hop, True, hop) if hop < 3 else [None] * cuts):
                came.wait_recv()
                if on is not None:
                    pl.when(z < 3)(on.start)
            over(z - hop).start()

        def above():
            for came, on in zip(line(z + hop, False, hop - 1), line(z + hop, False, hop) if hop < 3 else [None] * cuts):
                came.wait_recv()
                if on is not None:
                    pl.when(z > 0)(on.start)
            over(z + hop).start()

        pl.when(z >= hop)(below)
        pl.when(z + hop <= 3)(above)

    local = [pltpu.make_async_copy(grads[k], held.at[k], own_sem.at[k]) for k in range(4)]
    local.append(pltpu.make_async_copy(normed, held.at[4], own_sem.at[4]))
    stored = [
        pltpu.make_async_copy(held.at[k], rows(grad_all, (z + 4 - k) % 4), own_sem.at[k]) for k in range(4)
    ]
    stored.append(pltpu.make_async_copy(held.at[4], rows(normed_all, z), own_sem.at[4]))
    pl.when(z < 3)(lambda: line_start(z, True, 0))
    pl.when(z > 0)(lambda: line_start(z, False, 0))
    over(z, True).start()
    for copy in local:
        copy.start()
    for k in range(4):
        grad_over(k).start()
    for copy, store in zip(local, stored):
        copy.wait()
        store.start()
    for hop in range(1, 4):
        hop_step(hop)
    for copy in stored:
        copy.wait()
    for k in range(4):
        grad_over(k).wait()
    over(z, True).wait()
    for k in range(1, 4):
        over((z + k) % 4).wait()
    pl.when(z < 3)(lambda: line_drain(z, True, 0))
    pl.when(z > 0)(lambda: line_drain(z, False, 0))
    for hop in range(1, 3):
        pl.when((z >= hop) & (z < 3))(lambda: line_drain(z - hop, True, hop))
        pl.when((z + hop <= 3) & (z > 0))(lambda: line_drain(z + hop, False, hop))


def gather_rows(normed, grads):
    tok, model = normed.shape
    anyspec = pl.BlockSpec(memory_space=pl.ANY)
    dma = pltpu.SemaphoreType.DMA
    return pl.pallas_call(
        rows_kernel,
        in_specs=[anyspec] * 5,
        out_specs=[anyspec] * 4,
        out_shape=[jax.ShapeDtypeStruct((4 * tok, model), bf16)] * 4,
        scratch_shapes=[dma((2, 3, 4)), dma((2, 3, 4)), dma((2, 4)), dma((2, 4)), dma((5,)), pltpu.VMEM((5, tok, model), bf16)],
        compiler_params=pltpu.CompilerParams(collective_id=3, has_side_effects=True),
        name="gather_rows",
    )(normed, *grads)


def column_tiles(cols, size=512):
    return [(start, min(size, cols - start)) for start in range(0, cols, size)]


def feed_forward_kernel(
    normed, grad_out, weights, hidden, hidden_other, pair, pair_other, back,
    held, hidden_now, pair_now, sems, store_sem, core_send, core_recv,
):
    s, z, core, _, _ = places()
    step = pl.program_id(0)
    ff_part = held.shape[2]
    model = held.shape[1]
    rows = normed.shape[0]
    tiles = column_tiles(ff_part)
    made = ((hidden_now, hidden, hidden_other), (pair_now, pair, pair_other))

    def load(n, m):
        start, size = tiles[n]
        return pltpu.make_async_copy(
            weights.at[:, pl.ds(m * ff_part + start, size)], held.at[m, :, pl.ds(start, size)], sems.at[n, m]
        )

    def kept(n, turn):
        now, mine, _ = made[n]
        return pltpu.make_async_copy(now.at[turn], mine.at[pl.ds(turn * rows, rows), :], store_sem.at[turn, n])

    def handed(n, turn):
        now, _, other = made[n]
        return pltpu.make_async_remote_copy(
            src_ref=now.at[turn],
            dst_ref=other.at[pl.ds(turn * rows, rows), :],
            send_sem=core_send.at[turn, n],
            recv_sem=core_recv.at[turn, n],
            device_id=(core, z),
            device_id_type=MESH,
        )

    @pl.when(step == 0)
    def _():
        for n in range(len(tiles)):
            for m in range(3):
                load(n, m).start()
        greet([(core, z)])

    for n, (start, size) in enumerate(tiles):
        cols = slice(start, start + size)

        @pl.when(step == 0)
        def _(n=n):
            for m in range(3):
                load(n, m).wait()

        gate = mm(normed[...], held[0, :, cols], ((1,), (0,)))
        value, slope = gelu_parts(gate)
        up = mm(normed[...], held[1, :, cols], ((1,), (0,)))
        hidden_now[step, :, cols] = (value * up).astype(bf16)
        grad_hidden = mm(grad_out[...], held[2, :, cols], ((1,), (0,)))
        pair_now[step, :, cols] = (grad_hidden * up * slope).astype(bf16)
        pair_now[step, :, slice(ff_part + start, ff_part + start + size)] = (grad_hidden * value).astype(bf16)

    for turn in range(2):

        @pl.when(step == turn)
        def _(turn=turn):
            for n in range(2):
                handed(n, turn).start()
                kept(n, turn).start()

    def back_tile(turn, carry):
        cols = pl.ds(pl.multiple_of(turn * 512, 512), 512)
        total = mm(pair_now[step, :, :ff_part], held[0, cols, :], ((1,), (1,)))
        total = total + mm(pair_now[step, :, ff_part:], held[1, cols, :], ((1,), (1,)))
        back[:, cols] = total.astype(bf16)
        return carry

    lax.fori_loop(0, model // 512, back_tile, 0)

    @pl.when(step == 1)
    def _():
        for turn in range(2):
            for n in range(2):
                kept(n, turn).wait()
                handed(n, turn).wait()


def feed_forward(normed, grad_out, weights):
    tok, model = normed.shape
    ff_part = weights.shape[1] // 3
    rows = tok // 2
    anyspec = pl.BlockSpec(memory_space=pl.ANY)
    dma = pltpu.SemaphoreType.DMA
    block = pl.BlockSpec((rows, model), lambda i: (i, 0))
    return pl.pallas_call(
        feed_forward_kernel,
        grid=(2,),
        in_specs=[block, block, anyspec],
        out_specs=[anyspec] * 4 + [block],
        out_shape=[
            jax.ShapeDtypeStruct((tok, cols), bf16)
            for cols in (ff_part, ff_part, 2 * ff_part, 2 * ff_part, model)
        ],
        scratch_shapes=[
            pltpu.VMEM((3, model, ff_part), bf16),
            pltpu.VMEM((2, rows, ff_part), bf16),
            pltpu.VMEM((2, rows, 2 * ff_part), bf16),
            dma((len(column_tiles(ff_part)), 3)), dma((2, 2)), dma((2, 2)), dma((2, 2)),
        ],
        compiler_params=pltpu.CompilerParams(
            collective_id=4, has_side_effects=True, vmem_limit_bytes=60 * 1024 * 1024
        ),
        name="feed_forward",
    )(normed, grad_out, weights)


def products_kernel(sides, cuts, chips, spots, place, *refs):
    lefts = 1 + max(side for side, _ in sides)
    left_refs = refs[: 2 * lefts]
    right_refs = refs[2 * lefts : 2 * lefts + 2 * len(sides)]
    outs = refs[2 * lefts + 2 * len(sides) : -4]
    turned, slots, stage, sems = refs[-4:]
    tok = left_refs[0].shape[0]
    chip_cols = left_refs[0].shape[1] // 4
    half = chip_cols // 2
    step = pl.program_id(0)

    def load(side, q, who):
        cols = pl.ds(pl.multiple_of(place[chips[q]] * chip_cols, 128), chip_cols)
        return pltpu.make_async_copy(
            left_refs[2 * side + who].at[:, cols], slots.at[q % 2, who], sems.at[q % 2, who]
        )

    def fetch(side):
        for q in range(min(2, len(chips))):
            for who in range(2):
                load(side, q, who).start()

    def turn(side):
        piece = half // 2
        for q in range(len(chips)):
            for who in range(2):
                load(side, q, who).wait()
                stage[...] = slots[q % 2, who].T
                for part in range(2):
                    spot = spots[2 * q + part] * piece
                    turned[who, spot : spot + piece, :] = stage[
                        pl.ds(pl.multiple_of(place[4] * half + part * piece, 16), piece), :
                    ]
                if q + 2 < len(chips):
                    load(side, q + 2, who).start()

    def multiply(own, other):
        def tile(cols):
            block = mm(turned[0], own[:, cols], ((1,), (0,)))
            block = (block + mm(turned[1], other[:, cols], ((1,), (0,)))).astype(bf16)
            start = 0
            for out, size in zip(outs, cuts):
                out[:, cols] = block[start : start + size]
                start += size

        width = own.shape[1]

        def one(turn, carry):
            tile(pl.ds(pl.multiple_of(turn * 512, 512), 512))
            return carry

        lax.fori_loop(0, width // 512, one, 0)
        if width % 512:
            tile(slice(width // 512 * 512, width))

    first = 0
    before = None
    for n, (side, blocks) in enumerate(sides):
        if side != before:
            if first == 0:
                pl.when(step == 0)(functools.partial(fetch, side))
            pl.when(step == first)(functools.partial(turn, side))
        before = side
        inside = (step >= first) & (step < first + blocks)
        pl.when(inside)(functools.partial(multiply, right_refs[2 * n], right_refs[2 * n + 1]))
        first += blocks
        if n + 1 < len(sides) and sides[n + 1][0] != side:
            pl.when(step == first - 1)(functools.partial(fetch, sides[n + 1][0]))


def products(lefts, rights, cuts, chips, spots, width, name):
    seq = lax.axis_index("seq")
    core, x, y = seq % 2, (seq // 2) % 2, seq // 4
    place = jnp.stack([(1 - y) * 2 + 1 - x, y * 2 + 1 - x, (1 - y) * 2 + x, y * 2 + x, core]).astype(jnp.int32)
    tok, model = lefts[0][0].shape
    sides = tuple((side, own.shape[1] // width) for side, own, _ in rights)
    total = sum(blocks for _, blocks in sides)
    in_specs = [pl.BlockSpec(memory_space=pl.ANY)] * (2 * len(lefts))
    first = 0
    for _, blocks in sides:

        def index(j, place, first=first, blocks=blocks):
            return (0, jnp.clip(j - first, 0, blocks - 1))

        in_specs += [pl.BlockSpec((tok, width), index)] * 2
        first += blocks
    half = model // 8
    return pl.pallas_call(
        functools.partial(products_kernel, sides, cuts, chips, spots),
        grid_spec=pltpu.PrefetchScalarGridSpec(
            num_scalar_prefetch=1,
            grid=(total,),
            in_specs=in_specs,
            out_specs=[pl.BlockSpec((rows, width), lambda j, place: (0, j)) for rows in cuts],
            scratch_shapes=[
                pltpu.VMEM((2, len(chips) * half, tok), bf16),
                pltpu.VMEM((2, 2, tok, 2 * half), bf16),
                pltpu.VMEM((2 * half, tok), bf16),
                pltpu.SemaphoreType.DMA((2, 2)),
            ],
        ),
        out_shape=[jax.ShapeDtypeStruct((rows, total * width), bf16) for rows in cuts],
        compiler_params=pltpu.CompilerParams(vmem_limit_bytes=58 * 1024 * 1024),
        name=name,
    )(place, *[a for pair in lefts for a in pair], *[a for _, own, other in rights for a in (own, other)])


def add_columns(target, sources, start, size, step):
    def one(turn, carry):
        cols = pl.ds(pl.multiple_of(start + turn * step, 128), step)
        total = target[:, cols].astype(f32)
        for source in sources:
            total = total + source[:, cols].astype(f32)
        target[:, cols] = total.astype(target.dtype)
        return carry

    lax.fori_loop(0, size // step, one, 0)


def scatter_kernel(
    main, rest, mlp_low, mlp_high, grad_both, mixer_w, tokens, grad_middle, gain, mixer_sum, mlp_back, input_grad,
    held, cross, near, lined, both_now, wide_now, back_now, tokens_now, middle_now, gain_now, wide_sem,
    load_sem, flow_send, flow_recv, line_send, line_recv, swap_send, swap_recv, own_sem,
):
    s, z, _, beside, across = places()
    chip_diag, chip_beside, chip_across, chip = 0, 1, 2, 3
    rows = held.shape[1] // 4
    cols = held.shape[2]
    cut = cols // 256 * 128
    ff_part = mlp_low.shape[1] // 3
    parts = (main, rest)
    order = (3 * (1 - z // 2), (2 + 3 * z) % 5, 1 + z % 2, z)

    def remote(src, dst, send, recv, target):
        return pltpu.make_async_remote_copy(
            src_ref=src, dst_ref=dst, send_sem=send, recv_sem=recv, device_id=target, device_id_type=MESH
        )

    def span(k):
        return pl.ds(pl.multiple_of(k * rows, 16), rows)

    def loads(i):
        copies, start = [], 0
        for n, part in enumerate(parts):
            size = part.shape[2]
            copies.append(
                pltpu.make_async_copy(
                    part.at[:, span(order[i]), :], held.at[:, span(order[i]), pl.ds(start, size)], load_sem.at[i, n]
                )
            )
            start += size
        return copies

    left, right = pl.ds(0, cut), pl.ds(cut, cols - cut)

    def block(q, i, side):
        return held.at[q, span(order[i]), side]

    def flow(i, index):
        send, recv = flow_send.at[i, index], flow_recv.at[i, index]
        to_beside, to_across = (beside, z), (across, z)
        if index == 0:
            return remote(block(chip_diag, i, left), cross.at[i, :, left], send, recv, to_across)
        if index == 1:
            return remote(block(chip_diag, i, right), cross.at[i, :, right], send, recv, to_beside)
        if index == 2:
            return remote(block(chip_beside, i, right), near.at[0, i, :, right], send, recv, to_beside)
        if index == 3:
            return remote(block(chip_beside, i, left), near.at[0, i, :, left], send, recv, to_beside)
        if index == 4:
            return remote(block(chip_across, i, left), near.at[1, i, :, left], send, recv, to_across)
        return remote(block(chip_across, i, right), near.at[1, i, :, right], send, recv, to_across)

    def cross_step(i):
        flow(i, 0).wait_recv()
        add_columns(held.at[chip_beside, span(order[i]), :], [cross.at[i]], 0, cut, 512)
        flow(i, 3).start()
        flow(i, 1).wait_recv()
        add_columns(held.at[chip_across, span(order[i]), :], [cross.at[i]], cut, cols - cut, 384)
        flow(i, 5).start()

    def near_step(i):
        for index in (2, 4, 3, 5):
            flow(i, index).wait_recv()
        add_columns(held.at[chip, span(order[i]), :], [near.at[0, i], near.at[1, i]], 0, cols, 640)

    def line(k, slot, target):
        return remote(
            held.at[chip, span(k), :], lined.at[slot], line_send.at[k], line_recv.at[slot], (s, target)
        )

    def absorb(k, slot, source):
        line(k, slot, source).wait_recv()
        add_columns(held.at[chip, span(k), :], [lined.at[slot]], 0, cols, 640)

    def chain(i):
        k = order[i]
        if i == 3:
            pl.when(z > 0)(lambda: absorb(k, k, z - 1))
            pl.when(z < 3)(lambda: absorb(k, 4, z + 1))
            return

        @pl.when(k > z)
        def _():
            pl.when(z > 0)(lambda: absorb(k, k, z - 1))
            line(k, k, z + 1).start()

        @pl.when(k < z)
        def _():
            pl.when(z < 3)(lambda: absorb(k, k, z + 1))
            pl.when(k == z - 1)(lambda: line(k, 4, z - 1).start())
            pl.when(k < z - 1)(lambda: line(k, k, z - 1).start())

    def chain_drain():
        for i in range(3):
            k = order[i]
            line(k, k, (z + 1) % 4).wait_send()

    def swap(k, high=False):
        to = (z + k) % 4
        here = pl.ds(pl.multiple_of(z * ff_part, 128), ff_part)
        source = (mlp_high if high else mlp_low).at[span(to % 2), :]
        return [
            remote(
                source.at[:, pl.ds(m * ff_part, ff_part)],
                mlp_back.at[m, :, here],
                swap_send.at[k - 1, m],
                swap_recv.at[k - 1, m],
                (s, to),
            )
            for m in range(3)
        ]

    def swap_start(k):
        to = (z + k) % 4

        @pl.when(to < 2)
        def _():
            for copy in swap(k):
                copy.start()

        @pl.when(to >= 2)
        def _():
            for copy in swap(k, True):
                copy.start()

    def own(high=False):
        here = pl.ds(pl.multiple_of(z * ff_part, 128), ff_part)
        source = (mlp_high if high else mlp_low).at[span(z % 2), :]
        return [
            pltpu.make_async_copy(source.at[:, pl.ds(m * ff_part, ff_part)], mlp_back.at[m, :, here], own_sem.at[m])
            for m in range(3)
        ]

    wide_rows = wide_now.shape[1]
    wide_start = mixer_w.shape[1] - wide_now.shape[2] - tokens.shape[1]

    def wide(j):
        source = mixer_w.at[pl.ds(j * wide_rows, wide_rows), pl.ds(wide_start, wide_now.shape[2])]
        return pltpu.make_async_copy(source, wide_now.at[j % 2], wide_sem.at[j % 2])

    plain_loads = [
        pltpu.make_async_copy(source, target, wide_sem.at[2 + n])
        for n, (source, target) in enumerate(
            ((grad_both, both_now), (tokens, tokens_now), (grad_middle, middle_now), (gain, gain_now))
        )
    ]

    def back(first, last):
        for j in range(first, last):
            wide(j).wait()
            back_now[:, pl.ds(j * wide_rows, wide_rows)] = mm(both_now[...], wide_now[j % 2], ((1,), (1,)))
            if (j + 2) * wide_rows < mixer_w.shape[0]:
                wide(j + 2).start()

    def finish_rows(turn, carry):
        rows = pl.ds(pl.multiple_of(turn * 16, 16), 16)
        result = middle_now[rows, :] + norm_back(tokens_now[rows, :].astype(f32), gain_now[0:1, :], back_now[rows, :])
        tokens_now[rows, :] = result.astype(bf16)
        return carry

    for i in range(4):
        for copy in loads(i):
            copy.start()
    greet([(beside, z), (across, z)] + [(s, (z + k) % 4) for k in range(1, 4)])
    for k in (1, 3, 2):
        swap_start(k)

    @pl.when(z < 2)
    def _():
        for copy in own():
            copy.start()

    @pl.when(z >= 2)
    def _():
        for copy in own(True):
            copy.start()

    for i in range(2):
        for copy in loads(i):
            copy.wait()
        flow(i, 0).start()
        flow(i, 1).start()
        if i == 0:
            flow(i, 2).start()
            flow(i, 4).start()
    for i in range(4):
        cross_step(i)
        if i + 1 < 4:
            flow(i + 1, 2).start()
            flow(i + 1, 4).start()
        if i + 2 < 4:
            for copy in loads(i + 2):
                copy.wait()
            flow(i + 2, 0).start()
            flow(i + 2, 1).start()
        if i == 0:
            for copy in plain_loads:
                copy.start()
            wide(0).start()
            wide(1).start()
        if i > 0:
            near_step(i - 1)
            chain(i - 1)
        if i == 1:
            for copy in plain_loads:
                copy.wait()
        if i > 0:
            back(3 * i - 3, 3 * i)
    back(9, mixer_w.shape[0] // wide_rows)
    lax.fori_loop(0, tokens.shape[0] // 16, finish_rows, 0)
    finished = pltpu.make_async_copy(tokens_now, input_grad, wide_sem.at[2])
    finished.start()
    near_step(3)
    chain(3)
    done = pltpu.make_async_copy(held.at[chip, span(z), :], mixer_sum, own_sem.at[3])
    done.start()
    for i in range(4):
        for index in range(6):
            flow(i, index).wait_send()
    chain_drain()
    for k in range(1, 4):
        for copy in swap(k):
            copy.wait()
    for copy in own():
        copy.wait()
    finished.wait()
    done.wait()


def scatter(main, rest, mlp_low, mlp_high, grad_both, mixer_w, tokens, grad_middle, gain):
    rows = main.shape[1] // 4
    cols = main.shape[2] + rest.shape[2]
    ff_part = mlp_low.shape[1] // 3
    tok, model = tokens.shape
    anyspec = pl.BlockSpec(memory_space=pl.ANY)
    dma = pltpu.SemaphoreType.DMA
    return pl.pallas_call(
        scatter_kernel,
        in_specs=[anyspec] * 9,
        out_specs=[anyspec] * 3,
        out_shape=[
            jax.ShapeDtypeStruct((rows, cols), bf16),
            jax.ShapeDtypeStruct((3, rows, 4 * ff_part), bf16),
            jax.ShapeDtypeStruct((tok, model), bf16),
        ],
        scratch_shapes=[
            pltpu.VMEM((4, 4 * rows, cols), bf16),
            pltpu.VMEM((4, rows, cols), bf16),
            pltpu.VMEM((2, 4, rows, cols), bf16),
            pltpu.VMEM((5, rows, cols), bf16),
            pltpu.VMEM(grad_both.shape, bf16),
            pltpu.VMEM((2, 256, grad_both.shape[1]), bf16),
            pltpu.VMEM((tok, model), f32),
            pltpu.VMEM((tok, model), bf16),
            pltpu.VMEM((tok, model), f32),
            pltpu.VMEM((8, model), f32),
            dma((6,)),
            dma((4, 2)), dma((4, 6)), dma((4, 6)), dma((4,)), dma((5,)), dma((3, 3)), dma((3, 3)), dma((4,)),
        ],
        compiler_params=pltpu.CompilerParams(
            collective_id=2, has_side_effects=True, vmem_limit_bytes=62 * 1024 * 1024
        ),
        name="scatter_gradients",
    )(main, rest, mlp_low, mlp_high, grad_both, mixer_w, tokens, grad_middle, gain)


def gather_plain(mixer, gate, up, down):
    groups = lax.axis_size("fsdp")
    part_rows, ff = gate.shape
    own = jnp.stack([w.reshape(part_rows, groups, ff // groups) for w in (gate, up, down)], axis=2)
    mine = lax.all_to_all(jnp.transpose(own, (1, 0, 2, 3)), "fsdp", 0, 0, tiled=True)
    return lax.all_gather(mixer, both, axis=0, tiled=True), mine.reshape(groups * part_rows, -1)


def from_line(shard):
    count = lax.axis_size("fsdp")
    return [shard] + [
        lax.ppermute(shard, "fsdp", [(i, (i + k) % count) for i in range(count)]) for k in range(1, count)
    ]


def swap_cores(shard):
    count = lax.axis_size("seq")
    return lax.ppermute(shard, "seq", [(i, i + 1 - 2 * (i % 2)) for i in range(count)])


def swap_beside(shard):
    return lax.ppermute(shard, "seq", [(i, i ^ 2) for i in range(8)])


def swap_across(shard):
    return lax.ppermute(shard, "seq", [(i, i ^ 4) for i in range(8)])


def add_low(left, right):
    return (left.astype(f32) + right.astype(f32)).astype(bf16)


def scatter_paired(
    normed, grad_both, grad_mix, mixed, rest, mlp_parts, mixer_w, tokens, grad_middle, gain
):
    seq = lax.axis_index("seq")
    core, x, y = seq % 2, (seq // 2) % 2, seq // 4
    main = products(
        [(normed, swap_cores(normed)), (grad_mix, swap_cores(grad_mix))],
        [(0, grad_both, swap_cores(grad_both)), (1, mixed, swap_cores(mixed))],
        (normed.shape[1] // 2,),
        (0, 1, 2, 3),
        tuple(range(8)),
        normed.shape[1] // 2,
        "mixer_products",
    )[0]
    grouped = rest.reshape(4, 2, -1, rest.shape[1])
    own = lax.dynamic_index_in_dim(grouped, core, 1, False)
    other = swap_cores(lax.dynamic_index_in_dim(grouped, 1 - core, 1, False))
    rest = (own.astype(f32) + other.astype(f32)).astype(bf16)
    rest = jnp.concatenate(
        [
            lax.dynamic_slice_in_dim(rest, q, 1, 0)
            for q in ((1 - y) * 2 + 1 - x, y * 2 + 1 - x, (1 - y) * 2 + x, y * 2 + x)
        ],
        axis=0,
    )
    main, rest, mlp_parts = lax.optimization_barrier((main, rest, mlp_parts))
    low, high = [sum(part.astype(f32) for part in parts).astype(bf16) for parts in mlp_parts]
    gain = jnp.broadcast_to(gain[None], (8, gain.shape[0]))
    return scatter(
        main.reshape(4, -1, main.shape[1]), rest, low, high, grad_both, mixer_w, tokens, grad_middle, gain
    )


def scatter_plain(normed, grad_both, grad_mix, mixed, rest, mlp_sum):
    groups = lax.axis_size("fsdp")
    term_wide = mm(normed, grad_both, ((0,), (0,))).astype(bf16)
    term_out = mm(grad_mix, mixed, ((0,), (0,))).astype(bf16)
    mixer_sum = lax.psum_scatter(
        jnp.concatenate([term_wide, term_out, rest], axis=1), "seq", scatter_dimension=0, tiled=True
    )
    mixer_sum = lax.psum_scatter(mixer_sum, "fsdp", scatter_dimension=0, tiled=True)
    ff_part = mlp_sum.shape[1] // 3
    part_rows = mlp_sum.shape[0] // groups
    mlp_sum = mlp_sum.reshape(groups, part_rows, 3, ff_part)
    mlp_back = lax.all_to_all(mlp_sum, "fsdp", 0, 0, tiled=True)
    mlp_back = jnp.transpose(mlp_back, (2, 1, 0, 3)).reshape(3, part_rows, groups * ff_part)
    return mixer_sum, mlp_back


def call_heads(kernel, width, heads, ins, outs, scratch, name):
    def spec(rows_cols):
        rows, by_row = rows_cols
        if by_row:
            return pl.BlockSpec((rows, width), lambda h: (h, 0))
        return pl.BlockSpec((rows, width), lambda h: (0, h))

    in_specs = [spec((width, True)) if rowwise else spec((a.shape[0], False)) for a, rowwise in ins]
    out_specs = [spec((width, True)) if rowwise else spec((rows, False)) for rows, _, rowwise in outs]
    out_shape = [
        jax.ShapeDtypeStruct((heads * width, width) if rowwise else (rows, heads * width), kind)
        for rows, kind, rowwise in outs
    ]
    return pl.pallas_call(
        kernel,
        grid=(heads,),
        in_specs=in_specs,
        out_specs=out_specs,
        out_shape=out_shape,
        scratch_shapes=[pltpu.VMEM((rows, width), f32) for rows in scratch],
        compiler_params=pltpu.CompilerParams(vmem_limit_bytes=40 * 1024 * 1024),
        name=name,
    )(*[a for a, _ in ins])


def on_device(
    block_input,
    cotangent,
    mixer_gain,
    branch_proj,
    gelu_proj,
    conv_taps,
    conv_bias,
    rate_blocks,
    input_blocks,
    rate_bias,
    input_bias,
    decay_param,
    out_proj,
    mlp_gain,
    gate_proj,
    up_proj,
    down_proj,
):
    groups = lax.axis_size("fsdp")
    part_rows, lru = branch_proj.shape
    width = rate_blocks.shape[1]
    heads = lru // width
    margin = conv_taps.shape[0] - 1
    tokens = block_input[0].astype(f32)
    tok_count, model = tokens.shape
    ff = gate_proj.shape[1]
    ff_part = ff // groups
    grad_out = cotangent[0]

    smalls = jnp.stack(
        [conv_taps[k] for k in range(margin + 1)]
        + [conv_bias, rate_bias, input_bias, decay_param, mixer_gain, mlp_gain],
        axis=1,
    )
    small_count = smalls.shape[1]
    smalls = jnp.pad(smalls, ((0, 0), (0, 128 - small_count)))
    first_own = jnp.concatenate([smalls, rate_blocks, input_blocks], axis=1)
    mixer_own = (first_own, branch_proj, gelu_proj, out_proj)
    custom = lax.axis_size("seq") == 8 and groups == 4
    if custom:
        mixer_w, mlp_mine = gather(*mixer_own, gate_proj, up_proj, down_proj)
    else:
        mixer_w, mlp_mine = gather_plain(jnp.concatenate(mixer_own, axis=1), gate_proj, up_proj, down_proj)
    mlp_w = lax.all_gather(mlp_mine, "seq", axis=0, tiled=True)
    grad_out_late = lax.optimization_barrier((grad_out, mlp_mine))[0]
    if custom:
        grad_pieces = from_line(grad_out_late)
    first = lax.optimization_barrier(mixer_w[:, : 128 + 2 * width])
    wide = mixer_w[:, 128 + 2 * width : 128 + 2 * width + 2 * lru]
    proj_out = mixer_w[:, 128 + 2 * width + 2 * lru :]

    table = first[:, :small_count].astype(f32).T
    blocks_rate = first[:, 128 : 128 + width]
    blocks_input = first[:, 128 + width :]
    param_decay = table[margin + 4]
    gain_one = table[margin + 5]
    gain_two = table[margin + 6]
    small = jnp.concatenate(
        [
            table[: margin + 4],
            jax.nn.softplus(-param_decay)[None],
            -jax.nn.sigmoid(-param_decay)[None],
            jnp.zeros((16 - margin - 6, lru), f32),
        ],
        axis=0,
    )

    normed = norm_rows(tokens, gain_one).astype(bf16)
    both_pre = mm(normed, wide, ((1,), (0,)))
    branch = both_pre[:, :lru].astype(bf16)
    gelu_pre = both_pre[:, lru:]
    prior = from_behind(branch[tok_count - margin :], "seq", 1).astype(f32)
    prior = jnp.concatenate([jnp.zeros((8 - margin, lru), f32), prior], axis=0)
    conv, rate_pre, input_pre, cum, local = call_heads(
        mixer_forward,
        width,
        heads,
        [(branch, False), (prior, False), (small, False), (blocks_rate, True), (blocks_input, True)],
        [(tok_count, bf16, False)] + [(tok_count, f32, False)] * 4,
        [tok_count + 8],
        "mixer_forward",
    )
    carried = prefix((cum[-1], local[-1]), "seq", False)
    states = local + cum * carried[None]
    mixed = (states * jax.nn.gelu(gelu_pre, approximate=True)).astype(bf16)
    middle = tokens + mm(mixed, proj_out, ((1,), (1,)))
    normed_two = norm_rows(middle, gain_two).astype(bf16)

    if custom:
        normed_all, normed_other, grad_out_all, grad_out_other = gather_rows(normed_two, grad_pieces)
    else:
        normed_all = lax.all_gather(normed_two, "fsdp", axis=0, tiled=True)
        grad_out_all = lax.all_gather(grad_out_late, "fsdp", axis=0, tiled=True)
    w_gate, w_up, w_down = mlp_w[:, :ff_part], mlp_w[:, ff_part : 2 * ff_part], mlp_w[:, 2 * ff_part :]
    if custom:
        hidden, hidden_other, grad_pair, pair_other, grad_normed_part = feed_forward(
            normed_all, grad_out_all, mlp_w
        )
    else:
        gate = mm(normed_all, w_gate, ((1,), (0,)))
        up_val = mm(normed_all, w_up, ((1,), (0,)))
        gelu_gate, gelu_slope = gelu_parts(gate)
        hidden = (gelu_gate * up_val).astype(bf16)
        grad_hidden = mm(grad_out_all, w_down, ((1,), (0,)))
        grad_gate = (grad_hidden * up_val * gelu_slope).astype(bf16)
        grad_up = (grad_hidden * gelu_gate).astype(bf16)
        grad_normed_part = (
            mm(grad_gate, w_gate, ((1,), (1,))) + mm(grad_up, w_up, ((1,), (1,)))
        ).astype(bf16)
    grad_normed_two = lax.psum_scatter(grad_normed_part, "fsdp", scatter_dimension=0, tiled=True)
    if custom:
        half = model // 16
        lefts = [(normed_all, normed_other), (grad_out_all, grad_out_other)]
        rights = [(0, grad_pair, pair_other), (1, hidden, hidden_other)]
        diag_low, diag_high = products(lefts, rights, (half, half), (0,), (0, 1), ff_part, "diagonal_products")
        from_across, from_beside = swap_across(diag_low), swap_beside(diag_high)
        late = lax.optimization_barrier((grad_pair, diag_low))[0]
        rights = [(0, late, pair_other), (1, hidden, hidden_other)]
        beside_low, beside_high, across_low, across_high, mine = products(
            lefts, rights, (half,) * 4 + (2 * half,), (1, 2, 3), tuple(range(6)), ff_part, "feed_forward_products"
        )
        from_beside_high, from_across_low = swap_beside(beside_high), swap_across(across_low)
        hidden = lax.optimization_barrier((hidden, mine))[0]
        out_part = mm(hidden, w_down, ((1,), (1,))).astype(bf16)
        out_part, grad_normed_two = lax.optimization_barrier((out_part, grad_normed_two))
    else:
        grad_pair = jnp.concatenate([grad_gate, grad_up], axis=1)
        term_pair = mm(normed_all, grad_pair, ((0,), (0,))).astype(bf16)
        term_down = mm(grad_out_all, hidden, ((0,), (0,))).astype(bf16)
        pair_sum = lax.psum_scatter(term_pair, "seq", scatter_dimension=0, tiled=True)
        down_sum = lax.psum_scatter(term_down, "seq", scatter_dimension=0, tiled=True)
        mlp_sum = jnp.concatenate([pair_sum, down_sum], axis=1)
        out_part = mm(hidden, w_down, ((1,), (1,))).astype(bf16)
    out_sum = lax.psum_scatter(out_part, "fsdp", scatter_dimension=0, tiled=True)
    block_output = (middle + out_sum.astype(f32)).astype(bf16)[None]
    grad_normed_two = grad_normed_two.astype(f32)

    grad_middle = grad_out.astype(f32) + norm_back(middle, gain_two, grad_normed_two)
    grad_mix = grad_middle.astype(bf16)
    grad_mixed = mm(grad_mix, proj_out, ((1,), (0,)))
    carried_rows = jnp.broadcast_to(carried[None], (8, lru))
    grad_gelu_pre, rev_cum, rev_grad, pair_grad = call_heads(
        mixer_backward_scan,
        width,
        heads,
        [(a, False) for a in (grad_mixed, gelu_pre, rate_pre, cum, local, carried_rows, small)],
        [(tok_count, bf16, False), (tok_count, f32, False), (tok_count, f32, False), (8, f32, False)],
        [tok_count + 8],
        "mixer_backward_scan",
    )
    incoming = prefix((cum[-1], pair_grad[0]), "seq", True)
    incoming_rows = jnp.broadcast_to(incoming[None], (8, lru))
    own, head, rate_w_grad, input_w_grad, sums = call_heads(
        mixer_backward,
        width,
        heads,
        [
            (a, False)
            for a in (rev_cum, rev_grad, incoming_rows, cum, local, carried_rows, rate_pre, input_pre, conv, branch, prior, small)
        ]
        + [(blocks_rate, True), (blocks_input, True)],
        [(tok_count, f32, False), (8, f32, False), (0, bf16, True), (0, bf16, True), (8, f32, False)],
        [tok_count + 8, tok_count + 16],
        "mixer_backward",
    )
    if custom:
        from_across, from_beside, own = lax.optimization_barrier((from_across, from_beside, own))
        beside_low, across_high = add_low(beside_low, from_across), add_low(across_high, from_beside)
        beside_low, across_high, own = lax.optimization_barrier((beside_low, across_high, own))
        from_beside_low, from_across_high = swap_beside(beside_low), swap_across(across_high)
    received = from_behind(head[8 - margin :], "seq", -1)
    grad_branch = jnp.concatenate(
        [own[: tok_count - margin], own[tok_count - margin :] + received], axis=0
    ).astype(bf16)
    grad_both = jnp.concatenate([grad_branch, grad_gelu_pre], axis=1)
    vectors = jnp.pad(sums.T, ((0, 0), (0, 128 - sums.shape[0]))).astype(bf16)
    rest = jnp.concatenate([rate_w_grad, input_w_grad, vectors], axis=1)
    if custom:
        mlp_parts = (
            (mine[:half], from_across_low, from_beside_low),
            (mine[half:], from_across_high, from_beside_high),
        )
        mixer_sum, mlp_back, input_grad = scatter_paired(
            normed, grad_both, grad_mix, mixed, rest, mlp_parts, mixer_w, block_input[0], grad_middle, gain_one
        )
    else:
        mixer_sum, mlp_back = scatter_plain(normed, grad_both, grad_mix, mixed, rest, mlp_sum)
        grad_normed = mm(grad_both, wide, ((1,), (1,)))
        input_grad = (grad_middle + norm_back(tokens, gain_one, grad_normed)).astype(bf16)
    input_grad = input_grad[None]
    mlp_grads = [mlp_back[m].astype(f32) for m in range(3)]
    mixer_sum = mixer_sum.astype(f32)
    edges = [lru, 2 * lru, 3 * lru, 3 * lru + width, 3 * lru + 2 * width]
    dbranch, dgelu, dout, drate, dinput, vec = jnp.split(mixer_sum, edges, axis=1)
    vec = vec.T
    return (
        block_output,
        input_grad,
        gain_back(mixer_gain, (branch_proj, dbranch), (gelu_proj, dgelu)),
        dbranch,
        dgelu,
        vec[: margin + 1],
        vec[7],
        drate,
        dinput,
        vec[4],
        vec[5],
        vec[6],
        dout,
        gain_back(mlp_gain, (gate_proj, mlp_grads[0]), (up_proj, mlp_grads[1])),
        mlp_grads[0],
        mlp_grads[1],
        mlp_grads[2],
    )


def solution(mesh):
    tokens = P("fsdp", "seq", None)
    vector = P(both)
    matrix = P(both, None)
    taps = P(None, both)
    return jax.shard_map(
        on_device,
        mesh=mesh,
        in_specs=(
            tokens, tokens, vector, matrix, matrix, taps, vector, matrix, matrix,
            vector, vector, vector, matrix, vector, matrix, matrix, matrix,
        ),
        out_specs=(
            tokens, tokens, vector, matrix, matrix, taps, vector, matrix, matrix,
            vector, vector, vector, matrix, vector, matrix, matrix, matrix,
        ),
        check_vma=False,
    )
```

```python
import functools

import jax
import jax.numpy as jnp
from jax import lax
from jax.experimental import pallas as pl
from jax.experimental.pallas import tpu as pltpu
from jax.sharding import PartitionSpec as P

epsilon = 1e-06
f32 = jnp.float32
bf16 = jnp.bfloat16
both = ("seq", "fsdp")
MESH = pl.DeviceIdType.MESH
TAP, CONV_BIAS, RATE_BIAS, INPUT_BIAS, SOFT, SOFT_SLOPE = 0, 4, 5, 6, 7, 8
GELU_C = 0.7978845608028654
GELU_A = 0.044715


def from_behind(shard, axis, by):
    devices = lax.axis_size(axis)
    pairs = [(i, i + by) for i in range(devices) if 0 <= i + by < devices]
    return lax.ppermute(shard, axis, pairs)


def prefix(part, axis, reverse):
    count = lax.axis_size(axis)
    place = lax.axis_index(axis)
    gathered = lax.all_gather(jnp.stack(part), axis)
    state = jnp.zeros_like(part[1])
    for hop in range(count):
        source = count - 1 - hop if reverse else hop
        ahead = source > place if reverse else source < place
        state = jnp.where(ahead, gathered[source, 1] + gathered[source, 0] * state, state)
    return state


def norm_rows(values, scales):
    return values * lax.rsqrt(jnp.mean(values * values, axis=-1, keepdims=True) + epsilon) * scales


def norm_back(values, scales, grads):
    inverse = lax.rsqrt(jnp.mean(values * values, axis=-1, keepdims=True) + epsilon)
    scaled = grads * scales
    shared = jnp.mean(values * scaled, axis=-1, keepdims=True)
    return inverse * scaled - values * (inverse * inverse * inverse * shared)


def gain_back(gain, *pairs):
    total = sum(jnp.sum(weight.astype(f32) * grad, axis=1) for weight, grad in pairs)
    return total / gain.astype(f32)


def gelu_parts(x):
    inner = jnp.tanh(GELU_C * (x + GELU_A * x * x * x))
    return 0.5 * x * (1.0 + inner), 0.5 * (1.0 + inner) + 0.5 * x * (1.0 - inner * inner) * (
        GELU_C * (1.0 + 3.0 * GELU_A * x * x)
    )


def mm(left, right, dims):
    return lax.dot_general(left, right, (dims, ((), ())), preferred_element_type=f32)


def sigmoid(x):
    return 1.0 / (1.0 + jnp.exp(-x))


def scan_rows(decay, value, reverse):
    rows = decay.shape[0]
    place = lax.broadcasted_iota(jnp.int32, decay.shape, 0)
    step = 1
    while step < rows:
        shift = rows - step if reverse else step
        inside = place < rows - step if reverse else place >= step
        before_value = jnp.where(inside, pltpu.roll(value, shift, 0), 0.0)
        before_decay = jnp.where(inside, pltpu.roll(decay, shift, 0), 1.0)
        value = value + decay * before_value
        decay = decay * before_decay
        step *= 2
    return decay, value


def gates(rate_pre, input_pre, soft):
    rate = sigmoid(rate_pre)
    log_decay = -8.0 * rate * soft
    decay = jnp.exp(log_decay)
    square = decay * decay
    root = jnp.sqrt(-jnp.tanh(log_decay) * (1.0 + square))
    return rate, decay, square, root, sigmoid(input_pre)


def mixer_forward(branch, prior, small, rate_w, input_w, conv, rate_pre, input_pre, cum, local, ext):
    rows = branch.shape[0]
    ext[0:8, :] = prior[...]
    ext[8:, :] = branch[...].astype(f32)
    total = small[CONV_BIAS : CONV_BIAS + 1, :] + small[TAP : TAP + 1, :] * ext[8:, :]
    for offset in range(1, 4):
        total = total + small[TAP + offset : TAP + offset + 1, :] * ext[pl.ds(8 - offset, rows), :]
    low = total.astype(bf16)
    conv[...] = low
    rate = mm(low, rate_w[...], ((1,), (0,))) + small[RATE_BIAS : RATE_BIAS + 1, :]
    inp = mm(low, input_w[...], ((1,), (0,))) + small[INPUT_BIAS : INPUT_BIAS + 1, :]
    rate_pre[...] = rate
    input_pre[...] = inp
    _, decay, _, root, opened = gates(rate, inp, small[SOFT : SOFT + 1, :])
    product, states = scan_rows(decay, root * opened * low.astype(f32), False)
    cum[...] = product
    local[...] = states


def mixer_backward_scan(grad_mixed, gelu_pre, rate_pre, cum, local, carried, small, grad_pre, rev_cum, rev_grad, pair, ext):
    rows = grad_mixed.shape[0]
    states = local[...] + cum[...] * carried[0:1, :]
    value, slope = gelu_parts(gelu_pre[...])
    grad = grad_mixed[...]
    grad_pre[...] = (grad * states * slope).astype(bf16)
    decay = jnp.exp(-8.0 * sigmoid(rate_pre[...]) * small[SOFT : SOFT + 1, :])
    ext[0:rows, :] = decay
    ext[rows:, :] = jnp.ones((8, decay.shape[1]), f32)
    product, back = scan_rows(ext[pl.ds(1, rows), :], grad * value, True)
    rev_cum[...] = product
    rev_grad[...] = back
    pair[...] = jnp.broadcast_to(decay[0:1, :] * back[0:1, :], pair.shape)


def mixer_backward(
    rev_cum, rev_grad, incoming, cum, local, carried, rate_pre, input_pre, conv, branch, prior, small, rate_w, input_w,
    own, head, rate_w_grad, input_w_grad, sums, ext, gext,
):
    rows = rev_cum.shape[0]
    soft = small[SOFT : SOFT + 1, :]
    grad_states = rev_grad[...] + rev_cum[...] * incoming[0:1, :]
    rate, decay, square, root, opened = gates(rate_pre[...], input_pre[...], soft)
    ext[0:8, :] = jnp.broadcast_to(carried[0:1, :], (8, carried.shape[1]))
    ext[8:, :] = local[...] + cum[...] * carried[0:1, :]
    before = ext[pl.ds(7, rows), :]
    low = conv[...]
    conv_in = low.astype(f32)
    grad_log = grad_states * decay * before - grad_states * opened * conv_in * square / root
    driven = grad_states * root
    grad_input = (driven * conv_in * opened * (1.0 - opened)).astype(bf16)
    by_rate = grad_log * (-8.0 * rate)
    grad_rate = (by_rate * soft * (1.0 - rate)).astype(bf16)
    sums[6:7, :] = jnp.sum(by_rate, axis=0, keepdims=True) * small[SOFT_SLOPE : SOFT_SLOPE + 1, :]
    sums[4:5, :] = jnp.sum(grad_rate.astype(f32), axis=0, keepdims=True)
    sums[5:6, :] = jnp.sum(grad_input.astype(f32), axis=0, keepdims=True)
    rate_w_grad[...] = mm(low, grad_rate, ((0,), (0,))).astype(rate_w_grad.dtype)
    input_w_grad[...] = mm(low, grad_input, ((0,), (0,))).astype(input_w_grad.dtype)
    grad_conv = (
        driven * opened
        + mm(grad_rate, rate_w[...], ((1,), (1,)))
        + mm(grad_input, input_w[...], ((1,), (1,)))
    )
    sums[7:8, :] = jnp.sum(grad_conv, axis=0, keepdims=True)
    ext[0:8, :] = prior[...]
    ext[8:, :] = branch[...].astype(f32)
    gext[0:8, :] = jnp.zeros((8, grad_conv.shape[1]), f32)
    gext[8 : 8 + rows, :] = grad_conv
    gext[8 + rows :, :] = jnp.zeros((8, grad_conv.shape[1]), f32)
    back = jnp.zeros_like(grad_conv)
    front = jnp.zeros((8, grad_conv.shape[1]), f32)
    for offset in range(4):
        tap = small[TAP + offset : TAP + offset + 1, :]
        sums[offset : offset + 1, :] = jnp.sum(
            grad_conv * ext[pl.ds(8 - offset, rows), :], axis=0, keepdims=True
        )
        back = back + tap * gext[pl.ds(8 + offset, rows), :]
        front = front + tap * gext[pl.ds(offset, 8), :]
    own[...] = back
    head[...] = front


def places():
    s = lax.axis_index("seq")
    z = lax.axis_index("fsdp")
    core = s + 1 - 2 * (s % 2)
    beside = s + 2 - 4 * ((s // 2) % 2)
    across = s + 4 - 8 * (s // 4)
    return s, z, core, beside, across


def greet(peers):
    barrier = pltpu.get_barrier_semaphore()
    for peer in peers:
        pl.semaphore_signal(barrier, inc=1, device_id=peer, device_id_type=MESH)
    pl.semaphore_wait(barrier, len(peers))


def gather_kernel(
    first, branch, gelu, outer, gate, up, down, mixer_all, mlp_mine,
    mixer, load_sem, flow_send, flow_recv, line_send, line_recv, swap_send, swap_recv, own_sem,
):
    s, z, core, beside, across = places()
    rows, cols = mixer.shape
    ff_part = mlp_mine.shape[1] // 3
    cut = cols // 256 * 128
    diag = beside + across - s
    loads, start = [], 0
    for n, part in enumerate((first, branch, gelu, outer)):
        size = part.shape[1]
        loads.append(pltpu.make_async_copy(part, mixer.at[:, pl.ds(start, size)], load_sem.at[n]))
        loads[-1].start()
        start += size
    greet([(core, z), (beside, z), (across, z)] + [(s, (z + k) % 4) for k in range(1, 4)])

    def remote(src, dst, send, recv, target):
        return pltpu.make_async_remote_copy(
            src_ref=src, dst_ref=dst, send_sem=send, recv_sem=recv, device_id=target, device_id_type=MESH
        )

    def piece(seq, zz, half=None):
        span = pl.ds(pl.multiple_of((seq * 4 + zz) * rows, 16), rows)
        if half is None:
            return mixer_all.at[span, :]
        return mixer_all.at[span, pl.ds(0, cut) if half == 0 else pl.ds(cut, cols - cut)]

    def flow(zz, index, seq, half, target, src=None):
        ref = piece(seq, zz, half)
        return remote(
            ref if src is None else src, ref, flow_send.at[zz, index], flow_recv.at[zz, index], (target, z)
        )

    def sends(zz, src=None):
        return [
            flow(zz, 0, s, None, beside, src),
            flow(zz, 1, s, None, across, src),
            flow(zz, 4, s, None, core, src),
        ]

    def spread(zz, src=None):
        for copy in sends(zz, src):
            copy.start()

    def relay(zz):
        flow(zz, 0, beside, None, beside).wait_recv()
        flow(zz, 3, beside, 0, across).start()
        flow(zz, 5, beside, None, core).start()
        flow(zz, 1, across, None, across).wait_recv()
        flow(zz, 2, across, 1, beside).start()
        flow(zz, 6, across, None, core).start()

    def finish(zz):
        flow(zz, 3, diag, 0, across).wait_recv()
        flow(zz, 7, diag, 0, core).start()
        flow(zz, 2, diag, 1, beside).wait_recv()
        flow(zz, 8, diag, 1, core).start()

    def drain(zz, src=None):
        for copy in sends(zz, src):
            copy.wait_send()
        flow(zz, 3, beside, 0, across).wait_send()
        flow(zz, 5, beside, None, core).wait_send()
        flow(zz, 2, across, 1, beside).wait_send()
        flow(zz, 6, across, None, core).wait_send()
        flow(zz, 7, diag, 0, core).wait_send()
        flow(zz, 8, diag, 1, core).wait_send()
        flip = core - s
        flow(zz, 4, core, None, core).wait_recv()
        flow(zz, 5, beside + flip, None, core).wait_recv()
        flow(zz, 6, across + flip, None, core).wait_recv()
        flow(zz, 7, diag + flip, 0, core).wait_recv()
        flow(zz, 8, diag + flip, 1, core).wait_recv()

    def line(zz, up_way, hop, src=None):
        ref = piece(s, zz)
        way = 0 if up_way else 1
        target = z + 1 if up_way else z - 1
        return remote(
            ref if src is None else src, ref, line_send.at[way, hop], line_recv.at[way, hop], (s, target)
        )

    def line_hop(hop):
        def below():
            line(z - hop, True, hop - 1).wait_recv()
            pl.when(z < 3)(lambda: line(z - hop, True, hop).start())

        def above():
            line(z + hop, False, hop - 1).wait_recv()
            pl.when(z > 0)(lambda: line(z + hop, False, hop).start())

        pl.when(z >= hop)(below)
        pl.when(z + hop <= 3)(above)

    def at_hop(hop, act):
        pl.when(z >= hop)(lambda: act(z - hop))
        pl.when(z + hop <= 3)(lambda: act(z + hop))

    def landing(m, zz):
        return mlp_mine.at[pl.ds(pl.multiple_of(zz * rows, 16), rows), pl.ds(m * ff_part, ff_part)]

    def columns(m, zz):
        return (gate, up, down)[m].at[:, pl.ds(pl.multiple_of(zz * ff_part, 128), ff_part)]

    def swap(k, m, arriving=False):
        to = (z + k) % 4
        came = (z + 4 - k) % 4
        return remote(
            columns(m, to), landing(m, came if arriving else z), swap_send.at[k - 1, m], swap_recv.at[k - 1, m], (s, to)
        )

    local = [pltpu.make_async_copy(columns(m, z), landing(m, z), own_sem.at[m]) for m in range(3)]
    local.append(pltpu.make_async_copy(mixer, piece(s, z), own_sem.at[3]))
    for copy in loads:
        copy.wait()

    pl.when(z < 3)(lambda: line(z, True, 0, mixer).start())
    pl.when(z > 0)(lambda: line(z, False, 0, mixer).start())
    spread(z, mixer)
    for copy in local:
        copy.start()
    line_hop(1)
    at_hop(1, spread)
    relay(z)
    line_hop(2)
    at_hop(2, spread)
    finish(z)
    at_hop(1, relay)
    line_hop(3)
    at_hop(3, spread)
    for k in (1, 3, 2):
        for m in range(3):
            swap(k, m).start()
    at_hop(1, finish)
    at_hop(2, relay)
    at_hop(3, relay)
    at_hop(2, finish)
    at_hop(3, finish)
    drain(z, mixer)
    for hop in range(1, 4):
        at_hop(hop, drain)
    for copy in local:
        copy.wait()
    for k in (1, 3, 2):
        for m in range(3):
            swap(k, m).wait_send()
            swap(k, m, True).wait_recv()
    pl.when(z < 3)(lambda: line(z, True, 0, mixer).wait_send())
    pl.when(z > 0)(lambda: line(z, False, 0, mixer).wait_send())
    for hop in range(1, 3):
        pl.when((z >= hop) & (z < 3))(lambda: line(z - hop, True, hop).wait_send())
        pl.when((z + hop <= 3) & (z > 0))(lambda: line(z + hop, False, hop).wait_send())


def gather(first, branch, gelu, outer, gate, up, down):
    rows = first.shape[0]
    cols = first.shape[1] + branch.shape[1] + gelu.shape[1] + outer.shape[1]
    ff_part = gate.shape[1] // 4
    anyspec = pl.BlockSpec(memory_space=pl.ANY)
    dma = pltpu.SemaphoreType.DMA
    return pl.pallas_call(
        gather_kernel,
        in_specs=[anyspec] * 7,
        out_specs=[anyspec] * 2,
        out_shape=[
            jax.ShapeDtypeStruct((32 * rows, cols), bf16),
            jax.ShapeDtypeStruct((4 * rows, 3 * ff_part), bf16),
        ],
        scratch_shapes=[
            pltpu.VMEM((rows, cols), bf16), dma((4,)),
            dma((4, 9)), dma((4, 9)), dma((2, 3)), dma((2, 3)), dma((3, 3)), dma((3, 3)), dma((4,)),
        ],
        compiler_params=pltpu.CompilerParams(collective_id=1, has_side_effects=True),
        name="gather_weights",
    )(first, branch, gelu, outer, gate, up, down)


def rows_kernel(
    normed, grad0, grad1, grad2, grad3, normed_all, normed_other, grad_all, grad_other,
    line_send, line_recv, core_send, core_recv, own_sem, held,
):
    s, z, core, _, _ = places()
    tok = normed.shape[0]
    cuts = 4
    grads = (grad0, grad1, grad2, grad3)
    greet([(core, z)] + [(s, (z + k) % 4) for k in range(1, 4)])

    def rows(ref, zz):
        return ref.at[pl.ds(pl.multiple_of(zz * tok, 16), tok), :]

    def remote(src, dst, send, recv, target):
        return pltpu.make_async_remote_copy(
            src_ref=src, dst_ref=dst, send_sem=send, recv_sem=recv, device_id=target, device_id_type=MESH
        )

    def parts(ref):
        size = tok // cuts
        return [ref.at[pl.ds(n * size, size), :] for n in range(cuts)]

    def line(zz, up_way, hop):
        way = 0 if up_way else 1
        target = z + 1 if up_way else z - 1
        src = normed if hop == 0 else rows(normed_all, zz)
        dst = rows(normed_all, zz)
        return [
            remote(a, b, line_send.at[way, hop, n], line_recv.at[way, hop, n], (s, target))
            for n, (a, b) in enumerate(zip(parts(src), parts(dst)))
        ]

    def over(zz, own=False):
        src = normed if own else rows(normed_all, zz)
        return remote(src, rows(normed_other, zz), core_send.at[0, zz], core_recv.at[0, zz], (core, z))

    def grad_over(k):
        zz = (z + 4 - k) % 4
        return remote(grads[k], rows(grad_other, zz), core_send.at[1, zz], core_recv.at[1, zz], (core, z))

    def line_start(zz, up_way, hop):
        for copy in line(zz, up_way, hop):
            copy.start()

    def line_drain(zz, up_way, hop):
        for copy in line(zz, up_way, hop):
            copy.wait_send()

    def hop_step(hop):
        def below():
            for came, on in zip(line(z - hop, True, hop - 1), line(z - hop, True, hop) if hop < 3 else [None] * cuts):
                came.wait_recv()
                if on is not None:
                    pl.when(z < 3)(on.start)
            over(z - hop).start()

        def above():
            for came, on in zip(line(z + hop, False, hop - 1), line(z + hop, False, hop) if hop < 3 else [None] * cuts):
                came.wait_recv()
                if on is not None:
                    pl.when(z > 0)(on.start)
            over(z + hop).start()

        pl.when(z >= hop)(below)
        pl.when(z + hop <= 3)(above)

    local = [pltpu.make_async_copy(grads[k], held.at[k], own_sem.at[k]) for k in range(4)]
    local.append(pltpu.make_async_copy(normed, held.at[4], own_sem.at[4]))
    stored = [
        pltpu.make_async_copy(held.at[k], rows(grad_all, (z + 4 - k) % 4), own_sem.at[k]) for k in range(4)
    ]
    stored.append(pltpu.make_async_copy(held.at[4], rows(normed_all, z), own_sem.at[4]))
    pl.when(z < 3)(lambda: line_start(z, True, 0))
    pl.when(z > 0)(lambda: line_start(z, False, 0))
    over(z, True).start()
    for copy in local:
        copy.start()
    for k in range(4):
        grad_over(k).start()
    for copy, store in zip(local, stored):
        copy.wait()
        store.start()
    for hop in range(1, 4):
        hop_step(hop)
    for copy in stored:
        copy.wait()
    for k in range(4):
        grad_over(k).wait()
    over(z, True).wait()
    for k in range(1, 4):
        over((z + k) % 4).wait()
    pl.when(z < 3)(lambda: line_drain(z, True, 0))
    pl.when(z > 0)(lambda: line_drain(z, False, 0))
    for hop in range(1, 3):
        pl.when((z >= hop) & (z < 3))(lambda: line_drain(z - hop, True, hop))
        pl.when((z + hop <= 3) & (z > 0))(lambda: line_drain(z + hop, False, hop))


def gather_rows(normed, grads):
    tok, model = normed.shape
    anyspec = pl.BlockSpec(memory_space=pl.ANY)
    dma = pltpu.SemaphoreType.DMA
    return pl.pallas_call(
        rows_kernel,
        in_specs=[anyspec] * 5,
        out_specs=[anyspec] * 4,
        out_shape=[jax.ShapeDtypeStruct((4 * tok, model), bf16)] * 4,
        scratch_shapes=[dma((2, 3, 4)), dma((2, 3, 4)), dma((2, 4)), dma((2, 4)), dma((5,)), pltpu.VMEM((5, tok, model), bf16)],
        compiler_params=pltpu.CompilerParams(collective_id=3, has_side_effects=True),
        name="gather_rows",
    )(normed, *grads)


def column_tiles(cols, size=512):
    return [(start, min(size, cols - start)) for start in range(0, cols, size)]


def feed_forward_kernel(
    normed, grad_out, weights, hidden, hidden_other, pair, pair_other, back,
    held, hidden_now, pair_now, sems, store_sem, core_send, core_recv,
):
    s, z, core, _, _ = places()
    step = pl.program_id(0)
    ff_part = held.shape[2]
    model = held.shape[1]
    rows = normed.shape[0]
    tiles = column_tiles(ff_part)
    made = ((hidden_now, hidden, hidden_other), (pair_now, pair, pair_other))

    def load(n, m):
        start, size = tiles[n]
        return pltpu.make_async_copy(
            weights.at[:, pl.ds(m * ff_part + start, size)], held.at[m, :, pl.ds(start, size)], sems.at[n, m]
        )

    def kept(n, turn):
        now, mine, _ = made[n]
        return pltpu.make_async_copy(now.at[turn], mine.at[pl.ds(turn * rows, rows), :], store_sem.at[turn, n])

    def handed(n, turn):
        now, _, other = made[n]
        return pltpu.make_async_remote_copy(
            src_ref=now.at[turn],
            dst_ref=other.at[pl.ds(turn * rows, rows), :],
            send_sem=core_send.at[turn, n],
            recv_sem=core_recv.at[turn, n],
            device_id=(core, z),
            device_id_type=MESH,
        )

    @pl.when(step == 0)
    def _():
        for n in range(len(tiles)):
            for m in range(3):
                load(n, m).start()
        greet([(core, z)])

    for n, (start, size) in enumerate(tiles):
        cols = slice(start, start + size)

        @pl.when(step == 0)
        def _(n=n):
            for m in range(3):
                load(n, m).wait()

        gate = mm(normed[...], held[0, :, cols], ((1,), (0,)))
        value, slope = gelu_parts(gate)
        up = mm(normed[...], held[1, :, cols], ((1,), (0,)))
        hidden_now[step, :, cols] = (value * up).astype(bf16)
        grad_hidden = mm(grad_out[...], held[2, :, cols], ((1,), (0,)))
        pair_now[step, :, cols] = (grad_hidden * up * slope).astype(bf16)
        pair_now[step, :, slice(ff_part + start, ff_part + start + size)] = (grad_hidden * value).astype(bf16)

    for turn in range(2):

        @pl.when(step == turn)
        def _(turn=turn):
            for n in range(2):
                handed(n, turn).start()
                kept(n, turn).start()

    def back_tile(turn, carry):
        cols = pl.ds(pl.multiple_of(turn * 512, 512), 512)
        total = mm(pair_now[step, :, :ff_part], held[0, cols, :], ((1,), (1,)))
        total = total + mm(pair_now[step, :, ff_part:], held[1, cols, :], ((1,), (1,)))
        back[:, cols] = total.astype(bf16)
        return carry

    lax.fori_loop(0, model // 512, back_tile, 0)

    @pl.when(step == 1)
    def _():
        for turn in range(2):
            for n in range(2):
                kept(n, turn).wait()
                handed(n, turn).wait()


def feed_forward(normed, grad_out, weights):
    tok, model = normed.shape
    ff_part = weights.shape[1] // 3
    rows = tok // 2
    anyspec = pl.BlockSpec(memory_space=pl.ANY)
    dma = pltpu.SemaphoreType.DMA
    block = pl.BlockSpec((rows, model), lambda i: (i, 0))
    return pl.pallas_call(
        feed_forward_kernel,
        grid=(2,),
        in_specs=[block, block, anyspec],
        out_specs=[anyspec] * 4 + [block],
        out_shape=[
            jax.ShapeDtypeStruct((tok, cols), bf16)
            for cols in (ff_part, ff_part, 2 * ff_part, 2 * ff_part, model)
        ],
        scratch_shapes=[
            pltpu.VMEM((3, model, ff_part), bf16),
            pltpu.VMEM((2, rows, ff_part), bf16),
            pltpu.VMEM((2, rows, 2 * ff_part), bf16),
            dma((len(column_tiles(ff_part)), 3)), dma((2, 2)), dma((2, 2)), dma((2, 2)),
        ],
        compiler_params=pltpu.CompilerParams(
            collective_id=4, has_side_effects=True, vmem_limit_bytes=60 * 1024 * 1024
        ),
        name="feed_forward",
    )(normed, grad_out, weights)


def products_kernel(sides, cuts, chips, spots, place, *refs):
    lefts = 1 + max(side for side, _ in sides)
    left_refs = refs[: 2 * lefts]
    right_refs = refs[2 * lefts : 2 * lefts + 2 * len(sides)]
    outs = refs[2 * lefts + 2 * len(sides) : -4]
    turned, slots, stage, sems = refs[-4:]
    tok = left_refs[0].shape[0]
    chip_cols = left_refs[0].shape[1] // 4
    half = chip_cols // 2
    step = pl.program_id(0)

    def load(side, q, who):
        cols = pl.ds(pl.multiple_of(place[chips[q]] * chip_cols, 128), chip_cols)
        return pltpu.make_async_copy(
            left_refs[2 * side + who].at[:, cols], slots.at[q % 2, who], sems.at[q % 2, who]
        )

    def fetch(side):
        for q in range(min(2, len(chips))):
            for who in range(2):
                load(side, q, who).start()

    def turn(side):
        piece = half // 2
        for q in range(len(chips)):
            for who in range(2):
                load(side, q, who).wait()
                stage[...] = slots[q % 2, who].T
                for part in range(2):
                    spot = spots[2 * q + part] * piece
                    turned[who, spot : spot + piece, :] = stage[
                        pl.ds(pl.multiple_of(place[4] * half + part * piece, 16), piece), :
                    ]
                if q + 2 < len(chips):
                    load(side, q + 2, who).start()

    def multiply(own, other):
        def tile(cols):
            block = mm(turned[0], own[:, cols], ((1,), (0,)))
            block = (block + mm(turned[1], other[:, cols], ((1,), (0,)))).astype(bf16)
            start = 0
            for out, size in zip(outs, cuts):
                out[:, cols] = block[start : start + size]
                start += size

        width = own.shape[1]

        def one(turn, carry):
            tile(pl.ds(pl.multiple_of(turn * 512, 512), 512))
            return carry

        lax.fori_loop(0, width // 512, one, 0)
        if width % 512:
            tile(slice(width // 512 * 512, width))

    first = 0
    before = None
    for n, (side, blocks) in enumerate(sides):
        if side != before:
            if first == 0:
                pl.when(step == 0)(functools.partial(fetch, side))
            pl.when(step == first)(functools.partial(turn, side))
        before = side
        inside = (step >= first) & (step < first + blocks)
        pl.when(inside)(functools.partial(multiply, right_refs[2 * n], right_refs[2 * n + 1]))
        first += blocks
        if n + 1 < len(sides) and sides[n + 1][0] != side:
            pl.when(step == first - 1)(functools.partial(fetch, sides[n + 1][0]))


def products(lefts, rights, cuts, chips, spots, width, name):
    seq = lax.axis_index("seq")
    core, x, y = seq % 2, (seq // 2) % 2, seq // 4
    place = jnp.stack([(1 - y) * 2 + 1 - x, y * 2 + 1 - x, (1 - y) * 2 + x, y * 2 + x, core]).astype(jnp.int32)
    tok, model = lefts[0][0].shape
    sides = tuple((side, own.shape[1] // width) for side, own, _ in rights)
    total = sum(blocks for _, blocks in sides)
    in_specs = [pl.BlockSpec(memory_space=pl.ANY)] * (2 * len(lefts))
    first = 0
    for _, blocks in sides:

        def index(j, place, first=first, blocks=blocks):
            return (0, jnp.clip(j - first, 0, blocks - 1))

        in_specs += [pl.BlockSpec((tok, width), index)] * 2
        first += blocks
    half = model // 8
    return pl.pallas_call(
        functools.partial(products_kernel, sides, cuts, chips, spots),
        grid_spec=pltpu.PrefetchScalarGridSpec(
            num_scalar_prefetch=1,
            grid=(total,),
            in_specs=in_specs,
            out_specs=[pl.BlockSpec((rows, width), lambda j, place: (0, j)) for rows in cuts],
            scratch_shapes=[
                pltpu.VMEM((2, len(chips) * half, tok), bf16),
                pltpu.VMEM((2, 2, tok, 2 * half), bf16),
                pltpu.VMEM((2 * half, tok), bf16),
                pltpu.SemaphoreType.DMA((2, 2)),
            ],
        ),
        out_shape=[jax.ShapeDtypeStruct((rows, total * width), bf16) for rows in cuts],
        compiler_params=pltpu.CompilerParams(vmem_limit_bytes=58 * 1024 * 1024),
        cost_estimate=pl.CostEstimate(flops=1, bytes_accessed=1, transcendentals=0),
        name=name,
    )(place, *[a for pair in lefts for a in pair], *[a for _, own, other in rights for a in (own, other)])


def add_columns(target, sources, start, size, step):
    def one(turn, carry):
        cols = pl.ds(pl.multiple_of(start + turn * step, 128), step)
        total = target[:, cols].astype(f32)
        for source in sources:
            total = total + source[:, cols].astype(f32)
        target[:, cols] = total.astype(target.dtype)
        return carry

    lax.fori_loop(0, size // step, one, 0)


def shared_products_kernel(
    normed, normed_other, grad, grad_other, pair, pair_other, hidden, hidden_other,
    beside_high, across_low, mine, beside_low, across_high,
    turned, slots, stage, diag, landed, waiting, load_sem, send_sem, recv_sem, store_sem,
):
    s, z, _, beside, across = places()
    step = pl.program_id(0)
    lefts = ((normed, normed_other), (grad, grad_other))
    chip_cols = normed.shape[1] // 4
    half = chip_cols // 2
    piece = half // 2
    width = pair.shape[1]
    diagonal = beside + across - s
    chips = [q // 2 for q in (diagonal, beside, across, s)]

    def load(side, q, who):
        cols = pl.ds(pl.multiple_of(chips[q] * chip_cols, 128), chip_cols)
        return pltpu.make_async_copy(lefts[side][who].at[:, cols], slots.at[q % 2, who], load_sem.at[q % 2, who])

    def fetch(side):
        for q in range(2):
            for who in range(2):
                load(side, q, who).start()

    def turn(side):
        for q in range(4):
            for who in range(2):
                load(side, q, who).wait()
                stage[...] = slots[q % 2, who].T
                turned[who, q * half : (q + 1) * half, :] = stage[
                    pl.ds(pl.multiple_of(s % 2 * half, 16), half), :
                ]
                if q < 2:
                    load(side, q + 2, who).start()

    def tile(own, other, start, size):
        cols = pl.ds(start, size)
        block = mm(turned[0], own[:, cols], ((1,), (0,)))
        block = (block + mm(turned[1], other[:, cols], ((1,), (0,)))).astype(bf16)
        parts = [block[n * piece : (n + 1) * piece] for n in range(8)]
        there = pl.ds(pl.multiple_of(step * width + start, 128), size)
        diag[0, :, there] = parts[0]
        diag[1, :, there] = parts[1]
        waiting[0, :, there] = parts[2]
        beside_high[:, cols] = parts[3]
        across_low[:, cols] = parts[4]
        waiting[1, :, there] = parts[5]
        mine[0:piece, cols] = parts[6]
        mine[piece:, cols] = parts[7]

    def multiply(own, other):
        def one(turn, carry):
            tile(own, other, pl.multiple_of(turn * 512, 512), 512)
            return carry

        lax.fori_loop(0, width // 512, one, 0)
        if width % 512:
            tile(own, other, width // 512 * 512, width % 512)

    def push(way, j):
        cols = pl.ds(j * width, width)
        return pltpu.make_async_remote_copy(
            src_ref=diag.at[way, :, cols],
            dst_ref=landed.at[way, :, cols],
            send_sem=send_sem.at[way, j],
            recv_sem=recv_sem.at[way, j],
            device_id=(across if way == 0 else beside, z),
            device_id_type=MESH,
        )

    def store(way, j):
        cols = pl.ds(j * width, width)
        return pltpu.make_async_copy(
            waiting.at[way, :, cols], (beside_low, across_high)[way].at[:, cols], store_sem.at[way, j]
        )

    @pl.when(step == 0)
    def _():
        fetch(0)
        greet([(beside, z), (across, z)])
        turn(0)

    pl.when(step == 2)(functools.partial(turn, 1))
    pl.when(step < 2)(functools.partial(multiply, pair, pair_other))
    pl.when(step == 1)(functools.partial(fetch, 1))
    pl.when(step == 2)(functools.partial(multiply, hidden, hidden_other))
    for j in range(3):

        @pl.when(step == j)
        def _(j=j):
            push(0, j).start()
            push(1, j).start()

    @pl.when(step == 2)
    def _():
        for j in range(3):
            for way in range(2):
                push(way, j).wait_recv()
                add_columns(waiting.at[way], [landed.at[way]], j * width, width, 384)
                store(way, j).start()
        for j in range(3):
            for way in range(2):
                push(way, j).wait_send()
                store(way, j).wait()


def shared_products(lefts, pair, hidden):
    tok, model = lefts[0].shape
    width = hidden[0].shape[1]
    half = model // 8
    anyspec = pl.BlockSpec(memory_space=pl.ANY)
    dma = pltpu.SemaphoreType.DMA

    def block(rows):
        return pl.BlockSpec((rows, width), lambda j: (0, j))

    pair_spec = pl.BlockSpec((tok, width), lambda j: (0, jnp.minimum(j, 1)))
    hidden_spec = pl.BlockSpec((tok, width), lambda j: (0, 0))
    rows_out = (half // 2, half // 2, half, half // 2, half // 2)
    return pl.pallas_call(
        shared_products_kernel,
        grid=(3,),
        in_specs=[anyspec] * 4 + [pair_spec] * 2 + [hidden_spec] * 2,
        out_specs=[block(rows) for rows in rows_out[:3]] + [anyspec] * 2,
        out_shape=[jax.ShapeDtypeStruct((rows, 3 * width), bf16) for rows in rows_out],
        scratch_shapes=[
            pltpu.VMEM((2, 4 * half, tok), bf16),
            pltpu.VMEM((2, 2, tok, 2 * half), bf16),
            pltpu.VMEM((2 * half, tok), bf16),
            pltpu.VMEM((2, half // 2, 3 * width), bf16),
            pltpu.VMEM((2, half // 2, 3 * width), bf16),
            pltpu.VMEM((2, half // 2, 3 * width), bf16),
            dma((2, 2)), dma((2, 3)), dma((2, 3)), dma((2, 3)),
        ],
        compiler_params=pltpu.CompilerParams(
            collective_id=5, has_side_effects=True, vmem_limit_bytes=60 * 1024 * 1024
        ),
        name="feed_forward_products",
    )(*lefts, *pair, *hidden)


def scatter_kernel(
    main, rest, mlp_low, mlp_high, grad_both, mixer_w, tokens, grad_middle, gain, mixer_sum, mlp_back, input_grad,
    held, cross, near, lined, both_now, wide_now, back_now, tokens_now, middle_now, gain_now, wide_sem,
    load_sem, flow_send, flow_recv, line_send, line_recv, swap_send, swap_recv, own_sem,
):
    s, z, _, beside, across = places()
    chip_diag, chip_beside, chip_across, chip = 0, 1, 2, 3
    rows = held.shape[1] // 4
    cols = held.shape[2]
    cut = cols // 256 * 128
    ff_part = mlp_low.shape[1] // 3
    parts = (main, rest)
    order = (3 * (1 - z // 2), (2 + 3 * z) % 5, 1 + z % 2, z)

    def remote(src, dst, send, recv, target):
        return pltpu.make_async_remote_copy(
            src_ref=src, dst_ref=dst, send_sem=send, recv_sem=recv, device_id=target, device_id_type=MESH
        )

    def span(k):
        return pl.ds(pl.multiple_of(k * rows, 16), rows)

    def loads(i):
        copies, start = [], 0
        for n, part in enumerate(parts):
            size = part.shape[2]
            copies.append(
                pltpu.make_async_copy(
                    part.at[:, span(order[i]), :], held.at[:, span(order[i]), pl.ds(start, size)], load_sem.at[i, n]
                )
            )
            start += size
        return copies

    left, right = pl.ds(0, cut), pl.ds(cut, cols - cut)

    def block(q, i, side):
        return held.at[q, span(order[i]), side]

    def flow(i, index):
        send, recv = flow_send.at[i, index], flow_recv.at[i, index]
        to_beside, to_across = (beside, z), (across, z)
        if index == 0:
            return remote(block(chip_diag, i, left), cross.at[i, :, left], send, recv, to_across)
        if index == 1:
            return remote(block(chip_diag, i, right), cross.at[i, :, right], send, recv, to_beside)
        if index == 2:
            return remote(block(chip_beside, i, right), near.at[0, i, :, right], send, recv, to_beside)
        if index == 3:
            return remote(block(chip_beside, i, left), near.at[0, i, :, left], send, recv, to_beside)
        if index == 4:
            return remote(block(chip_across, i, left), near.at[1, i, :, left], send, recv, to_across)
        return remote(block(chip_across, i, right), near.at[1, i, :, right], send, recv, to_across)

    def cross_step(i):
        flow(i, 0).wait_recv()
        add_columns(held.at[chip_beside, span(order[i]), :], [cross.at[i]], 0, cut, 512)
        flow(i, 3).start()
        flow(i, 1).wait_recv()
        add_columns(held.at[chip_across, span(order[i]), :], [cross.at[i]], cut, cols - cut, 384)
        flow(i, 5).start()

    def near_step(i):
        for index in (2, 4, 3, 5):
            flow(i, index).wait_recv()
        add_columns(held.at[chip, span(order[i]), :], [near.at[0, i], near.at[1, i]], 0, cols, 640)

    def line(k, slot, target):
        return remote(
            held.at[chip, span(k), :], lined.at[slot], line_send.at[k], line_recv.at[slot], (s, target)
        )

    def absorb(k, slot, source):
        line(k, slot, source).wait_recv()
        add_columns(held.at[chip, span(k), :], [lined.at[slot]], 0, cols, 640)

    def chain(i):
        k = order[i]
        if i == 3:
            pl.when(z > 0)(lambda: absorb(k, k, z - 1))
            pl.when(z < 3)(lambda: absorb(k, 4, z + 1))
            return

        @pl.when(k > z)
        def _():
            pl.when(z > 0)(lambda: absorb(k, k, z - 1))
            line(k, k, z + 1).start()

        @pl.when(k < z)
        def _():
            pl.when(z < 3)(lambda: absorb(k, k, z + 1))
            pl.when(k == z - 1)(lambda: line(k, 4, z - 1).start())
            pl.when(k < z - 1)(lambda: line(k, k, z - 1).start())

    def chain_drain():
        for i in range(3):
            k = order[i]
            line(k, k, (z + 1) % 4).wait_send()

    def swap(k, high=False):
        to = (z + k) % 4
        here = pl.ds(pl.multiple_of(z * ff_part, 128), ff_part)
        source = (mlp_high if high else mlp_low).at[span(to % 2), :]
        return [
            remote(
                source.at[:, pl.ds(m * ff_part, ff_part)],
                mlp_back.at[m, :, here],
                swap_send.at[k - 1, m],
                swap_recv.at[k - 1, m],
                (s, to),
            )
            for m in range(3)
        ]

    def swap_start(k):
        to = (z + k) % 4

        @pl.when(to < 2)
        def _():
            for copy in swap(k):
                copy.start()

        @pl.when(to >= 2)
        def _():
            for copy in swap(k, True):
                copy.start()

    def own(high=False):
        here = pl.ds(pl.multiple_of(z * ff_part, 128), ff_part)
        source = (mlp_high if high else mlp_low).at[span(z % 2), :]
        return [
            pltpu.make_async_copy(source.at[:, pl.ds(m * ff_part, ff_part)], mlp_back.at[m, :, here], own_sem.at[m])
            for m in range(3)
        ]

    wide_rows = wide_now.shape[1]
    wide_start = mixer_w.shape[1] - wide_now.shape[2] - tokens.shape[1]

    def wide(j):
        source = mixer_w.at[pl.ds(j * wide_rows, wide_rows), pl.ds(wide_start, wide_now.shape[2])]
        return pltpu.make_async_copy(source, wide_now.at[j % 2], wide_sem.at[j % 2])

    plain_loads = [
        pltpu.make_async_copy(source, target, wide_sem.at[2 + n])
        for n, (source, target) in enumerate(
            ((grad_both, both_now), (tokens, tokens_now), (grad_middle, middle_now), (gain, gain_now))
        )
    ]

    def back(first, last):
        for j in range(first, last):
            wide(j).wait()
            back_now[:, pl.ds(j * wide_rows, wide_rows)] = mm(both_now[...], wide_now[j % 2], ((1,), (1,)))
            if (j + 2) * wide_rows < mixer_w.shape[0]:
                wide(j + 2).start()

    def finish_rows(turn, carry):
        rows = pl.ds(pl.multiple_of(turn * 16, 16), 16)
        result = middle_now[rows, :] + norm_back(tokens_now[rows, :].astype(f32), gain_now[0:1, :], back_now[rows, :])
        tokens_now[rows, :] = result.astype(bf16)
        return carry

    for i in range(4):
        for copy in loads(i):
            copy.start()
    greet([(beside, z), (across, z)] + [(s, (z + k) % 4) for k in range(1, 4)])
    for k in (1, 3, 2):
        swap_start(k)

    @pl.when(z < 2)
    def _():
        for copy in own():
            copy.start()

    @pl.when(z >= 2)
    def _():
        for copy in own(True):
            copy.start()

    for i in range(2):
        for copy in loads(i):
            copy.wait()
        flow(i, 0).start()
        flow(i, 1).start()
        if i == 0:
            flow(i, 2).start()
            flow(i, 4).start()
    for i in range(4):
        cross_step(i)
        if i + 1 < 4:
            flow(i + 1, 2).start()
            flow(i + 1, 4).start()
        if i + 2 < 4:
            for copy in loads(i + 2):
                copy.wait()
            flow(i + 2, 0).start()
            flow(i + 2, 1).start()
        if i == 0:
            for copy in plain_loads:
                copy.start()
            wide(0).start()
            wide(1).start()
        if i > 0:
            near_step(i - 1)
            chain(i - 1)
        if i == 1:
            for copy in plain_loads:
                copy.wait()
        if i > 0:
            back(3 * i - 3, 3 * i)
    back(9, mixer_w.shape[0] // wide_rows)
    lax.fori_loop(0, tokens.shape[0] // 16, finish_rows, 0)
    finished = pltpu.make_async_copy(tokens_now, input_grad, wide_sem.at[2])
    finished.start()
    near_step(3)
    chain(3)
    done = pltpu.make_async_copy(held.at[chip, span(z), :], mixer_sum, own_sem.at[3])
    done.start()
    for i in range(4):
        for index in range(6):
            flow(i, index).wait_send()
    chain_drain()
    for k in range(1, 4):
        for copy in swap(k):
            copy.wait()
    for copy in own():
        copy.wait()
    finished.wait()
    done.wait()


def scatter(main, rest, mlp_low, mlp_high, grad_both, mixer_w, tokens, grad_middle, gain):
    rows = main.shape[1] // 4
    cols = main.shape[2] + rest.shape[2]
    ff_part = mlp_low.shape[1] // 3
    tok, model = tokens.shape
    anyspec = pl.BlockSpec(memory_space=pl.ANY)
    dma = pltpu.SemaphoreType.DMA
    return pl.pallas_call(
        scatter_kernel,
        in_specs=[anyspec] * 9,
        out_specs=[anyspec] * 3,
        out_shape=[
            jax.ShapeDtypeStruct((rows, cols), bf16),
            jax.ShapeDtypeStruct((3, rows, 4 * ff_part), bf16),
            jax.ShapeDtypeStruct((tok, model), bf16),
        ],
        scratch_shapes=[
            pltpu.VMEM((4, 4 * rows, cols), bf16),
            pltpu.VMEM((4, rows, cols), bf16),
            pltpu.VMEM((2, 4, rows, cols), bf16),
            pltpu.VMEM((5, rows, cols), bf16),
            pltpu.VMEM(grad_both.shape, bf16),
            pltpu.VMEM((2, 256, grad_both.shape[1]), bf16),
            pltpu.VMEM((tok, model), f32),
            pltpu.VMEM((tok, model), bf16),
            pltpu.VMEM((tok, model), f32),
            pltpu.VMEM((8, model), f32),
            dma((6,)),
            dma((4, 2)), dma((4, 6)), dma((4, 6)), dma((4,)), dma((5,)), dma((3, 3)), dma((3, 3)), dma((4,)),
        ],
        compiler_params=pltpu.CompilerParams(
            collective_id=2, has_side_effects=True, vmem_limit_bytes=62 * 1024 * 1024
        ),
        name="scatter_gradients",
    )(main, rest, mlp_low, mlp_high, grad_both, mixer_w, tokens, grad_middle, gain)


def gather_plain(mixer, gate, up, down):
    groups = lax.axis_size("fsdp")
    part_rows, ff = gate.shape
    own = jnp.stack([w.reshape(part_rows, groups, ff // groups) for w in (gate, up, down)], axis=2)
    mine = lax.all_to_all(jnp.transpose(own, (1, 0, 2, 3)), "fsdp", 0, 0, tiled=True)
    return lax.all_gather(mixer, both, axis=0, tiled=True), mine.reshape(groups * part_rows, -1)


def from_line(shard):
    count = lax.axis_size("fsdp")
    return [shard] + [
        lax.ppermute(shard, "fsdp", [(i, (i + k) % count) for i in range(count)]) for k in range(1, count)
    ]


def swap_cores(shard):
    count = lax.axis_size("seq")
    return lax.ppermute(shard, "seq", [(i, i + 1 - 2 * (i % 2)) for i in range(count)])


def swap_beside(shard):
    return lax.ppermute(shard, "seq", [(i, i ^ 2) for i in range(8)])


def swap_across(shard):
    return lax.ppermute(shard, "seq", [(i, i ^ 4) for i in range(8)])


def add_low(left, right):
    return (left.astype(f32) + right.astype(f32)).astype(bf16)


def scatter_paired(
    normed, grad_both, grad_mix, mixed, rest, mlp_parts, mixer_w, tokens, grad_middle, gain
):
    seq = lax.axis_index("seq")
    core, x, y = seq % 2, (seq // 2) % 2, seq // 4
    main = products(
        [(normed, swap_cores(normed)), (grad_mix, swap_cores(grad_mix))],
        [(0, grad_both, swap_cores(grad_both)), (1, mixed, swap_cores(mixed))],
        (normed.shape[1] // 2,),
        (0, 1, 2, 3),
        tuple(range(8)),
        normed.shape[1] // 2,
        "mixer_products",
    )[0]
    grouped = rest.reshape(4, 2, -1, rest.shape[1])
    own = lax.dynamic_index_in_dim(grouped, core, 1, False)
    other = swap_cores(lax.dynamic_index_in_dim(grouped, 1 - core, 1, False))
    rest = (own.astype(f32) + other.astype(f32)).astype(bf16)
    rest = jnp.concatenate(
        [
            lax.dynamic_slice_in_dim(rest, q, 1, 0)
            for q in ((1 - y) * 2 + 1 - x, y * 2 + 1 - x, (1 - y) * 2 + x, y * 2 + x)
        ],
        axis=0,
    )
    main, rest, mlp_parts = lax.optimization_barrier((main, rest, mlp_parts))
    low, high = [sum(part.astype(f32) for part in parts).astype(bf16) for parts in mlp_parts]
    gain = jnp.broadcast_to(gain[None], (8, gain.shape[0]))
    return scatter(
        main.reshape(4, -1, main.shape[1]), rest, low, high, grad_both, mixer_w, tokens, grad_middle, gain
    )


def scatter_plain(normed, grad_both, grad_mix, mixed, rest, mlp_sum):
    groups = lax.axis_size("fsdp")
    term_wide = mm(normed, grad_both, ((0,), (0,))).astype(bf16)
    term_out = mm(grad_mix, mixed, ((0,), (0,))).astype(bf16)
    mixer_sum = lax.psum_scatter(
        jnp.concatenate([term_wide, term_out, rest], axis=1), "seq", scatter_dimension=0, tiled=True
    )
    mixer_sum = lax.psum_scatter(mixer_sum, "fsdp", scatter_dimension=0, tiled=True)
    ff_part = mlp_sum.shape[1] // 3
    part_rows = mlp_sum.shape[0] // groups
    mlp_sum = mlp_sum.reshape(groups, part_rows, 3, ff_part)
    mlp_back = lax.all_to_all(mlp_sum, "fsdp", 0, 0, tiled=True)
    mlp_back = jnp.transpose(mlp_back, (2, 1, 0, 3)).reshape(3, part_rows, groups * ff_part)
    return mixer_sum, mlp_back


def call_heads(kernel, width, heads, ins, outs, scratch, name):
    def spec(rows_cols):
        rows, by_row = rows_cols
        if by_row:
            return pl.BlockSpec((rows, width), lambda h: (h, 0))
        return pl.BlockSpec((rows, width), lambda h: (0, h))

    in_specs = [spec((width, True)) if rowwise else spec((a.shape[0], False)) for a, rowwise in ins]
    out_specs = [spec((width, True)) if rowwise else spec((rows, False)) for rows, _, rowwise in outs]
    out_shape = [
        jax.ShapeDtypeStruct((heads * width, width) if rowwise else (rows, heads * width), kind)
        for rows, kind, rowwise in outs
    ]
    return pl.pallas_call(
        kernel,
        grid=(heads,),
        in_specs=in_specs,
        out_specs=out_specs,
        out_shape=out_shape,
        scratch_shapes=[pltpu.VMEM((rows, width), f32) for rows in scratch],
        compiler_params=pltpu.CompilerParams(vmem_limit_bytes=40 * 1024 * 1024),
        cost_estimate=pl.CostEstimate(flops=1, bytes_accessed=1, transcendentals=0),
        name=name,
    )(*[a for a, _ in ins])


def on_device(
    block_input,
    cotangent,
    mixer_gain,
    branch_proj,
    gelu_proj,
    conv_taps,
    conv_bias,
    rate_blocks,
    input_blocks,
    rate_bias,
    input_bias,
    decay_param,
    out_proj,
    mlp_gain,
    gate_proj,
    up_proj,
    down_proj,
):
    groups = lax.axis_size("fsdp")
    part_rows, lru = branch_proj.shape
    width = rate_blocks.shape[1]
    heads = lru // width
    margin = conv_taps.shape[0] - 1
    tokens = block_input[0].astype(f32)
    tok_count, model = tokens.shape
    ff = gate_proj.shape[1]
    ff_part = ff // groups
    grad_out = cotangent[0]

    smalls = jnp.stack(
        [conv_taps[k] for k in range(margin + 1)]
        + [conv_bias, rate_bias, input_bias, decay_param, mixer_gain, mlp_gain],
        axis=1,
    )
    small_count = smalls.shape[1]
    smalls = jnp.pad(smalls, ((0, 0), (0, 128 - small_count)))
    first_own = jnp.concatenate([smalls, rate_blocks, input_blocks], axis=1)
    mixer_own = (first_own, branch_proj, gelu_proj, out_proj)
    custom = lax.axis_size("seq") == 8 and groups == 4
    if custom:
        mixer_w, mlp_mine = gather(*mixer_own, gate_proj, up_proj, down_proj)
    else:
        mixer_w, mlp_mine = gather_plain(jnp.concatenate(mixer_own, axis=1), gate_proj, up_proj, down_proj)
    mlp_w = lax.all_gather(mlp_mine, "seq", axis=0, tiled=True)
    grad_out_late = lax.optimization_barrier((grad_out, mlp_mine))[0]
    if custom:
        grad_pieces = from_line(grad_out_late)
    first = lax.optimization_barrier(mixer_w[:, : 128 + 2 * width])
    wide = mixer_w[:, 128 + 2 * width : 128 + 2 * width + 2 * lru]
    proj_out = mixer_w[:, 128 + 2 * width + 2 * lru :]

    table = first[:, :small_count].astype(f32).T
    blocks_rate = first[:, 128 : 128 + width]
    blocks_input = first[:, 128 + width :]
    param_decay = table[margin + 4]
    gain_one = table[margin + 5]
    gain_two = table[margin + 6]
    small = jnp.concatenate(
        [
            table[: margin + 4],
            jax.nn.softplus(-param_decay)[None],
            -jax.nn.sigmoid(-param_decay)[None],
            jnp.zeros((16 - margin - 6, lru), f32),
        ],
        axis=0,
    )

    normed = norm_rows(tokens, gain_one).astype(bf16)
    both_pre = mm(normed, wide, ((1,), (0,)))
    branch = both_pre[:, :lru].astype(bf16)
    gelu_pre = both_pre[:, lru:]
    prior = from_behind(branch[tok_count - margin :], "seq", 1).astype(f32)
    prior = jnp.concatenate([jnp.zeros((8 - margin, lru), f32), prior], axis=0)
    conv, rate_pre, input_pre, cum, local = call_heads(
        mixer_forward,
        width,
        heads,
        [(branch, False), (prior, False), (small, False), (blocks_rate, True), (blocks_input, True)],
        [(tok_count, bf16, False)] + [(tok_count, f32, False)] * 4,
        [tok_count + 8],
        "mixer_forward",
    )
    carried = prefix((cum[-1], local[-1]), "seq", False)
    states = local + cum * carried[None]
    mixed = (states * jax.nn.gelu(gelu_pre, approximate=True)).astype(bf16)
    middle = tokens + mm(mixed, proj_out, ((1,), (1,)))
    normed_two = norm_rows(middle, gain_two).astype(bf16)

    if custom:
        normed_all, normed_other, grad_out_all, grad_out_other = gather_rows(normed_two, grad_pieces)
    else:
        normed_all = lax.all_gather(normed_two, "fsdp", axis=0, tiled=True)
        grad_out_all = lax.all_gather(grad_out_late, "fsdp", axis=0, tiled=True)
    w_gate, w_up, w_down = mlp_w[:, :ff_part], mlp_w[:, ff_part : 2 * ff_part], mlp_w[:, 2 * ff_part :]
    if custom:
        hidden, hidden_other, grad_pair, pair_other, grad_normed_part = feed_forward(
            normed_all, grad_out_all, mlp_w
        )
    else:
        gate = mm(normed_all, w_gate, ((1,), (0,)))
        up_val = mm(normed_all, w_up, ((1,), (0,)))
        gelu_gate, gelu_slope = gelu_parts(gate)
        hidden = (gelu_gate * up_val).astype(bf16)
        grad_hidden = mm(grad_out_all, w_down, ((1,), (0,)))
        grad_gate = (grad_hidden * up_val * gelu_slope).astype(bf16)
        grad_up = (grad_hidden * gelu_gate).astype(bf16)
        grad_normed_part = (
            mm(grad_gate, w_gate, ((1,), (1,))) + mm(grad_up, w_up, ((1,), (1,)))
        ).astype(bf16)
    grad_normed_two = lax.psum_scatter(grad_normed_part, "fsdp", scatter_dimension=0, tiled=True)
    if custom:
        half = model // 16
        beside_high, across_low, mine, beside_low, across_high = shared_products(
            (normed_all, normed_other, grad_out_all, grad_out_other), (grad_pair, pair_other), (hidden, hidden_other)
        )
        from_beside_high, from_across_low = swap_beside(beside_high), swap_across(across_low)
        hidden = lax.optimization_barrier((hidden, mine))[0]
        out_part = mm(hidden, w_down, ((1,), (1,))).astype(bf16)
        out_part, grad_normed_two = lax.optimization_barrier((out_part, grad_normed_two))
    else:
        grad_pair = jnp.concatenate([grad_gate, grad_up], axis=1)
        term_pair = mm(normed_all, grad_pair, ((0,), (0,))).astype(bf16)
        term_down = mm(grad_out_all, hidden, ((0,), (0,))).astype(bf16)
        pair_sum = lax.psum_scatter(term_pair, "seq", scatter_dimension=0, tiled=True)
        down_sum = lax.psum_scatter(term_down, "seq", scatter_dimension=0, tiled=True)
        mlp_sum = jnp.concatenate([pair_sum, down_sum], axis=1)
        out_part = mm(hidden, w_down, ((1,), (1,))).astype(bf16)
    out_sum = lax.psum_scatter(out_part, "fsdp", scatter_dimension=0, tiled=True)
    grad_normed_two = grad_normed_two.astype(f32)

    grad_middle = grad_out.astype(f32) + norm_back(middle, gain_two, grad_normed_two)
    grad_mix = grad_middle.astype(bf16)
    grad_mixed = mm(grad_mix, proj_out, ((1,), (0,)))
    carried_rows = jnp.broadcast_to(carried[None], (8, lru))
    grad_gelu_pre, rev_cum, rev_grad, pair_grad = call_heads(
        mixer_backward_scan,
        width,
        heads,
        [(a, False) for a in (grad_mixed, gelu_pre, rate_pre, cum, local, carried_rows, small)],
        [(tok_count, bf16, False), (tok_count, f32, False), (tok_count, f32, False), (8, f32, False)],
        [tok_count + 8],
        "mixer_backward_scan",
    )
    if custom:
        from_beside_high, from_across_low, pair_grad = lax.optimization_barrier(
            (from_beside_high, from_across_low, pair_grad)
        )
    incoming = prefix((cum[-1], pair_grad[0]), "seq", True)
    if custom:
        beside_low, across_high, incoming = lax.optimization_barrier((beside_low, across_high, incoming))
        from_beside_low, from_across_high = swap_beside(beside_low), swap_across(across_high)
    incoming_rows = jnp.broadcast_to(incoming[None], (8, lru))
    own, head, rate_w_grad, input_w_grad, sums = call_heads(
        mixer_backward,
        width,
        heads,
        [
            (a, False)
            for a in (rev_cum, rev_grad, incoming_rows, cum, local, carried_rows, rate_pre, input_pre, conv, branch, prior, small)
        ]
        + [(blocks_rate, True), (blocks_input, True)],
        [(tok_count, f32, False), (8, f32, False), (0, bf16, True), (0, bf16, True), (8, f32, False)],
        [tok_count + 8, tok_count + 16],
        "mixer_backward",
    )
    received = from_behind(head[8 - margin :], "seq", -1)
    grad_branch = jnp.concatenate(
        [own[: tok_count - margin], own[tok_count - margin :] + received], axis=0
    ).astype(bf16)
    grad_both = jnp.concatenate([grad_branch, grad_gelu_pre], axis=1)
    middle, out_sum, sums = lax.optimization_barrier((middle, out_sum, sums))
    block_output = (middle + out_sum.astype(f32)).astype(bf16)[None]
    vectors = jnp.pad(sums.T, ((0, 0), (0, 128 - sums.shape[0]))).astype(bf16)
    rest = jnp.concatenate([rate_w_grad, input_w_grad, vectors], axis=1)
    if custom:
        mlp_parts = (
            (mine[:half], from_across_low, from_beside_low),
            (mine[half:], from_across_high, from_beside_high),
        )
        mixer_sum, mlp_back, input_grad = scatter_paired(
            normed, grad_both, grad_mix, mixed, rest, mlp_parts, mixer_w, block_input[0], grad_middle, gain_one
        )
    else:
        mixer_sum, mlp_back = scatter_plain(normed, grad_both, grad_mix, mixed, rest, mlp_sum)
        grad_normed = mm(grad_both, wide, ((1,), (1,)))
        input_grad = (grad_middle + norm_back(tokens, gain_one, grad_normed)).astype(bf16)
    input_grad = input_grad[None]
    mlp_grads = [mlp_back[m].astype(f32) for m in range(3)]
    mixer_sum = mixer_sum.astype(f32)
    edges = [lru, 2 * lru, 3 * lru, 3 * lru + width, 3 * lru + 2 * width]
    dbranch, dgelu, dout, drate, dinput, vec = jnp.split(mixer_sum, edges, axis=1)
    vec = vec.T
    return (
        block_output,
        input_grad,
        gain_back(mixer_gain, (branch_proj, dbranch), (gelu_proj, dgelu)),
        dbranch,
        dgelu,
        vec[: margin + 1],
        vec[7],
        drate,
        dinput,
        vec[4],
        vec[5],
        vec[6],
        dout,
        gain_back(mlp_gain, (gate_proj, mlp_grads[0]), (up_proj, mlp_grads[1])),
        mlp_grads[0],
        mlp_grads[1],
        mlp_grads[2],
    )


def solution(mesh):
    tokens = P("fsdp", "seq", None)
    vector = P(both)
    matrix = P(both, None)
    taps = P(None, both)
    return jax.shard_map(
        on_device,
        mesh=mesh,
        in_specs=(
            tokens, tokens, vector, matrix, matrix, taps, vector, matrix, matrix,
            vector, vector, vector, matrix, vector, matrix, matrix, matrix,
        ),
        out_specs=(
            tokens, tokens, vector, matrix, matrix, taps, vector, matrix, matrix,
            vector, vector, vector, matrix, vector, matrix, matrix, matrix,
        ),
        check_vma=False,
    )
```

```python
import functools

import jax
import jax.numpy as jnp
from jax import lax
from jax.experimental import pallas as pl
from jax.experimental.pallas import tpu as pltpu
from jax.sharding import PartitionSpec as P

epsilon = 1e-06
f32 = jnp.float32
bf16 = jnp.bfloat16
both = ("seq", "fsdp")
MESH = pl.DeviceIdType.MESH
TAP, CONV_BIAS, RATE_BIAS, INPUT_BIAS, SOFT, SOFT_SLOPE = 0, 4, 5, 6, 7, 8
GELU_C = 0.7978845608028654
GELU_A = 0.044715


def from_behind(shard, axis, by):
    devices = lax.axis_size(axis)
    pairs = [(i, i + by) for i in range(devices) if 0 <= i + by < devices]
    return lax.ppermute(shard, axis, pairs)


def prefix(part, axis, reverse):
    count = lax.axis_size(axis)
    place = lax.axis_index(axis)
    gathered = lax.all_gather(jnp.stack(part), axis)
    state = jnp.zeros_like(part[1])
    for hop in range(count):
        source = count - 1 - hop if reverse else hop
        ahead = source > place if reverse else source < place
        state = jnp.where(ahead, gathered[source, 1] + gathered[source, 0] * state, state)
    return state


def norm_rows(values, scales):
    return values * lax.rsqrt(jnp.mean(values * values, axis=-1, keepdims=True) + epsilon) * scales


def norm_back(values, scales, grads):
    inverse = lax.rsqrt(jnp.mean(values * values, axis=-1, keepdims=True) + epsilon)
    scaled = grads * scales
    shared = jnp.mean(values * scaled, axis=-1, keepdims=True)
    return inverse * scaled - values * (inverse * inverse * inverse * shared)


def gain_back(gain, *pairs):
    total = sum(jnp.sum(weight.astype(f32) * grad, axis=1) for weight, grad in pairs)
    return total / gain.astype(f32)


def gelu_parts(x):
    inner = jnp.tanh(GELU_C * (x + GELU_A * x * x * x))
    return 0.5 * x * (1.0 + inner), 0.5 * (1.0 + inner) + 0.5 * x * (1.0 - inner * inner) * (
        GELU_C * (1.0 + 3.0 * GELU_A * x * x)
    )


def mm(left, right, dims):
    return lax.dot_general(left, right, (dims, ((), ())), preferred_element_type=f32)


def sigmoid(x):
    return 1.0 / (1.0 + jnp.exp(-x))


def scan_rows(decay, value, reverse):
    rows = decay.shape[0]
    place = lax.broadcasted_iota(jnp.int32, decay.shape, 0)
    step = 1
    while step < rows:
        shift = rows - step if reverse else step
        inside = place < rows - step if reverse else place >= step
        before_value = jnp.where(inside, pltpu.roll(value, shift, 0), 0.0)
        before_decay = jnp.where(inside, pltpu.roll(decay, shift, 0), 1.0)
        value = value + decay * before_value
        decay = decay * before_decay
        step *= 2
    return decay, value


def gates(rate_pre, input_pre, soft):
    rate = sigmoid(rate_pre)
    log_decay = -8.0 * rate * soft
    decay = jnp.exp(log_decay)
    square = decay * decay
    root = jnp.sqrt(-jnp.tanh(log_decay) * (1.0 + square))
    return rate, decay, square, root, sigmoid(input_pre)


def mixer_forward(branch, prior, small, rate_w, input_w, conv, rate_pre, input_pre, cum, local, ext):
    rows = branch.shape[0]
    ext[0:8, :] = prior[...]
    ext[8:, :] = branch[...].astype(f32)
    total = small[CONV_BIAS : CONV_BIAS + 1, :] + small[TAP : TAP + 1, :] * ext[8:, :]
    for offset in range(1, 4):
        total = total + small[TAP + offset : TAP + offset + 1, :] * ext[pl.ds(8 - offset, rows), :]
    low = total.astype(bf16)
    conv[...] = low
    rate = mm(low, rate_w[...], ((1,), (0,))) + small[RATE_BIAS : RATE_BIAS + 1, :]
    inp = mm(low, input_w[...], ((1,), (0,))) + small[INPUT_BIAS : INPUT_BIAS + 1, :]
    rate_pre[...] = rate
    input_pre[...] = inp
    _, decay, _, root, opened = gates(rate, inp, small[SOFT : SOFT + 1, :])
    product, states = scan_rows(decay, root * opened * low.astype(f32), False)
    cum[...] = product
    local[...] = states


def mixer_backward_scan(grad_mixed, gelu_pre, rate_pre, cum, local, carried, small, grad_pre, rev_cum, rev_grad, pair, ext):
    rows = grad_mixed.shape[0]
    states = local[...] + cum[...] * carried[0:1, :]
    value, slope = gelu_parts(gelu_pre[...])
    grad = grad_mixed[...]
    grad_pre[...] = (grad * states * slope).astype(bf16)
    decay = jnp.exp(-8.0 * sigmoid(rate_pre[...]) * small[SOFT : SOFT + 1, :])
    ext[0:rows, :] = decay
    ext[rows:, :] = jnp.ones((8, decay.shape[1]), f32)
    product, back = scan_rows(ext[pl.ds(1, rows), :], grad * value, True)
    rev_cum[...] = product
    rev_grad[...] = back
    pair[...] = jnp.broadcast_to(decay[0:1, :] * back[0:1, :], pair.shape)


def mixer_backward(
    rev_cum, rev_grad, incoming, cum, local, carried, rate_pre, input_pre, conv, branch, prior, small, rate_w, input_w,
    own, head, rate_w_grad, input_w_grad, sums, ext, gext,
):
    rows = rev_cum.shape[0]
    soft = small[SOFT : SOFT + 1, :]
    grad_states = rev_grad[...] + rev_cum[...] * incoming[0:1, :]
    rate, decay, square, root, opened = gates(rate_pre[...], input_pre[...], soft)
    ext[0:8, :] = jnp.broadcast_to(carried[0:1, :], (8, carried.shape[1]))
    ext[8:, :] = local[...] + cum[...] * carried[0:1, :]
    before = ext[pl.ds(7, rows), :]
    low = conv[...]
    conv_in = low.astype(f32)
    grad_log = grad_states * decay * before - grad_states * opened * conv_in * square / root
    driven = grad_states * root
    grad_input = (driven * conv_in * opened * (1.0 - opened)).astype(bf16)
    by_rate = grad_log * (-8.0 * rate)
    grad_rate = (by_rate * soft * (1.0 - rate)).astype(bf16)
    sums[6:7, :] = jnp.sum(by_rate, axis=0, keepdims=True) * small[SOFT_SLOPE : SOFT_SLOPE + 1, :]
    sums[4:5, :] = jnp.sum(grad_rate.astype(f32), axis=0, keepdims=True)
    sums[5:6, :] = jnp.sum(grad_input.astype(f32), axis=0, keepdims=True)
    rate_w_grad[...] = mm(low, grad_rate, ((0,), (0,))).astype(rate_w_grad.dtype)
    input_w_grad[...] = mm(low, grad_input, ((0,), (0,))).astype(input_w_grad.dtype)
    grad_conv = (
        driven * opened
        + mm(grad_rate, rate_w[...], ((1,), (1,)))
        + mm(grad_input, input_w[...], ((1,), (1,)))
    )
    sums[7:8, :] = jnp.sum(grad_conv, axis=0, keepdims=True)
    ext[0:8, :] = prior[...]
    ext[8:, :] = branch[...].astype(f32)
    gext[0:8, :] = jnp.zeros((8, grad_conv.shape[1]), f32)
    gext[8 : 8 + rows, :] = grad_conv
    gext[8 + rows :, :] = jnp.zeros((8, grad_conv.shape[1]), f32)
    back = jnp.zeros_like(grad_conv)
    front = jnp.zeros((8, grad_conv.shape[1]), f32)
    for offset in range(4):
        tap = small[TAP + offset : TAP + offset + 1, :]
        sums[offset : offset + 1, :] = jnp.sum(
            grad_conv * ext[pl.ds(8 - offset, rows), :], axis=0, keepdims=True
        )
        back = back + tap * gext[pl.ds(8 + offset, rows), :]
        front = front + tap * gext[pl.ds(offset, 8), :]
    own[...] = back
    head[...] = front


def places():
    s = lax.axis_index("seq")
    z = lax.axis_index("fsdp")
    core = s + 1 - 2 * (s % 2)
    beside = s + 2 - 4 * ((s // 2) % 2)
    across = s + 4 - 8 * (s // 4)
    return s, z, core, beside, across


def greet(peers):
    barrier = pltpu.get_barrier_semaphore()
    for peer in peers:
        pl.semaphore_signal(barrier, inc=1, device_id=peer, device_id_type=MESH)
    pl.semaphore_wait(barrier, len(peers))


def gather_kernel(
    first, branch, gelu, outer, gate, up, down, mixer_all, mlp_mine,
    mixer, load_sem, flow_send, flow_recv, line_send, line_recv, swap_send, swap_recv, own_sem,
):
    s, z, core, beside, across = places()
    rows, cols = mixer.shape
    ff_part = mlp_mine.shape[1] // 3
    cut = cols // 256 * 128
    diag = beside + across - s
    loads, start = [], 0
    for n, part in enumerate((first, branch, gelu, outer)):
        size = part.shape[1]
        loads.append(pltpu.make_async_copy(part, mixer.at[:, pl.ds(start, size)], load_sem.at[n]))
        loads[-1].start()
        start += size
    greet([(core, z), (beside, z), (across, z)] + [(s, (z + k) % 4) for k in range(1, 4)])

    def remote(src, dst, send, recv, target):
        return pltpu.make_async_remote_copy(
            src_ref=src, dst_ref=dst, send_sem=send, recv_sem=recv, device_id=target, device_id_type=MESH
        )

    def piece(seq, zz, half=None):
        span = pl.ds(pl.multiple_of((seq * 4 + zz) * rows, 16), rows)
        if half is None:
            return mixer_all.at[span, :]
        return mixer_all.at[span, pl.ds(0, cut) if half == 0 else pl.ds(cut, cols - cut)]

    def flow(zz, index, seq, half, target, src=None):
        ref = piece(seq, zz, half)
        return remote(
            ref if src is None else src, ref, flow_send.at[zz, index], flow_recv.at[zz, index], (target, z)
        )

    def sends(zz, src=None):
        return [
            flow(zz, 0, s, None, beside, src),
            flow(zz, 1, s, None, across, src),
            flow(zz, 4, s, None, core, src),
        ]

    def spread(zz, src=None):
        for copy in sends(zz, src):
            copy.start()

    def relay(zz):
        flow(zz, 0, beside, None, beside).wait_recv()
        flow(zz, 3, beside, 0, across).start()
        flow(zz, 5, beside, None, core).start()
        flow(zz, 1, across, None, across).wait_recv()
        flow(zz, 2, across, 1, beside).start()
        flow(zz, 6, across, None, core).start()

    def finish(zz):
        flow(zz, 3, diag, 0, across).wait_recv()
        flow(zz, 7, diag, 0, core).start()
        flow(zz, 2, diag, 1, beside).wait_recv()
        flow(zz, 8, diag, 1, core).start()

    def drain(zz, src=None):
        for copy in sends(zz, src):
            copy.wait_send()
        flow(zz, 3, beside, 0, across).wait_send()
        flow(zz, 5, beside, None, core).wait_send()
        flow(zz, 2, across, 1, beside).wait_send()
        flow(zz, 6, across, None, core).wait_send()
        flow(zz, 7, diag, 0, core).wait_send()
        flow(zz, 8, diag, 1, core).wait_send()
        flip = core - s
        flow(zz, 4, core, None, core).wait_recv()
        flow(zz, 5, beside + flip, None, core).wait_recv()
        flow(zz, 6, across + flip, None, core).wait_recv()
        flow(zz, 7, diag + flip, 0, core).wait_recv()
        flow(zz, 8, diag + flip, 1, core).wait_recv()

    def line(zz, up_way, hop, src=None):
        ref = piece(s, zz)
        way = 0 if up_way else 1
        target = z + 1 if up_way else z - 1
        return remote(
            ref if src is None else src, ref, line_send.at[way, hop], line_recv.at[way, hop], (s, target)
        )

    def line_hop(hop):
        def below():
            line(z - hop, True, hop - 1).wait_recv()
            pl.when(z < 3)(lambda: line(z - hop, True, hop).start())

        def above():
            line(z + hop, False, hop - 1).wait_recv()
            pl.when(z > 0)(lambda: line(z + hop, False, hop).start())

        pl.when(z >= hop)(below)
        pl.when(z + hop <= 3)(above)

    def at_hop(hop, act):
        pl.when(z >= hop)(lambda: act(z - hop))
        pl.when(z + hop <= 3)(lambda: act(z + hop))

    def landing(m, zz):
        return mlp_mine.at[pl.ds(pl.multiple_of(zz * rows, 16), rows), pl.ds(m * ff_part, ff_part)]

    def columns(m, zz):
        return (gate, up, down)[m].at[:, pl.ds(pl.multiple_of(zz * ff_part, 128), ff_part)]

    def swap(k, m, arriving=False):
        to = (z + k) % 4
        came = (z + 4 - k) % 4
        return remote(
            columns(m, to), landing(m, came if arriving else z), swap_send.at[k - 1, m], swap_recv.at[k - 1, m], (s, to)
        )

    local = [pltpu.make_async_copy(columns(m, z), landing(m, z), own_sem.at[m]) for m in range(3)]
    local.append(pltpu.make_async_copy(mixer, piece(s, z), own_sem.at[3]))
    for copy in loads:
        copy.wait()

    pl.when(z < 3)(lambda: line(z, True, 0, mixer).start())
    pl.when(z > 0)(lambda: line(z, False, 0, mixer).start())
    spread(z, mixer)
    for copy in local:
        copy.start()
    line_hop(1)
    at_hop(1, spread)
    relay(z)
    line_hop(2)
    at_hop(2, spread)
    finish(z)
    at_hop(1, relay)
    line_hop(3)
    at_hop(3, spread)
    for k in (1, 3, 2):
        for m in range(3):
            swap(k, m).start()
    at_hop(1, finish)
    at_hop(2, relay)
    at_hop(3, relay)
    at_hop(2, finish)
    at_hop(3, finish)
    drain(z, mixer)
    for hop in range(1, 4):
        at_hop(hop, drain)
    for copy in local:
        copy.wait()
    for k in (1, 3, 2):
        for m in range(3):
            swap(k, m).wait_send()
            swap(k, m, True).wait_recv()
    pl.when(z < 3)(lambda: line(z, True, 0, mixer).wait_send())
    pl.when(z > 0)(lambda: line(z, False, 0, mixer).wait_send())
    for hop in range(1, 3):
        pl.when((z >= hop) & (z < 3))(lambda: line(z - hop, True, hop).wait_send())
        pl.when((z + hop <= 3) & (z > 0))(lambda: line(z + hop, False, hop).wait_send())


def gather(first, branch, gelu, outer, gate, up, down):
    rows = first.shape[0]
    cols = first.shape[1] + branch.shape[1] + gelu.shape[1] + outer.shape[1]
    ff_part = gate.shape[1] // 4
    anyspec = pl.BlockSpec(memory_space=pl.ANY)
    dma = pltpu.SemaphoreType.DMA
    return pl.pallas_call(
        gather_kernel,
        in_specs=[anyspec] * 7,
        out_specs=[anyspec] * 2,
        out_shape=[
            jax.ShapeDtypeStruct((32 * rows, cols), bf16),
            jax.ShapeDtypeStruct((4 * rows, 3 * ff_part), bf16),
        ],
        scratch_shapes=[
            pltpu.VMEM((rows, cols), bf16), dma((4,)),
            dma((4, 9)), dma((4, 9)), dma((2, 3)), dma((2, 3)), dma((3, 3)), dma((3, 3)), dma((4,)),
        ],
        compiler_params=pltpu.CompilerParams(collective_id=1, has_side_effects=True),
        name="gather_weights",
    )(first, branch, gelu, outer, gate, up, down)


def rows_kernel(
    normed, grad0, grad1, grad2, grad3, normed_all, normed_other, grad_all, grad_other,
    line_send, line_recv, core_send, core_recv, own_sem, held,
):
    s, z, core, _, _ = places()
    tok = normed.shape[0]
    cuts = 4
    grads = (grad0, grad1, grad2, grad3)
    greet([(core, z)] + [(s, (z + k) % 4) for k in range(1, 4)])

    def rows(ref, zz):
        return ref.at[pl.ds(pl.multiple_of(zz * tok, 16), tok), :]

    def remote(src, dst, send, recv, target):
        return pltpu.make_async_remote_copy(
            src_ref=src, dst_ref=dst, send_sem=send, recv_sem=recv, device_id=target, device_id_type=MESH
        )

    def parts(ref):
        size = tok // cuts
        return [ref.at[pl.ds(n * size, size), :] for n in range(cuts)]

    def line(zz, up_way, hop):
        way = 0 if up_way else 1
        target = z + 1 if up_way else z - 1
        src = normed if hop == 0 else rows(normed_all, zz)
        dst = rows(normed_all, zz)
        return [
            remote(a, b, line_send.at[way, hop, n], line_recv.at[way, hop, n], (s, target))
            for n, (a, b) in enumerate(zip(parts(src), parts(dst)))
        ]

    def over(zz, own=False):
        src = normed if own else rows(normed_all, zz)
        return remote(src, rows(normed_other, zz), core_send.at[0, zz], core_recv.at[0, zz], (core, z))

    def grad_over(k):
        zz = (z + 4 - k) % 4
        return remote(grads[k], rows(grad_other, zz), core_send.at[1, zz], core_recv.at[1, zz], (core, z))

    def line_start(zz, up_way, hop):
        for copy in line(zz, up_way, hop):
            copy.start()

    def line_drain(zz, up_way, hop):
        for copy in line(zz, up_way, hop):
            copy.wait_send()

    def hop_step(hop):
        def below():
            for came, on in zip(line(z - hop, True, hop - 1), line(z - hop, True, hop) if hop < 3 else [None] * cuts):
                came.wait_recv()
                if on is not None:
                    pl.when(z < 3)(on.start)
            over(z - hop).start()

        def above():
            for came, on in zip(line(z + hop, False, hop - 1), line(z + hop, False, hop) if hop < 3 else [None] * cuts):
                came.wait_recv()
                if on is not None:
                    pl.when(z > 0)(on.start)
            over(z + hop).start()

        pl.when(z >= hop)(below)
        pl.when(z + hop <= 3)(above)

    local = [pltpu.make_async_copy(grads[k], held.at[k], own_sem.at[k]) for k in range(4)]
    local.append(pltpu.make_async_copy(normed, held.at[4], own_sem.at[4]))
    stored = [
        pltpu.make_async_copy(held.at[k], rows(grad_all, (z + 4 - k) % 4), own_sem.at[k]) for k in range(4)
    ]
    stored.append(pltpu.make_async_copy(held.at[4], rows(normed_all, z), own_sem.at[4]))
    pl.when(z < 3)(lambda: line_start(z, True, 0))
    pl.when(z > 0)(lambda: line_start(z, False, 0))
    over(z, True).start()
    for copy in local:
        copy.start()
    for k in range(4):
        grad_over(k).start()
    for copy, store in zip(local, stored):
        copy.wait()
        store.start()
    for hop in range(1, 4):
        hop_step(hop)
    for copy in stored:
        copy.wait()
    for k in range(4):
        grad_over(k).wait()
    over(z, True).wait()
    for k in range(1, 4):
        over((z + k) % 4).wait()
    pl.when(z < 3)(lambda: line_drain(z, True, 0))
    pl.when(z > 0)(lambda: line_drain(z, False, 0))
    for hop in range(1, 3):
        pl.when((z >= hop) & (z < 3))(lambda: line_drain(z - hop, True, hop))
        pl.when((z + hop <= 3) & (z > 0))(lambda: line_drain(z + hop, False, hop))


def gather_rows(normed, grads):
    tok, model = normed.shape
    anyspec = pl.BlockSpec(memory_space=pl.ANY)
    dma = pltpu.SemaphoreType.DMA
    return pl.pallas_call(
        rows_kernel,
        in_specs=[anyspec] * 5,
        out_specs=[anyspec] * 4,
        out_shape=[jax.ShapeDtypeStruct((4 * tok, model), bf16)] * 4,
        scratch_shapes=[dma((2, 3, 4)), dma((2, 3, 4)), dma((2, 4)), dma((2, 4)), dma((5,)), pltpu.VMEM((5, tok, model), bf16)],
        compiler_params=pltpu.CompilerParams(collective_id=3, has_side_effects=True),
        name="gather_rows",
    )(normed, *grads)


def column_tiles(cols, size=512):
    return [(start, min(size, cols - start)) for start in range(0, cols, size)]


def feed_forward_kernel(
    normed, grad_out, weights, hidden, hidden_other, pair, pair_other, back,
    held, hidden_now, pair_now, sems, store_sem, core_send, core_recv,
):
    s, z, core, _, _ = places()
    step = pl.program_id(0)
    ff_part = held.shape[2]
    model = held.shape[1]
    rows = normed.shape[0]
    tiles = column_tiles(ff_part)
    made = ((hidden_now, hidden, hidden_other), (pair_now, pair, pair_other))

    def load(n, m):
        start, size = tiles[n]
        return pltpu.make_async_copy(
            weights.at[:, pl.ds(m * ff_part + start, size)], held.at[m, :, pl.ds(start, size)], sems.at[n, m]
        )

    def kept(n, turn):
        now, mine, _ = made[n]
        return pltpu.make_async_copy(now.at[turn], mine.at[pl.ds(turn * rows, rows), :], store_sem.at[turn, n])

    def handed(n, turn):
        now, _, other = made[n]
        return pltpu.make_async_remote_copy(
            src_ref=now.at[turn],
            dst_ref=other.at[pl.ds(turn * rows, rows), :],
            send_sem=core_send.at[turn, n],
            recv_sem=core_recv.at[turn, n],
            device_id=(core, z),
            device_id_type=MESH,
        )

    @pl.when(step == 0)
    def _():
        for n in range(len(tiles)):
            for m in range(3):
                load(n, m).start()
        greet([(core, z)])

    for n, (start, size) in enumerate(tiles):
        cols = slice(start, start + size)

        @pl.when(step == 0)
        def _(n=n):
            for m in range(3):
                load(n, m).wait()

        gate = mm(normed[...], held[0, :, cols], ((1,), (0,)))
        value, slope = gelu_parts(gate)
        up = mm(normed[...], held[1, :, cols], ((1,), (0,)))
        hidden_now[step, :, cols] = (value * up).astype(bf16)
        grad_hidden = mm(grad_out[...], held[2, :, cols], ((1,), (0,)))
        pair_now[step, :, cols] = (grad_hidden * up * slope).astype(bf16)
        pair_now[step, :, slice(ff_part + start, ff_part + start + size)] = (grad_hidden * value).astype(bf16)

    for turn in range(2):

        @pl.when(step == turn)
        def _(turn=turn):
            for n in range(2):
                handed(n, turn).start()
                kept(n, turn).start()

    def back_tile(turn, carry):
        cols = pl.ds(pl.multiple_of(turn * 512, 512), 512)
        total = mm(pair_now[step, :, :ff_part], held[0, cols, :], ((1,), (1,)))
        total = total + mm(pair_now[step, :, ff_part:], held[1, cols, :], ((1,), (1,)))
        back[:, cols] = total.astype(bf16)
        return carry

    lax.fori_loop(0, model // 512, back_tile, 0)

    @pl.when(step == 1)
    def _():
        for turn in range(2):
            for n in range(2):
                kept(n, turn).wait()
                handed(n, turn).wait()


def feed_forward(normed, grad_out, weights):
    tok, model = normed.shape
    ff_part = weights.shape[1] // 3
    rows = tok // 2
    anyspec = pl.BlockSpec(memory_space=pl.ANY)
    dma = pltpu.SemaphoreType.DMA
    block = pl.BlockSpec((rows, model), lambda i: (i, 0))
    return pl.pallas_call(
        feed_forward_kernel,
        grid=(2,),
        in_specs=[block, block, anyspec],
        out_specs=[anyspec] * 4 + [block],
        out_shape=[
            jax.ShapeDtypeStruct((tok, cols), bf16)
            for cols in (ff_part, ff_part, 2 * ff_part, 2 * ff_part, model)
        ],
        scratch_shapes=[
            pltpu.VMEM((3, model, ff_part), bf16),
            pltpu.VMEM((2, rows, ff_part), bf16),
            pltpu.VMEM((2, rows, 2 * ff_part), bf16),
            dma((len(column_tiles(ff_part)), 3)), dma((2, 2)), dma((2, 2)), dma((2, 2)),
        ],
        compiler_params=pltpu.CompilerParams(
            collective_id=4, has_side_effects=True, vmem_limit_bytes=60 * 1024 * 1024
        ),
        name="feed_forward",
    )(normed, grad_out, weights)


def add_columns(target, sources, start, size, step):
    def one(turn, carry):
        cols = pl.ds(pl.multiple_of(start + turn * step, 128), step)
        total = target[:, cols].astype(f32)
        for source in sources:
            total = total + source[:, cols].astype(f32)
        target[:, cols] = total.astype(target.dtype)
        return carry

    lax.fori_loop(0, size // step, one, 0)


def shared_products_kernel(
    normed, normed_other, grad, grad_other, weights, pair, pair_other, hidden, hidden_other,
    beside_high, across_low, mine, beside_low, across_high, out,
    turned, slots, stage, diag, landed, waiting, down_now, out_now,
    load_sem, send_sem, recv_sem, store_sem, down_sem, out_sem,
):
    s, z, _, beside, across = places()
    step = pl.program_id(0)
    lefts = ((normed, normed_other), (grad, grad_other))
    chip_cols = normed.shape[1] // 4
    half = chip_cols // 2
    piece = half // 2
    width = pair.shape[1]
    diagonal = beside + across - s
    chips = [q // 2 for q in (diagonal, beside, across, s)]

    def load(side, q, who):
        cols = pl.ds(pl.multiple_of(chips[q] * chip_cols, 128), chip_cols)
        return pltpu.make_async_copy(lefts[side][who].at[:, cols], slots.at[q % 2, who], load_sem.at[q % 2, who])

    def fetch(side):
        for q in range(2):
            for who in range(2):
                load(side, q, who).start()

    def turn(side):
        for q in range(4):
            for who in range(2):
                load(side, q, who).wait()
                stage[...] = slots[q % 2, who].T
                turned[who, q * half : (q + 1) * half, :] = stage[
                    pl.ds(pl.multiple_of(s % 2 * half, 16), half), :
                ]
                if q < 2:
                    load(side, q + 2, who).start()

    def tile(own, other, start, size):
        cols = pl.ds(start, size)
        block = mm(turned[0], own[:, cols], ((1,), (0,)))
        block = (block + mm(turned[1], other[:, cols], ((1,), (0,)))).astype(bf16)
        parts = [block[n * piece : (n + 1) * piece] for n in range(8)]
        there = pl.ds(pl.multiple_of(step * width + start, 128), size)
        diag[0, :, there] = parts[0]
        diag[1, :, there] = parts[1]
        waiting[0, :, there] = parts[2]
        beside_high[:, cols] = parts[3]
        across_low[:, cols] = parts[4]
        waiting[1, :, there] = parts[5]
        mine[0:piece, cols] = parts[6]
        mine[piece:, cols] = parts[7]

    def multiply(own, other):
        def one(turn, carry):
            tile(own, other, pl.multiple_of(turn * 512, 512), 512)
            return carry

        lax.fori_loop(0, width // 512, one, 0)
        if width % 512:
            tile(own, other, width // 512 * 512, width % 512)

    def push(way, j):
        cols = pl.ds(j * width, width)
        return pltpu.make_async_remote_copy(
            src_ref=diag.at[way, :, cols],
            dst_ref=landed.at[way, :, cols],
            send_sem=send_sem.at[way, j],
            recv_sem=recv_sem.at[way, j],
            device_id=(across if way == 0 else beside, z),
            device_id_type=MESH,
        )

    def store(way, j):
        cols = pl.ds(j * width, width)
        return pltpu.make_async_copy(
            waiting.at[way, :, cols], (beside_low, across_high)[way].at[:, cols], store_sem.at[way, j]
        )

    out_rows = down_now.shape[1]
    out_tiles = weights.shape[0] // out_rows

    def down(t):
        source = weights.at[pl.ds(t * out_rows, out_rows), pl.ds(2 * width, width)]
        return pltpu.make_async_copy(source, down_now.at[t % 2], down_sem.at[t % 2])

    def out_store(t):
        return pltpu.make_async_copy(
            out_now.at[t % 2], out.at[:, pl.ds(t * out_rows, out_rows)], out_sem.at[t % 2]
        )

    def out_product():
        for t in range(out_tiles):
            down(t).wait()
            if t > 1:
                out_store(t - 2).wait()
            out_now[t % 2] = mm(hidden[...], down_now[t % 2], ((1,), (1,))).astype(bf16)
            out_store(t).start()
            if t + 2 < out_tiles:
                down(t + 2).start()

    @pl.when(step == 0)
    def _():
        fetch(0)
        greet([(beside, z), (across, z)])
        turn(0)

    @pl.when(step == 2)
    def _():
        down(0).start()
        down(1).start()
        turn(1)

    pl.when(step < 2)(functools.partial(multiply, pair, pair_other))
    pl.when(step == 1)(functools.partial(fetch, 1))
    pl.when(step == 2)(functools.partial(multiply, hidden, hidden_other))
    for j in range(3):

        @pl.when(step == j)
        def _(j=j):
            push(0, j).start()
            push(1, j).start()

    @pl.when(step == 2)
    def _():
        out_product()
        for j in range(3):
            for way in range(2):
                push(way, j).wait_recv()
                add_columns(waiting.at[way], [landed.at[way]], j * width, width, 384)
                store(way, j).start()
        for j in range(3):
            for way in range(2):
                push(way, j).wait_send()
                store(way, j).wait()
        for t in range(out_tiles - 2, out_tiles):
            out_store(t).wait()


def shared_products(lefts, weights, pair, hidden):
    tok, model = lefts[0].shape
    width = hidden[0].shape[1]
    half = model // 8
    anyspec = pl.BlockSpec(memory_space=pl.ANY)
    dma = pltpu.SemaphoreType.DMA

    def block(rows):
        return pl.BlockSpec((rows, width), lambda j: (0, j))

    pair_spec = pl.BlockSpec((tok, width), lambda j: (0, jnp.minimum(j, 1)))
    hidden_spec = pl.BlockSpec((tok, width), lambda j: (0, 0))
    rows_out = (half // 2, half // 2, half, half // 2, half // 2)
    return pl.pallas_call(
        shared_products_kernel,
        grid=(3,),
        in_specs=[anyspec] * 5 + [pair_spec] * 2 + [hidden_spec] * 2,
        out_specs=[block(rows) for rows in rows_out[:3]] + [anyspec] * 3,
        out_shape=[jax.ShapeDtypeStruct((rows, 3 * width), bf16) for rows in rows_out]
        + [jax.ShapeDtypeStruct((tok, model), bf16)],
        scratch_shapes=[
            pltpu.VMEM((2, 4 * half, tok), bf16),
            pltpu.VMEM((2, 2, tok, 2 * half), bf16),
            pltpu.VMEM((2 * half, tok), bf16),
            pltpu.VMEM((2, half // 2, 3 * width), bf16),
            pltpu.VMEM((2, half // 2, 3 * width), bf16),
            pltpu.VMEM((2, half // 2, 3 * width), bf16),
            pltpu.VMEM((2, 512, width), bf16),
            pltpu.VMEM((2, tok, 512), bf16),
            dma((2, 2)), dma((2, 3)), dma((2, 3)), dma((2, 3)), dma((2,)), dma((2,)),
        ],
        compiler_params=pltpu.CompilerParams(
            collective_id=5, has_side_effects=True, vmem_limit_bytes=60 * 1024 * 1024
        ),
        name="feed_forward_products",
    )(*lefts, weights, *pair, *hidden)


def scatter_kernel(
    normed, grad_mix, grad_both, mixed, rest, mlp_low, mlp_high, mixer_w, tokens, gain, mixer_sum, mlp_back, input_grad,
    held, cross, near, lined, left_now, both_now, mixed_now, turned, stage, rest_other, back_now, wide_now, gain_now,
    load_sem, core_send, core_recv, wide_sem,
    flow_send, flow_recv, line_send, line_recv, swap_send, swap_recv, own_sem,
):
    s, z, core, beside, across = places()
    chip_diag, chip_beside, chip_across, chip = 0, 1, 2, 3
    chips = [q // 2 for q in (beside + across - s, beside, across, s)]
    rows = held.shape[1] // 4
    cols = held.shape[2]
    cut = cols // 256 * 128
    ff_part = mlp_low.shape[1] // 3
    tok, model = tokens.shape
    half = 4 * rows
    lru2 = grad_both.shape[1]
    rest_start = lru2 + mixed.shape[1]
    order = (3 * (1 - z // 2), (2 + 3 * z) % 5, 1 + z % 2, z)

    def remote(src, dst, send, recv, target):
        return pltpu.make_async_remote_copy(
            src_ref=src, dst_ref=dst, send_sem=send, recv_sem=recv, device_id=target, device_id_type=MESH
        )

    def span(k):
        return pl.ds(pl.multiple_of(k * rows, 16), rows)

    shared = (
        (normed, left_now.at[0]), (grad_both, both_now), (grad_mix, left_now.at[1]), (mixed, mixed_now),
    )
    loads = [
        pltpu.make_async_copy(source, target.at[pl.ds(0, tok), :], load_sem.at[n])
        for n, (source, target) in enumerate(shared)
    ]
    pushes = [
        (source, target.at[pl.ds(tok, tok), :]) for source, target in shared
    ]

    def push(n):
        if n < 4:
            source, target = pushes[n]
        else:
            source = rest.at[pl.ds(pl.multiple_of(chips[n - 4] * 2 * half + (1 - s % 2) * half, 16), half), :]
            target = rest_other.at[n - 4]
        return pltpu.make_async_remote_copy(
            src_ref=source,
            dst_ref=target,
            send_sem=core_send.at[n],
            recv_sem=core_recv.at[n],
            device_id=(core, z),
            device_id_type=MESH,
        )

    def rest_load(q):
        source = rest.at[pl.ds(pl.multiple_of(chips[q] * 2 * half + s % 2 * half, 16), half), :]
        return pltpu.make_async_copy(
            source, held.at[q, :, pl.ds(rest_start, cols - rest_start)], load_sem.at[4 + q]
        )

    def turn(side):
        for q in range(4):
            source = left_now[side, :, pl.ds(pl.multiple_of(chips[q] * 2 * half, 128), 2 * half)]
            stage[...] = source.T
            turned[side, q * half : (q + 1) * half, :] = stage[
                pl.ds(pl.multiple_of(s % 2 * half, 16), half), :
            ]

    def multiply(q):
        for side, right, start in ((0, both_now, 0), (1, mixed_now, lru2)):

            def one(turn, carry, side=side, right=right, start=start):
                here = pl.multiple_of(turn * 512, 512)
                block = mm(turned[side, q * half : (q + 1) * half, :], right[:, pl.ds(here, 512)], ((1,), (0,)))
                held[q, :, pl.ds(pl.multiple_of(start + here, 512), 512)] = block.astype(bf16)
                return carry

            lax.fori_loop(0, right.shape[1] // 512, one, 0)

    left, right = pl.ds(0, cut), pl.ds(cut, cols - cut)

    def block(q, i, side):
        return held.at[q, span(order[i]), side]

    def flow(i, index):
        send, recv = flow_send.at[i, index], flow_recv.at[i, index]
        to_beside, to_across = (beside, z), (across, z)
        if index == 0:
            return remote(block(chip_diag, i, left), cross.at[i, :, left], send, recv, to_across)
        if index == 1:
            return remote(block(chip_diag, i, right), cross.at[i, :, right], send, recv, to_beside)
        if index == 2:
            return remote(block(chip_beside, i, right), near.at[0, i, :, right], send, recv, to_beside)
        if index == 3:
            return remote(block(chip_beside, i, left), near.at[0, i, :, left], send, recv, to_beside)
        if index == 4:
            return remote(block(chip_across, i, left), near.at[1, i, :, left], send, recv, to_across)
        return remote(block(chip_across, i, right), near.at[1, i, :, right], send, recv, to_across)

    def cross_step(i):
        flow(i, 0).wait_recv()
        add_columns(held.at[chip_beside, span(order[i]), :], [cross.at[i]], 0, cut, 512)
        flow(i, 3).start()
        flow(i, 1).wait_recv()
        add_columns(held.at[chip_across, span(order[i]), :], [cross.at[i]], cut, cols - cut, 384)
        flow(i, 5).start()

    def near_step(i):
        for index in (2, 4, 3, 5):
            flow(i, index).wait_recv()
        add_columns(held.at[chip, span(order[i]), :], [near.at[0, i], near.at[1, i]], 0, cols, 640)

    def line(k, slot, target):
        return remote(
            held.at[chip, span(k), :], lined.at[slot], line_send.at[k], line_recv.at[slot], (s, target)
        )

    def absorb(k, slot, source):
        line(k, slot, source).wait_recv()
        add_columns(held.at[chip, span(k), :], [lined.at[slot]], 0, cols, 640)

    def chain(i):
        k = order[i]
        if i == 3:
            pl.when(z > 0)(lambda: absorb(k, k, z - 1))
            pl.when(z < 3)(lambda: absorb(k, 4, z + 1))
            return

        @pl.when(k > z)
        def _():
            pl.when(z > 0)(lambda: absorb(k, k, z - 1))
            line(k, k, z + 1).start()

        @pl.when(k < z)
        def _():
            pl.when(z < 3)(lambda: absorb(k, k, z + 1))
            pl.when(k == z - 1)(lambda: line(k, 4, z - 1).start())
            pl.when(k < z - 1)(lambda: line(k, k, z - 1).start())

    def chain_drain():
        for i in range(3):
            k = order[i]
            line(k, k, (z + 1) % 4).wait_send()

    def swap(k, high=False):
        to = (z + k) % 4
        here = pl.ds(pl.multiple_of(z * ff_part, 128), ff_part)
        source = (mlp_high if high else mlp_low).at[span(to % 2), :]
        return [
            remote(
                source.at[:, pl.ds(m * ff_part, ff_part)],
                mlp_back.at[m, :, here],
                swap_send.at[k - 1, m],
                swap_recv.at[k - 1, m],
                (s, to),
            )
            for m in range(3)
        ]

    def swap_start(k):
        to = (z + k) % 4

        @pl.when(to < 2)
        def _():
            for copy in swap(k):
                copy.start()

        @pl.when(to >= 2)
        def _():
            for copy in swap(k, True):
                copy.start()

    def own(high=False):
        here = pl.ds(pl.multiple_of(z * ff_part, 128), ff_part)
        source = (mlp_high if high else mlp_low).at[span(z % 2), :]
        return [
            pltpu.make_async_copy(source.at[:, pl.ds(m * ff_part, ff_part)], mlp_back.at[m, :, here], own_sem.at[m])
            for m in range(3)
        ]

    wide_rows = wide_now.shape[0]
    wide_tiles = mixer_w.shape[0] // wide_rows
    wide_start = mixer_w.shape[1] - lru2 - model
    wide_slots = (both_now.at[pl.ds(tok, wide_rows), :], wide_now)

    def wide(j):
        source = mixer_w.at[pl.ds(j * wide_rows, wide_rows), pl.ds(wide_start, lru2)]
        return pltpu.make_async_copy(source, wide_slots[j % 2], wide_sem.at[j % 2])

    plain_loads = [
        pltpu.make_async_copy(tokens, left_now.at[0, pl.ds(0, tok), :], wide_sem.at[2]),
        pltpu.make_async_copy(gain, gain_now, wide_sem.at[3]),
    ]

    def back(first, last):
        for j in range(first, last):
            wide(j).wait()
            back_now[:, pl.ds(j * wide_rows, wide_rows)] = mm(
                both_now[0:tok, :], wide_slots[j % 2][...], ((1,), (1,))
            )
            if j + 2 < wide_tiles:
                wide(j + 2).start()

    def finish_rows(turn, carry):
        at = pl.ds(pl.multiple_of(turn * 16, 16), 16)
        result = left_now[1, at, :].astype(f32) + norm_back(
            left_now[0, at, :].astype(f32), gain_now[0:1, :], back_now[at, :]
        )
        left_now[0, at, :] = result.astype(bf16)
        return carry

    for copy in loads:
        copy.start()
    for q in range(4):
        rest_load(q).start()
    greet([(core, z), (beside, z), (across, z)] + [(s, (z + k) % 4) for k in range(1, 4)])
    for n in range(8):
        push(n).start()
    for k in (1, 3, 2):
        swap_start(k)

    @pl.when(z < 2)
    def _():
        for copy in own():
            copy.start()

    @pl.when(z >= 2)
    def _():
        for copy in own(True):
            copy.start()

    for n in (0, 1):
        loads[n].wait()
        push(n).wait_recv()
    turn(0)
    for n in (2, 3):
        loads[n].wait()
        push(n).wait_recv()
    turn(1)
    multiply(chip_diag)
    for q in range(4):
        rest_load(q).wait()
        push(4 + q).wait_recv()
        held[q, :, rest_start:] = add_low(held[q, :, rest_start:], rest_other[q])
    for i in range(2):
        flow(i, 0).start()
        flow(i, 1).start()
    multiply(chip_beside)
    flow(0, 2).start()
    multiply(chip_across)
    flow(0, 4).start()
    multiply(chip)
    for copy in plain_loads:
        copy.start()
    wide(0).start()
    wide(1).start()
    for i in range(4):
        cross_step(i)
        if i + 1 < 4:
            flow(i + 1, 2).start()
            flow(i + 1, 4).start()
        if i + 2 < 4:
            flow(i + 2, 0).start()
            flow(i + 2, 1).start()
        if i > 0:
            near_step(i - 1)
            chain(i - 1)
            back(wide_tiles * (i - 1) // 3, wide_tiles * i // 3)
    for copy in plain_loads:
        copy.wait()
    lax.fori_loop(0, tok // 16, finish_rows, 0)
    finished = pltpu.make_async_copy(left_now.at[0, pl.ds(0, tok), :], input_grad, wide_sem.at[2])
    finished.start()
    near_step(3)
    chain(3)
    done = pltpu.make_async_copy(held.at[chip, span(z), :], mixer_sum, own_sem.at[3])
    done.start()
    for i in range(4):
        for index in range(6):
            flow(i, index).wait_send()
    chain_drain()
    for k in range(1, 4):
        for copy in swap(k):
            copy.wait()
    for copy in own():
        copy.wait()
    for n in range(8):
        push(n).wait_send()
    finished.wait()
    done.wait()


def scatter(normed, grad_mix, grad_both, mixed, rest, mlp_low, mlp_high, mixer_w, tokens, gain):
    tok, model = tokens.shape
    rows = model // 32
    cols = grad_both.shape[1] + mixed.shape[1] + rest.shape[1]
    ff_part = mlp_low.shape[1] // 3
    anyspec = pl.BlockSpec(memory_space=pl.ANY)
    dma = pltpu.SemaphoreType.DMA
    return pl.pallas_call(
        scatter_kernel,
        in_specs=[anyspec] * 10,
        out_specs=[anyspec] * 3,
        out_shape=[
            jax.ShapeDtypeStruct((rows, cols), bf16),
            jax.ShapeDtypeStruct((3, rows, 4 * ff_part), bf16),
            jax.ShapeDtypeStruct((tok, model), bf16),
        ],
        scratch_shapes=[
            pltpu.VMEM((4, 4 * rows, cols), bf16),
            pltpu.VMEM((4, rows, cols), bf16),
            pltpu.VMEM((2, 4, rows, cols), bf16),
            pltpu.VMEM((5, rows, cols), bf16),
            pltpu.VMEM((2, 2 * tok, model), bf16),
            pltpu.VMEM((2 * tok, grad_both.shape[1]), bf16),
            pltpu.VMEM((2 * tok, mixed.shape[1]), bf16),
            pltpu.VMEM((2, 16 * rows, 2 * tok), bf16),
            pltpu.VMEM((8 * rows, 2 * tok), bf16),
            pltpu.VMEM((4, 4 * rows, rest.shape[1]), bf16),
            pltpu.VMEM((tok, model), f32),
            pltpu.VMEM((128, grad_both.shape[1]), bf16),
            pltpu.VMEM((8, model), f32),
            dma((8,)), dma((8,)), dma((8,)), dma((4,)),
            dma((4, 6)), dma((4, 6)), dma((4,)), dma((5,)), dma((3, 3)), dma((3, 3)), dma((4,)),
        ],
        compiler_params=pltpu.CompilerParams(
            collective_id=2, has_side_effects=True, vmem_limit_bytes=62 * 1024 * 1024
        ),
        name="scatter_gradients",
    )(normed, grad_mix, grad_both, mixed, rest, mlp_low, mlp_high, mixer_w, tokens, gain)


def gather_plain(mixer, gate, up, down):
    groups = lax.axis_size("fsdp")
    part_rows, ff = gate.shape
    own = jnp.stack([w.reshape(part_rows, groups, ff // groups) for w in (gate, up, down)], axis=2)
    mine = lax.all_to_all(jnp.transpose(own, (1, 0, 2, 3)), "fsdp", 0, 0, tiled=True)
    return lax.all_gather(mixer, both, axis=0, tiled=True), mine.reshape(groups * part_rows, -1)


def from_line(shard):
    count = lax.axis_size("fsdp")
    return [shard] + [
        lax.ppermute(shard, "fsdp", [(i, (i + k) % count) for i in range(count)]) for k in range(1, count)
    ]


def swap_cores(shard):
    count = lax.axis_size("seq")
    return lax.ppermute(shard, "seq", [(i, i + 1 - 2 * (i % 2)) for i in range(count)])


def swap_beside(shard):
    return lax.ppermute(shard, "seq", [(i, i ^ 2) for i in range(8)])


def swap_across(shard):
    return lax.ppermute(shard, "seq", [(i, i ^ 4) for i in range(8)])


def add_low(left, right):
    return (left.astype(f32) + right.astype(f32)).astype(bf16)


def scatter_plain(normed, grad_both, grad_mix, mixed, rest, mlp_sum):
    groups = lax.axis_size("fsdp")
    term_wide = mm(normed, grad_both, ((0,), (0,))).astype(bf16)
    term_out = mm(grad_mix, mixed, ((0,), (0,))).astype(bf16)
    mixer_sum = lax.psum_scatter(
        jnp.concatenate([term_wide, term_out, rest], axis=1), "seq", scatter_dimension=0, tiled=True
    )
    mixer_sum = lax.psum_scatter(mixer_sum, "fsdp", scatter_dimension=0, tiled=True)
    ff_part = mlp_sum.shape[1] // 3
    part_rows = mlp_sum.shape[0] // groups
    mlp_sum = mlp_sum.reshape(groups, part_rows, 3, ff_part)
    mlp_back = lax.all_to_all(mlp_sum, "fsdp", 0, 0, tiled=True)
    mlp_back = jnp.transpose(mlp_back, (2, 1, 0, 3)).reshape(3, part_rows, groups * ff_part)
    return mixer_sum, mlp_back


def call_heads(kernel, width, heads, ins, outs, scratch, name):
    def spec(rows_cols):
        rows, by_row = rows_cols
        if by_row:
            return pl.BlockSpec((rows, width), lambda h: (h, 0))
        return pl.BlockSpec((rows, width), lambda h: (0, h))

    in_specs = [spec((width, True)) if rowwise else spec((a.shape[0], False)) for a, rowwise in ins]
    out_specs = [spec((width, True)) if rowwise else spec((rows, False)) for rows, _, rowwise in outs]
    out_shape = [
        jax.ShapeDtypeStruct((heads * width, width) if rowwise else (rows, heads * width), kind)
        for rows, kind, rowwise in outs
    ]
    return pl.pallas_call(
        kernel,
        grid=(heads,),
        in_specs=in_specs,
        out_specs=out_specs,
        out_shape=out_shape,
        scratch_shapes=[pltpu.VMEM((rows, width), f32) for rows in scratch],
        compiler_params=pltpu.CompilerParams(vmem_limit_bytes=40 * 1024 * 1024),
        cost_estimate=pl.CostEstimate(flops=1, bytes_accessed=1, transcendentals=0),
        name=name,
    )(*[a for a, _ in ins])


def on_device(
    block_input,
    cotangent,
    mixer_gain,
    branch_proj,
    gelu_proj,
    conv_taps,
    conv_bias,
    rate_blocks,
    input_blocks,
    rate_bias,
    input_bias,
    decay_param,
    out_proj,
    mlp_gain,
    gate_proj,
    up_proj,
    down_proj,
):
    groups = lax.axis_size("fsdp")
    part_rows, lru = branch_proj.shape
    width = rate_blocks.shape[1]
    heads = lru // width
    margin = conv_taps.shape[0] - 1
    tokens = block_input[0].astype(f32)
    tok_count, model = tokens.shape
    ff = gate_proj.shape[1]
    ff_part = ff // groups
    grad_out = cotangent[0]

    smalls = jnp.stack(
        [conv_taps[k] for k in range(margin + 1)]
        + [conv_bias, rate_bias, input_bias, decay_param, mixer_gain, mlp_gain],
        axis=1,
    )
    small_count = smalls.shape[1]
    smalls = jnp.pad(smalls, ((0, 0), (0, 128 - small_count)))
    first_own = jnp.concatenate([smalls, rate_blocks, input_blocks], axis=1)
    mixer_own = (first_own, branch_proj, gelu_proj, out_proj)
    custom = lax.axis_size("seq") == 8 and groups == 4
    if custom:
        mixer_w, mlp_mine = gather(*mixer_own, gate_proj, up_proj, down_proj)
    else:
        mixer_w, mlp_mine = gather_plain(jnp.concatenate(mixer_own, axis=1), gate_proj, up_proj, down_proj)
    mlp_w = lax.all_gather(mlp_mine, "seq", axis=0, tiled=True)
    grad_out_late = lax.optimization_barrier((grad_out, mlp_mine))[0]
    if custom:
        grad_pieces = from_line(grad_out_late)
    first = lax.optimization_barrier(mixer_w[:, : 128 + 2 * width])
    wide = mixer_w[:, 128 + 2 * width : 128 + 2 * width + 2 * lru]
    proj_out = mixer_w[:, 128 + 2 * width + 2 * lru :]

    table = first[:, :small_count].astype(f32).T
    blocks_rate = first[:, 128 : 128 + width]
    blocks_input = first[:, 128 + width :]
    param_decay = table[margin + 4]
    gain_one = table[margin + 5]
    gain_two = table[margin + 6]
    small = jnp.concatenate(
        [
            table[: margin + 4],
            jax.nn.softplus(-param_decay)[None],
            -jax.nn.sigmoid(-param_decay)[None],
            jnp.zeros((16 - margin - 6, lru), f32),
        ],
        axis=0,
    )

    normed = norm_rows(tokens, gain_one).astype(bf16)
    both_pre = mm(normed, wide, ((1,), (0,)))
    branch = both_pre[:, :lru].astype(bf16)
    gelu_pre = both_pre[:, lru:]
    prior = from_behind(branch[tok_count - margin :], "seq", 1).astype(f32)
    prior = jnp.concatenate([jnp.zeros((8 - margin, lru), f32), prior], axis=0)
    conv, rate_pre, input_pre, cum, local = call_heads(
        mixer_forward,
        width,
        heads,
        [(branch, False), (prior, False), (small, False), (blocks_rate, True), (blocks_input, True)],
        [(tok_count, bf16, False)] + [(tok_count, f32, False)] * 4,
        [tok_count + 8],
        "mixer_forward",
    )
    carried = prefix((cum[-1], local[-1]), "seq", False)
    states = local + cum * carried[None]
    mixed = (states * jax.nn.gelu(gelu_pre, approximate=True)).astype(bf16)
    middle = tokens + mm(mixed, proj_out, ((1,), (1,)))
    normed_two = norm_rows(middle, gain_two).astype(bf16)

    if custom:
        normed_all, normed_other, grad_out_all, grad_out_other = gather_rows(normed_two, grad_pieces)
    else:
        normed_all = lax.all_gather(normed_two, "fsdp", axis=0, tiled=True)
        grad_out_all = lax.all_gather(grad_out_late, "fsdp", axis=0, tiled=True)
    w_gate, w_up, w_down = mlp_w[:, :ff_part], mlp_w[:, ff_part : 2 * ff_part], mlp_w[:, 2 * ff_part :]
    if custom:
        hidden, hidden_other, grad_pair, pair_other, grad_normed_part = feed_forward(
            normed_all, grad_out_all, mlp_w
        )
    else:
        gate = mm(normed_all, w_gate, ((1,), (0,)))
        up_val = mm(normed_all, w_up, ((1,), (0,)))
        gelu_gate, gelu_slope = gelu_parts(gate)
        hidden = (gelu_gate * up_val).astype(bf16)
        grad_hidden = mm(grad_out_all, w_down, ((1,), (0,)))
        grad_gate = (grad_hidden * up_val * gelu_slope).astype(bf16)
        grad_up = (grad_hidden * gelu_gate).astype(bf16)
        grad_normed_part = (
            mm(grad_gate, w_gate, ((1,), (1,))) + mm(grad_up, w_up, ((1,), (1,)))
        ).astype(bf16)
    grad_normed_two = lax.psum_scatter(grad_normed_part, "fsdp", scatter_dimension=0, tiled=True)
    if custom:
        half = model // 16
        beside_high, across_low, mine, beside_low, across_high, out_part = shared_products(
            (normed_all, normed_other, grad_out_all, grad_out_other),
            mlp_w,
            (grad_pair, pair_other),
            (hidden, hidden_other),
        )
        from_beside_high, from_across_low = swap_beside(beside_high), swap_across(across_low)
    else:
        grad_pair = jnp.concatenate([grad_gate, grad_up], axis=1)
        term_pair = mm(normed_all, grad_pair, ((0,), (0,))).astype(bf16)
        term_down = mm(grad_out_all, hidden, ((0,), (0,))).astype(bf16)
        pair_sum = lax.psum_scatter(term_pair, "seq", scatter_dimension=0, tiled=True)
        down_sum = lax.psum_scatter(term_down, "seq", scatter_dimension=0, tiled=True)
        mlp_sum = jnp.concatenate([pair_sum, down_sum], axis=1)
        out_part = mm(hidden, w_down, ((1,), (1,))).astype(bf16)
    out_sum = lax.psum_scatter(out_part, "fsdp", scatter_dimension=0, tiled=True)
    grad_normed_two = grad_normed_two.astype(f32)

    grad_middle = grad_out.astype(f32) + norm_back(middle, gain_two, grad_normed_two)
    grad_mix = grad_middle.astype(bf16)
    grad_mixed = mm(grad_mix, proj_out, ((1,), (0,)))
    carried_rows = jnp.broadcast_to(carried[None], (8, lru))
    grad_gelu_pre, rev_cum, rev_grad, pair_grad = call_heads(
        mixer_backward_scan,
        width,
        heads,
        [(a, False) for a in (grad_mixed, gelu_pre, rate_pre, cum, local, carried_rows, small)],
        [(tok_count, bf16, False), (tok_count, f32, False), (tok_count, f32, False), (8, f32, False)],
        [tok_count + 8],
        "mixer_backward_scan",
    )
    if custom:
        from_beside_high, from_across_low, pair_grad = lax.optimization_barrier(
            (from_beside_high, from_across_low, pair_grad)
        )
    incoming = prefix((cum[-1], pair_grad[0]), "seq", True)
    if custom:
        beside_low, across_high, incoming = lax.optimization_barrier((beside_low, across_high, incoming))
        from_beside_low, from_across_high = swap_beside(beside_low), swap_across(across_high)
    incoming_rows = jnp.broadcast_to(incoming[None], (8, lru))
    own, head, rate_w_grad, input_w_grad, sums = call_heads(
        mixer_backward,
        width,
        heads,
        [
            (a, False)
            for a in (rev_cum, rev_grad, incoming_rows, cum, local, carried_rows, rate_pre, input_pre, conv, branch, prior, small)
        ]
        + [(blocks_rate, True), (blocks_input, True)],
        [(tok_count, f32, False), (8, f32, False), (0, bf16, True), (0, bf16, True), (8, f32, False)],
        [tok_count + 8, tok_count + 16],
        "mixer_backward",
    )
    received = from_behind(head[8 - margin :], "seq", -1)
    grad_branch = jnp.concatenate(
        [own[: tok_count - margin], own[tok_count - margin :] + received], axis=0
    ).astype(bf16)
    grad_both = jnp.concatenate([grad_branch, grad_gelu_pre], axis=1)
    middle, out_sum, sums = lax.optimization_barrier((middle, out_sum, sums))
    block_output = (middle + out_sum.astype(f32)).astype(bf16)[None]
    vectors = jnp.pad(sums.T, ((0, 0), (0, 128 - sums.shape[0]))).astype(bf16)
    rest = jnp.concatenate([rate_w_grad, input_w_grad, vectors], axis=1)
    if custom:
        mlp_parts = (
            (mine[:half], from_across_low, from_beside_low),
            (mine[half:], from_across_high, from_beside_high),
        )
        low, high = [sum(part.astype(f32) for part in parts).astype(bf16) for parts in mlp_parts]
        gain_rows = jnp.broadcast_to(gain_one[None], (8, model))
        mixer_sum, mlp_back, input_grad = scatter(
            normed, grad_mix, grad_both, mixed, rest, low, high, mixer_w, block_input[0], gain_rows
        )
    else:
        mixer_sum, mlp_back = scatter_plain(normed, grad_both, grad_mix, mixed, rest, mlp_sum)
        grad_normed = mm(grad_both, wide, ((1,), (1,)))
        input_grad = (grad_middle + norm_back(tokens, gain_one, grad_normed)).astype(bf16)
    input_grad = input_grad[None]
    mlp_grads = [mlp_back[m].astype(f32) for m in range(3)]
    mixer_sum = mixer_sum.astype(f32)
    edges = [lru, 2 * lru, 3 * lru, 3 * lru + width, 3 * lru + 2 * width]
    dbranch, dgelu, dout, drate, dinput, vec = jnp.split(mixer_sum, edges, axis=1)
    vec = vec.T
    return (
        block_output,
        input_grad,
        gain_back(mixer_gain, (branch_proj, dbranch), (gelu_proj, dgelu)),
        dbranch,
        dgelu,
        vec[: margin + 1],
        vec[7],
        drate,
        dinput,
        vec[4],
        vec[5],
        vec[6],
        dout,
        gain_back(mlp_gain, (gate_proj, mlp_grads[0]), (up_proj, mlp_grads[1])),
        mlp_grads[0],
        mlp_grads[1],
        mlp_grads[2],
    )


def solution(mesh):
    tokens = P("fsdp", "seq", None)
    vector = P(both)
    matrix = P(both, None)
    taps = P(None, both)
    return jax.shard_map(
        on_device,
        mesh=mesh,
        in_specs=(
            tokens, tokens, vector, matrix, matrix, taps, vector, matrix, matrix,
            vector, vector, vector, matrix, vector, matrix, matrix, matrix,
        ),
        out_specs=(
            tokens, tokens, vector, matrix, matrix, taps, vector, matrix, matrix,
            vector, vector, vector, matrix, vector, matrix, matrix, matrix,
        ),
        check_vma=False,
    )
```

```python
import functools

import jax
import jax.numpy as jnp
from jax import lax
from jax.experimental import pallas as pl
from jax.experimental.pallas import tpu as pltpu
from jax.sharding import PartitionSpec as P

epsilon = 1e-06
f32 = jnp.float32
bf16 = jnp.bfloat16
both = ("seq", "fsdp")
MESH = pl.DeviceIdType.MESH
TAP, CONV_BIAS, RATE_BIAS, INPUT_BIAS, SOFT, SOFT_SLOPE = 0, 4, 5, 6, 7, 8
GELU_C = 0.7978845608028654
GELU_A = 0.044715


def from_behind(shard, axis, by):
    devices = lax.axis_size(axis)
    pairs = [(i, i + by) for i in range(devices) if 0 <= i + by < devices]
    return lax.ppermute(shard, axis, pairs)


def prefix(part, axis, reverse):
    count = lax.axis_size(axis)
    place = lax.axis_index(axis)
    gathered = lax.all_gather(jnp.stack(part), axis)
    state = jnp.zeros_like(part[1])
    for hop in range(count):
        source = count - 1 - hop if reverse else hop
        ahead = source > place if reverse else source < place
        state = jnp.where(ahead, gathered[source, 1] + gathered[source, 0] * state, state)
    return state


def norm_rows(values, scales):
    return values * lax.rsqrt(jnp.mean(values * values, axis=-1, keepdims=True) + epsilon) * scales


def norm_back(values, scales, grads):
    inverse = lax.rsqrt(jnp.mean(values * values, axis=-1, keepdims=True) + epsilon)
    scaled = grads * scales
    shared = jnp.mean(values * scaled, axis=-1, keepdims=True)
    return inverse * scaled - values * (inverse * inverse * inverse * shared)


def gain_back(gain, *pairs):
    total = sum(jnp.sum(weight.astype(f32) * grad, axis=1) for weight, grad in pairs)
    return total / gain.astype(f32)


def gelu_parts(x):
    inner = jnp.tanh(GELU_C * (x + GELU_A * x * x * x))
    return 0.5 * x * (1.0 + inner), 0.5 * (1.0 + inner) + 0.5 * x * (1.0 - inner * inner) * (
        GELU_C * (1.0 + 3.0 * GELU_A * x * x)
    )


def mm(left, right, dims):
    return lax.dot_general(left, right, (dims, ((), ())), preferred_element_type=f32)


def sigmoid(x):
    return 1.0 / (1.0 + jnp.exp(-x))


def scan_rows(decay, value, reverse):
    rows = decay.shape[0]
    place = lax.broadcasted_iota(jnp.int32, decay.shape, 0)
    step = 1
    while step < rows:
        shift = rows - step if reverse else step
        inside = place < rows - step if reverse else place >= step
        before_value = jnp.where(inside, pltpu.roll(value, shift, 0), 0.0)
        before_decay = jnp.where(inside, pltpu.roll(decay, shift, 0), 1.0)
        value = value + decay * before_value
        decay = decay * before_decay
        step *= 2
    return decay, value


def gates(rate_pre, input_pre, soft):
    rate = sigmoid(rate_pre)
    log_decay = -8.0 * rate * soft
    decay = jnp.exp(log_decay)
    square = decay * decay
    root = jnp.sqrt(-jnp.tanh(log_decay) * (1.0 + square))
    return rate, decay, square, root, sigmoid(input_pre)


def mixer_forward(branch, prior, small, rate_w, input_w, conv, rate_pre, input_pre, cum, local, ext):
    rows = branch.shape[0]
    ext[0:8, :] = prior[...]
    ext[8:, :] = branch[...].astype(f32)
    total = small[CONV_BIAS : CONV_BIAS + 1, :] + small[TAP : TAP + 1, :] * ext[8:, :]
    for offset in range(1, 4):
        total = total + small[TAP + offset : TAP + offset + 1, :] * ext[pl.ds(8 - offset, rows), :]
    low = total.astype(bf16)
    conv[...] = low
    rate = mm(low, rate_w[...], ((1,), (0,))) + small[RATE_BIAS : RATE_BIAS + 1, :]
    inp = mm(low, input_w[...], ((1,), (0,))) + small[INPUT_BIAS : INPUT_BIAS + 1, :]
    rate_pre[...] = rate
    input_pre[...] = inp
    _, decay, _, root, opened = gates(rate, inp, small[SOFT : SOFT + 1, :])
    product, states = scan_rows(decay, root * opened * low.astype(f32), False)
    cum[...] = product
    local[...] = states


def mixer_backward_scan(grad_mixed, gelu_pre, rate_pre, cum, local, carried, small, grad_pre, rev_cum, rev_grad, pair, ext):
    rows = grad_mixed.shape[0]
    states = local[...] + cum[...] * carried[0:1, :]
    value, slope = gelu_parts(gelu_pre[...])
    grad = grad_mixed[...]
    grad_pre[...] = (grad * states * slope).astype(bf16)
    decay = jnp.exp(-8.0 * sigmoid(rate_pre[...]) * small[SOFT : SOFT + 1, :])
    ext[0:rows, :] = decay
    ext[rows:, :] = jnp.ones((8, decay.shape[1]), f32)
    product, back = scan_rows(ext[pl.ds(1, rows), :], grad * value, True)
    rev_cum[...] = product
    rev_grad[...] = back
    pair[...] = jnp.broadcast_to(decay[0:1, :] * back[0:1, :], pair.shape)


def mixer_backward(
    rev_cum, rev_grad, incoming, cum, local, carried, rate_pre, input_pre, conv, branch, prior, small, rate_w, input_w,
    own, head, rate_w_grad, input_w_grad, sums, ext, gext,
):
    rows = rev_cum.shape[0]
    soft = small[SOFT : SOFT + 1, :]
    grad_states = rev_grad[...] + rev_cum[...] * incoming[0:1, :]
    rate, decay, square, root, opened = gates(rate_pre[...], input_pre[...], soft)
    ext[0:8, :] = jnp.broadcast_to(carried[0:1, :], (8, carried.shape[1]))
    ext[8:, :] = local[...] + cum[...] * carried[0:1, :]
    before = ext[pl.ds(7, rows), :]
    low = conv[...]
    conv_in = low.astype(f32)
    grad_log = grad_states * decay * before - grad_states * opened * conv_in * square / root
    driven = grad_states * root
    grad_input = (driven * conv_in * opened * (1.0 - opened)).astype(bf16)
    by_rate = grad_log * (-8.0 * rate)
    grad_rate = (by_rate * soft * (1.0 - rate)).astype(bf16)
    sums[6:7, :] = jnp.sum(by_rate, axis=0, keepdims=True) * small[SOFT_SLOPE : SOFT_SLOPE + 1, :]
    sums[4:5, :] = jnp.sum(grad_rate.astype(f32), axis=0, keepdims=True)
    sums[5:6, :] = jnp.sum(grad_input.astype(f32), axis=0, keepdims=True)
    rate_w_grad[...] = mm(low, grad_rate, ((0,), (0,))).astype(rate_w_grad.dtype)
    input_w_grad[...] = mm(low, grad_input, ((0,), (0,))).astype(input_w_grad.dtype)
    grad_conv = (
        driven * opened
        + mm(grad_rate, rate_w[...], ((1,), (1,)))
        + mm(grad_input, input_w[...], ((1,), (1,)))
    )
    sums[7:8, :] = jnp.sum(grad_conv, axis=0, keepdims=True)
    ext[0:8, :] = prior[...]
    ext[8:, :] = branch[...].astype(f32)
    gext[0:8, :] = jnp.zeros((8, grad_conv.shape[1]), f32)
    gext[8 : 8 + rows, :] = grad_conv
    gext[8 + rows :, :] = jnp.zeros((8, grad_conv.shape[1]), f32)
    back = jnp.zeros_like(grad_conv)
    front = jnp.zeros((8, grad_conv.shape[1]), f32)
    for offset in range(4):
        tap = small[TAP + offset : TAP + offset + 1, :]
        sums[offset : offset + 1, :] = jnp.sum(
            grad_conv * ext[pl.ds(8 - offset, rows), :], axis=0, keepdims=True
        )
        back = back + tap * gext[pl.ds(8 + offset, rows), :]
        front = front + tap * gext[pl.ds(offset, 8), :]
    own[...] = back
    head[...] = front


def places():
    s = lax.axis_index("seq")
    z = lax.axis_index("fsdp")
    core = s + 1 - 2 * (s % 2)
    beside = s + 2 - 4 * ((s // 2) % 2)
    across = s + 4 - 8 * (s // 4)
    return s, z, core, beside, across


def greet(peers):
    barrier = pltpu.get_barrier_semaphore()
    for peer in peers:
        pl.semaphore_signal(barrier, inc=1, device_id=peer, device_id_type=MESH)
    pl.semaphore_wait(barrier, len(peers))


def gather_kernel(
    first, branch, gelu, outer, gate, up, down, mixer_all, mlp_mine,
    mixer, load_sem, flow_send, flow_recv, line_send, line_recv, swap_send, swap_recv, own_sem,
):
    s, z, core, beside, across = places()
    rows, cols = mixer.shape
    ff_part = mlp_mine.shape[1] // 3
    cut = cols // 256 * 128
    diag = beside + across - s
    loads, start = [], 0
    for n, part in enumerate((first, branch, gelu, outer)):
        size = part.shape[1]
        loads.append(pltpu.make_async_copy(part, mixer.at[:, pl.ds(start, size)], load_sem.at[n]))
        loads[-1].start()
        start += size
    greet([(core, z), (beside, z), (across, z)] + [(s, (z + k) % 4) for k in range(1, 4)])

    def remote(src, dst, send, recv, target):
        return pltpu.make_async_remote_copy(
            src_ref=src, dst_ref=dst, send_sem=send, recv_sem=recv, device_id=target, device_id_type=MESH
        )

    def piece(seq, zz, half=None):
        span = pl.ds(pl.multiple_of((seq * 4 + zz) * rows, 16), rows)
        if half is None:
            return mixer_all.at[span, :]
        return mixer_all.at[span, pl.ds(0, cut) if half == 0 else pl.ds(cut, cols - cut)]

    def flow(zz, index, seq, half, target, src=None):
        ref = piece(seq, zz, half)
        return remote(
            ref if src is None else src, ref, flow_send.at[zz, index], flow_recv.at[zz, index], (target, z)
        )

    def sends(zz, src=None):
        return [
            flow(zz, 0, s, None, beside, src),
            flow(zz, 1, s, None, across, src),
            flow(zz, 4, s, None, core, src),
        ]

    def spread(zz, src=None):
        for copy in sends(zz, src):
            copy.start()

    def relay(zz):
        flow(zz, 0, beside, None, beside).wait_recv()
        flow(zz, 3, beside, 0, across).start()
        flow(zz, 5, beside, None, core).start()
        flow(zz, 1, across, None, across).wait_recv()
        flow(zz, 2, across, 1, beside).start()
        flow(zz, 6, across, None, core).start()

    def finish(zz):
        flow(zz, 3, diag, 0, across).wait_recv()
        flow(zz, 7, diag, 0, core).start()
        flow(zz, 2, diag, 1, beside).wait_recv()
        flow(zz, 8, diag, 1, core).start()

    def drain(zz, src=None):
        for copy in sends(zz, src):
            copy.wait_send()
        flow(zz, 3, beside, 0, across).wait_send()
        flow(zz, 5, beside, None, core).wait_send()
        flow(zz, 2, across, 1, beside).wait_send()
        flow(zz, 6, across, None, core).wait_send()
        flow(zz, 7, diag, 0, core).wait_send()
        flow(zz, 8, diag, 1, core).wait_send()
        flip = core - s
        flow(zz, 4, core, None, core).wait_recv()
        flow(zz, 5, beside + flip, None, core).wait_recv()
        flow(zz, 6, across + flip, None, core).wait_recv()
        flow(zz, 7, diag + flip, 0, core).wait_recv()
        flow(zz, 8, diag + flip, 1, core).wait_recv()

    def line(zz, up_way, hop, src=None):
        ref = piece(s, zz)
        way = 0 if up_way else 1
        target = z + 1 if up_way else z - 1
        return remote(
            ref if src is None else src, ref, line_send.at[way, hop], line_recv.at[way, hop], (s, target)
        )

    def line_hop(hop):
        def below():
            line(z - hop, True, hop - 1).wait_recv()
            pl.when(z < 3)(lambda: line(z - hop, True, hop).start())

        def above():
            line(z + hop, False, hop - 1).wait_recv()
            pl.when(z > 0)(lambda: line(z + hop, False, hop).start())

        pl.when(z >= hop)(below)
        pl.when(z + hop <= 3)(above)

    def at_hop(hop, act):
        pl.when(z >= hop)(lambda: act(z - hop))
        pl.when(z + hop <= 3)(lambda: act(z + hop))

    def landing(m, zz):
        return mlp_mine.at[pl.ds(pl.multiple_of(zz * rows, 16), rows), pl.ds(m * ff_part, ff_part)]

    def columns(m, zz):
        return (gate, up, down)[m].at[:, pl.ds(pl.multiple_of(zz * ff_part, 128), ff_part)]

    def swap(k, m, arriving=False):
        to = (z + k) % 4
        came = (z + 4 - k) % 4
        return remote(
            columns(m, to), landing(m, came if arriving else z), swap_send.at[k - 1, m], swap_recv.at[k - 1, m], (s, to)
        )

    local = [pltpu.make_async_copy(columns(m, z), landing(m, z), own_sem.at[m]) for m in range(3)]
    local.append(pltpu.make_async_copy(mixer, piece(s, z), own_sem.at[3]))
    for copy in loads:
        copy.wait()

    pl.when(z < 3)(lambda: line(z, True, 0, mixer).start())
    pl.when(z > 0)(lambda: line(z, False, 0, mixer).start())
    spread(z, mixer)
    for copy in local:
        copy.start()
    line_hop(1)
    at_hop(1, spread)
    relay(z)
    line_hop(2)
    at_hop(2, spread)
    finish(z)
    at_hop(1, relay)
    line_hop(3)
    at_hop(3, spread)
    for k in (1, 3, 2):
        for m in range(3):
            swap(k, m).start()
    at_hop(1, finish)
    at_hop(2, relay)
    at_hop(3, relay)
    at_hop(2, finish)
    at_hop(3, finish)
    drain(z, mixer)
    for hop in range(1, 4):
        at_hop(hop, drain)
    for copy in local:
        copy.wait()
    for k in (1, 3, 2):
        for m in range(3):
            swap(k, m).wait_send()
            swap(k, m, True).wait_recv()
    pl.when(z < 3)(lambda: line(z, True, 0, mixer).wait_send())
    pl.when(z > 0)(lambda: line(z, False, 0, mixer).wait_send())
    for hop in range(1, 3):
        pl.when((z >= hop) & (z < 3))(lambda: line(z - hop, True, hop).wait_send())
        pl.when((z + hop <= 3) & (z > 0))(lambda: line(z + hop, False, hop).wait_send())


def gather(first, branch, gelu, outer, gate, up, down):
    rows = first.shape[0]
    cols = first.shape[1] + branch.shape[1] + gelu.shape[1] + outer.shape[1]
    ff_part = gate.shape[1] // 4
    anyspec = pl.BlockSpec(memory_space=pl.ANY)
    dma = pltpu.SemaphoreType.DMA
    return pl.pallas_call(
        gather_kernel,
        in_specs=[anyspec] * 7,
        out_specs=[anyspec] * 2,
        out_shape=[
            jax.ShapeDtypeStruct((32 * rows, cols), bf16),
            jax.ShapeDtypeStruct((4 * rows, 3 * ff_part), bf16),
        ],
        scratch_shapes=[
            pltpu.VMEM((rows, cols), bf16), dma((4,)),
            dma((4, 9)), dma((4, 9)), dma((2, 3)), dma((2, 3)), dma((3, 3)), dma((3, 3)), dma((4,)),
        ],
        compiler_params=pltpu.CompilerParams(collective_id=1, has_side_effects=True),
        name="gather_weights",
    )(first, branch, gelu, outer, gate, up, down)


def rows_kernel(
    normed, grad0, grad1, grad2, grad3, first, mixed, normed_all, normed_other, grad_all, grad_other,
    first_other, mixed_other, line_send, line_recv, core_send, core_recv, own_sem, held, give_send, give_recv,
):
    s, z, core, _, _ = places()
    tok = normed.shape[0]
    cuts = 4
    grads = (grad0, grad1, grad2, grad3)
    greet([(core, z)] + [(s, (z + k) % 4) for k in range(1, 4)])

    def rows(ref, zz):
        return ref.at[pl.ds(pl.multiple_of(zz * tok, 16), tok), :]

    def remote(src, dst, send, recv, target):
        return pltpu.make_async_remote_copy(
            src_ref=src, dst_ref=dst, send_sem=send, recv_sem=recv, device_id=target, device_id_type=MESH
        )

    def parts(ref):
        size = tok // cuts
        return [ref.at[pl.ds(n * size, size), :] for n in range(cuts)]

    def line(zz, up_way, hop):
        way = 0 if up_way else 1
        target = z + 1 if up_way else z - 1
        src = normed if hop == 0 else rows(normed_all, zz)
        dst = rows(normed_all, zz)
        return [
            remote(a, b, line_send.at[way, hop, n], line_recv.at[way, hop, n], (s, target))
            for n, (a, b) in enumerate(zip(parts(src), parts(dst)))
        ]

    def over(zz, own=False):
        src = normed if own else rows(normed_all, zz)
        return remote(src, rows(normed_other, zz), core_send.at[0, zz], core_recv.at[0, zz], (core, z))

    def grad_over(k):
        zz = (z + 4 - k) % 4
        return remote(grads[k], rows(grad_other, zz), core_send.at[1, zz], core_recv.at[1, zz], (core, z))

    def line_start(zz, up_way, hop):
        for copy in line(zz, up_way, hop):
            copy.start()

    def line_drain(zz, up_way, hop):
        for copy in line(zz, up_way, hop):
            copy.wait_send()

    def hop_step(hop):
        def below():
            for came, on in zip(line(z - hop, True, hop - 1), line(z - hop, True, hop) if hop < 3 else [None] * cuts):
                came.wait_recv()
                if on is not None:
                    pl.when(z < 3)(on.start)
            over(z - hop).start()

        def above():
            for came, on in zip(line(z + hop, False, hop - 1), line(z + hop, False, hop) if hop < 3 else [None] * cuts):
                came.wait_recv()
                if on is not None:
                    pl.when(z > 0)(on.start)
            over(z + hop).start()

        pl.when(z >= hop)(below)
        pl.when(z + hop <= 3)(above)

    given = [
        remote(source, target, give_send.at[n], give_recv.at[n], (core, z))
        for n, (source, target) in enumerate(((first, first_other), (mixed, mixed_other)))
    ]
    local = [pltpu.make_async_copy(grads[k], held.at[k], own_sem.at[k]) for k in range(4)]
    local.append(pltpu.make_async_copy(normed, held.at[4], own_sem.at[4]))
    stored = [
        pltpu.make_async_copy(held.at[k], rows(grad_all, (z + 4 - k) % 4), own_sem.at[k]) for k in range(4)
    ]
    stored.append(pltpu.make_async_copy(held.at[4], rows(normed_all, z), own_sem.at[4]))
    pl.when(z < 3)(lambda: line_start(z, True, 0))
    pl.when(z > 0)(lambda: line_start(z, False, 0))
    over(z, True).start()
    for copy in local:
        copy.start()
    for k in range(4):
        grad_over(k).start()
    for copy in given:
        copy.start()
    for copy, store in zip(local, stored):
        copy.wait()
        store.start()
    for hop in range(1, 4):
        hop_step(hop)
    for copy in stored:
        copy.wait()
    for k in range(4):
        grad_over(k).wait()
    for copy in given:
        copy.wait()
    over(z, True).wait()
    for k in range(1, 4):
        over((z + k) % 4).wait()
    pl.when(z < 3)(lambda: line_drain(z, True, 0))
    pl.when(z > 0)(lambda: line_drain(z, False, 0))
    for hop in range(1, 3):
        pl.when((z >= hop) & (z < 3))(lambda: line_drain(z - hop, True, hop))
        pl.when((z + hop <= 3) & (z > 0))(lambda: line_drain(z + hop, False, hop))


def gather_rows(normed, grads, first, mixed):
    tok, model = normed.shape
    anyspec = pl.BlockSpec(memory_space=pl.ANY)
    dma = pltpu.SemaphoreType.DMA
    return pl.pallas_call(
        rows_kernel,
        in_specs=[anyspec] * 7,
        out_specs=[anyspec] * 6,
        out_shape=[jax.ShapeDtypeStruct((4 * tok, model), bf16)] * 4
        + [jax.ShapeDtypeStruct(first.shape, bf16), jax.ShapeDtypeStruct(mixed.shape, bf16)],
        scratch_shapes=[
            dma((2, 3, 4)), dma((2, 3, 4)), dma((2, 4)), dma((2, 4)), dma((5,)),
            pltpu.VMEM((5, tok, model), bf16), dma((2,)), dma((2,)),
        ],
        compiler_params=pltpu.CompilerParams(collective_id=3, has_side_effects=True),
        name="gather_rows",
    )(normed, *grads, first, mixed)


def column_tiles(cols, size=512):
    return [(start, min(size, cols - start)) for start in range(0, cols, size)]


def feed_forward_kernel(
    normed, grad_out, weights, hidden, hidden_other, pair, pair_other, back,
    held, hidden_now, pair_now, sems, store_sem, core_send, core_recv,
):
    s, z, core, _, _ = places()
    step = pl.program_id(0)
    ff_part = held.shape[2]
    model = held.shape[1]
    rows = normed.shape[0]
    tiles = column_tiles(ff_part)
    made = ((hidden_now, hidden, hidden_other), (pair_now, pair, pair_other))

    def load(n, m):
        start, size = tiles[n]
        return pltpu.make_async_copy(
            weights.at[:, pl.ds(m * ff_part + start, size)], held.at[m, :, pl.ds(start, size)], sems.at[n, m]
        )

    def kept(n, turn):
        now, mine, _ = made[n]
        return pltpu.make_async_copy(now.at[turn], mine.at[pl.ds(turn * rows, rows), :], store_sem.at[turn, n])

    def handed(n, turn):
        now, _, other = made[n]
        return pltpu.make_async_remote_copy(
            src_ref=now.at[turn],
            dst_ref=other.at[pl.ds(turn * rows, rows), :],
            send_sem=core_send.at[turn, n],
            recv_sem=core_recv.at[turn, n],
            device_id=(core, z),
            device_id_type=MESH,
        )

    @pl.when(step == 0)
    def _():
        for n in range(len(tiles)):
            for m in range(3):
                load(n, m).start()
        greet([(core, z)])

    for n, (start, size) in enumerate(tiles):
        cols = slice(start, start + size)

        @pl.when(step == 0)
        def _(n=n):
            for m in range(3):
                load(n, m).wait()

        gate = mm(normed[...], held[0, :, cols], ((1,), (0,)))
        value, slope = gelu_parts(gate)
        up = mm(normed[...], held[1, :, cols], ((1,), (0,)))
        hidden_now[step, :, cols] = (value * up).astype(bf16)
        grad_hidden = mm(grad_out[...], held[2, :, cols], ((1,), (0,)))
        pair_now[step, :, cols] = (grad_hidden * up * slope).astype(bf16)
        pair_now[step, :, slice(ff_part + start, ff_part + start + size)] = (grad_hidden * value).astype(bf16)

    for turn in range(2):

        @pl.when(step == turn)
        def _(turn=turn):
            for n in range(2):
                handed(n, turn).start()
                kept(n, turn).start()

    def back_tile(turn, carry):
        cols = pl.ds(pl.multiple_of(turn * 512, 512), 512)
        total = mm(pair_now[step, :, :ff_part], held[0, cols, :], ((1,), (1,)))
        total = total + mm(pair_now[step, :, ff_part:], held[1, cols, :], ((1,), (1,)))
        back[:, cols] = total.astype(bf16)
        return carry

    lax.fori_loop(0, model // 512, back_tile, 0)

    @pl.when(step == 1)
    def _():
        for turn in range(2):
            for n in range(2):
                kept(n, turn).wait()
                handed(n, turn).wait()


def feed_forward(normed, grad_out, weights):
    tok, model = normed.shape
    ff_part = weights.shape[1] // 3
    rows = tok // 2
    anyspec = pl.BlockSpec(memory_space=pl.ANY)
    dma = pltpu.SemaphoreType.DMA
    block = pl.BlockSpec((rows, model), lambda i: (i, 0))
    return pl.pallas_call(
        feed_forward_kernel,
        grid=(2,),
        in_specs=[block, block, anyspec],
        out_specs=[anyspec] * 4 + [block],
        out_shape=[
            jax.ShapeDtypeStruct((tok, cols), bf16)
            for cols in (ff_part, ff_part, 2 * ff_part, 2 * ff_part, model)
        ],
        scratch_shapes=[
            pltpu.VMEM((3, model, ff_part), bf16),
            pltpu.VMEM((2, rows, ff_part), bf16),
            pltpu.VMEM((2, rows, 2 * ff_part), bf16),
            dma((len(column_tiles(ff_part)), 3)), dma((2, 2)), dma((2, 2)), dma((2, 2)),
        ],
        compiler_params=pltpu.CompilerParams(
            collective_id=4, has_side_effects=True, vmem_limit_bytes=60 * 1024 * 1024
        ),
        name="feed_forward",
    )(normed, grad_out, weights)


def add_columns(target, sources, start, size, step):
    def one(turn, carry):
        cols = pl.ds(pl.multiple_of(start + turn * step, 128), step)
        total = target[:, cols].astype(f32)
        for source in sources:
            total = total + source[:, cols].astype(f32)
        target[:, cols] = total.astype(target.dtype)
        return carry

    lax.fori_loop(0, size // step, one, 0)


def shared_products_kernel(
    normed, normed_other, grad, grad_other, weights, pair, pair_other, hidden, hidden_other,
    beside_high, across_low, mine, beside_low, across_high, out,
    turned, slots, stage, diag, landed, waiting, down_now, out_now,
    load_sem, send_sem, recv_sem, store_sem, down_sem, out_sem,
):
    s, z, _, beside, across = places()
    step = pl.program_id(0)
    lefts = ((normed, normed_other), (grad, grad_other))
    chip_cols = normed.shape[1] // 4
    half = chip_cols // 2
    piece = half // 2
    width = pair.shape[1]
    diagonal = beside + across - s
    chips = [q // 2 for q in (diagonal, beside, across, s)]

    def load(side, q, who):
        cols = pl.ds(pl.multiple_of(chips[q] * chip_cols, 128), chip_cols)
        return pltpu.make_async_copy(lefts[side][who].at[:, cols], slots.at[q % 2, who], load_sem.at[q % 2, who])

    def fetch(side):
        for q in range(2):
            for who in range(2):
                load(side, q, who).start()

    def turn(side):
        for q in range(4):
            for who in range(2):
                load(side, q, who).wait()
                stage[...] = slots[q % 2, who].T
                turned[who, q * half : (q + 1) * half, :] = stage[
                    pl.ds(pl.multiple_of(s % 2 * half, 16), half), :
                ]
                if q < 2:
                    load(side, q + 2, who).start()

    def tile(own, other, start, size):
        cols = pl.ds(start, size)
        block = mm(turned[0], own[:, cols], ((1,), (0,)))
        block = (block + mm(turned[1], other[:, cols], ((1,), (0,)))).astype(bf16)
        parts = [block[n * piece : (n + 1) * piece] for n in range(8)]
        there = pl.ds(pl.multiple_of(step * width + start, 128), size)
        diag[0, :, there] = parts[0]
        diag[1, :, there] = parts[1]
        waiting[0, :, there] = parts[2]
        beside_high[:, cols] = parts[3]
        across_low[:, cols] = parts[4]
        waiting[1, :, there] = parts[5]
        mine[0:piece, cols] = parts[6]
        mine[piece:, cols] = parts[7]

    def multiply(own, other):
        def one(turn, carry):
            tile(own, other, pl.multiple_of(turn * 512, 512), 512)
            return carry

        lax.fori_loop(0, width // 512, one, 0)
        if width % 512:
            tile(own, other, width // 512 * 512, width % 512)

    def push(way, j):
        cols = pl.ds(j * width, width)
        return pltpu.make_async_remote_copy(
            src_ref=diag.at[way, :, cols],
            dst_ref=landed.at[way, :, cols],
            send_sem=send_sem.at[way, j],
            recv_sem=recv_sem.at[way, j],
            device_id=(across if way == 0 else beside, z),
            device_id_type=MESH,
        )

    def store(way, j):
        cols = pl.ds(j * width, width)
        return pltpu.make_async_copy(
            waiting.at[way, :, cols], (beside_low, across_high)[way].at[:, cols], store_sem.at[way, j]
        )

    out_rows = down_now.shape[1]
    out_tiles = weights.shape[0] // out_rows

    def down(t):
        source = weights.at[pl.ds(t * out_rows, out_rows), pl.ds(2 * width, width)]
        return pltpu.make_async_copy(source, down_now.at[t % 2], down_sem.at[t % 2])

    def out_store(t):
        return pltpu.make_async_copy(
            out_now.at[t % 2], out.at[:, pl.ds(t * out_rows, out_rows)], out_sem.at[t % 2]
        )

    def out_product():
        for t in range(out_tiles):
            down(t).wait()
            if t > 1:
                out_store(t - 2).wait()
            out_now[t % 2] = mm(hidden[...], down_now[t % 2], ((1,), (1,))).astype(bf16)
            out_store(t).start()
            if t + 2 < out_tiles:
                down(t + 2).start()

    @pl.when(step == 0)
    def _():
        fetch(0)
        greet([(beside, z), (across, z)])
        turn(0)

    @pl.when(step == 2)
    def _():
        down(0).start()
        down(1).start()
        turn(1)

    pl.when(step < 2)(functools.partial(multiply, pair, pair_other))
    pl.when(step == 1)(functools.partial(fetch, 1))
    pl.when(step == 2)(functools.partial(multiply, hidden, hidden_other))
    for j in range(3):

        @pl.when(step == j)
        def _(j=j):
            push(0, j).start()
            push(1, j).start()

    @pl.when(step == 2)
    def _():
        out_product()
        for j in range(3):
            for way in range(2):
                push(way, j).wait_recv()
                add_columns(waiting.at[way], [landed.at[way]], j * width, width, 384)
                store(way, j).start()
        for j in range(3):
            for way in range(2):
                push(way, j).wait_send()
                store(way, j).wait()
        for t in range(out_tiles - 2, out_tiles):
            out_store(t).wait()


def shared_products(lefts, weights, pair, hidden):
    tok, model = lefts[0].shape
    width = hidden[0].shape[1]
    half = model // 8
    anyspec = pl.BlockSpec(memory_space=pl.ANY)
    dma = pltpu.SemaphoreType.DMA

    def block(rows):
        return pl.BlockSpec((rows, width), lambda j: (0, j))

    pair_spec = pl.BlockSpec((tok, width), lambda j: (0, jnp.minimum(j, 1)))
    hidden_spec = pl.BlockSpec((tok, width), lambda j: (0, 0))
    rows_out = (half // 2, half // 2, half, half // 2, half // 2)
    return pl.pallas_call(
        shared_products_kernel,
        grid=(3,),
        in_specs=[anyspec] * 5 + [pair_spec] * 2 + [hidden_spec] * 2,
        out_specs=[block(rows) for rows in rows_out[:3]] + [anyspec] * 3,
        out_shape=[jax.ShapeDtypeStruct((rows, 3 * width), bf16) for rows in rows_out]
        + [jax.ShapeDtypeStruct((tok, model), bf16)],
        scratch_shapes=[
            pltpu.VMEM((2, 4 * half, tok), bf16),
            pltpu.VMEM((2, 2, tok, 2 * half), bf16),
            pltpu.VMEM((2 * half, tok), bf16),
            pltpu.VMEM((2, half // 2, 3 * width), bf16),
            pltpu.VMEM((2, half // 2, 3 * width), bf16),
            pltpu.VMEM((2, half // 2, 3 * width), bf16),
            pltpu.VMEM((2, 512, width), bf16),
            pltpu.VMEM((2, tok, 512), bf16),
            dma((2, 2)), dma((2, 3)), dma((2, 3)), dma((2, 3)), dma((2,)), dma((2,)),
        ],
        compiler_params=pltpu.CompilerParams(
            collective_id=5, has_side_effects=True, vmem_limit_bytes=60 * 1024 * 1024
        ),
        name="feed_forward_products",
    )(*lefts, weights, *pair, *hidden)


def scatter_kernel(
    normed, normed_other, grad_mix, mix_other, mixed, mixed_other, grad_both, rest, mlp_low, mlp_high, mixer_w,
    tokens, gain, mixer_sum, mlp_back, input_grad,
    held, cross, near, lined, left_now, both_now, mixed_now, turned, stage, rest_other, back_now, wide_now, gain_now,
    load_sem, core_send, core_recv, wide_sem,
    flow_send, flow_recv, line_send, line_recv, swap_send, swap_recv, own_sem,
):
    s, z, core, beside, across = places()
    chip_diag, chip_beside, chip_across, chip = 0, 1, 2, 3
    chips = [q // 2 for q in (beside + across - s, beside, across, s)]
    rows = held.shape[1] // 4
    cols = held.shape[2]
    cut = cols // 256 * 128
    ff_part = mlp_low.shape[1] // 3
    tok, model = tokens.shape
    half = 4 * rows
    lru2 = grad_both.shape[1]
    rest_start = lru2 + mixed.shape[1]
    order = (3 * (1 - z // 2), (2 + 3 * z) % 5, 1 + z % 2, z)

    def remote(src, dst, send, recv, target):
        return pltpu.make_async_remote_copy(
            src_ref=src, dst_ref=dst, send_sem=send, recv_sem=recv, device_id=target, device_id_type=MESH
        )

    def span(k):
        return pl.ds(pl.multiple_of(k * rows, 16), rows)

    mine, other = pl.ds(0, tok), pl.ds(tok, tok)
    loads = [
        pltpu.make_async_copy(source, target, load_sem.at[n])
        for n, (source, target) in enumerate(
            (
                (grad_mix, left_now.at[1, mine, :]),
                (mix_other, left_now.at[1, other, :]),
                (mixed, mixed_now.at[mine, :]),
                (mixed_other, mixed_now.at[other, :]),
                (normed, left_now.at[0, mine, :]),
                (normed_other, left_now.at[0, other, :]),
                (grad_both, both_now.at[mine, :]),
            )
        )
    ]

    def push(n):
        if n == 0:
            source, target = grad_both, both_now.at[other, :]
        else:
            source = rest.at[pl.ds(pl.multiple_of(chips[n - 1] * 2 * half + (1 - s % 2) * half, 16), half), :]
            target = rest_other.at[n - 1]
        return pltpu.make_async_remote_copy(
            src_ref=source,
            dst_ref=target,
            send_sem=core_send.at[n],
            recv_sem=core_recv.at[n],
            device_id=(core, z),
            device_id_type=MESH,
        )

    def rest_load(q):
        source = rest.at[pl.ds(pl.multiple_of(chips[q] * 2 * half + s % 2 * half, 16), half), :]
        return pltpu.make_async_copy(
            source, held.at[q, :, pl.ds(rest_start, cols - rest_start)], load_sem.at[7 + q]
        )

    def turn(side):
        for q in range(4):
            source = left_now[side, :, pl.ds(pl.multiple_of(chips[q] * 2 * half, 128), 2 * half)]
            stage[...] = source.T
            turned[side, q * half : (q + 1) * half, :] = stage[
                pl.ds(pl.multiple_of(s % 2 * half, 16), half), :
            ]

    def multiply(q, side):
        right, start = ((both_now, 0), (mixed_now, lru2))[side]

        def one(turn, carry):
            here = pl.multiple_of(turn * 512, 512)
            block = mm(turned[side, q * half : (q + 1) * half, :], right[:, pl.ds(here, 512)], ((1,), (0,)))
            held[q, :, pl.ds(pl.multiple_of(start + here, 512), 512)] = block.astype(bf16)
            return carry

        lax.fori_loop(0, right.shape[1] // 512, one, 0)

    def add_rest(q):
        rest_load(q).wait()
        push(1 + q).wait_recv()
        held[q, :, rest_start:] = add_low(held[q, :, rest_start:], rest_other[q])

    left, right = pl.ds(0, cut), pl.ds(cut, cols - cut)

    def block(q, i, side):
        return held.at[q, span(order[i]), side]

    def flow(i, index):
        send, recv = flow_send.at[i, index], flow_recv.at[i, index]
        to_beside, to_across = (beside, z), (across, z)
        if index == 0:
            return remote(block(chip_diag, i, left), cross.at[i, :, left], send, recv, to_across)
        if index == 1:
            return remote(block(chip_diag, i, right), cross.at[i, :, right], send, recv, to_beside)
        if index == 2:
            return remote(block(chip_beside, i, right), near.at[0, i, :, right], send, recv, to_beside)
        if index == 3:
            return remote(block(chip_beside, i, left), near.at[0, i, :, left], send, recv, to_beside)
        if index == 4:
            return remote(block(chip_across, i, left), near.at[1, i, :, left], send, recv, to_across)
        return remote(block(chip_across, i, right), near.at[1, i, :, right], send, recv, to_across)

    def cross_step(i):
        flow(i, 0).wait_recv()
        add_columns(held.at[chip_beside, span(order[i]), :], [cross.at[i]], 0, cut, 512)
        flow(i, 3).start()
        flow(i, 1).wait_recv()
        add_columns(held.at[chip_across, span(order[i]), :], [cross.at[i]], cut, cols - cut, 384)
        flow(i, 5).start()

    def near_step(i):
        for index in (2, 4, 3, 5):
            flow(i, index).wait_recv()
        add_columns(held.at[chip, span(order[i]), :], [near.at[0, i], near.at[1, i]], 0, cols, 640)

    def line(k, slot, target):
        return remote(
            held.at[chip, span(k), :], lined.at[slot], line_send.at[k], line_recv.at[slot], (s, target)
        )

    def absorb(k, slot, source):
        line(k, slot, source).wait_recv()
        add_columns(held.at[chip, span(k), :], [lined.at[slot]], 0, cols, 640)

    def chain(i):
        k = order[i]
        if i == 3:
            pl.when(z > 0)(lambda: absorb(k, k, z - 1))
            pl.when(z < 3)(lambda: absorb(k, 4, z + 1))
            return

        @pl.when(k > z)
        def _():
            pl.when(z > 0)(lambda: absorb(k, k, z - 1))
            line(k, k, z + 1).start()

        @pl.when(k < z)
        def _():
            pl.when(z < 3)(lambda: absorb(k, k, z + 1))
            pl.when(k == z - 1)(lambda: line(k, 4, z - 1).start())
            pl.when(k < z - 1)(lambda: line(k, k, z - 1).start())

    def chain_drain():
        for i in range(3):
            k = order[i]
            line(k, k, (z + 1) % 4).wait_send()

    def swap(k, high=False):
        to = (z + k) % 4
        here = pl.ds(pl.multiple_of(z * ff_part, 128), ff_part)
        source = (mlp_high if high else mlp_low).at[span(to % 2), :]
        return [
            remote(
                source.at[:, pl.ds(m * ff_part, ff_part)],
                mlp_back.at[m, :, here],
                swap_send.at[k - 1, m],
                swap_recv.at[k - 1, m],
                (s, to),
            )
            for m in range(3)
        ]

    def swap_start(k):
        to = (z + k) % 4

        @pl.when(to < 2)
        def _():
            for copy in swap(k):
                copy.start()

        @pl.when(to >= 2)
        def _():
            for copy in swap(k, True):
                copy.start()

    def own(high=False):
        here = pl.ds(pl.multiple_of(z * ff_part, 128), ff_part)
        source = (mlp_high if high else mlp_low).at[span(z % 2), :]
        return [
            pltpu.make_async_copy(source.at[:, pl.ds(m * ff_part, ff_part)], mlp_back.at[m, :, here], own_sem.at[m])
            for m in range(3)
        ]

    wide_rows = wide_now.shape[0]
    wide_tiles = mixer_w.shape[0] // wide_rows
    wide_start = mixer_w.shape[1] - lru2 - model
    wide_slots = (both_now.at[pl.ds(tok, wide_rows), :], wide_now)

    def wide(j):
        source = mixer_w.at[pl.ds(j * wide_rows, wide_rows), pl.ds(wide_start, lru2)]
        return pltpu.make_async_copy(source, wide_slots[j % 2], wide_sem.at[j % 2])

    plain_loads = [
        pltpu.make_async_copy(tokens, left_now.at[0, pl.ds(0, tok), :], wide_sem.at[2]),
        pltpu.make_async_copy(gain, gain_now, wide_sem.at[3]),
    ]

    def back(first, last):
        for j in range(first, last):
            wide(j).wait()
            back_now[:, pl.ds(j * wide_rows, wide_rows)] = mm(
                both_now[0:tok, :], wide_slots[j % 2][...], ((1,), (1,))
            )
            if j + 2 < wide_tiles:
                wide(j + 2).start()

    def finish_rows(turn, carry):
        at = pl.ds(pl.multiple_of(turn * 16, 16), 16)
        result = left_now[1, at, :].astype(f32) + norm_back(
            left_now[0, at, :].astype(f32), gain_now[0:1, :], back_now[at, :]
        )
        left_now[0, at, :] = result.astype(bf16)
        return carry

    for copy in loads:
        copy.start()
    for q in range(4):
        rest_load(q).start()
    greet([(core, z), (beside, z), (across, z)] + [(s, (z + k) % 4) for k in range(1, 4)])
    for n in range(5):
        push(n).start()
    for k in (1, 3, 2):
        swap_start(k)

    @pl.when(z < 2)
    def _():
        for copy in own():
            copy.start()

    @pl.when(z >= 2)
    def _():
        for copy in own(True):
            copy.start()

    for copy in loads[:4]:
        copy.wait()
    turn(1)
    multiply(chip_diag, 1)
    for copy in loads[4:]:
        copy.wait()
    turn(0)
    push(0).wait_recv()
    multiply(chip_diag, 0)
    add_rest(chip_diag)
    for i in range(2):
        flow(i, 0).start()
        flow(i, 1).start()
    for q in (chip_beside, chip_across, chip):
        multiply(q, 0)
        multiply(q, 1)
        add_rest(q)
        if q == chip_beside:
            flow(0, 2).start()
        if q == chip_across:
            flow(0, 4).start()
    for copy in plain_loads:
        copy.start()
    wide(0).start()
    wide(1).start()
    for i in range(4):
        cross_step(i)
        if i + 1 < 4:
            flow(i + 1, 2).start()
            flow(i + 1, 4).start()
        if i + 2 < 4:
            flow(i + 2, 0).start()
            flow(i + 2, 1).start()
        if i > 0:
            near_step(i - 1)
            chain(i - 1)
            back(wide_tiles * (i - 1) // 3, wide_tiles * i // 3)
    for copy in plain_loads:
        copy.wait()
    lax.fori_loop(0, tok // 16, finish_rows, 0)
    finished = pltpu.make_async_copy(left_now.at[0, pl.ds(0, tok), :], input_grad, wide_sem.at[2])
    finished.start()
    near_step(3)
    chain(3)
    done = pltpu.make_async_copy(held.at[chip, span(z), :], mixer_sum, own_sem.at[3])
    done.start()
    for i in range(4):
        for index in range(6):
            flow(i, index).wait_send()
    chain_drain()
    for k in range(1, 4):
        for copy in swap(k):
            copy.wait()
    for copy in own():
        copy.wait()
    for n in range(5):
        push(n).wait_send()
    finished.wait()
    done.wait()


def scatter(rows_pairs, grad_both, rest, mlp_low, mlp_high, mixer_w, tokens, gain):
    tok, model = tokens.shape
    rows = model // 32
    mixed = rows_pairs[4]
    cols = grad_both.shape[1] + mixed.shape[1] + rest.shape[1]
    ff_part = mlp_low.shape[1] // 3
    anyspec = pl.BlockSpec(memory_space=pl.ANY)
    dma = pltpu.SemaphoreType.DMA
    return pl.pallas_call(
        scatter_kernel,
        in_specs=[anyspec] * 13,
        out_specs=[anyspec] * 3,
        out_shape=[
            jax.ShapeDtypeStruct((rows, cols), bf16),
            jax.ShapeDtypeStruct((3, rows, 4 * ff_part), bf16),
            jax.ShapeDtypeStruct((tok, model), bf16),
        ],
        scratch_shapes=[
            pltpu.VMEM((4, 4 * rows, cols), bf16),
            pltpu.VMEM((4, rows, cols), bf16),
            pltpu.VMEM((2, 4, rows, cols), bf16),
            pltpu.VMEM((5, rows, cols), bf16),
            pltpu.VMEM((2, 2 * tok, model), bf16),
            pltpu.VMEM((2 * tok, grad_both.shape[1]), bf16),
            pltpu.VMEM((2 * tok, mixed.shape[1]), bf16),
            pltpu.VMEM((2, 16 * rows, 2 * tok), bf16),
            pltpu.VMEM((8 * rows, 2 * tok), bf16),
            pltpu.VMEM((4, 4 * rows, rest.shape[1]), bf16),
            pltpu.VMEM((tok, model), f32),
            pltpu.VMEM((128, grad_both.shape[1]), bf16),
            pltpu.VMEM((8, model), f32),
            dma((11,)), dma((5,)), dma((5,)), dma((4,)),
            dma((4, 6)), dma((4, 6)), dma((4,)), dma((5,)), dma((3, 3)), dma((3, 3)), dma((4,)),
        ],
        compiler_params=pltpu.CompilerParams(
            collective_id=2, has_side_effects=True, vmem_limit_bytes=62 * 1024 * 1024
        ),
        name="scatter_gradients",
    )(*rows_pairs, grad_both, rest, mlp_low, mlp_high, mixer_w, tokens, gain)


def gather_plain(mixer, gate, up, down):
    groups = lax.axis_size("fsdp")
    part_rows, ff = gate.shape
    own = jnp.stack([w.reshape(part_rows, groups, ff // groups) for w in (gate, up, down)], axis=2)
    mine = lax.all_to_all(jnp.transpose(own, (1, 0, 2, 3)), "fsdp", 0, 0, tiled=True)
    return lax.all_gather(mixer, both, axis=0, tiled=True), mine.reshape(groups * part_rows, -1)


def from_line(shard):
    count = lax.axis_size("fsdp")
    return [shard] + [
        lax.ppermute(shard, "fsdp", [(i, (i + k) % count) for i in range(count)]) for k in range(1, count)
    ]


def swap_cores(shard):
    count = lax.axis_size("seq")
    return lax.ppermute(shard, "seq", [(i, i + 1 - 2 * (i % 2)) for i in range(count)])


def swap_beside(shard):
    return lax.ppermute(shard, "seq", [(i, i ^ 2) for i in range(8)])


def swap_across(shard):
    return lax.ppermute(shard, "seq", [(i, i ^ 4) for i in range(8)])


def add_low(left, right):
    return (left.astype(f32) + right.astype(f32)).astype(bf16)


def scatter_plain(normed, grad_both, grad_mix, mixed, rest, mlp_sum):
    groups = lax.axis_size("fsdp")
    term_wide = mm(normed, grad_both, ((0,), (0,))).astype(bf16)
    term_out = mm(grad_mix, mixed, ((0,), (0,))).astype(bf16)
    mixer_sum = lax.psum_scatter(
        jnp.concatenate([term_wide, term_out, rest], axis=1), "seq", scatter_dimension=0, tiled=True
    )
    mixer_sum = lax.psum_scatter(mixer_sum, "fsdp", scatter_dimension=0, tiled=True)
    ff_part = mlp_sum.shape[1] // 3
    part_rows = mlp_sum.shape[0] // groups
    mlp_sum = mlp_sum.reshape(groups, part_rows, 3, ff_part)
    mlp_back = lax.all_to_all(mlp_sum, "fsdp", 0, 0, tiled=True)
    mlp_back = jnp.transpose(mlp_back, (2, 1, 0, 3)).reshape(3, part_rows, groups * ff_part)
    return mixer_sum, mlp_back


def call_heads(kernel, width, heads, ins, outs, scratch, name):
    def spec(rows, place):
        if place is None:
            return pl.BlockSpec((rows, width), lambda h: (0, h))
        return pl.BlockSpec((width, width), lambda h: (h, place))

    in_specs = [spec(a.shape[0], place) for a, place in ins]
    out_specs = [spec(rows, 0 if rowwise else None) for rows, _, rowwise in outs]
    out_shape = [
        jax.ShapeDtypeStruct((heads * width, width) if rowwise else (rows, heads * width), kind)
        for rows, kind, rowwise in outs
    ]
    return pl.pallas_call(
        kernel,
        grid=(heads,),
        in_specs=in_specs,
        out_specs=out_specs,
        out_shape=out_shape,
        scratch_shapes=[pltpu.VMEM((rows, width), f32) for rows in scratch],
        compiler_params=pltpu.CompilerParams(vmem_limit_bytes=40 * 1024 * 1024),
        cost_estimate=pl.CostEstimate(flops=1, bytes_accessed=1, transcendentals=0),
        name=name,
    )(*[a for a, _ in ins])


def on_device(
    block_input,
    cotangent,
    mixer_gain,
    branch_proj,
    gelu_proj,
    conv_taps,
    conv_bias,
    rate_blocks,
    input_blocks,
    rate_bias,
    input_bias,
    decay_param,
    out_proj,
    mlp_gain,
    gate_proj,
    up_proj,
    down_proj,
):
    groups = lax.axis_size("fsdp")
    part_rows, lru = branch_proj.shape
    width = rate_blocks.shape[1]
    heads = lru // width
    margin = conv_taps.shape[0] - 1
    tokens = block_input[0].astype(f32)
    tok_count, model = tokens.shape
    ff = gate_proj.shape[1]
    ff_part = ff // groups
    grad_out = cotangent[0]

    smalls = jnp.stack(
        [conv_taps[k] for k in range(margin + 1)]
        + [conv_bias, rate_bias, input_bias, decay_param, mixer_gain, mlp_gain],
        axis=1,
    )
    small_count = smalls.shape[1]
    smalls = jnp.pad(smalls, ((0, 0), (0, 128 - small_count)))
    first_own = jnp.concatenate([rate_blocks, input_blocks, smalls], axis=1)
    mixer_own = (first_own, branch_proj, gelu_proj, out_proj)
    custom = lax.axis_size("seq") == 8 and groups == 4
    if custom:
        mixer_w, mlp_mine = gather(*mixer_own, gate_proj, up_proj, down_proj)
    else:
        mixer_w, mlp_mine = gather_plain(jnp.concatenate(mixer_own, axis=1), gate_proj, up_proj, down_proj)
    mlp_w = lax.all_gather(mlp_mine, "seq", axis=0, tiled=True)
    grad_out_late = lax.optimization_barrier((grad_out, mlp_mine))[0]
    if custom:
        grad_pieces = from_line(grad_out_late)
    smalls = lax.optimization_barrier(mixer_w[:, 2 * width : 2 * width + 128])
    wide = mixer_w[:, 128 + 2 * width : 128 + 2 * width + 2 * lru]
    proj_out = mixer_w[:, 128 + 2 * width + 2 * lru :]

    table = smalls[:, :small_count].astype(f32).T
    param_decay = table[margin + 4]
    gain_one = table[margin + 5]
    gain_two = table[margin + 6]
    small = jnp.concatenate(
        [
            table[: margin + 4],
            jax.nn.softplus(-param_decay)[None],
            -jax.nn.sigmoid(-param_decay)[None],
            jnp.zeros((16 - margin - 6, lru), f32),
        ],
        axis=0,
    )

    normed = norm_rows(tokens, gain_one).astype(bf16)
    both_pre = mm(normed, wide, ((1,), (0,)))
    branch = both_pre[:, :lru].astype(bf16)
    gelu_pre = both_pre[:, lru:]
    prior = from_behind(branch[tok_count - margin :], "seq", 1).astype(f32)
    prior = jnp.concatenate([jnp.zeros((8 - margin, lru), f32), prior], axis=0)
    conv, rate_pre, input_pre, cum, local = call_heads(
        mixer_forward,
        width,
        heads,
        [(branch, None), (prior, None), (small, None), (mixer_w, 0), (mixer_w, 1)],
        [(tok_count, bf16, False)] + [(tok_count, f32, False)] * 4,
        [tok_count + 8],
        "mixer_forward",
    )
    carried = prefix((cum[-1], local[-1]), "seq", False)
    states = local + cum * carried[None]
    mixed = (states * jax.nn.gelu(gelu_pre, approximate=True)).astype(bf16)
    middle = tokens + mm(mixed, proj_out, ((1,), (1,)))
    normed_two = norm_rows(middle, gain_two).astype(bf16)

    if custom:
        normed_all, normed_other, grad_out_all, grad_out_other, first_other, mixed_other = gather_rows(
            normed_two, grad_pieces, normed, mixed
        )
    else:
        normed_all = lax.all_gather(normed_two, "fsdp", axis=0, tiled=True)
        grad_out_all = lax.all_gather(grad_out_late, "fsdp", axis=0, tiled=True)
    w_gate, w_up, w_down = mlp_w[:, :ff_part], mlp_w[:, ff_part : 2 * ff_part], mlp_w[:, 2 * ff_part :]
    if custom:
        hidden, hidden_other, grad_pair, pair_other, grad_normed_part = feed_forward(
            normed_all, grad_out_all, mlp_w
        )
    else:
        gate = mm(normed_all, w_gate, ((1,), (0,)))
        up_val = mm(normed_all, w_up, ((1,), (0,)))
        gelu_gate, gelu_slope = gelu_parts(gate)
        hidden = (gelu_gate * up_val).astype(bf16)
        grad_hidden = mm(grad_out_all, w_down, ((1,), (0,)))
        grad_gate = (grad_hidden * up_val * gelu_slope).astype(bf16)
        grad_up = (grad_hidden * gelu_gate).astype(bf16)
        grad_normed_part = (
            mm(grad_gate, w_gate, ((1,), (1,))) + mm(grad_up, w_up, ((1,), (1,)))
        ).astype(bf16)
    grad_normed_two = lax.psum_scatter(grad_normed_part, "fsdp", scatter_dimension=0, tiled=True)
    if custom:
        half = model // 16
        beside_high, across_low, mine, beside_low, across_high, out_part = shared_products(
            (normed_all, normed_other, grad_out_all, grad_out_other),
            mlp_w,
            (grad_pair, pair_other),
            (hidden, hidden_other),
        )
        from_beside_high, from_across_low = swap_beside(beside_high), swap_across(across_low)
    else:
        grad_pair = jnp.concatenate([grad_gate, grad_up], axis=1)
        term_pair = mm(normed_all, grad_pair, ((0,), (0,))).astype(bf16)
        term_down = mm(grad_out_all, hidden, ((0,), (0,))).astype(bf16)
        pair_sum = lax.psum_scatter(term_pair, "seq", scatter_dimension=0, tiled=True)
        down_sum = lax.psum_scatter(term_down, "seq", scatter_dimension=0, tiled=True)
        mlp_sum = jnp.concatenate([pair_sum, down_sum], axis=1)
        out_part = mm(hidden, w_down, ((1,), (1,))).astype(bf16)
    out_sum = lax.psum_scatter(out_part, "fsdp", scatter_dimension=0, tiled=True)
    grad_normed_two = grad_normed_two.astype(f32)

    grad_middle = grad_out.astype(f32) + norm_back(middle, gain_two, grad_normed_two)
    grad_mix = grad_middle.astype(bf16)
    if custom:
        mix_other = swap_cores(grad_mix)
    grad_mixed = mm(grad_mix, proj_out, ((1,), (0,)))
    carried_rows = jnp.broadcast_to(carried[None], (8, lru))
    grad_gelu_pre, rev_cum, rev_grad, pair_grad = call_heads(
        mixer_backward_scan,
        width,
        heads,
        [(a, None) for a in (grad_mixed, gelu_pre, rate_pre, cum, local, carried_rows, small)],
        [(tok_count, bf16, False), (tok_count, f32, False), (tok_count, f32, False), (8, f32, False)],
        [tok_count + 8],
        "mixer_backward_scan",
    )
    if custom:
        from_beside_high, from_across_low, pair_grad = lax.optimization_barrier(
            (from_beside_high, from_across_low, pair_grad)
        )
    incoming = prefix((cum[-1], pair_grad[0]), "seq", True)
    if custom:
        beside_low, across_high, incoming = lax.optimization_barrier((beside_low, across_high, incoming))
        from_beside_low, from_across_high = swap_beside(beside_low), swap_across(across_high)
    incoming_rows = jnp.broadcast_to(incoming[None], (8, lru))
    own, head, rate_w_grad, input_w_grad, sums = call_heads(
        mixer_backward,
        width,
        heads,
        [
            (a, None)
            for a in (rev_cum, rev_grad, incoming_rows, cum, local, carried_rows, rate_pre, input_pre, conv, branch, prior, small)
        ]
        + [(mixer_w, 0), (mixer_w, 1)],
        [(tok_count, f32, False), (8, f32, False), (0, bf16, True), (0, bf16, True), (8, f32, False)],
        [tok_count + 8, tok_count + 16],
        "mixer_backward",
    )
    received = from_behind(head[8 - margin :], "seq", -1)
    grad_branch = jnp.concatenate(
        [own[: tok_count - margin], own[tok_count - margin :] + received], axis=0
    ).astype(bf16)
    grad_both = jnp.concatenate([grad_branch, grad_gelu_pre], axis=1)
    vectors = jnp.pad(sums.T, ((0, 0), (0, 128 - sums.shape[0]))).astype(bf16)
    rest = jnp.concatenate([rate_w_grad, input_w_grad, vectors], axis=1)
    if custom:
        mlp_parts = (
            (mine[:half], from_across_low, from_beside_low),
            (mine[half:], from_across_high, from_beside_high),
        )
        low, high = [sum(part.astype(f32) for part in parts).astype(bf16) for parts in mlp_parts]
        gain_rows = jnp.broadcast_to(gain_one[None], (8, model))
        mixer_sum, mlp_back, input_grad = scatter(
            (normed, first_other, grad_mix, mix_other, mixed, mixed_other),
            grad_both, rest, low, high, mixer_w, block_input[0], gain_rows,
        )
    else:
        mixer_sum, mlp_back = scatter_plain(normed, grad_both, grad_mix, mixed, rest, mlp_sum)
        grad_normed = mm(grad_both, wide, ((1,), (1,)))
        input_grad = (grad_middle + norm_back(tokens, gain_one, grad_normed)).astype(bf16)
    input_grad = input_grad[None]
    middle = lax.optimization_barrier((middle, mixer_sum))[0]
    block_output = (middle + out_sum.astype(f32)).astype(bf16)[None]
    mlp_grads = [mlp_back[m].astype(f32) for m in range(3)]
    mixer_sum = mixer_sum.astype(f32)
    edges = [lru, 2 * lru, 3 * lru, 3 * lru + width, 3 * lru + 2 * width]
    dbranch, dgelu, dout, drate, dinput, vec = jnp.split(mixer_sum, edges, axis=1)
    vec = vec.T
    return (
        block_output,
        input_grad,
        gain_back(mixer_gain, (branch_proj, dbranch), (gelu_proj, dgelu)),
        dbranch,
        dgelu,
        vec[: margin + 1],
        vec[7],
        drate,
        dinput,
        vec[4],
        vec[5],
        vec[6],
        dout,
        gain_back(mlp_gain, (gate_proj, mlp_grads[0]), (up_proj, mlp_grads[1])),
        mlp_grads[0],
        mlp_grads[1],
        mlp_grads[2],
    )


def solution(mesh):
    tokens = P("fsdp", "seq", None)
    vector = P(both)
    matrix = P(both, None)
    taps = P(None, both)
    return jax.shard_map(
        on_device,
        mesh=mesh,
        in_specs=(
            tokens, tokens, vector, matrix, matrix, taps, vector, matrix, matrix,
            vector, vector, vector, matrix, vector, matrix, matrix, matrix,
        ),
        out_specs=(
            tokens, tokens, vector, matrix, matrix, taps, vector, matrix, matrix,
            vector, vector, vector, matrix, vector, matrix, matrix, matrix,
        ),
        check_vma=False,
    )
```

```python
import functools

import jax
import jax.numpy as jnp
from jax import lax
from jax.experimental import pallas as pl
from jax.experimental.pallas import tpu as pltpu
from jax.sharding import PartitionSpec as P

epsilon = 1e-06
f32 = jnp.float32
bf16 = jnp.bfloat16
both = ("seq", "fsdp")
MESH = pl.DeviceIdType.MESH
TAP, CONV_BIAS, RATE_BIAS, INPUT_BIAS, SOFT, SOFT_SLOPE, GAIN_ONE, GAIN_TWO = 0, 4, 5, 6, 7, 8, 9, 10
GELU_C = 0.7978845608028654
GELU_A = 0.044715


def from_behind(shard, axis, by):
    devices = lax.axis_size(axis)
    pairs = [(i, i + by) for i in range(devices) if 0 <= i + by < devices]
    return lax.ppermute(shard, axis, pairs)


def prefix(part, axis, reverse):
    count = lax.axis_size(axis)
    place = lax.axis_index(axis)
    gathered = lax.all_gather(jnp.stack(part), axis)
    state = jnp.zeros_like(part[1])
    for hop in range(count):
        source = count - 1 - hop if reverse else hop
        ahead = source > place if reverse else source < place
        state = jnp.where(ahead, gathered[source, 1] + gathered[source, 0] * state, state)
    return state


def norm_rows(values, scales):
    return values * lax.rsqrt(jnp.mean(values * values, axis=-1, keepdims=True) + epsilon) * scales


def norm_back(values, scales, grads):
    inverse = lax.rsqrt(jnp.mean(values * values, axis=-1, keepdims=True) + epsilon)
    scaled = grads * scales
    shared = jnp.mean(values * scaled, axis=-1, keepdims=True)
    return inverse * scaled - values * (inverse * inverse * inverse * shared)


def gain_back(gain, *pairs):
    total = sum(jnp.sum(weight.astype(f32) * grad, axis=1) for weight, grad in pairs)
    return total / gain.astype(f32)


def gelu_parts(x):
    inner = jnp.tanh(GELU_C * (x + GELU_A * x * x * x))
    return 0.5 * x * (1.0 + inner), 0.5 * (1.0 + inner) + 0.5 * x * (1.0 - inner * inner) * (
        GELU_C * (1.0 + 3.0 * GELU_A * x * x)
    )


def mm(left, right, dims):
    return lax.dot_general(left, right, (dims, ((), ())), preferred_element_type=f32)


def sigmoid(x):
    return 1.0 / (1.0 + jnp.exp(-x))


def scan_rows(decay, value, reverse):
    rows = decay.shape[0]
    place = lax.broadcasted_iota(jnp.int32, decay.shape, 0)
    step = 1
    while step < rows:
        shift = rows - step if reverse else step
        inside = place < rows - step if reverse else place >= step
        before_value = jnp.where(inside, pltpu.roll(value, shift, 0), 0.0)
        before_decay = jnp.where(inside, pltpu.roll(decay, shift, 0), 1.0)
        value = value + decay * before_value
        decay = decay * before_decay
        step *= 2
    return decay, value


def gates(rate_pre, input_pre, soft):
    rate = sigmoid(rate_pre)
    log_decay = -8.0 * rate * soft
    decay = jnp.exp(log_decay)
    square = decay * decay
    root = jnp.sqrt(-jnp.tanh(log_decay) * (1.0 + square))
    return rate, decay, square, root, sigmoid(input_pre)


def table_kernel(columns, table):
    rows = columns[...].T[0:16, :].astype(f32)
    decay_param = rows[7:8, :]
    fast = jnp.exp(-decay_param)
    table[0:7, :] = rows[0:7, :]
    table[7:8, :] = jnp.log1p(fast)
    table[8:9, :] = -fast / (1.0 + fast)
    table[9:11, :] = rows[8:10, :]
    table[11:16, :] = jnp.zeros((5, rows.shape[1]), f32)


def small_table(mixer_w, block):
    model = mixer_w.shape[0]
    return pl.pallas_call(
        table_kernel,
        grid=(1,),
        in_specs=[pl.BlockSpec((model, 128), lambda i: (0, block))],
        out_specs=pl.BlockSpec((16, model), lambda i: (0, 0)),
        out_shape=jax.ShapeDtypeStruct((16, model), f32),
        name="small_table",
    )(mixer_w)


def mixer_forward(branch, prior, small, rate_w, input_w, conv, rate_pre, input_pre, cum, local, ext):
    rows = branch.shape[0]
    ext[0:8, :] = prior[...]
    ext[8:, :] = branch[...].astype(f32)
    total = small[CONV_BIAS : CONV_BIAS + 1, :] + small[TAP : TAP + 1, :] * ext[8:, :]
    for offset in range(1, 4):
        total = total + small[TAP + offset : TAP + offset + 1, :] * ext[pl.ds(8 - offset, rows), :]
    low = total.astype(bf16)
    conv[...] = low
    rate = mm(low, rate_w[...], ((1,), (0,))) + small[RATE_BIAS : RATE_BIAS + 1, :]
    inp = mm(low, input_w[...], ((1,), (0,))) + small[INPUT_BIAS : INPUT_BIAS + 1, :]
    rate_pre[...] = rate
    input_pre[...] = inp
    _, decay, _, root, opened = gates(rate, inp, small[SOFT : SOFT + 1, :])
    product, states = scan_rows(decay, root * opened * low.astype(f32), False)
    cum[...] = product
    local[...] = states


def mixer_backward_scan(grad_mixed, gelu_pre, rate_pre, cum, local, carried, small, grad_pre, rev_cum, rev_grad, pair, ext):
    rows = grad_mixed.shape[0]
    states = local[...] + cum[...] * carried[0:1, :]
    value, slope = gelu_parts(gelu_pre[...])
    grad = grad_mixed[...]
    grad_pre[...] = (grad * states * slope).astype(bf16)
    decay = jnp.exp(-8.0 * sigmoid(rate_pre[...]) * small[SOFT : SOFT + 1, :])
    ext[0:rows, :] = decay
    ext[rows:, :] = jnp.ones((8, decay.shape[1]), f32)
    product, back = scan_rows(ext[pl.ds(1, rows), :], grad * value, True)
    rev_cum[...] = product
    rev_grad[...] = back
    pair[...] = jnp.broadcast_to(decay[0:1, :] * back[0:1, :], pair.shape)


def mixer_backward(
    rev_cum, rev_grad, incoming, cum, local, carried, rate_pre, input_pre, conv, branch, prior, small, rate_w, input_w,
    own, head, rate_w_grad, input_w_grad, sums, ext, gext,
):
    rows = rev_cum.shape[0]
    soft = small[SOFT : SOFT + 1, :]
    grad_states = rev_grad[...] + rev_cum[...] * incoming[0:1, :]
    rate, decay, square, root, opened = gates(rate_pre[...], input_pre[...], soft)
    ext[0:8, :] = jnp.broadcast_to(carried[0:1, :], (8, carried.shape[1]))
    ext[8:, :] = local[...] + cum[...] * carried[0:1, :]
    before = ext[pl.ds(7, rows), :]
    low = conv[...]
    conv_in = low.astype(f32)
    grad_log = grad_states * decay * before - grad_states * opened * conv_in * square / root
    driven = grad_states * root
    grad_input = (driven * conv_in * opened * (1.0 - opened)).astype(bf16)
    by_rate = grad_log * (-8.0 * rate)
    grad_rate = (by_rate * soft * (1.0 - rate)).astype(bf16)
    sums[6:7, :] = jnp.sum(by_rate, axis=0, keepdims=True) * small[SOFT_SLOPE : SOFT_SLOPE + 1, :]
    sums[4:5, :] = jnp.sum(grad_rate.astype(f32), axis=0, keepdims=True)
    sums[5:6, :] = jnp.sum(grad_input.astype(f32), axis=0, keepdims=True)
    rate_w_grad[...] = mm(low, grad_rate, ((0,), (0,))).astype(rate_w_grad.dtype)
    input_w_grad[...] = mm(low, grad_input, ((0,), (0,))).astype(input_w_grad.dtype)
    grad_conv = (
        driven * opened
        + mm(grad_rate, rate_w[...], ((1,), (1,)))
        + mm(grad_input, input_w[...], ((1,), (1,)))
    )
    sums[7:8, :] = jnp.sum(grad_conv, axis=0, keepdims=True)
    ext[0:8, :] = prior[...]
    ext[8:, :] = branch[...].astype(f32)
    gext[0:8, :] = jnp.zeros((8, grad_conv.shape[1]), f32)
    gext[8 : 8 + rows, :] = grad_conv
    gext[8 + rows :, :] = jnp.zeros((8, grad_conv.shape[1]), f32)
    back = jnp.zeros_like(grad_conv)
    front = jnp.zeros((8, grad_conv.shape[1]), f32)
    for offset in range(4):
        tap = small[TAP + offset : TAP + offset + 1, :]
        sums[offset : offset + 1, :] = jnp.sum(
            grad_conv * ext[pl.ds(8 - offset, rows), :], axis=0, keepdims=True
        )
        back = back + tap * gext[pl.ds(8 + offset, rows), :]
        front = front + tap * gext[pl.ds(offset, 8), :]
    own[...] = back
    head[...] = front


def places():
    s = lax.axis_index("seq")
    z = lax.axis_index("fsdp")
    core = s + 1 - 2 * (s % 2)
    beside = s + 2 - 4 * ((s // 2) % 2)
    across = s + 4 - 8 * (s // 4)
    return s, z, core, beside, across


def greet(peers):
    barrier = pltpu.get_barrier_semaphore()
    for peer in peers:
        pl.semaphore_signal(barrier, inc=1, device_id=peer, device_id_type=MESH)
    pl.semaphore_wait(barrier, len(peers))


def gather_kernel(
    first, branch, gelu, outer, gate, up, down, mixer_all, mlp_mine,
    mixer, load_sem, flow_send, flow_recv, line_send, line_recv, swap_send, swap_recv, own_sem,
):
    s, z, core, beside, across = places()
    rows, cols = mixer.shape
    ff_part = mlp_mine.shape[1] // 3
    cut = cols // 256 * 128
    diag = beside + across - s
    loads, start = [], 0
    for n, part in enumerate((first, branch, gelu, outer)):
        size = part.shape[1]
        loads.append(pltpu.make_async_copy(part, mixer.at[:, pl.ds(start, size)], load_sem.at[n]))
        loads[-1].start()
        start += size
    greet([(core, z), (beside, z), (across, z)] + [(s, (z + k) % 4) for k in range(1, 4)])

    def remote(src, dst, send, recv, target):
        return pltpu.make_async_remote_copy(
            src_ref=src, dst_ref=dst, send_sem=send, recv_sem=recv, device_id=target, device_id_type=MESH
        )

    def piece(seq, zz, half=None):
        span = pl.ds(pl.multiple_of((seq * 4 + zz) * rows, 16), rows)
        if half is None:
            return mixer_all.at[span, :]
        return mixer_all.at[span, pl.ds(0, cut) if half == 0 else pl.ds(cut, cols - cut)]

    def flow(zz, index, seq, half, target, src=None):
        ref = piece(seq, zz, half)
        return remote(
            ref if src is None else src, ref, flow_send.at[zz, index], flow_recv.at[zz, index], (target, z)
        )

    def sends(zz, src=None):
        return [
            flow(zz, 0, s, None, beside, src),
            flow(zz, 1, s, None, across, src),
            flow(zz, 4, s, None, core, src),
        ]

    def spread(zz, src=None):
        for copy in sends(zz, src):
            copy.start()

    def relay(zz):
        flow(zz, 0, beside, None, beside).wait_recv()
        flow(zz, 3, beside, 0, across).start()
        flow(zz, 5, beside, None, core).start()
        flow(zz, 1, across, None, across).wait_recv()
        flow(zz, 2, across, 1, beside).start()
        flow(zz, 6, across, None, core).start()

    def finish(zz):
        flow(zz, 3, diag, 0, across).wait_recv()
        flow(zz, 7, diag, 0, core).start()
        flow(zz, 2, diag, 1, beside).wait_recv()
        flow(zz, 8, diag, 1, core).start()

    def drain(zz, src=None):
        for copy in sends(zz, src):
            copy.wait_send()
        flow(zz, 3, beside, 0, across).wait_send()
        flow(zz, 5, beside, None, core).wait_send()
        flow(zz, 2, across, 1, beside).wait_send()
        flow(zz, 6, across, None, core).wait_send()
        flow(zz, 7, diag, 0, core).wait_send()
        flow(zz, 8, diag, 1, core).wait_send()
        flip = core - s
        flow(zz, 4, core, None, core).wait_recv()
        flow(zz, 5, beside + flip, None, core).wait_recv()
        flow(zz, 6, across + flip, None, core).wait_recv()
        flow(zz, 7, diag + flip, 0, core).wait_recv()
        flow(zz, 8, diag + flip, 1, core).wait_recv()

    def line(zz, up_way, hop, src=None):
        ref = piece(s, zz)
        way = 0 if up_way else 1
        target = z + 1 if up_way else z - 1
        return remote(
            ref if src is None else src, ref, line_send.at[way, hop], line_recv.at[way, hop], (s, target)
        )

    def line_hop(hop):
        def below():
            line(z - hop, True, hop - 1).wait_recv()
            pl.when(z < 3)(lambda: line(z - hop, True, hop).start())

        def above():
            line(z + hop, False, hop - 1).wait_recv()
            pl.when(z > 0)(lambda: line(z + hop, False, hop).start())

        pl.when(z >= hop)(below)
        pl.when(z + hop <= 3)(above)

    def at_hop(hop, act):
        pl.when(z >= hop)(lambda: act(z - hop))
        pl.when(z + hop <= 3)(lambda: act(z + hop))

    def landing(m, zz):
        return mlp_mine.at[pl.ds(pl.multiple_of(zz * rows, 16), rows), pl.ds(m * ff_part, ff_part)]

    def columns(m, zz):
        return (gate, up, down)[m].at[:, pl.ds(pl.multiple_of(zz * ff_part, 128), ff_part)]

    def swap(k, m, arriving=False):
        to = (z + k) % 4
        came = (z + 4 - k) % 4
        return remote(
            columns(m, to), landing(m, came if arriving else z), swap_send.at[k - 1, m], swap_recv.at[k - 1, m], (s, to)
        )

    local = [pltpu.make_async_copy(columns(m, z), landing(m, z), own_sem.at[m]) for m in range(3)]
    local.append(pltpu.make_async_copy(mixer, piece(s, z), own_sem.at[3]))
    for copy in loads:
        copy.wait()

    pl.when(z < 3)(lambda: line(z, True, 0, mixer).start())
    pl.when(z > 0)(lambda: line(z, False, 0, mixer).start())
    spread(z, mixer)
    for copy in local:
        copy.start()
    line_hop(1)
    at_hop(1, spread)
    relay(z)
    line_hop(2)
    at_hop(2, spread)
    finish(z)
    at_hop(1, relay)
    line_hop(3)
    at_hop(3, spread)
    for k in (1, 3, 2):
        for m in range(3):
            swap(k, m).start()
    at_hop(1, finish)
    at_hop(2, relay)
    at_hop(3, relay)
    at_hop(2, finish)
    at_hop(3, finish)
    drain(z, mixer)
    for hop in range(1, 4):
        at_hop(hop, drain)
    for copy in local:
        copy.wait()
    for k in (1, 3, 2):
        for m in range(3):
            swap(k, m).wait_send()
            swap(k, m, True).wait_recv()
    pl.when(z < 3)(lambda: line(z, True, 0, mixer).wait_send())
    pl.when(z > 0)(lambda: line(z, False, 0, mixer).wait_send())
    for hop in range(1, 3):
        pl.when((z >= hop) & (z < 3))(lambda: line(z - hop, True, hop).wait_send())
        pl.when((z + hop <= 3) & (z > 0))(lambda: line(z + hop, False, hop).wait_send())


def gather(first, branch, gelu, outer, gate, up, down):
    rows = first.shape[0]
    cols = first.shape[1] + branch.shape[1] + gelu.shape[1] + outer.shape[1]
    ff_part = gate.shape[1] // 4
    anyspec = pl.BlockSpec(memory_space=pl.ANY)
    dma = pltpu.SemaphoreType.DMA
    return pl.pallas_call(
        gather_kernel,
        in_specs=[anyspec] * 7,
        out_specs=[anyspec] * 2,
        out_shape=[
            jax.ShapeDtypeStruct((32 * rows, cols), bf16),
            jax.ShapeDtypeStruct((4 * rows, 3 * ff_part), bf16),
        ],
        scratch_shapes=[
            pltpu.VMEM((rows, cols), bf16), dma((4,)),
            dma((4, 9)), dma((4, 9)), dma((2, 3)), dma((2, 3)), dma((3, 3)), dma((3, 3)), dma((4,)),
        ],
        compiler_params=pltpu.CompilerParams(collective_id=1, has_side_effects=True),
        name="gather_weights",
    )(first, branch, gelu, outer, gate, up, down)


def rows_kernel(
    normed, grad0, grad1, grad2, grad3, first, mixed, normed_all, normed_other, grad_all, grad_other,
    first_other, mixed_other, line_send, line_recv, core_send, core_recv, own_sem, held, give_send, give_recv,
):
    s, z, core, _, _ = places()
    tok = normed.shape[0]
    cuts = 4
    grads = (grad0, grad1, grad2, grad3)
    greet([(core, z)] + [(s, (z + k) % 4) for k in range(1, 4)])

    def rows(ref, zz):
        return ref.at[pl.ds(pl.multiple_of(zz * tok, 16), tok), :]

    def remote(src, dst, send, recv, target):
        return pltpu.make_async_remote_copy(
            src_ref=src, dst_ref=dst, send_sem=send, recv_sem=recv, device_id=target, device_id_type=MESH
        )

    def parts(ref):
        size = tok // cuts
        return [ref.at[pl.ds(n * size, size), :] for n in range(cuts)]

    def line(zz, up_way, hop):
        way = 0 if up_way else 1
        target = z + 1 if up_way else z - 1
        src = normed if hop == 0 else rows(normed_all, zz)
        dst = rows(normed_all, zz)
        return [
            remote(a, b, line_send.at[way, hop, n], line_recv.at[way, hop, n], (s, target))
            for n, (a, b) in enumerate(zip(parts(src), parts(dst)))
        ]

    def over(zz, own=False):
        src = normed if own else rows(normed_all, zz)
        return remote(src, rows(normed_other, zz), core_send.at[0, zz], core_recv.at[0, zz], (core, z))

    def grad_over(k):
        zz = (z + 4 - k) % 4
        return remote(grads[k], rows(grad_other, zz), core_send.at[1, zz], core_recv.at[1, zz], (core, z))

    def line_start(zz, up_way, hop):
        for copy in line(zz, up_way, hop):
            copy.start()

    def line_drain(zz, up_way, hop):
        for copy in line(zz, up_way, hop):
            copy.wait_send()

    def hop_step(hop):
        def below():
            for came, on in zip(line(z - hop, True, hop - 1), line(z - hop, True, hop) if hop < 3 else [None] * cuts):
                came.wait_recv()
                if on is not None:
                    pl.when(z < 3)(on.start)
            over(z - hop).start()

        def above():
            for came, on in zip(line(z + hop, False, hop - 1), line(z + hop, False, hop) if hop < 3 else [None] * cuts):
                came.wait_recv()
                if on is not None:
                    pl.when(z > 0)(on.start)
            over(z + hop).start()

        pl.when(z >= hop)(below)
        pl.when(z + hop <= 3)(above)

    given = [
        remote(source, target, give_send.at[n], give_recv.at[n], (core, z))
        for n, (source, target) in enumerate(((first, first_other), (mixed, mixed_other)))
    ]
    local = [pltpu.make_async_copy(grads[k], held.at[k], own_sem.at[k]) for k in range(4)]
    local.append(pltpu.make_async_copy(normed, held.at[4], own_sem.at[4]))
    stored = [
        pltpu.make_async_copy(held.at[k], rows(grad_all, (z + 4 - k) % 4), own_sem.at[k]) for k in range(4)
    ]
    stored.append(pltpu.make_async_copy(held.at[4], rows(normed_all, z), own_sem.at[4]))
    pl.when(z < 3)(lambda: line_start(z, True, 0))
    pl.when(z > 0)(lambda: line_start(z, False, 0))
    over(z, True).start()
    for copy in local:
        copy.start()
    for k in range(4):
        grad_over(k).start()
    for copy in given:
        copy.start()
    for copy, store in zip(local, stored):
        copy.wait()
        store.start()
    for hop in range(1, 4):
        hop_step(hop)
    for copy in stored:
        copy.wait()
    for k in range(4):
        grad_over(k).wait()
    for copy in given:
        copy.wait()
    over(z, True).wait()
    for k in range(1, 4):
        over((z + k) % 4).wait()
    pl.when(z < 3)(lambda: line_drain(z, True, 0))
    pl.when(z > 0)(lambda: line_drain(z, False, 0))
    for hop in range(1, 3):
        pl.when((z >= hop) & (z < 3))(lambda: line_drain(z - hop, True, hop))
        pl.when((z + hop <= 3) & (z > 0))(lambda: line_drain(z + hop, False, hop))


def gather_rows(normed, grads, first, mixed):
    tok, model = normed.shape
    anyspec = pl.BlockSpec(memory_space=pl.ANY)
    dma = pltpu.SemaphoreType.DMA
    return pl.pallas_call(
        rows_kernel,
        in_specs=[anyspec] * 7,
        out_specs=[anyspec] * 6,
        out_shape=[jax.ShapeDtypeStruct((4 * tok, model), bf16)] * 4
        + [jax.ShapeDtypeStruct(first.shape, bf16), jax.ShapeDtypeStruct(mixed.shape, bf16)],
        scratch_shapes=[
            dma((2, 3, 4)), dma((2, 3, 4)), dma((2, 4)), dma((2, 4)), dma((5,)),
            pltpu.VMEM((5, tok, model), bf16), dma((2,)), dma((2,)),
        ],
        compiler_params=pltpu.CompilerParams(collective_id=3, has_side_effects=True),
        name="gather_rows",
    )(normed, *grads, first, mixed)


def column_tiles(cols, size=512):
    return [(start, min(size, cols - start)) for start in range(0, cols, size)]


def feed_forward_kernel(
    normed, grad_out, weights, hidden, hidden_other, pair, pair_other, back,
    held, hidden_now, pair_now, sems, store_sem, core_send, core_recv,
):
    s, z, core, _, _ = places()
    step = pl.program_id(0)
    ff_part = held.shape[2]
    model = held.shape[1]
    rows = normed.shape[0]
    tiles = column_tiles(ff_part)
    made = ((hidden_now, hidden, hidden_other), (pair_now, pair, pair_other))

    def load(n, m):
        start, size = tiles[n]
        return pltpu.make_async_copy(
            weights.at[:, pl.ds(m * ff_part + start, size)], held.at[m, :, pl.ds(start, size)], sems.at[n, m]
        )

    def kept(n, turn):
        now, mine, _ = made[n]
        return pltpu.make_async_copy(now.at[turn], mine.at[pl.ds(turn * rows, rows), :], store_sem.at[turn, n])

    def handed(n, turn):
        now, _, other = made[n]
        return pltpu.make_async_remote_copy(
            src_ref=now.at[turn],
            dst_ref=other.at[pl.ds(turn * rows, rows), :],
            send_sem=core_send.at[turn, n],
            recv_sem=core_recv.at[turn, n],
            device_id=(core, z),
            device_id_type=MESH,
        )

    @pl.when(step == 0)
    def _():
        for n in range(len(tiles)):
            for m in range(3):
                load(n, m).start()
        greet([(core, z)])

    for n, (start, size) in enumerate(tiles):
        cols = slice(start, start + size)

        @pl.when(step == 0)
        def _(n=n):
            for m in range(3):
                load(n, m).wait()

        gate = mm(normed[...], held[0, :, cols], ((1,), (0,)))
        value, slope = gelu_parts(gate)
        up = mm(normed[...], held[1, :, cols], ((1,), (0,)))
        hidden_now[step, :, cols] = (value * up).astype(bf16)
        grad_hidden = mm(grad_out[...], held[2, :, cols], ((1,), (0,)))
        pair_now[step, :, cols] = (grad_hidden * up * slope).astype(bf16)
        pair_now[step, :, slice(ff_part + start, ff_part + start + size)] = (grad_hidden * value).astype(bf16)

    for turn in range(2):

        @pl.when(step == turn)
        def _(turn=turn):
            for n in range(2):
                handed(n, turn).start()
                kept(n, turn).start()

    def back_tile(turn, carry):
        cols = pl.ds(pl.multiple_of(turn * 512, 512), 512)
        total = mm(pair_now[step, :, :ff_part], held[0, cols, :], ((1,), (1,)))
        total = total + mm(pair_now[step, :, ff_part:], held[1, cols, :], ((1,), (1,)))
        back[:, cols] = total.astype(bf16)
        return carry

    lax.fori_loop(0, model // 512, back_tile, 0)

    @pl.when(step == 1)
    def _():
        for turn in range(2):
            for n in range(2):
                kept(n, turn).wait()
                handed(n, turn).wait()


def feed_forward(normed, grad_out, weights):
    tok, model = normed.shape
    ff_part = weights.shape[1] // 3
    rows = tok // 2
    anyspec = pl.BlockSpec(memory_space=pl.ANY)
    dma = pltpu.SemaphoreType.DMA
    block = pl.BlockSpec((rows, model), lambda i: (i, 0))
    return pl.pallas_call(
        feed_forward_kernel,
        grid=(2,),
        in_specs=[block, block, anyspec],
        out_specs=[anyspec] * 4 + [block],
        out_shape=[
            jax.ShapeDtypeStruct((tok, cols), bf16)
            for cols in (ff_part, ff_part, 2 * ff_part, 2 * ff_part, model)
        ],
        scratch_shapes=[
            pltpu.VMEM((3, model, ff_part), bf16),
            pltpu.VMEM((2, rows, ff_part), bf16),
            pltpu.VMEM((2, rows, 2 * ff_part), bf16),
            dma((len(column_tiles(ff_part)), 3)), dma((2, 2)), dma((2, 2)), dma((2, 2)),
        ],
        compiler_params=pltpu.CompilerParams(
            collective_id=4, has_side_effects=True, vmem_limit_bytes=60 * 1024 * 1024
        ),
        name="feed_forward",
    )(normed, grad_out, weights)


def add_columns(target, sources, start, size, step):
    def one(turn, carry):
        cols = pl.ds(pl.multiple_of(start + turn * step, 128), step)
        total = target[:, cols].astype(f32)
        for source in sources:
            total = total + source[:, cols].astype(f32)
        target[:, cols] = total.astype(target.dtype)
        return carry

    lax.fori_loop(0, size // step, one, 0)


def shared_products_kernel(
    normed, normed_other, grad, grad_other, weights, pair, pair_other, hidden, hidden_other,
    beside_high, across_low, mine, beside_low, across_high, out,
    turned, slots, stage, diag, landed, waiting, down_now, out_now,
    load_sem, send_sem, recv_sem, store_sem, down_sem, out_sem,
):
    s, z, _, beside, across = places()
    step = pl.program_id(0)
    lefts = ((normed, normed_other), (grad, grad_other))
    chip_cols = normed.shape[1] // 4
    half = chip_cols // 2
    piece = half // 2
    width = pair.shape[1]
    diagonal = beside + across - s
    chips = [q // 2 for q in (diagonal, beside, across, s)]

    def load(side, q, who):
        cols = pl.ds(pl.multiple_of(chips[q] * chip_cols, 128), chip_cols)
        return pltpu.make_async_copy(lefts[side][who].at[:, cols], slots.at[q % 2, who], load_sem.at[q % 2, who])

    def fetch(side):
        for q in range(2):
            for who in range(2):
                load(side, q, who).start()

    def turn(side):
        for q in range(4):
            for who in range(2):
                load(side, q, who).wait()
                stage[...] = slots[q % 2, who].T
                turned[who, q * half : (q + 1) * half, :] = stage[
                    pl.ds(pl.multiple_of(s % 2 * half, 16), half), :
                ]
                if q < 2:
                    load(side, q + 2, who).start()

    def tile(own, other, start, size):
        cols = pl.ds(start, size)
        block = mm(turned[0], own[:, cols], ((1,), (0,)))
        block = (block + mm(turned[1], other[:, cols], ((1,), (0,)))).astype(bf16)
        parts = [block[n * piece : (n + 1) * piece] for n in range(8)]
        there = pl.ds(pl.multiple_of(step * width + start, 128), size)
        diag[0, :, there] = parts[0]
        diag[1, :, there] = parts[1]
        waiting[0, :, there] = parts[2]
        beside_high[:, cols] = parts[3]
        across_low[:, cols] = parts[4]
        waiting[1, :, there] = parts[5]
        mine[0:piece, cols] = parts[6]
        mine[piece:, cols] = parts[7]

    def multiply(own, other):
        def one(turn, carry):
            tile(own, other, pl.multiple_of(turn * 512, 512), 512)
            return carry

        lax.fori_loop(0, width // 512, one, 0)
        if width % 512:
            tile(own, other, width // 512 * 512, width % 512)

    def push(way, j):
        cols = pl.ds(j * width, width)
        return pltpu.make_async_remote_copy(
            src_ref=diag.at[way, :, cols],
            dst_ref=landed.at[way, :, cols],
            send_sem=send_sem.at[way, j],
            recv_sem=recv_sem.at[way, j],
            device_id=(across if way == 0 else beside, z),
            device_id_type=MESH,
        )

    def store(way, j):
        cols = pl.ds(j * width, width)
        return pltpu.make_async_copy(
            waiting.at[way, :, cols], (beside_low, across_high)[way].at[:, cols], store_sem.at[way, j]
        )

    out_rows = down_now.shape[1]
    out_tiles = weights.shape[0] // out_rows

    def down(t):
        source = weights.at[pl.ds(t * out_rows, out_rows), pl.ds(2 * width, width)]
        return pltpu.make_async_copy(source, down_now.at[t % 2], down_sem.at[t % 2])

    def out_store(t):
        return pltpu.make_async_copy(
            out_now.at[t % 2], out.at[:, pl.ds(t * out_rows, out_rows)], out_sem.at[t % 2]
        )

    def out_product():
        for t in range(out_tiles):
            down(t).wait()
            if t > 1:
                out_store(t - 2).wait()
            out_now[t % 2] = mm(hidden[...], down_now[t % 2], ((1,), (1,))).astype(bf16)
            out_store(t).start()
            if t + 2 < out_tiles:
                down(t + 2).start()

    @pl.when(step == 0)
    def _():
        fetch(0)
        greet([(beside, z), (across, z)])
        turn(0)

    @pl.when(step == 2)
    def _():
        down(0).start()
        down(1).start()
        turn(1)

    pl.when(step < 2)(functools.partial(multiply, pair, pair_other))
    pl.when(step == 1)(functools.partial(fetch, 1))
    pl.when(step == 2)(functools.partial(multiply, hidden, hidden_other))
    for j in range(3):

        @pl.when(step == j)
        def _(j=j):
            push(0, j).start()
            push(1, j).start()

    @pl.when(step == 2)
    def _():
        out_product()
        for j in range(3):
            for way in range(2):
                push(way, j).wait_recv()
                add_columns(waiting.at[way], [landed.at[way]], j * width, width, 384)
                store(way, j).start()
        for j in range(3):
            for way in range(2):
                push(way, j).wait_send()
                store(way, j).wait()
        for t in range(out_tiles - 2, out_tiles):
            out_store(t).wait()


def shared_products(lefts, weights, pair, hidden):
    tok, model = lefts[0].shape
    width = hidden[0].shape[1]
    half = model // 8
    anyspec = pl.BlockSpec(memory_space=pl.ANY)
    dma = pltpu.SemaphoreType.DMA

    def block(rows):
        return pl.BlockSpec((rows, width), lambda j: (0, j))

    pair_spec = pl.BlockSpec((tok, width), lambda j: (0, jnp.minimum(j, 1)))
    hidden_spec = pl.BlockSpec((tok, width), lambda j: (0, 0))
    rows_out = (half // 2, half // 2, half, half // 2, half // 2)
    return pl.pallas_call(
        shared_products_kernel,
        grid=(3,),
        in_specs=[anyspec] * 5 + [pair_spec] * 2 + [hidden_spec] * 2,
        out_specs=[block(rows) for rows in rows_out[:3]] + [anyspec] * 3,
        out_shape=[jax.ShapeDtypeStruct((rows, 3 * width), bf16) for rows in rows_out]
        + [jax.ShapeDtypeStruct((tok, model), bf16)],
        scratch_shapes=[
            pltpu.VMEM((2, 4 * half, tok), bf16),
            pltpu.VMEM((2, 2, tok, 2 * half), bf16),
            pltpu.VMEM((2 * half, tok), bf16),
            pltpu.VMEM((2, half // 2, 3 * width), bf16),
            pltpu.VMEM((2, half // 2, 3 * width), bf16),
            pltpu.VMEM((2, half // 2, 3 * width), bf16),
            pltpu.VMEM((2, 512, width), bf16),
            pltpu.VMEM((2, tok, 512), bf16),
            dma((2, 2)), dma((2, 3)), dma((2, 3)), dma((2, 3)), dma((2,)), dma((2,)),
        ],
        compiler_params=pltpu.CompilerParams(
            collective_id=5, has_side_effects=True, vmem_limit_bytes=60 * 1024 * 1024
        ),
        name="feed_forward_products",
    )(*lefts, weights, *pair, *hidden)


def scatter_kernel(
    normed, normed_other, grad_mix, mix_other, mixed, mixed_other, grad_gelu, gelu_other, grad_branch, rest,
    mlp_low, mlp_high, mixer_w, tokens, gain, mixer_sum, mlp_back, input_grad,
    held, cross, near, lined, left_now, both_now, mixed_now, turned, stage, rest_other, back_now, wide_now, gain_now,
    load_sem, core_send, core_recv, wide_sem,
    flow_send, flow_recv, line_send, line_recv, swap_send, swap_recv, own_sem,
):
    s, z, core, beside, across = places()
    chip_diag, chip_beside, chip_across, chip = 0, 1, 2, 3
    chips = [q // 2 for q in (beside + across - s, beside, across, s)]
    rows = held.shape[1] // 4
    cols = held.shape[2]
    cut = cols // 256 * 128
    ff_part = mlp_low.shape[1] // 3
    tok, model = tokens.shape
    half = 4 * rows
    lru = grad_branch.shape[1]
    lru2 = 2 * lru
    rest_start = lru2 + mixed.shape[1]
    order = (3 * (1 - z // 2), (2 + 3 * z) % 5, 1 + z % 2, z)

    def remote(src, dst, send, recv, target):
        return pltpu.make_async_remote_copy(
            src_ref=src, dst_ref=dst, send_sem=send, recv_sem=recv, device_id=target, device_id_type=MESH
        )

    def span(k):
        return pl.ds(pl.multiple_of(k * rows, 16), rows)

    mine, other = pl.ds(0, tok), pl.ds(tok, tok)
    loads = [
        pltpu.make_async_copy(source, target, load_sem.at[n])
        for n, (source, target) in enumerate(
            (
                (grad_mix, left_now.at[1, mine, :]),
                (mix_other, left_now.at[1, other, :]),
                (mixed, mixed_now.at[mine, :]),
                (mixed_other, mixed_now.at[other, :]),
                (normed, left_now.at[0, mine, :]),
                (normed_other, left_now.at[0, other, :]),
                (grad_gelu, both_now.at[mine, pl.ds(lru, lru)]),
                (gelu_other, both_now.at[other, pl.ds(lru, lru)]),
                (grad_branch, both_now.at[mine, pl.ds(0, lru)]),
            )
        )
    ]

    def push(n):
        if n == 0:
            source, target = grad_branch, both_now.at[other, pl.ds(0, lru)]
        else:
            source = rest.at[pl.ds(pl.multiple_of(chips[n - 1] * 2 * half + (1 - s % 2) * half, 16), half), :]
            target = rest_other.at[n - 1]
        return pltpu.make_async_remote_copy(
            src_ref=source,
            dst_ref=target,
            send_sem=core_send.at[n],
            recv_sem=core_recv.at[n],
            device_id=(core, z),
            device_id_type=MESH,
        )

    def rest_load(q):
        source = rest.at[pl.ds(pl.multiple_of(chips[q] * 2 * half + s % 2 * half, 16), half), :]
        return pltpu.make_async_copy(
            source, held.at[q, :, pl.ds(rest_start, cols - rest_start)], load_sem.at[9 + q]
        )

    def turn(side):
        for q in range(4):
            source = left_now[side, :, pl.ds(pl.multiple_of(chips[q] * 2 * half, 128), 2 * half)]
            stage[...] = source.T
            turned[side, q * half : (q + 1) * half, :] = stage[
                pl.ds(pl.multiple_of(s % 2 * half, 16), half), :
            ]

    def multiply(q, side, first=0, last=None):
        right, start = ((both_now, 0), (mixed_now, lru2))[side]

        def one(turn, carry):
            here = pl.multiple_of(turn * 512, 512)
            block = mm(turned[side, q * half : (q + 1) * half, :], right[:, pl.ds(here, 512)], ((1,), (0,)))
            held[q, :, pl.ds(pl.multiple_of(start + here, 512), 512)] = block.astype(bf16)
            return carry

        lax.fori_loop(first // 512, (right.shape[1] if last is None else last) // 512, one, 0)

    def add_rest(q):
        rest_load(q).wait()
        push(1 + q).wait_recv()
        held[q, :, rest_start:] = add_low(held[q, :, rest_start:], rest_other[q])

    left, right = pl.ds(0, cut), pl.ds(cut, cols - cut)

    def block(q, i, side):
        return held.at[q, span(order[i]), side]

    def flow(i, index):
        send, recv = flow_send.at[i, index], flow_recv.at[i, index]
        to_beside, to_across = (beside, z), (across, z)
        if index == 0:
            return remote(block(chip_diag, i, left), cross.at[i, :, left], send, recv, to_across)
        if index == 1:
            return remote(block(chip_diag, i, right), cross.at[i, :, right], send, recv, to_beside)
        if index == 2:
            return remote(block(chip_beside, i, right), near.at[0, i, :, right], send, recv, to_beside)
        if index == 3:
            return remote(block(chip_beside, i, left), near.at[0, i, :, left], send, recv, to_beside)
        if index == 4:
            return remote(block(chip_across, i, left), near.at[1, i, :, left], send, recv, to_across)
        return remote(block(chip_across, i, right), near.at[1, i, :, right], send, recv, to_across)

    def cross_step(i):
        flow(i, 0).wait_recv()
        add_columns(held.at[chip_beside, span(order[i]), :], [cross.at[i]], 0, cut, 512)
        flow(i, 3).start()
        flow(i, 1).wait_recv()
        add_columns(held.at[chip_across, span(order[i]), :], [cross.at[i]], cut, cols - cut, 384)
        flow(i, 5).start()

    def near_step(i):
        for index in (2, 4, 3, 5):
            flow(i, index).wait_recv()
        add_columns(held.at[chip, span(order[i]), :], [near.at[0, i], near.at[1, i]], 0, cols, 640)

    def line(k, slot, target):
        return remote(
            held.at[chip, span(k), :], lined.at[slot], line_send.at[k], line_recv.at[slot], (s, target)
        )

    def absorb(k, slot, source):
        line(k, slot, source).wait_recv()
        add_columns(held.at[chip, span(k), :], [lined.at[slot]], 0, cols, 640)

    def chain(i):
        k = order[i]
        if i == 3:
            pl.when(z > 0)(lambda: absorb(k, k, z - 1))
            pl.when(z < 3)(lambda: absorb(k, 4, z + 1))
            return

        @pl.when(k > z)
        def _():
            pl.when(z > 0)(lambda: absorb(k, k, z - 1))
            line(k, k, z + 1).start()

        @pl.when(k < z)
        def _():
            pl.when(z < 3)(lambda: absorb(k, k, z + 1))
            pl.when(k == z - 1)(lambda: line(k, 4, z - 1).start())
            pl.when(k < z - 1)(lambda: line(k, k, z - 1).start())

    def chain_drain():
        for i in range(3):
            k = order[i]
            line(k, k, (z + 1) % 4).wait_send()

    def swap(k, high=False):
        to = (z + k) % 4
        here = pl.ds(pl.multiple_of(z * ff_part, 128), ff_part)
        source = (mlp_high if high else mlp_low).at[span(to % 2), :]
        return [
            remote(
                source.at[:, pl.ds(m * ff_part, ff_part)],
                mlp_back.at[m, :, here],
                swap_send.at[k - 1, m],
                swap_recv.at[k - 1, m],
                (s, to),
            )
            for m in range(3)
        ]

    def swap_start(k):
        to = (z + k) % 4

        @pl.when(to < 2)
        def _():
            for copy in swap(k):
                copy.start()

        @pl.when(to >= 2)
        def _():
            for copy in swap(k, True):
                copy.start()

    def own(high=False):
        here = pl.ds(pl.multiple_of(z * ff_part, 128), ff_part)
        source = (mlp_high if high else mlp_low).at[span(z % 2), :]
        return [
            pltpu.make_async_copy(source.at[:, pl.ds(m * ff_part, ff_part)], mlp_back.at[m, :, here], own_sem.at[m])
            for m in range(3)
        ]

    wide_rows = wide_now.shape[0]
    wide_tiles = mixer_w.shape[0] // wide_rows
    wide_start = mixer_w.shape[1] - lru2 - model
    wide_slots = (both_now.at[pl.ds(tok, wide_rows), :], wide_now)

    def wide(j):
        source = mixer_w.at[pl.ds(j * wide_rows, wide_rows), pl.ds(wide_start, lru2)]
        return pltpu.make_async_copy(source, wide_slots[j % 2], wide_sem.at[j % 2])

    plain_loads = [
        pltpu.make_async_copy(tokens, left_now.at[0, pl.ds(0, tok), :], wide_sem.at[2]),
        pltpu.make_async_copy(gain, gain_now, wide_sem.at[3]),
    ]

    def back(first, last):
        for j in range(first, last):
            wide(j).wait()
            back_now[:, pl.ds(j * wide_rows, wide_rows)] = mm(
                both_now[0:tok, :], wide_slots[j % 2][...], ((1,), (1,))
            )
            if j + 2 < wide_tiles:
                wide(j + 2).start()

    def finish_rows(turn, carry):
        at = pl.ds(pl.multiple_of(turn * 16, 16), 16)
        result = left_now[1, at, :].astype(f32) + norm_back(
            left_now[0, at, :].astype(f32), gain_now[GAIN_ONE : GAIN_ONE + 1, :], back_now[at, :]
        )
        left_now[0, at, :] = result.astype(bf16)
        return carry

    for copy in loads:
        copy.start()
    for q in range(4):
        rest_load(q).start()
    greet([(core, z), (beside, z), (across, z)] + [(s, (z + k) % 4) for k in range(1, 4)])
    for n in range(5):
        push(n).start()
    for k in (1, 3, 2):
        swap_start(k)

    @pl.when(z < 2)
    def _():
        for copy in own():
            copy.start()

    @pl.when(z >= 2)
    def _():
        for copy in own(True):
            copy.start()

    for copy in loads[:4]:
        copy.wait()
    turn(1)
    multiply(chip_diag, 1)
    for copy in loads[4:]:
        copy.wait()
    turn(0)
    multiply(chip_diag, 0, lru)
    push(0).wait_recv()
    multiply(chip_diag, 0, 0, lru)
    add_rest(chip_diag)
    for i in range(2):
        flow(i, 0).start()
        flow(i, 1).start()
    for q in (chip_beside, chip_across, chip):
        multiply(q, 0)
        multiply(q, 1)
        add_rest(q)
        if q == chip_beside:
            flow(0, 2).start()
        if q == chip_across:
            flow(0, 4).start()
    for copy in plain_loads:
        copy.start()
    wide(0).start()
    wide(1).start()
    for i in range(4):
        cross_step(i)
        if i + 1 < 4:
            flow(i + 1, 2).start()
            flow(i + 1, 4).start()
        if i + 2 < 4:
            flow(i + 2, 0).start()
            flow(i + 2, 1).start()
        if i > 0:
            near_step(i - 1)
            chain(i - 1)
            back(wide_tiles * (i - 1) // 3, wide_tiles * i // 3)
    for copy in plain_loads:
        copy.wait()
    lax.fori_loop(0, tok // 16, finish_rows, 0)
    finished = pltpu.make_async_copy(left_now.at[0, pl.ds(0, tok), :], input_grad, wide_sem.at[2])
    finished.start()
    near_step(3)
    chain(3)
    done = pltpu.make_async_copy(held.at[chip, span(z), :], mixer_sum, own_sem.at[3])
    done.start()
    for i in range(4):
        for index in range(6):
            flow(i, index).wait_send()
    chain_drain()
    for k in range(1, 4):
        for copy in swap(k):
            copy.wait()
    for copy in own():
        copy.wait()
    for n in range(5):
        push(n).wait_send()
    finished.wait()
    done.wait()


def scatter(rows_pairs, grad_branch, rest, mlp_low, mlp_high, mixer_w, tokens, gain):
    tok, model = tokens.shape
    rows = model // 32
    lru = grad_branch.shape[1]
    cols = 3 * lru + rest.shape[1]
    ff_part = mlp_low.shape[1] // 3
    anyspec = pl.BlockSpec(memory_space=pl.ANY)
    dma = pltpu.SemaphoreType.DMA
    return pl.pallas_call(
        scatter_kernel,
        in_specs=[anyspec] * 15,
        out_specs=[anyspec] * 3,
        out_shape=[
            jax.ShapeDtypeStruct((rows, cols), bf16),
            jax.ShapeDtypeStruct((3, rows, 4 * ff_part), bf16),
            jax.ShapeDtypeStruct((tok, model), bf16),
        ],
        scratch_shapes=[
            pltpu.VMEM((4, 4 * rows, cols), bf16),
            pltpu.VMEM((4, rows, cols), bf16),
            pltpu.VMEM((2, 4, rows, cols), bf16),
            pltpu.VMEM((5, rows, cols), bf16),
            pltpu.VMEM((2, 2 * tok, model), bf16),
            pltpu.VMEM((2 * tok, 2 * lru), bf16),
            pltpu.VMEM((2 * tok, lru), bf16),
            pltpu.VMEM((2, 16 * rows, 2 * tok), bf16),
            pltpu.VMEM((8 * rows, 2 * tok), bf16),
            pltpu.VMEM((4, 4 * rows, rest.shape[1]), bf16),
            pltpu.VMEM((tok, model), f32),
            pltpu.VMEM((128, 2 * lru), bf16),
            pltpu.VMEM(gain.shape, f32),
            dma((13,)), dma((5,)), dma((5,)), dma((4,)),
            dma((4, 6)), dma((4, 6)), dma((4,)), dma((5,)), dma((3, 3)), dma((3, 3)), dma((4,)),
        ],
        compiler_params=pltpu.CompilerParams(
            collective_id=2, has_side_effects=True, vmem_limit_bytes=62 * 1024 * 1024
        ),
        name="scatter_gradients",
    )(*rows_pairs, grad_branch, rest, mlp_low, mlp_high, mixer_w, tokens, gain)


def gather_plain(mixer, gate, up, down):
    groups = lax.axis_size("fsdp")
    part_rows, ff = gate.shape
    own = jnp.stack([w.reshape(part_rows, groups, ff // groups) for w in (gate, up, down)], axis=2)
    mine = lax.all_to_all(jnp.transpose(own, (1, 0, 2, 3)), "fsdp", 0, 0, tiled=True)
    return lax.all_gather(mixer, both, axis=0, tiled=True), mine.reshape(groups * part_rows, -1)


def from_line(shard):
    count = lax.axis_size("fsdp")
    return [shard] + [
        lax.ppermute(shard, "fsdp", [(i, (i + k) % count) for i in range(count)]) for k in range(1, count)
    ]


def swap_cores(shard):
    count = lax.axis_size("seq")
    return lax.ppermute(shard, "seq", [(i, i + 1 - 2 * (i % 2)) for i in range(count)])


def swap_beside(shard):
    return lax.ppermute(shard, "seq", [(i, i ^ 2) for i in range(8)])


def swap_across(shard):
    return lax.ppermute(shard, "seq", [(i, i ^ 4) for i in range(8)])


def add_low(left, right):
    return (left.astype(f32) + right.astype(f32)).astype(bf16)


def scatter_plain(normed, grad_both, grad_mix, mixed, rest, mlp_sum):
    groups = lax.axis_size("fsdp")
    term_wide = mm(normed, grad_both, ((0,), (0,))).astype(bf16)
    term_out = mm(grad_mix, mixed, ((0,), (0,))).astype(bf16)
    mixer_sum = lax.psum_scatter(
        jnp.concatenate([term_wide, term_out, rest], axis=1), "seq", scatter_dimension=0, tiled=True
    )
    mixer_sum = lax.psum_scatter(mixer_sum, "fsdp", scatter_dimension=0, tiled=True)
    ff_part = mlp_sum.shape[1] // 3
    part_rows = mlp_sum.shape[0] // groups
    mlp_sum = mlp_sum.reshape(groups, part_rows, 3, ff_part)
    mlp_back = lax.all_to_all(mlp_sum, "fsdp", 0, 0, tiled=True)
    mlp_back = jnp.transpose(mlp_back, (2, 1, 0, 3)).reshape(3, part_rows, groups * ff_part)
    return mixer_sum, mlp_back


def call_heads(kernel, width, heads, ins, outs, scratch, name):
    def spec(rows, place):
        if place is None:
            return pl.BlockSpec((rows, width), lambda h: (0, h))
        return pl.BlockSpec((width, width), lambda h: (h, place))

    in_specs = [spec(a.shape[0], place) for a, place in ins]
    out_specs = [spec(rows, 0 if rowwise else None) for rows, _, rowwise in outs]
    out_shape = [
        jax.ShapeDtypeStruct((heads * width, width) if rowwise else (rows, heads * width), kind)
        for rows, kind, rowwise in outs
    ]
    return pl.pallas_call(
        kernel,
        grid=(heads,),
        in_specs=in_specs,
        out_specs=out_specs,
        out_shape=out_shape,
        scratch_shapes=[pltpu.VMEM((rows, width), f32) for rows in scratch],
        compiler_params=pltpu.CompilerParams(vmem_limit_bytes=40 * 1024 * 1024),
        cost_estimate=pl.CostEstimate(flops=1, bytes_accessed=1, transcendentals=0),
        name=name,
    )(*[a for a, _ in ins])


def on_device(
    block_input,
    cotangent,
    mixer_gain,
    branch_proj,
    gelu_proj,
    conv_taps,
    conv_bias,
    rate_blocks,
    input_blocks,
    rate_bias,
    input_bias,
    decay_param,
    out_proj,
    mlp_gain,
    gate_proj,
    up_proj,
    down_proj,
):
    groups = lax.axis_size("fsdp")
    part_rows, lru = branch_proj.shape
    width = rate_blocks.shape[1]
    heads = lru // width
    margin = conv_taps.shape[0] - 1
    tokens = block_input[0].astype(f32)
    tok_count, model = tokens.shape
    ff = gate_proj.shape[1]
    ff_part = ff // groups
    grad_out = cotangent[0]

    smalls = jnp.stack(
        [conv_taps[k] for k in range(margin + 1)]
        + [conv_bias, rate_bias, input_bias, decay_param, mixer_gain, mlp_gain],
        axis=1,
    )
    small_count = smalls.shape[1]
    smalls = jnp.pad(smalls, ((0, 0), (0, 128 - small_count)))
    first_own = jnp.concatenate([rate_blocks, input_blocks, smalls], axis=1)
    mixer_own = (first_own, branch_proj, gelu_proj, out_proj)
    custom = lax.axis_size("seq") == 8 and groups == 4
    if custom:
        mixer_w, mlp_mine = gather(*mixer_own, gate_proj, up_proj, down_proj)
    else:
        mixer_w, mlp_mine = gather_plain(jnp.concatenate(mixer_own, axis=1), gate_proj, up_proj, down_proj)
    mlp_w = lax.all_gather(mlp_mine, "seq", axis=0, tiled=True)
    grad_out_late = lax.optimization_barrier((grad_out, mlp_mine))[0]
    if custom:
        grad_pieces = from_line(grad_out_late)
    wide = mixer_w[:, 128 + 2 * width : 128 + 2 * width + 2 * lru]
    proj_out = mixer_w[:, 128 + 2 * width + 2 * lru :]

    small = small_table(mixer_w, 2 * width // 128)
    gain_one, gain_two = small[GAIN_ONE], small[GAIN_TWO]

    normed = norm_rows(tokens, gain_one).astype(bf16)
    both_pre = mm(normed, wide, ((1,), (0,)))
    branch = both_pre[:, :lru].astype(bf16)
    gelu_pre = both_pre[:, lru:]
    prior = from_behind(branch[tok_count - margin :], "seq", 1).astype(f32)
    prior = jnp.concatenate([jnp.zeros((8 - margin, lru), f32), prior], axis=0)
    conv, rate_pre, input_pre, cum, local = call_heads(
        mixer_forward,
        width,
        heads,
        [(branch, None), (prior, None), (small, None), (mixer_w, 0), (mixer_w, 1)],
        [(tok_count, bf16, False)] + [(tok_count, f32, False)] * 4,
        [tok_count + 8],
        "mixer_forward",
    )
    carried = prefix((cum[-1], local[-1]), "seq", False)
    states = local + cum * carried[None]
    mixed = (states * jax.nn.gelu(gelu_pre, approximate=True)).astype(bf16)
    middle = tokens + mm(mixed, proj_out, ((1,), (1,)))
    normed_two = norm_rows(middle, gain_two).astype(bf16)

    if custom:
        normed_all, normed_other, grad_out_all, grad_out_other, first_other, mixed_other = gather_rows(
            normed_two, grad_pieces, normed, mixed
        )
    else:
        normed_all = lax.all_gather(normed_two, "fsdp", axis=0, tiled=True)
        grad_out_all = lax.all_gather(grad_out_late, "fsdp", axis=0, tiled=True)
    w_gate, w_up, w_down = mlp_w[:, :ff_part], mlp_w[:, ff_part : 2 * ff_part], mlp_w[:, 2 * ff_part :]
    if custom:
        hidden, hidden_other, grad_pair, pair_other, grad_normed_part = feed_forward(
            normed_all, grad_out_all, mlp_w
        )
    else:
        gate = mm(normed_all, w_gate, ((1,), (0,)))
        up_val = mm(normed_all, w_up, ((1,), (0,)))
        gelu_gate, gelu_slope = gelu_parts(gate)
        hidden = (gelu_gate * up_val).astype(bf16)
        grad_hidden = mm(grad_out_all, w_down, ((1,), (0,)))
        grad_gate = (grad_hidden * up_val * gelu_slope).astype(bf16)
        grad_up = (grad_hidden * gelu_gate).astype(bf16)
        grad_normed_part = (
            mm(grad_gate, w_gate, ((1,), (1,))) + mm(grad_up, w_up, ((1,), (1,)))
        ).astype(bf16)
    grad_normed_two = lax.psum_scatter(grad_normed_part, "fsdp", scatter_dimension=0, tiled=True)
    if custom:
        half = model // 16
        beside_high, across_low, mine, beside_low, across_high, out_part = shared_products(
            (normed_all, normed_other, grad_out_all, grad_out_other),
            mlp_w,
            (grad_pair, pair_other),
            (hidden, hidden_other),
        )
        from_beside_high, from_across_low = swap_beside(beside_high), swap_across(across_low)
    else:
        grad_pair = jnp.concatenate([grad_gate, grad_up], axis=1)
        term_pair = mm(normed_all, grad_pair, ((0,), (0,))).astype(bf16)
        term_down = mm(grad_out_all, hidden, ((0,), (0,))).astype(bf16)
        pair_sum = lax.psum_scatter(term_pair, "seq", scatter_dimension=0, tiled=True)
        down_sum = lax.psum_scatter(term_down, "seq", scatter_dimension=0, tiled=True)
        mlp_sum = jnp.concatenate([pair_sum, down_sum], axis=1)
        out_part = mm(hidden, w_down, ((1,), (1,))).astype(bf16)
    out_sum = lax.psum_scatter(out_part, "fsdp", scatter_dimension=0, tiled=True)
    grad_normed_two = grad_normed_two.astype(f32)

    grad_middle = grad_out.astype(f32) + norm_back(middle, gain_two, grad_normed_two)
    grad_mix = grad_middle.astype(bf16)
    if custom:
        mix_other = swap_cores(grad_mix)
    grad_mixed = mm(grad_mix, proj_out, ((1,), (0,)))
    carried_rows = jnp.broadcast_to(carried[None], (8, lru))
    grad_gelu_pre, rev_cum, rev_grad, pair_grad = call_heads(
        mixer_backward_scan,
        width,
        heads,
        [(a, None) for a in (grad_mixed, gelu_pre, rate_pre, cum, local, carried_rows, small)],
        [(tok_count, bf16, False), (tok_count, f32, False), (tok_count, f32, False), (8, f32, False)],
        [tok_count + 8],
        "mixer_backward_scan",
    )
    if custom:
        from_beside_high, from_across_low, pair_grad = lax.optimization_barrier(
            (from_beside_high, from_across_low, pair_grad)
        )
    if custom:
        gelu_other = swap_cores(grad_gelu_pre)
    incoming = prefix((cum[-1], pair_grad[0]), "seq", True)
    if custom:
        beside_low, across_high, incoming = lax.optimization_barrier((beside_low, across_high, incoming))
        from_beside_low, from_across_high = swap_beside(beside_low), swap_across(across_high)
    incoming_rows = jnp.broadcast_to(incoming[None], (8, lru))
    own, head, rate_w_grad, input_w_grad, sums = call_heads(
        mixer_backward,
        width,
        heads,
        [
            (a, None)
            for a in (rev_cum, rev_grad, incoming_rows, cum, local, carried_rows, rate_pre, input_pre, conv, branch, prior, small)
        ]
        + [(mixer_w, 0), (mixer_w, 1)],
        [(tok_count, f32, False), (8, f32, False), (0, bf16, True), (0, bf16, True), (8, f32, False)],
        [tok_count + 8, tok_count + 16],
        "mixer_backward",
    )
    received = from_behind(head[8 - margin :], "seq", -1)
    grad_branch = jnp.concatenate(
        [own[: tok_count - margin], own[tok_count - margin :] + received], axis=0
    ).astype(bf16)
    grad_both = jnp.concatenate([grad_branch, grad_gelu_pre], axis=1)
    vectors = jnp.pad(sums.T, ((0, 0), (0, 128 - sums.shape[0]))).astype(bf16)
    rest = jnp.concatenate([rate_w_grad, input_w_grad, vectors], axis=1)
    if custom:
        low = add_low(mine[:half], from_across_low)
        high = add_low(mine[half:], from_beside_high)
        low, high, grad_branch = lax.optimization_barrier((low, high, grad_branch))
        low, high = add_low(low, from_beside_low), add_low(high, from_across_high)
        mixer_sum, mlp_back, input_grad = scatter(
            (normed, first_other, grad_mix, mix_other, mixed, mixed_other, grad_gelu_pre, gelu_other),
            grad_branch, rest, low, high, mixer_w, block_input[0], small,
        )
    else:
        mixer_sum, mlp_back = scatter_plain(normed, grad_both, grad_mix, mixed, rest, mlp_sum)
        grad_normed = mm(grad_both, wide, ((1,), (1,)))
        input_grad = (grad_middle + norm_back(tokens, gain_one, grad_normed)).astype(bf16)
    input_grad = input_grad[None]
    middle = lax.optimization_barrier((middle, mixer_sum))[0]
    block_output = (middle + out_sum.astype(f32)).astype(bf16)[None]
    mlp_grads = [mlp_back[m].astype(f32) for m in range(3)]
    mixer_sum = mixer_sum.astype(f32)
    edges = [lru, 2 * lru, 3 * lru, 3 * lru + width, 3 * lru + 2 * width]
    dbranch, dgelu, dout, drate, dinput, vec = jnp.split(mixer_sum, edges, axis=1)
    vec = vec.T
    return (
        block_output,
        input_grad,
        gain_back(mixer_gain, (branch_proj, dbranch), (gelu_proj, dgelu)),
        dbranch,
        dgelu,
        vec[: margin + 1],
        vec[7],
        drate,
        dinput,
        vec[4],
        vec[5],
        vec[6],
        dout,
        gain_back(mlp_gain, (gate_proj, mlp_grads[0]), (up_proj, mlp_grads[1])),
        mlp_grads[0],
        mlp_grads[1],
        mlp_grads[2],
    )


def solution(mesh):
    tokens = P("fsdp", "seq", None)
    vector = P(both)
    matrix = P(both, None)
    taps = P(None, both)
    return jax.shard_map(
        on_device,
        mesh=mesh,
        in_specs=(
            tokens, tokens, vector, matrix, matrix, taps, vector, matrix, matrix,
            vector, vector, vector, matrix, vector, matrix, matrix, matrix,
        ),
        out_specs=(
            tokens, tokens, vector, matrix, matrix, taps, vector, matrix, matrix,
            vector, vector, vector, matrix, vector, matrix, matrix, matrix,
        ),
        check_vma=False,
    )
```

```python
import functools

import jax
import jax.numpy as jnp
from jax import lax
from jax.experimental import pallas as pl
from jax.experimental.pallas import tpu as pltpu
from jax.sharding import PartitionSpec as P

epsilon = 1e-06
f32 = jnp.float32
bf16 = jnp.bfloat16
both = ("seq", "fsdp")
MESH = pl.DeviceIdType.MESH
TAP, CONV_BIAS, RATE_BIAS, INPUT_BIAS, SOFT, SOFT_SLOPE, GAIN_ONE, GAIN_TWO = 0, 4, 5, 6, 7, 8, 9, 10
GELU_C = 0.7978845608028654
GELU_A = 0.044715


def from_behind(shard, axis, by):
    devices = lax.axis_size(axis)
    pairs = [(i, i + by) for i in range(devices) if 0 <= i + by < devices]
    return lax.ppermute(shard, axis, pairs)


def prefix(part, axis, reverse):
    count = lax.axis_size(axis)
    place = lax.axis_index(axis)
    gathered = lax.all_gather(jnp.stack(part), axis)
    state = jnp.zeros_like(part[1])
    for hop in range(count):
        source = count - 1 - hop if reverse else hop
        ahead = source > place if reverse else source < place
        state = jnp.where(ahead, gathered[source, 1] + gathered[source, 0] * state, state)
    return state


def norm_rows(values, scales):
    return values * lax.rsqrt(jnp.mean(values * values, axis=-1, keepdims=True) + epsilon) * scales


def norm_back(values, scales, grads):
    inverse = lax.rsqrt(jnp.mean(values * values, axis=-1, keepdims=True) + epsilon)
    scaled = grads * scales
    shared = jnp.mean(values * scaled, axis=-1, keepdims=True)
    return inverse * scaled - values * (inverse * inverse * inverse * shared)


def gain_back(*pairs):
    return sum(jnp.sum(weight.astype(f32) * grad, axis=1) for weight, grad in pairs)


def gelu_parts(x):
    inner = jnp.tanh(GELU_C * (x + GELU_A * x * x * x))
    return 0.5 * x * (1.0 + inner), 0.5 * (1.0 + inner) + 0.5 * x * (1.0 - inner * inner) * (
        GELU_C * (1.0 + 3.0 * GELU_A * x * x)
    )


def mm(left, right, dims):
    return lax.dot_general(left, right, (dims, ((), ())), preferred_element_type=f32)


def sigmoid(x):
    return 1.0 / (1.0 + jnp.exp(-x))


def scan_rows(decay, value, reverse):
    rows = decay.shape[0]
    place = lax.broadcasted_iota(jnp.int32, decay.shape, 0)
    step = 1
    while step < rows:
        shift = rows - step if reverse else step
        inside = place < rows - step if reverse else place >= step
        before_value = jnp.where(inside, pltpu.roll(value, shift, 0), 0.0)
        before_decay = jnp.where(inside, pltpu.roll(decay, shift, 0), 1.0)
        value = value + decay * before_value
        decay = decay * before_decay
        step *= 2
    return decay, value


def gates(rate_pre, input_pre, soft):
    rate = sigmoid(rate_pre)
    log_decay = -8.0 * rate * soft
    decay = jnp.exp(log_decay)
    square = decay * decay
    root = jnp.sqrt(-jnp.tanh(log_decay) * (1.0 + square))
    return rate, decay, square, root, sigmoid(input_pre)


def table_kernel(columns, table):
    rows = columns[...].T[0:16, :].astype(f32)
    decay_param = rows[7:8, :]
    fast = jnp.exp(-decay_param)
    table[0:7, :] = rows[0:7, :]
    table[7:8, :] = jnp.log1p(fast)
    table[8:9, :] = -fast / (1.0 + fast)
    table[9:11, :] = rows[8:10, :]
    table[11:16, :] = jnp.zeros((5, rows.shape[1]), f32)


def small_table(mixer_w, block):
    model = mixer_w.shape[0]
    return pl.pallas_call(
        table_kernel,
        grid=(1,),
        in_specs=[pl.BlockSpec((model, 128), lambda i: (0, block))],
        out_specs=pl.BlockSpec((16, model), lambda i: (0, 0)),
        out_shape=jax.ShapeDtypeStruct((16, model), f32),
        name="small_table",
    )(mixer_w)


def mixer_in_kernel(tokens, table, weights, normed, branch, gelu_pre):
    step = pl.program_id(0)

    @pl.when(step == 0)
    def _():
        normed[...] = norm_rows(tokens[...].astype(f32), table[GAIN_ONE : GAIN_ONE + 1, :]).astype(bf16)

    product = mm(normed[...], weights[...], ((1,), (0,)))
    half = pl.num_programs(0) // 2

    @pl.when(step < half)
    def _():
        branch[...] = product.astype(bf16)

    @pl.when(step >= half)
    def _():
        gelu_pre[...] = product


def mixer_in(tokens, table, mixer_w, lru, start):
    tok, model = tokens.shape
    tile = start
    tiles = lru // tile
    return pl.pallas_call(
        mixer_in_kernel,
        grid=(2 * tiles,),
        in_specs=[
            pl.BlockSpec((tok, model), lambda j: (0, 0)),
            pl.BlockSpec(table.shape, lambda j: (0, 0)),
            pl.BlockSpec((model, tile), lambda j: (0, 1 + j)),
        ],
        out_specs=[
            pl.BlockSpec((tok, model), lambda j: (0, 0)),
            pl.BlockSpec((tok, tile), lambda j: (0, jnp.minimum(j, tiles - 1))),
            pl.BlockSpec((tok, tile), lambda j: (0, jnp.maximum(j - tiles, 0))),
        ],
        out_shape=[
            jax.ShapeDtypeStruct((tok, model), bf16),
            jax.ShapeDtypeStruct((tok, lru), bf16),
            jax.ShapeDtypeStruct((tok, lru), f32),
        ],
        compiler_params=pltpu.CompilerParams(vmem_limit_bytes=40 * 1024 * 1024),
        cost_estimate=pl.CostEstimate(flops=1, bytes_accessed=1, transcendentals=0),
        name="mixer_in",
    )(tokens, table, mixer_w)


def finish_kernel(mixer, mlp, branch, gelu, gate, up, dbranch, dgelu, dout, drate, dinput, dgate, dup, ddown, totals):
    lru = branch.shape[1]
    width = drate.shape[1]
    ff = gate.shape[1]

    def met(weight, grad, cols):
        def one(turn, carry):
            here = pl.ds(pl.multiple_of(turn * 512, 512), 512)
            return carry + jnp.sum(weight[:, here].astype(f32) * grad[:, here], axis=1, keepdims=True)

        return lax.fori_loop(0, cols // 512, one, jnp.zeros((weight.shape[0], 1), f32))

    start = 0
    for grad in (dbranch, dgelu, dout, drate, dinput):
        size = grad.shape[1]
        grad[...] = mixer[:, start : start + size].astype(f32)
        start += size
    for m, grad in enumerate((dgate, dup, ddown)):
        grad[...] = mlp[m].astype(f32)
    first = met(branch, dbranch, lru) + met(gelu, dgelu, lru)
    second = met(gate, dgate, ff) + met(up, dup, ff)
    totals[...] = jnp.concatenate([jnp.broadcast_to(first, (first.shape[0], 128)), jnp.broadcast_to(second, (second.shape[0], 128))], axis=1)


def finish(mixer, mlp, branch, gelu, gate, up, width):
    rows, ff = gate.shape
    lru = branch.shape[1]
    step = 16

    def spec(cols):
        return pl.BlockSpec((step, cols), lambda i: (i, 0))

    sizes = [lru, lru, lru, width, width, ff, ff, ff, 256]
    return pl.pallas_call(
        finish_kernel,
        grid=(rows // step,),
        in_specs=[
            spec(mixer.shape[1]), pl.BlockSpec((3, step, ff), lambda i: (0, i, 0)),
            spec(lru), spec(lru), spec(ff), spec(ff),
        ],
        out_specs=[spec(cols) for cols in sizes],
        out_shape=[jax.ShapeDtypeStruct((rows, cols), f32) for cols in sizes],
        compiler_params=pltpu.CompilerParams(vmem_limit_bytes=40 * 1024 * 1024),
        name="finish_gradients",
    )(mixer, mlp, branch, gelu, gate, up)


def mixer_forward(branch, prior, small, rate_w, input_w, conv, rate_pre, input_pre, cum, local, ext):
    rows = branch.shape[0]
    ext[0:8, :] = prior[...]
    ext[8:, :] = branch[...].astype(f32)
    total = small[CONV_BIAS : CONV_BIAS + 1, :] + small[TAP : TAP + 1, :] * ext[8:, :]
    for offset in range(1, 4):
        total = total + small[TAP + offset : TAP + offset + 1, :] * ext[pl.ds(8 - offset, rows), :]
    low = total.astype(bf16)
    conv[...] = low
    rate = mm(low, rate_w[...], ((1,), (0,))) + small[RATE_BIAS : RATE_BIAS + 1, :]
    inp = mm(low, input_w[...], ((1,), (0,))) + small[INPUT_BIAS : INPUT_BIAS + 1, :]
    rate_pre[...] = rate
    input_pre[...] = inp
    _, decay, _, root, opened = gates(rate, inp, small[SOFT : SOFT + 1, :])
    product, states = scan_rows(decay, root * opened * low.astype(f32), False)
    cum[...] = product
    local[...] = states


def mixer_backward_scan(grad_mixed, gelu_pre, rate_pre, cum, local, carried, small, grad_pre, rev_cum, rev_grad, pair, ext):
    rows = grad_mixed.shape[0]
    states = local[...] + cum[...] * carried[0:1, :]
    value, slope = gelu_parts(gelu_pre[...])
    grad = grad_mixed[...]
    grad_pre[...] = (grad * states * slope).astype(bf16)
    decay = jnp.exp(-8.0 * sigmoid(rate_pre[...]) * small[SOFT : SOFT + 1, :])
    ext[0:rows, :] = decay
    ext[rows:, :] = jnp.ones((8, decay.shape[1]), f32)
    product, back = scan_rows(ext[pl.ds(1, rows), :], grad * value, True)
    rev_cum[...] = product
    rev_grad[...] = back
    pair[...] = jnp.broadcast_to(decay[0:1, :] * back[0:1, :], pair.shape)


def mixer_backward(
    rev_cum, rev_grad, incoming, cum, local, carried, rate_pre, input_pre, conv, branch, prior, small, rate_w, input_w,
    own, head, rate_w_grad, input_w_grad, sums, ext, gext,
):
    rows = rev_cum.shape[0]
    soft = small[SOFT : SOFT + 1, :]
    grad_states = rev_grad[...] + rev_cum[...] * incoming[0:1, :]
    rate, decay, square, root, opened = gates(rate_pre[...], input_pre[...], soft)
    ext[0:8, :] = jnp.broadcast_to(carried[0:1, :], (8, carried.shape[1]))
    ext[8:, :] = local[...] + cum[...] * carried[0:1, :]
    before = ext[pl.ds(7, rows), :]
    low = conv[...]
    conv_in = low.astype(f32)
    grad_log = grad_states * decay * before - grad_states * opened * conv_in * square / root
    driven = grad_states * root
    grad_input = (driven * conv_in * opened * (1.0 - opened)).astype(bf16)
    by_rate = grad_log * (-8.0 * rate)
    grad_rate = (by_rate * soft * (1.0 - rate)).astype(bf16)
    sums[6:7, :] = jnp.sum(by_rate, axis=0, keepdims=True) * small[SOFT_SLOPE : SOFT_SLOPE + 1, :]
    sums[4:5, :] = jnp.sum(grad_rate.astype(f32), axis=0, keepdims=True)
    sums[5:6, :] = jnp.sum(grad_input.astype(f32), axis=0, keepdims=True)
    rate_w_grad[...] = mm(low, grad_rate, ((0,), (0,))).astype(rate_w_grad.dtype)
    input_w_grad[...] = mm(low, grad_input, ((0,), (0,))).astype(input_w_grad.dtype)
    grad_conv = (
        driven * opened
        + mm(grad_rate, rate_w[...], ((1,), (1,)))
        + mm(grad_input, input_w[...], ((1,), (1,)))
    )
    sums[7:8, :] = jnp.sum(grad_conv, axis=0, keepdims=True)
    ext[0:8, :] = prior[...]
    ext[8:, :] = branch[...].astype(f32)
    gext[0:8, :] = jnp.zeros((8, grad_conv.shape[1]), f32)
    gext[8 : 8 + rows, :] = grad_conv
    gext[8 + rows :, :] = jnp.zeros((8, grad_conv.shape[1]), f32)
    back = jnp.zeros_like(grad_conv)
    front = jnp.zeros((8, grad_conv.shape[1]), f32)
    for offset in range(4):
        tap = small[TAP + offset : TAP + offset + 1, :]
        sums[offset : offset + 1, :] = jnp.sum(
            grad_conv * ext[pl.ds(8 - offset, rows), :], axis=0, keepdims=True
        )
        back = back + tap * gext[pl.ds(8 + offset, rows), :]
        front = front + tap * gext[pl.ds(offset, 8), :]
    own[...] = back
    head[...] = front


def places():
    s = lax.axis_index("seq")
    z = lax.axis_index("fsdp")
    core = s + 1 - 2 * (s % 2)
    beside = s + 2 - 4 * ((s // 2) % 2)
    across = s + 4 - 8 * (s // 4)
    return s, z, core, beside, across


def greet(peers):
    barrier = pltpu.get_barrier_semaphore()
    for peer in peers:
        pl.semaphore_signal(barrier, inc=1, device_id=peer, device_id_type=MESH)
    pl.semaphore_wait(barrier, len(peers))


def gather_kernel(
    first, branch, gelu, outer, gate, up, down, mixer_all, mlp_mine,
    mixer, load_sem, flow_send, flow_recv, line_send, line_recv, swap_send, swap_recv, own_sem,
):
    s, z, core, beside, across = places()
    rows, cols = mixer.shape
    ff_part = mlp_mine.shape[1] // 3
    cut = cols // 256 * 128
    diag = beside + across - s
    loads, start = [], 0
    for n, part in enumerate((first, branch, gelu, outer)):
        size = part.shape[1]
        loads.append(pltpu.make_async_copy(part, mixer.at[:, pl.ds(start, size)], load_sem.at[n]))
        loads[-1].start()
        start += size
    greet([(core, z), (beside, z), (across, z)] + [(s, (z + k) % 4) for k in range(1, 4)])

    def remote(src, dst, send, recv, target):
        return pltpu.make_async_remote_copy(
            src_ref=src, dst_ref=dst, send_sem=send, recv_sem=recv, device_id=target, device_id_type=MESH
        )

    def piece(seq, zz, half=None):
        span = pl.ds(pl.multiple_of((seq * 4 + zz) * rows, 16), rows)
        if half is None:
            return mixer_all.at[span, :]
        return mixer_all.at[span, pl.ds(0, cut) if half == 0 else pl.ds(cut, cols - cut)]

    def flow(zz, index, seq, half, target, src=None):
        ref = piece(seq, zz, half)
        return remote(
            ref if src is None else src, ref, flow_send.at[zz, index], flow_recv.at[zz, index], (target, z)
        )

    def sends(zz, src=None):
        return [
            flow(zz, 0, s, None, beside, src),
            flow(zz, 1, s, None, across, src),
            flow(zz, 4, s, None, core, src),
        ]

    def spread(zz, src=None):
        for copy in sends(zz, src):
            copy.start()

    def relay(zz):
        flow(zz, 0, beside, None, beside).wait_recv()
        flow(zz, 3, beside, 0, across).start()
        flow(zz, 5, beside, None, core).start()
        flow(zz, 1, across, None, across).wait_recv()
        flow(zz, 2, across, 1, beside).start()
        flow(zz, 6, across, None, core).start()

    def finish(zz):
        flow(zz, 3, diag, 0, across).wait_recv()
        flow(zz, 7, diag, 0, core).start()
        flow(zz, 2, diag, 1, beside).wait_recv()
        flow(zz, 8, diag, 1, core).start()

    def drain(zz, src=None):
        for copy in sends(zz, src):
            copy.wait_send()
        flow(zz, 3, beside, 0, across).wait_send()
        flow(zz, 5, beside, None, core).wait_send()
        flow(zz, 2, across, 1, beside).wait_send()
        flow(zz, 6, across, None, core).wait_send()
        flow(zz, 7, diag, 0, core).wait_send()
        flow(zz, 8, diag, 1, core).wait_send()
        flip = core - s
        flow(zz, 4, core, None, core).wait_recv()
        flow(zz, 5, beside + flip, None, core).wait_recv()
        flow(zz, 6, across + flip, None, core).wait_recv()
        flow(zz, 7, diag + flip, 0, core).wait_recv()
        flow(zz, 8, diag + flip, 1, core).wait_recv()

    def line(zz, up_way, hop, src=None):
        ref = piece(s, zz)
        way = 0 if up_way else 1
        target = z + 1 if up_way else z - 1
        return remote(
            ref if src is None else src, ref, line_send.at[way, hop], line_recv.at[way, hop], (s, target)
        )

    def line_hop(hop):
        def below():
            line(z - hop, True, hop - 1).wait_recv()
            pl.when(z < 3)(lambda: line(z - hop, True, hop).start())

        def above():
            line(z + hop, False, hop - 1).wait_recv()
            pl.when(z > 0)(lambda: line(z + hop, False, hop).start())

        pl.when(z >= hop)(below)
        pl.when(z + hop <= 3)(above)

    def at_hop(hop, act):
        pl.when(z >= hop)(lambda: act(z - hop))
        pl.when(z + hop <= 3)(lambda: act(z + hop))

    def landing(m, zz):
        return mlp_mine.at[pl.ds(pl.multiple_of(zz * rows, 16), rows), pl.ds(m * ff_part, ff_part)]

    def columns(m, zz):
        return (gate, up, down)[m].at[:, pl.ds(pl.multiple_of(zz * ff_part, 128), ff_part)]

    def swap(k, m, arriving=False):
        to = (z + k) % 4
        came = (z + 4 - k) % 4
        return remote(
            columns(m, to), landing(m, came if arriving else z), swap_send.at[k - 1, m], swap_recv.at[k - 1, m], (s, to)
        )

    local = [pltpu.make_async_copy(columns(m, z), landing(m, z), own_sem.at[m]) for m in range(3)]
    local.append(pltpu.make_async_copy(mixer, piece(s, z), own_sem.at[3]))
    for copy in loads:
        copy.wait()

    pl.when(z < 3)(lambda: line(z, True, 0, mixer).start())
    pl.when(z > 0)(lambda: line(z, False, 0, mixer).start())
    spread(z, mixer)
    for copy in local:
        copy.start()
    line_hop(1)
    at_hop(1, spread)
    relay(z)
    line_hop(2)
    at_hop(2, spread)
    finish(z)
    at_hop(1, relay)
    line_hop(3)
    at_hop(3, spread)
    for k in (1, 3, 2):
        for m in range(3):
            swap(k, m).start()
    at_hop(1, finish)
    at_hop(2, relay)
    at_hop(3, relay)
    at_hop(2, finish)
    at_hop(3, finish)
    drain(z, mixer)
    for hop in range(1, 4):
        at_hop(hop, drain)
    for copy in local:
        copy.wait()
    for k in (1, 3, 2):
        for m in range(3):
            swap(k, m).wait_send()
            swap(k, m, True).wait_recv()
    pl.when(z < 3)(lambda: line(z, True, 0, mixer).wait_send())
    pl.when(z > 0)(lambda: line(z, False, 0, mixer).wait_send())
    for hop in range(1, 3):
        pl.when((z >= hop) & (z < 3))(lambda: line(z - hop, True, hop).wait_send())
        pl.when((z + hop <= 3) & (z > 0))(lambda: line(z + hop, False, hop).wait_send())


def gather(first, branch, gelu, outer, gate, up, down):
    rows = first.shape[0]
    cols = first.shape[1] + branch.shape[1] + gelu.shape[1] + outer.shape[1]
    ff_part = gate.shape[1] // 4
    anyspec = pl.BlockSpec(memory_space=pl.ANY)
    dma = pltpu.SemaphoreType.DMA
    return pl.pallas_call(
        gather_kernel,
        in_specs=[anyspec] * 7,
        out_specs=[anyspec] * 2,
        out_shape=[
            jax.ShapeDtypeStruct((32 * rows, cols), bf16),
            jax.ShapeDtypeStruct((4 * rows, 3 * ff_part), bf16),
        ],
        scratch_shapes=[
            pltpu.VMEM((rows, cols), bf16), dma((4,)),
            dma((4, 9)), dma((4, 9)), dma((2, 3)), dma((2, 3)), dma((3, 3)), dma((3, 3)), dma((4,)),
        ],
        compiler_params=pltpu.CompilerParams(collective_id=1, has_side_effects=True),
        name="gather_weights",
    )(first, branch, gelu, outer, gate, up, down)


def rows_kernel(
    normed, grad0, grad1, grad2, grad3, first, mixed, normed_all, normed_other, grad_all, grad_other,
    first_other, mixed_other, line_send, line_recv, core_send, core_recv, own_sem, held, give_send, give_recv,
):
    s, z, core, _, _ = places()
    tok = normed.shape[0]
    cuts = 4
    grads = (grad0, grad1, grad2, grad3)
    greet([(core, z)] + [(s, (z + k) % 4) for k in range(1, 4)])

    def rows(ref, zz):
        return ref.at[pl.ds(pl.multiple_of(zz * tok, 16), tok), :]

    def remote(src, dst, send, recv, target):
        return pltpu.make_async_remote_copy(
            src_ref=src, dst_ref=dst, send_sem=send, recv_sem=recv, device_id=target, device_id_type=MESH
        )

    def parts(ref):
        size = tok // cuts
        return [ref.at[pl.ds(n * size, size), :] for n in range(cuts)]

    def line(zz, up_way, hop):
        way = 0 if up_way else 1
        target = z + 1 if up_way else z - 1
        src = normed if hop == 0 else rows(normed_all, zz)
        dst = rows(normed_all, zz)
        return [
            remote(a, b, line_send.at[way, hop, n], line_recv.at[way, hop, n], (s, target))
            for n, (a, b) in enumerate(zip(parts(src), parts(dst)))
        ]

    def over(zz, own=False):
        src = normed if own else rows(normed_all, zz)
        return remote(src, rows(normed_other, zz), core_send.at[0, zz], core_recv.at[0, zz], (core, z))

    def grad_over(k):
        zz = (z + 4 - k) % 4
        return remote(grads[k], rows(grad_other, zz), core_send.at[1, zz], core_recv.at[1, zz], (core, z))

    def line_start(zz, up_way, hop):
        for copy in line(zz, up_way, hop):
            copy.start()

    def line_drain(zz, up_way, hop):
        for copy in line(zz, up_way, hop):
            copy.wait_send()

    def hop_step(hop):
        def below():
            for came, on in zip(line(z - hop, True, hop - 1), line(z - hop, True, hop) if hop < 3 else [None] * cuts):
                came.wait_recv()
                if on is not None:
                    pl.when(z < 3)(on.start)
            over(z - hop).start()

        def above():
            for came, on in zip(line(z + hop, False, hop - 1), line(z + hop, False, hop) if hop < 3 else [None] * cuts):
                came.wait_recv()
                if on is not None:
                    pl.when(z > 0)(on.start)
            over(z + hop).start()

        pl.when(z >= hop)(below)
        pl.when(z + hop <= 3)(above)

    given = [
        remote(source, target, give_send.at[n], give_recv.at[n], (core, z))
        for n, (source, target) in enumerate(((first, first_other), (mixed, mixed_other)))
    ]
    local = [pltpu.make_async_copy(grads[k], held.at[k], own_sem.at[k]) for k in range(4)]
    local.append(pltpu.make_async_copy(normed, held.at[4], own_sem.at[4]))
    stored = [
        pltpu.make_async_copy(held.at[k], rows(grad_all, (z + 4 - k) % 4), own_sem.at[k]) for k in range(4)
    ]
    stored.append(pltpu.make_async_copy(held.at[4], rows(normed_all, z), own_sem.at[4]))
    pl.when(z < 3)(lambda: line_start(z, True, 0))
    pl.when(z > 0)(lambda: line_start(z, False, 0))
    over(z, True).start()
    for copy in local:
        copy.start()
    for k in range(4):
        grad_over(k).start()
    for copy in given:
        copy.start()
    for copy, store in zip(local, stored):
        copy.wait()
        store.start()
    for hop in range(1, 4):
        hop_step(hop)
    for copy in stored:
        copy.wait()
    for k in range(4):
        grad_over(k).wait()
    for copy in given:
        copy.wait()
    over(z, True).wait()
    for k in range(1, 4):
        over((z + k) % 4).wait()
    pl.when(z < 3)(lambda: line_drain(z, True, 0))
    pl.when(z > 0)(lambda: line_drain(z, False, 0))
    for hop in range(1, 3):
        pl.when((z >= hop) & (z < 3))(lambda: line_drain(z - hop, True, hop))
        pl.when((z + hop <= 3) & (z > 0))(lambda: line_drain(z + hop, False, hop))


def gather_rows(normed, grads, first, mixed):
    tok, model = normed.shape
    anyspec = pl.BlockSpec(memory_space=pl.ANY)
    dma = pltpu.SemaphoreType.DMA
    return pl.pallas_call(
        rows_kernel,
        in_specs=[anyspec] * 7,
        out_specs=[anyspec] * 6,
        out_shape=[jax.ShapeDtypeStruct((4 * tok, model), bf16)] * 4
        + [jax.ShapeDtypeStruct(first.shape, bf16), jax.ShapeDtypeStruct(mixed.shape, bf16)],
        scratch_shapes=[
            dma((2, 3, 4)), dma((2, 3, 4)), dma((2, 4)), dma((2, 4)), dma((5,)),
            pltpu.VMEM((5, tok, model), bf16), dma((2,)), dma((2,)),
        ],
        compiler_params=pltpu.CompilerParams(collective_id=3, has_side_effects=True),
        name="gather_rows",
    )(normed, *grads, first, mixed)


def column_tiles(cols, size=512):
    return [(start, min(size, cols - start)) for start in range(0, cols, size)]


def feed_forward_kernel(
    normed, grad_out, weights, hidden, hidden_other, pair, pair_other, back,
    held, hidden_now, pair_now, sems, store_sem, core_send, core_recv,
):
    s, z, core, _, _ = places()
    step = pl.program_id(0)
    ff_part = held.shape[2]
    model = held.shape[1]
    rows = normed.shape[0]
    tiles = column_tiles(ff_part)
    made = ((hidden_now, hidden, hidden_other), (pair_now, pair, pair_other))

    def load(n, m):
        start, size = tiles[n]
        return pltpu.make_async_copy(
            weights.at[:, pl.ds(m * ff_part + start, size)], held.at[m, :, pl.ds(start, size)], sems.at[n, m]
        )

    def kept(n, turn):
        now, mine, _ = made[n]
        return pltpu.make_async_copy(now.at[turn], mine.at[pl.ds(turn * rows, rows), :], store_sem.at[turn, n])

    def handed(n, turn):
        now, _, other = made[n]
        return pltpu.make_async_remote_copy(
            src_ref=now.at[turn],
            dst_ref=other.at[pl.ds(turn * rows, rows), :],
            send_sem=core_send.at[turn, n],
            recv_sem=core_recv.at[turn, n],
            device_id=(core, z),
            device_id_type=MESH,
        )

    @pl.when(step == 0)
    def _():
        for n in range(len(tiles)):
            for m in range(3):
                load(n, m).start()
        greet([(core, z)])

    for n, (start, size) in enumerate(tiles):
        cols = slice(start, start + size)

        @pl.when(step == 0)
        def _(n=n):
            for m in range(3):
                load(n, m).wait()

        gate = mm(normed[...], held[0, :, cols], ((1,), (0,)))
        value, slope = gelu_parts(gate)
        up = mm(normed[...], held[1, :, cols], ((1,), (0,)))
        hidden_now[step, :, cols] = (value * up).astype(bf16)
        grad_hidden = mm(grad_out[...], held[2, :, cols], ((1,), (0,)))
        pair_now[step, :, cols] = (grad_hidden * up * slope).astype(bf16)
        pair_now[step, :, slice(ff_part + start, ff_part + start + size)] = (grad_hidden * value).astype(bf16)

    for turn in range(2):

        @pl.when(step == turn)
        def _(turn=turn):
            for n in range(2):
                handed(n, turn).start()
                kept(n, turn).start()

    def back_tile(turn, carry):
        cols = pl.ds(pl.multiple_of(turn * 512, 512), 512)
        total = mm(pair_now[step, :, :ff_part], held[0, cols, :], ((1,), (1,)))
        total = total + mm(pair_now[step, :, ff_part:], held[1, cols, :], ((1,), (1,)))
        back[:, cols] = total.astype(bf16)
        return carry

    lax.fori_loop(0, model // 512, back_tile, 0)

    @pl.when(step == 1)
    def _():
        for turn in range(2):
            for n in range(2):
                kept(n, turn).wait()
                handed(n, turn).wait()


def feed_forward(normed, grad_out, weights):
    tok, model = normed.shape
    ff_part = weights.shape[1] // 3
    rows = tok // 2
    anyspec = pl.BlockSpec(memory_space=pl.ANY)
    dma = pltpu.SemaphoreType.DMA
    block = pl.BlockSpec((rows, model), lambda i: (i, 0))
    return pl.pallas_call(
        feed_forward_kernel,
        grid=(2,),
        in_specs=[block, block, anyspec],
        out_specs=[anyspec] * 4 + [block],
        out_shape=[
            jax.ShapeDtypeStruct((tok, cols), bf16)
            for cols in (ff_part, ff_part, 2 * ff_part, 2 * ff_part, model)
        ],
        scratch_shapes=[
            pltpu.VMEM((3, model, ff_part), bf16),
            pltpu.VMEM((2, rows, ff_part), bf16),
            pltpu.VMEM((2, rows, 2 * ff_part), bf16),
            dma((len(column_tiles(ff_part)), 3)), dma((2, 2)), dma((2, 2)), dma((2, 2)),
        ],
        compiler_params=pltpu.CompilerParams(
            collective_id=4, has_side_effects=True, vmem_limit_bytes=60 * 1024 * 1024
        ),
        name="feed_forward",
    )(normed, grad_out, weights)


def add_columns(target, sources, start, size, step):
    def one(turn, carry):
        cols = pl.ds(pl.multiple_of(start + turn * step, 128), step)
        total = target[:, cols].astype(f32)
        for source in sources:
            total = total + source[:, cols].astype(f32)
        target[:, cols] = total.astype(target.dtype)
        return carry

    lax.fori_loop(0, size // step, one, 0)


def shared_products_kernel(
    normed, normed_other, grad, grad_other, weights, pair, pair_other, hidden, hidden_other,
    beside_high, across_low, mine, beside_low, across_high, out,
    turned, slots, stage, diag, landed, waiting, down_now, out_now,
    load_sem, send_sem, recv_sem, store_sem, down_sem, out_sem,
):
    s, z, _, beside, across = places()
    step = pl.program_id(0)
    lefts = ((normed, normed_other), (grad, grad_other))
    chip_cols = normed.shape[1] // 4
    half = chip_cols // 2
    piece = half // 2
    width = pair.shape[1]
    diagonal = beside + across - s
    chips = [q // 2 for q in (diagonal, beside, across, s)]

    def load(side, q, who):
        cols = pl.ds(pl.multiple_of(chips[q] * chip_cols, 128), chip_cols)
        return pltpu.make_async_copy(lefts[side][who].at[:, cols], slots.at[q % 2, who], load_sem.at[q % 2, who])

    def fetch(side):
        for q in range(2):
            for who in range(2):
                load(side, q, who).start()

    def turn(side):
        for q in range(4):
            for who in range(2):
                load(side, q, who).wait()
                stage[...] = slots[q % 2, who].T
                turned[who, q * half : (q + 1) * half, :] = stage[
                    pl.ds(pl.multiple_of(s % 2 * half, 16), half), :
                ]
                if q < 2:
                    load(side, q + 2, who).start()

    def tile(own, other, start, size):
        cols = pl.ds(start, size)
        block = mm(turned[0], own[:, cols], ((1,), (0,)))
        block = (block + mm(turned[1], other[:, cols], ((1,), (0,)))).astype(bf16)
        parts = [block[n * piece : (n + 1) * piece] for n in range(8)]
        there = pl.ds(pl.multiple_of(step * width + start, 128), size)
        diag[0, :, there] = parts[0]
        diag[1, :, there] = parts[1]
        waiting[0, :, there] = parts[2]
        beside_high[:, cols] = parts[3]
        across_low[:, cols] = parts[4]
        waiting[1, :, there] = parts[5]
        mine[0:piece, cols] = parts[6]
        mine[piece:, cols] = parts[7]

    def multiply(own, other):
        def one(turn, carry):
            tile(own, other, pl.multiple_of(turn * 512, 512), 512)
            return carry

        lax.fori_loop(0, width // 512, one, 0)
        if width % 512:
            tile(own, other, width // 512 * 512, width % 512)

    def push(way, j):
        cols = pl.ds(j * width, width)
        return pltpu.make_async_remote_copy(
            src_ref=diag.at[way, :, cols],
            dst_ref=landed.at[way, :, cols],
            send_sem=send_sem.at[way, j],
            recv_sem=recv_sem.at[way, j],
            device_id=(across if way == 0 else beside, z),
            device_id_type=MESH,
        )

    def store(way, j):
        cols = pl.ds(j * width, width)
        return pltpu.make_async_copy(
            waiting.at[way, :, cols], (beside_low, across_high)[way].at[:, cols], store_sem.at[way, j]
        )

    out_rows = down_now.shape[1]
    out_tiles = weights.shape[0] // out_rows

    def down(t):
        source = weights.at[pl.ds(t * out_rows, out_rows), pl.ds(2 * width, width)]
        return pltpu.make_async_copy(source, down_now.at[t % 2], down_sem.at[t % 2])

    def out_store(t):
        return pltpu.make_async_copy(
            out_now.at[t % 2], out.at[:, pl.ds(t * out_rows, out_rows)], out_sem.at[t % 2]
        )

    def out_product():
        for t in range(out_tiles):
            down(t).wait()
            if t > 1:
                out_store(t - 2).wait()
            out_now[t % 2] = mm(hidden[...], down_now[t % 2], ((1,), (1,))).astype(bf16)
            out_store(t).start()
            if t + 2 < out_tiles:
                down(t + 2).start()

    @pl.when(step == 0)
    def _():
        fetch(0)
        greet([(beside, z), (across, z)])
        turn(0)

    @pl.when(step == 2)
    def _():
        down(0).start()
        down(1).start()
        turn(1)

    pl.when(step < 2)(functools.partial(multiply, pair, pair_other))
    pl.when(step == 1)(functools.partial(fetch, 1))
    pl.when(step == 2)(functools.partial(multiply, hidden, hidden_other))
    for j in range(3):

        @pl.when(step == j)
        def _(j=j):
            push(0, j).start()
            push(1, j).start()

    @pl.when(step == 2)
    def _():
        out_product()
        for j in range(3):
            for way in range(2):
                push(way, j).wait_recv()
                add_columns(waiting.at[way], [landed.at[way]], j * width, width, 384)
                store(way, j).start()
        for j in range(3):
            for way in range(2):
                push(way, j).wait_send()
                store(way, j).wait()
        for t in range(out_tiles - 2, out_tiles):
            out_store(t).wait()


def shared_products(lefts, weights, pair, hidden):
    tok, model = lefts[0].shape
    width = hidden[0].shape[1]
    half = model // 8
    anyspec = pl.BlockSpec(memory_space=pl.ANY)
    dma = pltpu.SemaphoreType.DMA

    def block(rows):
        return pl.BlockSpec((rows, width), lambda j: (0, j))

    pair_spec = pl.BlockSpec((tok, width), lambda j: (0, jnp.minimum(j, 1)))
    hidden_spec = pl.BlockSpec((tok, width), lambda j: (0, 0))
    rows_out = (half // 2, half // 2, half, half // 2, half // 2)
    return pl.pallas_call(
        shared_products_kernel,
        grid=(3,),
        in_specs=[anyspec] * 5 + [pair_spec] * 2 + [hidden_spec] * 2,
        out_specs=[block(rows) for rows in rows_out[:3]] + [anyspec] * 3,
        out_shape=[jax.ShapeDtypeStruct((rows, 3 * width), bf16) for rows in rows_out]
        + [jax.ShapeDtypeStruct((tok, model), bf16)],
        scratch_shapes=[
            pltpu.VMEM((2, 4 * half, tok), bf16),
            pltpu.VMEM((2, 2, tok, 2 * half), bf16),
            pltpu.VMEM((2 * half, tok), bf16),
            pltpu.VMEM((2, half // 2, 3 * width), bf16),
            pltpu.VMEM((2, half // 2, 3 * width), bf16),
            pltpu.VMEM((2, half // 2, 3 * width), bf16),
            pltpu.VMEM((2, 512, width), bf16),
            pltpu.VMEM((2, tok, 512), bf16),
            dma((2, 2)), dma((2, 3)), dma((2, 3)), dma((2, 3)), dma((2,)), dma((2,)),
        ],
        compiler_params=pltpu.CompilerParams(
            collective_id=5, has_side_effects=True, vmem_limit_bytes=60 * 1024 * 1024
        ),
        name="feed_forward_products",
    )(*lefts, weights, *pair, *hidden)


def scatter_kernel(
    normed, normed_other, grad_mix, mix_other, mixed, mixed_other, grad_gelu, gelu_other, grad_branch, rest,
    mlp_low, mlp_high, mixer_w, tokens, gain, mixer_sum, mlp_back, input_grad,
    held, cross, near, lined, left_now, both_now, mixed_now, turned, stage, rest_other, back_now, wide_now, gain_now,
    load_sem, core_send, core_recv, wide_sem,
    flow_send, flow_recv, line_send, line_recv, swap_send, swap_recv, own_sem,
):
    s, z, core, beside, across = places()
    chip_diag, chip_beside, chip_across, chip = 0, 1, 2, 3
    chips = [q // 2 for q in (beside + across - s, beside, across, s)]
    rows = held.shape[1] // 4
    cols = held.shape[2]
    cut = cols // 256 * 128
    ff_part = mlp_low.shape[1] // 3
    tok, model = tokens.shape
    half = 4 * rows
    lru = grad_branch.shape[1]
    lru2 = 2 * lru
    rest_start = lru2 + mixed.shape[1]
    order = (3 * (1 - z // 2), (2 + 3 * z) % 5, 1 + z % 2, z)

    def remote(src, dst, send, recv, target):
        return pltpu.make_async_remote_copy(
            src_ref=src, dst_ref=dst, send_sem=send, recv_sem=recv, device_id=target, device_id_type=MESH
        )

    def span(k):
        return pl.ds(pl.multiple_of(k * rows, 16), rows)

    mine, other = pl.ds(0, tok), pl.ds(tok, tok)
    loads = [
        pltpu.make_async_copy(source, target, load_sem.at[n])
        for n, (source, target) in enumerate(
            (
                (grad_mix, left_now.at[1, mine, :]),
                (mix_other, left_now.at[1, other, :]),
                (mixed, mixed_now.at[mine, :]),
                (mixed_other, mixed_now.at[other, :]),
                (normed, left_now.at[0, mine, :]),
                (normed_other, left_now.at[0, other, :]),
                (grad_gelu, both_now.at[mine, pl.ds(lru, lru)]),
                (gelu_other, both_now.at[other, pl.ds(lru, lru)]),
                (grad_branch, both_now.at[mine, pl.ds(0, lru)]),
            )
        )
    ]

    def push(n):
        if n == 0:
            source, target = grad_branch, both_now.at[other, pl.ds(0, lru)]
        else:
            source = rest.at[pl.ds(pl.multiple_of(chips[n - 1] * 2 * half + (1 - s % 2) * half, 16), half), :]
            target = rest_other.at[n - 1]
        return pltpu.make_async_remote_copy(
            src_ref=source,
            dst_ref=target,
            send_sem=core_send.at[n],
            recv_sem=core_recv.at[n],
            device_id=(core, z),
            device_id_type=MESH,
        )

    def rest_load(q):
        source = rest.at[pl.ds(pl.multiple_of(chips[q] * 2 * half + s % 2 * half, 16), half), :]
        return pltpu.make_async_copy(
            source, held.at[q, :, pl.ds(rest_start, cols - rest_start)], load_sem.at[9 + q]
        )

    def turn(side):
        for q in range(4):
            source = left_now[side, :, pl.ds(pl.multiple_of(chips[q] * 2 * half, 128), 2 * half)]
            stage[...] = source.T
            turned[side, q * half : (q + 1) * half, :] = stage[
                pl.ds(pl.multiple_of(s % 2 * half, 16), half), :
            ]

    def multiply(q, side, first=0, last=None):
        right, start = ((both_now, 0), (mixed_now, lru2))[side]

        def one(turn, carry):
            here = pl.multiple_of(turn * 512, 512)
            block = mm(turned[side, q * half : (q + 1) * half, :], right[:, pl.ds(here, 512)], ((1,), (0,)))
            held[q, :, pl.ds(pl.multiple_of(start + here, 512), 512)] = block.astype(bf16)
            return carry

        lax.fori_loop(first // 512, (right.shape[1] if last is None else last) // 512, one, 0)

    def add_rest(q):
        rest_load(q).wait()
        push(1 + q).wait_recv()
        held[q, :, rest_start:] = add_low(held[q, :, rest_start:], rest_other[q])

    left, right = pl.ds(0, cut), pl.ds(cut, cols - cut)

    def block(q, i, side):
        return held.at[q, span(order[i]), side]

    def flow(i, index):
        send, recv = flow_send.at[i, index], flow_recv.at[i, index]
        to_beside, to_across = (beside, z), (across, z)
        if index == 0:
            return remote(block(chip_diag, i, left), cross.at[i, :, left], send, recv, to_across)
        if index == 1:
            return remote(block(chip_diag, i, right), cross.at[i, :, right], send, recv, to_beside)
        if index == 2:
            return remote(block(chip_beside, i, right), near.at[0, i, :, right], send, recv, to_beside)
        if index == 3:
            return remote(block(chip_beside, i, left), near.at[0, i, :, left], send, recv, to_beside)
        if index == 4:
            return remote(block(chip_across, i, left), near.at[1, i, :, left], send, recv, to_across)
        return remote(block(chip_across, i, right), near.at[1, i, :, right], send, recv, to_across)

    def cross_step(i):
        flow(i, 0).wait_recv()
        add_columns(held.at[chip_beside, span(order[i]), :], [cross.at[i]], 0, cut, 512)
        flow(i, 3).start()
        flow(i, 1).wait_recv()
        add_columns(held.at[chip_across, span(order[i]), :], [cross.at[i]], cut, cols - cut, 384)
        flow(i, 5).start()

    def near_step(i):
        for index in (2, 4, 3, 5):
            flow(i, index).wait_recv()
        add_columns(held.at[chip, span(order[i]), :], [near.at[0, i], near.at[1, i]], 0, cols, 640)

    def line(k, slot, target):
        return remote(
            held.at[chip, span(k), :], lined.at[slot], line_send.at[k], line_recv.at[slot], (s, target)
        )

    def absorb(k, slot, source):
        line(k, slot, source).wait_recv()
        add_columns(held.at[chip, span(k), :], [lined.at[slot]], 0, cols, 640)

    def chain(i):
        k = order[i]
        if i == 3:
            pl.when(z > 0)(lambda: absorb(k, k, z - 1))
            pl.when(z < 3)(lambda: absorb(k, 4, z + 1))
            return

        @pl.when(k > z)
        def _():
            pl.when(z > 0)(lambda: absorb(k, k, z - 1))
            line(k, k, z + 1).start()

        @pl.when(k < z)
        def _():
            pl.when(z < 3)(lambda: absorb(k, k, z + 1))
            pl.when(k == z - 1)(lambda: line(k, 4, z - 1).start())
            pl.when(k < z - 1)(lambda: line(k, k, z - 1).start())

    def chain_drain():
        for i in range(3):
            k = order[i]
            line(k, k, (z + 1) % 4).wait_send()

    def swap(k, high=False):
        to = (z + k) % 4
        here = pl.ds(pl.multiple_of(z * ff_part, 128), ff_part)
        source = (mlp_high if high else mlp_low).at[span(to % 2), :]
        return [
            remote(
                source.at[:, pl.ds(m * ff_part, ff_part)],
                mlp_back.at[m, :, here],
                swap_send.at[k - 1, m],
                swap_recv.at[k - 1, m],
                (s, to),
            )
            for m in range(3)
        ]

    def swap_start(k):
        to = (z + k) % 4

        @pl.when(to < 2)
        def _():
            for copy in swap(k):
                copy.start()

        @pl.when(to >= 2)
        def _():
            for copy in swap(k, True):
                copy.start()

    def own(high=False):
        here = pl.ds(pl.multiple_of(z * ff_part, 128), ff_part)
        source = (mlp_high if high else mlp_low).at[span(z % 2), :]
        return [
            pltpu.make_async_copy(source.at[:, pl.ds(m * ff_part, ff_part)], mlp_back.at[m, :, here], own_sem.at[m])
            for m in range(3)
        ]

    wide_rows = wide_now.shape[0]
    wide_tiles = mixer_w.shape[0] // wide_rows
    wide_start = mixer_w.shape[1] - lru2 - model
    wide_slots = (both_now.at[pl.ds(tok, wide_rows), :], wide_now)

    def wide(j):
        source = mixer_w.at[pl.ds(j * wide_rows, wide_rows), pl.ds(wide_start, lru2)]
        return pltpu.make_async_copy(source, wide_slots[j % 2], wide_sem.at[j % 2])

    plain_loads = [
        pltpu.make_async_copy(tokens, left_now.at[0, pl.ds(0, tok), :], wide_sem.at[2]),
        pltpu.make_async_copy(gain, gain_now, wide_sem.at[3]),
    ]

    def back(first, last):
        for j in range(first, last):
            wide(j).wait()
            back_now[:, pl.ds(j * wide_rows, wide_rows)] = mm(
                both_now[0:tok, :], wide_slots[j % 2][...], ((1,), (1,))
            )
            if j + 2 < wide_tiles:
                wide(j + 2).start()

    def finish_rows(turn, carry):
        at = pl.ds(pl.multiple_of(turn * 16, 16), 16)
        result = left_now[1, at, :].astype(f32) + norm_back(
            left_now[0, at, :].astype(f32), gain_now[GAIN_ONE : GAIN_ONE + 1, :], back_now[at, :]
        )
        left_now[0, at, :] = result.astype(bf16)
        return carry

    for copy in loads:
        copy.start()
    for q in range(4):
        rest_load(q).start()
    greet([(core, z), (beside, z), (across, z)] + [(s, (z + k) % 4) for k in range(1, 4)])
    for n in range(5):
        push(n).start()
    for k in (1, 3, 2):
        swap_start(k)

    @pl.when(z < 2)
    def _():
        for copy in own():
            copy.start()

    @pl.when(z >= 2)
    def _():
        for copy in own(True):
            copy.start()

    for copy in loads[:4]:
        copy.wait()
    turn(1)
    multiply(chip_diag, 1)
    for copy in loads[4:]:
        copy.wait()
    turn(0)
    multiply(chip_diag, 0, lru)
    push(0).wait_recv()
    multiply(chip_diag, 0, 0, lru)
    add_rest(chip_diag)
    for i in range(2):
        flow(i, 0).start()
        flow(i, 1).start()
    for q in (chip_beside, chip_across, chip):
        multiply(q, 0)
        multiply(q, 1)
        add_rest(q)
        if q == chip_beside:
            flow(0, 2).start()
        if q == chip_across:
            flow(0, 4).start()
    for copy in plain_loads:
        copy.start()
    wide(0).start()
    wide(1).start()
    for i in range(4):
        cross_step(i)
        if i + 1 < 4:
            flow(i + 1, 2).start()
            flow(i + 1, 4).start()
        if i + 2 < 4:
            flow(i + 2, 0).start()
            flow(i + 2, 1).start()
        if i > 0:
            near_step(i - 1)
            chain(i - 1)
            back(wide_tiles * (i - 1) // 3, wide_tiles * i // 3)
    for copy in plain_loads:
        copy.wait()
    lax.fori_loop(0, tok // 16, finish_rows, 0)
    finished = pltpu.make_async_copy(left_now.at[0, pl.ds(0, tok), :], input_grad, wide_sem.at[2])
    finished.start()
    near_step(3)
    chain(3)
    done = pltpu.make_async_copy(held.at[chip, span(z), :], mixer_sum, own_sem.at[3])
    done.start()
    for i in range(4):
        for index in range(6):
            flow(i, index).wait_send()
    chain_drain()
    for k in range(1, 4):
        for copy in swap(k):
            copy.wait()
    for copy in own():
        copy.wait()
    for n in range(5):
        push(n).wait_send()
    finished.wait()
    done.wait()


def scatter(rows_pairs, grad_branch, rest, mlp_low, mlp_high, mixer_w, tokens, gain):
    tok, model = tokens.shape
    rows = model // 32
    lru = grad_branch.shape[1]
    cols = 3 * lru + rest.shape[1]
    ff_part = mlp_low.shape[1] // 3
    anyspec = pl.BlockSpec(memory_space=pl.ANY)
    dma = pltpu.SemaphoreType.DMA
    return pl.pallas_call(
        scatter_kernel,
        in_specs=[anyspec] * 15,
        out_specs=[anyspec] * 3,
        out_shape=[
            jax.ShapeDtypeStruct((rows, cols), bf16),
            jax.ShapeDtypeStruct((3, rows, 4 * ff_part), bf16),
            jax.ShapeDtypeStruct((tok, model), bf16),
        ],
        scratch_shapes=[
            pltpu.VMEM((4, 4 * rows, cols), bf16),
            pltpu.VMEM((4, rows, cols), bf16),
            pltpu.VMEM((2, 4, rows, cols), bf16),
            pltpu.VMEM((5, rows, cols), bf16),
            pltpu.VMEM((2, 2 * tok, model), bf16),
            pltpu.VMEM((2 * tok, 2 * lru), bf16),
            pltpu.VMEM((2 * tok, lru), bf16),
            pltpu.VMEM((2, 16 * rows, 2 * tok), bf16),
            pltpu.VMEM((8 * rows, 2 * tok), bf16),
            pltpu.VMEM((4, 4 * rows, rest.shape[1]), bf16),
            pltpu.VMEM((tok, model), f32),
            pltpu.VMEM((128, 2 * lru), bf16),
            pltpu.VMEM(gain.shape, f32),
            dma((13,)), dma((5,)), dma((5,)), dma((4,)),
            dma((4, 6)), dma((4, 6)), dma((4,)), dma((5,)), dma((3, 3)), dma((3, 3)), dma((4,)),
        ],
        compiler_params=pltpu.CompilerParams(
            collective_id=2, has_side_effects=True, vmem_limit_bytes=62 * 1024 * 1024
        ),
        name="scatter_gradients",
    )(*rows_pairs, grad_branch, rest, mlp_low, mlp_high, mixer_w, tokens, gain)


def gather_plain(mixer, gate, up, down):
    groups = lax.axis_size("fsdp")
    part_rows, ff = gate.shape
    own = jnp.stack([w.reshape(part_rows, groups, ff // groups) for w in (gate, up, down)], axis=2)
    mine = lax.all_to_all(jnp.transpose(own, (1, 0, 2, 3)), "fsdp", 0, 0, tiled=True)
    return lax.all_gather(mixer, both, axis=0, tiled=True), mine.reshape(groups * part_rows, -1)


def from_line(shard):
    count = lax.axis_size("fsdp")
    return [shard] + [
        lax.ppermute(shard, "fsdp", [(i, (i + k) % count) for i in range(count)]) for k in range(1, count)
    ]


def swap_cores(shard):
    count = lax.axis_size("seq")
    return lax.ppermute(shard, "seq", [(i, i + 1 - 2 * (i % 2)) for i in range(count)])


def swap_beside(shard):
    return lax.ppermute(shard, "seq", [(i, i ^ 2) for i in range(8)])


def swap_across(shard):
    return lax.ppermute(shard, "seq", [(i, i ^ 4) for i in range(8)])


def add_low(left, right):
    return (left.astype(f32) + right.astype(f32)).astype(bf16)


def scatter_plain(normed, grad_both, grad_mix, mixed, rest, mlp_sum):
    groups = lax.axis_size("fsdp")
    term_wide = mm(normed, grad_both, ((0,), (0,))).astype(bf16)
    term_out = mm(grad_mix, mixed, ((0,), (0,))).astype(bf16)
    mixer_sum = lax.psum_scatter(
        jnp.concatenate([term_wide, term_out, rest], axis=1), "seq", scatter_dimension=0, tiled=True
    )
    mixer_sum = lax.psum_scatter(mixer_sum, "fsdp", scatter_dimension=0, tiled=True)
    ff_part = mlp_sum.shape[1] // 3
    part_rows = mlp_sum.shape[0] // groups
    mlp_sum = mlp_sum.reshape(groups, part_rows, 3, ff_part)
    mlp_back = lax.all_to_all(mlp_sum, "fsdp", 0, 0, tiled=True)
    mlp_back = jnp.transpose(mlp_back, (2, 1, 0, 3)).reshape(3, part_rows, groups * ff_part)
    return mixer_sum, mlp_back


def call_heads(kernel, width, heads, ins, outs, scratch, name):
    def spec(rows, place):
        if place is None:
            return pl.BlockSpec((rows, width), lambda h: (0, h))
        return pl.BlockSpec((width, width), lambda h: (h, place))

    in_specs = [spec(a.shape[0], place) for a, place in ins]
    out_specs = [spec(rows, 0 if rowwise else None) for rows, _, rowwise in outs]
    out_shape = [
        jax.ShapeDtypeStruct((heads * width, width) if rowwise else (rows, heads * width), kind)
        for rows, kind, rowwise in outs
    ]
    return pl.pallas_call(
        kernel,
        grid=(heads,),
        in_specs=in_specs,
        out_specs=out_specs,
        out_shape=out_shape,
        scratch_shapes=[pltpu.VMEM((rows, width), f32) for rows in scratch],
        compiler_params=pltpu.CompilerParams(vmem_limit_bytes=40 * 1024 * 1024),
        cost_estimate=pl.CostEstimate(flops=1, bytes_accessed=1, transcendentals=0),
        name=name,
    )(*[a for a, _ in ins])


def on_device(
    block_input,
    cotangent,
    mixer_gain,
    branch_proj,
    gelu_proj,
    conv_taps,
    conv_bias,
    rate_blocks,
    input_blocks,
    rate_bias,
    input_bias,
    decay_param,
    out_proj,
    mlp_gain,
    gate_proj,
    up_proj,
    down_proj,
):
    groups = lax.axis_size("fsdp")
    part_rows, lru = branch_proj.shape
    width = rate_blocks.shape[1]
    heads = lru // width
    margin = conv_taps.shape[0] - 1
    tokens = block_input[0].astype(f32)
    tok_count, model = tokens.shape
    ff = gate_proj.shape[1]
    ff_part = ff // groups
    grad_out = cotangent[0]

    smalls = jnp.stack(
        [conv_taps[k] for k in range(margin + 1)]
        + [conv_bias, rate_bias, input_bias, decay_param, mixer_gain, mlp_gain],
        axis=1,
    )
    small_count = smalls.shape[1]
    smalls = jnp.pad(smalls, ((0, 0), (0, 128 - small_count)))
    first_own = jnp.concatenate([rate_blocks, input_blocks, smalls], axis=1)
    mixer_own = (first_own, branch_proj, gelu_proj, out_proj)
    custom = lax.axis_size("seq") == 8 and groups == 4
    if custom:
        mixer_w, mlp_mine = gather(*mixer_own, gate_proj, up_proj, down_proj)
    else:
        mixer_w, mlp_mine = gather_plain(jnp.concatenate(mixer_own, axis=1), gate_proj, up_proj, down_proj)
    mlp_w = lax.all_gather(mlp_mine, "seq", axis=0, tiled=True)
    grad_out_late = lax.optimization_barrier((grad_out, mlp_mine))[0]
    if custom:
        grad_pieces = from_line(grad_out_late)
    wide = mixer_w[:, 128 + 2 * width : 128 + 2 * width + 2 * lru]
    proj_out = mixer_w[:, 128 + 2 * width + 2 * lru :]

    small = small_table(mixer_w, 2 * width // 128)
    gain_one, gain_two = small[GAIN_ONE], small[GAIN_TWO]

    normed, branch, gelu_pre = mixer_in(block_input[0], small, mixer_w, lru, 2 * width + 128)
    prior = from_behind(branch[tok_count - margin :], "seq", 1).astype(f32)
    prior = jnp.concatenate([jnp.zeros((8 - margin, lru), f32), prior], axis=0)
    conv, rate_pre, input_pre, cum, local = call_heads(
        mixer_forward,
        width,
        heads,
        [(branch, None), (prior, None), (small, None), (mixer_w, 0), (mixer_w, 1)],
        [(tok_count, bf16, False)] + [(tok_count, f32, False)] * 4,
        [tok_count + 8],
        "mixer_forward",
    )
    carried = prefix((cum[-1], local[-1]), "seq", False)
    states = local + cum * carried[None]
    mixed = (states * jax.nn.gelu(gelu_pre, approximate=True)).astype(bf16)
    middle = tokens + mm(mixed, proj_out, ((1,), (1,)))
    normed_two = norm_rows(middle, gain_two).astype(bf16)

    if custom:
        normed_all, normed_other, grad_out_all, grad_out_other, first_other, mixed_other = gather_rows(
            normed_two, grad_pieces, normed, mixed
        )
    else:
        normed_all = lax.all_gather(normed_two, "fsdp", axis=0, tiled=True)
        grad_out_all = lax.all_gather(grad_out_late, "fsdp", axis=0, tiled=True)
    w_gate, w_up, w_down = mlp_w[:, :ff_part], mlp_w[:, ff_part : 2 * ff_part], mlp_w[:, 2 * ff_part :]
    if custom:
        hidden, hidden_other, grad_pair, pair_other, grad_normed_part = feed_forward(
            normed_all, grad_out_all, mlp_w
        )
    else:
        gate = mm(normed_all, w_gate, ((1,), (0,)))
        up_val = mm(normed_all, w_up, ((1,), (0,)))
        gelu_gate, gelu_slope = gelu_parts(gate)
        hidden = (gelu_gate * up_val).astype(bf16)
        grad_hidden = mm(grad_out_all, w_down, ((1,), (0,)))
        grad_gate = (grad_hidden * up_val * gelu_slope).astype(bf16)
        grad_up = (grad_hidden * gelu_gate).astype(bf16)
        grad_normed_part = (
            mm(grad_gate, w_gate, ((1,), (1,))) + mm(grad_up, w_up, ((1,), (1,)))
        ).astype(bf16)
    grad_normed_two = lax.psum_scatter(grad_normed_part, "fsdp", scatter_dimension=0, tiled=True)
    if custom:
        half = model // 16
        beside_high, across_low, mine, beside_low, across_high, out_part = shared_products(
            (normed_all, normed_other, grad_out_all, grad_out_other),
            mlp_w,
            (grad_pair, pair_other),
            (hidden, hidden_other),
        )
        from_beside_high, from_across_low = swap_beside(beside_high), swap_across(across_low)
    else:
        grad_pair = jnp.concatenate([grad_gate, grad_up], axis=1)
        term_pair = mm(normed_all, grad_pair, ((0,), (0,))).astype(bf16)
        term_down = mm(grad_out_all, hidden, ((0,), (0,))).astype(bf16)
        pair_sum = lax.psum_scatter(term_pair, "seq", scatter_dimension=0, tiled=True)
        down_sum = lax.psum_scatter(term_down, "seq", scatter_dimension=0, tiled=True)
        mlp_sum = jnp.concatenate([pair_sum, down_sum], axis=1)
        out_part = mm(hidden, w_down, ((1,), (1,))).astype(bf16)
    out_sum = lax.psum_scatter(out_part, "fsdp", scatter_dimension=0, tiled=True)
    grad_normed_two = grad_normed_two.astype(f32)

    grad_middle = grad_out.astype(f32) + norm_back(middle, gain_two, grad_normed_two)
    grad_mix = grad_middle.astype(bf16)
    if custom:
        mix_other = swap_cores(grad_mix)
    grad_mixed = mm(grad_mix, proj_out, ((1,), (0,)))
    carried_rows = jnp.broadcast_to(carried[None], (8, lru))
    grad_gelu_pre, rev_cum, rev_grad, pair_grad = call_heads(
        mixer_backward_scan,
        width,
        heads,
        [(a, None) for a in (grad_mixed, gelu_pre, rate_pre, cum, local, carried_rows, small)],
        [(tok_count, bf16, False), (tok_count, f32, False), (tok_count, f32, False), (8, f32, False)],
        [tok_count + 8],
        "mixer_backward_scan",
    )
    if custom:
        from_beside_high, from_across_low, pair_grad = lax.optimization_barrier(
            (from_beside_high, from_across_low, pair_grad)
        )
    if custom:
        gelu_other = swap_cores(grad_gelu_pre)
    incoming = prefix((cum[-1], pair_grad[0]), "seq", True)
    if custom:
        beside_low, across_high, incoming = lax.optimization_barrier((beside_low, across_high, incoming))
        from_beside_low, from_across_high = swap_beside(beside_low), swap_across(across_high)
    incoming_rows = jnp.broadcast_to(incoming[None], (8, lru))
    own, head, rate_w_grad, input_w_grad, sums = call_heads(
        mixer_backward,
        width,
        heads,
        [
            (a, None)
            for a in (rev_cum, rev_grad, incoming_rows, cum, local, carried_rows, rate_pre, input_pre, conv, branch, prior, small)
        ]
        + [(mixer_w, 0), (mixer_w, 1)],
        [(tok_count, f32, False), (8, f32, False), (0, bf16, True), (0, bf16, True), (8, f32, False)],
        [tok_count + 8, tok_count + 16],
        "mixer_backward",
    )
    received = from_behind(head[8 - margin :], "seq", -1)
    grad_branch = jnp.concatenate(
        [own[: tok_count - margin], own[tok_count - margin :] + received], axis=0
    ).astype(bf16)
    grad_both = jnp.concatenate([grad_branch, grad_gelu_pre], axis=1)
    vectors = jnp.pad(sums.T, ((0, 0), (0, 128 - sums.shape[0]))).astype(bf16)
    rest = jnp.concatenate([rate_w_grad, input_w_grad, vectors], axis=1)
    if custom:
        low = add_low(mine[:half], from_across_low)
        high = add_low(mine[half:], from_beside_high)
        low, high, grad_branch = lax.optimization_barrier((low, high, grad_branch))
        middle = lax.optimization_barrier((middle, low))[0]
        low, high = add_low(low, from_beside_low), add_low(high, from_across_high)
        mixer_sum, mlp_back, input_grad = scatter(
            (normed, first_other, grad_mix, mix_other, mixed, mixed_other, grad_gelu_pre, gelu_other),
            grad_branch, rest, low, high, mixer_w, block_input[0], small,
        )
    else:
        mixer_sum, mlp_back = scatter_plain(normed, grad_both, grad_mix, mixed, rest, mlp_sum)
        grad_normed = mm(grad_both, wide, ((1,), (1,)))
        input_grad = (grad_middle + norm_back(tokens, gain_one, grad_normed)).astype(bf16)
    input_grad = input_grad[None]
    block_output = (middle + out_sum.astype(f32)).astype(bf16)[None]
    edge = 3 * lru + 2 * width
    vec = mixer_sum[:, edge:].astype(f32).T
    if custom:
        *weight_grads, totals = finish(mixer_sum, mlp_back, branch_proj, gelu_proj, gate_proj, up_proj, width)
        first_total, second_total = totals[:, 0], totals[:, 128]
    else:
        weight_grads = list(
            jnp.split(mixer_sum[:, :edge].astype(f32), [lru, 2 * lru, 3 * lru, 3 * lru + width], axis=1)
        ) + [mlp_back[m].astype(f32) for m in range(3)]
        first_total = gain_back((branch_proj, weight_grads[0]), (gelu_proj, weight_grads[1]))
        second_total = gain_back((gate_proj, weight_grads[5]), (up_proj, weight_grads[6]))
    dbranch, dgelu, dout, drate, dinput, dgate, dup, ddown = weight_grads
    return (
        block_output,
        input_grad,
        first_total / mixer_gain.astype(f32),
        dbranch,
        dgelu,
        vec[: margin + 1],
        vec[7],
        drate,
        dinput,
        vec[4],
        vec[5],
        vec[6],
        dout,
        second_total / mlp_gain.astype(f32),
        dgate,
        dup,
        ddown,
    )


def solution(mesh):
    tokens = P("fsdp", "seq", None)
    vector = P(both)
    matrix = P(both, None)
    taps = P(None, both)
    return jax.shard_map(
        on_device,
        mesh=mesh,
        in_specs=(
            tokens, tokens, vector, matrix, matrix, taps, vector, matrix, matrix,
            vector, vector, vector, matrix, vector, matrix, matrix, matrix,
        ),
        out_specs=(
            tokens, tokens, vector, matrix, matrix, taps, vector, matrix, matrix,
            vector, vector, vector, matrix, vector, matrix, matrix, matrix,
        ),
        check_vma=False,
    )
```

```python
import functools

import jax
import jax.numpy as jnp
from jax import lax
from jax.experimental import pallas as pl
from jax.experimental.pallas import tpu as pltpu
from jax.sharding import PartitionSpec as P

epsilon = 1e-06
f32 = jnp.float32
bf16 = jnp.bfloat16
both = ("seq", "fsdp")
MESH = pl.DeviceIdType.MESH
TAP, CONV_BIAS, RATE_BIAS, INPUT_BIAS, SOFT, SOFT_SLOPE, GAIN_ONE, GAIN_TWO = 0, 4, 5, 6, 7, 8, 9, 10
GELU_C = 0.7978845608028654
GELU_A = 0.044715


def from_behind(shard, axis, by):
    devices = lax.axis_size(axis)
    pairs = [(i, i + by) for i in range(devices) if 0 <= i + by < devices]
    return lax.ppermute(shard, axis, pairs)


def prefix(part, axis, reverse):
    count = lax.axis_size(axis)
    place = lax.axis_index(axis)
    gathered = lax.all_gather(jnp.stack(part), axis)
    state = jnp.zeros_like(part[1])
    for hop in range(count):
        source = count - 1 - hop if reverse else hop
        ahead = source > place if reverse else source < place
        state = jnp.where(ahead, gathered[source, 1] + gathered[source, 0] * state, state)
    return state


def norm_rows(values, scales):
    return values * lax.rsqrt(jnp.mean(values * values, axis=-1, keepdims=True) + epsilon) * scales


def norm_back(values, scales, grads):
    inverse = lax.rsqrt(jnp.mean(values * values, axis=-1, keepdims=True) + epsilon)
    scaled = grads * scales
    shared = jnp.mean(values * scaled, axis=-1, keepdims=True)
    return inverse * scaled - values * (inverse * inverse * inverse * shared)


def gain_back(*pairs):
    return sum(jnp.sum(weight.astype(f32) * grad, axis=1) for weight, grad in pairs)


def gelu_parts(x):
    inner = jnp.tanh(GELU_C * (x + GELU_A * x * x * x))
    return 0.5 * x * (1.0 + inner), 0.5 * (1.0 + inner) + 0.5 * x * (1.0 - inner * inner) * (
        GELU_C * (1.0 + 3.0 * GELU_A * x * x)
    )


def mm(left, right, dims):
    return lax.dot_general(left, right, (dims, ((), ())), preferred_element_type=f32)


def sigmoid(x):
    return 1.0 / (1.0 + jnp.exp(-x))


def scan_rows(decay, value, reverse):
    rows = decay.shape[0]
    place = lax.broadcasted_iota(jnp.int32, decay.shape, 0)
    step = 1
    while step < rows:
        shift = rows - step if reverse else step
        inside = place < rows - step if reverse else place >= step
        before_value = jnp.where(inside, pltpu.roll(value, shift, 0), 0.0)
        before_decay = jnp.where(inside, pltpu.roll(decay, shift, 0), 1.0)
        value = value + decay * before_value
        decay = decay * before_decay
        step *= 2
    return decay, value


def gates(rate_pre, input_pre, soft):
    rate = sigmoid(rate_pre)
    log_decay = -8.0 * rate * soft
    decay = jnp.exp(log_decay)
    square = decay * decay
    root = jnp.sqrt(-jnp.tanh(log_decay) * (1.0 + square))
    return rate, decay, square, root, sigmoid(input_pre)


def table_kernel(columns, table):
    rows = columns[...].T[0:16, :].astype(f32)
    decay_param = rows[7:8, :]
    fast = jnp.exp(-decay_param)
    table[0:7, :] = rows[0:7, :]
    table[7:8, :] = jnp.log1p(fast)
    table[8:9, :] = -fast / (1.0 + fast)
    table[9:11, :] = rows[8:10, :]
    table[11:16, :] = jnp.zeros((5, rows.shape[1]), f32)


def small_table(mixer_w, block):
    model = mixer_w.shape[0]
    return pl.pallas_call(
        table_kernel,
        grid=(1,),
        in_specs=[pl.BlockSpec((model, 128), lambda i: (0, block))],
        out_specs=pl.BlockSpec((16, model), lambda i: (0, 0)),
        out_shape=jax.ShapeDtypeStruct((16, model), f32),
        name="small_table",
    )(mixer_w)


def mixer_in_kernel(tokens, table, weights, normed, branch, gelu_pre):
    step = pl.program_id(0)

    @pl.when(step == 0)
    def _():
        normed[...] = norm_rows(tokens[...].astype(f32), table[GAIN_ONE : GAIN_ONE + 1, :]).astype(bf16)

    product = mm(normed[...], weights[...], ((1,), (0,)))
    half = pl.num_programs(0) // 2

    @pl.when(step < half)
    def _():
        branch[...] = product.astype(bf16)

    @pl.when(step >= half)
    def _():
        gelu_pre[...] = product


def mixer_in(tokens, table, mixer_w, lru, start):
    tok, model = tokens.shape
    tile = start
    tiles = lru // tile
    return pl.pallas_call(
        mixer_in_kernel,
        grid=(2 * tiles,),
        in_specs=[
            pl.BlockSpec((tok, model), lambda j: (0, 0)),
            pl.BlockSpec(table.shape, lambda j: (0, 0)),
            pl.BlockSpec((model, tile), lambda j: (0, 1 + j)),
        ],
        out_specs=[
            pl.BlockSpec((tok, model), lambda j: (0, 0)),
            pl.BlockSpec((tok, tile), lambda j: (0, jnp.minimum(j, tiles - 1))),
            pl.BlockSpec((tok, tile), lambda j: (0, jnp.maximum(j - tiles, 0))),
        ],
        out_shape=[
            jax.ShapeDtypeStruct((tok, model), bf16),
            jax.ShapeDtypeStruct((tok, lru), bf16),
            jax.ShapeDtypeStruct((tok, lru), f32),
        ],
        compiler_params=pltpu.CompilerParams(vmem_limit_bytes=40 * 1024 * 1024),
        cost_estimate=pl.CostEstimate(flops=1, bytes_accessed=1, transcendentals=0),
        name="mixer_in",
    )(tokens, table, mixer_w)


def mixer_forward(branch, prior, small, rate_w, input_w, conv, rate_pre, input_pre, cum, local, ext):
    rows = branch.shape[0]
    ext[0:8, :] = prior[...]
    ext[8:, :] = branch[...].astype(f32)
    total = small[CONV_BIAS : CONV_BIAS + 1, :] + small[TAP : TAP + 1, :] * ext[8:, :]
    for offset in range(1, 4):
        total = total + small[TAP + offset : TAP + offset + 1, :] * ext[pl.ds(8 - offset, rows), :]
    low = total.astype(bf16)
    conv[...] = low
    rate = mm(low, rate_w[...], ((1,), (0,))) + small[RATE_BIAS : RATE_BIAS + 1, :]
    inp = mm(low, input_w[...], ((1,), (0,))) + small[INPUT_BIAS : INPUT_BIAS + 1, :]
    rate_pre[...] = rate
    input_pre[...] = inp
    _, decay, _, root, opened = gates(rate, inp, small[SOFT : SOFT + 1, :])
    product, states = scan_rows(decay, root * opened * low.astype(f32), False)
    cum[...] = product
    local[...] = states


def mixer_backward_scan(grad_mixed, gelu_pre, rate_pre, cum, local, carried, small, grad_pre, rev_cum, rev_grad, pair, ext):
    rows = grad_mixed.shape[0]
    states = local[...] + cum[...] * carried[0:1, :]
    value, slope = gelu_parts(gelu_pre[...])
    grad = grad_mixed[...]
    grad_pre[...] = (grad * states * slope).astype(bf16)
    decay = jnp.exp(-8.0 * sigmoid(rate_pre[...]) * small[SOFT : SOFT + 1, :])
    ext[0:rows, :] = decay
    ext[rows:, :] = jnp.ones((8, decay.shape[1]), f32)
    product, back = scan_rows(ext[pl.ds(1, rows), :], grad * value, True)
    rev_cum[...] = product
    rev_grad[...] = back
    pair[...] = jnp.broadcast_to(decay[0:1, :] * back[0:1, :], pair.shape)


def mixer_backward(
    rev_cum, rev_grad, incoming, cum, local, carried, rate_pre, input_pre, conv, branch, prior, small, rate_w, input_w,
    own, head, rate_w_grad, input_w_grad, sums, ext, gext,
):
    rows = rev_cum.shape[0]
    soft = small[SOFT : SOFT + 1, :]
    grad_states = rev_grad[...] + rev_cum[...] * incoming[0:1, :]
    rate, decay, square, root, opened = gates(rate_pre[...], input_pre[...], soft)
    ext[0:8, :] = jnp.broadcast_to(carried[0:1, :], (8, carried.shape[1]))
    ext[8:, :] = local[...] + cum[...] * carried[0:1, :]
    before = ext[pl.ds(7, rows), :]
    low = conv[...]
    conv_in = low.astype(f32)
    grad_log = grad_states * decay * before - grad_states * opened * conv_in * square / root
    driven = grad_states * root
    grad_input = (driven * conv_in * opened * (1.0 - opened)).astype(bf16)
    by_rate = grad_log * (-8.0 * rate)
    grad_rate = (by_rate * soft * (1.0 - rate)).astype(bf16)
    sums[6:7, :] = jnp.sum(by_rate, axis=0, keepdims=True) * small[SOFT_SLOPE : SOFT_SLOPE + 1, :]
    sums[4:5, :] = jnp.sum(grad_rate.astype(f32), axis=0, keepdims=True)
    sums[5:6, :] = jnp.sum(grad_input.astype(f32), axis=0, keepdims=True)
    rate_w_grad[...] = mm(low, grad_rate, ((0,), (0,))).astype(rate_w_grad.dtype)
    input_w_grad[...] = mm(low, grad_input, ((0,), (0,))).astype(input_w_grad.dtype)
    grad_conv = (
        driven * opened
        + mm(grad_rate, rate_w[...], ((1,), (1,)))
        + mm(grad_input, input_w[...], ((1,), (1,)))
    )
    sums[7:8, :] = jnp.sum(grad_conv, axis=0, keepdims=True)
    ext[0:8, :] = prior[...]
    ext[8:, :] = branch[...].astype(f32)
    gext[0:8, :] = jnp.zeros((8, grad_conv.shape[1]), f32)
    gext[8 : 8 + rows, :] = grad_conv
    gext[8 + rows :, :] = jnp.zeros((8, grad_conv.shape[1]), f32)
    back = jnp.zeros_like(grad_conv)
    front = jnp.zeros((8, grad_conv.shape[1]), f32)
    for offset in range(4):
        tap = small[TAP + offset : TAP + offset + 1, :]
        sums[offset : offset + 1, :] = jnp.sum(
            grad_conv * ext[pl.ds(8 - offset, rows), :], axis=0, keepdims=True
        )
        back = back + tap * gext[pl.ds(8 + offset, rows), :]
        front = front + tap * gext[pl.ds(offset, 8), :]
    own[...] = back
    head[...] = front


def places():
    s = lax.axis_index("seq")
    z = lax.axis_index("fsdp")
    core = s + 1 - 2 * (s % 2)
    beside = s + 2 - 4 * ((s // 2) % 2)
    across = s + 4 - 8 * (s // 4)
    return s, z, core, beside, across


def greet(peers):
    barrier = pltpu.get_barrier_semaphore()
    for peer in peers:
        pl.semaphore_signal(barrier, inc=1, device_id=peer, device_id_type=MESH)
    pl.semaphore_wait(barrier, len(peers))


def gather_kernel(
    first, branch, gelu, outer, gate, up, down, mixer_all, mlp_mine,
    mixer, load_sem, flow_send, flow_recv, line_send, line_recv, swap_send, swap_recv, own_sem,
):
    s, z, core, beside, across = places()
    rows, cols = mixer.shape
    ff_part = mlp_mine.shape[1] // 3
    cut = cols // 256 * 128
    diag = beside + across - s
    loads, start = [], 0
    for n, part in enumerate((first, branch, gelu, outer)):
        size = part.shape[1]
        loads.append(pltpu.make_async_copy(part, mixer.at[:, pl.ds(start, size)], load_sem.at[n]))
        loads[-1].start()
        start += size
    greet([(core, z), (beside, z), (across, z)] + [(s, (z + k) % 4) for k in range(1, 4)])

    def remote(src, dst, send, recv, target):
        return pltpu.make_async_remote_copy(
            src_ref=src, dst_ref=dst, send_sem=send, recv_sem=recv, device_id=target, device_id_type=MESH
        )

    def piece(seq, zz, half=None):
        span = pl.ds(pl.multiple_of((seq * 4 + zz) * rows, 16), rows)
        if half is None:
            return mixer_all.at[span, :]
        return mixer_all.at[span, pl.ds(0, cut) if half == 0 else pl.ds(cut, cols - cut)]

    def flow(zz, index, seq, half, target, src=None):
        ref = piece(seq, zz, half)
        return remote(
            ref if src is None else src, ref, flow_send.at[zz, index], flow_recv.at[zz, index], (target, z)
        )

    def sends(zz, src=None):
        return [
            flow(zz, 0, s, None, beside, src),
            flow(zz, 1, s, None, across, src),
            flow(zz, 4, s, None, core, src),
        ]

    def spread(zz, src=None):
        for copy in sends(zz, src):
            copy.start()

    def relay(zz):
        flow(zz, 0, beside, None, beside).wait_recv()
        flow(zz, 3, beside, 0, across).start()
        flow(zz, 5, beside, None, core).start()
        flow(zz, 1, across, None, across).wait_recv()
        flow(zz, 2, across, 1, beside).start()
        flow(zz, 6, across, None, core).start()

    def finish(zz):
        flow(zz, 3, diag, 0, across).wait_recv()
        flow(zz, 7, diag, 0, core).start()
        flow(zz, 2, diag, 1, beside).wait_recv()
        flow(zz, 8, diag, 1, core).start()

    def drain(zz, src=None):
        for copy in sends(zz, src):
            copy.wait_send()
        flow(zz, 3, beside, 0, across).wait_send()
        flow(zz, 5, beside, None, core).wait_send()
        flow(zz, 2, across, 1, beside).wait_send()
        flow(zz, 6, across, None, core).wait_send()
        flow(zz, 7, diag, 0, core).wait_send()
        flow(zz, 8, diag, 1, core).wait_send()
        flip = core - s
        flow(zz, 4, core, None, core).wait_recv()
        flow(zz, 5, beside + flip, None, core).wait_recv()
        flow(zz, 6, across + flip, None, core).wait_recv()
        flow(zz, 7, diag + flip, 0, core).wait_recv()
        flow(zz, 8, diag + flip, 1, core).wait_recv()

    def line(zz, up_way, hop, src=None):
        ref = piece(s, zz)
        way = 0 if up_way else 1
        target = z + 1 if up_way else z - 1
        return remote(
            ref if src is None else src, ref, line_send.at[way, hop], line_recv.at[way, hop], (s, target)
        )

    def line_hop(hop):
        def below():
            line(z - hop, True, hop - 1).wait_recv()
            pl.when(z < 3)(lambda: line(z - hop, True, hop).start())

        def above():
            line(z + hop, False, hop - 1).wait_recv()
            pl.when(z > 0)(lambda: line(z + hop, False, hop).start())

        pl.when(z >= hop)(below)
        pl.when(z + hop <= 3)(above)

    def at_hop(hop, act):
        pl.when(z >= hop)(lambda: act(z - hop))
        pl.when(z + hop <= 3)(lambda: act(z + hop))

    def landing(m, zz):
        return mlp_mine.at[pl.ds(pl.multiple_of(zz * rows, 16), rows), pl.ds(m * ff_part, ff_part)]

    def columns(m, zz):
        return (gate, up, down)[m].at[:, pl.ds(pl.multiple_of(zz * ff_part, 128), ff_part)]

    def swap(k, m, arriving=False):
        to = (z + k) % 4
        came = (z + 4 - k) % 4
        return remote(
            columns(m, to), landing(m, came if arriving else z), swap_send.at[k - 1, m], swap_recv.at[k - 1, m], (s, to)
        )

    local = [pltpu.make_async_copy(columns(m, z), landing(m, z), own_sem.at[m]) for m in range(3)]
    local.append(pltpu.make_async_copy(mixer, piece(s, z), own_sem.at[3]))
    for copy in loads:
        copy.wait()

    pl.when(z < 3)(lambda: line(z, True, 0, mixer).start())
    pl.when(z > 0)(lambda: line(z, False, 0, mixer).start())
    spread(z, mixer)
    for copy in local:
        copy.start()
    line_hop(1)
    at_hop(1, spread)
    relay(z)
    line_hop(2)
    at_hop(2, spread)
    finish(z)
    at_hop(1, relay)
    line_hop(3)
    at_hop(3, spread)
    for k in (1, 3, 2):
        for m in range(3):
            swap(k, m).start()
    at_hop(1, finish)
    at_hop(2, relay)
    at_hop(3, relay)
    at_hop(2, finish)
    at_hop(3, finish)
    drain(z, mixer)
    for hop in range(1, 4):
        at_hop(hop, drain)
    for copy in local:
        copy.wait()
    for k in (1, 3, 2):
        for m in range(3):
            swap(k, m).wait_send()
            swap(k, m, True).wait_recv()
    pl.when(z < 3)(lambda: line(z, True, 0, mixer).wait_send())
    pl.when(z > 0)(lambda: line(z, False, 0, mixer).wait_send())
    for hop in range(1, 3):
        pl.when((z >= hop) & (z < 3))(lambda: line(z - hop, True, hop).wait_send())
        pl.when((z + hop <= 3) & (z > 0))(lambda: line(z + hop, False, hop).wait_send())


def gather(first, branch, gelu, outer, gate, up, down):
    rows = first.shape[0]
    cols = first.shape[1] + branch.shape[1] + gelu.shape[1] + outer.shape[1]
    ff_part = gate.shape[1] // 4
    anyspec = pl.BlockSpec(memory_space=pl.ANY)
    dma = pltpu.SemaphoreType.DMA
    return pl.pallas_call(
        gather_kernel,
        in_specs=[anyspec] * 7,
        out_specs=[anyspec] * 2,
        out_shape=[
            jax.ShapeDtypeStruct((32 * rows, cols), bf16),
            jax.ShapeDtypeStruct((4 * rows, 3 * ff_part), bf16),
        ],
        scratch_shapes=[
            pltpu.VMEM((rows, cols), bf16), dma((4,)),
            dma((4, 9)), dma((4, 9)), dma((2, 3)), dma((2, 3)), dma((3, 3)), dma((3, 3)), dma((4,)),
        ],
        compiler_params=pltpu.CompilerParams(collective_id=1, has_side_effects=True),
        name="gather_weights",
    )(first, branch, gelu, outer, gate, up, down)


def rows_kernel(
    normed, grad0, grad1, grad2, grad3, first, mixed, normed_all, normed_other, grad_all, grad_other,
    first_other, mixed_other, line_send, line_recv, core_send, core_recv, own_sem, held, give_send, give_recv,
):
    s, z, core, _, _ = places()
    tok = normed.shape[0]
    cuts = 4
    grads = (grad0, grad1, grad2, grad3)
    greet([(core, z)] + [(s, (z + k) % 4) for k in range(1, 4)])

    def rows(ref, zz):
        return ref.at[pl.ds(pl.multiple_of(zz * tok, 16), tok), :]

    def remote(src, dst, send, recv, target):
        return pltpu.make_async_remote_copy(
            src_ref=src, dst_ref=dst, send_sem=send, recv_sem=recv, device_id=target, device_id_type=MESH
        )

    def parts(ref):
        size = tok // cuts
        return [ref.at[pl.ds(n * size, size), :] for n in range(cuts)]

    def line(zz, up_way, hop):
        way = 0 if up_way else 1
        target = z + 1 if up_way else z - 1
        src = normed if hop == 0 else rows(normed_all, zz)
        dst = rows(normed_all, zz)
        return [
            remote(a, b, line_send.at[way, hop, n], line_recv.at[way, hop, n], (s, target))
            for n, (a, b) in enumerate(zip(parts(src), parts(dst)))
        ]

    def over(zz, own=False):
        src = normed if own else rows(normed_all, zz)
        return remote(src, rows(normed_other, zz), core_send.at[0, zz], core_recv.at[0, zz], (core, z))

    def grad_over(k):
        zz = (z + 4 - k) % 4
        return remote(grads[k], rows(grad_other, zz), core_send.at[1, zz], core_recv.at[1, zz], (core, z))

    def line_start(zz, up_way, hop):
        for copy in line(zz, up_way, hop):
            copy.start()

    def line_drain(zz, up_way, hop):
        for copy in line(zz, up_way, hop):
            copy.wait_send()

    def hop_step(hop):
        def below():
            for came, on in zip(line(z - hop, True, hop - 1), line(z - hop, True, hop) if hop < 3 else [None] * cuts):
                came.wait_recv()
                if on is not None:
                    pl.when(z < 3)(on.start)
            over(z - hop).start()

        def above():
            for came, on in zip(line(z + hop, False, hop - 1), line(z + hop, False, hop) if hop < 3 else [None] * cuts):
                came.wait_recv()
                if on is not None:
                    pl.when(z > 0)(on.start)
            over(z + hop).start()

        pl.when(z >= hop)(below)
        pl.when(z + hop <= 3)(above)

    given = [
        remote(source, target, give_send.at[n], give_recv.at[n], (core, z))
        for n, (source, target) in enumerate(((first, first_other), (mixed, mixed_other)))
    ]
    local = [pltpu.make_async_copy(grads[k], held.at[k], own_sem.at[k]) for k in range(4)]
    local.append(pltpu.make_async_copy(normed, held.at[4], own_sem.at[4]))
    stored = [
        pltpu.make_async_copy(held.at[k], rows(grad_all, (z + 4 - k) % 4), own_sem.at[k]) for k in range(4)
    ]
    stored.append(pltpu.make_async_copy(held.at[4], rows(normed_all, z), own_sem.at[4]))
    pl.when(z < 3)(lambda: line_start(z, True, 0))
    pl.when(z > 0)(lambda: line_start(z, False, 0))
    over(z, True).start()
    for copy in local:
        copy.start()
    for k in range(4):
        grad_over(k).start()
    for copy in given:
        copy.start()
    for copy, store in zip(local, stored):
        copy.wait()
        store.start()
    for hop in range(1, 4):
        hop_step(hop)
    for copy in stored:
        copy.wait()
    for k in range(4):
        grad_over(k).wait()
    for copy in given:
        copy.wait()
    over(z, True).wait()
    for k in range(1, 4):
        over((z + k) % 4).wait()
    pl.when(z < 3)(lambda: line_drain(z, True, 0))
    pl.when(z > 0)(lambda: line_drain(z, False, 0))
    for hop in range(1, 3):
        pl.when((z >= hop) & (z < 3))(lambda: line_drain(z - hop, True, hop))
        pl.when((z + hop <= 3) & (z > 0))(lambda: line_drain(z + hop, False, hop))


def gather_rows(normed, grads, first, mixed):
    tok, model = normed.shape
    anyspec = pl.BlockSpec(memory_space=pl.ANY)
    dma = pltpu.SemaphoreType.DMA
    return pl.pallas_call(
        rows_kernel,
        in_specs=[anyspec] * 7,
        out_specs=[anyspec] * 6,
        out_shape=[jax.ShapeDtypeStruct((4 * tok, model), bf16)] * 4
        + [jax.ShapeDtypeStruct(first.shape, bf16), jax.ShapeDtypeStruct(mixed.shape, bf16)],
        scratch_shapes=[
            dma((2, 3, 4)), dma((2, 3, 4)), dma((2, 4)), dma((2, 4)), dma((5,)),
            pltpu.VMEM((5, tok, model), bf16), dma((2,)), dma((2,)),
        ],
        compiler_params=pltpu.CompilerParams(collective_id=3, has_side_effects=True),
        name="gather_rows",
    )(normed, *grads, first, mixed)


def column_tiles(cols, size=512):
    return [(start, min(size, cols - start)) for start in range(0, cols, size)]


def feed_forward_kernel(
    normed, grad_out, weights, hidden, hidden_other, pair, pair_other, back,
    held, hidden_now, pair_now, sems, store_sem, core_send, core_recv,
):
    s, z, core, _, _ = places()
    step = pl.program_id(0)
    ff_part = held.shape[2]
    model = held.shape[1]
    rows = normed.shape[0]
    tiles = column_tiles(ff_part)
    made = ((hidden_now, hidden, hidden_other), (pair_now, pair, pair_other))

    def load(n, m):
        start, size = tiles[n]
        return pltpu.make_async_copy(
            weights.at[:, pl.ds(m * ff_part + start, size)], held.at[m, :, pl.ds(start, size)], sems.at[n, m]
        )

    def kept(n, turn):
        now, mine, _ = made[n]
        return pltpu.make_async_copy(now.at[turn], mine.at[pl.ds(turn * rows, rows), :], store_sem.at[turn, n])

    def handed(n, turn):
        now, _, other = made[n]
        return pltpu.make_async_remote_copy(
            src_ref=now.at[turn],
            dst_ref=other.at[pl.ds(turn * rows, rows), :],
            send_sem=core_send.at[turn, n],
            recv_sem=core_recv.at[turn, n],
            device_id=(core, z),
            device_id_type=MESH,
        )

    @pl.when(step == 0)
    def _():
        for n in range(len(tiles)):
            for m in range(3):
                load(n, m).start()
        greet([(core, z)])

    for n, (start, size) in enumerate(tiles):
        cols = slice(start, start + size)

        @pl.when(step == 0)
        def _(n=n):
            for m in range(3):
                load(n, m).wait()

        gate = mm(normed[...], held[0, :, cols], ((1,), (0,)))
        value, slope = gelu_parts(gate)
        up = mm(normed[...], held[1, :, cols], ((1,), (0,)))
        hidden_now[step, :, cols] = (value * up).astype(bf16)
        grad_hidden = mm(grad_out[...], held[2, :, cols], ((1,), (0,)))
        pair_now[step, :, cols] = (grad_hidden * up * slope).astype(bf16)
        pair_now[step, :, slice(ff_part + start, ff_part + start + size)] = (grad_hidden * value).astype(bf16)

    for turn in range(2):

        @pl.when(step == turn)
        def _(turn=turn):
            for n in range(2):
                handed(n, turn).start()
                kept(n, turn).start()

    def back_tile(turn, carry):
        cols = pl.ds(pl.multiple_of(turn * 512, 512), 512)
        total = mm(pair_now[step, :, :ff_part], held[0, cols, :], ((1,), (1,)))
        total = total + mm(pair_now[step, :, ff_part:], held[1, cols, :], ((1,), (1,)))
        back[:, cols] = total.astype(bf16)
        return carry

    lax.fori_loop(0, model // 512, back_tile, 0)

    @pl.when(step == 1)
    def _():
        for turn in range(2):
            for n in range(2):
                kept(n, turn).wait()
                handed(n, turn).wait()


def feed_forward(normed, grad_out, weights):
    tok, model = normed.shape
    ff_part = weights.shape[1] // 3
    rows = tok // 2
    anyspec = pl.BlockSpec(memory_space=pl.ANY)
    dma = pltpu.SemaphoreType.DMA
    block = pl.BlockSpec((rows, model), lambda i: (i, 0))
    return pl.pallas_call(
        feed_forward_kernel,
        grid=(2,),
        in_specs=[block, block, anyspec],
        out_specs=[anyspec] * 4 + [block],
        out_shape=[
            jax.ShapeDtypeStruct((tok, cols), bf16)
            for cols in (ff_part, ff_part, 2 * ff_part, 2 * ff_part, model)
        ],
        scratch_shapes=[
            pltpu.VMEM((3, model, ff_part), bf16),
            pltpu.VMEM((2, rows, ff_part), bf16),
            pltpu.VMEM((2, rows, 2 * ff_part), bf16),
            dma((len(column_tiles(ff_part)), 3)), dma((2, 2)), dma((2, 2)), dma((2, 2)),
        ],
        compiler_params=pltpu.CompilerParams(
            collective_id=4, has_side_effects=True, vmem_limit_bytes=60 * 1024 * 1024
        ),
        name="feed_forward",
    )(normed, grad_out, weights)


def add_columns(target, sources, start, size, step):
    def one(turn, carry):
        cols = pl.ds(pl.multiple_of(start + turn * step, 128), step)
        total = target[:, cols].astype(f32)
        for source in sources:
            total = total + source[:, cols].astype(f32)
        target[:, cols] = total.astype(target.dtype)
        return carry

    lax.fori_loop(0, size // step, one, 0)


def shared_products_kernel(
    normed, normed_other, grad, grad_other, weights, pair, pair_other, hidden, hidden_other,
    beside_high, across_low, mine, beside_low, across_high, out,
    turned, slots, stage, diag, landed, waiting, down_now, out_now,
    load_sem, send_sem, recv_sem, store_sem, down_sem, out_sem,
):
    s, z, _, beside, across = places()
    step = pl.program_id(0)
    lefts = ((normed, normed_other), (grad, grad_other))
    chip_cols = normed.shape[1] // 4
    half = chip_cols // 2
    piece = half // 2
    width = pair.shape[1]
    diagonal = beside + across - s
    chips = [q // 2 for q in (diagonal, beside, across, s)]

    def load(side, q, who):
        cols = pl.ds(pl.multiple_of(chips[q] * chip_cols, 128), chip_cols)
        return pltpu.make_async_copy(lefts[side][who].at[:, cols], slots.at[q % 2, who], load_sem.at[q % 2, who])

    def fetch(side):
        for q in range(2):
            for who in range(2):
                load(side, q, who).start()

    def turn(side):
        for q in range(4):
            for who in range(2):
                load(side, q, who).wait()
                stage[...] = slots[q % 2, who].T
                turned[who, q * half : (q + 1) * half, :] = stage[
                    pl.ds(pl.multiple_of(s % 2 * half, 16), half), :
                ]
                if q < 2:
                    load(side, q + 2, who).start()

    def tile(own, other, start, size):
        cols = pl.ds(start, size)
        block = mm(turned[0], own[:, cols], ((1,), (0,)))
        block = (block + mm(turned[1], other[:, cols], ((1,), (0,)))).astype(bf16)
        parts = [block[n * piece : (n + 1) * piece] for n in range(8)]
        there = pl.ds(pl.multiple_of(step * width + start, 128), size)
        diag[0, :, there] = parts[0]
        diag[1, :, there] = parts[1]
        waiting[0, :, there] = parts[2]
        beside_high[:, cols] = parts[3]
        across_low[:, cols] = parts[4]
        waiting[1, :, there] = parts[5]
        mine[0:piece, cols] = parts[6]
        mine[piece:, cols] = parts[7]

    def multiply(own, other):
        def one(turn, carry):
            tile(own, other, pl.multiple_of(turn * 512, 512), 512)
            return carry

        lax.fori_loop(0, width // 512, one, 0)
        if width % 512:
            tile(own, other, width // 512 * 512, width % 512)

    def push(way, j):
        cols = pl.ds(j * width, width)
        return pltpu.make_async_remote_copy(
            src_ref=diag.at[way, :, cols],
            dst_ref=landed.at[way, :, cols],
            send_sem=send_sem.at[way, j],
            recv_sem=recv_sem.at[way, j],
            device_id=(across if way == 0 else beside, z),
            device_id_type=MESH,
        )

    def store(way, j):
        cols = pl.ds(j * width, width)
        return pltpu.make_async_copy(
            waiting.at[way, :, cols], (beside_low, across_high)[way].at[:, cols], store_sem.at[way, j]
        )

    out_rows = down_now.shape[1]
    out_tiles = weights.shape[0] // out_rows

    def down(t):
        source = weights.at[pl.ds(t * out_rows, out_rows), pl.ds(2 * width, width)]
        return pltpu.make_async_copy(source, down_now.at[t % 2], down_sem.at[t % 2])

    def out_store(t):
        return pltpu.make_async_copy(
            out_now.at[t % 2], out.at[:, pl.ds(t * out_rows, out_rows)], out_sem.at[t % 2]
        )

    def out_product():
        for t in range(out_tiles):
            down(t).wait()
            if t > 1:
                out_store(t - 2).wait()
            out_now[t % 2] = mm(hidden[...], down_now[t % 2], ((1,), (1,))).astype(bf16)
            out_store(t).start()
            if t + 2 < out_tiles:
                down(t + 2).start()

    @pl.when(step == 0)
    def _():
        fetch(0)
        greet([(beside, z), (across, z)])
        turn(0)

    @pl.when(step == 2)
    def _():
        down(0).start()
        down(1).start()
        turn(1)

    pl.when(step < 2)(functools.partial(multiply, pair, pair_other))
    pl.when(step == 1)(functools.partial(fetch, 1))
    pl.when(step == 2)(functools.partial(multiply, hidden, hidden_other))
    for j in range(3):

        @pl.when(step == j)
        def _(j=j):
            push(0, j).start()
            push(1, j).start()

    @pl.when(step == 2)
    def _():
        out_product()
        for j in range(3):
            for way in range(2):
                push(way, j).wait_recv()
                add_columns(waiting.at[way], [landed.at[way]], j * width, width, 384)
                store(way, j).start()
        for j in range(3):
            for way in range(2):
                push(way, j).wait_send()
                store(way, j).wait()
        for t in range(out_tiles - 2, out_tiles):
            out_store(t).wait()


def shared_products(lefts, weights, pair, hidden):
    tok, model = lefts[0].shape
    width = hidden[0].shape[1]
    half = model // 8
    anyspec = pl.BlockSpec(memory_space=pl.ANY)
    dma = pltpu.SemaphoreType.DMA

    def block(rows):
        return pl.BlockSpec((rows, width), lambda j: (0, j))

    pair_spec = pl.BlockSpec((tok, width), lambda j: (0, jnp.minimum(j, 1)))
    hidden_spec = pl.BlockSpec((tok, width), lambda j: (0, 0))
    rows_out = (half // 2, half // 2, half, half // 2, half // 2)
    return pl.pallas_call(
        shared_products_kernel,
        grid=(3,),
        in_specs=[anyspec] * 5 + [pair_spec] * 2 + [hidden_spec] * 2,
        out_specs=[block(rows) for rows in rows_out[:3]] + [anyspec] * 3,
        out_shape=[jax.ShapeDtypeStruct((rows, 3 * width), bf16) for rows in rows_out]
        + [jax.ShapeDtypeStruct((tok, model), bf16)],
        scratch_shapes=[
            pltpu.VMEM((2, 4 * half, tok), bf16),
            pltpu.VMEM((2, 2, tok, 2 * half), bf16),
            pltpu.VMEM((2 * half, tok), bf16),
            pltpu.VMEM((2, half // 2, 3 * width), bf16),
            pltpu.VMEM((2, half // 2, 3 * width), bf16),
            pltpu.VMEM((2, half // 2, 3 * width), bf16),
            pltpu.VMEM((2, 512, width), bf16),
            pltpu.VMEM((2, tok, 512), bf16),
            dma((2, 2)), dma((2, 3)), dma((2, 3)), dma((2, 3)), dma((2,)), dma((2,)),
        ],
        compiler_params=pltpu.CompilerParams(
            collective_id=5, has_side_effects=True, vmem_limit_bytes=60 * 1024 * 1024
        ),
        name="feed_forward_products",
    )(*lefts, weights, *pair, *hidden)


def scatter_kernel(
    normed, normed_other, grad_mix, mix_other, mixed, mixed_other, grad_gelu, gelu_other, grad_branch, rest,
    mlp_low, mlp_high, mixer_w, tokens, gain, mixer_sum, mlp_back, input_grad,
    held, cross, near, lined, left_now, both_now, mixed_now, turned, stage, rest_other, back_now, wide_now, gain_now,
    load_sem, core_send, core_recv, wide_sem,
    flow_send, flow_recv, line_send, line_recv, swap_send, swap_recv, own_sem,
):
    s, z, core, beside, across = places()
    chip_diag, chip_beside, chip_across, chip = 0, 1, 2, 3
    chips = [q // 2 for q in (beside + across - s, beside, across, s)]
    rows = held.shape[1] // 4
    cols = held.shape[2]
    cut = cols // 256 * 128
    ff_part = mlp_low.shape[1] // 3
    tok, model = tokens.shape
    half = 4 * rows
    lru = grad_branch.shape[1]
    lru2 = 2 * lru
    rest_start = lru2 + mixed.shape[1]
    order = (3 * (1 - z // 2), (2 + 3 * z) % 5, 1 + z % 2, z)

    def remote(src, dst, send, recv, target):
        return pltpu.make_async_remote_copy(
            src_ref=src, dst_ref=dst, send_sem=send, recv_sem=recv, device_id=target, device_id_type=MESH
        )

    def span(k):
        return pl.ds(pl.multiple_of(k * rows, 16), rows)

    mine, other = pl.ds(0, tok), pl.ds(tok, tok)
    loads = [
        pltpu.make_async_copy(source, target, load_sem.at[n])
        for n, (source, target) in enumerate(
            (
                (grad_mix, left_now.at[1, mine, :]),
                (mix_other, left_now.at[1, other, :]),
                (mixed, mixed_now.at[mine, :]),
                (mixed_other, mixed_now.at[other, :]),
                (normed, left_now.at[0, mine, :]),
                (normed_other, left_now.at[0, other, :]),
                (grad_gelu, both_now.at[mine, pl.ds(lru, lru)]),
                (gelu_other, both_now.at[other, pl.ds(lru, lru)]),
                (grad_branch, both_now.at[mine, pl.ds(0, lru)]),
            )
        )
    ]

    def push(n):
        if n == 0:
            source, target = grad_branch, both_now.at[other, pl.ds(0, lru)]
        else:
            source = rest.at[pl.ds(pl.multiple_of(chips[n - 1] * 2 * half + (1 - s % 2) * half, 16), half), :]
            target = rest_other.at[n - 1]
        return pltpu.make_async_remote_copy(
            src_ref=source,
            dst_ref=target,
            send_sem=core_send.at[n],
            recv_sem=core_recv.at[n],
            device_id=(core, z),
            device_id_type=MESH,
        )

    def rest_load(q):
        source = rest.at[pl.ds(pl.multiple_of(chips[q] * 2 * half + s % 2 * half, 16), half), :]
        return pltpu.make_async_copy(
            source, held.at[q, :, pl.ds(rest_start, cols - rest_start)], load_sem.at[9 + q]
        )

    def turn(side):
        for q in range(4):
            source = left_now[side, :, pl.ds(pl.multiple_of(chips[q] * 2 * half, 128), 2 * half)]
            stage[...] = source.T
            turned[side, q * half : (q + 1) * half, :] = stage[
                pl.ds(pl.multiple_of(s % 2 * half, 16), half), :
            ]

    def multiply(q, side, first=0, last=None):
        right, start = ((both_now, 0), (mixed_now, lru2))[side]

        def one(turn, carry):
            here = pl.multiple_of(turn * 512, 512)
            block = mm(turned[side, q * half : (q + 1) * half, :], right[:, pl.ds(here, 512)], ((1,), (0,)))
            held[q, :, pl.ds(pl.multiple_of(start + here, 512), 512)] = block.astype(bf16)
            return carry

        lax.fori_loop(first // 512, (right.shape[1] if last is None else last) // 512, one, 0)

    def add_rest(q):
        rest_load(q).wait()
        push(1 + q).wait_recv()
        held[q, :, rest_start:] = add_low(held[q, :, rest_start:], rest_other[q])

    left, right = pl.ds(0, cut), pl.ds(cut, cols - cut)

    def block(q, i, side):
        return held.at[q, span(order[i]), side]

    def flow(i, index):
        send, recv = flow_send.at[i, index], flow_recv.at[i, index]
        to_beside, to_across = (beside, z), (across, z)
        if index == 0:
            return remote(block(chip_diag, i, left), cross.at[i, :, left], send, recv, to_across)
        if index == 1:
            return remote(block(chip_diag, i, right), cross.at[i, :, right], send, recv, to_beside)
        if index == 2:
            return remote(block(chip_beside, i, right), near.at[0, i, :, right], send, recv, to_beside)
        if index == 3:
            return remote(block(chip_beside, i, left), near.at[0, i, :, left], send, recv, to_beside)
        if index == 4:
            return remote(block(chip_across, i, left), near.at[1, i, :, left], send, recv, to_across)
        return remote(block(chip_across, i, right), near.at[1, i, :, right], send, recv, to_across)

    def cross_step(i):
        flow(i, 0).wait_recv()
        add_columns(held.at[chip_beside, span(order[i]), :], [cross.at[i]], 0, cut, 512)
        flow(i, 3).start()
        flow(i, 1).wait_recv()
        add_columns(held.at[chip_across, span(order[i]), :], [cross.at[i]], cut, cols - cut, 384)
        flow(i, 5).start()

    def near_step(i):
        for index in (2, 4, 3, 5):
            flow(i, index).wait_recv()
        add_columns(held.at[chip, span(order[i]), :], [near.at[0, i], near.at[1, i]], 0, cols, 640)

    def line(k, slot, target):
        return remote(
            held.at[chip, span(k), :], lined.at[slot], line_send.at[k], line_recv.at[slot], (s, target)
        )

    def absorb(k, slot, source):
        line(k, slot, source).wait_recv()
        add_columns(held.at[chip, span(k), :], [lined.at[slot]], 0, cols, 640)

    def chain(i):
        k = order[i]
        if i == 3:
            pl.when(z > 0)(lambda: absorb(k, k, z - 1))
            pl.when(z < 3)(lambda: absorb(k, 4, z + 1))
            return

        @pl.when(k > z)
        def _():
            pl.when(z > 0)(lambda: absorb(k, k, z - 1))
            line(k, k, z + 1).start()

        @pl.when(k < z)
        def _():
            pl.when(z < 3)(lambda: absorb(k, k, z + 1))
            pl.when(k == z - 1)(lambda: line(k, 4, z - 1).start())
            pl.when(k < z - 1)(lambda: line(k, k, z - 1).start())

    def chain_drain():
        for i in range(3):
            k = order[i]
            line(k, k, (z + 1) % 4).wait_send()

    def swap(k, high=False):
        to = (z + k) % 4
        here = pl.ds(pl.multiple_of(z * ff_part, 128), ff_part)
        source = (mlp_high if high else mlp_low).at[span(to % 2), :]
        return [
            remote(
                source.at[:, pl.ds(m * ff_part, ff_part)],
                mlp_back.at[m, :, here],
                swap_send.at[k - 1, m],
                swap_recv.at[k - 1, m],
                (s, to),
            )
            for m in range(3)
        ]

    def swap_start(k):
        to = (z + k) % 4

        @pl.when(to < 2)
        def _():
            for copy in swap(k):
                copy.start()

        @pl.when(to >= 2)
        def _():
            for copy in swap(k, True):
                copy.start()

    def own(high=False):
        here = pl.ds(pl.multiple_of(z * ff_part, 128), ff_part)
        source = (mlp_high if high else mlp_low).at[span(z % 2), :]
        return [
            pltpu.make_async_copy(source.at[:, pl.ds(m * ff_part, ff_part)], mlp_back.at[m, :, here], own_sem.at[m])
            for m in range(3)
        ]

    wide_rows = wide_now.shape[0]
    wide_tiles = mixer_w.shape[0] // wide_rows
    wide_start = mixer_w.shape[1] - lru2 - model
    wide_slots = (both_now.at[pl.ds(tok, wide_rows), :], wide_now)

    def wide(j):
        source = mixer_w.at[pl.ds(j * wide_rows, wide_rows), pl.ds(wide_start, lru2)]
        return pltpu.make_async_copy(source, wide_slots[j % 2], wide_sem.at[j % 2])

    plain_loads = [
        pltpu.make_async_copy(tokens, left_now.at[0, pl.ds(0, tok), :], wide_sem.at[2]),
        pltpu.make_async_copy(gain, gain_now, wide_sem.at[3]),
    ]

    def back(first, last):
        for j in range(first, last):
            wide(j).wait()
            back_now[:, pl.ds(j * wide_rows, wide_rows)] = mm(
                both_now[0:tok, :], wide_slots[j % 2][...], ((1,), (1,))
            )
            if j + 2 < wide_tiles:
                wide(j + 2).start()

    def finish_rows(turn, carry):
        at = pl.ds(pl.multiple_of(turn * 16, 16), 16)
        result = left_now[1, at, :].astype(f32) + norm_back(
            left_now[0, at, :].astype(f32), gain_now[GAIN_ONE : GAIN_ONE + 1, :], back_now[at, :]
        )
        left_now[0, at, :] = result.astype(bf16)
        return carry

    for copy in loads:
        copy.start()
    for q in range(4):
        rest_load(q).start()
    greet([(core, z), (beside, z), (across, z)] + [(s, (z + k) % 4) for k in range(1, 4)])
    for n in range(5):
        push(n).start()
    for k in (1, 3, 2):
        swap_start(k)

    @pl.when(z < 2)
    def _():
        for copy in own():
            copy.start()

    @pl.when(z >= 2)
    def _():
        for copy in own(True):
            copy.start()

    for copy in loads[:4]:
        copy.wait()
    turn(1)
    multiply(chip_diag, 1)
    for copy in loads[4:]:
        copy.wait()
    turn(0)
    multiply(chip_diag, 0, lru)
    push(0).wait_recv()
    multiply(chip_diag, 0, 0, lru)
    add_rest(chip_diag)
    for i in range(2):
        flow(i, 0).start()
        flow(i, 1).start()
    for q in (chip_beside, chip_across, chip):
        multiply(q, 0)
        multiply(q, 1)
        add_rest(q)
        if q == chip_beside:
            flow(0, 2).start()
        if q == chip_across:
            flow(0, 4).start()
    for copy in plain_loads:
        copy.start()
    wide(0).start()
    wide(1).start()
    for i in range(4):
        cross_step(i)
        if i + 1 < 4:
            flow(i + 1, 2).start()
            flow(i + 1, 4).start()
        if i + 2 < 4:
            flow(i + 2, 0).start()
            flow(i + 2, 1).start()
        if i > 0:
            near_step(i - 1)
            chain(i - 1)
            back(wide_tiles * (i - 1) // 3, wide_tiles * i // 3)
    for copy in plain_loads:
        copy.wait()
    lax.fori_loop(0, tok // 16, finish_rows, 0)
    finished = pltpu.make_async_copy(left_now.at[0, pl.ds(0, tok), :], input_grad, wide_sem.at[2])
    finished.start()
    near_step(3)
    chain(3)
    done = pltpu.make_async_copy(held.at[chip, span(z), :], mixer_sum, own_sem.at[3])
    done.start()
    for i in range(4):
        for index in range(6):
            flow(i, index).wait_send()
    chain_drain()
    for k in range(1, 4):
        for copy in swap(k):
            copy.wait()
    for copy in own():
        copy.wait()
    for n in range(5):
        push(n).wait_send()
    finished.wait()
    done.wait()


def scatter(rows_pairs, grad_branch, rest, mlp_low, mlp_high, mixer_w, tokens, gain):
    tok, model = tokens.shape
    rows = model // 32
    lru = grad_branch.shape[1]
    cols = 3 * lru + rest.shape[1]
    ff_part = mlp_low.shape[1] // 3
    anyspec = pl.BlockSpec(memory_space=pl.ANY)
    dma = pltpu.SemaphoreType.DMA
    return pl.pallas_call(
        scatter_kernel,
        in_specs=[anyspec] * 15,
        out_specs=[anyspec] * 3,
        out_shape=[
            jax.ShapeDtypeStruct((rows, cols), bf16),
            jax.ShapeDtypeStruct((3, rows, 4 * ff_part), bf16),
            jax.ShapeDtypeStruct((tok, model), bf16),
        ],
        scratch_shapes=[
            pltpu.VMEM((4, 4 * rows, cols), bf16),
            pltpu.VMEM((4, rows, cols), bf16),
            pltpu.VMEM((2, 4, rows, cols), bf16),
            pltpu.VMEM((5, rows, cols), bf16),
            pltpu.VMEM((2, 2 * tok, model), bf16),
            pltpu.VMEM((2 * tok, 2 * lru), bf16),
            pltpu.VMEM((2 * tok, lru), bf16),
            pltpu.VMEM((2, 16 * rows, 2 * tok), bf16),
            pltpu.VMEM((8 * rows, 2 * tok), bf16),
            pltpu.VMEM((4, 4 * rows, rest.shape[1]), bf16),
            pltpu.VMEM((tok, model), f32),
            pltpu.VMEM((128, 2 * lru), bf16),
            pltpu.VMEM(gain.shape, f32),
            dma((13,)), dma((5,)), dma((5,)), dma((4,)),
            dma((4, 6)), dma((4, 6)), dma((4,)), dma((5,)), dma((3, 3)), dma((3, 3)), dma((4,)),
        ],
        compiler_params=pltpu.CompilerParams(
            collective_id=2, has_side_effects=True, vmem_limit_bytes=62 * 1024 * 1024
        ),
        name="scatter_gradients",
    )(*rows_pairs, grad_branch, rest, mlp_low, mlp_high, mixer_w, tokens, gain)


def gather_plain(mixer, gate, up, down):
    groups = lax.axis_size("fsdp")
    part_rows, ff = gate.shape
    own = jnp.stack([w.reshape(part_rows, groups, ff // groups) for w in (gate, up, down)], axis=2)
    mine = lax.all_to_all(jnp.transpose(own, (1, 0, 2, 3)), "fsdp", 0, 0, tiled=True)
    return lax.all_gather(mixer, both, axis=0, tiled=True), mine.reshape(groups * part_rows, -1)


def from_line(shard):
    count = lax.axis_size("fsdp")
    return [shard] + [
        lax.ppermute(shard, "fsdp", [(i, (i + k) % count) for i in range(count)]) for k in range(1, count)
    ]


def swap_cores(shard):
    count = lax.axis_size("seq")
    return lax.ppermute(shard, "seq", [(i, i + 1 - 2 * (i % 2)) for i in range(count)])


def swap_beside(shard):
    return lax.ppermute(shard, "seq", [(i, i ^ 2) for i in range(8)])


def swap_across(shard):
    return lax.ppermute(shard, "seq", [(i, i ^ 4) for i in range(8)])


def add_low(left, right):
    return (left.astype(f32) + right.astype(f32)).astype(bf16)


def scatter_plain(normed, grad_both, grad_mix, mixed, rest, mlp_sum):
    groups = lax.axis_size("fsdp")
    term_wide = mm(normed, grad_both, ((0,), (0,))).astype(bf16)
    term_out = mm(grad_mix, mixed, ((0,), (0,))).astype(bf16)
    mixer_sum = lax.psum_scatter(
        jnp.concatenate([term_wide, term_out, rest], axis=1), "seq", scatter_dimension=0, tiled=True
    )
    mixer_sum = lax.psum_scatter(mixer_sum, "fsdp", scatter_dimension=0, tiled=True)
    ff_part = mlp_sum.shape[1] // 3
    part_rows = mlp_sum.shape[0] // groups
    mlp_sum = mlp_sum.reshape(groups, part_rows, 3, ff_part)
    mlp_back = lax.all_to_all(mlp_sum, "fsdp", 0, 0, tiled=True)
    mlp_back = jnp.transpose(mlp_back, (2, 1, 0, 3)).reshape(3, part_rows, groups * ff_part)
    return mixer_sum, mlp_back


def call_heads(kernel, width, heads, ins, outs, scratch, name):
    def spec(rows, place):
        if place is None:
            return pl.BlockSpec((rows, width), lambda h: (0, h))
        return pl.BlockSpec((width, width), lambda h: (h, place))

    in_specs = [spec(a.shape[0], place) for a, place in ins]
    out_specs = [spec(rows, 0 if rowwise else None) for rows, _, rowwise in outs]
    out_shape = [
        jax.ShapeDtypeStruct((heads * width, width) if rowwise else (rows, heads * width), kind)
        for rows, kind, rowwise in outs
    ]
    return pl.pallas_call(
        kernel,
        grid=(heads,),
        in_specs=in_specs,
        out_specs=out_specs,
        out_shape=out_shape,
        scratch_shapes=[pltpu.VMEM((rows, width), f32) for rows in scratch],
        compiler_params=pltpu.CompilerParams(vmem_limit_bytes=40 * 1024 * 1024),
        cost_estimate=pl.CostEstimate(flops=1, bytes_accessed=1, transcendentals=0),
        name=name,
    )(*[a for a, _ in ins])


def on_device(
    block_input,
    cotangent,
    mixer_gain,
    branch_proj,
    gelu_proj,
    conv_taps,
    conv_bias,
    rate_blocks,
    input_blocks,
    rate_bias,
    input_bias,
    decay_param,
    out_proj,
    mlp_gain,
    gate_proj,
    up_proj,
    down_proj,
):
    groups = lax.axis_size("fsdp")
    part_rows, lru = branch_proj.shape
    width = rate_blocks.shape[1]
    heads = lru // width
    margin = conv_taps.shape[0] - 1
    tokens = block_input[0].astype(f32)
    tok_count, model = tokens.shape
    ff = gate_proj.shape[1]
    ff_part = ff // groups
    grad_out = cotangent[0]

    smalls = jnp.stack(
        [conv_taps[k] for k in range(margin + 1)]
        + [conv_bias, rate_bias, input_bias, decay_param, mixer_gain, mlp_gain],
        axis=1,
    )
    small_count = smalls.shape[1]
    smalls = jnp.pad(smalls, ((0, 0), (0, 128 - small_count)))
    first_own = jnp.concatenate([rate_blocks, input_blocks, smalls], axis=1)
    mixer_own = (first_own, branch_proj, gelu_proj, out_proj)
    custom = lax.axis_size("seq") == 8 and groups == 4
    if custom:
        mixer_w, mlp_mine = gather(*mixer_own, gate_proj, up_proj, down_proj)
    else:
        mixer_w, mlp_mine = gather_plain(jnp.concatenate(mixer_own, axis=1), gate_proj, up_proj, down_proj)
    mlp_w = lax.all_gather(mlp_mine, "seq", axis=0, tiled=True)
    grad_out_late = lax.optimization_barrier((grad_out, mlp_mine))[0]
    if custom:
        grad_pieces = from_line(grad_out_late)
    wide = mixer_w[:, 128 + 2 * width : 128 + 2 * width + 2 * lru]
    proj_out = mixer_w[:, 128 + 2 * width + 2 * lru :]

    small = small_table(mixer_w, 2 * width // 128)
    gain_one, gain_two = small[GAIN_ONE], small[GAIN_TWO]

    normed, branch, gelu_pre = mixer_in(block_input[0], small, mixer_w, lru, 2 * width + 128)
    prior = from_behind(branch[tok_count - margin :], "seq", 1).astype(f32)
    prior = jnp.concatenate([jnp.zeros((8 - margin, lru), f32), prior], axis=0)
    conv, rate_pre, input_pre, cum, local = call_heads(
        mixer_forward,
        width,
        heads,
        [(branch, None), (prior, None), (small, None), (mixer_w, 0), (mixer_w, 1)],
        [(tok_count, bf16, False)] + [(tok_count, f32, False)] * 4,
        [tok_count + 8],
        "mixer_forward",
    )
    carried = prefix((cum[-1], local[-1]), "seq", False)
    states = local + cum * carried[None]
    mixed = (states * jax.nn.gelu(gelu_pre, approximate=True)).astype(bf16)
    middle = tokens + mm(mixed, proj_out, ((1,), (1,)))
    normed_two = norm_rows(middle, gain_two).astype(bf16)

    if custom:
        normed_all, normed_other, grad_out_all, grad_out_other, first_other, mixed_other = gather_rows(
            normed_two, grad_pieces, normed, mixed
        )
    else:
        normed_all = lax.all_gather(normed_two, "fsdp", axis=0, tiled=True)
        grad_out_all = lax.all_gather(grad_out_late, "fsdp", axis=0, tiled=True)
    w_gate, w_up, w_down = mlp_w[:, :ff_part], mlp_w[:, ff_part : 2 * ff_part], mlp_w[:, 2 * ff_part :]
    if custom:
        hidden, hidden_other, grad_pair, pair_other, grad_normed_part = feed_forward(
            normed_all, grad_out_all, mlp_w
        )
    else:
        gate = mm(normed_all, w_gate, ((1,), (0,)))
        up_val = mm(normed_all, w_up, ((1,), (0,)))
        gelu_gate, gelu_slope = gelu_parts(gate)
        hidden = (gelu_gate * up_val).astype(bf16)
        grad_hidden = mm(grad_out_all, w_down, ((1,), (0,)))
        grad_gate = (grad_hidden * up_val * gelu_slope).astype(bf16)
        grad_up = (grad_hidden * gelu_gate).astype(bf16)
        grad_normed_part = (
            mm(grad_gate, w_gate, ((1,), (1,))) + mm(grad_up, w_up, ((1,), (1,)))
        ).astype(bf16)
    grad_normed_two = lax.psum_scatter(grad_normed_part, "fsdp", scatter_dimension=0, tiled=True)
    if custom:
        half = model // 16
        beside_high, across_low, mine, beside_low, across_high, out_part = shared_products(
            (normed_all, normed_other, grad_out_all, grad_out_other),
            mlp_w,
            (grad_pair, pair_other),
            (hidden, hidden_other),
        )
        from_beside_high, from_across_low = swap_beside(beside_high), swap_across(across_low)
    else:
        grad_pair = jnp.concatenate([grad_gate, grad_up], axis=1)
        term_pair = mm(normed_all, grad_pair, ((0,), (0,))).astype(bf16)
        term_down = mm(grad_out_all, hidden, ((0,), (0,))).astype(bf16)
        pair_sum = lax.psum_scatter(term_pair, "seq", scatter_dimension=0, tiled=True)
        down_sum = lax.psum_scatter(term_down, "seq", scatter_dimension=0, tiled=True)
        mlp_sum = jnp.concatenate([pair_sum, down_sum], axis=1)
        out_part = mm(hidden, w_down, ((1,), (1,))).astype(bf16)
    out_sum = lax.psum_scatter(out_part, "fsdp", scatter_dimension=0, tiled=True)
    grad_normed_two = grad_normed_two.astype(f32)

    grad_middle = grad_out.astype(f32) + norm_back(middle, gain_two, grad_normed_two)
    grad_mix = grad_middle.astype(bf16)
    if custom:
        mix_other = swap_cores(grad_mix)
    grad_mixed = mm(grad_mix, proj_out, ((1,), (0,)))
    carried_rows = jnp.broadcast_to(carried[None], (8, lru))
    grad_gelu_pre, rev_cum, rev_grad, pair_grad = call_heads(
        mixer_backward_scan,
        width,
        heads,
        [(a, None) for a in (grad_mixed, gelu_pre, rate_pre, cum, local, carried_rows, small)],
        [(tok_count, bf16, False), (tok_count, f32, False), (tok_count, f32, False), (8, f32, False)],
        [tok_count + 8],
        "mixer_backward_scan",
    )
    if custom:
        from_beside_high, from_across_low, pair_grad = lax.optimization_barrier(
            (from_beside_high, from_across_low, pair_grad)
        )
    if custom:
        gelu_other = swap_cores(grad_gelu_pre)
    incoming = prefix((cum[-1], pair_grad[0]), "seq", True)
    if custom:
        beside_low, across_high, incoming = lax.optimization_barrier((beside_low, across_high, incoming))
        from_beside_low, from_across_high = swap_beside(beside_low), swap_across(across_high)
    incoming_rows = jnp.broadcast_to(incoming[None], (8, lru))
    own, head, rate_w_grad, input_w_grad, sums = call_heads(
        mixer_backward,
        width,
        heads,
        [
            (a, None)
            for a in (rev_cum, rev_grad, incoming_rows, cum, local, carried_rows, rate_pre, input_pre, conv, branch, prior, small)
        ]
        + [(mixer_w, 0), (mixer_w, 1)],
        [(tok_count, f32, False), (8, f32, False), (0, bf16, True), (0, bf16, True), (8, f32, False)],
        [tok_count + 8, tok_count + 16],
        "mixer_backward",
    )
    received = from_behind(head[8 - margin :], "seq", -1)
    grad_branch = jnp.concatenate(
        [own[: tok_count - margin], own[tok_count - margin :] + received], axis=0
    ).astype(bf16)
    grad_both = jnp.concatenate([grad_branch, grad_gelu_pre], axis=1)
    vectors = jnp.pad(sums.T, ((0, 0), (0, 128 - sums.shape[0]))).astype(bf16)
    rest = jnp.concatenate([rate_w_grad, input_w_grad, vectors], axis=1)
    if custom:
        low, high = [
            sum(part.astype(f32) for part in parts).astype(bf16)
            for parts in (
                (mine[:half], from_across_low, from_beside_low),
                (mine[half:], from_across_high, from_beside_high),
            )
        ]
        mixer_sum, mlp_back, input_grad = scatter(
            (normed, first_other, grad_mix, mix_other, mixed, mixed_other, grad_gelu_pre, gelu_other),
            grad_branch, rest, low, high, mixer_w, block_input[0], small,
        )
    else:
        mixer_sum, mlp_back = scatter_plain(normed, grad_both, grad_mix, mixed, rest, mlp_sum)
        grad_normed = mm(grad_both, wide, ((1,), (1,)))
        input_grad = (grad_middle + norm_back(tokens, gain_one, grad_normed)).astype(bf16)
    input_grad = input_grad[None]
    middle = lax.optimization_barrier((middle, mixer_sum))[0]
    block_output = (middle + out_sum.astype(f32)).astype(bf16)[None]
    edge = 3 * lru + 2 * width
    vec = mixer_sum[:, edge:].astype(f32).T
    weight_grads = list(
        jnp.split(mixer_sum[:, :edge].astype(f32), [lru, 2 * lru, 3 * lru, 3 * lru + width], axis=1)
    ) + [mlp_back[m].astype(f32) for m in range(3)]
    first_total = gain_back((branch_proj, weight_grads[0]), (gelu_proj, weight_grads[1]))
    second_total = gain_back((gate_proj, weight_grads[5]), (up_proj, weight_grads[6]))
    dbranch, dgelu, dout, drate, dinput, dgate, dup, ddown = weight_grads
    return (
        block_output,
        input_grad,
        first_total / mixer_gain.astype(f32),
        dbranch,
        dgelu,
        vec[: margin + 1],
        vec[7],
        drate,
        dinput,
        vec[4],
        vec[5],
        vec[6],
        dout,
        second_total / mlp_gain.astype(f32),
        dgate,
        dup,
        ddown,
    )


def solution(mesh):
    tokens = P("fsdp", "seq", None)
    vector = P(both)
    matrix = P(both, None)
    taps = P(None, both)
    return jax.shard_map(
        on_device,
        mesh=mesh,
        in_specs=(
            tokens, tokens, vector, matrix, matrix, taps, vector, matrix, matrix,
            vector, vector, vector, matrix, vector, matrix, matrix, matrix,
        ),
        out_specs=(
            tokens, tokens, vector, matrix, matrix, taps, vector, matrix, matrix,
            vector, vector, vector, matrix, vector, matrix, matrix, matrix,
        ),
        check_vma=False,
    )
```

```python
import functools

import jax
import jax.numpy as jnp
from jax import lax
from jax.experimental import pallas as pl
from jax.experimental.pallas import tpu as pltpu
from jax.sharding import PartitionSpec as P

epsilon = 1e-06
f32 = jnp.float32
bf16 = jnp.bfloat16
both = ("seq", "fsdp")
MESH = pl.DeviceIdType.MESH
TAP, CONV_BIAS, RATE_BIAS, INPUT_BIAS, SOFT, SOFT_SLOPE, GAIN_ONE, GAIN_TWO = 0, 4, 5, 6, 7, 8, 9, 10
GELU_C = 0.7978845608028654
GELU_A = 0.044715


def from_behind(shard, axis, by):
    devices = lax.axis_size(axis)
    pairs = [(i, i + by) for i in range(devices) if 0 <= i + by < devices]
    return lax.ppermute(shard, axis, pairs)


def prefix(part, axis, reverse):
    count = lax.axis_size(axis)
    place = lax.axis_index(axis)
    gathered = lax.all_gather(jnp.stack(part), axis)
    state = jnp.zeros_like(part[1])
    for hop in range(count):
        source = count - 1 - hop if reverse else hop
        ahead = source > place if reverse else source < place
        state = jnp.where(ahead, gathered[source, 1] + gathered[source, 0] * state, state)
    return state


def norm_rows(values, scales):
    return values * lax.rsqrt(jnp.mean(values * values, axis=-1, keepdims=True) + epsilon) * scales


def norm_back(values, scales, grads):
    inverse = lax.rsqrt(jnp.mean(values * values, axis=-1, keepdims=True) + epsilon)
    scaled = grads * scales
    shared = jnp.mean(values * scaled, axis=-1, keepdims=True)
    return inverse * scaled - values * (inverse * inverse * inverse * shared)


def gain_back(*pairs):
    return sum(jnp.sum(weight.astype(f32) * grad, axis=1) for weight, grad in pairs)


def gelu_parts(x):
    inner = jnp.tanh(GELU_C * (x + GELU_A * x * x * x))
    return 0.5 * x * (1.0 + inner), 0.5 * (1.0 + inner) + 0.5 * x * (1.0 - inner * inner) * (
        GELU_C * (1.0 + 3.0 * GELU_A * x * x)
    )


def mm(left, right, dims):
    return lax.dot_general(left, right, (dims, ((), ())), preferred_element_type=f32)


def sigmoid(x):
    return 1.0 / (1.0 + jnp.exp(-x))


def scan_rows(decay, value, reverse):
    rows = decay.shape[0]
    place = lax.broadcasted_iota(jnp.int32, decay.shape, 0)
    step = 1
    while step < rows:
        shift = rows - step if reverse else step
        inside = place < rows - step if reverse else place >= step
        before_value = jnp.where(inside, pltpu.roll(value, shift, 0), 0.0)
        before_decay = jnp.where(inside, pltpu.roll(decay, shift, 0), 1.0)
        value = value + decay * before_value
        decay = decay * before_decay
        step *= 2
    return decay, value


def gates(rate_pre, input_pre, soft):
    rate = sigmoid(rate_pre)
    log_decay = -8.0 * rate * soft
    decay = jnp.exp(log_decay)
    square = decay * decay
    root = jnp.sqrt(-jnp.tanh(log_decay) * (1.0 + square))
    return rate, decay, square, root, sigmoid(input_pre)


def table_kernel(columns, table):
    rows = columns[...].T[0:16, :].astype(f32)
    decay_param = rows[7:8, :]
    fast = jnp.exp(-decay_param)
    table[0:7, :] = rows[0:7, :]
    table[7:8, :] = jnp.log1p(fast)
    table[8:9, :] = -fast / (1.0 + fast)
    table[9:11, :] = rows[8:10, :]
    table[11:16, :] = jnp.zeros((5, rows.shape[1]), f32)


def small_table(mixer_w, block):
    model = mixer_w.shape[0]
    return pl.pallas_call(
        table_kernel,
        grid=(1,),
        in_specs=[pl.BlockSpec((model, 128), lambda i: (0, block))],
        out_specs=pl.BlockSpec((16, model), lambda i: (0, 0)),
        out_shape=jax.ShapeDtypeStruct((16, model), f32),
        name="small_table",
    )(mixer_w)


def mixer_in_kernel(tokens, table, weights, normed, branch, gelu_pre):
    step = pl.program_id(0)

    @pl.when(step == 0)
    def _():
        normed[...] = norm_rows(tokens[...].astype(f32), table[GAIN_ONE : GAIN_ONE + 1, :]).astype(bf16)

    product = mm(normed[...], weights[...], ((1,), (0,)))
    half = pl.num_programs(0) // 2

    @pl.when(step < half)
    def _():
        branch[...] = product.astype(bf16)

    @pl.when(step >= half)
    def _():
        gelu_pre[...] = product


def mixer_in(tokens, table, mixer_w, lru, start):
    tok, model = tokens.shape
    tile = start
    tiles = lru // tile
    return pl.pallas_call(
        mixer_in_kernel,
        grid=(2 * tiles,),
        in_specs=[
            pl.BlockSpec((tok, model), lambda j: (0, 0)),
            pl.BlockSpec(table.shape, lambda j: (0, 0)),
            pl.BlockSpec((model, tile), lambda j: (0, 1 + j)),
        ],
        out_specs=[
            pl.BlockSpec((tok, model), lambda j: (0, 0)),
            pl.BlockSpec((tok, tile), lambda j: (0, jnp.minimum(j, tiles - 1))),
            pl.BlockSpec((tok, tile), lambda j: (0, jnp.maximum(j - tiles, 0))),
        ],
        out_shape=[
            jax.ShapeDtypeStruct((tok, model), bf16),
            jax.ShapeDtypeStruct((tok, lru), bf16),
            jax.ShapeDtypeStruct((tok, lru), f32),
        ],
        compiler_params=pltpu.CompilerParams(vmem_limit_bytes=16 * 1024 * 1024),
        cost_estimate=pl.CostEstimate(flops=1, bytes_accessed=1, transcendentals=0),
        name="mixer_in",
    )(tokens, table, mixer_w)


def mixer_forward(branch, prior, small, rate_w, input_w, conv, rate_pre, input_pre, cum, local, ext):
    rows = branch.shape[0]
    ext[0:8, :] = prior[...]
    ext[8:, :] = branch[...].astype(f32)
    total = small[CONV_BIAS : CONV_BIAS + 1, :] + small[TAP : TAP + 1, :] * ext[8:, :]
    for offset in range(1, 4):
        total = total + small[TAP + offset : TAP + offset + 1, :] * ext[pl.ds(8 - offset, rows), :]
    low = total.astype(bf16)
    conv[...] = low
    rate = mm(low, rate_w[...], ((1,), (0,))) + small[RATE_BIAS : RATE_BIAS + 1, :]
    inp = mm(low, input_w[...], ((1,), (0,))) + small[INPUT_BIAS : INPUT_BIAS + 1, :]
    rate_pre[...] = rate
    input_pre[...] = inp
    _, decay, _, root, opened = gates(rate, inp, small[SOFT : SOFT + 1, :])
    product, states = scan_rows(decay, root * opened * low.astype(f32), False)
    cum[...] = product
    local[...] = states


def mixer_backward_scan(grad_mixed, gelu_pre, rate_pre, cum, local, carried, small, grad_pre, rev_cum, rev_grad, pair, ext):
    rows = grad_mixed.shape[0]
    states = local[...] + cum[...] * carried[0:1, :]
    value, slope = gelu_parts(gelu_pre[...])
    grad = grad_mixed[...]
    grad_pre[...] = (grad * states * slope).astype(bf16)
    decay = jnp.exp(-8.0 * sigmoid(rate_pre[...]) * small[SOFT : SOFT + 1, :])
    ext[0:rows, :] = decay
    ext[rows:, :] = jnp.ones((8, decay.shape[1]), f32)
    product, back = scan_rows(ext[pl.ds(1, rows), :], grad * value, True)
    rev_cum[...] = product
    rev_grad[...] = back
    pair[...] = jnp.broadcast_to(decay[0:1, :] * back[0:1, :], pair.shape)


def mixer_backward(
    rev_cum, rev_grad, incoming, cum, local, carried, rate_pre, input_pre, conv, branch, prior, small, rate_w, input_w,
    own, head, rate_w_grad, input_w_grad, sums, ext, gext,
):
    rows = rev_cum.shape[0]
    soft = small[SOFT : SOFT + 1, :]
    grad_states = rev_grad[...] + rev_cum[...] * incoming[0:1, :]
    rate, decay, square, root, opened = gates(rate_pre[...], input_pre[...], soft)
    ext[0:8, :] = jnp.broadcast_to(carried[0:1, :], (8, carried.shape[1]))
    ext[8:, :] = local[...] + cum[...] * carried[0:1, :]
    before = ext[pl.ds(7, rows), :]
    low = conv[...]
    conv_in = low.astype(f32)
    grad_log = grad_states * decay * before - grad_states * opened * conv_in * square / root
    driven = grad_states * root
    grad_input = (driven * conv_in * opened * (1.0 - opened)).astype(bf16)
    by_rate = grad_log * (-8.0 * rate)
    grad_rate = (by_rate * soft * (1.0 - rate)).astype(bf16)
    sums[6:7, :] = jnp.sum(by_rate, axis=0, keepdims=True) * small[SOFT_SLOPE : SOFT_SLOPE + 1, :]
    sums[4:5, :] = jnp.sum(grad_rate.astype(f32), axis=0, keepdims=True)
    sums[5:6, :] = jnp.sum(grad_input.astype(f32), axis=0, keepdims=True)
    rate_w_grad[...] = mm(low, grad_rate, ((0,), (0,))).astype(rate_w_grad.dtype)
    input_w_grad[...] = mm(low, grad_input, ((0,), (0,))).astype(input_w_grad.dtype)
    grad_conv = (
        driven * opened
        + mm(grad_rate, rate_w[...], ((1,), (1,)))
        + mm(grad_input, input_w[...], ((1,), (1,)))
    )
    sums[7:8, :] = jnp.sum(grad_conv, axis=0, keepdims=True)
    ext[0:8, :] = prior[...]
    ext[8:, :] = branch[...].astype(f32)
    gext[0:8, :] = jnp.zeros((8, grad_conv.shape[1]), f32)
    gext[8 : 8 + rows, :] = grad_conv
    gext[8 + rows :, :] = jnp.zeros((8, grad_conv.shape[1]), f32)
    back = jnp.zeros_like(grad_conv)
    front = jnp.zeros((8, grad_conv.shape[1]), f32)
    for offset in range(4):
        tap = small[TAP + offset : TAP + offset + 1, :]
        sums[offset : offset + 1, :] = jnp.sum(
            grad_conv * ext[pl.ds(8 - offset, rows), :], axis=0, keepdims=True
        )
        back = back + tap * gext[pl.ds(8 + offset, rows), :]
        front = front + tap * gext[pl.ds(offset, 8), :]
    own[...] = back
    head[...] = front


def places():
    s = lax.axis_index("seq")
    z = lax.axis_index("fsdp")
    core = s + 1 - 2 * (s % 2)
    beside = s + 2 - 4 * ((s // 2) % 2)
    across = s + 4 - 8 * (s // 4)
    return s, z, core, beside, across


def greet(peers):
    barrier = pltpu.get_barrier_semaphore()
    for peer in peers:
        pl.semaphore_signal(barrier, inc=1, device_id=peer, device_id_type=MESH)
    pl.semaphore_wait(barrier, len(peers))


def gather_kernel(
    first, branch, gelu, outer, gate, up, down, mixer_all, mlp_mine,
    mixer, load_sem, flow_send, flow_recv, line_send, line_recv, swap_send, swap_recv, own_sem,
):
    s, z, core, beside, across = places()
    rows, cols = mixer.shape
    ff_part = mlp_mine.shape[1] // 3
    cut = cols // 256 * 128
    diag = beside + across - s
    loads, start = [], 0
    for n, part in enumerate((first, branch, gelu, outer)):
        size = part.shape[1]
        loads.append(pltpu.make_async_copy(part, mixer.at[:, pl.ds(start, size)], load_sem.at[n]))
        loads[-1].start()
        start += size
    greet([(core, z), (beside, z), (across, z)] + [(s, (z + k) % 4) for k in range(1, 4)])

    def remote(src, dst, send, recv, target):
        return pltpu.make_async_remote_copy(
            src_ref=src, dst_ref=dst, send_sem=send, recv_sem=recv, device_id=target, device_id_type=MESH
        )

    def piece(seq, zz, half=None):
        span = pl.ds(pl.multiple_of((seq * 4 + zz) * rows, 16), rows)
        if half is None:
            return mixer_all.at[span, :]
        return mixer_all.at[span, pl.ds(0, cut) if half == 0 else pl.ds(cut, cols - cut)]

    def flow(zz, index, seq, half, target, src=None):
        ref = piece(seq, zz, half)
        return remote(
            ref if src is None else src, ref, flow_send.at[zz, index], flow_recv.at[zz, index], (target, z)
        )

    def sends(zz, src=None):
        return [
            flow(zz, 0, s, None, beside, src),
            flow(zz, 1, s, None, across, src),
            flow(zz, 4, s, None, core, src),
        ]

    def spread(zz, src=None):
        for copy in sends(zz, src):
            copy.start()

    def relay(zz):
        flow(zz, 0, beside, None, beside).wait_recv()
        flow(zz, 3, beside, 0, across).start()
        flow(zz, 5, beside, None, core).start()
        flow(zz, 1, across, None, across).wait_recv()
        flow(zz, 2, across, 1, beside).start()
        flow(zz, 6, across, None, core).start()

    def finish(zz):
        flow(zz, 3, diag, 0, across).wait_recv()
        flow(zz, 7, diag, 0, core).start()
        flow(zz, 2, diag, 1, beside).wait_recv()
        flow(zz, 8, diag, 1, core).start()

    def drain(zz, src=None):
        for copy in sends(zz, src):
            copy.wait_send()
        flow(zz, 3, beside, 0, across).wait_send()
        flow(zz, 5, beside, None, core).wait_send()
        flow(zz, 2, across, 1, beside).wait_send()
        flow(zz, 6, across, None, core).wait_send()
        flow(zz, 7, diag, 0, core).wait_send()
        flow(zz, 8, diag, 1, core).wait_send()
        flip = core - s
        flow(zz, 4, core, None, core).wait_recv()
        flow(zz, 5, beside + flip, None, core).wait_recv()
        flow(zz, 6, across + flip, None, core).wait_recv()
        flow(zz, 7, diag + flip, 0, core).wait_recv()
        flow(zz, 8, diag + flip, 1, core).wait_recv()

    def line(zz, up_way, hop, src=None):
        ref = piece(s, zz)
        way = 0 if up_way else 1
        target = z + 1 if up_way else z - 1
        return remote(
            ref if src is None else src, ref, line_send.at[way, hop], line_recv.at[way, hop], (s, target)
        )

    def line_hop(hop):
        def below():
            line(z - hop, True, hop - 1).wait_recv()
            pl.when(z < 3)(lambda: line(z - hop, True, hop).start())

        def above():
            line(z + hop, False, hop - 1).wait_recv()
            pl.when(z > 0)(lambda: line(z + hop, False, hop).start())

        pl.when(z >= hop)(below)
        pl.when(z + hop <= 3)(above)

    def at_hop(hop, act):
        pl.when(z >= hop)(lambda: act(z - hop))
        pl.when(z + hop <= 3)(lambda: act(z + hop))

    def landing(m, zz):
        return mlp_mine.at[pl.ds(pl.multiple_of(zz * rows, 16), rows), pl.ds(m * ff_part, ff_part)]

    def columns(m, zz):
        return (gate, up, down)[m].at[:, pl.ds(pl.multiple_of(zz * ff_part, 128), ff_part)]

    def swap(k, m, arriving=False):
        to = (z + k) % 4
        came = (z + 4 - k) % 4
        return remote(
            columns(m, to), landing(m, came if arriving else z), swap_send.at[k - 1, m], swap_recv.at[k - 1, m], (s, to)
        )

    local = [pltpu.make_async_copy(columns(m, z), landing(m, z), own_sem.at[m]) for m in range(3)]
    local.append(pltpu.make_async_copy(mixer, piece(s, z), own_sem.at[3]))
    for copy in loads:
        copy.wait()

    pl.when(z < 3)(lambda: line(z, True, 0, mixer).start())
    pl.when(z > 0)(lambda: line(z, False, 0, mixer).start())
    spread(z, mixer)
    for copy in local:
        copy.start()
    line_hop(1)
    at_hop(1, spread)
    relay(z)
    line_hop(2)
    at_hop(2, spread)
    finish(z)
    at_hop(1, relay)
    line_hop(3)
    at_hop(3, spread)
    for k in (1, 3, 2):
        for m in range(3):
            swap(k, m).start()
    at_hop(1, finish)
    at_hop(2, relay)
    at_hop(3, relay)
    at_hop(2, finish)
    at_hop(3, finish)
    drain(z, mixer)
    for hop in range(1, 4):
        at_hop(hop, drain)
    for copy in local:
        copy.wait()
    for k in (1, 3, 2):
        for m in range(3):
            swap(k, m).wait_send()
            swap(k, m, True).wait_recv()
    pl.when(z < 3)(lambda: line(z, True, 0, mixer).wait_send())
    pl.when(z > 0)(lambda: line(z, False, 0, mixer).wait_send())
    for hop in range(1, 3):
        pl.when((z >= hop) & (z < 3))(lambda: line(z - hop, True, hop).wait_send())
        pl.when((z + hop <= 3) & (z > 0))(lambda: line(z + hop, False, hop).wait_send())


def gather(first, branch, gelu, outer, gate, up, down):
    rows = first.shape[0]
    cols = first.shape[1] + branch.shape[1] + gelu.shape[1] + outer.shape[1]
    ff_part = gate.shape[1] // 4
    anyspec = pl.BlockSpec(memory_space=pl.ANY)
    dma = pltpu.SemaphoreType.DMA
    return pl.pallas_call(
        gather_kernel,
        in_specs=[anyspec] * 7,
        out_specs=[anyspec] * 2,
        out_shape=[
            jax.ShapeDtypeStruct((32 * rows, cols), bf16),
            jax.ShapeDtypeStruct((4 * rows, 3 * ff_part), bf16),
        ],
        scratch_shapes=[
            pltpu.VMEM((rows, cols), bf16), dma((4,)),
            dma((4, 9)), dma((4, 9)), dma((2, 3)), dma((2, 3)), dma((3, 3)), dma((3, 3)), dma((4,)),
        ],
        compiler_params=pltpu.CompilerParams(collective_id=1, has_side_effects=True),
        name="gather_weights",
    )(first, branch, gelu, outer, gate, up, down)


def rows_kernel(
    normed, grad0, grad1, grad2, grad3, first, mixed, normed_all, normed_other, grad_all, grad_other,
    first_other, mixed_other, line_send, line_recv, core_send, core_recv, own_sem, held, give_send, give_recv,
):
    s, z, core, _, _ = places()
    tok = normed.shape[0]
    cuts = 4
    grads = (grad0, grad1, grad2, grad3)
    greet([(core, z)] + [(s, (z + k) % 4) for k in range(1, 4)])

    def rows(ref, zz):
        return ref.at[pl.ds(pl.multiple_of(zz * tok, 16), tok), :]

    def remote(src, dst, send, recv, target):
        return pltpu.make_async_remote_copy(
            src_ref=src, dst_ref=dst, send_sem=send, recv_sem=recv, device_id=target, device_id_type=MESH
        )

    def parts(ref):
        size = tok // cuts
        return [ref.at[pl.ds(n * size, size), :] for n in range(cuts)]

    def line(zz, up_way, hop):
        way = 0 if up_way else 1
        target = z + 1 if up_way else z - 1
        src = normed if hop == 0 else rows(normed_all, zz)
        dst = rows(normed_all, zz)
        return [
            remote(a, b, line_send.at[way, hop, n], line_recv.at[way, hop, n], (s, target))
            for n, (a, b) in enumerate(zip(parts(src), parts(dst)))
        ]

    def over(zz, own=False):
        src = normed if own else rows(normed_all, zz)
        return remote(src, rows(normed_other, zz), core_send.at[0, zz], core_recv.at[0, zz], (core, z))

    def grad_over(k):
        zz = (z + 4 - k) % 4
        return remote(grads[k], rows(grad_other, zz), core_send.at[1, zz], core_recv.at[1, zz], (core, z))

    def line_start(zz, up_way, hop):
        for copy in line(zz, up_way, hop):
            copy.start()

    def line_drain(zz, up_way, hop):
        for copy in line(zz, up_way, hop):
            copy.wait_send()

    def hop_step(hop):
        def below():
            for came, on in zip(line(z - hop, True, hop - 1), line(z - hop, True, hop) if hop < 3 else [None] * cuts):
                came.wait_recv()
                if on is not None:
                    pl.when(z < 3)(on.start)
            over(z - hop).start()

        def above():
            for came, on in zip(line(z + hop, False, hop - 1), line(z + hop, False, hop) if hop < 3 else [None] * cuts):
                came.wait_recv()
                if on is not None:
                    pl.when(z > 0)(on.start)
            over(z + hop).start()

        pl.when(z >= hop)(below)
        pl.when(z + hop <= 3)(above)

    given = [
        remote(source, target, give_send.at[n], give_recv.at[n], (core, z))
        for n, (source, target) in enumerate(((first, first_other), (mixed, mixed_other)))
    ]
    local = [pltpu.make_async_copy(grads[k], held.at[k], own_sem.at[k]) for k in range(4)]
    local.append(pltpu.make_async_copy(normed, held.at[4], own_sem.at[4]))
    stored = [
        pltpu.make_async_copy(held.at[k], rows(grad_all, (z + 4 - k) % 4), own_sem.at[k]) for k in range(4)
    ]
    stored.append(pltpu.make_async_copy(held.at[4], rows(normed_all, z), own_sem.at[4]))
    pl.when(z < 3)(lambda: line_start(z, True, 0))
    pl.when(z > 0)(lambda: line_start(z, False, 0))
    over(z, True).start()
    for copy in local:
        copy.start()
    for k in range(4):
        grad_over(k).start()
    for copy in given:
        copy.start()
    for copy, store in zip(local, stored):
        copy.wait()
        store.start()
    for hop in range(1, 4):
        hop_step(hop)
    for copy in stored:
        copy.wait()
    for k in range(4):
        grad_over(k).wait()
    for copy in given:
        copy.wait()
    over(z, True).wait()
    for k in range(1, 4):
        over((z + k) % 4).wait()
    pl.when(z < 3)(lambda: line_drain(z, True, 0))
    pl.when(z > 0)(lambda: line_drain(z, False, 0))
    for hop in range(1, 3):
        pl.when((z >= hop) & (z < 3))(lambda: line_drain(z - hop, True, hop))
        pl.when((z + hop <= 3) & (z > 0))(lambda: line_drain(z + hop, False, hop))


def gather_rows(normed, grads, first, mixed):
    tok, model = normed.shape
    anyspec = pl.BlockSpec(memory_space=pl.ANY)
    dma = pltpu.SemaphoreType.DMA
    return pl.pallas_call(
        rows_kernel,
        in_specs=[anyspec] * 7,
        out_specs=[anyspec] * 6,
        out_shape=[jax.ShapeDtypeStruct((4 * tok, model), bf16)] * 4
        + [jax.ShapeDtypeStruct(first.shape, bf16), jax.ShapeDtypeStruct(mixed.shape, bf16)],
        scratch_shapes=[
            dma((2, 3, 4)), dma((2, 3, 4)), dma((2, 4)), dma((2, 4)), dma((5,)),
            pltpu.VMEM((5, tok, model), bf16), dma((2,)), dma((2,)),
        ],
        compiler_params=pltpu.CompilerParams(collective_id=3, has_side_effects=True),
        name="gather_rows",
    )(normed, *grads, first, mixed)


def column_tiles(cols, size=512):
    return [(start, min(size, cols - start)) for start in range(0, cols, size)]


def feed_forward_kernel(
    normed, grad_out, weights, hidden, hidden_other, pair, pair_other, back,
    held, hidden_now, pair_now, sems, store_sem, core_send, core_recv,
):
    s, z, core, _, _ = places()
    step = pl.program_id(0)
    ff_part = held.shape[2]
    model = held.shape[1]
    rows = normed.shape[0]
    tiles = column_tiles(ff_part)
    made = ((hidden_now, hidden, hidden_other), (pair_now, pair, pair_other))

    def load(n, m):
        start, size = tiles[n]
        return pltpu.make_async_copy(
            weights.at[:, pl.ds(m * ff_part + start, size)], held.at[m, :, pl.ds(start, size)], sems.at[n, m]
        )

    def kept(n, turn):
        now, mine, _ = made[n]
        return pltpu.make_async_copy(now.at[turn], mine.at[pl.ds(turn * rows, rows), :], store_sem.at[turn, n])

    def handed(n, turn):
        now, _, other = made[n]
        return pltpu.make_async_remote_copy(
            src_ref=now.at[turn],
            dst_ref=other.at[pl.ds(turn * rows, rows), :],
            send_sem=core_send.at[turn, n],
            recv_sem=core_recv.at[turn, n],
            device_id=(core, z),
            device_id_type=MESH,
        )

    @pl.when(step == 0)
    def _():
        for n in range(len(tiles)):
            for m in range(3):
                load(n, m).start()
        greet([(core, z)])

    for n, (start, size) in enumerate(tiles):
        cols = slice(start, start + size)

        @pl.when(step == 0)
        def _(n=n):
            for m in range(3):
                load(n, m).wait()

        gate = mm(normed[...], held[0, :, cols], ((1,), (0,)))
        value, slope = gelu_parts(gate)
        up = mm(normed[...], held[1, :, cols], ((1,), (0,)))
        hidden_now[step, :, cols] = (value * up).astype(bf16)
        grad_hidden = mm(grad_out[...], held[2, :, cols], ((1,), (0,)))
        pair_now[step, :, cols] = (grad_hidden * up * slope).astype(bf16)
        pair_now[step, :, slice(ff_part + start, ff_part + start + size)] = (grad_hidden * value).astype(bf16)

    for turn in range(2):

        @pl.when(step == turn)
        def _(turn=turn):
            for n in range(2):
                handed(n, turn).start()
                kept(n, turn).start()

    def back_tile(turn, carry):
        cols = pl.ds(pl.multiple_of(turn * 512, 512), 512)
        total = mm(pair_now[step, :, :ff_part], held[0, cols, :], ((1,), (1,)))
        total = total + mm(pair_now[step, :, ff_part:], held[1, cols, :], ((1,), (1,)))
        back[:, cols] = total.astype(bf16)
        return carry

    lax.fori_loop(0, model // 512, back_tile, 0)

    @pl.when(step == 1)
    def _():
        for turn in range(2):
            for n in range(2):
                kept(n, turn).wait()
                handed(n, turn).wait()


def feed_forward(normed, grad_out, weights):
    tok, model = normed.shape
    ff_part = weights.shape[1] // 3
    rows = tok // 2
    anyspec = pl.BlockSpec(memory_space=pl.ANY)
    dma = pltpu.SemaphoreType.DMA
    block = pl.BlockSpec((rows, model), lambda i: (i, 0))
    return pl.pallas_call(
        feed_forward_kernel,
        grid=(2,),
        in_specs=[block, block, anyspec],
        out_specs=[anyspec] * 4 + [block],
        out_shape=[
            jax.ShapeDtypeStruct((tok, cols), bf16)
            for cols in (ff_part, ff_part, 2 * ff_part, 2 * ff_part, model)
        ],
        scratch_shapes=[
            pltpu.VMEM((3, model, ff_part), bf16),
            pltpu.VMEM((2, rows, ff_part), bf16),
            pltpu.VMEM((2, rows, 2 * ff_part), bf16),
            dma((len(column_tiles(ff_part)), 3)), dma((2, 2)), dma((2, 2)), dma((2, 2)),
        ],
        compiler_params=pltpu.CompilerParams(
            collective_id=4, has_side_effects=True, vmem_limit_bytes=60 * 1024 * 1024
        ),
        name="feed_forward",
    )(normed, grad_out, weights)


def add_columns(target, sources, start, size, step):
    def one(turn, carry):
        cols = pl.ds(pl.multiple_of(start + turn * step, 128), step)
        total = target[:, cols].astype(f32)
        for source in sources:
            total = total + source[:, cols].astype(f32)
        target[:, cols] = total.astype(target.dtype)
        return carry

    lax.fori_loop(0, size // step, one, 0)


def shared_products_kernel(
    normed, normed_other, grad, grad_other, weights, pair, pair_other, hidden, hidden_other,
    beside_high, across_low, mine, beside_low, across_high, out,
    turned, slots, stage, right, diag, landed, waiting, down_now, out_now,
    load_sem, right_sem, send_sem, recv_sem, store_sem, down_sem, out_sem,
):
    s, z, _, beside, across = places()
    step = pl.program_id(0)
    lefts = ((normed, normed_other), (grad, grad_other))
    chip_cols = normed.shape[1] // 4
    half = chip_cols // 2
    piece = half // 2
    width = hidden.shape[1]
    tok = normed.shape[0]
    diagonal = beside + across - s
    chips = [q // 2 for q in (diagonal, beside, across, s)]

    def load(side, q, who):
        cols = pl.ds(pl.multiple_of(chips[q] * chip_cols, 128), chip_cols)
        return pltpu.make_async_copy(lefts[side][who].at[:, cols], slots.at[q % 2, who], load_sem.at[q % 2, who])

    def fetch(side):
        for q in range(2):
            for who in range(2):
                load(side, q, who).start()

    def turn(side):
        for q in range(4):
            for who in range(2):
                load(side, q, who).wait()
                stage[...] = slots[q % 2, who].T
                turned[q * half : (q + 1) * half, who * tok : (who + 1) * tok] = stage[
                    pl.ds(pl.multiple_of(s % 2 * half, 16), half), :
                ]
                if q < 2:
                    load(side, q + 2, who).start()

    def take(j):
        sources = (hidden, hidden_other) if j == 2 else (pair, pair_other)
        return [
            pltpu.make_async_copy(
                source.at[:, pl.ds(0 if j == 2 else j * width, width)],
                right.at[j % 2, pl.ds(who * tok, tok), :],
                right_sem.at[j % 2, who],
            )
            for who, source in enumerate(sources)
        ]

    def take_start(j):
        for copy in take(j):
            copy.start()

    def take_wait(j):
        for copy in take(j):
            copy.wait()

    def tile(start, size):
        cols = pl.ds(start, size)
        block = mm(turned[...], right[step % 2, :, cols], ((1,), (0,))).astype(bf16)
        parts = [block[n * piece : (n + 1) * piece] for n in range(8)]
        there = pl.ds(pl.multiple_of(step * width + start, 128), size)
        diag[0, :, there] = parts[0]
        diag[1, :, there] = parts[1]
        waiting[0, :, there] = parts[2]
        beside_high[:, cols] = parts[3]
        across_low[:, cols] = parts[4]
        waiting[1, :, there] = parts[5]
        mine[0:piece, cols] = parts[6]
        mine[piece:, cols] = parts[7]

    def multiply():
        def one(turn, carry):
            tile(pl.multiple_of(turn * 512, 512), 512)
            return carry

        lax.fori_loop(0, width // 512, one, 0)
        if width % 512:
            tile(width // 512 * 512, width % 512)

    def push(way, j):
        cols = pl.ds(j * width, width)
        return pltpu.make_async_remote_copy(
            src_ref=diag.at[way, :, cols],
            dst_ref=landed.at[way, :, cols],
            send_sem=send_sem.at[way, j],
            recv_sem=recv_sem.at[way, j],
            device_id=(across if way == 0 else beside, z),
            device_id_type=MESH,
        )

    def store(way, j):
        cols = pl.ds(j * width, width)
        return pltpu.make_async_copy(
            waiting.at[way, :, cols], (beside_low, across_high)[way].at[:, cols], store_sem.at[way, j]
        )

    out_rows = down_now.shape[1]
    out_tiles = weights.shape[0] // out_rows

    def down(t):
        source = weights.at[pl.ds(t * out_rows, out_rows), pl.ds(2 * width, width)]
        return pltpu.make_async_copy(source, down_now.at[t % 2], down_sem.at[t % 2])

    def out_store(t):
        return pltpu.make_async_copy(
            out_now.at[t % 2], out.at[:, pl.ds(t * out_rows, out_rows)], out_sem.at[t % 2]
        )

    def out_product():
        for t in range(out_tiles):
            down(t).wait()
            if t > 1:
                out_store(t - 2).wait()
            out_now[t % 2] = mm(right[0, 0:tok, :], down_now[t % 2], ((1,), (1,))).astype(bf16)
            out_store(t).start()
            if t + 2 < out_tiles:
                down(t + 2).start()

    @pl.when(step == 0)
    def _():
        fetch(0)
        take_start(0)
        take_start(1)
        greet([(beside, z), (across, z)])
        turn(0)
        take_wait(0)

    @pl.when(step == 1)
    def _():
        take_wait(1)
        take_start(2)
        fetch(1)

    @pl.when(step == 2)
    def _():
        down(0).start()
        down(1).start()
        turn(1)
        take_wait(2)

    multiply()
    for j in range(3):

        @pl.when(step == j)
        def _(j=j):
            push(0, j).start()
            push(1, j).start()

    @pl.when(step == 2)
    def _():
        out_product()
        for j in range(3):
            for way in range(2):
                push(way, j).wait_recv()
                add_columns(waiting.at[way], [landed.at[way]], j * width, width, 384)
                store(way, j).start()
        for j in range(3):
            for way in range(2):
                push(way, j).wait_send()
                store(way, j).wait()
        for t in range(out_tiles - 2, out_tiles):
            out_store(t).wait()


def shared_products(lefts, weights, pair, hidden):
    tok, model = lefts[0].shape
    width = hidden[0].shape[1]
    half = model // 8
    anyspec = pl.BlockSpec(memory_space=pl.ANY)
    dma = pltpu.SemaphoreType.DMA

    def block(rows):
        return pl.BlockSpec((rows, width), lambda j: (0, j))

    rows_out = (half // 2, half // 2, half, half // 2, half // 2)
    return pl.pallas_call(
        shared_products_kernel,
        grid=(3,),
        in_specs=[anyspec] * 9,
        out_specs=[block(rows) for rows in rows_out[:3]] + [anyspec] * 3,
        out_shape=[jax.ShapeDtypeStruct((rows, 3 * width), bf16) for rows in rows_out]
        + [jax.ShapeDtypeStruct((tok, model), bf16)],
        scratch_shapes=[
            pltpu.VMEM((4 * half, 2 * tok), bf16),
            pltpu.VMEM((2, 2, tok, 2 * half), bf16),
            pltpu.VMEM((2 * half, tok), bf16),
            pltpu.VMEM((2, 2 * tok, width), bf16),
            pltpu.VMEM((2, half // 2, 3 * width), bf16),
            pltpu.VMEM((2, half // 2, 3 * width), bf16),
            pltpu.VMEM((2, half // 2, 3 * width), bf16),
            pltpu.VMEM((2, 512, width), bf16),
            pltpu.VMEM((2, tok, 512), bf16),
            dma((2, 2)), dma((2, 2)), dma((2, 3)), dma((2, 3)), dma((2, 3)), dma((2,)), dma((2,)),
        ],
        compiler_params=pltpu.CompilerParams(
            collective_id=5, has_side_effects=True, vmem_limit_bytes=60 * 1024 * 1024
        ),
        name="feed_forward_products",
    )(*lefts, weights, *pair, *hidden)


def scatter_kernel(
    normed, normed_other, grad_mix, mix_other, mixed, mixed_other, grad_gelu, gelu_other, grad_branch, rest,
    mlp_low, mlp_high, mixer_w, tokens, gain, mixer_sum, mlp_back, input_grad,
    held, cross, near, lined, left_now, both_now, mixed_now, turned, stage, rest_other, back_now, wide_now, gain_now,
    load_sem, core_send, core_recv, wide_sem,
    flow_send, flow_recv, line_send, line_recv, swap_send, swap_recv, own_sem,
):
    s, z, core, beside, across = places()
    chip_diag, chip_beside, chip_across, chip = 0, 1, 2, 3
    chips = [q // 2 for q in (beside + across - s, beside, across, s)]
    rows = held.shape[1] // 4
    cols = held.shape[2]
    cut = cols // 256 * 128
    ff_part = mlp_low.shape[1] // 3
    tok, model = tokens.shape
    half = 4 * rows
    lru = grad_branch.shape[1]
    lru2 = 2 * lru
    rest_start = lru2 + mixed.shape[1]
    order = (3 * (1 - z // 2), (2 + 3 * z) % 5, 1 + z % 2, z)

    def remote(src, dst, send, recv, target):
        return pltpu.make_async_remote_copy(
            src_ref=src, dst_ref=dst, send_sem=send, recv_sem=recv, device_id=target, device_id_type=MESH
        )

    def span(k):
        return pl.ds(pl.multiple_of(k * rows, 16), rows)

    mine, other = pl.ds(0, tok), pl.ds(tok, tok)
    loads = [
        pltpu.make_async_copy(source, target, load_sem.at[n])
        for n, (source, target) in enumerate(
            (
                (grad_mix, left_now.at[1, mine, :]),
                (mix_other, left_now.at[1, other, :]),
                (mixed, mixed_now.at[mine, :]),
                (mixed_other, mixed_now.at[other, :]),
                (normed, left_now.at[0, mine, :]),
                (normed_other, left_now.at[0, other, :]),
                (grad_gelu, both_now.at[mine, pl.ds(lru, lru)]),
                (gelu_other, both_now.at[other, pl.ds(lru, lru)]),
                (grad_branch, both_now.at[mine, pl.ds(0, lru)]),
            )
        )
    ]

    def push(n):
        if n == 0:
            source, target = grad_branch, both_now.at[other, pl.ds(0, lru)]
        else:
            source = rest.at[pl.ds(pl.multiple_of(chips[n - 1] * 2 * half + (1 - s % 2) * half, 16), half), :]
            target = rest_other.at[n - 1]
        return pltpu.make_async_remote_copy(
            src_ref=source,
            dst_ref=target,
            send_sem=core_send.at[n],
            recv_sem=core_recv.at[n],
            device_id=(core, z),
            device_id_type=MESH,
        )

    def rest_load(q):
        source = rest.at[pl.ds(pl.multiple_of(chips[q] * 2 * half + s % 2 * half, 16), half), :]
        return pltpu.make_async_copy(
            source, held.at[q, :, pl.ds(rest_start, cols - rest_start)], load_sem.at[9 + q]
        )

    def turn(side):
        for q in range(4):
            source = left_now[side, :, pl.ds(pl.multiple_of(chips[q] * 2 * half, 128), 2 * half)]
            stage[...] = source.T
            turned[side, q * half : (q + 1) * half, :] = stage[
                pl.ds(pl.multiple_of(s % 2 * half, 16), half), :
            ]

    def multiply(q, side, first=0, last=None):
        right, start = ((both_now, 0), (mixed_now, lru2))[side]

        def one(turn, carry):
            here = pl.multiple_of(turn * 512, 512)
            block = mm(turned[side, q * half : (q + 1) * half, :], right[:, pl.ds(here, 512)], ((1,), (0,)))
            held[q, :, pl.ds(pl.multiple_of(start + here, 512), 512)] = block.astype(bf16)
            return carry

        lax.fori_loop(first // 512, (right.shape[1] if last is None else last) // 512, one, 0)

    def add_rest(q):
        rest_load(q).wait()
        push(1 + q).wait_recv()
        held[q, :, rest_start:] = add_low(held[q, :, rest_start:], rest_other[q])

    left, right = pl.ds(0, cut), pl.ds(cut, cols - cut)

    def block(q, i, side):
        return held.at[q, span(order[i]), side]

    def flow(i, index):
        send, recv = flow_send.at[i, index], flow_recv.at[i, index]
        to_beside, to_across = (beside, z), (across, z)
        if index == 0:
            return remote(block(chip_diag, i, left), cross.at[i, :, left], send, recv, to_across)
        if index == 1:
            return remote(block(chip_diag, i, right), cross.at[i, :, right], send, recv, to_beside)
        if index == 2:
            return remote(block(chip_beside, i, right), near.at[0, i, :, right], send, recv, to_beside)
        if index == 3:
            return remote(block(chip_beside, i, left), near.at[0, i, :, left], send, recv, to_beside)
        if index == 4:
            return remote(block(chip_across, i, left), near.at[1, i, :, left], send, recv, to_across)
        return remote(block(chip_across, i, right), near.at[1, i, :, right], send, recv, to_across)

    def cross_step(i):
        flow(i, 0).wait_recv()
        add_columns(held.at[chip_beside, span(order[i]), :], [cross.at[i]], 0, cut, 512)
        flow(i, 3).start()
        flow(i, 1).wait_recv()
        add_columns(held.at[chip_across, span(order[i]), :], [cross.at[i]], cut, cols - cut, 384)
        flow(i, 5).start()

    def near_step(i):
        for index in (2, 4, 3, 5):
            flow(i, index).wait_recv()
        add_columns(held.at[chip, span(order[i]), :], [near.at[0, i], near.at[1, i]], 0, cols, 640)

    def line(k, slot, target):
        return remote(
            held.at[chip, span(k), :], lined.at[slot], line_send.at[k], line_recv.at[slot], (s, target)
        )

    def absorb(k, slot, source):
        line(k, slot, source).wait_recv()
        add_columns(held.at[chip, span(k), :], [lined.at[slot]], 0, cols, 640)

    def chain(i):
        k = order[i]
        if i == 3:
            pl.when(z > 0)(lambda: absorb(k, k, z - 1))
            pl.when(z < 3)(lambda: absorb(k, 4, z + 1))
            return

        @pl.when(k > z)
        def _():
            pl.when(z > 0)(lambda: absorb(k, k, z - 1))
            line(k, k, z + 1).start()

        @pl.when(k < z)
        def _():
            pl.when(z < 3)(lambda: absorb(k, k, z + 1))
            pl.when(k == z - 1)(lambda: line(k, 4, z - 1).start())
            pl.when(k < z - 1)(lambda: line(k, k, z - 1).start())

    def chain_drain():
        for i in range(3):
            k = order[i]
            line(k, k, (z + 1) % 4).wait_send()

    def swap(k, high=False):
        to = (z + k) % 4
        here = pl.ds(pl.multiple_of(z * ff_part, 128), ff_part)
        source = (mlp_high if high else mlp_low).at[span(to % 2), :]
        return [
            remote(
                source.at[:, pl.ds(m * ff_part, ff_part)],
                mlp_back.at[m, :, here],
                swap_send.at[k - 1, m],
                swap_recv.at[k - 1, m],
                (s, to),
            )
            for m in range(3)
        ]

    def swap_start(k):
        to = (z + k) % 4

        @pl.when(to < 2)
        def _():
            for copy in swap(k):
                copy.start()

        @pl.when(to >= 2)
        def _():
            for copy in swap(k, True):
                copy.start()

    def own(high=False):
        here = pl.ds(pl.multiple_of(z * ff_part, 128), ff_part)
        source = (mlp_high if high else mlp_low).at[span(z % 2), :]
        return [
            pltpu.make_async_copy(source.at[:, pl.ds(m * ff_part, ff_part)], mlp_back.at[m, :, here], own_sem.at[m])
            for m in range(3)
        ]

    wide_rows = wide_now.shape[0]
    wide_tiles = mixer_w.shape[0] // wide_rows
    wide_start = mixer_w.shape[1] - lru2 - model
    wide_slots = (both_now.at[pl.ds(tok, wide_rows), :], wide_now)

    def wide(j):
        source = mixer_w.at[pl.ds(j * wide_rows, wide_rows), pl.ds(wide_start, lru2)]
        return pltpu.make_async_copy(source, wide_slots[j % 2], wide_sem.at[j % 2])

    plain_loads = [
        pltpu.make_async_copy(tokens, left_now.at[0, pl.ds(0, tok), :], wide_sem.at[2]),
        pltpu.make_async_copy(gain, gain_now, wide_sem.at[3]),
    ]

    def back(first, last):
        for j in range(first, last):
            wide(j).wait()
            back_now[:, pl.ds(j * wide_rows, wide_rows)] = mm(
                both_now[0:tok, :], wide_slots[j % 2][...], ((1,), (1,))
            )
            if j + 2 < wide_tiles:
                wide(j + 2).start()

    def finish_rows(turn, carry):
        at = pl.ds(pl.multiple_of(turn * 16, 16), 16)
        result = left_now[1, at, :].astype(f32) + norm_back(
            left_now[0, at, :].astype(f32), gain_now[GAIN_ONE : GAIN_ONE + 1, :], back_now[at, :]
        )
        left_now[0, at, :] = result.astype(bf16)
        return carry

    for copy in loads:
        copy.start()
    for q in range(4):
        rest_load(q).start()
    greet([(core, z), (beside, z), (across, z)] + [(s, (z + k) % 4) for k in range(1, 4)])
    for n in range(5):
        push(n).start()
    for k in (1, 3, 2):
        swap_start(k)

    @pl.when(z < 2)
    def _():
        for copy in own():
            copy.start()

    @pl.when(z >= 2)
    def _():
        for copy in own(True):
            copy.start()

    for copy in loads[:4]:
        copy.wait()
    turn(1)
    multiply(chip_diag, 1)
    for copy in loads[4:]:
        copy.wait()
    turn(0)
    multiply(chip_diag, 0, lru)
    add_rest(chip_diag)
    for i in range(2):
        flow(i, 1).start()
    push(0).wait_recv()
    multiply(chip_diag, 0, 0, lru)
    for i in range(2):
        flow(i, 0).start()
    for q in (chip_beside, chip_across, chip):
        multiply(q, 0)
        multiply(q, 1)
        add_rest(q)
        if q == chip_beside:
            flow(0, 2).start()
        if q == chip_across:
            flow(0, 4).start()
    for copy in plain_loads:
        copy.start()
    wide(0).start()
    wide(1).start()
    for i in range(4):
        cross_step(i)
        if i + 1 < 4:
            flow(i + 1, 2).start()
            flow(i + 1, 4).start()
        if i + 2 < 4:
            flow(i + 2, 0).start()
            flow(i + 2, 1).start()
        if i > 0:
            near_step(i - 1)
            chain(i - 1)
            back(wide_tiles * (i - 1) // 3, wide_tiles * i // 3)
    for copy in plain_loads:
        copy.wait()
    lax.fori_loop(0, tok // 16, finish_rows, 0)
    finished = pltpu.make_async_copy(left_now.at[0, pl.ds(0, tok), :], input_grad, wide_sem.at[2])
    finished.start()
    near_step(3)
    chain(3)
    done = pltpu.make_async_copy(held.at[chip, span(z), :], mixer_sum, own_sem.at[3])
    done.start()
    for i in range(4):
        for index in range(6):
            flow(i, index).wait_send()
    chain_drain()
    for k in range(1, 4):
        for copy in swap(k):
            copy.wait()
    for copy in own():
        copy.wait()
    for n in range(5):
        push(n).wait_send()
    finished.wait()
    done.wait()


def scatter(rows_pairs, grad_branch, rest, mlp_low, mlp_high, mixer_w, tokens, gain):
    tok, model = tokens.shape
    rows = model // 32
    lru = grad_branch.shape[1]
    cols = 3 * lru + rest.shape[1]
    ff_part = mlp_low.shape[1] // 3
    anyspec = pl.BlockSpec(memory_space=pl.ANY)
    dma = pltpu.SemaphoreType.DMA
    return pl.pallas_call(
        scatter_kernel,
        in_specs=[anyspec] * 15,
        out_specs=[anyspec] * 3,
        out_shape=[
            jax.ShapeDtypeStruct((rows, cols), bf16),
            jax.ShapeDtypeStruct((3, rows, 4 * ff_part), bf16),
            jax.ShapeDtypeStruct((tok, model), bf16),
        ],
        scratch_shapes=[
            pltpu.VMEM((4, 4 * rows, cols), bf16),
            pltpu.VMEM((4, rows, cols), bf16),
            pltpu.VMEM((2, 4, rows, cols), bf16),
            pltpu.VMEM((5, rows, cols), bf16),
            pltpu.VMEM((2, 2 * tok, model), bf16),
            pltpu.VMEM((2 * tok, 2 * lru), bf16),
            pltpu.VMEM((2 * tok, lru), bf16),
            pltpu.VMEM((2, 16 * rows, 2 * tok), bf16),
            pltpu.VMEM((8 * rows, 2 * tok), bf16),
            pltpu.VMEM((4, 4 * rows, rest.shape[1]), bf16),
            pltpu.VMEM((tok, model), f32),
            pltpu.VMEM((128, 2 * lru), bf16),
            pltpu.VMEM(gain.shape, f32),
            dma((13,)), dma((5,)), dma((5,)), dma((4,)),
            dma((4, 6)), dma((4, 6)), dma((4,)), dma((5,)), dma((3, 3)), dma((3, 3)), dma((4,)),
        ],
        compiler_params=pltpu.CompilerParams(
            collective_id=2, has_side_effects=True, vmem_limit_bytes=62 * 1024 * 1024
        ),
        name="scatter_gradients",
    )(*rows_pairs, grad_branch, rest, mlp_low, mlp_high, mixer_w, tokens, gain)


def gather_plain(mixer, gate, up, down):
    groups = lax.axis_size("fsdp")
    part_rows, ff = gate.shape
    own = jnp.stack([w.reshape(part_rows, groups, ff // groups) for w in (gate, up, down)], axis=2)
    mine = lax.all_to_all(jnp.transpose(own, (1, 0, 2, 3)), "fsdp", 0, 0, tiled=True)
    return lax.all_gather(mixer, both, axis=0, tiled=True), mine.reshape(groups * part_rows, -1)


def from_line(shard):
    count = lax.axis_size("fsdp")
    return [shard] + [
        lax.ppermute(shard, "fsdp", [(i, (i + k) % count) for i in range(count)]) for k in range(1, count)
    ]


def swap_cores(shard):
    count = lax.axis_size("seq")
    return lax.ppermute(shard, "seq", [(i, i + 1 - 2 * (i % 2)) for i in range(count)])


def swap_beside(shard):
    return lax.ppermute(shard, "seq", [(i, i ^ 2) for i in range(8)])


def swap_across(shard):
    return lax.ppermute(shard, "seq", [(i, i ^ 4) for i in range(8)])


def add_low(left, right):
    return (left.astype(f32) + right.astype(f32)).astype(bf16)


def scatter_plain(normed, grad_both, grad_mix, mixed, rest, mlp_sum):
    groups = lax.axis_size("fsdp")
    term_wide = mm(normed, grad_both, ((0,), (0,))).astype(bf16)
    term_out = mm(grad_mix, mixed, ((0,), (0,))).astype(bf16)
    mixer_sum = lax.psum_scatter(
        jnp.concatenate([term_wide, term_out, rest], axis=1), "seq", scatter_dimension=0, tiled=True
    )
    mixer_sum = lax.psum_scatter(mixer_sum, "fsdp", scatter_dimension=0, tiled=True)
    ff_part = mlp_sum.shape[1] // 3
    part_rows = mlp_sum.shape[0] // groups
    mlp_sum = mlp_sum.reshape(groups, part_rows, 3, ff_part)
    mlp_back = lax.all_to_all(mlp_sum, "fsdp", 0, 0, tiled=True)
    mlp_back = jnp.transpose(mlp_back, (2, 1, 0, 3)).reshape(3, part_rows, groups * ff_part)
    return mixer_sum, mlp_back


def call_heads(kernel, width, heads, ins, outs, scratch, name):
    def spec(rows, place):
        if place is None:
            return pl.BlockSpec((rows, width), lambda h: (0, h))
        return pl.BlockSpec((width, width), lambda h: (h, place))

    in_specs = [spec(a.shape[0], place) for a, place in ins]
    out_specs = [spec(rows, 0 if rowwise else None) for rows, _, rowwise in outs]
    out_shape = [
        jax.ShapeDtypeStruct((heads * width, width) if rowwise else (rows, heads * width), kind)
        for rows, kind, rowwise in outs
    ]
    return pl.pallas_call(
        kernel,
        grid=(heads,),
        in_specs=in_specs,
        out_specs=out_specs,
        out_shape=out_shape,
        scratch_shapes=[pltpu.VMEM((rows, width), f32) for rows in scratch],
        compiler_params=pltpu.CompilerParams(vmem_limit_bytes=16 * 1024 * 1024),
        cost_estimate=pl.CostEstimate(flops=1, bytes_accessed=1, transcendentals=0),
        name=name,
    )(*[a for a, _ in ins])


def on_device(
    block_input,
    cotangent,
    mixer_gain,
    branch_proj,
    gelu_proj,
    conv_taps,
    conv_bias,
    rate_blocks,
    input_blocks,
    rate_bias,
    input_bias,
    decay_param,
    out_proj,
    mlp_gain,
    gate_proj,
    up_proj,
    down_proj,
):
    groups = lax.axis_size("fsdp")
    part_rows, lru = branch_proj.shape
    width = rate_blocks.shape[1]
    heads = lru // width
    margin = conv_taps.shape[0] - 1
    tokens = block_input[0].astype(f32)
    tok_count, model = tokens.shape
    ff = gate_proj.shape[1]
    ff_part = ff // groups
    grad_out = cotangent[0]

    smalls = jnp.stack(
        [conv_taps[k] for k in range(margin + 1)]
        + [conv_bias, rate_bias, input_bias, decay_param, mixer_gain, mlp_gain],
        axis=1,
    )
    small_count = smalls.shape[1]
    smalls = jnp.pad(smalls, ((0, 0), (0, 128 - small_count)))
    first_own = jnp.concatenate([rate_blocks, input_blocks, smalls], axis=1)
    mixer_own = (first_own, branch_proj, gelu_proj, out_proj)
    custom = lax.axis_size("seq") == 8 and groups == 4
    if custom:
        mixer_w, mlp_mine = gather(*mixer_own, gate_proj, up_proj, down_proj)
    else:
        mixer_w, mlp_mine = gather_plain(jnp.concatenate(mixer_own, axis=1), gate_proj, up_proj, down_proj)
    mlp_w = lax.all_gather(mlp_mine, "seq", axis=0, tiled=True)
    grad_out_late = lax.optimization_barrier((grad_out, mlp_mine))[0]
    if custom:
        grad_pieces = from_line(grad_out_late)
    wide = mixer_w[:, 128 + 2 * width : 128 + 2 * width + 2 * lru]
    proj_out = mixer_w[:, 128 + 2 * width + 2 * lru :]

    small = small_table(mixer_w, 2 * width // 128)
    gain_one, gain_two = small[GAIN_ONE], small[GAIN_TWO]

    normed, branch, gelu_pre = mixer_in(block_input[0], small, mixer_w, lru, 2 * width + 128)
    prior = from_behind(branch[tok_count - margin :], "seq", 1).astype(f32)
    prior = jnp.concatenate([jnp.zeros((8 - margin, lru), f32), prior], axis=0)
    conv, rate_pre, input_pre, cum, local = call_heads(
        mixer_forward,
        width,
        heads,
        [(branch, None), (prior, None), (small, None), (mixer_w, 0), (mixer_w, 1)],
        [(tok_count, bf16, False)] + [(tok_count, f32, False)] * 4,
        [tok_count + 8],
        "mixer_forward",
    )
    carried = prefix((cum[-1], local[-1]), "seq", False)
    states = local + cum * carried[None]
    mixed = (states * jax.nn.gelu(gelu_pre, approximate=True)).astype(bf16)
    middle = tokens + mm(mixed, proj_out, ((1,), (1,)))
    normed_two = norm_rows(middle, gain_two).astype(bf16)

    if custom:
        normed_all, normed_other, grad_out_all, grad_out_other, first_other, mixed_other = gather_rows(
            normed_two, grad_pieces, normed, mixed
        )
    else:
        normed_all = lax.all_gather(normed_two, "fsdp", axis=0, tiled=True)
        grad_out_all = lax.all_gather(grad_out_late, "fsdp", axis=0, tiled=True)
    w_gate, w_up, w_down = mlp_w[:, :ff_part], mlp_w[:, ff_part : 2 * ff_part], mlp_w[:, 2 * ff_part :]
    if custom:
        hidden, hidden_other, grad_pair, pair_other, grad_normed_part = feed_forward(
            normed_all, grad_out_all, mlp_w
        )
    else:
        gate = mm(normed_all, w_gate, ((1,), (0,)))
        up_val = mm(normed_all, w_up, ((1,), (0,)))
        gelu_gate, gelu_slope = gelu_parts(gate)
        hidden = (gelu_gate * up_val).astype(bf16)
        grad_hidden = mm(grad_out_all, w_down, ((1,), (0,)))
        grad_gate = (grad_hidden * up_val * gelu_slope).astype(bf16)
        grad_up = (grad_hidden * gelu_gate).astype(bf16)
        grad_normed_part = (
            mm(grad_gate, w_gate, ((1,), (1,))) + mm(grad_up, w_up, ((1,), (1,)))
        ).astype(bf16)
    grad_normed_two = lax.psum_scatter(grad_normed_part, "fsdp", scatter_dimension=0, tiled=True)
    if custom:
        half = model // 16
        beside_high, across_low, mine, beside_low, across_high, out_part = shared_products(
            (normed_all, normed_other, grad_out_all, grad_out_other),
            mlp_w,
            (grad_pair, pair_other),
            (hidden, hidden_other),
        )
        from_beside_high, from_across_low = swap_beside(beside_high), swap_across(across_low)
    else:
        grad_pair = jnp.concatenate([grad_gate, grad_up], axis=1)
        term_pair = mm(normed_all, grad_pair, ((0,), (0,))).astype(bf16)
        term_down = mm(grad_out_all, hidden, ((0,), (0,))).astype(bf16)
        pair_sum = lax.psum_scatter(term_pair, "seq", scatter_dimension=0, tiled=True)
        down_sum = lax.psum_scatter(term_down, "seq", scatter_dimension=0, tiled=True)
        mlp_sum = jnp.concatenate([pair_sum, down_sum], axis=1)
        out_part = mm(hidden, w_down, ((1,), (1,))).astype(bf16)
    out_sum = lax.psum_scatter(out_part, "fsdp", scatter_dimension=0, tiled=True)
    grad_normed_two = grad_normed_two.astype(f32)

    grad_middle = grad_out.astype(f32) + norm_back(middle, gain_two, grad_normed_two)
    grad_mix = grad_middle.astype(bf16)
    if custom:
        mix_other = swap_cores(grad_mix)
    grad_mixed = mm(grad_mix, proj_out, ((1,), (0,)))
    carried_rows = jnp.broadcast_to(carried[None], (8, lru))
    grad_gelu_pre, rev_cum, rev_grad, pair_grad = call_heads(
        mixer_backward_scan,
        width,
        heads,
        [(a, None) for a in (grad_mixed, gelu_pre, rate_pre, cum, local, carried_rows, small)],
        [(tok_count, bf16, False), (tok_count, f32, False), (tok_count, f32, False), (8, f32, False)],
        [tok_count + 8],
        "mixer_backward_scan",
    )
    if custom:
        from_beside_high, from_across_low, pair_grad = lax.optimization_barrier(
            (from_beside_high, from_across_low, pair_grad)
        )
    if custom:
        gelu_other = swap_cores(grad_gelu_pre)
    incoming = prefix((cum[-1], pair_grad[0]), "seq", True)
    if custom:
        beside_low, across_high, incoming = lax.optimization_barrier((beside_low, across_high, incoming))
        from_beside_low, from_across_high = swap_beside(beside_low), swap_across(across_high)
    incoming_rows = jnp.broadcast_to(incoming[None], (8, lru))
    own, head, rate_w_grad, input_w_grad, sums = call_heads(
        mixer_backward,
        width,
        heads,
        [
            (a, None)
            for a in (rev_cum, rev_grad, incoming_rows, cum, local, carried_rows, rate_pre, input_pre, conv, branch, prior, small)
        ]
        + [(mixer_w, 0), (mixer_w, 1)],
        [(tok_count, f32, False), (8, f32, False), (0, bf16, True), (0, bf16, True), (8, f32, False)],
        [tok_count + 8, tok_count + 16],
        "mixer_backward",
    )
    received = from_behind(head[8 - margin :], "seq", -1)
    grad_branch = jnp.concatenate(
        [own[: tok_count - margin], own[tok_count - margin :] + received], axis=0
    ).astype(bf16)
    grad_both = jnp.concatenate([grad_branch, grad_gelu_pre], axis=1)
    vectors = jnp.pad(sums.T, ((0, 0), (0, 128 - sums.shape[0]))).astype(bf16)
    rest = jnp.concatenate([rate_w_grad, input_w_grad, vectors], axis=1)
    if custom:
        low, high = [
            sum(part.astype(f32) for part in parts).astype(bf16)
            for parts in (
                (mine[:half], from_across_low, from_beside_low),
                (mine[half:], from_across_high, from_beside_high),
            )
        ]
        mixer_sum, mlp_back, input_grad = scatter(
            (normed, first_other, grad_mix, mix_other, mixed, mixed_other, grad_gelu_pre, gelu_other),
            grad_branch, rest, low, high, mixer_w, block_input[0], small,
        )
    else:
        mixer_sum, mlp_back = scatter_plain(normed, grad_both, grad_mix, mixed, rest, mlp_sum)
        grad_normed = mm(grad_both, wide, ((1,), (1,)))
        input_grad = (grad_middle + norm_back(tokens, gain_one, grad_normed)).astype(bf16)
    input_grad = input_grad[None]
    middle = lax.optimization_barrier((middle, mixer_sum))[0]
    block_output = (middle + out_sum.astype(f32)).astype(bf16)[None]
    edge = 3 * lru + 2 * width
    vec = mixer_sum[:, edge:].astype(f32).T
    weight_grads = list(
        jnp.split(mixer_sum[:, :edge].astype(f32), [lru, 2 * lru, 3 * lru, 3 * lru + width], axis=1)
    ) + [mlp_back[m].astype(f32) for m in range(3)]
    first_total = gain_back((branch_proj, weight_grads[0]), (gelu_proj, weight_grads[1]))
    second_total = gain_back((gate_proj, weight_grads[5]), (up_proj, weight_grads[6]))
    dbranch, dgelu, dout, drate, dinput, dgate, dup, ddown = weight_grads
    return (
        block_output,
        input_grad,
        first_total / mixer_gain.astype(f32),
        dbranch,
        dgelu,
        vec[: margin + 1],
        vec[7],
        drate,
        dinput,
        vec[4],
        vec[5],
        vec[6],
        dout,
        second_total / mlp_gain.astype(f32),
        dgate,
        dup,
        ddown,
    )


def solution(mesh):
    tokens = P("fsdp", "seq", None)
    vector = P(both)
    matrix = P(both, None)
    taps = P(None, both)
    return jax.shard_map(
        on_device,
        mesh=mesh,
        in_specs=(
            tokens, tokens, vector, matrix, matrix, taps, vector, matrix, matrix,
            vector, vector, vector, matrix, vector, matrix, matrix, matrix,
        ),
        out_specs=(
            tokens, tokens, vector, matrix, matrix, taps, vector, matrix, matrix,
            vector, vector, vector, matrix, vector, matrix, matrix, matrix,
        ),
        check_vma=False,
    )
```

```python
import functools

import jax
import jax.numpy as jnp
from jax import lax
from jax.experimental import pallas as pl
from jax.experimental.pallas import tpu as pltpu
from jax.sharding import PartitionSpec as P

epsilon = 1e-06
f32 = jnp.float32
bf16 = jnp.bfloat16
both = ("seq", "fsdp")
MESH = pl.DeviceIdType.MESH
TAP, CONV_BIAS, RATE_BIAS, INPUT_BIAS, SOFT, SOFT_SLOPE, GAIN_ONE, GAIN_TWO = 0, 4, 5, 6, 7, 8, 9, 10
GELU_C = 0.7978845608028654
GELU_A = 0.044715


def from_behind(shard, axis, by):
    devices = lax.axis_size(axis)
    pairs = [(i, i + by) for i in range(devices) if 0 <= i + by < devices]
    return lax.ppermute(shard, axis, pairs)


def prefix(part, axis, reverse):
    count = lax.axis_size(axis)
    place = lax.axis_index(axis)
    gathered = lax.all_gather(jnp.stack(part), axis)
    state = jnp.zeros_like(part[1])
    for hop in range(count):
        source = count - 1 - hop if reverse else hop
        ahead = source > place if reverse else source < place
        state = jnp.where(ahead, gathered[source, 1] + gathered[source, 0] * state, state)
    return state


def norm_rows(values, scales):
    return values * lax.rsqrt(jnp.mean(values * values, axis=-1, keepdims=True) + epsilon) * scales


def norm_back(values, scales, grads):
    inverse = lax.rsqrt(jnp.mean(values * values, axis=-1, keepdims=True) + epsilon)
    scaled = grads * scales
    shared = jnp.mean(values * scaled, axis=-1, keepdims=True)
    return inverse * scaled - values * (inverse * inverse * inverse * shared)


def gain_back(*pairs):
    return sum(jnp.sum(weight.astype(f32) * grad, axis=1) for weight, grad in pairs)


def gelu_parts(x):
    square = x * x
    inner = jnp.tanh(x * (GELU_C + GELU_C * GELU_A * square))
    open_part = 0.5 + 0.5 * inner
    value = x * open_part
    return value, open_part + value * (1.0 - inner) * (GELU_C + 3.0 * GELU_C * GELU_A * square)


def mm(left, right, dims):
    return lax.dot_general(left, right, (dims, ((), ())), preferred_element_type=f32)


def sigmoid(x):
    return 1.0 / (1.0 + jnp.exp(-x))


def scan_rows(decay, value, reverse):
    rows = decay.shape[0]
    place = lax.broadcasted_iota(jnp.int32, decay.shape, 0)
    step = 1
    while step < rows:
        shift = rows - step if reverse else step
        inside = place < rows - step if reverse else place >= step
        before_value = jnp.where(inside, pltpu.roll(value, shift, 0), 0.0)
        before_decay = jnp.where(inside, pltpu.roll(decay, shift, 0), 1.0)
        value = value + decay * before_value
        decay = decay * before_decay
        step *= 2
    return decay, value


def gates(rate_pre, input_pre, soft):
    rate = sigmoid(rate_pre)
    log_decay = -8.0 * rate * soft
    decay = jnp.exp(log_decay)
    square = decay * decay
    root = jnp.sqrt(-jnp.tanh(log_decay) * (1.0 + square))
    return rate, decay, square, root, sigmoid(input_pre)


def table_kernel(columns, table):
    rows = columns[...].T[0:16, :].astype(f32)
    decay_param = rows[7:8, :]
    fast = jnp.exp(-decay_param)
    table[0:7, :] = rows[0:7, :]
    table[7:8, :] = jnp.log1p(fast)
    table[8:9, :] = -fast / (1.0 + fast)
    table[9:11, :] = rows[8:10, :]
    table[11:16, :] = jnp.zeros((5, rows.shape[1]), f32)


def small_table(mixer_w, block):
    model = mixer_w.shape[0]
    return pl.pallas_call(
        table_kernel,
        grid=(1,),
        in_specs=[pl.BlockSpec((model, 128), lambda i: (0, block))],
        out_specs=pl.BlockSpec((16, model), lambda i: (0, 0)),
        out_shape=jax.ShapeDtypeStruct((16, model), f32),
        name="small_table",
    )(mixer_w)


def mixer_in_kernel(tokens, table, weights, normed, branch, gelu_pre):
    step = pl.program_id(0)

    @pl.when(step == 0)
    def _():
        normed[...] = norm_rows(tokens[...].astype(f32), table[GAIN_ONE : GAIN_ONE + 1, :]).astype(bf16)

    product = mm(normed[...], weights[...], ((1,), (0,)))
    half = pl.num_programs(0) // 2

    @pl.when(step < half)
    def _():
        branch[...] = product.astype(bf16)

    @pl.when(step >= half)
    def _():
        gelu_pre[...] = product


def mixer_in(tokens, table, mixer_w, lru, start):
    tok, model = tokens.shape
    tile = start
    tiles = lru // tile
    return pl.pallas_call(
        mixer_in_kernel,
        grid=(2 * tiles,),
        in_specs=[
            pl.BlockSpec((tok, model), lambda j: (0, 0)),
            pl.BlockSpec(table.shape, lambda j: (0, 0)),
            pl.BlockSpec((model, tile), lambda j: (0, 1 + j)),
        ],
        out_specs=[
            pl.BlockSpec((tok, model), lambda j: (0, 0)),
            pl.BlockSpec((tok, tile), lambda j: (0, jnp.minimum(j, tiles - 1))),
            pl.BlockSpec((tok, tile), lambda j: (0, jnp.maximum(j - tiles, 0))),
        ],
        out_shape=[
            jax.ShapeDtypeStruct((tok, model), bf16),
            jax.ShapeDtypeStruct((tok, lru), bf16),
            jax.ShapeDtypeStruct((tok, lru), f32),
        ],
        compiler_params=pltpu.CompilerParams(vmem_limit_bytes=16 * 1024 * 1024),
        cost_estimate=pl.CostEstimate(flops=1, bytes_accessed=1, transcendentals=0),
        name="mixer_in",
    )(tokens, table, mixer_w)


def mixer_forward(branch, prior, small, rate_w, input_w, conv, rate_pre, input_pre, cum, local, ext):
    rows = branch.shape[0]
    ext[0:8, :] = prior[...]
    ext[8:, :] = branch[...].astype(f32)
    total = small[CONV_BIAS : CONV_BIAS + 1, :] + small[TAP : TAP + 1, :] * ext[8:, :]
    for offset in range(1, 4):
        total = total + small[TAP + offset : TAP + offset + 1, :] * ext[pl.ds(8 - offset, rows), :]
    low = total.astype(bf16)
    conv[...] = low
    rate = mm(low, rate_w[...], ((1,), (0,))) + small[RATE_BIAS : RATE_BIAS + 1, :]
    inp = mm(low, input_w[...], ((1,), (0,))) + small[INPUT_BIAS : INPUT_BIAS + 1, :]
    rate_pre[...] = rate
    input_pre[...] = inp
    _, decay, _, root, opened = gates(rate, inp, small[SOFT : SOFT + 1, :])
    product, states = scan_rows(decay, root * opened * low.astype(f32), False)
    cum[...] = product
    local[...] = states


def mixer_backward_scan(grad_mixed, gelu_pre, rate_pre, cum, local, carried, small, grad_pre, rev_cum, rev_grad, pair, ext):
    rows = grad_mixed.shape[0]
    states = local[...] + cum[...] * carried[0:1, :]
    value, slope = gelu_parts(gelu_pre[...])
    grad = grad_mixed[...]
    grad_pre[...] = (grad * states * slope).astype(bf16)
    decay = jnp.exp(-8.0 * sigmoid(rate_pre[...]) * small[SOFT : SOFT + 1, :])
    ext[0:rows, :] = decay
    ext[rows:, :] = jnp.ones((8, decay.shape[1]), f32)
    product, back = scan_rows(ext[pl.ds(1, rows), :], grad * value, True)
    rev_cum[...] = product
    rev_grad[...] = back
    pair[...] = jnp.broadcast_to(decay[0:1, :] * back[0:1, :], pair.shape)


def mixer_backward(
    rev_cum, rev_grad, incoming, cum, local, carried, rate_pre, input_pre, conv, branch, prior, small, rate_w, input_w,
    own, head, rate_w_grad, input_w_grad, sums, ext, gext,
):
    rows = rev_cum.shape[0]
    soft = small[SOFT : SOFT + 1, :]
    grad_states = rev_grad[...] + rev_cum[...] * incoming[0:1, :]
    rate, decay, square, root, opened = gates(rate_pre[...], input_pre[...], soft)
    ext[0:8, :] = jnp.broadcast_to(carried[0:1, :], (8, carried.shape[1]))
    ext[8:, :] = local[...] + cum[...] * carried[0:1, :]
    before = ext[pl.ds(7, rows), :]
    low = conv[...]
    conv_in = low.astype(f32)
    grad_log = grad_states * decay * before - grad_states * opened * conv_in * square / root
    driven = grad_states * root
    grad_input = (driven * conv_in * opened * (1.0 - opened)).astype(bf16)
    by_rate = grad_log * (-8.0 * rate)
    grad_rate = (by_rate * soft * (1.0 - rate)).astype(bf16)
    sums[6:7, :] = jnp.sum(by_rate, axis=0, keepdims=True) * small[SOFT_SLOPE : SOFT_SLOPE + 1, :]
    sums[4:5, :] = jnp.sum(grad_rate.astype(f32), axis=0, keepdims=True)
    sums[5:6, :] = jnp.sum(grad_input.astype(f32), axis=0, keepdims=True)
    rate_w_grad[...] = mm(low, grad_rate, ((0,), (0,))).astype(rate_w_grad.dtype)
    input_w_grad[...] = mm(low, grad_input, ((0,), (0,))).astype(input_w_grad.dtype)
    grad_conv = (
        driven * opened
        + mm(grad_rate, rate_w[...], ((1,), (1,)))
        + mm(grad_input, input_w[...], ((1,), (1,)))
    )
    sums[7:8, :] = jnp.sum(grad_conv, axis=0, keepdims=True)
    ext[0:8, :] = prior[...]
    ext[8:, :] = branch[...].astype(f32)
    gext[0:8, :] = jnp.zeros((8, grad_conv.shape[1]), f32)
    gext[8 : 8 + rows, :] = grad_conv
    gext[8 + rows :, :] = jnp.zeros((8, grad_conv.shape[1]), f32)
    back = jnp.zeros_like(grad_conv)
    front = jnp.zeros((8, grad_conv.shape[1]), f32)
    for offset in range(4):
        tap = small[TAP + offset : TAP + offset + 1, :]
        sums[offset : offset + 1, :] = jnp.sum(
            grad_conv * ext[pl.ds(8 - offset, rows), :], axis=0, keepdims=True
        )
        back = back + tap * gext[pl.ds(8 + offset, rows), :]
        front = front + tap * gext[pl.ds(offset, 8), :]
    own[...] = back
    head[...] = front


def places():
    s = lax.axis_index("seq")
    z = lax.axis_index("fsdp")
    core = s + 1 - 2 * (s % 2)
    beside = s + 2 - 4 * ((s // 2) % 2)
    across = s + 4 - 8 * (s // 4)
    return s, z, core, beside, across


def greet(peers):
    barrier = pltpu.get_barrier_semaphore()
    for peer in peers:
        pl.semaphore_signal(barrier, inc=1, device_id=peer, device_id_type=MESH)
    pl.semaphore_wait(barrier, len(peers))


def gather_kernel(
    first, branch, gelu, outer, gate, up, down, mixer_all, mlp_mine,
    mixer, load_sem, flow_send, flow_recv, line_send, line_recv, swap_send, swap_recv, own_sem,
):
    s, z, core, beside, across = places()
    rows, cols = mixer.shape
    ff_part = mlp_mine.shape[1] // 3
    cut = cols // 256 * 128
    diag = beside + across - s
    loads, start = [], 0
    for n, part in enumerate((first, branch, gelu, outer)):
        size = part.shape[1]
        loads.append(pltpu.make_async_copy(part, mixer.at[:, pl.ds(start, size)], load_sem.at[n]))
        loads[-1].start()
        start += size
    greet([(core, z), (beside, z), (across, z)] + [(s, (z + k) % 4) for k in range(1, 4)])

    def remote(src, dst, send, recv, target):
        return pltpu.make_async_remote_copy(
            src_ref=src, dst_ref=dst, send_sem=send, recv_sem=recv, device_id=target, device_id_type=MESH
        )

    def piece(seq, zz, half=None):
        span = pl.ds(pl.multiple_of((seq * 4 + zz) * rows, 16), rows)
        if half is None:
            return mixer_all.at[span, :]
        return mixer_all.at[span, pl.ds(0, cut) if half == 0 else pl.ds(cut, cols - cut)]

    def flow(zz, index, seq, half, target, src=None):
        ref = piece(seq, zz, half)
        return remote(
            ref if src is None else src, ref, flow_send.at[zz, index], flow_recv.at[zz, index], (target, z)
        )

    def sends(zz, src=None):
        return [
            flow(zz, 0, s, None, beside, src),
            flow(zz, 1, s, None, across, src),
            flow(zz, 4, s, None, core, src),
        ]

    def spread(zz, src=None):
        for copy in sends(zz, src):
            copy.start()

    def relay(zz):
        flow(zz, 0, beside, None, beside).wait_recv()
        flow(zz, 3, beside, 0, across).start()
        flow(zz, 5, beside, None, core).start()
        flow(zz, 1, across, None, across).wait_recv()
        flow(zz, 2, across, 1, beside).start()
        flow(zz, 6, across, None, core).start()

    def finish(zz):
        flow(zz, 3, diag, 0, across).wait_recv()
        flow(zz, 7, diag, 0, core).start()
        flow(zz, 2, diag, 1, beside).wait_recv()
        flow(zz, 8, diag, 1, core).start()

    def drain(zz, src=None):
        for copy in sends(zz, src):
            copy.wait_send()
        flow(zz, 3, beside, 0, across).wait_send()
        flow(zz, 5, beside, None, core).wait_send()
        flow(zz, 2, across, 1, beside).wait_send()
        flow(zz, 6, across, None, core).wait_send()
        flow(zz, 7, diag, 0, core).wait_send()
        flow(zz, 8, diag, 1, core).wait_send()
        flip = core - s
        flow(zz, 4, core, None, core).wait_recv()
        flow(zz, 5, beside + flip, None, core).wait_recv()
        flow(zz, 6, across + flip, None, core).wait_recv()
        flow(zz, 7, diag + flip, 0, core).wait_recv()
        flow(zz, 8, diag + flip, 1, core).wait_recv()

    def line(zz, up_way, hop, src=None):
        ref = piece(s, zz)
        way = 0 if up_way else 1
        target = z + 1 if up_way else z - 1
        return remote(
            ref if src is None else src, ref, line_send.at[way, hop], line_recv.at[way, hop], (s, target)
        )

    def line_hop(hop):
        def below():
            line(z - hop, True, hop - 1).wait_recv()
            pl.when(z < 3)(lambda: line(z - hop, True, hop).start())

        def above():
            line(z + hop, False, hop - 1).wait_recv()
            pl.when(z > 0)(lambda: line(z + hop, False, hop).start())

        pl.when(z >= hop)(below)
        pl.when(z + hop <= 3)(above)

    def at_hop(hop, act):
        pl.when(z >= hop)(lambda: act(z - hop))
        pl.when(z + hop <= 3)(lambda: act(z + hop))

    def landing(m, zz):
        return mlp_mine.at[pl.ds(pl.multiple_of(zz * rows, 16), rows), pl.ds(m * ff_part, ff_part)]

    def columns(m, zz):
        return (gate, up, down)[m].at[:, pl.ds(pl.multiple_of(zz * ff_part, 128), ff_part)]

    def swap(k, m, arriving=False):
        to = (z + k) % 4
        came = (z + 4 - k) % 4
        return remote(
            columns(m, to), landing(m, came if arriving else z), swap_send.at[k - 1, m], swap_recv.at[k - 1, m], (s, to)
        )

    local = [pltpu.make_async_copy(columns(m, z), landing(m, z), own_sem.at[m]) for m in range(3)]
    local.append(pltpu.make_async_copy(mixer, piece(s, z), own_sem.at[3]))
    for copy in loads:
        copy.wait()

    pl.when(z < 3)(lambda: line(z, True, 0, mixer).start())
    pl.when(z > 0)(lambda: line(z, False, 0, mixer).start())
    spread(z, mixer)
    for copy in local:
        copy.start()
    line_hop(1)
    at_hop(1, spread)
    relay(z)
    line_hop(2)
    at_hop(2, spread)
    finish(z)
    at_hop(1, relay)
    line_hop(3)
    at_hop(3, spread)
    for k in (1, 3, 2):
        for m in range(3):
            swap(k, m).start()
    at_hop(1, finish)
    at_hop(2, relay)
    at_hop(3, relay)
    at_hop(2, finish)
    at_hop(3, finish)
    drain(z, mixer)
    for hop in range(1, 4):
        at_hop(hop, drain)
    for copy in local:
        copy.wait()
    for k in (1, 3, 2):
        for m in range(3):
            swap(k, m).wait_send()
            swap(k, m, True).wait_recv()
    pl.when(z < 3)(lambda: line(z, True, 0, mixer).wait_send())
    pl.when(z > 0)(lambda: line(z, False, 0, mixer).wait_send())
    for hop in range(1, 3):
        pl.when((z >= hop) & (z < 3))(lambda: line(z - hop, True, hop).wait_send())
        pl.when((z + hop <= 3) & (z > 0))(lambda: line(z + hop, False, hop).wait_send())


def gather(first, branch, gelu, outer, gate, up, down):
    rows = first.shape[0]
    cols = first.shape[1] + branch.shape[1] + gelu.shape[1] + outer.shape[1]
    ff_part = gate.shape[1] // 4
    anyspec = pl.BlockSpec(memory_space=pl.ANY)
    dma = pltpu.SemaphoreType.DMA
    return pl.pallas_call(
        gather_kernel,
        in_specs=[anyspec] * 7,
        out_specs=[anyspec] * 2,
        out_shape=[
            jax.ShapeDtypeStruct((32 * rows, cols), bf16),
            jax.ShapeDtypeStruct((4 * rows, 3 * ff_part), bf16),
        ],
        scratch_shapes=[
            pltpu.VMEM((rows, cols), bf16), dma((4,)),
            dma((4, 9)), dma((4, 9)), dma((2, 3)), dma((2, 3)), dma((3, 3)), dma((3, 3)), dma((4,)),
        ],
        compiler_params=pltpu.CompilerParams(collective_id=1, has_side_effects=True),
        name="gather_weights",
    )(first, branch, gelu, outer, gate, up, down)


def rows_kernel(
    normed, grad0, grad1, grad2, grad3, first, mixed, normed_all, normed_other, grad_all, grad_other,
    first_other, mixed_other, line_send, line_recv, core_send, core_recv, own_sem, held, give_send, give_recv,
):
    s, z, core, _, _ = places()
    tok = normed.shape[0]
    cuts = 4
    grads = (grad0, grad1, grad2, grad3)
    greet([(core, z)] + [(s, (z + k) % 4) for k in range(1, 4)])

    def rows(ref, zz):
        return ref.at[pl.ds(pl.multiple_of(zz * tok, 16), tok), :]

    def remote(src, dst, send, recv, target):
        return pltpu.make_async_remote_copy(
            src_ref=src, dst_ref=dst, send_sem=send, recv_sem=recv, device_id=target, device_id_type=MESH
        )

    def parts(ref):
        size = tok // cuts
        return [ref.at[pl.ds(n * size, size), :] for n in range(cuts)]

    def line(zz, up_way, hop):
        way = 0 if up_way else 1
        target = z + 1 if up_way else z - 1
        src = normed if hop == 0 else rows(normed_all, zz)
        dst = rows(normed_all, zz)
        return [
            remote(a, b, line_send.at[way, hop, n], line_recv.at[way, hop, n], (s, target))
            for n, (a, b) in enumerate(zip(parts(src), parts(dst)))
        ]

    def over(zz, own=False):
        src = normed if own else rows(normed_all, zz)
        return remote(src, rows(normed_other, zz), core_send.at[0, zz], core_recv.at[0, zz], (core, z))

    def grad_over(k):
        zz = (z + 4 - k) % 4
        return remote(grads[k], rows(grad_other, zz), core_send.at[1, zz], core_recv.at[1, zz], (core, z))

    def line_start(zz, up_way, hop):
        for copy in line(zz, up_way, hop):
            copy.start()

    def line_drain(zz, up_way, hop):
        for copy in line(zz, up_way, hop):
            copy.wait_send()

    def hop_step(hop):
        def below():
            for came, on in zip(line(z - hop, True, hop - 1), line(z - hop, True, hop) if hop < 3 else [None] * cuts):
                came.wait_recv()
                if on is not None:
                    pl.when(z < 3)(on.start)
            over(z - hop).start()

        def above():
            for came, on in zip(line(z + hop, False, hop - 1), line(z + hop, False, hop) if hop < 3 else [None] * cuts):
                came.wait_recv()
                if on is not None:
                    pl.when(z > 0)(on.start)
            over(z + hop).start()

        pl.when(z >= hop)(below)
        pl.when(z + hop <= 3)(above)

    given = [
        remote(source, target, give_send.at[n], give_recv.at[n], (core, z))
        for n, (source, target) in enumerate(((first, first_other), (mixed, mixed_other)))
    ]
    local = [pltpu.make_async_copy(grads[k], held.at[k], own_sem.at[k]) for k in range(4)]
    local.append(pltpu.make_async_copy(normed, held.at[4], own_sem.at[4]))
    stored = [
        pltpu.make_async_copy(held.at[k], rows(grad_all, (z + 4 - k) % 4), own_sem.at[k]) for k in range(4)
    ]
    stored.append(pltpu.make_async_copy(held.at[4], rows(normed_all, z), own_sem.at[4]))
    pl.when(z < 3)(lambda: line_start(z, True, 0))
    pl.when(z > 0)(lambda: line_start(z, False, 0))
    over(z, True).start()
    for copy in local:
        copy.start()
    for k in range(4):
        grad_over(k).start()
    for copy in given:
        copy.start()
    for copy, store in zip(local, stored):
        copy.wait()
        store.start()
    for hop in range(1, 4):
        hop_step(hop)
    for copy in stored:
        copy.wait()
    for k in range(4):
        grad_over(k).wait()
    for copy in given:
        copy.wait()
    over(z, True).wait()
    for k in range(1, 4):
        over((z + k) % 4).wait()
    pl.when(z < 3)(lambda: line_drain(z, True, 0))
    pl.when(z > 0)(lambda: line_drain(z, False, 0))
    for hop in range(1, 3):
        pl.when((z >= hop) & (z < 3))(lambda: line_drain(z - hop, True, hop))
        pl.when((z + hop <= 3) & (z > 0))(lambda: line_drain(z + hop, False, hop))


def gather_rows(normed, grads, first, mixed):
    tok, model = normed.shape
    anyspec = pl.BlockSpec(memory_space=pl.ANY)
    dma = pltpu.SemaphoreType.DMA
    return pl.pallas_call(
        rows_kernel,
        in_specs=[anyspec] * 7,
        out_specs=[anyspec] * 6,
        out_shape=[jax.ShapeDtypeStruct((4 * tok, model), bf16)] * 4
        + [jax.ShapeDtypeStruct(first.shape, bf16), jax.ShapeDtypeStruct(mixed.shape, bf16)],
        scratch_shapes=[
            dma((2, 3, 4)), dma((2, 3, 4)), dma((2, 4)), dma((2, 4)), dma((5,)),
            pltpu.VMEM((5, tok, model), bf16), dma((2,)), dma((2,)),
        ],
        compiler_params=pltpu.CompilerParams(collective_id=3, has_side_effects=True),
        name="gather_rows",
    )(normed, *grads, first, mixed)


def column_tiles(cols, size=512):
    return [(start, min(size, cols - start)) for start in range(0, cols, size)]


def feed_forward_kernel(
    normed, grad_out, weights, hidden, hidden_other, pair, pair_other, back,
    held, hidden_now, pair_now, sems, store_sem, core_send, core_recv,
):
    s, z, core, _, _ = places()
    step = pl.program_id(0)
    ff_part = held.shape[2]
    model = held.shape[1]
    rows = normed.shape[0]
    tiles = column_tiles(ff_part)
    made = ((hidden_now, hidden, hidden_other), (pair_now, pair, pair_other))

    def load(n, m):
        start, size = tiles[n]
        return pltpu.make_async_copy(
            weights.at[:, pl.ds(m * ff_part + start, size)], held.at[m, :, pl.ds(start, size)], sems.at[n, m]
        )

    def kept(n, turn):
        now, mine, _ = made[n]
        return pltpu.make_async_copy(now.at[turn], mine.at[pl.ds(turn * rows, rows), :], store_sem.at[turn, n])

    def handed(n, turn):
        now, _, other = made[n]
        return pltpu.make_async_remote_copy(
            src_ref=now.at[turn],
            dst_ref=other.at[pl.ds(turn * rows, rows), :],
            send_sem=core_send.at[turn, n],
            recv_sem=core_recv.at[turn, n],
            device_id=(core, z),
            device_id_type=MESH,
        )

    @pl.when(step == 0)
    def _():
        for n in range(len(tiles)):
            for m in range(3):
                load(n, m).start()
        greet([(core, z)])

    for n, (start, size) in enumerate(tiles):
        cols = slice(start, start + size)

        @pl.when(step == 0)
        def _(n=n):
            for m in range(3):
                load(n, m).wait()

        gate = mm(normed[...], held[0, :, cols], ((1,), (0,)))
        value, slope = gelu_parts(gate)
        up = mm(normed[...], held[1, :, cols], ((1,), (0,)))
        hidden_now[step, :, cols] = (value * up).astype(bf16)
        grad_hidden = mm(grad_out[...], held[2, :, cols], ((1,), (0,)))
        pair_now[step, :, cols] = (grad_hidden * up * slope).astype(bf16)
        pair_now[step, :, slice(ff_part + start, ff_part + start + size)] = (grad_hidden * value).astype(bf16)

    for turn in range(2):

        @pl.when(step == turn)
        def _(turn=turn):
            for n in range(2):
                handed(n, turn).start()
                kept(n, turn).start()

    def back_tile(turn, carry):
        cols = pl.ds(pl.multiple_of(turn * 512, 512), 512)
        total = mm(pair_now[step, :, :ff_part], held[0, cols, :], ((1,), (1,)))
        total = total + mm(pair_now[step, :, ff_part:], held[1, cols, :], ((1,), (1,)))
        back[:, cols] = total.astype(bf16)
        return carry

    lax.fori_loop(0, model // 512, back_tile, 0)

    @pl.when(step == 1)
    def _():
        for turn in range(2):
            for n in range(2):
                kept(n, turn).wait()
                handed(n, turn).wait()


def feed_forward(normed, grad_out, weights):
    tok, model = normed.shape
    ff_part = weights.shape[1] // 3
    rows = tok // 2
    anyspec = pl.BlockSpec(memory_space=pl.ANY)
    dma = pltpu.SemaphoreType.DMA
    block = pl.BlockSpec((rows, model), lambda i: (i, 0))
    return pl.pallas_call(
        feed_forward_kernel,
        grid=(2,),
        in_specs=[block, block, anyspec],
        out_specs=[anyspec] * 4 + [block],
        out_shape=[
            jax.ShapeDtypeStruct((tok, cols), bf16)
            for cols in (ff_part, ff_part, 2 * ff_part, 2 * ff_part, model)
        ],
        scratch_shapes=[
            pltpu.VMEM((3, model, ff_part), bf16),
            pltpu.VMEM((2, rows, ff_part), bf16),
            pltpu.VMEM((2, rows, 2 * ff_part), bf16),
            dma((len(column_tiles(ff_part)), 3)), dma((2, 2)), dma((2, 2)), dma((2, 2)),
        ],
        compiler_params=pltpu.CompilerParams(
            collective_id=4, has_side_effects=True, vmem_limit_bytes=60 * 1024 * 1024
        ),
        name="feed_forward",
    )(normed, grad_out, weights)


def add_columns(target, sources, start, size, step):
    def one(turn, carry):
        cols = pl.ds(pl.multiple_of(start + turn * step, 128), step)
        total = target[:, cols].astype(f32)
        for source in sources:
            total = total + source[:, cols].astype(f32)
        target[:, cols] = total.astype(target.dtype)
        return carry

    lax.fori_loop(0, size // step, one, 0)


def shared_products_kernel(
    normed, normed_other, grad, grad_other, weights, pair, pair_other, hidden, hidden_other,
    beside_high, across_low, mine, beside_low, across_high, out,
    turned, slots, stage, right, diag, landed, waiting, down_now, out_now,
    load_sem, right_sem, send_sem, recv_sem, store_sem, down_sem, out_sem,
):
    s, z, _, beside, across = places()
    step = pl.program_id(0)
    lefts = ((normed, normed_other), (grad, grad_other))
    chip_cols = normed.shape[1] // 4
    half = chip_cols // 2
    piece = half // 2
    width = hidden.shape[1]
    tok = normed.shape[0]
    diagonal = beside + across - s
    chips = [q // 2 for q in (diagonal, beside, across, s)]

    def load(side, q, who):
        cols = pl.ds(pl.multiple_of(chips[q] * chip_cols, 128), chip_cols)
        return pltpu.make_async_copy(lefts[side][who].at[:, cols], slots.at[q % 2, who], load_sem.at[q % 2, who])

    def fetch(side):
        for q in range(2):
            for who in range(2):
                load(side, q, who).start()

    def turn(side):
        for q in range(4):
            for who in range(2):
                load(side, q, who).wait()
                stage[...] = slots[q % 2, who].T
                turned[q * half : (q + 1) * half, who * tok : (who + 1) * tok] = stage[
                    pl.ds(pl.multiple_of(s % 2 * half, 16), half), :
                ]
                if q < 2:
                    load(side, q + 2, who).start()

    pieces = column_tiles(width)

    def push(way, cols, index):
        return pltpu.make_async_remote_copy(
            src_ref=diag.at[way, :, cols],
            dst_ref=landed.at[way, :, cols],
            send_sem=send_sem.at[way, index],
            recv_sem=recv_sem.at[way, index],
            device_id=(across if way == 0 else beside, z),
            device_id_type=MESH,
        )

    def take(j):
        sources = (hidden, hidden_other) if j == 2 else (pair, pair_other)
        return [
            pltpu.make_async_copy(
                source.at[:, pl.ds(0 if j == 2 else j * width, width)],
                right.at[j % 2, pl.ds(who * tok, tok), :],
                right_sem.at[j % 2, who],
            )
            for who, source in enumerate(sources)
        ]

    def take_start(j):
        for copy in take(j):
            copy.start()

    def take_wait(j):
        for copy in take(j):
            copy.wait()

    def tile(start, size):
        cols = pl.ds(start, size)
        block = mm(turned[...], right[step % 2, :, cols], ((1,), (0,))).astype(bf16)
        parts = [block[n * piece : (n + 1) * piece] for n in range(8)]
        there = pl.ds(pl.multiple_of(step * width + start, 128), size)
        index = step * len(pieces) + start // 512
        diag[0, :, there] = parts[0]
        diag[1, :, there] = parts[1]
        waiting[0, :, there] = parts[2]
        beside_high[:, cols] = parts[3]
        across_low[:, cols] = parts[4]
        waiting[1, :, there] = parts[5]
        mine[0:piece, cols] = parts[6]
        mine[piece:, cols] = parts[7]
        for way in range(2):
            push(way, there, index).start()

    def multiply():
        def one(turn, carry):
            tile(pl.multiple_of(turn * 512, 512), 512)
            return carry

        lax.fori_loop(0, width // 512, one, 0)
        if width % 512:
            tile(width // 512 * 512, width % 512)

    def store(way, j):
        cols = pl.ds(j * width, width)
        return pltpu.make_async_copy(
            waiting.at[way, :, cols], (beside_low, across_high)[way].at[:, cols], store_sem.at[way, j]
        )

    out_rows = down_now.shape[1]
    out_tiles = weights.shape[0] // out_rows

    def down(t):
        source = weights.at[pl.ds(t * out_rows, out_rows), pl.ds(2 * width, width)]
        return pltpu.make_async_copy(source, down_now.at[t % 2], down_sem.at[t % 2])

    def out_store(t):
        return pltpu.make_async_copy(
            out_now.at[t % 2], out.at[:, pl.ds(t * out_rows, out_rows)], out_sem.at[t % 2]
        )

    def out_product():
        for t in range(out_tiles):
            down(t).wait()
            if t > 1:
                out_store(t - 2).wait()
            out_now[t % 2] = mm(right[0, 0:tok, :], down_now[t % 2], ((1,), (1,))).astype(bf16)
            out_store(t).start()
            if t + 2 < out_tiles:
                down(t + 2).start()

    @pl.when(step == 0)
    def _():
        fetch(0)
        take_start(0)
        take_start(1)
        greet([(beside, z), (across, z)])
        turn(0)
        take_wait(0)

    @pl.when(step == 1)
    def _():
        take_wait(1)
        take_start(2)
        fetch(1)

    @pl.when(step == 2)
    def _():
        down(0).start()
        down(1).start()
        turn(1)
        take_wait(2)

    multiply()
    @pl.when(step == 2)
    def _():
        out_product()
        pushed = [
            (way, pl.ds(j * width + start, size), j * len(pieces) + n, j)
            for j in range(3)
            for n, (start, size) in enumerate(pieces)
            for way in range(2)
        ]
        for way, cols, index, j in pushed:
            push(way, cols, index).wait_recv()
            if index % len(pieces) == len(pieces) - 1:
                add_columns(waiting.at[way], [landed.at[way]], j * width, width, 384)
                store(way, j).start()
        for way, cols, index, j in pushed:
            push(way, cols, index).wait_send()
        for j in range(3):
            for way in range(2):
                store(way, j).wait()
        for t in range(out_tiles - 2, out_tiles):
            out_store(t).wait()


def shared_products(lefts, weights, pair, hidden):
    tok, model = lefts[0].shape
    width = hidden[0].shape[1]
    half = model // 8
    anyspec = pl.BlockSpec(memory_space=pl.ANY)
    dma = pltpu.SemaphoreType.DMA

    def block(rows):
        return pl.BlockSpec((rows, width), lambda j: (0, j))

    rows_out = (half // 2, half // 2, half, half // 2, half // 2)
    return pl.pallas_call(
        shared_products_kernel,
        grid=(3,),
        in_specs=[anyspec] * 9,
        out_specs=[block(rows) for rows in rows_out[:3]] + [anyspec] * 3,
        out_shape=[jax.ShapeDtypeStruct((rows, 3 * width), bf16) for rows in rows_out]
        + [jax.ShapeDtypeStruct((tok, model), bf16)],
        scratch_shapes=[
            pltpu.VMEM((4 * half, 2 * tok), bf16),
            pltpu.VMEM((2, 2, tok, 2 * half), bf16),
            pltpu.VMEM((2 * half, tok), bf16),
            pltpu.VMEM((2, 2 * tok, width), bf16),
            pltpu.VMEM((2, half // 2, 3 * width), bf16),
            pltpu.VMEM((2, half // 2, 3 * width), bf16),
            pltpu.VMEM((2, half // 2, 3 * width), bf16),
            pltpu.VMEM((2, 512, width), bf16),
            pltpu.VMEM((2, tok, 512), bf16),
            dma((2, 2)), dma((2, 2)), dma((2, 12)), dma((2, 12)), dma((2, 3)), dma((2,)), dma((2,)),
        ],
        compiler_params=pltpu.CompilerParams(
            collective_id=5, has_side_effects=True, vmem_limit_bytes=60 * 1024 * 1024
        ),
        name="feed_forward_products",
    )(*lefts, weights, *pair, *hidden)


def scatter_kernel(
    normed, normed_other, grad_mix, mix_other, mixed, mixed_other, grad_gelu, gelu_other, grad_branch, rest,
    mlp_low, mlp_high, mixer_w, tokens, gain, mixer_sum, mlp_back, input_grad,
    held, cross, near, lined, left_now, both_now, mixed_now, turned, stage, rest_other, back_now, wide_now, gain_now,
    load_sem, core_send, core_recv, wide_sem,
    flow_send, flow_recv, line_send, line_recv, swap_send, swap_recv, own_sem,
):
    s, z, core, beside, across = places()
    chip_diag, chip_beside, chip_across, chip = 0, 1, 2, 3
    chips = [q // 2 for q in (beside + across - s, beside, across, s)]
    rows = held.shape[1] // 4
    cols = held.shape[2]
    cut = cols // 256 * 128
    ff_part = mlp_low.shape[1] // 3
    tok, model = tokens.shape
    half = 4 * rows
    lru = grad_branch.shape[1]
    lru2 = 2 * lru
    rest_start = lru2 + mixed.shape[1]
    order = (3 * (1 - z // 2), (2 + 3 * z) % 5, 1 + z % 2, z)

    def remote(src, dst, send, recv, target):
        return pltpu.make_async_remote_copy(
            src_ref=src, dst_ref=dst, send_sem=send, recv_sem=recv, device_id=target, device_id_type=MESH
        )

    def span(k):
        return pl.ds(pl.multiple_of(k * rows, 16), rows)

    mine, other = pl.ds(0, tok), pl.ds(tok, tok)
    loads = [
        pltpu.make_async_copy(source, target, load_sem.at[n])
        for n, (source, target) in enumerate(
            (
                (grad_mix, left_now.at[1, mine, :]),
                (mix_other, left_now.at[1, other, :]),
                (mixed, mixed_now.at[mine, :]),
                (mixed_other, mixed_now.at[other, :]),
                (normed, left_now.at[0, mine, :]),
                (normed_other, left_now.at[0, other, :]),
                (grad_gelu, both_now.at[mine, pl.ds(lru, lru)]),
                (gelu_other, both_now.at[other, pl.ds(lru, lru)]),
                (grad_branch, both_now.at[mine, pl.ds(0, lru)]),
            )
        )
    ]

    def push(n):
        if n == 0:
            source, target = grad_branch, both_now.at[other, pl.ds(0, lru)]
        else:
            source = rest.at[pl.ds(pl.multiple_of(chips[n - 1] * 2 * half + (1 - s % 2) * half, 16), half), :]
            target = rest_other.at[n - 1]
        return pltpu.make_async_remote_copy(
            src_ref=source,
            dst_ref=target,
            send_sem=core_send.at[n],
            recv_sem=core_recv.at[n],
            device_id=(core, z),
            device_id_type=MESH,
        )

    def rest_load(q):
        source = rest.at[pl.ds(pl.multiple_of(chips[q] * 2 * half + s % 2 * half, 16), half), :]
        return pltpu.make_async_copy(
            source, held.at[q, :, pl.ds(rest_start, cols - rest_start)], load_sem.at[9 + q]
        )

    def turn(side):
        for q in range(4):
            source = left_now[side, :, pl.ds(pl.multiple_of(chips[q] * 2 * half, 128), 2 * half)]
            stage[...] = source.T
            turned[side, q * half : (q + 1) * half, :] = stage[
                pl.ds(pl.multiple_of(s % 2 * half, 16), half), :
            ]

    def multiply(q, side, first=0, last=None):
        right, start = ((both_now, 0), (mixed_now, lru2))[side]

        def one(turn, carry):
            here = pl.multiple_of(turn * 512, 512)
            block = mm(turned[side, q * half : (q + 1) * half, :], right[:, pl.ds(here, 512)], ((1,), (0,)))
            held[q, :, pl.ds(pl.multiple_of(start + here, 512), 512)] = block.astype(bf16)
            return carry

        lax.fori_loop(first // 512, (right.shape[1] if last is None else last) // 512, one, 0)

    def add_rest(q):
        rest_load(q).wait()
        push(1 + q).wait_recv()
        held[q, :, rest_start:] = add_low(held[q, :, rest_start:], rest_other[q])

    left, right = pl.ds(0, cut), pl.ds(cut, cols - cut)

    def block(q, i, side):
        return held.at[q, span(order[i]), side]

    def flow(i, index):
        send, recv = flow_send.at[i, index], flow_recv.at[i, index]
        to_beside, to_across = (beside, z), (across, z)
        if index == 0:
            return remote(block(chip_diag, i, left), cross.at[i, :, left], send, recv, to_across)
        if index == 1:
            return remote(block(chip_diag, i, right), cross.at[i, :, right], send, recv, to_beside)
        if index == 2:
            return remote(block(chip_beside, i, right), near.at[0, i, :, right], send, recv, to_beside)
        if index == 3:
            return remote(block(chip_beside, i, left), near.at[0, i, :, left], send, recv, to_beside)
        if index == 4:
            return remote(block(chip_across, i, left), near.at[1, i, :, left], send, recv, to_across)
        return remote(block(chip_across, i, right), near.at[1, i, :, right], send, recv, to_across)

    def cross_step(i):
        flow(i, 0).wait_recv()
        add_columns(held.at[chip_beside, span(order[i]), :], [cross.at[i]], 0, cut, 512)
        flow(i, 3).start()
        flow(i, 1).wait_recv()
        add_columns(held.at[chip_across, span(order[i]), :], [cross.at[i]], cut, cols - cut, 384)
        flow(i, 5).start()

    def near_step(i):
        for index in (2, 4, 3, 5):
            flow(i, index).wait_recv()
        add_columns(held.at[chip, span(order[i]), :], [near.at[0, i], near.at[1, i]], 0, cols, 640)

    def line(k, slot, target):
        return remote(
            held.at[chip, span(k), :], lined.at[slot], line_send.at[k], line_recv.at[slot], (s, target)
        )

    def absorb(k, slot, source):
        line(k, slot, source).wait_recv()
        add_columns(held.at[chip, span(k), :], [lined.at[slot]], 0, cols, 640)

    def chain(i):
        k = order[i]
        if i == 3:
            pl.when(z > 0)(lambda: absorb(k, k, z - 1))
            pl.when(z < 3)(lambda: absorb(k, 4, z + 1))
            return

        @pl.when(k > z)
        def _():
            pl.when(z > 0)(lambda: absorb(k, k, z - 1))
            line(k, k, z + 1).start()

        @pl.when(k < z)
        def _():
            pl.when(z < 3)(lambda: absorb(k, k, z + 1))
            pl.when(k == z - 1)(lambda: line(k, 4, z - 1).start())
            pl.when(k < z - 1)(lambda: line(k, k, z - 1).start())

    def chain_drain():
        for i in range(3):
            k = order[i]
            line(k, k, (z + 1) % 4).wait_send()

    def swap(k, high=False):
        to = (z + k) % 4
        here = pl.ds(pl.multiple_of(z * ff_part, 128), ff_part)
        source = (mlp_high if high else mlp_low).at[span(to % 2), :]
        return [
            remote(
                source.at[:, pl.ds(m * ff_part, ff_part)],
                mlp_back.at[m, :, here],
                swap_send.at[k - 1, m],
                swap_recv.at[k - 1, m],
                (s, to),
            )
            for m in range(3)
        ]

    def swap_start(k):
        to = (z + k) % 4

        @pl.when(to < 2)
        def _():
            for copy in swap(k):
                copy.start()

        @pl.when(to >= 2)
        def _():
            for copy in swap(k, True):
                copy.start()

    def own(high=False):
        here = pl.ds(pl.multiple_of(z * ff_part, 128), ff_part)
        source = (mlp_high if high else mlp_low).at[span(z % 2), :]
        return [
            pltpu.make_async_copy(source.at[:, pl.ds(m * ff_part, ff_part)], mlp_back.at[m, :, here], own_sem.at[m])
            for m in range(3)
        ]

    wide_rows = wide_now.shape[0]
    wide_tiles = mixer_w.shape[0] // wide_rows
    wide_start = mixer_w.shape[1] - lru2 - model
    wide_slots = (both_now.at[pl.ds(tok, wide_rows), :], wide_now)

    def wide(j):
        source = mixer_w.at[pl.ds(j * wide_rows, wide_rows), pl.ds(wide_start, lru2)]
        return pltpu.make_async_copy(source, wide_slots[j % 2], wide_sem.at[j % 2])

    plain_loads = [
        pltpu.make_async_copy(tokens, left_now.at[0, pl.ds(0, tok), :], wide_sem.at[2]),
        pltpu.make_async_copy(gain, gain_now, wide_sem.at[3]),
    ]

    def back(first, last):
        for j in range(first, last):
            wide(j).wait()
            back_now[:, pl.ds(j * wide_rows, wide_rows)] = mm(
                both_now[0:tok, :], wide_slots[j % 2][...], ((1,), (1,))
            )
            if j + 2 < wide_tiles:
                wide(j + 2).start()

    def finish_rows(turn, carry):
        at = pl.ds(pl.multiple_of(turn * 16, 16), 16)
        result = left_now[1, at, :].astype(f32) + norm_back(
            left_now[0, at, :].astype(f32), gain_now[GAIN_ONE : GAIN_ONE + 1, :], back_now[at, :]
        )
        left_now[0, at, :] = result.astype(bf16)
        return carry

    for copy in loads:
        copy.start()
    for q in range(4):
        rest_load(q).start()
    greet([(core, z), (beside, z), (across, z)] + [(s, (z + k) % 4) for k in range(1, 4)])
    for n in range(5):
        push(n).start()
    for k in (1, 3, 2):
        swap_start(k)

    @pl.when(z < 2)
    def _():
        for copy in own():
            copy.start()

    @pl.when(z >= 2)
    def _():
        for copy in own(True):
            copy.start()

    for copy in loads[:4]:
        copy.wait()
    turn(1)
    multiply(chip_diag, 1)
    for copy in loads[4:]:
        copy.wait()
    turn(0)
    multiply(chip_diag, 0, lru)
    add_rest(chip_diag)
    for i in range(2):
        flow(i, 1).start()
    push(0).wait_recv()
    multiply(chip_diag, 0, 0, lru)
    for i in range(2):
        flow(i, 0).start()
    for q in (chip_beside, chip_across, chip):
        multiply(q, 0)
        multiply(q, 1)
        add_rest(q)
        if q == chip_beside:
            flow(0, 2).start()
        if q == chip_across:
            flow(0, 4).start()
    for copy in plain_loads:
        copy.start()
    wide(0).start()
    wide(1).start()
    for i in range(4):
        cross_step(i)
        if i + 1 < 4:
            flow(i + 1, 2).start()
            flow(i + 1, 4).start()
        if i + 2 < 4:
            flow(i + 2, 0).start()
            flow(i + 2, 1).start()
        if i > 0:
            near_step(i - 1)
            chain(i - 1)
            back(wide_tiles * (i - 1) // 3, wide_tiles * i // 3)
    for copy in plain_loads:
        copy.wait()
    lax.fori_loop(0, tok // 16, finish_rows, 0)
    finished = pltpu.make_async_copy(left_now.at[0, pl.ds(0, tok), :], input_grad, wide_sem.at[2])
    finished.start()
    near_step(3)
    chain(3)
    done = pltpu.make_async_copy(held.at[chip, span(z), :], mixer_sum, own_sem.at[3])
    done.start()
    for i in range(4):
        for index in range(6):
            flow(i, index).wait_send()
    chain_drain()
    for k in range(1, 4):
        for copy in swap(k):
            copy.wait()
    for copy in own():
        copy.wait()
    for n in range(5):
        push(n).wait_send()
    finished.wait()
    done.wait()


def scatter(rows_pairs, grad_branch, rest, mlp_low, mlp_high, mixer_w, tokens, gain):
    tok, model = tokens.shape
    rows = model // 32
    lru = grad_branch.shape[1]
    cols = 3 * lru + rest.shape[1]
    ff_part = mlp_low.shape[1] // 3
    anyspec = pl.BlockSpec(memory_space=pl.ANY)
    dma = pltpu.SemaphoreType.DMA
    return pl.pallas_call(
        scatter_kernel,
        in_specs=[anyspec] * 15,
        out_specs=[anyspec] * 3,
        out_shape=[
            jax.ShapeDtypeStruct((rows, cols), bf16),
            jax.ShapeDtypeStruct((3, rows, 4 * ff_part), bf16),
            jax.ShapeDtypeStruct((tok, model), bf16),
        ],
        scratch_shapes=[
            pltpu.VMEM((4, 4 * rows, cols), bf16),
            pltpu.VMEM((4, rows, cols), bf16),
            pltpu.VMEM((2, 4, rows, cols), bf16),
            pltpu.VMEM((5, rows, cols), bf16),
            pltpu.VMEM((2, 2 * tok, model), bf16),
            pltpu.VMEM((2 * tok, 2 * lru), bf16),
            pltpu.VMEM((2 * tok, lru), bf16),
            pltpu.VMEM((2, 16 * rows, 2 * tok), bf16),
            pltpu.VMEM((8 * rows, 2 * tok), bf16),
            pltpu.VMEM((4, 4 * rows, rest.shape[1]), bf16),
            pltpu.VMEM((tok, model), f32),
            pltpu.VMEM((128, 2 * lru), bf16),
            pltpu.VMEM(gain.shape, f32),
            dma((13,)), dma((5,)), dma((5,)), dma((4,)),
            dma((4, 6)), dma((4, 6)), dma((4,)), dma((5,)), dma((3, 3)), dma((3, 3)), dma((4,)),
        ],
        compiler_params=pltpu.CompilerParams(
            collective_id=2, has_side_effects=True, vmem_limit_bytes=62 * 1024 * 1024
        ),
        name="scatter_gradients",
    )(*rows_pairs, grad_branch, rest, mlp_low, mlp_high, mixer_w, tokens, gain)


def gather_plain(mixer, gate, up, down):
    groups = lax.axis_size("fsdp")
    part_rows, ff = gate.shape
    own = jnp.stack([w.reshape(part_rows, groups, ff // groups) for w in (gate, up, down)], axis=2)
    mine = lax.all_to_all(jnp.transpose(own, (1, 0, 2, 3)), "fsdp", 0, 0, tiled=True)
    return lax.all_gather(mixer, both, axis=0, tiled=True), mine.reshape(groups * part_rows, -1)


def from_line(shard):
    count = lax.axis_size("fsdp")
    return [shard] + [
        lax.ppermute(shard, "fsdp", [(i, (i + k) % count) for i in range(count)]) for k in range(1, count)
    ]


def swap_cores(shard):
    count = lax.axis_size("seq")
    return lax.ppermute(shard, "seq", [(i, i + 1 - 2 * (i % 2)) for i in range(count)])


def swap_beside(shard):
    return lax.ppermute(shard, "seq", [(i, i ^ 2) for i in range(8)])


def swap_across(shard):
    return lax.ppermute(shard, "seq", [(i, i ^ 4) for i in range(8)])


def add_low(left, right):
    return (left.astype(f32) + right.astype(f32)).astype(bf16)


def scatter_plain(normed, grad_both, grad_mix, mixed, rest, mlp_sum):
    groups = lax.axis_size("fsdp")
    term_wide = mm(normed, grad_both, ((0,), (0,))).astype(bf16)
    term_out = mm(grad_mix, mixed, ((0,), (0,))).astype(bf16)
    mixer_sum = lax.psum_scatter(
        jnp.concatenate([term_wide, term_out, rest], axis=1), "seq", scatter_dimension=0, tiled=True
    )
    mixer_sum = lax.psum_scatter(mixer_sum, "fsdp", scatter_dimension=0, tiled=True)
    ff_part = mlp_sum.shape[1] // 3
    part_rows = mlp_sum.shape[0] // groups
    mlp_sum = mlp_sum.reshape(groups, part_rows, 3, ff_part)
    mlp_back = lax.all_to_all(mlp_sum, "fsdp", 0, 0, tiled=True)
    mlp_back = jnp.transpose(mlp_back, (2, 1, 0, 3)).reshape(3, part_rows, groups * ff_part)
    return mixer_sum, mlp_back


def call_heads(kernel, width, heads, ins, outs, scratch, name):
    def spec(rows, place):
        if place is None:
            return pl.BlockSpec((rows, width), lambda h: (0, h))
        return pl.BlockSpec((width, width), lambda h: (h, place))

    in_specs = [spec(a.shape[0], place) for a, place in ins]
    out_specs = [spec(rows, 0 if rowwise else None) for rows, _, rowwise in outs]
    out_shape = [
        jax.ShapeDtypeStruct((heads * width, width) if rowwise else (rows, heads * width), kind)
        for rows, kind, rowwise in outs
    ]
    return pl.pallas_call(
        kernel,
        grid=(heads,),
        in_specs=in_specs,
        out_specs=out_specs,
        out_shape=out_shape,
        scratch_shapes=[pltpu.VMEM((rows, width), f32) for rows in scratch],
        compiler_params=pltpu.CompilerParams(vmem_limit_bytes=16 * 1024 * 1024),
        cost_estimate=pl.CostEstimate(flops=1, bytes_accessed=1, transcendentals=0),
        name=name,
    )(*[a for a, _ in ins])


def on_device(
    block_input,
    cotangent,
    mixer_gain,
    branch_proj,
    gelu_proj,
    conv_taps,
    conv_bias,
    rate_blocks,
    input_blocks,
    rate_bias,
    input_bias,
    decay_param,
    out_proj,
    mlp_gain,
    gate_proj,
    up_proj,
    down_proj,
):
    groups = lax.axis_size("fsdp")
    part_rows, lru = branch_proj.shape
    width = rate_blocks.shape[1]
    heads = lru // width
    margin = conv_taps.shape[0] - 1
    tokens = block_input[0].astype(f32)
    tok_count, model = tokens.shape
    ff = gate_proj.shape[1]
    ff_part = ff // groups
    grad_out = cotangent[0]

    smalls = jnp.stack(
        [conv_taps[k] for k in range(margin + 1)]
        + [conv_bias, rate_bias, input_bias, decay_param, mixer_gain, mlp_gain],
        axis=1,
    )
    small_count = smalls.shape[1]
    smalls = jnp.pad(smalls, ((0, 0), (0, 128 - small_count)))
    first_own = jnp.concatenate([rate_blocks, input_blocks, smalls], axis=1)
    mixer_own = (first_own, branch_proj, gelu_proj, out_proj)
    custom = lax.axis_size("seq") == 8 and groups == 4
    if custom:
        mixer_w, mlp_mine = gather(*mixer_own, gate_proj, up_proj, down_proj)
    else:
        mixer_w, mlp_mine = gather_plain(jnp.concatenate(mixer_own, axis=1), gate_proj, up_proj, down_proj)
    mlp_w = lax.all_gather(mlp_mine, "seq", axis=0, tiled=True)
    grad_out_late = lax.optimization_barrier((grad_out, mlp_mine))[0]
    if custom:
        grad_pieces = from_line(grad_out_late)
    wide = mixer_w[:, 128 + 2 * width : 128 + 2 * width + 2 * lru]
    proj_out = mixer_w[:, 128 + 2 * width + 2 * lru :]

    small = small_table(mixer_w, 2 * width // 128)
    gain_one, gain_two = small[GAIN_ONE], small[GAIN_TWO]

    normed, branch, gelu_pre = mixer_in(block_input[0], small, mixer_w, lru, 2 * width + 128)
    prior = from_behind(branch[tok_count - margin :], "seq", 1).astype(f32)
    prior = jnp.concatenate([jnp.zeros((8 - margin, lru), f32), prior], axis=0)
    conv, rate_pre, input_pre, cum, local = call_heads(
        mixer_forward,
        width,
        heads,
        [(branch, None), (prior, None), (small, None), (mixer_w, 0), (mixer_w, 1)],
        [(tok_count, bf16, False)] + [(tok_count, f32, False)] * 4,
        [tok_count + 8],
        "mixer_forward",
    )
    carried = prefix((cum[-1], local[-1]), "seq", False)
    states = local + cum * carried[None]
    mixed = (states * jax.nn.gelu(gelu_pre, approximate=True)).astype(bf16)
    middle = tokens + mm(mixed, proj_out, ((1,), (1,)))
    normed_two = norm_rows(middle, gain_two).astype(bf16)

    if custom:
        normed_all, normed_other, grad_out_all, grad_out_other, first_other, mixed_other = gather_rows(
            normed_two, grad_pieces, normed, mixed
        )
    else:
        normed_all = lax.all_gather(normed_two, "fsdp", axis=0, tiled=True)
        grad_out_all = lax.all_gather(grad_out_late, "fsdp", axis=0, tiled=True)
    w_gate, w_up, w_down = mlp_w[:, :ff_part], mlp_w[:, ff_part : 2 * ff_part], mlp_w[:, 2 * ff_part :]
    if custom:
        hidden, hidden_other, grad_pair, pair_other, grad_normed_part = feed_forward(
            normed_all, grad_out_all, mlp_w
        )
    else:
        gate = mm(normed_all, w_gate, ((1,), (0,)))
        up_val = mm(normed_all, w_up, ((1,), (0,)))
        gelu_gate, gelu_slope = gelu_parts(gate)
        hidden = (gelu_gate * up_val).astype(bf16)
        grad_hidden = mm(grad_out_all, w_down, ((1,), (0,)))
        grad_gate = (grad_hidden * up_val * gelu_slope).astype(bf16)
        grad_up = (grad_hidden * gelu_gate).astype(bf16)
        grad_normed_part = (
            mm(grad_gate, w_gate, ((1,), (1,))) + mm(grad_up, w_up, ((1,), (1,)))
        ).astype(bf16)
    grad_normed_two = lax.psum_scatter(grad_normed_part, "fsdp", scatter_dimension=0, tiled=True)
    if custom:
        half = model // 16
        beside_high, across_low, mine, beside_low, across_high, out_part = shared_products(
            (normed_all, normed_other, grad_out_all, grad_out_other),
            mlp_w,
            (grad_pair, pair_other),
            (hidden, hidden_other),
        )
        from_beside_high, from_across_low = swap_beside(beside_high), swap_across(across_low)
    else:
        grad_pair = jnp.concatenate([grad_gate, grad_up], axis=1)
        term_pair = mm(normed_all, grad_pair, ((0,), (0,))).astype(bf16)
        term_down = mm(grad_out_all, hidden, ((0,), (0,))).astype(bf16)
        pair_sum = lax.psum_scatter(term_pair, "seq", scatter_dimension=0, tiled=True)
        down_sum = lax.psum_scatter(term_down, "seq", scatter_dimension=0, tiled=True)
        mlp_sum = jnp.concatenate([pair_sum, down_sum], axis=1)
        out_part = mm(hidden, w_down, ((1,), (1,))).astype(bf16)
    out_sum = lax.psum_scatter(out_part, "fsdp", scatter_dimension=0, tiled=True)
    grad_normed_two = grad_normed_two.astype(f32)

    grad_middle = grad_out.astype(f32) + norm_back(middle, gain_two, grad_normed_two)
    grad_mix = grad_middle.astype(bf16)
    if custom:
        mix_other = swap_cores(grad_mix)
    grad_mixed = mm(grad_mix, proj_out, ((1,), (0,)))
    carried_rows = jnp.broadcast_to(carried[None], (8, lru))
    grad_gelu_pre, rev_cum, rev_grad, pair_grad = call_heads(
        mixer_backward_scan,
        width,
        heads,
        [(a, None) for a in (grad_mixed, gelu_pre, rate_pre, cum, local, carried_rows, small)],
        [(tok_count, bf16, False), (tok_count, f32, False), (tok_count, f32, False), (8, f32, False)],
        [tok_count + 8],
        "mixer_backward_scan",
    )
    if custom:
        from_beside_high, from_across_low, pair_grad = lax.optimization_barrier(
            (from_beside_high, from_across_low, pair_grad)
        )
    if custom:
        gelu_other = swap_cores(grad_gelu_pre)
    incoming = prefix((cum[-1], pair_grad[0]), "seq", True)
    if custom:
        beside_low, across_high, incoming = lax.optimization_barrier((beside_low, across_high, incoming))
        from_beside_low, from_across_high = swap_beside(beside_low), swap_across(across_high)
    incoming_rows = jnp.broadcast_to(incoming[None], (8, lru))
    own, head, rate_w_grad, input_w_grad, sums = call_heads(
        mixer_backward,
        width,
        heads,
        [
            (a, None)
            for a in (rev_cum, rev_grad, incoming_rows, cum, local, carried_rows, rate_pre, input_pre, conv, branch, prior, small)
        ]
        + [(mixer_w, 0), (mixer_w, 1)],
        [(tok_count, f32, False), (8, f32, False), (0, bf16, True), (0, bf16, True), (8, f32, False)],
        [tok_count + 8, tok_count + 16],
        "mixer_backward",
    )
    received = from_behind(head[8 - margin :], "seq", -1)
    grad_branch = jnp.concatenate(
        [own[: tok_count - margin], own[tok_count - margin :] + received], axis=0
    ).astype(bf16)
    grad_both = jnp.concatenate([grad_branch, grad_gelu_pre], axis=1)
    vectors = jnp.pad(sums.T, ((0, 0), (0, 128 - sums.shape[0]))).astype(bf16)
    rest = jnp.concatenate([rate_w_grad, input_w_grad, vectors], axis=1)
    if custom:
        low, high = [
            sum(part.astype(f32) for part in parts).astype(bf16)
            for parts in (
                (mine[:half], from_across_low, from_beside_low),
                (mine[half:], from_across_high, from_beside_high),
            )
        ]
        mixer_sum, mlp_back, input_grad = scatter(
            (normed, first_other, grad_mix, mix_other, mixed, mixed_other, grad_gelu_pre, gelu_other),
            grad_branch, rest, low, high, mixer_w, block_input[0], small,
        )
    else:
        mixer_sum, mlp_back = scatter_plain(normed, grad_both, grad_mix, mixed, rest, mlp_sum)
        grad_normed = mm(grad_both, wide, ((1,), (1,)))
        input_grad = (grad_middle + norm_back(tokens, gain_one, grad_normed)).astype(bf16)
    input_grad = input_grad[None]
    middle = lax.optimization_barrier((middle, mixer_sum))[0]
    block_output = (middle + out_sum.astype(f32)).astype(bf16)[None]
    edge = 3 * lru + 2 * width
    vec = mixer_sum[:, edge:].astype(f32).T
    weight_grads = list(
        jnp.split(mixer_sum[:, :edge].astype(f32), [lru, 2 * lru, 3 * lru, 3 * lru + width], axis=1)
    ) + [mlp_back[m].astype(f32) for m in range(3)]
    first_total = gain_back((branch_proj, weight_grads[0]), (gelu_proj, weight_grads[1]))
    second_total = gain_back((gate_proj, weight_grads[5]), (up_proj, weight_grads[6]))
    dbranch, dgelu, dout, drate, dinput, dgate, dup, ddown = weight_grads
    return (
        block_output,
        input_grad,
        first_total / mixer_gain.astype(f32),
        dbranch,
        dgelu,
        vec[: margin + 1],
        vec[7],
        drate,
        dinput,
        vec[4],
        vec[5],
        vec[6],
        dout,
        second_total / mlp_gain.astype(f32),
        dgate,
        dup,
        ddown,
    )


def solution(mesh):
    tokens = P("fsdp", "seq", None)
    vector = P(both)
    matrix = P(both, None)
    taps = P(None, both)
    return jax.shard_map(
        on_device,
        mesh=mesh,
        in_specs=(
            tokens, tokens, vector, matrix, matrix, taps, vector, matrix, matrix,
            vector, vector, vector, matrix, vector, matrix, matrix, matrix,
        ),
        out_specs=(
            tokens, tokens, vector, matrix, matrix, taps, vector, matrix, matrix,
            vector, vector, vector, matrix, vector, matrix, matrix, matrix,
        ),
        check_vma=False,
    )
```

```python
import functools

import jax
import jax.numpy as jnp
from jax import lax
from jax.experimental import pallas as pl
from jax.experimental.pallas import tpu as pltpu
from jax.sharding import PartitionSpec as P

epsilon = 1e-06
f32 = jnp.float32
bf16 = jnp.bfloat16
both = ("seq", "fsdp")
MESH = pl.DeviceIdType.MESH
TAP, CONV_BIAS, RATE_BIAS, INPUT_BIAS, SOFT, SOFT_SLOPE, GAIN_ONE, GAIN_TWO = 0, 4, 5, 6, 7, 8, 9, 10
GELU_C = 0.7978845608028654
GELU_A = 0.044715


def from_behind(shard, axis, by):
    devices = lax.axis_size(axis)
    pairs = [(i, i + by) for i in range(devices) if 0 <= i + by < devices]
    return lax.ppermute(shard, axis, pairs)


def prefix(part, axis, reverse):
    count = lax.axis_size(axis)
    place = lax.axis_index(axis)
    gathered = lax.all_gather(jnp.stack(part), axis)
    state = jnp.zeros_like(part[1])
    for hop in range(count):
        source = count - 1 - hop if reverse else hop
        ahead = source > place if reverse else source < place
        state = jnp.where(ahead, gathered[source, 1] + gathered[source, 0] * state, state)
    return state


def norm_rows(values, scales):
    return values * lax.rsqrt(jnp.mean(values * values, axis=-1, keepdims=True) + epsilon) * scales


def norm_back(values, scales, grads):
    inverse = lax.rsqrt(jnp.mean(values * values, axis=-1, keepdims=True) + epsilon)
    scaled = grads * scales
    shared = jnp.mean(values * scaled, axis=-1, keepdims=True)
    return inverse * scaled - values * (inverse * inverse * inverse * shared)


def gain_back(*pairs):
    return sum(jnp.sum(weight.astype(f32) * grad, axis=1) for weight, grad in pairs)


def gelu_parts(x):
    square = x * x
    inner = jnp.tanh(x * (GELU_C + GELU_C * GELU_A * square))
    open_part = 0.5 + 0.5 * inner
    value = x * open_part
    return value, open_part + value * (1.0 - inner) * (GELU_C + 3.0 * GELU_C * GELU_A * square)


def mm(left, right, dims):
    return lax.dot_general(left, right, (dims, ((), ())), preferred_element_type=f32)


def sigmoid(x):
    return 1.0 / (1.0 + jnp.exp(-x))


def scan_rows(decay, value, reverse):
    rows = decay.shape[0]
    place = lax.broadcasted_iota(jnp.int32, decay.shape, 0)
    step = 1
    while step < rows:
        shift = rows - step if reverse else step
        inside = place < rows - step if reverse else place >= step
        before_value = jnp.where(inside, pltpu.roll(value, shift, 0), 0.0)
        before_decay = jnp.where(inside, pltpu.roll(decay, shift, 0), 1.0)
        value = value + decay * before_value
        decay = decay * before_decay
        step *= 2
    return decay, value


def gates(rate_pre, input_pre, soft):
    rate = sigmoid(rate_pre)
    log_decay = -8.0 * rate * soft
    decay = jnp.exp(log_decay)
    square = decay * decay
    root = jnp.sqrt(-jnp.tanh(log_decay) * (1.0 + square))
    return rate, decay, square, root, sigmoid(input_pre)


def table_kernel(columns, table):
    rows = columns[...].T[0:16, :].astype(f32)
    decay_param = rows[7:8, :]
    fast = jnp.exp(-decay_param)
    table[0:7, :] = rows[0:7, :]
    table[7:8, :] = jnp.log1p(fast)
    table[8:9, :] = -fast / (1.0 + fast)
    table[9:11, :] = rows[8:10, :]
    table[11:16, :] = jnp.zeros((5, rows.shape[1]), f32)


def small_table(mixer_w, block):
    model = mixer_w.shape[0]
    return pl.pallas_call(
        table_kernel,
        grid=(1,),
        in_specs=[pl.BlockSpec((model, 128), lambda i: (0, block))],
        out_specs=pl.BlockSpec((16, model), lambda i: (0, 0)),
        out_shape=jax.ShapeDtypeStruct((16, model), f32),
        name="small_table",
    )(mixer_w)


def mixer_in_kernel(tokens, table, weights, normed, branch, gelu_pre):
    step = pl.program_id(0)

    @pl.when(step == 0)
    def _():
        normed[...] = norm_rows(tokens[...].astype(f32), table[GAIN_ONE : GAIN_ONE + 1, :]).astype(bf16)

    product = mm(normed[...], weights[...], ((1,), (0,)))
    half = pl.num_programs(0) // 2

    @pl.when(step < half)
    def _():
        branch[...] = product.astype(bf16)

    @pl.when(step >= half)
    def _():
        gelu_pre[...] = product


def mixer_in(tokens, table, mixer_w, lru, start):
    tok, model = tokens.shape
    tile = start
    tiles = lru // tile
    return pl.pallas_call(
        mixer_in_kernel,
        grid=(2 * tiles,),
        in_specs=[
            pl.BlockSpec((tok, model), lambda j: (0, 0)),
            pl.BlockSpec(table.shape, lambda j: (0, 0)),
            pl.BlockSpec((model, tile), lambda j: (0, 1 + j)),
        ],
        out_specs=[
            pl.BlockSpec((tok, model), lambda j: (0, 0)),
            pl.BlockSpec((tok, tile), lambda j: (0, jnp.minimum(j, tiles - 1))),
            pl.BlockSpec((tok, tile), lambda j: (0, jnp.maximum(j - tiles, 0))),
        ],
        out_shape=[
            jax.ShapeDtypeStruct((tok, model), bf16),
            jax.ShapeDtypeStruct((tok, lru), bf16),
            jax.ShapeDtypeStruct((tok, lru), f32),
        ],
        compiler_params=pltpu.CompilerParams(vmem_limit_bytes=16 * 1024 * 1024),
        cost_estimate=pl.CostEstimate(flops=1, bytes_accessed=1, transcendentals=0),
        name="mixer_in",
    )(tokens, table, mixer_w)


def mixer_forward(branch, prior, small, rate_w, input_w, conv, rate_pre, input_pre, cum, local, ext):
    rows = branch.shape[0]
    ext[0:8, :] = prior[...]
    ext[8:, :] = branch[...].astype(f32)
    total = small[CONV_BIAS : CONV_BIAS + 1, :] + small[TAP : TAP + 1, :] * ext[8:, :]
    for offset in range(1, 4):
        total = total + small[TAP + offset : TAP + offset + 1, :] * ext[pl.ds(8 - offset, rows), :]
    low = total.astype(bf16)
    conv[...] = low
    rate = mm(low, rate_w[...], ((1,), (0,))) + small[RATE_BIAS : RATE_BIAS + 1, :]
    inp = mm(low, input_w[...], ((1,), (0,))) + small[INPUT_BIAS : INPUT_BIAS + 1, :]
    rate_pre[...] = rate
    input_pre[...] = inp
    _, decay, _, root, opened = gates(rate, inp, small[SOFT : SOFT + 1, :])
    product, states = scan_rows(decay, root * opened * low.astype(f32), False)
    cum[...] = product
    local[...] = states


def mixer_backward_scan(grad_mixed, gelu_pre, rate_pre, cum, local, carried, small, grad_pre, rev_cum, rev_grad, pair, ext):
    rows = grad_mixed.shape[0]
    states = local[...] + cum[...] * carried[0:1, :]
    value, slope = gelu_parts(gelu_pre[...])
    grad = grad_mixed[...]
    grad_pre[...] = (grad * states * slope).astype(bf16)
    decay = jnp.exp(-8.0 * sigmoid(rate_pre[...]) * small[SOFT : SOFT + 1, :])
    ext[0:rows, :] = decay
    ext[rows:, :] = jnp.ones((8, decay.shape[1]), f32)
    product, back = scan_rows(ext[pl.ds(1, rows), :], grad * value, True)
    rev_cum[...] = product
    rev_grad[...] = back
    pair[...] = jnp.broadcast_to(decay[0:1, :] * back[0:1, :], pair.shape)


def mixer_backward(
    rev_cum, rev_grad, incoming, cum, local, carried, rate_pre, input_pre, conv, branch, prior, small, rate_w, input_w,
    own, head, rate_w_grad, input_w_grad, sums, ext, gext,
):
    rows = rev_cum.shape[0]
    soft = small[SOFT : SOFT + 1, :]
    grad_states = rev_grad[...] + rev_cum[...] * incoming[0:1, :]
    rate, decay, square, root, opened = gates(rate_pre[...], input_pre[...], soft)
    ext[0:8, :] = jnp.broadcast_to(carried[0:1, :], (8, carried.shape[1]))
    ext[8:, :] = local[...] + cum[...] * carried[0:1, :]
    before = ext[pl.ds(7, rows), :]
    low = conv[...]
    conv_in = low.astype(f32)
    grad_log = grad_states * decay * before - grad_states * opened * conv_in * square / root
    driven = grad_states * root
    grad_input = (driven * conv_in * opened * (1.0 - opened)).astype(bf16)
    by_rate = grad_log * (-8.0 * rate)
    grad_rate = (by_rate * soft * (1.0 - rate)).astype(bf16)
    sums[6:7, :] = jnp.sum(by_rate, axis=0, keepdims=True) * small[SOFT_SLOPE : SOFT_SLOPE + 1, :]
    sums[4:5, :] = jnp.sum(grad_rate.astype(f32), axis=0, keepdims=True)
    sums[5:6, :] = jnp.sum(grad_input.astype(f32), axis=0, keepdims=True)
    rate_w_grad[...] = mm(low, grad_rate, ((0,), (0,))).astype(rate_w_grad.dtype)
    input_w_grad[...] = mm(low, grad_input, ((0,), (0,))).astype(input_w_grad.dtype)
    grad_conv = (
        driven * opened
        + mm(grad_rate, rate_w[...], ((1,), (1,)))
        + mm(grad_input, input_w[...], ((1,), (1,)))
    )
    sums[7:8, :] = jnp.sum(grad_conv, axis=0, keepdims=True)
    ext[0:8, :] = prior[...]
    ext[8:, :] = branch[...].astype(f32)
    gext[0:8, :] = jnp.zeros((8, grad_conv.shape[1]), f32)
    gext[8 : 8 + rows, :] = grad_conv
    gext[8 + rows :, :] = jnp.zeros((8, grad_conv.shape[1]), f32)
    back = jnp.zeros_like(grad_conv)
    front = jnp.zeros((8, grad_conv.shape[1]), f32)
    for offset in range(4):
        tap = small[TAP + offset : TAP + offset + 1, :]
        sums[offset : offset + 1, :] = jnp.sum(
            grad_conv * ext[pl.ds(8 - offset, rows), :], axis=0, keepdims=True
        )
        back = back + tap * gext[pl.ds(8 + offset, rows), :]
        front = front + tap * gext[pl.ds(offset, 8), :]
    own[...] = back
    head[...] = front


def places():
    s = lax.axis_index("seq")
    z = lax.axis_index("fsdp")
    core = s + 1 - 2 * (s % 2)
    beside = s + 2 - 4 * ((s // 2) % 2)
    across = s + 4 - 8 * (s // 4)
    return s, z, core, beside, across


def greet(peers):
    barrier = pltpu.get_barrier_semaphore()
    for peer in peers:
        pl.semaphore_signal(barrier, inc=1, device_id=peer, device_id_type=MESH)
    pl.semaphore_wait(barrier, len(peers))


def gather_kernel(
    first, branch, gelu, outer, gate, up, down, mixer_all, mlp_mine,
    mixer, load_sem, flow_send, flow_recv, line_send, line_recv, swap_send, swap_recv, own_sem,
):
    s, z, core, beside, across = places()
    rows, cols = mixer.shape
    ff_part = mlp_mine.shape[1] // 3
    cut = cols // 256 * 128
    diag = beside + across - s
    loads, start = [], 0
    for n, part in enumerate((first, branch, gelu, outer)):
        size = part.shape[1]
        loads.append(pltpu.make_async_copy(part, mixer.at[:, pl.ds(start, size)], load_sem.at[n]))
        loads[-1].start()
        start += size
    greet([(core, z), (beside, z), (across, z)] + [(s, (z + k) % 4) for k in range(1, 4)])

    def remote(src, dst, send, recv, target):
        return pltpu.make_async_remote_copy(
            src_ref=src, dst_ref=dst, send_sem=send, recv_sem=recv, device_id=target, device_id_type=MESH
        )

    def piece(seq, zz, half=None):
        span = pl.ds(pl.multiple_of((seq * 4 + zz) * rows, 16), rows)
        if half is None:
            return mixer_all.at[span, :]
        return mixer_all.at[span, pl.ds(0, cut) if half == 0 else pl.ds(cut, cols - cut)]

    def flow(zz, index, seq, half, target, src=None):
        ref = piece(seq, zz, half)
        return remote(
            ref if src is None else src, ref, flow_send.at[zz, index], flow_recv.at[zz, index], (target, z)
        )

    def sends(zz, src=None):
        return [
            flow(zz, 0, s, None, beside, src),
            flow(zz, 1, s, None, across, src),
            flow(zz, 4, s, None, core, src),
        ]

    def spread(zz, src=None):
        for copy in sends(zz, src):
            copy.start()

    def relay(zz):
        flow(zz, 0, beside, None, beside).wait_recv()
        flow(zz, 3, beside, 0, across).start()
        flow(zz, 5, beside, None, core).start()
        flow(zz, 1, across, None, across).wait_recv()
        flow(zz, 2, across, 1, beside).start()
        flow(zz, 6, across, None, core).start()

    def finish(zz):
        flow(zz, 3, diag, 0, across).wait_recv()
        flow(zz, 7, diag, 0, core).start()
        flow(zz, 2, diag, 1, beside).wait_recv()
        flow(zz, 8, diag, 1, core).start()

    def drain(zz, src=None):
        for copy in sends(zz, src):
            copy.wait_send()
        flow(zz, 3, beside, 0, across).wait_send()
        flow(zz, 5, beside, None, core).wait_send()
        flow(zz, 2, across, 1, beside).wait_send()
        flow(zz, 6, across, None, core).wait_send()
        flow(zz, 7, diag, 0, core).wait_send()
        flow(zz, 8, diag, 1, core).wait_send()
        flip = core - s
        flow(zz, 4, core, None, core).wait_recv()
        flow(zz, 5, beside + flip, None, core).wait_recv()
        flow(zz, 6, across + flip, None, core).wait_recv()
        flow(zz, 7, diag + flip, 0, core).wait_recv()
        flow(zz, 8, diag + flip, 1, core).wait_recv()

    def line(zz, up_way, hop, src=None):
        ref = piece(s, zz)
        way = 0 if up_way else 1
        target = z + 1 if up_way else z - 1
        return remote(
            ref if src is None else src, ref, line_send.at[way, hop], line_recv.at[way, hop], (s, target)
        )

    def line_hop(hop):
        def below():
            line(z - hop, True, hop - 1).wait_recv()
            pl.when(z < 3)(lambda: line(z - hop, True, hop).start())

        def above():
            line(z + hop, False, hop - 1).wait_recv()
            pl.when(z > 0)(lambda: line(z + hop, False, hop).start())

        pl.when(z >= hop)(below)
        pl.when(z + hop <= 3)(above)

    def at_hop(hop, act):
        pl.when(z >= hop)(lambda: act(z - hop))
        pl.when(z + hop <= 3)(lambda: act(z + hop))

    def landing(m, zz):
        return mlp_mine.at[pl.ds(pl.multiple_of(zz * rows, 16), rows), pl.ds(m * ff_part, ff_part)]

    def columns(m, zz):
        return (gate, up, down)[m].at[:, pl.ds(pl.multiple_of(zz * ff_part, 128), ff_part)]

    def swap(k, m, arriving=False):
        to = (z + k) % 4
        came = (z + 4 - k) % 4
        return remote(
            columns(m, to), landing(m, came if arriving else z), swap_send.at[k - 1, m], swap_recv.at[k - 1, m], (s, to)
        )

    local = [pltpu.make_async_copy(columns(m, z), landing(m, z), own_sem.at[m]) for m in range(3)]
    local.append(pltpu.make_async_copy(mixer, piece(s, z), own_sem.at[3]))
    for copy in loads:
        copy.wait()

    pl.when(z < 3)(lambda: line(z, True, 0, mixer).start())
    pl.when(z > 0)(lambda: line(z, False, 0, mixer).start())
    spread(z, mixer)
    for copy in local:
        copy.start()
    line_hop(1)
    at_hop(1, spread)
    relay(z)
    line_hop(2)
    at_hop(2, spread)
    finish(z)
    at_hop(1, relay)
    line_hop(3)
    at_hop(3, spread)
    for k in (1, 3, 2):
        for m in range(3):
            swap(k, m).start()
    at_hop(1, finish)
    at_hop(2, relay)
    at_hop(3, relay)
    at_hop(2, finish)
    at_hop(3, finish)
    drain(z, mixer)
    for hop in range(1, 4):
        at_hop(hop, drain)
    for copy in local:
        copy.wait()
    for k in (1, 3, 2):
        for m in range(3):
            swap(k, m).wait_send()
            swap(k, m, True).wait_recv()
    pl.when(z < 3)(lambda: line(z, True, 0, mixer).wait_send())
    pl.when(z > 0)(lambda: line(z, False, 0, mixer).wait_send())
    for hop in range(1, 3):
        pl.when((z >= hop) & (z < 3))(lambda: line(z - hop, True, hop).wait_send())
        pl.when((z + hop <= 3) & (z > 0))(lambda: line(z + hop, False, hop).wait_send())


def gather(first, branch, gelu, outer, gate, up, down):
    rows = first.shape[0]
    cols = first.shape[1] + branch.shape[1] + gelu.shape[1] + outer.shape[1]
    ff_part = gate.shape[1] // 4
    anyspec = pl.BlockSpec(memory_space=pl.ANY)
    dma = pltpu.SemaphoreType.DMA
    return pl.pallas_call(
        gather_kernel,
        in_specs=[anyspec] * 7,
        out_specs=[anyspec] * 2,
        out_shape=[
            jax.ShapeDtypeStruct((32 * rows, cols), bf16),
            jax.ShapeDtypeStruct((4 * rows, 3 * ff_part), bf16),
        ],
        scratch_shapes=[
            pltpu.VMEM((rows, cols), bf16), dma((4,)),
            dma((4, 9)), dma((4, 9)), dma((2, 3)), dma((2, 3)), dma((3, 3)), dma((3, 3)), dma((4,)),
        ],
        compiler_params=pltpu.CompilerParams(collective_id=1, has_side_effects=True),
        name="gather_weights",
    )(first, branch, gelu, outer, gate, up, down)


def rows_kernel(
    normed, grad0, grad1, grad2, grad3, first, mixed, normed_all, normed_other, grad_all, grad_other,
    first_other, mixed_other, line_send, line_recv, core_send, core_recv, own_sem, held, give_send, give_recv,
):
    s, z, core, _, _ = places()
    tok = normed.shape[0]
    cuts = 4
    grads = (grad0, grad1, grad2, grad3)
    greet([(core, z)] + [(s, (z + k) % 4) for k in range(1, 4)])

    def rows(ref, zz):
        return ref.at[pl.ds(pl.multiple_of(zz * tok, 16), tok), :]

    def remote(src, dst, send, recv, target):
        return pltpu.make_async_remote_copy(
            src_ref=src, dst_ref=dst, send_sem=send, recv_sem=recv, device_id=target, device_id_type=MESH
        )

    def parts(ref):
        size = tok // cuts
        return [ref.at[pl.ds(n * size, size), :] for n in range(cuts)]

    def line(zz, up_way, hop):
        way = 0 if up_way else 1
        target = z + 1 if up_way else z - 1
        src = normed if hop == 0 else rows(normed_all, zz)
        dst = rows(normed_all, zz)
        return [
            remote(a, b, line_send.at[way, hop, n], line_recv.at[way, hop, n], (s, target))
            for n, (a, b) in enumerate(zip(parts(src), parts(dst)))
        ]

    def over(zz, own=False):
        src = normed if own else rows(normed_all, zz)
        return remote(src, rows(normed_other, zz), core_send.at[0, zz], core_recv.at[0, zz], (core, z))

    def grad_over(k):
        zz = (z + 4 - k) % 4
        return remote(grads[k], rows(grad_other, zz), core_send.at[1, zz], core_recv.at[1, zz], (core, z))

    def line_start(zz, up_way, hop):
        for copy in line(zz, up_way, hop):
            copy.start()

    def line_drain(zz, up_way, hop):
        for copy in line(zz, up_way, hop):
            copy.wait_send()

    def hop_step(hop):
        def below():
            for came, on in zip(line(z - hop, True, hop - 1), line(z - hop, True, hop) if hop < 3 else [None] * cuts):
                came.wait_recv()
                if on is not None:
                    pl.when(z < 3)(on.start)
            over(z - hop).start()

        def above():
            for came, on in zip(line(z + hop, False, hop - 1), line(z + hop, False, hop) if hop < 3 else [None] * cuts):
                came.wait_recv()
                if on is not None:
                    pl.when(z > 0)(on.start)
            over(z + hop).start()

        pl.when(z >= hop)(below)
        pl.when(z + hop <= 3)(above)

    given = [
        remote(source, target, give_send.at[n], give_recv.at[n], (core, z))
        for n, (source, target) in enumerate(((first, first_other), (mixed, mixed_other)))
    ]
    local = [pltpu.make_async_copy(grads[k], held.at[k], own_sem.at[k]) for k in range(4)]
    local.append(pltpu.make_async_copy(normed, held.at[4], own_sem.at[4]))
    stored = [
        pltpu.make_async_copy(held.at[k], rows(grad_all, (z + 4 - k) % 4), own_sem.at[k]) for k in range(4)
    ]
    stored.append(pltpu.make_async_copy(held.at[4], rows(normed_all, z), own_sem.at[4]))
    pl.when(z < 3)(lambda: line_start(z, True, 0))
    pl.when(z > 0)(lambda: line_start(z, False, 0))
    over(z, True).start()
    for copy in local:
        copy.start()
    for k in range(4):
        grad_over(k).start()
    for copy in given:
        copy.start()
    for copy, store in zip(local, stored):
        copy.wait()
        store.start()
    for hop in range(1, 4):
        hop_step(hop)
    for copy in stored:
        copy.wait()
    for k in range(4):
        grad_over(k).wait()
    for copy in given:
        copy.wait()
    over(z, True).wait()
    for k in range(1, 4):
        over((z + k) % 4).wait()
    pl.when(z < 3)(lambda: line_drain(z, True, 0))
    pl.when(z > 0)(lambda: line_drain(z, False, 0))
    for hop in range(1, 3):
        pl.when((z >= hop) & (z < 3))(lambda: line_drain(z - hop, True, hop))
        pl.when((z + hop <= 3) & (z > 0))(lambda: line_drain(z + hop, False, hop))


def gather_rows(normed, grads, first, mixed):
    tok, model = normed.shape
    anyspec = pl.BlockSpec(memory_space=pl.ANY)
    dma = pltpu.SemaphoreType.DMA
    return pl.pallas_call(
        rows_kernel,
        in_specs=[anyspec] * 7,
        out_specs=[anyspec] * 6,
        out_shape=[jax.ShapeDtypeStruct((4 * tok, model), bf16)] * 4
        + [jax.ShapeDtypeStruct(first.shape, bf16), jax.ShapeDtypeStruct(mixed.shape, bf16)],
        scratch_shapes=[
            dma((2, 3, 4)), dma((2, 3, 4)), dma((2, 4)), dma((2, 4)), dma((5,)),
            pltpu.VMEM((5, tok, model), bf16), dma((2,)), dma((2,)),
        ],
        compiler_params=pltpu.CompilerParams(collective_id=3, has_side_effects=True),
        name="gather_rows",
    )(normed, *grads, first, mixed)


def column_tiles(cols, size=512):
    return [(start, min(size, cols - start)) for start in range(0, cols, size)]


def feed_forward_kernel(
    normed, grad_out, weights, hidden, hidden_other, pair, pair_other, back,
    held, hidden_now, pair_now, sems, store_sem, core_send, core_recv,
):
    s, z, core, _, _ = places()
    step = pl.program_id(0)
    ff_part = held.shape[2]
    model = held.shape[1]
    rows = normed.shape[0]
    tiles = column_tiles(ff_part)
    made = ((hidden_now, hidden, hidden_other), (pair_now, pair, pair_other))

    def load(n, m):
        start, size = tiles[n]
        return pltpu.make_async_copy(
            weights.at[:, pl.ds(m * ff_part + start, size)], held.at[m, :, pl.ds(start, size)], sems.at[n, m]
        )

    def kept(n, turn):
        now, mine, _ = made[n]
        return pltpu.make_async_copy(now.at[turn], mine.at[pl.ds(turn * rows, rows), :], store_sem.at[turn, n])

    def handed(n, turn):
        now, _, other = made[n]
        return pltpu.make_async_remote_copy(
            src_ref=now.at[turn],
            dst_ref=other.at[pl.ds(turn * rows, rows), :],
            send_sem=core_send.at[turn, n],
            recv_sem=core_recv.at[turn, n],
            device_id=(core, z),
            device_id_type=MESH,
        )

    @pl.when(step == 0)
    def _():
        for n in range(len(tiles)):
            for m in range(3):
                load(n, m).start()
        greet([(core, z)])

    def forth(turn):
        for n, (start, size) in enumerate(tiles):
            cols = slice(start, start + size)
            if turn == 0:
                for m in range(3):
                    load(n, m).wait()
            gate = mm(normed[...], held[0, :, cols], ((1,), (0,)))
            up = mm(normed[...], held[1, :, cols], ((1,), (0,)))
            grad_hidden = mm(grad_out[...], held[2, :, cols], ((1,), (0,)))
            value, slope = gelu_parts(gate)
            hidden_now[turn, :, cols] = (value * up).astype(bf16)
            pair_now[turn, :, cols] = (grad_hidden * up * slope).astype(bf16)
            pair_now[turn, :, slice(ff_part + start, ff_part + start + size)] = (grad_hidden * value).astype(bf16)
        for n in range(2):
            handed(n, turn).start()
            kept(n, turn).start()

    for turn in range(2):
        pl.when(step == turn)(functools.partial(forth, turn))

    def back_tile(turn, carry):
        cols = pl.ds(pl.multiple_of(turn * 512, 512), 512)
        total = mm(pair_now[step, :, :ff_part], held[0, cols, :], ((1,), (1,)))
        total = total + mm(pair_now[step, :, ff_part:], held[1, cols, :], ((1,), (1,)))
        back[:, cols] = total.astype(bf16)
        return carry

    lax.fori_loop(0, model // 512, back_tile, 0)

    @pl.when(step == 1)
    def _():
        for turn in range(2):
            for n in range(2):
                kept(n, turn).wait()
                handed(n, turn).wait()


def feed_forward(normed, grad_out, weights):
    tok, model = normed.shape
    ff_part = weights.shape[1] // 3
    rows = tok // 2
    anyspec = pl.BlockSpec(memory_space=pl.ANY)
    dma = pltpu.SemaphoreType.DMA
    block = pl.BlockSpec((rows, model), lambda i: (i, 0))
    return pl.pallas_call(
        feed_forward_kernel,
        grid=(2,),
        in_specs=[block, block, anyspec],
        out_specs=[anyspec] * 4 + [block],
        out_shape=[
            jax.ShapeDtypeStruct((tok, cols), bf16)
            for cols in (ff_part, ff_part, 2 * ff_part, 2 * ff_part, model)
        ],
        scratch_shapes=[
            pltpu.VMEM((3, model, ff_part), bf16),
            pltpu.VMEM((2, rows, ff_part), bf16),
            pltpu.VMEM((2, rows, 2 * ff_part), bf16),
            dma((len(column_tiles(ff_part)), 3)), dma((2, 2)), dma((2, 2)), dma((2, 2)),
        ],
        compiler_params=pltpu.CompilerParams(
            collective_id=4, has_side_effects=True, vmem_limit_bytes=60 * 1024 * 1024
        ),
        name="feed_forward",
    )(normed, grad_out, weights)


def add_columns(target, sources, start, size, step):
    def one(turn, carry):
        cols = pl.ds(pl.multiple_of(start + turn * step, 128), step)
        total = target[:, cols].astype(f32)
        for source in sources:
            total = total + source[:, cols].astype(f32)
        target[:, cols] = total.astype(target.dtype)
        return carry

    lax.fori_loop(0, size // step, one, 0)


def shared_products_kernel(
    normed, normed_other, grad, grad_other, weights, pair, pair_other, hidden, hidden_other,
    beside_high, across_low, mine, beside_low, across_high, out,
    turned, slots, stage, right, diag, landed, waiting, down_now, out_now,
    load_sem, right_sem, send_sem, recv_sem, store_sem, down_sem, out_sem,
):
    s, z, _, beside, across = places()
    step = pl.program_id(0)
    lefts = ((normed, normed_other), (grad, grad_other))
    chip_cols = normed.shape[1] // 4
    half = chip_cols // 2
    piece = half // 2
    width = hidden.shape[1]
    tok = normed.shape[0]
    diagonal = beside + across - s
    chips = [q // 2 for q in (diagonal, beside, across, s)]

    def load(side, q, who):
        cols = pl.ds(pl.multiple_of(chips[q] * chip_cols, 128), chip_cols)
        return pltpu.make_async_copy(lefts[side][who].at[:, cols], slots.at[q % 2, who], load_sem.at[q % 2, who])

    def fetch(side):
        for q in range(2):
            for who in range(2):
                load(side, q, who).start()

    def turn(side):
        for q in range(4):
            for who in range(2):
                load(side, q, who).wait()
                stage[...] = slots[q % 2, who].T
                turned[q * half : (q + 1) * half, who * tok : (who + 1) * tok] = stage[
                    pl.ds(pl.multiple_of(s % 2 * half, 16), half), :
                ]
                if q < 2:
                    load(side, q + 2, who).start()

    pieces = column_tiles(width)

    def push(way, cols, index):
        return pltpu.make_async_remote_copy(
            src_ref=diag.at[way, :, cols],
            dst_ref=landed.at[way, :, cols],
            send_sem=send_sem.at[way, index],
            recv_sem=recv_sem.at[way, index],
            device_id=(across if way == 0 else beside, z),
            device_id_type=MESH,
        )

    def take(j):
        sources = (hidden, hidden_other) if j == 2 else (pair, pair_other)
        return [
            pltpu.make_async_copy(
                source.at[:, pl.ds(0 if j == 2 else j * width, width)],
                right.at[j % 2, pl.ds(who * tok, tok), :],
                right_sem.at[j % 2, who],
            )
            for who, source in enumerate(sources)
        ]

    def take_start(j):
        for copy in take(j):
            copy.start()

    def take_wait(j):
        for copy in take(j):
            copy.wait()

    def tile(start, size):
        cols = pl.ds(start, size)
        block = mm(turned[...], right[step % 2, :, cols], ((1,), (0,))).astype(bf16)
        parts = [block[n * piece : (n + 1) * piece] for n in range(8)]
        there = pl.ds(pl.multiple_of(step * width + start, 128), size)
        index = step * len(pieces) + start // 512
        diag[0, :, there] = parts[0]
        diag[1, :, there] = parts[1]
        waiting[0, :, there] = parts[2]
        beside_high[:, cols] = parts[3]
        across_low[:, cols] = parts[4]
        waiting[1, :, there] = parts[5]
        mine[0:piece, cols] = parts[6]
        mine[piece:, cols] = parts[7]
        for way in range(2):
            push(way, there, index).start()

    def multiply():
        def one(turn, carry):
            tile(pl.multiple_of(turn * 512, 512), 512)
            return carry

        lax.fori_loop(0, width // 512, one, 0)
        if width % 512:
            tile(width // 512 * 512, width % 512)

    def store(way, j):
        cols = pl.ds(j * width, width)
        return pltpu.make_async_copy(
            waiting.at[way, :, cols], (beside_low, across_high)[way].at[:, cols], store_sem.at[way, j]
        )

    out_rows = down_now.shape[1]
    out_tiles = weights.shape[0] // out_rows

    def down(t):
        source = weights.at[pl.ds(t * out_rows, out_rows), pl.ds(2 * width, width)]
        return pltpu.make_async_copy(source, down_now.at[t % 2], down_sem.at[t % 2])

    def out_store(t):
        return pltpu.make_async_copy(
            out_now.at[t % 2], out.at[:, pl.ds(t * out_rows, out_rows)], out_sem.at[t % 2]
        )

    def out_product():
        for t in range(out_tiles):
            down(t).wait()
            if t > 1:
                out_store(t - 2).wait()
            out_now[t % 2] = mm(right[0, 0:tok, :], down_now[t % 2], ((1,), (1,))).astype(bf16)
            out_store(t).start()
            if t + 2 < out_tiles:
                down(t + 2).start()

    @pl.when(step == 0)
    def _():
        fetch(0)
        take_start(0)
        take_start(1)
        greet([(beside, z), (across, z)])
        turn(0)
        take_wait(0)

    @pl.when(step == 1)
    def _():
        take_wait(1)
        take_start(2)
        fetch(1)

    @pl.when(step == 2)
    def _():
        down(0).start()
        down(1).start()
        turn(1)
        take_wait(2)

    multiply()
    @pl.when(step == 2)
    def _():
        out_product()
        pushed = [
            (way, pl.ds(j * width + start, size), j * len(pieces) + n, j)
            for j in range(3)
            for n, (start, size) in enumerate(pieces)
            for way in range(2)
        ]
        for way, cols, index, j in pushed:
            push(way, cols, index).wait_recv()
            if index % len(pieces) == len(pieces) - 1:
                add_columns(waiting.at[way], [landed.at[way]], j * width, width, 384)
                store(way, j).start()
        for way, cols, index, j in pushed:
            push(way, cols, index).wait_send()
        for j in range(3):
            for way in range(2):
                store(way, j).wait()
        for t in range(out_tiles - 2, out_tiles):
            out_store(t).wait()


def shared_products(lefts, weights, pair, hidden):
    tok, model = lefts[0].shape
    width = hidden[0].shape[1]
    half = model // 8
    anyspec = pl.BlockSpec(memory_space=pl.ANY)
    dma = pltpu.SemaphoreType.DMA

    def block(rows):
        return pl.BlockSpec((rows, width), lambda j: (0, j))

    rows_out = (half // 2, half // 2, half, half // 2, half // 2)
    return pl.pallas_call(
        shared_products_kernel,
        grid=(3,),
        in_specs=[anyspec] * 9,
        out_specs=[block(rows) for rows in rows_out[:3]] + [anyspec] * 3,
        out_shape=[jax.ShapeDtypeStruct((rows, 3 * width), bf16) for rows in rows_out]
        + [jax.ShapeDtypeStruct((tok, model), bf16)],
        scratch_shapes=[
            pltpu.VMEM((4 * half, 2 * tok), bf16),
            pltpu.VMEM((2, 2, tok, 2 * half), bf16),
            pltpu.VMEM((2 * half, tok), bf16),
            pltpu.VMEM((2, 2 * tok, width), bf16),
            pltpu.VMEM((2, half // 2, 3 * width), bf16),
            pltpu.VMEM((2, half // 2, 3 * width), bf16),
            pltpu.VMEM((2, half // 2, 3 * width), bf16),
            pltpu.VMEM((2, 512, width), bf16),
            pltpu.VMEM((2, tok, 512), bf16),
            dma((2, 2)), dma((2, 2)), dma((2, 12)), dma((2, 12)), dma((2, 3)), dma((2,)), dma((2,)),
        ],
        compiler_params=pltpu.CompilerParams(
            collective_id=5, has_side_effects=True, vmem_limit_bytes=60 * 1024 * 1024
        ),
        name="feed_forward_products",
    )(*lefts, weights, *pair, *hidden)


def scatter_kernel(
    normed, normed_other, grad_mix, mix_other, mixed, mixed_other, grad_gelu, gelu_other, grad_branch, rest,
    mlp_low, mlp_high, mixer_w, tokens, gain, mixer_sum, mlp_back, input_grad,
    held, cross, near, lined, left_now, both_now, mixed_now, turned, stage, rest_other, back_now, wide_now, gain_now,
    load_sem, core_send, core_recv, wide_sem,
    flow_send, flow_recv, line_send, line_recv, swap_send, swap_recv, own_sem,
):
    s, z, core, beside, across = places()
    chip_diag, chip_beside, chip_across, chip = 0, 1, 2, 3
    chips = [q // 2 for q in (beside + across - s, beside, across, s)]
    rows = held.shape[1] // 4
    cols = held.shape[2]
    cut = cols // 256 * 128
    ff_part = mlp_low.shape[1] // 3
    tok, model = tokens.shape
    half = 4 * rows
    lru = grad_branch.shape[1]
    lru2 = 2 * lru
    rest_start = lru2 + mixed.shape[1]
    order = (3 * (1 - z // 2), (2 + 3 * z) % 5, 1 + z % 2, z)

    def remote(src, dst, send, recv, target):
        return pltpu.make_async_remote_copy(
            src_ref=src, dst_ref=dst, send_sem=send, recv_sem=recv, device_id=target, device_id_type=MESH
        )

    def span(k):
        return pl.ds(pl.multiple_of(k * rows, 16), rows)

    mine, other = pl.ds(0, tok), pl.ds(tok, tok)
    loads = [
        pltpu.make_async_copy(source, target, load_sem.at[n])
        for n, (source, target) in enumerate(
            (
                (grad_mix, left_now.at[1, mine, :]),
                (mix_other, left_now.at[1, other, :]),
                (mixed, mixed_now.at[mine, :]),
                (mixed_other, mixed_now.at[other, :]),
                (normed, left_now.at[0, mine, :]),
                (normed_other, left_now.at[0, other, :]),
                (grad_gelu, both_now.at[mine, pl.ds(lru, lru)]),
                (gelu_other, both_now.at[other, pl.ds(lru, lru)]),
                (grad_branch, both_now.at[mine, pl.ds(0, lru)]),
            )
        )
    ]

    def push(n):
        if n == 0:
            source, target = grad_branch, both_now.at[other, pl.ds(0, lru)]
        else:
            source = rest.at[pl.ds(pl.multiple_of(chips[n - 1] * 2 * half + (1 - s % 2) * half, 16), half), :]
            target = rest_other.at[n - 1]
        return pltpu.make_async_remote_copy(
            src_ref=source,
            dst_ref=target,
            send_sem=core_send.at[n],
            recv_sem=core_recv.at[n],
            device_id=(core, z),
            device_id_type=MESH,
        )

    def rest_load(q):
        source = rest.at[pl.ds(pl.multiple_of(chips[q] * 2 * half + s % 2 * half, 16), half), :]
        return pltpu.make_async_copy(
            source, held.at[q, :, pl.ds(rest_start, cols - rest_start)], load_sem.at[9 + q]
        )

    def turn(side):
        for q in range(4):
            source = left_now[side, :, pl.ds(pl.multiple_of(chips[q] * 2 * half, 128), 2 * half)]
            stage[...] = source.T
            turned[side, q * half : (q + 1) * half, :] = stage[
                pl.ds(pl.multiple_of(s % 2 * half, 16), half), :
            ]

    def multiply(q, side, first=0, last=None):
        right, start = ((both_now, 0), (mixed_now, lru2))[side]

        def one(turn, carry):
            here = pl.multiple_of(turn * 512, 512)
            block = mm(turned[side, q * half : (q + 1) * half, :], right[:, pl.ds(here, 512)], ((1,), (0,)))
            held[q, :, pl.ds(pl.multiple_of(start + here, 512), 512)] = block.astype(bf16)
            return carry

        lax.fori_loop(first // 512, (right.shape[1] if last is None else last) // 512, one, 0)

    def add_rest(q):
        rest_load(q).wait()
        push(1 + q).wait_recv()
        held[q, :, rest_start:] = add_low(held[q, :, rest_start:], rest_other[q])

    left, right = pl.ds(0, cut), pl.ds(cut, cols - cut)

    def block(q, i, side):
        return held.at[q, span(order[i]), side]

    def flow(i, index):
        send, recv = flow_send.at[i, index], flow_recv.at[i, index]
        to_beside, to_across = (beside, z), (across, z)
        if index == 0:
            return remote(block(chip_diag, i, left), cross.at[i, :, left], send, recv, to_across)
        if index == 1:
            return remote(block(chip_diag, i, right), cross.at[i, :, right], send, recv, to_beside)
        if index == 2:
            return remote(block(chip_beside, i, right), near.at[0, i, :, right], send, recv, to_beside)
        if index == 3:
            return remote(block(chip_beside, i, left), near.at[0, i, :, left], send, recv, to_beside)
        if index == 4:
            return remote(block(chip_across, i, left), near.at[1, i, :, left], send, recv, to_across)
        return remote(block(chip_across, i, right), near.at[1, i, :, right], send, recv, to_across)

    def cross_step(i):
        flow(i, 0).wait_recv()
        add_columns(held.at[chip_beside, span(order[i]), :], [cross.at[i]], 0, cut, 512)
        flow(i, 3).start()
        flow(i, 1).wait_recv()
        add_columns(held.at[chip_across, span(order[i]), :], [cross.at[i]], cut, cols - cut, 384)
        flow(i, 5).start()

    def near_step(i):
        for index in (2, 4, 3, 5):
            flow(i, index).wait_recv()
        add_columns(held.at[chip, span(order[i]), :], [near.at[0, i], near.at[1, i]], 0, cols, 640)

    def line(k, slot, target):
        return remote(
            held.at[chip, span(k), :], lined.at[slot], line_send.at[k], line_recv.at[slot], (s, target)
        )

    def absorb(k, slot, source):
        line(k, slot, source).wait_recv()
        add_columns(held.at[chip, span(k), :], [lined.at[slot]], 0, cols, 640)

    def chain(i):
        k = order[i]
        if i == 3:
            pl.when(z > 0)(lambda: absorb(k, k, z - 1))
            pl.when(z < 3)(lambda: absorb(k, 4, z + 1))
            return

        @pl.when(k > z)
        def _():
            pl.when(z > 0)(lambda: absorb(k, k, z - 1))
            line(k, k, z + 1).start()

        @pl.when(k < z)
        def _():
            pl.when(z < 3)(lambda: absorb(k, k, z + 1))
            pl.when(k == z - 1)(lambda: line(k, 4, z - 1).start())
            pl.when(k < z - 1)(lambda: line(k, k, z - 1).start())

    def chain_drain():
        for i in range(3):
            k = order[i]
            line(k, k, (z + 1) % 4).wait_send()

    def swap(k, high=False):
        to = (z + k) % 4
        here = pl.ds(pl.multiple_of(z * ff_part, 128), ff_part)
        source = (mlp_high if high else mlp_low).at[span(to % 2), :]
        return [
            remote(
                source.at[:, pl.ds(m * ff_part, ff_part)],
                mlp_back.at[m, :, here],
                swap_send.at[k - 1, m],
                swap_recv.at[k - 1, m],
                (s, to),
            )
            for m in range(3)
        ]

    def swap_start(k):
        to = (z + k) % 4

        @pl.when(to < 2)
        def _():
            for copy in swap(k):
                copy.start()

        @pl.when(to >= 2)
        def _():
            for copy in swap(k, True):
                copy.start()

    def own(high=False):
        here = pl.ds(pl.multiple_of(z * ff_part, 128), ff_part)
        source = (mlp_high if high else mlp_low).at[span(z % 2), :]
        return [
            pltpu.make_async_copy(source.at[:, pl.ds(m * ff_part, ff_part)], mlp_back.at[m, :, here], own_sem.at[m])
            for m in range(3)
        ]

    wide_rows = wide_now.shape[0]
    wide_tiles = mixer_w.shape[0] // wide_rows
    wide_start = mixer_w.shape[1] - lru2 - model
    wide_slots = (both_now.at[pl.ds(tok, wide_rows), :], wide_now)

    def wide(j):
        source = mixer_w.at[pl.ds(j * wide_rows, wide_rows), pl.ds(wide_start, lru2)]
        return pltpu.make_async_copy(source, wide_slots[j % 2], wide_sem.at[j % 2])

    plain_loads = [
        pltpu.make_async_copy(tokens, left_now.at[0, pl.ds(0, tok), :], wide_sem.at[2]),
        pltpu.make_async_copy(gain, gain_now, wide_sem.at[3]),
    ]

    def back(first, last):
        for j in range(first, last):
            wide(j).wait()
            back_now[:, pl.ds(j * wide_rows, wide_rows)] = mm(
                both_now[0:tok, :], wide_slots[j % 2][...], ((1,), (1,))
            )
            if j + 2 < wide_tiles:
                wide(j + 2).start()

    def finish_rows(turn, carry):
        at = pl.ds(pl.multiple_of(turn * 16, 16), 16)
        result = left_now[1, at, :].astype(f32) + norm_back(
            left_now[0, at, :].astype(f32), gain_now[GAIN_ONE : GAIN_ONE + 1, :], back_now[at, :]
        )
        left_now[0, at, :] = result.astype(bf16)
        return carry

    for copy in loads:
        copy.start()
    for q in range(4):
        rest_load(q).start()
    greet([(core, z), (beside, z), (across, z)] + [(s, (z + k) % 4) for k in range(1, 4)])
    for n in range(5):
        push(n).start()
    for k in (1, 3, 2):
        swap_start(k)

    @pl.when(z < 2)
    def _():
        for copy in own():
            copy.start()

    @pl.when(z >= 2)
    def _():
        for copy in own(True):
            copy.start()

    for copy in loads[:4]:
        copy.wait()
    turn(1)
    multiply(chip_diag, 1)
    for copy in loads[4:]:
        copy.wait()
    turn(0)
    multiply(chip_diag, 0, lru)
    add_rest(chip_diag)
    for i in range(2):
        flow(i, 1).start()
    push(0).wait_recv()
    multiply(chip_diag, 0, 0, lru)
    for i in range(2):
        flow(i, 0).start()
    for q in (chip_beside, chip_across, chip):
        multiply(q, 0)
        multiply(q, 1)
        add_rest(q)
        if q == chip_beside:
            flow(0, 2).start()
        if q == chip_across:
            flow(0, 4).start()
    for copy in plain_loads:
        copy.start()
    wide(0).start()
    wide(1).start()
    for i in range(4):
        cross_step(i)
        if i + 1 < 4:
            flow(i + 1, 2).start()
            flow(i + 1, 4).start()
        if i + 2 < 4:
            flow(i + 2, 0).start()
            flow(i + 2, 1).start()
        if i > 0:
            near_step(i - 1)
            chain(i - 1)
            back(wide_tiles * (i - 1) // 3, wide_tiles * i // 3)
    for copy in plain_loads:
        copy.wait()
    lax.fori_loop(0, tok // 16, finish_rows, 0)
    finished = pltpu.make_async_copy(left_now.at[0, pl.ds(0, tok), :], input_grad, wide_sem.at[2])
    finished.start()
    near_step(3)
    chain(3)
    done = pltpu.make_async_copy(held.at[chip, span(z), :], mixer_sum, own_sem.at[3])
    done.start()
    for i in range(4):
        for index in range(6):
            flow(i, index).wait_send()
    chain_drain()
    for k in range(1, 4):
        for copy in swap(k):
            copy.wait()
    for copy in own():
        copy.wait()
    for n in range(5):
        push(n).wait_send()
    finished.wait()
    done.wait()


def scatter(rows_pairs, grad_branch, rest, mlp_low, mlp_high, mixer_w, tokens, gain):
    tok, model = tokens.shape
    rows = model // 32
    lru = grad_branch.shape[1]
    cols = 3 * lru + rest.shape[1]
    ff_part = mlp_low.shape[1] // 3
    anyspec = pl.BlockSpec(memory_space=pl.ANY)
    dma = pltpu.SemaphoreType.DMA
    return pl.pallas_call(
        scatter_kernel,
        in_specs=[anyspec] * 15,
        out_specs=[anyspec] * 3,
        out_shape=[
            jax.ShapeDtypeStruct((rows, cols), bf16),
            jax.ShapeDtypeStruct((3, rows, 4 * ff_part), bf16),
            jax.ShapeDtypeStruct((tok, model), bf16),
        ],
        scratch_shapes=[
            pltpu.VMEM((4, 4 * rows, cols), bf16),
            pltpu.VMEM((4, rows, cols), bf16),
            pltpu.VMEM((2, 4, rows, cols), bf16),
            pltpu.VMEM((5, rows, cols), bf16),
            pltpu.VMEM((2, 2 * tok, model), bf16),
            pltpu.VMEM((2 * tok, 2 * lru), bf16),
            pltpu.VMEM((2 * tok, lru), bf16),
            pltpu.VMEM((2, 16 * rows, 2 * tok), bf16),
            pltpu.VMEM((8 * rows, 2 * tok), bf16),
            pltpu.VMEM((4, 4 * rows, rest.shape[1]), bf16),
            pltpu.VMEM((tok, model), f32),
            pltpu.VMEM((128, 2 * lru), bf16),
            pltpu.VMEM(gain.shape, f32),
            dma((13,)), dma((5,)), dma((5,)), dma((4,)),
            dma((4, 6)), dma((4, 6)), dma((4,)), dma((5,)), dma((3, 3)), dma((3, 3)), dma((4,)),
        ],
        compiler_params=pltpu.CompilerParams(
            collective_id=2, has_side_effects=True, vmem_limit_bytes=62 * 1024 * 1024
        ),
        name="scatter_gradients",
    )(*rows_pairs, grad_branch, rest, mlp_low, mlp_high, mixer_w, tokens, gain)


def gather_plain(mixer, gate, up, down):
    groups = lax.axis_size("fsdp")
    part_rows, ff = gate.shape
    own = jnp.stack([w.reshape(part_rows, groups, ff // groups) for w in (gate, up, down)], axis=2)
    mine = lax.all_to_all(jnp.transpose(own, (1, 0, 2, 3)), "fsdp", 0, 0, tiled=True)
    return lax.all_gather(mixer, both, axis=0, tiled=True), mine.reshape(groups * part_rows, -1)


def from_line(shard):
    count = lax.axis_size("fsdp")
    return [shard] + [
        lax.ppermute(shard, "fsdp", [(i, (i + k) % count) for i in range(count)]) for k in range(1, count)
    ]


def swap_cores(shard):
    count = lax.axis_size("seq")
    return lax.ppermute(shard, "seq", [(i, i + 1 - 2 * (i % 2)) for i in range(count)])


def swap_beside(shard):
    return lax.ppermute(shard, "seq", [(i, i ^ 2) for i in range(8)])


def swap_across(shard):
    return lax.ppermute(shard, "seq", [(i, i ^ 4) for i in range(8)])


def add_low(left, right):
    return (left.astype(f32) + right.astype(f32)).astype(bf16)


def scatter_plain(normed, grad_both, grad_mix, mixed, rest, mlp_sum):
    groups = lax.axis_size("fsdp")
    term_wide = mm(normed, grad_both, ((0,), (0,))).astype(bf16)
    term_out = mm(grad_mix, mixed, ((0,), (0,))).astype(bf16)
    mixer_sum = lax.psum_scatter(
        jnp.concatenate([term_wide, term_out, rest], axis=1), "seq", scatter_dimension=0, tiled=True
    )
    mixer_sum = lax.psum_scatter(mixer_sum, "fsdp", scatter_dimension=0, tiled=True)
    ff_part = mlp_sum.shape[1] // 3
    part_rows = mlp_sum.shape[0] // groups
    mlp_sum = mlp_sum.reshape(groups, part_rows, 3, ff_part)
    mlp_back = lax.all_to_all(mlp_sum, "fsdp", 0, 0, tiled=True)
    mlp_back = jnp.transpose(mlp_back, (2, 1, 0, 3)).reshape(3, part_rows, groups * ff_part)
    return mixer_sum, mlp_back


def call_heads(kernel, width, heads, ins, outs, scratch, name):
    def spec(rows, place):
        if place is None:
            return pl.BlockSpec((rows, width), lambda h: (0, h))
        return pl.BlockSpec((width, width), lambda h: (h, place))

    in_specs = [spec(a.shape[0], place) for a, place in ins]
    out_specs = [spec(rows, 0 if rowwise else None) for rows, _, rowwise in outs]
    out_shape = [
        jax.ShapeDtypeStruct((heads * width, width) if rowwise else (rows, heads * width), kind)
        for rows, kind, rowwise in outs
    ]
    return pl.pallas_call(
        kernel,
        grid=(heads,),
        in_specs=in_specs,
        out_specs=out_specs,
        out_shape=out_shape,
        scratch_shapes=[pltpu.VMEM((rows, width), f32) for rows in scratch],
        compiler_params=pltpu.CompilerParams(vmem_limit_bytes=16 * 1024 * 1024),
        cost_estimate=pl.CostEstimate(flops=1, bytes_accessed=1, transcendentals=0),
        name=name,
    )(*[a for a, _ in ins])


def on_device(
    block_input,
    cotangent,
    mixer_gain,
    branch_proj,
    gelu_proj,
    conv_taps,
    conv_bias,
    rate_blocks,
    input_blocks,
    rate_bias,
    input_bias,
    decay_param,
    out_proj,
    mlp_gain,
    gate_proj,
    up_proj,
    down_proj,
):
    groups = lax.axis_size("fsdp")
    part_rows, lru = branch_proj.shape
    width = rate_blocks.shape[1]
    heads = lru // width
    margin = conv_taps.shape[0] - 1
    tokens = block_input[0].astype(f32)
    tok_count, model = tokens.shape
    ff = gate_proj.shape[1]
    ff_part = ff // groups
    grad_out = cotangent[0]

    smalls = jnp.stack(
        [conv_taps[k] for k in range(margin + 1)]
        + [conv_bias, rate_bias, input_bias, decay_param, mixer_gain, mlp_gain],
        axis=1,
    )
    small_count = smalls.shape[1]
    smalls = jnp.pad(smalls, ((0, 0), (0, 128 - small_count)))
    first_own = jnp.concatenate([rate_blocks, input_blocks, smalls], axis=1)
    mixer_own = (first_own, branch_proj, gelu_proj, out_proj)
    custom = lax.axis_size("seq") == 8 and groups == 4
    if custom:
        mixer_w, mlp_mine = gather(*mixer_own, gate_proj, up_proj, down_proj)
    else:
        mixer_w, mlp_mine = gather_plain(jnp.concatenate(mixer_own, axis=1), gate_proj, up_proj, down_proj)
    mlp_w = lax.all_gather(mlp_mine, "seq", axis=0, tiled=True)
    grad_out_late = lax.optimization_barrier((grad_out, mlp_mine))[0]
    if custom:
        grad_pieces = from_line(grad_out_late)
    wide = mixer_w[:, 128 + 2 * width : 128 + 2 * width + 2 * lru]
    proj_out = mixer_w[:, 128 + 2 * width + 2 * lru :]

    small = small_table(mixer_w, 2 * width // 128)
    gain_one, gain_two = small[GAIN_ONE], small[GAIN_TWO]

    normed, branch, gelu_pre = mixer_in(block_input[0], small, mixer_w, lru, 2 * width + 128)
    prior = from_behind(branch[tok_count - margin :], "seq", 1).astype(f32)
    prior = jnp.concatenate([jnp.zeros((8 - margin, lru), f32), prior], axis=0)
    conv, rate_pre, input_pre, cum, local = call_heads(
        mixer_forward,
        width,
        heads,
        [(branch, None), (prior, None), (small, None), (mixer_w, 0), (mixer_w, 1)],
        [(tok_count, bf16, False)] + [(tok_count, f32, False)] * 4,
        [tok_count + 8],
        "mixer_forward",
    )
    carried = prefix((cum[-1], local[-1]), "seq", False)
    states = local + cum * carried[None]
    mixed = (states * jax.nn.gelu(gelu_pre, approximate=True)).astype(bf16)
    middle = tokens + mm(mixed, proj_out, ((1,), (1,)))
    normed_two = norm_rows(middle, gain_two).astype(bf16)

    if custom:
        normed_all, normed_other, grad_out_all, grad_out_other, first_other, mixed_other = gather_rows(
            normed_two, grad_pieces, normed, mixed
        )
    else:
        normed_all = lax.all_gather(normed_two, "fsdp", axis=0, tiled=True)
        grad_out_all = lax.all_gather(grad_out_late, "fsdp", axis=0, tiled=True)
    w_gate, w_up, w_down = mlp_w[:, :ff_part], mlp_w[:, ff_part : 2 * ff_part], mlp_w[:, 2 * ff_part :]
    if custom:
        hidden, hidden_other, grad_pair, pair_other, grad_normed_part = feed_forward(
            normed_all, grad_out_all, mlp_w
        )
    else:
        gate = mm(normed_all, w_gate, ((1,), (0,)))
        up_val = mm(normed_all, w_up, ((1,), (0,)))
        gelu_gate, gelu_slope = gelu_parts(gate)
        hidden = (gelu_gate * up_val).astype(bf16)
        grad_hidden = mm(grad_out_all, w_down, ((1,), (0,)))
        grad_gate = (grad_hidden * up_val * gelu_slope).astype(bf16)
        grad_up = (grad_hidden * gelu_gate).astype(bf16)
        grad_normed_part = (
            mm(grad_gate, w_gate, ((1,), (1,))) + mm(grad_up, w_up, ((1,), (1,)))
        ).astype(bf16)
    grad_normed_two = lax.psum_scatter(grad_normed_part, "fsdp", scatter_dimension=0, tiled=True)
    if custom:
        half = model // 16
        beside_high, across_low, mine, beside_low, across_high, out_part = shared_products(
            (normed_all, normed_other, grad_out_all, grad_out_other),
            mlp_w,
            (grad_pair, pair_other),
            (hidden, hidden_other),
        )
        from_beside_high, from_across_low = swap_beside(beside_high), swap_across(across_low)
    else:
        grad_pair = jnp.concatenate([grad_gate, grad_up], axis=1)
        term_pair = mm(normed_all, grad_pair, ((0,), (0,))).astype(bf16)
        term_down = mm(grad_out_all, hidden, ((0,), (0,))).astype(bf16)
        pair_sum = lax.psum_scatter(term_pair, "seq", scatter_dimension=0, tiled=True)
        down_sum = lax.psum_scatter(term_down, "seq", scatter_dimension=0, tiled=True)
        mlp_sum = jnp.concatenate([pair_sum, down_sum], axis=1)
        out_part = mm(hidden, w_down, ((1,), (1,))).astype(bf16)
    out_sum = lax.psum_scatter(out_part, "fsdp", scatter_dimension=0, tiled=True)
    grad_normed_two = grad_normed_two.astype(f32)

    grad_middle = grad_out.astype(f32) + norm_back(middle, gain_two, grad_normed_two)
    grad_mix = grad_middle.astype(bf16)
    if custom:
        mix_other = swap_cores(grad_mix)
    grad_mixed = mm(grad_mix, proj_out, ((1,), (0,)))
    carried_rows = jnp.broadcast_to(carried[None], (8, lru))
    grad_gelu_pre, rev_cum, rev_grad, pair_grad = call_heads(
        mixer_backward_scan,
        width,
        heads,
        [(a, None) for a in (grad_mixed, gelu_pre, rate_pre, cum, local, carried_rows, small)],
        [(tok_count, bf16, False), (tok_count, f32, False), (tok_count, f32, False), (8, f32, False)],
        [tok_count + 8],
        "mixer_backward_scan",
    )
    if custom:
        from_beside_high, from_across_low, pair_grad = lax.optimization_barrier(
            (from_beside_high, from_across_low, pair_grad)
        )
    if custom:
        gelu_other = swap_cores(grad_gelu_pre)
    incoming = prefix((cum[-1], pair_grad[0]), "seq", True)
    if custom:
        beside_low, across_high, incoming = lax.optimization_barrier((beside_low, across_high, incoming))
        from_beside_low, from_across_high = swap_beside(beside_low), swap_across(across_high)
    incoming_rows = jnp.broadcast_to(incoming[None], (8, lru))
    own, head, rate_w_grad, input_w_grad, sums = call_heads(
        mixer_backward,
        width,
        heads,
        [
            (a, None)
            for a in (rev_cum, rev_grad, incoming_rows, cum, local, carried_rows, rate_pre, input_pre, conv, branch, prior, small)
        ]
        + [(mixer_w, 0), (mixer_w, 1)],
        [(tok_count, f32, False), (8, f32, False), (0, bf16, True), (0, bf16, True), (8, f32, False)],
        [tok_count + 8, tok_count + 16],
        "mixer_backward",
    )
    received = from_behind(head[8 - margin :], "seq", -1)
    grad_branch = jnp.concatenate(
        [own[: tok_count - margin], own[tok_count - margin :] + received], axis=0
    ).astype(bf16)
    grad_both = jnp.concatenate([grad_branch, grad_gelu_pre], axis=1)
    vectors = jnp.pad(sums.T, ((0, 0), (0, 128 - sums.shape[0]))).astype(bf16)
    rest = jnp.concatenate([rate_w_grad, input_w_grad, vectors], axis=1)
    if custom:
        low, high = [
            sum(part.astype(f32) for part in parts).astype(bf16)
            for parts in (
                (mine[:half], from_across_low, from_beside_low),
                (mine[half:], from_across_high, from_beside_high),
            )
        ]
        mixer_sum, mlp_back, input_grad = scatter(
            (normed, first_other, grad_mix, mix_other, mixed, mixed_other, grad_gelu_pre, gelu_other),
            grad_branch, rest, low, high, mixer_w, block_input[0], small,
        )
    else:
        mixer_sum, mlp_back = scatter_plain(normed, grad_both, grad_mix, mixed, rest, mlp_sum)
        grad_normed = mm(grad_both, wide, ((1,), (1,)))
        input_grad = (grad_middle + norm_back(tokens, gain_one, grad_normed)).astype(bf16)
    input_grad = input_grad[None]
    middle = lax.optimization_barrier((middle, rest))[0]
    block_output = (middle + out_sum.astype(f32)).astype(bf16)[None]
    edge = 3 * lru + 2 * width
    vec = mixer_sum[:, edge:].astype(f32).T
    weight_grads = list(
        jnp.split(mixer_sum[:, :edge].astype(f32), [lru, 2 * lru, 3 * lru, 3 * lru + width], axis=1)
    ) + [mlp_back[m].astype(f32) for m in range(3)]
    first_total = gain_back((branch_proj, weight_grads[0]), (gelu_proj, weight_grads[1]))
    second_total = gain_back((gate_proj, weight_grads[5]), (up_proj, weight_grads[6]))
    dbranch, dgelu, dout, drate, dinput, dgate, dup, ddown = weight_grads
    return (
        block_output,
        input_grad,
        first_total / mixer_gain.astype(f32),
        dbranch,
        dgelu,
        vec[: margin + 1],
        vec[7],
        drate,
        dinput,
        vec[4],
        vec[5],
        vec[6],
        dout,
        second_total / mlp_gain.astype(f32),
        dgate,
        dup,
        ddown,
    )


def solution(mesh):
    tokens = P("fsdp", "seq", None)
    vector = P(both)
    matrix = P(both, None)
    taps = P(None, both)
    return jax.shard_map(
        on_device,
        mesh=mesh,
        in_specs=(
            tokens, tokens, vector, matrix, matrix, taps, vector, matrix, matrix,
            vector, vector, vector, matrix, vector, matrix, matrix, matrix,
        ),
        out_specs=(
            tokens, tokens, vector, matrix, matrix, taps, vector, matrix, matrix,
            vector, vector, vector, matrix, vector, matrix, matrix, matrix,
        ),
        check_vma=False,
    )
```

```python
import functools

import jax
import jax.numpy as jnp
from jax import lax
from jax.experimental import pallas as pl
from jax.experimental.pallas import tpu as pltpu
from jax.sharding import PartitionSpec as P

epsilon = 1e-06
f32 = jnp.float32
bf16 = jnp.bfloat16
both = ("seq", "fsdp")
MESH = pl.DeviceIdType.MESH
TAP, CONV_BIAS, RATE_BIAS, INPUT_BIAS, SOFT, SOFT_SLOPE, GAIN_ONE, GAIN_TWO = 0, 4, 5, 6, 7, 8, 9, 10
GELU_C = 0.7978845608028654
GELU_A = 0.044715


def from_behind(shard, axis, by):
    devices = lax.axis_size(axis)
    pairs = [(i, i + by) for i in range(devices) if 0 <= i + by < devices]
    return lax.ppermute(shard, axis, pairs)


def prefix(part, axis, reverse):
    count = lax.axis_size(axis)
    place = lax.axis_index(axis)
    gathered = lax.all_gather(jnp.stack(part), axis)
    state = jnp.zeros_like(part[1])
    for hop in range(count):
        source = count - 1 - hop if reverse else hop
        ahead = source > place if reverse else source < place
        state = jnp.where(ahead, gathered[source, 1] + gathered[source, 0] * state, state)
    return state


def norm_rows(values, scales):
    return values * lax.rsqrt(jnp.mean(values * values, axis=-1, keepdims=True) + epsilon) * scales


def norm_back(values, scales, grads):
    inverse = lax.rsqrt(jnp.mean(values * values, axis=-1, keepdims=True) + epsilon)
    scaled = grads * scales
    shared = jnp.mean(values * scaled, axis=-1, keepdims=True)
    return inverse * scaled - values * (inverse * inverse * inverse * shared)


def gain_back(*pairs):
    return sum(jnp.sum(weight.astype(f32) * grad, axis=1) for weight, grad in pairs)


def gelu_parts(x):
    square = x * x
    inner = jnp.tanh(x * (GELU_C + GELU_C * GELU_A * square))
    open_part = 0.5 + 0.5 * inner
    value = x * open_part
    return value, open_part + value * (1.0 - inner) * (GELU_C + 3.0 * GELU_C * GELU_A * square)


def mm(left, right, dims):
    return lax.dot_general(left, right, (dims, ((), ())), preferred_element_type=f32)


def sigmoid(x):
    return 1.0 / (1.0 + jnp.exp(-x))


def scan_rows(decay, value, reverse):
    rows = decay.shape[0]
    place = lax.broadcasted_iota(jnp.int32, decay.shape, 0)
    step = 1
    while step < rows:
        shift = rows - step if reverse else step
        inside = place < rows - step if reverse else place >= step
        before_value = jnp.where(inside, pltpu.roll(value, shift, 0), 0.0)
        before_decay = jnp.where(inside, pltpu.roll(decay, shift, 0), 1.0)
        value = value + decay * before_value
        decay = decay * before_decay
        step *= 2
    return decay, value


def gates(rate_pre, input_pre, soft):
    rate = sigmoid(rate_pre)
    log_decay = -8.0 * rate * soft
    decay = jnp.exp(log_decay)
    square = decay * decay
    root = jnp.sqrt(-jnp.tanh(log_decay) * (1.0 + square))
    return rate, decay, square, root, sigmoid(input_pre)


def table_kernel(columns, table):
    rows = columns[...].T[0:16, :].astype(f32)
    decay_param = rows[7:8, :]
    fast = jnp.exp(-decay_param)
    table[0:7, :] = rows[0:7, :]
    series = 1.0 / 6.0
    for term in (5, 4, 3, 2, 1):
        series = 1.0 / term - fast * series
    table[7:8, :] = jnp.where(fast < 0.05, fast * series, jnp.log1p(fast))
    table[8:9, :] = -fast / (1.0 + fast)
    table[9:11, :] = rows[8:10, :]
    table[11:16, :] = jnp.zeros((5, rows.shape[1]), f32)


def small_table(mixer_w, block):
    model = mixer_w.shape[0]
    return pl.pallas_call(
        table_kernel,
        grid=(1,),
        in_specs=[pl.BlockSpec((model, 128), lambda i: (0, block))],
        out_specs=pl.BlockSpec((16, model), lambda i: (0, 0)),
        out_shape=jax.ShapeDtypeStruct((16, model), f32),
        name="small_table",
    )(mixer_w)


def mixer_in_kernel(tokens, table, weights, normed, branch, gelu_pre):
    step = pl.program_id(0)

    @pl.when(step == 0)
    def _():
        normed[...] = norm_rows(tokens[...].astype(f32), table[GAIN_ONE : GAIN_ONE + 1, :]).astype(bf16)

    product = mm(normed[...], weights[...], ((1,), (0,)))
    half = pl.num_programs(0) // 2

    @pl.when(step < half)
    def _():
        branch[...] = product.astype(bf16)

    @pl.when(step >= half)
    def _():
        gelu_pre[...] = product


def mixer_in(tokens, table, mixer_w, lru, start):
    tok, model = tokens.shape
    tile = start
    tiles = lru // tile
    return pl.pallas_call(
        mixer_in_kernel,
        grid=(2 * tiles,),
        in_specs=[
            pl.BlockSpec((tok, model), lambda j: (0, 0)),
            pl.BlockSpec(table.shape, lambda j: (0, 0)),
            pl.BlockSpec((model, tile), lambda j: (0, 1 + j)),
        ],
        out_specs=[
            pl.BlockSpec((tok, model), lambda j: (0, 0)),
            pl.BlockSpec((tok, tile), lambda j: (0, jnp.minimum(j, tiles - 1))),
            pl.BlockSpec((tok, tile), lambda j: (0, jnp.maximum(j - tiles, 0))),
        ],
        out_shape=[
            jax.ShapeDtypeStruct((tok, model), bf16),
            jax.ShapeDtypeStruct((tok, lru), bf16),
            jax.ShapeDtypeStruct((tok, lru), f32),
        ],
        compiler_params=pltpu.CompilerParams(vmem_limit_bytes=16 * 1024 * 1024),
        cost_estimate=pl.CostEstimate(flops=1, bytes_accessed=1, transcendentals=0),
        name="mixer_in",
    )(tokens, table, mixer_w)


def mixer_forward(branch, prior, small, rate_w, input_w, conv, rate_pre, input_pre, cum, local, ext):
    rows = branch.shape[0]
    ext[0:8, :] = prior[...]
    ext[8:, :] = branch[...].astype(f32)
    total = small[CONV_BIAS : CONV_BIAS + 1, :] + small[TAP : TAP + 1, :] * ext[8:, :]
    for offset in range(1, 4):
        total = total + small[TAP + offset : TAP + offset + 1, :] * ext[pl.ds(8 - offset, rows), :]
    low = total.astype(bf16)
    conv[...] = low
    rate = mm(low, rate_w[...], ((1,), (0,))) + small[RATE_BIAS : RATE_BIAS + 1, :]
    inp = mm(low, input_w[...], ((1,), (0,))) + small[INPUT_BIAS : INPUT_BIAS + 1, :]
    rate_pre[...] = rate
    input_pre[...] = inp
    _, decay, _, root, opened = gates(rate, inp, small[SOFT : SOFT + 1, :])
    product, states = scan_rows(decay, root * opened * low.astype(f32), False)
    cum[...] = product
    local[...] = states


def mixer_backward_scan(grad_mixed, gelu_pre, rate_pre, cum, local, carried, small, grad_pre, rev_cum, rev_grad, pair, ext):
    rows = grad_mixed.shape[0]
    states = local[...] + cum[...] * carried[0:1, :]
    value, slope = gelu_parts(gelu_pre[...])
    grad = grad_mixed[...]
    grad_pre[...] = (grad * states * slope).astype(bf16)
    decay = jnp.exp(-8.0 * sigmoid(rate_pre[...]) * small[SOFT : SOFT + 1, :])
    ext[0:rows, :] = decay
    ext[rows:, :] = jnp.ones((8, decay.shape[1]), f32)
    product, back = scan_rows(ext[pl.ds(1, rows), :], grad * value, True)
    rev_cum[...] = product
    rev_grad[...] = back
    pair[...] = jnp.broadcast_to(decay[0:1, :] * back[0:1, :], pair.shape)


def mixer_backward(
    rev_cum, rev_grad, incoming, cum, local, carried, rate_pre, input_pre, conv, branch, prior, small, rate_w, input_w,
    own, head, rate_w_grad, input_w_grad, sums, ext, gext,
):
    rows = rev_cum.shape[0]
    soft = small[SOFT : SOFT + 1, :]
    grad_states = rev_grad[...] + rev_cum[...] * incoming[0:1, :]
    rate, decay, square, root, opened = gates(rate_pre[...], input_pre[...], soft)
    ext[0:8, :] = jnp.broadcast_to(carried[0:1, :], (8, carried.shape[1]))
    ext[8:, :] = local[...] + cum[...] * carried[0:1, :]
    before = ext[pl.ds(7, rows), :]
    low = conv[...]
    conv_in = low.astype(f32)
    grad_log = grad_states * decay * before - grad_states * opened * conv_in * square / root
    driven = grad_states * root
    grad_input = (driven * conv_in * opened * (1.0 - opened)).astype(bf16)
    by_rate = grad_log * (-8.0 * rate)
    grad_rate = (by_rate * soft * (1.0 - rate)).astype(bf16)
    sums[6:7, :] = jnp.sum(by_rate, axis=0, keepdims=True) * small[SOFT_SLOPE : SOFT_SLOPE + 1, :]
    sums[4:5, :] = jnp.sum(grad_rate.astype(f32), axis=0, keepdims=True)
    sums[5:6, :] = jnp.sum(grad_input.astype(f32), axis=0, keepdims=True)
    rate_w_grad[...] = mm(low, grad_rate, ((0,), (0,))).astype(rate_w_grad.dtype)
    input_w_grad[...] = mm(low, grad_input, ((0,), (0,))).astype(input_w_grad.dtype)
    grad_conv = (
        driven * opened
        + mm(grad_rate, rate_w[...], ((1,), (1,)))
        + mm(grad_input, input_w[...], ((1,), (1,)))
    )
    sums[7:8, :] = jnp.sum(grad_conv, axis=0, keepdims=True)
    ext[0:8, :] = prior[...]
    ext[8:, :] = branch[...].astype(f32)
    gext[0:8, :] = jnp.zeros((8, grad_conv.shape[1]), f32)
    gext[8 : 8 + rows, :] = grad_conv
    gext[8 + rows :, :] = jnp.zeros((8, grad_conv.shape[1]), f32)
    back = jnp.zeros_like(grad_conv)
    front = jnp.zeros((8, grad_conv.shape[1]), f32)
    for offset in range(4):
        tap = small[TAP + offset : TAP + offset + 1, :]
        sums[offset : offset + 1, :] = jnp.sum(
            grad_conv * ext[pl.ds(8 - offset, rows), :], axis=0, keepdims=True
        )
        back = back + tap * gext[pl.ds(8 + offset, rows), :]
        front = front + tap * gext[pl.ds(offset, 8), :]
    own[...] = back
    head[...] = front


def places():
    s = lax.axis_index("seq")
    z = lax.axis_index("fsdp")
    core = s + 1 - 2 * (s % 2)
    beside = s + 2 - 4 * ((s // 2) % 2)
    across = s + 4 - 8 * (s // 4)
    return s, z, core, beside, across


def greet(peers):
    barrier = pltpu.get_barrier_semaphore()
    for peer in peers:
        pl.semaphore_signal(barrier, inc=1, device_id=peer, device_id_type=MESH)
    pl.semaphore_wait(barrier, len(peers))


def gather_kernel(
    first, branch, gelu, outer, gate, up, down, mixer_all, mlp_mine,
    mixer, load_sem, flow_send, flow_recv, line_send, line_recv, swap_send, swap_recv, own_sem,
):
    s, z, core, beside, across = places()
    rows, cols = mixer.shape
    ff_part = mlp_mine.shape[1] // 3
    cut = cols // 256 * 128
    diag = beside + across - s
    loads, start = [], 0
    for n, part in enumerate((first, branch, gelu, outer)):
        size = part.shape[1]
        loads.append(pltpu.make_async_copy(part, mixer.at[:, pl.ds(start, size)], load_sem.at[n]))
        loads[-1].start()
        start += size
    greet([(core, z), (beside, z), (across, z)] + [(s, (z + k) % 4) for k in range(1, 4)])

    def remote(src, dst, send, recv, target):
        return pltpu.make_async_remote_copy(
            src_ref=src, dst_ref=dst, send_sem=send, recv_sem=recv, device_id=target, device_id_type=MESH
        )

    def piece(seq, zz, half=None):
        span = pl.ds(pl.multiple_of((seq * 4 + zz) * rows, 16), rows)
        if half is None:
            return mixer_all.at[span, :]
        return mixer_all.at[span, pl.ds(0, cut) if half == 0 else pl.ds(cut, cols - cut)]

    def flow(zz, index, seq, half, target, src=None):
        ref = piece(seq, zz, half)
        return remote(
            ref if src is None else src, ref, flow_send.at[zz, index], flow_recv.at[zz, index], (target, z)
        )

    def sends(zz, src=None):
        return [
            flow(zz, 0, s, None, beside, src),
            flow(zz, 1, s, None, across, src),
            flow(zz, 4, s, None, core, src),
        ]

    def spread(zz, src=None):
        for copy in sends(zz, src):
            copy.start()

    def relay(zz):
        flow(zz, 0, beside, None, beside).wait_recv()
        flow(zz, 3, beside, 0, across).start()
        flow(zz, 5, beside, None, core).start()
        flow(zz, 1, across, None, across).wait_recv()
        flow(zz, 2, across, 1, beside).start()
        flow(zz, 6, across, None, core).start()

    def finish(zz):
        flow(zz, 3, diag, 0, across).wait_recv()
        flow(zz, 7, diag, 0, core).start()
        flow(zz, 2, diag, 1, beside).wait_recv()
        flow(zz, 8, diag, 1, core).start()

    def drain(zz, src=None):
        for copy in sends(zz, src):
            copy.wait_send()
        flow(zz, 3, beside, 0, across).wait_send()
        flow(zz, 5, beside, None, core).wait_send()
        flow(zz, 2, across, 1, beside).wait_send()
        flow(zz, 6, across, None, core).wait_send()
        flow(zz, 7, diag, 0, core).wait_send()
        flow(zz, 8, diag, 1, core).wait_send()
        flip = core - s
        flow(zz, 4, core, None, core).wait_recv()
        flow(zz, 5, beside + flip, None, core).wait_recv()
        flow(zz, 6, across + flip, None, core).wait_recv()
        flow(zz, 7, diag + flip, 0, core).wait_recv()
        flow(zz, 8, diag + flip, 1, core).wait_recv()

    def line(zz, up_way, hop, src=None):
        ref = piece(s, zz)
        way = 0 if up_way else 1
        target = z + 1 if up_way else z - 1
        return remote(
            ref if src is None else src, ref, line_send.at[way, hop], line_recv.at[way, hop], (s, target)
        )

    def line_hop(hop):
        def below():
            line(z - hop, True, hop - 1).wait_recv()
            pl.when(z < 3)(lambda: line(z - hop, True, hop).start())

        def above():
            line(z + hop, False, hop - 1).wait_recv()
            pl.when(z > 0)(lambda: line(z + hop, False, hop).start())

        pl.when(z >= hop)(below)
        pl.when(z + hop <= 3)(above)

    def at_hop(hop, act):
        pl.when(z >= hop)(lambda: act(z - hop))
        pl.when(z + hop <= 3)(lambda: act(z + hop))

    def landing(m, zz):
        return mlp_mine.at[pl.ds(pl.multiple_of(zz * rows, 16), rows), pl.ds(m * ff_part, ff_part)]

    def columns(m, zz):
        return (gate, up, down)[m].at[:, pl.ds(pl.multiple_of(zz * ff_part, 128), ff_part)]

    def swap(k, m, arriving=False):
        to = (z + k) % 4
        came = (z + 4 - k) % 4
        return remote(
            columns(m, to), landing(m, came if arriving else z), swap_send.at[k - 1, m], swap_recv.at[k - 1, m], (s, to)
        )

    local = [pltpu.make_async_copy(columns(m, z), landing(m, z), own_sem.at[m]) for m in range(3)]
    local.append(pltpu.make_async_copy(mixer, piece(s, z), own_sem.at[3]))
    for copy in loads:
        copy.wait()

    pl.when(z < 3)(lambda: line(z, True, 0, mixer).start())
    pl.when(z > 0)(lambda: line(z, False, 0, mixer).start())
    spread(z, mixer)
    for copy in local:
        copy.start()
    line_hop(1)
    at_hop(1, spread)
    relay(z)
    line_hop(2)
    at_hop(2, spread)
    finish(z)
    at_hop(1, relay)
    line_hop(3)
    at_hop(3, spread)
    for k in (1, 3, 2):
        for m in range(3):
            swap(k, m).start()
    at_hop(1, finish)
    at_hop(2, relay)
    at_hop(3, relay)
    at_hop(2, finish)
    at_hop(3, finish)
    drain(z, mixer)
    for hop in range(1, 4):
        at_hop(hop, drain)
    for copy in local:
        copy.wait()
    for k in (1, 3, 2):
        for m in range(3):
            swap(k, m).wait_send()
            swap(k, m, True).wait_recv()
    pl.when(z < 3)(lambda: line(z, True, 0, mixer).wait_send())
    pl.when(z > 0)(lambda: line(z, False, 0, mixer).wait_send())
    for hop in range(1, 3):
        pl.when((z >= hop) & (z < 3))(lambda: line(z - hop, True, hop).wait_send())
        pl.when((z + hop <= 3) & (z > 0))(lambda: line(z + hop, False, hop).wait_send())


def gather(first, branch, gelu, outer, gate, up, down):
    rows = first.shape[0]
    cols = first.shape[1] + branch.shape[1] + gelu.shape[1] + outer.shape[1]
    ff_part = gate.shape[1] // 4
    anyspec = pl.BlockSpec(memory_space=pl.ANY)
    dma = pltpu.SemaphoreType.DMA
    return pl.pallas_call(
        gather_kernel,
        in_specs=[anyspec] * 7,
        out_specs=[anyspec] * 2,
        out_shape=[
            jax.ShapeDtypeStruct((32 * rows, cols), bf16),
            jax.ShapeDtypeStruct((4 * rows, 3 * ff_part), bf16),
        ],
        scratch_shapes=[
            pltpu.VMEM((rows, cols), bf16), dma((4,)),
            dma((4, 9)), dma((4, 9)), dma((2, 3)), dma((2, 3)), dma((3, 3)), dma((3, 3)), dma((4,)),
        ],
        compiler_params=pltpu.CompilerParams(collective_id=1, has_side_effects=True),
        name="gather_weights",
    )(first, branch, gelu, outer, gate, up, down)


def rows_kernel(
    normed, grad0, grad1, grad2, grad3, first, mixed, normed_all, normed_other, grad_all, grad_other,
    first_other, mixed_other, line_send, line_recv, core_send, core_recv, own_sem, held, give_send, give_recv,
):
    s, z, core, _, _ = places()
    tok = normed.shape[0]
    cuts = 4
    grads = (grad0, grad1, grad2, grad3)
    greet([(core, z)] + [(s, (z + k) % 4) for k in range(1, 4)])

    def rows(ref, zz):
        return ref.at[pl.ds(pl.multiple_of(zz * tok, 16), tok), :]

    def remote(src, dst, send, recv, target):
        return pltpu.make_async_remote_copy(
            src_ref=src, dst_ref=dst, send_sem=send, recv_sem=recv, device_id=target, device_id_type=MESH
        )

    def parts(ref):
        size = tok // cuts
        return [ref.at[pl.ds(n * size, size), :] for n in range(cuts)]

    def line(zz, up_way, hop):
        way = 0 if up_way else 1
        target = z + 1 if up_way else z - 1
        src = normed if hop == 0 else rows(normed_all, zz)
        dst = rows(normed_all, zz)
        return [
            remote(a, b, line_send.at[way, hop, n], line_recv.at[way, hop, n], (s, target))
            for n, (a, b) in enumerate(zip(parts(src), parts(dst)))
        ]

    def over(zz, own=False):
        src = normed if own else rows(normed_all, zz)
        return remote(src, rows(normed_other, zz), core_send.at[0, zz], core_recv.at[0, zz], (core, z))

    def grad_over(k):
        zz = (z + 4 - k) % 4
        return remote(grads[k], rows(grad_other, zz), core_send.at[1, zz], core_recv.at[1, zz], (core, z))

    def line_start(zz, up_way, hop):
        for copy in line(zz, up_way, hop):
            copy.start()

    def line_drain(zz, up_way, hop):
        for copy in line(zz, up_way, hop):
            copy.wait_send()

    def hop_step(hop):
        def below():
            for came, on in zip(line(z - hop, True, hop - 1), line(z - hop, True, hop) if hop < 3 else [None] * cuts):
                came.wait_recv()
                if on is not None:
                    pl.when(z < 3)(on.start)
            over(z - hop).start()

        def above():
            for came, on in zip(line(z + hop, False, hop - 1), line(z + hop, False, hop) if hop < 3 else [None] * cuts):
                came.wait_recv()
                if on is not None:
                    pl.when(z > 0)(on.start)
            over(z + hop).start()

        pl.when(z >= hop)(below)
        pl.when(z + hop <= 3)(above)

    given = [
        remote(source, target, give_send.at[n], give_recv.at[n], (core, z))
        for n, (source, target) in enumerate(((first, first_other), (mixed, mixed_other)))
    ]
    local = [pltpu.make_async_copy(grads[k], held.at[k], own_sem.at[k]) for k in range(4)]
    local.append(pltpu.make_async_copy(normed, held.at[4], own_sem.at[4]))
    stored = [
        pltpu.make_async_copy(held.at[k], rows(grad_all, (z + 4 - k) % 4), own_sem.at[k]) for k in range(4)
    ]
    stored.append(pltpu.make_async_copy(held.at[4], rows(normed_all, z), own_sem.at[4]))
    pl.when(z < 3)(lambda: line_start(z, True, 0))
    pl.when(z > 0)(lambda: line_start(z, False, 0))
    over(z, True).start()
    for copy in local:
        copy.start()
    for k in range(4):
        grad_over(k).start()
    for copy in given:
        copy.start()
    for copy, store in zip(local, stored):
        copy.wait()
        store.start()
    for hop in range(1, 4):
        hop_step(hop)
    for copy in stored:
        copy.wait()
    for k in range(4):
        grad_over(k).wait()
    for copy in given:
        copy.wait()
    over(z, True).wait()
    for k in range(1, 4):
        over((z + k) % 4).wait()
    pl.when(z < 3)(lambda: line_drain(z, True, 0))
    pl.when(z > 0)(lambda: line_drain(z, False, 0))
    for hop in range(1, 3):
        pl.when((z >= hop) & (z < 3))(lambda: line_drain(z - hop, True, hop))
        pl.when((z + hop <= 3) & (z > 0))(lambda: line_drain(z + hop, False, hop))


def gather_rows(normed, grads, first, mixed):
    tok, model = normed.shape
    anyspec = pl.BlockSpec(memory_space=pl.ANY)
    dma = pltpu.SemaphoreType.DMA
    return pl.pallas_call(
        rows_kernel,
        in_specs=[anyspec] * 7,
        out_specs=[anyspec] * 6,
        out_shape=[jax.ShapeDtypeStruct((4 * tok, model), bf16)] * 4
        + [jax.ShapeDtypeStruct(first.shape, bf16), jax.ShapeDtypeStruct(mixed.shape, bf16)],
        scratch_shapes=[
            dma((2, 3, 4)), dma((2, 3, 4)), dma((2, 4)), dma((2, 4)), dma((5,)),
            pltpu.VMEM((5, tok, model), bf16), dma((2,)), dma((2,)),
        ],
        compiler_params=pltpu.CompilerParams(collective_id=3, has_side_effects=True),
        name="gather_rows",
    )(normed, *grads, first, mixed)


def column_tiles(cols, size=512):
    return [(start, min(size, cols - start)) for start in range(0, cols, size)]


def feed_forward_kernel(
    normed, grad_out, weights, hidden, hidden_other, pair, pair_other, back,
    held, hidden_now, pair_now, sems, store_sem, core_send, core_recv,
):
    s, z, core, _, _ = places()
    step = pl.program_id(0)
    ff_part = held.shape[2]
    model = held.shape[1]
    rows = normed.shape[0]
    tiles = column_tiles(ff_part)
    made = ((hidden_now, hidden, hidden_other), (pair_now, pair, pair_other))

    def load(n, m):
        start, size = tiles[n]
        return pltpu.make_async_copy(
            weights.at[:, pl.ds(m * ff_part + start, size)], held.at[m, :, pl.ds(start, size)], sems.at[n, m]
        )

    def kept(n, turn):
        now, mine, _ = made[n]
        return pltpu.make_async_copy(now.at[turn], mine.at[pl.ds(turn * rows, rows), :], store_sem.at[turn, n])

    def handed(n, turn):
        now, _, other = made[n]
        return pltpu.make_async_remote_copy(
            src_ref=now.at[turn],
            dst_ref=other.at[pl.ds(turn * rows, rows), :],
            send_sem=core_send.at[turn, n],
            recv_sem=core_recv.at[turn, n],
            device_id=(core, z),
            device_id_type=MESH,
        )

    @pl.when(step == 0)
    def _():
        for n in range(len(tiles)):
            for m in range(3):
                load(n, m).start()
        greet([(core, z)])

    def forth(turn):
        for n, (start, size) in enumerate(tiles):
            cols = slice(start, start + size)
            if turn == 0:
                for m in range(3):
                    load(n, m).wait()
            gate = mm(normed[...], held[0, :, cols], ((1,), (0,)))
            up = mm(normed[...], held[1, :, cols], ((1,), (0,)))
            grad_hidden = mm(grad_out[...], held[2, :, cols], ((1,), (0,)))
            value, slope = gelu_parts(gate)
            hidden_now[turn, :, cols] = (value * up).astype(bf16)
            pair_now[turn, :, cols] = (grad_hidden * up * slope).astype(bf16)
            pair_now[turn, :, slice(ff_part + start, ff_part + start + size)] = (grad_hidden * value).astype(bf16)
        for n in range(2):
            handed(n, turn).start()
            kept(n, turn).start()

    for turn in range(2):
        pl.when(step == turn)(functools.partial(forth, turn))

    def back_tile(turn, carry):
        cols = pl.ds(pl.multiple_of(turn * 512, 512), 512)
        total = mm(pair_now[step, :, :ff_part], held[0, cols, :], ((1,), (1,)))
        total = total + mm(pair_now[step, :, ff_part:], held[1, cols, :], ((1,), (1,)))
        back[:, cols] = total.astype(bf16)
        return carry

    lax.fori_loop(0, model // 512, back_tile, 0)

    @pl.when(step == 1)
    def _():
        for turn in range(2):
            for n in range(2):
                kept(n, turn).wait()
                handed(n, turn).wait()


def feed_forward(normed, grad_out, weights):
    tok, model = normed.shape
    ff_part = weights.shape[1] // 3
    rows = tok // 2
    anyspec = pl.BlockSpec(memory_space=pl.ANY)
    dma = pltpu.SemaphoreType.DMA
    block = pl.BlockSpec((rows, model), lambda i: (i, 0))
    return pl.pallas_call(
        feed_forward_kernel,
        grid=(2,),
        in_specs=[block, block, anyspec],
        out_specs=[anyspec] * 4 + [block],
        out_shape=[
            jax.ShapeDtypeStruct((tok, cols), bf16)
            for cols in (ff_part, ff_part, 2 * ff_part, 2 * ff_part, model)
        ],
        scratch_shapes=[
            pltpu.VMEM((3, model, ff_part), bf16),
            pltpu.VMEM((2, rows, ff_part), bf16),
            pltpu.VMEM((2, rows, 2 * ff_part), bf16),
            dma((len(column_tiles(ff_part)), 3)), dma((2, 2)), dma((2, 2)), dma((2, 2)),
        ],
        compiler_params=pltpu.CompilerParams(
            collective_id=4, has_side_effects=True, vmem_limit_bytes=60 * 1024 * 1024
        ),
        name="feed_forward",
    )(normed, grad_out, weights)


def add_columns(target, sources, start, size, step):
    def one(turn, carry):
        cols = pl.ds(pl.multiple_of(start + turn * step, 128), step)
        total = target[:, cols].astype(f32)
        for source in sources:
            total = total + source[:, cols].astype(f32)
        target[:, cols] = total.astype(target.dtype)
        return carry

    lax.fori_loop(0, size // step, one, 0)


def shared_products_kernel(
    normed, normed_other, grad, grad_other, weights, pair, pair_other, hidden, hidden_other,
    beside_high, across_low, mine, beside_low, across_high, out,
    turned, slots, stage, right, diag, landed, waiting, down_now, out_now,
    load_sem, right_sem, send_sem, recv_sem, store_sem, down_sem, out_sem,
):
    s, z, _, beside, across = places()
    step = pl.program_id(0)
    lefts = ((normed, normed_other), (grad, grad_other))
    chip_cols = normed.shape[1] // 4
    half = chip_cols // 2
    piece = half // 2
    width = hidden.shape[1]
    tok = normed.shape[0]
    diagonal = beside + across - s
    chips = [q // 2 for q in (diagonal, beside, across, s)]

    def load(side, q, who):
        cols = pl.ds(pl.multiple_of(chips[q] * chip_cols, 128), chip_cols)
        return pltpu.make_async_copy(lefts[side][who].at[:, cols], slots.at[q % 2, who], load_sem.at[q % 2, who])

    def fetch(side):
        for q in range(2):
            for who in range(2):
                load(side, q, who).start()

    def turn(side):
        for q in range(4):
            for who in range(2):
                load(side, q, who).wait()
                stage[...] = slots[q % 2, who].T
                turned[q * half : (q + 1) * half, who * tok : (who + 1) * tok] = stage[
                    pl.ds(pl.multiple_of(s % 2 * half, 16), half), :
                ]
                if q < 2:
                    load(side, q + 2, who).start()

    pieces = column_tiles(width)

    def push(way, cols, index):
        return pltpu.make_async_remote_copy(
            src_ref=diag.at[way, :, cols],
            dst_ref=landed.at[way, :, cols],
            send_sem=send_sem.at[way, index],
            recv_sem=recv_sem.at[way, index],
            device_id=(across if way == 0 else beside, z),
            device_id_type=MESH,
        )

    def take(j):
        sources = (hidden, hidden_other) if j == 2 else (pair, pair_other)
        return [
            pltpu.make_async_copy(
                source.at[:, pl.ds(0 if j == 2 else j * width, width)],
                right.at[j % 2, pl.ds(who * tok, tok), :],
                right_sem.at[j % 2, who],
            )
            for who, source in enumerate(sources)
        ]

    def take_start(j):
        for copy in take(j):
            copy.start()

    def take_wait(j):
        for copy in take(j):
            copy.wait()

    def tile(start, size):
        cols = pl.ds(start, size)
        block = mm(turned[...], right[step % 2, :, cols], ((1,), (0,))).astype(bf16)
        parts = [block[n * piece : (n + 1) * piece] for n in range(8)]
        there = pl.ds(pl.multiple_of(step * width + start, 128), size)
        index = step * len(pieces) + start // 512
        diag[0, :, there] = parts[0]
        diag[1, :, there] = parts[1]
        waiting[0, :, there] = parts[2]
        beside_high[:, cols] = parts[3]
        across_low[:, cols] = parts[4]
        waiting[1, :, there] = parts[5]
        mine[0:piece, cols] = parts[6]
        mine[piece:, cols] = parts[7]
        for way in range(2):
            push(way, there, index).start()

    def multiply():
        def one(turn, carry):
            tile(pl.multiple_of(turn * 512, 512), 512)
            return carry

        lax.fori_loop(0, width // 512, one, 0)
        if width % 512:
            tile(width // 512 * 512, width % 512)

    def store(way, j):
        cols = pl.ds(j * width, width)
        return pltpu.make_async_copy(
            waiting.at[way, :, cols], (beside_low, across_high)[way].at[:, cols], store_sem.at[way, j]
        )

    out_rows = down_now.shape[1]
    out_tiles = weights.shape[0] // out_rows

    def down(t):
        source = weights.at[pl.ds(t * out_rows, out_rows), pl.ds(2 * width, width)]
        return pltpu.make_async_copy(source, down_now.at[t % 2], down_sem.at[t % 2])

    def out_store(t):
        return pltpu.make_async_copy(
            out_now.at[t % 2], out.at[:, pl.ds(t * out_rows, out_rows)], out_sem.at[t % 2]
        )

    def out_product():
        for t in range(out_tiles):
            down(t).wait()
            if t > 1:
                out_store(t - 2).wait()
            out_now[t % 2] = mm(right[0, 0:tok, :], down_now[t % 2], ((1,), (1,))).astype(bf16)
            out_store(t).start()
            if t + 2 < out_tiles:
                down(t + 2).start()

    @pl.when(step == 0)
    def _():
        fetch(0)
        take_start(0)
        take_start(1)
        greet([(beside, z), (across, z)])
        turn(0)
        take_wait(0)

    @pl.when(step == 1)
    def _():
        take_wait(1)
        take_start(2)
        fetch(1)

    @pl.when(step == 2)
    def _():
        down(0).start()
        down(1).start()
        turn(1)
        take_wait(2)

    multiply()
    @pl.when(step == 2)
    def _():
        out_product()
        pushed = [
            (way, pl.ds(j * width + start, size), j * len(pieces) + n, j)
            for j in range(3)
            for n, (start, size) in enumerate(pieces)
            for way in range(2)
        ]
        for way, cols, index, j in pushed:
            push(way, cols, index).wait_recv()
            if index % len(pieces) == len(pieces) - 1:
                add_columns(waiting.at[way], [landed.at[way]], j * width, width, 384)
                store(way, j).start()
        for way, cols, index, j in pushed:
            push(way, cols, index).wait_send()
        for j in range(3):
            for way in range(2):
                store(way, j).wait()
        for t in range(out_tiles - 2, out_tiles):
            out_store(t).wait()


def shared_products(lefts, weights, pair, hidden):
    tok, model = lefts[0].shape
    width = hidden[0].shape[1]
    half = model // 8
    anyspec = pl.BlockSpec(memory_space=pl.ANY)
    dma = pltpu.SemaphoreType.DMA

    def block(rows):
        return pl.BlockSpec((rows, width), lambda j: (0, j))

    rows_out = (half // 2, half // 2, half, half // 2, half // 2)
    return pl.pallas_call(
        shared_products_kernel,
        grid=(3,),
        in_specs=[anyspec] * 9,
        out_specs=[block(rows) for rows in rows_out[:3]] + [anyspec] * 3,
        out_shape=[jax.ShapeDtypeStruct((rows, 3 * width), bf16) for rows in rows_out]
        + [jax.ShapeDtypeStruct((tok, model), bf16)],
        scratch_shapes=[
            pltpu.VMEM((4 * half, 2 * tok), bf16),
            pltpu.VMEM((2, 2, tok, 2 * half), bf16),
            pltpu.VMEM((2 * half, tok), bf16),
            pltpu.VMEM((2, 2 * tok, width), bf16),
            pltpu.VMEM((2, half // 2, 3 * width), bf16),
            pltpu.VMEM((2, half // 2, 3 * width), bf16),
            pltpu.VMEM((2, half // 2, 3 * width), bf16),
            pltpu.VMEM((2, 512, width), bf16),
            pltpu.VMEM((2, tok, 512), bf16),
            dma((2, 2)), dma((2, 2)), dma((2, 12)), dma((2, 12)), dma((2, 3)), dma((2,)), dma((2,)),
        ],
        compiler_params=pltpu.CompilerParams(
            collective_id=5, has_side_effects=True, vmem_limit_bytes=60 * 1024 * 1024
        ),
        name="feed_forward_products",
    )(*lefts, weights, *pair, *hidden)


def scatter_kernel(
    normed, normed_other, grad_mix, mix_other, mixed, mixed_other, grad_gelu, gelu_other, grad_branch, rest,
    mlp_low, mlp_high, mixer_w, tokens, gain, mixer_sum, mlp_back, input_grad,
    held, cross, near, lined, left_now, both_now, mixed_now, turned, stage, rest_other, back_now, wide_now, gain_now,
    load_sem, core_send, core_recv, wide_sem,
    flow_send, flow_recv, line_send, line_recv, swap_send, swap_recv, own_sem,
):
    s, z, core, beside, across = places()
    chip_diag, chip_beside, chip_across, chip = 0, 1, 2, 3
    chips = [q // 2 for q in (beside + across - s, beside, across, s)]
    rows = held.shape[1] // 4
    cols = held.shape[2]
    cut = cols // 256 * 128
    ff_part = mlp_low.shape[1] // 3
    tok, model = tokens.shape
    half = 4 * rows
    lru = grad_branch.shape[1]
    lru2 = 2 * lru
    rest_start = lru2 + mixed.shape[1]
    order = (3 * (1 - z // 2), (2 + 3 * z) % 5, 1 + z % 2, z)

    def remote(src, dst, send, recv, target):
        return pltpu.make_async_remote_copy(
            src_ref=src, dst_ref=dst, send_sem=send, recv_sem=recv, device_id=target, device_id_type=MESH
        )

    def span(k):
        return pl.ds(pl.multiple_of(k * rows, 16), rows)

    mine, other = pl.ds(0, tok), pl.ds(tok, tok)
    loads = [
        pltpu.make_async_copy(source, target, load_sem.at[n])
        for n, (source, target) in enumerate(
            (
                (grad_mix, left_now.at[1, mine, :]),
                (mix_other, left_now.at[1, other, :]),
                (mixed, mixed_now.at[mine, :]),
                (mixed_other, mixed_now.at[other, :]),
                (normed, left_now.at[0, mine, :]),
                (normed_other, left_now.at[0, other, :]),
                (grad_gelu, both_now.at[mine, pl.ds(lru, lru)]),
                (gelu_other, both_now.at[other, pl.ds(lru, lru)]),
                (grad_branch, both_now.at[mine, pl.ds(0, lru)]),
            )
        )
    ]

    def push(n):
        if n == 0:
            source, target = grad_branch, both_now.at[other, pl.ds(0, lru)]
        else:
            source = rest.at[pl.ds(pl.multiple_of(chips[n - 1] * 2 * half + (1 - s % 2) * half, 16), half), :]
            target = rest_other.at[n - 1]
        return pltpu.make_async_remote_copy(
            src_ref=source,
            dst_ref=target,
            send_sem=core_send.at[n],
            recv_sem=core_recv.at[n],
            device_id=(core, z),
            device_id_type=MESH,
        )

    def rest_load(q):
        source = rest.at[pl.ds(pl.multiple_of(chips[q] * 2 * half + s % 2 * half, 16), half), :]
        return pltpu.make_async_copy(
            source, held.at[q, :, pl.ds(rest_start, cols - rest_start)], load_sem.at[9 + q]
        )

    def turn(side):
        for q in range(4):
            source = left_now[side, :, pl.ds(pl.multiple_of(chips[q] * 2 * half, 128), 2 * half)]
            stage[...] = source.T
            turned[side, q * half : (q + 1) * half, :] = stage[
                pl.ds(pl.multiple_of(s % 2 * half, 16), half), :
            ]

    def multiply(q, side, first=0, last=None):
        right, start = ((both_now, 0), (mixed_now, lru2))[side]

        def one(turn, carry):
            here = pl.multiple_of(turn * 512, 512)
            block = mm(turned[side, q * half : (q + 1) * half, :], right[:, pl.ds(here, 512)], ((1,), (0,)))
            held[q, :, pl.ds(pl.multiple_of(start + here, 512), 512)] = block.astype(bf16)
            return carry

        lax.fori_loop(first // 512, (right.shape[1] if last is None else last) // 512, one, 0)

    def add_rest(q):
        rest_load(q).wait()
        push(1 + q).wait_recv()
        held[q, :, rest_start:] = add_low(held[q, :, rest_start:], rest_other[q])

    left, right = pl.ds(0, cut), pl.ds(cut, cols - cut)

    def block(q, i, side):
        return held.at[q, span(order[i]), side]

    def flow(i, index):
        send, recv = flow_send.at[i, index], flow_recv.at[i, index]
        to_beside, to_across = (beside, z), (across, z)
        if index == 0:
            return remote(block(chip_diag, i, left), cross.at[i, :, left], send, recv, to_across)
        if index == 1:
            return remote(block(chip_diag, i, right), cross.at[i, :, right], send, recv, to_beside)
        if index == 2:
            return remote(block(chip_beside, i, right), near.at[0, i, :, right], send, recv, to_beside)
        if index == 3:
            return remote(block(chip_beside, i, left), near.at[0, i, :, left], send, recv, to_beside)
        if index == 4:
            return remote(block(chip_across, i, left), near.at[1, i, :, left], send, recv, to_across)
        return remote(block(chip_across, i, right), near.at[1, i, :, right], send, recv, to_across)

    def cross_step(i):
        flow(i, 0).wait_recv()
        add_columns(held.at[chip_beside, span(order[i]), :], [cross.at[i]], 0, cut, 512)
        flow(i, 3).start()
        flow(i, 1).wait_recv()
        add_columns(held.at[chip_across, span(order[i]), :], [cross.at[i]], cut, cols - cut, 384)
        flow(i, 5).start()

    def near_step(i):
        for index in (2, 4, 3, 5):
            flow(i, index).wait_recv()
        add_columns(held.at[chip, span(order[i]), :], [near.at[0, i], near.at[1, i]], 0, cols, 640)

    def line(k, slot, target):
        return remote(
            held.at[chip, span(k), :], lined.at[slot], line_send.at[k], line_recv.at[slot], (s, target)
        )

    def absorb(k, slot, source):
        line(k, slot, source).wait_recv()
        add_columns(held.at[chip, span(k), :], [lined.at[slot]], 0, cols, 640)

    def chain(i):
        k = order[i]
        if i == 3:
            pl.when(z > 0)(lambda: absorb(k, k, z - 1))
            pl.when(z < 3)(lambda: absorb(k, 4, z + 1))
            return

        @pl.when(k > z)
        def _():
            pl.when(z > 0)(lambda: absorb(k, k, z - 1))
            line(k, k, z + 1).start()

        @pl.when(k < z)
        def _():
            pl.when(z < 3)(lambda: absorb(k, k, z + 1))
            pl.when(k == z - 1)(lambda: line(k, 4, z - 1).start())
            pl.when(k < z - 1)(lambda: line(k, k, z - 1).start())

    def chain_drain():
        for i in range(3):
            k = order[i]
            line(k, k, (z + 1) % 4).wait_send()

    def swap(k, high=False):
        to = (z + k) % 4
        here = pl.ds(pl.multiple_of(z * ff_part, 128), ff_part)
        source = (mlp_high if high else mlp_low).at[span(to % 2), :]
        return [
            remote(
                source.at[:, pl.ds(m * ff_part, ff_part)],
                mlp_back.at[m, :, here],
                swap_send.at[k - 1, m],
                swap_recv.at[k - 1, m],
                (s, to),
            )
            for m in range(3)
        ]

    def swap_start(k):
        to = (z + k) % 4

        @pl.when(to < 2)
        def _():
            for copy in swap(k):
                copy.start()

        @pl.when(to >= 2)
        def _():
            for copy in swap(k, True):
                copy.start()

    def own(high=False):
        here = pl.ds(pl.multiple_of(z * ff_part, 128), ff_part)
        source = (mlp_high if high else mlp_low).at[span(z % 2), :]
        return [
            pltpu.make_async_copy(source.at[:, pl.ds(m * ff_part, ff_part)], mlp_back.at[m, :, here], own_sem.at[m])
            for m in range(3)
        ]

    wide_rows = wide_now.shape[0]
    wide_tiles = mixer_w.shape[0] // wide_rows
    wide_start = mixer_w.shape[1] - lru2 - model
    wide_slots = (both_now.at[pl.ds(tok, wide_rows), :], wide_now)

    def wide(j):
        source = mixer_w.at[pl.ds(j * wide_rows, wide_rows), pl.ds(wide_start, lru2)]
        return pltpu.make_async_copy(source, wide_slots[j % 2], wide_sem.at[j % 2])

    plain_loads = [
        pltpu.make_async_copy(tokens, left_now.at[0, pl.ds(0, tok), :], wide_sem.at[2]),
        pltpu.make_async_copy(gain, gain_now, wide_sem.at[3]),
    ]

    def back(first, last):
        for j in range(first, last):
            wide(j).wait()
            back_now[:, pl.ds(j * wide_rows, wide_rows)] = mm(
                both_now[0:tok, :], wide_slots[j % 2][...], ((1,), (1,))
            )
            if j + 2 < wide_tiles:
                wide(j + 2).start()

    def finish_rows(turn, carry):
        at = pl.ds(pl.multiple_of(turn * 16, 16), 16)
        result = left_now[1, at, :].astype(f32) + norm_back(
            left_now[0, at, :].astype(f32), gain_now[GAIN_ONE : GAIN_ONE + 1, :], back_now[at, :]
        )
        left_now[0, at, :] = result.astype(bf16)
        return carry

    for copy in loads:
        copy.start()
    for q in range(4):
        rest_load(q).start()
    greet([(core, z), (beside, z), (across, z)] + [(s, (z + k) % 4) for k in range(1, 4)])
    for n in range(5):
        push(n).start()
    for k in (1, 3, 2):
        swap_start(k)

    @pl.when(z < 2)
    def _():
        for copy in own():
            copy.start()

    @pl.when(z >= 2)
    def _():
        for copy in own(True):
            copy.start()

    for copy in loads[:4]:
        copy.wait()
    turn(1)
    multiply(chip_diag, 1)
    for copy in loads[4:]:
        copy.wait()
    turn(0)
    multiply(chip_diag, 0, lru)
    add_rest(chip_diag)
    for i in range(2):
        flow(i, 1).start()
    push(0).wait_recv()
    multiply(chip_diag, 0, 0, lru)
    for i in range(2):
        flow(i, 0).start()
    for q in (chip_beside, chip_across, chip):
        multiply(q, 0)
        multiply(q, 1)
        add_rest(q)
        if q == chip_beside:
            flow(0, 2).start()
        if q == chip_across:
            flow(0, 4).start()
    for copy in plain_loads:
        copy.start()
    wide(0).start()
    wide(1).start()
    for i in range(4):
        cross_step(i)
        if i + 1 < 4:
            flow(i + 1, 2).start()
            flow(i + 1, 4).start()
        if i + 2 < 4:
            flow(i + 2, 0).start()
            flow(i + 2, 1).start()
        if i > 0:
            near_step(i - 1)
            chain(i - 1)
            back(wide_tiles * (i - 1) // 3, wide_tiles * i // 3)
    for copy in plain_loads:
        copy.wait()
    lax.fori_loop(0, tok // 16, finish_rows, 0)
    finished = pltpu.make_async_copy(left_now.at[0, pl.ds(0, tok), :], input_grad, wide_sem.at[2])
    finished.start()
    near_step(3)
    chain(3)
    done = pltpu.make_async_copy(held.at[chip, span(z), :], mixer_sum, own_sem.at[3])
    done.start()
    for i in range(4):
        for index in range(6):
            flow(i, index).wait_send()
    chain_drain()
    for k in range(1, 4):
        for copy in swap(k):
            copy.wait()
    for copy in own():
        copy.wait()
    for n in range(5):
        push(n).wait_send()
    finished.wait()
    done.wait()


def scatter(rows_pairs, grad_branch, rest, mlp_low, mlp_high, mixer_w, tokens, gain):
    tok, model = tokens.shape
    rows = model // 32
    lru = grad_branch.shape[1]
    cols = 3 * lru + rest.shape[1]
    ff_part = mlp_low.shape[1] // 3
    anyspec = pl.BlockSpec(memory_space=pl.ANY)
    dma = pltpu.SemaphoreType.DMA
    return pl.pallas_call(
        scatter_kernel,
        in_specs=[anyspec] * 15,
        out_specs=[anyspec] * 3,
        out_shape=[
            jax.ShapeDtypeStruct((rows, cols), bf16),
            jax.ShapeDtypeStruct((3, rows, 4 * ff_part), bf16),
            jax.ShapeDtypeStruct((tok, model), bf16),
        ],
        scratch_shapes=[
            pltpu.VMEM((4, 4 * rows, cols), bf16),
            pltpu.VMEM((4, rows, cols), bf16),
            pltpu.VMEM((2, 4, rows, cols), bf16),
            pltpu.VMEM((5, rows, cols), bf16),
            pltpu.VMEM((2, 2 * tok, model), bf16),
            pltpu.VMEM((2 * tok, 2 * lru), bf16),
            pltpu.VMEM((2 * tok, lru), bf16),
            pltpu.VMEM((2, 16 * rows, 2 * tok), bf16),
            pltpu.VMEM((8 * rows, 2 * tok), bf16),
            pltpu.VMEM((4, 4 * rows, rest.shape[1]), bf16),
            pltpu.VMEM((tok, model), f32),
            pltpu.VMEM((128, 2 * lru), bf16),
            pltpu.VMEM(gain.shape, f32),
            dma((13,)), dma((5,)), dma((5,)), dma((4,)),
            dma((4, 6)), dma((4, 6)), dma((4,)), dma((5,)), dma((3, 3)), dma((3, 3)), dma((4,)),
        ],
        compiler_params=pltpu.CompilerParams(
            collective_id=2, has_side_effects=True, vmem_limit_bytes=62 * 1024 * 1024
        ),
        name="scatter_gradients",
    )(*rows_pairs, grad_branch, rest, mlp_low, mlp_high, mixer_w, tokens, gain)


def gather_plain(mixer, gate, up, down):
    groups = lax.axis_size("fsdp")
    part_rows, ff = gate.shape
    own = jnp.stack([w.reshape(part_rows, groups, ff // groups) for w in (gate, up, down)], axis=2)
    mine = lax.all_to_all(jnp.transpose(own, (1, 0, 2, 3)), "fsdp", 0, 0, tiled=True)
    return lax.all_gather(mixer, both, axis=0, tiled=True), mine.reshape(groups * part_rows, -1)


def from_line(shard):
    count = lax.axis_size("fsdp")
    return [shard] + [
        lax.ppermute(shard, "fsdp", [(i, (i + k) % count) for i in range(count)]) for k in range(1, count)
    ]


def swap_cores(shard):
    count = lax.axis_size("seq")
    return lax.ppermute(shard, "seq", [(i, i + 1 - 2 * (i % 2)) for i in range(count)])


def swap_beside(shard):
    return lax.ppermute(shard, "seq", [(i, i ^ 2) for i in range(8)])


def swap_across(shard):
    return lax.ppermute(shard, "seq", [(i, i ^ 4) for i in range(8)])


def add_low(left, right):
    return (left.astype(f32) + right.astype(f32)).astype(bf16)


def scatter_plain(normed, grad_both, grad_mix, mixed, rest, mlp_sum):
    groups = lax.axis_size("fsdp")
    term_wide = mm(normed, grad_both, ((0,), (0,))).astype(bf16)
    term_out = mm(grad_mix, mixed, ((0,), (0,))).astype(bf16)
    mixer_sum = lax.psum_scatter(
        jnp.concatenate([term_wide, term_out, rest], axis=1), "seq", scatter_dimension=0, tiled=True
    )
    mixer_sum = lax.psum_scatter(mixer_sum, "fsdp", scatter_dimension=0, tiled=True)
    ff_part = mlp_sum.shape[1] // 3
    part_rows = mlp_sum.shape[0] // groups
    mlp_sum = mlp_sum.reshape(groups, part_rows, 3, ff_part)
    mlp_back = lax.all_to_all(mlp_sum, "fsdp", 0, 0, tiled=True)
    mlp_back = jnp.transpose(mlp_back, (2, 1, 0, 3)).reshape(3, part_rows, groups * ff_part)
    return mixer_sum, mlp_back


def call_heads(kernel, width, heads, ins, outs, scratch, name):
    def spec(rows, place):
        if place is None:
            return pl.BlockSpec((rows, width), lambda h: (0, h))
        return pl.BlockSpec((width, width), lambda h: (h, place))

    in_specs = [spec(a.shape[0], place) for a, place in ins]
    out_specs = [spec(rows, 0 if rowwise else None) for rows, _, rowwise in outs]
    out_shape = [
        jax.ShapeDtypeStruct((heads * width, width) if rowwise else (rows, heads * width), kind)
        for rows, kind, rowwise in outs
    ]
    return pl.pallas_call(
        kernel,
        grid=(heads,),
        in_specs=in_specs,
        out_specs=out_specs,
        out_shape=out_shape,
        scratch_shapes=[pltpu.VMEM((rows, width), f32) for rows in scratch],
        compiler_params=pltpu.CompilerParams(vmem_limit_bytes=16 * 1024 * 1024),
        cost_estimate=pl.CostEstimate(flops=1, bytes_accessed=1, transcendentals=0),
        name=name,
    )(*[a for a, _ in ins])


def on_device(
    block_input,
    cotangent,
    mixer_gain,
    branch_proj,
    gelu_proj,
    conv_taps,
    conv_bias,
    rate_blocks,
    input_blocks,
    rate_bias,
    input_bias,
    decay_param,
    out_proj,
    mlp_gain,
    gate_proj,
    up_proj,
    down_proj,
):
    groups = lax.axis_size("fsdp")
    part_rows, lru = branch_proj.shape
    width = rate_blocks.shape[1]
    heads = lru // width
    margin = conv_taps.shape[0] - 1
    tokens = block_input[0].astype(f32)
    tok_count, model = tokens.shape
    ff = gate_proj.shape[1]
    ff_part = ff // groups
    grad_out = cotangent[0]

    smalls = jnp.stack(
        [conv_taps[k] for k in range(margin + 1)]
        + [conv_bias, rate_bias, input_bias, decay_param, mixer_gain, mlp_gain],
        axis=1,
    )
    small_count = smalls.shape[1]
    smalls = jnp.pad(smalls, ((0, 0), (0, 128 - small_count)))
    first_own = jnp.concatenate([rate_blocks, input_blocks, smalls], axis=1)
    mixer_own = (first_own, branch_proj, gelu_proj, out_proj)
    custom = lax.axis_size("seq") == 8 and groups == 4
    if custom:
        mixer_w, mlp_mine = gather(*mixer_own, gate_proj, up_proj, down_proj)
    else:
        mixer_w, mlp_mine = gather_plain(jnp.concatenate(mixer_own, axis=1), gate_proj, up_proj, down_proj)
    mlp_w = lax.all_gather(mlp_mine, "seq", axis=0, tiled=True)
    grad_out_late = lax.optimization_barrier((grad_out, mlp_mine))[0]
    if custom:
        grad_pieces = from_line(grad_out_late)
    wide = mixer_w[:, 128 + 2 * width : 128 + 2 * width + 2 * lru]
    proj_out = mixer_w[:, 128 + 2 * width + 2 * lru :]

    small = small_table(mixer_w, 2 * width // 128)
    gain_one, gain_two = small[GAIN_ONE], small[GAIN_TWO]

    normed, branch, gelu_pre = mixer_in(block_input[0], small, mixer_w, lru, 2 * width + 128)
    prior = from_behind(branch[tok_count - margin :], "seq", 1).astype(f32)
    prior = jnp.concatenate([jnp.zeros((8 - margin, lru), f32), prior], axis=0)
    conv, rate_pre, input_pre, cum, local = call_heads(
        mixer_forward,
        width,
        heads,
        [(branch, None), (prior, None), (small, None), (mixer_w, 0), (mixer_w, 1)],
        [(tok_count, bf16, False)] + [(tok_count, f32, False)] * 4,
        [tok_count + 8],
        "mixer_forward",
    )
    carried = prefix((cum[-1], local[-1]), "seq", False)
    states = local + cum * carried[None]
    mixed = (states * jax.nn.gelu(gelu_pre, approximate=True)).astype(bf16)
    middle = tokens + mm(mixed, proj_out, ((1,), (1,)))
    normed_two = norm_rows(middle, gain_two).astype(bf16)

    if custom:
        normed_all, normed_other, grad_out_all, grad_out_other, first_other, mixed_other = gather_rows(
            normed_two, grad_pieces, normed, mixed
        )
    else:
        normed_all = lax.all_gather(normed_two, "fsdp", axis=0, tiled=True)
        grad_out_all = lax.all_gather(grad_out_late, "fsdp", axis=0, tiled=True)
    w_gate, w_up, w_down = mlp_w[:, :ff_part], mlp_w[:, ff_part : 2 * ff_part], mlp_w[:, 2 * ff_part :]
    if custom:
        hidden, hidden_other, grad_pair, pair_other, grad_normed_part = feed_forward(
            normed_all, grad_out_all, mlp_w
        )
    else:
        gate = mm(normed_all, w_gate, ((1,), (0,)))
        up_val = mm(normed_all, w_up, ((1,), (0,)))
        gelu_gate, gelu_slope = gelu_parts(gate)
        hidden = (gelu_gate * up_val).astype(bf16)
        grad_hidden = mm(grad_out_all, w_down, ((1,), (0,)))
        grad_gate = (grad_hidden * up_val * gelu_slope).astype(bf16)
        grad_up = (grad_hidden * gelu_gate).astype(bf16)
        grad_normed_part = (
            mm(grad_gate, w_gate, ((1,), (1,))) + mm(grad_up, w_up, ((1,), (1,)))
        ).astype(bf16)
    grad_normed_two = lax.psum_scatter(grad_normed_part, "fsdp", scatter_dimension=0, tiled=True)
    if custom:
        half = model // 16
        beside_high, across_low, mine, beside_low, across_high, out_part = shared_products(
            (normed_all, normed_other, grad_out_all, grad_out_other),
            mlp_w,
            (grad_pair, pair_other),
            (hidden, hidden_other),
        )
        from_beside_high, from_across_low = swap_beside(beside_high), swap_across(across_low)
    else:
        grad_pair = jnp.concatenate([grad_gate, grad_up], axis=1)
        term_pair = mm(normed_all, grad_pair, ((0,), (0,))).astype(bf16)
        term_down = mm(grad_out_all, hidden, ((0,), (0,))).astype(bf16)
        pair_sum = lax.psum_scatter(term_pair, "seq", scatter_dimension=0, tiled=True)
        down_sum = lax.psum_scatter(term_down, "seq", scatter_dimension=0, tiled=True)
        mlp_sum = jnp.concatenate([pair_sum, down_sum], axis=1)
        out_part = mm(hidden, w_down, ((1,), (1,))).astype(bf16)
    out_sum = lax.psum_scatter(out_part, "fsdp", scatter_dimension=0, tiled=True)
    grad_normed_two = grad_normed_two.astype(f32)

    grad_middle = grad_out.astype(f32) + norm_back(middle, gain_two, grad_normed_two)
    grad_mix = grad_middle.astype(bf16)
    if custom:
        mix_other = swap_cores(grad_mix)
    grad_mixed = mm(grad_mix, proj_out, ((1,), (0,)))
    carried_rows = jnp.broadcast_to(carried[None], (8, lru))
    grad_gelu_pre, rev_cum, rev_grad, pair_grad = call_heads(
        mixer_backward_scan,
        width,
        heads,
        [(a, None) for a in (grad_mixed, gelu_pre, rate_pre, cum, local, carried_rows, small)],
        [(tok_count, bf16, False), (tok_count, f32, False), (tok_count, f32, False), (8, f32, False)],
        [tok_count + 8],
        "mixer_backward_scan",
    )
    if custom:
        from_beside_high, from_across_low, pair_grad = lax.optimization_barrier(
            (from_beside_high, from_across_low, pair_grad)
        )
    if custom:
        gelu_other = swap_cores(grad_gelu_pre)
    incoming = prefix((cum[-1], pair_grad[0]), "seq", True)
    if custom:
        beside_low, across_high, incoming = lax.optimization_barrier((beside_low, across_high, incoming))
        from_beside_low, from_across_high = swap_beside(beside_low), swap_across(across_high)
    incoming_rows = jnp.broadcast_to(incoming[None], (8, lru))
    own, head, rate_w_grad, input_w_grad, sums = call_heads(
        mixer_backward,
        width,
        heads,
        [
            (a, None)
            for a in (rev_cum, rev_grad, incoming_rows, cum, local, carried_rows, rate_pre, input_pre, conv, branch, prior, small)
        ]
        + [(mixer_w, 0), (mixer_w, 1)],
        [(tok_count, f32, False), (8, f32, False), (0, bf16, True), (0, bf16, True), (8, f32, False)],
        [tok_count + 8, tok_count + 16],
        "mixer_backward",
    )
    received = from_behind(head[8 - margin :], "seq", -1)
    grad_branch = jnp.concatenate(
        [own[: tok_count - margin], own[tok_count - margin :] + received], axis=0
    ).astype(bf16)
    grad_both = jnp.concatenate([grad_branch, grad_gelu_pre], axis=1)
    vectors = jnp.pad(sums.T, ((0, 0), (0, 128 - sums.shape[0]))).astype(bf16)
    rest = jnp.concatenate([rate_w_grad, input_w_grad, vectors], axis=1)
    if custom:
        low, high = [
            sum(part.astype(f32) for part in parts).astype(bf16)
            for parts in (
                (mine[:half], from_across_low, from_beside_low),
                (mine[half:], from_across_high, from_beside_high),
            )
        ]
        mixer_sum, mlp_back, input_grad = scatter(
            (normed, first_other, grad_mix, mix_other, mixed, mixed_other, grad_gelu_pre, gelu_other),
            grad_branch, rest, low, high, mixer_w, block_input[0], small,
        )
    else:
        mixer_sum, mlp_back = scatter_plain(normed, grad_both, grad_mix, mixed, rest, mlp_sum)
        grad_normed = mm(grad_both, wide, ((1,), (1,)))
        input_grad = (grad_middle + norm_back(tokens, gain_one, grad_normed)).astype(bf16)
    input_grad = input_grad[None]
    middle = lax.optimization_barrier((middle, rest))[0]
    block_output = (middle + out_sum.astype(f32)).astype(bf16)[None]
    edge = 3 * lru + 2 * width
    vec = mixer_sum[:, edge:].astype(f32).T
    weight_grads = list(
        jnp.split(mixer_sum[:, :edge].astype(f32), [lru, 2 * lru, 3 * lru, 3 * lru + width], axis=1)
    ) + [mlp_back[m].astype(f32) for m in range(3)]
    first_total = gain_back((branch_proj, weight_grads[0]), (gelu_proj, weight_grads[1]))
    second_total = gain_back((gate_proj, weight_grads[5]), (up_proj, weight_grads[6]))
    dbranch, dgelu, dout, drate, dinput, dgate, dup, ddown = weight_grads
    return (
        block_output,
        input_grad,
        first_total / mixer_gain.astype(f32),
        dbranch,
        dgelu,
        vec[: margin + 1],
        vec[7],
        drate,
        dinput,
        vec[4],
        vec[5],
        vec[6],
        dout,
        second_total / mlp_gain.astype(f32),
        dgate,
        dup,
        ddown,
    )


def solution(mesh):
    tokens = P("fsdp", "seq", None)
    vector = P(both)
    matrix = P(both, None)
    taps = P(None, both)
    return jax.shard_map(
        on_device,
        mesh=mesh,
        in_specs=(
            tokens, tokens, vector, matrix, matrix, taps, vector, matrix, matrix,
            vector, vector, vector, matrix, vector, matrix, matrix, matrix,
        ),
        out_specs=(
            tokens, tokens, vector, matrix, matrix, taps, vector, matrix, matrix,
            vector, vector, vector, matrix, vector, matrix, matrix, matrix,
        ),
        check_vma=False,
    )
```
